32 devices in a mesh: dp: 8 (over y, x, core), blk: 4 (over z).
Axes of the slice: x: 2, y: 2, z: 4, core: 2. Of those that a mesh axis runs over, the one named last changes fastest.
Arguments:
- replay: float32 [42, 116736], P(None, ('dp', 'blk')), may hold values from -27 to 27, as said below
- model_rows: float32 [42, 38912], P(None, ('dp', 'blk')), may hold values from -27 to 27, as said below
- requests: int32 [256, 8], P(('dp', 'blk')), may hold values from -1 to 3647, as said below
- member_of: int32 [256, 8], P(('dp', 'blk')), may hold values from 0 to 6
- model_live: int32 [38912], P(('dp', 'blk')), may hold values from 0 to 1
- noise: float32 [2, 40960, 6], P(None, ('dp', 'blk')), may hold values from -4 to 4
- sac_hidden: float32 [3, 256, 256], P(None, 'blk'), may hold values from -0.375 to 0.375
- sac_hidden_mom: float32 [3, 256, 256], P(None, 'blk'), may hold values from -0.21875 to 0.21875
- dyn_hidden: float32 [7, 200, 200], P(None, 'blk'), may hold values from -0.4375 to 0.4375
- dyn_hidden_mom: float32 [7, 200, 200], P(None, 'blk'), may hold values from -0.046875 to 0.046875
- crit_in: float32 [2, 23, 256], replicated, may hold values from -1.25 to 1.25
- crit_in_m: float32 [2, 23, 256], replicated, may hold values from -0.0234375 to 0.0234375
- crit_in_v: float32 [2, 23, 256], replicated, may hold values from 2.4414064e-07 to 9.765625e-07
- act_in: float32 [17, 256], replicated, may hold values from -1.5 to 1.5
- act_in_m: float32 [17, 256], replicated, may hold values from -0.0234375 to 0.0234375
- act_in_v: float32 [17, 256], replicated, may hold values from 2.4414064e-07 to 9.765625e-07
- dyn_in: float32 [7, 23, 200], replicated, may hold values from -1.25 to 1.25
- dyn_in_m: float32 [7, 23, 200], replicated, may hold values from -0.00390625 to 0.00390625
- dyn_in_v: float32 [7, 23, 200], replicated, may hold values from 9.765625e-09 to 3.90625e-08
- crit_out: float32 [2, 256], replicated, may hold values from -0.375 to 0.375
- crit_out_m: float32 [2, 256], replicated, may hold values from -0.0234375 to 0.0234375
- crit_out_v: float32 [2, 256], replicated, may hold values from 2.4414064e-07 to 9.765625e-07
- act_out: float32 [256, 12], replicated, may hold values from -0.375 to 0.375
- act_out_m: float32 [256, 12], replicated, may hold values from -0.0234375 to 0.0234375
- act_out_v: float32 [256, 12], replicated, may hold values from 2.4414064e-07 to 9.765625e-07
- dyn_out: float32 [7, 200, 36], replicated, may hold values from -0.4375 to 0.4375
- dyn_out_m: float32 [7, 200, 36], replicated, may hold values from -0.00390625 to 0.00390625
- dyn_out_v: float32 [7, 200, 36], replicated, may hold values from 9.765625e-09 to 3.90625e-08
- biases: float32 [4639], replicated, may hold values from -1.5 to 1.5
- biases_m: float32 [4639], replicated, may hold values from -0.0234375 to 0.0234375
- biases_v: float32 [4639], replicated, may hold values from 2.4414064e-07 to 9.765625e-07
- targ_in: float32 [2, 23, 256], replicated, may hold values from -1.25 to 1.25
- targ_hidden: float32 [2, 256, 256], replicated, may hold values from -0.375 to 0.375
- targ_out: float32 [2, 256], replicated, may hold values from -0.375 to 0.375
- targ_bias: float32 [2, 513], replicated, may hold values from -1.5 to 1.5
Outputs:
- sac_hidden_new: float32 [3, 256, 256], P(None, 'blk')
- sac_hidden_mom_new: float32 [3, 256, 256], P(None, 'blk')
- dyn_hidden_new: float32 [7, 200, 200], P(None, 'blk')
- dyn_hidden_mom_new: float32 [7, 200, 200], P(None, 'blk')
- crit_in_new: float32 [2, 23, 256], replicated
- crit_in_m_new: float32 [2, 23, 256], replicated
- crit_in_v_new: float32 [2, 23, 256], replicated
- act_in_new: float32 [17, 256], replicated
- act_in_m_new: float32 [17, 256], replicated
- act_in_v_new: float32 [17, 256], replicated
- dyn_in_new: float32 [7, 23, 200], replicated
- dyn_in_m_new: float32 [7, 23, 200], replicated
- dyn_in_v_new: float32 [7, 23, 200], replicated
- crit_out_new: float32 [2, 256], replicated
- crit_out_m_new: float32 [2, 256], replicated
- crit_out_v_new: float32 [2, 256], replicated
- act_out_new: float32 [256, 12], replicated
- act_out_m_new: float32 [256, 12], replicated
- act_out_v_new: float32 [256, 12], replicated
- dyn_out_new: float32 [7, 200, 36], replicated
- dyn_out_m_new: float32 [7, 200, 36], replicated
- dyn_out_v_new: float32 [7, 200, 36], replicated
- biases_new: float32 [4639], replicated
- biases_m_new: float32 [4639], replicated
- biases_v_new: float32 [4639], replicated
- loss_sum: float32 [], replicated
- loss_count: float32 [], replicated
The draws below stay inside these ranges and needn't reach their ends.
Inputs may be any that keep to these rules, and one draw needn't show every extreme that they name: `replay`: transition columns: observation entries, actions in -1..1, a reward, next observation entries, and a done flag that is 0 or 1. `model_rows`: same layout as replay. `requests`: each row of 8 slots names rows of its owner's 3648 replay rows; filled slots come first, at least one in every row, and -1 marks an empty slot. In every draw some owner receives full rows from every device that asks it.
All inputs are finite; a program needn't handle non-finite values.
Results may differ from the reference program's by a relative error of at most 0.00035.
The reference program's roundings to bfloat16 on the way count: a program that leaves them out, or rounds other values in their place, can miss the bound.
Values may be sent and summed in bfloat16 or wider, within the bound.
A program may use at most 192 MiB of HBM per device.

```python
import math
import jax
import jax.numpy as jnp
from jax import lax

OBS = 17
ACT = 6
HDYN = 200
HSAC = 256
MEMBERS = 7
CAP = 8
ROWS_DEV = 3648
NS_ITERS = 5
STEP = 10
IN = 23
DOUT = 36
FEAT = 42
NB = 4639
MODEL_DEV = 1216
ROWS = 116736
BATCH_ALL = 40960
N_DP = 8
N_BLK = 4
DEVICES = 32


def transition_rows(key, columns, per_device):
    device = jnp.arange(columns) // per_device
    scale = 1.0 + ((device // N_BLK).astype(jnp.float32) / (N_DP - 1) + (device % N_BLK).astype(jnp.float32) / (N_BLK - 1))
    first, second, third, fourth, fifth = jax.random.split(key, 5)
    states = scale[None, :] * jnp.clip(jax.random.normal(first, (OBS, columns)), -4.0, 4.0)
    actions = jax.random.uniform(second, (ACT, columns), minval=-1.0, maxval=1.0)
    rewards = jnp.clip(jax.random.normal(third, (1, columns)), -4.0, 4.0)
    following = states + jnp.clip(jax.random.normal(fourth, (OBS, columns)), -4.0, 4.0)
    finished = jax.random.bernoulli(fifth, 0.05, (1, columns)).astype(jnp.float32)
    return jnp.concatenate([states, actions, rewards, following, finished], 0).astype(jnp.float32)


def draw_replay(key, part):
    key = jax.random.fold_in(key, 5)
    return transition_rows(key, ROWS_DEV * N_DP * N_BLK, ROWS_DEV)


def draw_model_rows(key, part):
    key = jax.random.fold_in(key, 7)
    return transition_rows(key, MODEL_DEV * N_DP * N_BLK, MODEL_DEV)


def draw_requests(key, part):
    key = jax.random.fold_in(key, 11)
    rows_total = N_DP * N_BLK * N_DP
    busiest = jax.random.randint(jax.random.fold_in(key, 1), (), 0, N_DP)
    counts = jax.random.randint(jax.random.fold_in(key, 2), (rows_total,), 1, CAP + 1)
    owner = jnp.arange(rows_total) % N_DP
    counts = jnp.where(owner == busiest, CAP, counts)
    picks = jax.random.randint(jax.random.fold_in(key, 3), (rows_total, CAP), 0, ROWS_DEV)
    slots = jnp.arange(CAP)[None, :]
    return jnp.where(slots < counts[:, None], picks, -1).astype(jnp.int32)


def draw_model_live(key, part):
    key = jax.random.fold_in(key, 23)
    columns = MODEL_DEV * N_DP * N_BLK
    device = jnp.arange(columns) // MODEL_DEV
    threshold = 200 + 350 * (device // N_BLK) // (N_DP - 1) + 350 * (device % N_BLK) // (N_BLK - 1)
    return (jax.random.randint(key, (columns,), 0, 1000) < threshold).astype(jnp.int32)


def set_ends(entries, key, least, high):
    spot = [jax.random.randint(jax.random.fold_in(key, axis), (), 0, length) for axis, length in enumerate(entries.shape)]
    longest = entries.shape.index(max(entries.shape))
    beside = spot[:longest] + [(spot[longest] + 1) % entries.shape[longest]] + spot[longest + 1:]
    return entries.at[tuple(spot)].set(least).at[tuple(beside)].set(high)


def block_scale(own_key, extent, cuts, low, top_value):
    def one(axis_at, blocks):
        draws = jax.random.uniform(jax.random.fold_in(jax.random.fold_in(own_key, 6), axis_at), (blocks,), jnp.float32, low / len(cuts), top_value / len(cuts))
        return jnp.repeat(jnp.exp(draws), extent[axis_at] // blocks).reshape((-1,) + (1,) * (len(extent) - axis_at - 1))

    gain = one(*cuts[0])
    for cut in cuts[1:]:
        gain = gain * one(*cut)
    return gain


def scatter_about(stream_key, shape, deviation, limit, shards=(), kind=jnp.bfloat16):
    level = block_scale(stream_key, shape, shards, -0.22, 0.18) if shards else 1.0
    result = jax.random.normal(stream_key, shape, jnp.float32) * deviation * level
    return jnp.minimum(jnp.maximum(result, -limit), limit).astype(kind)


def setup_inputs(seed: int = 0) -> dict:
    keys = jax.random.split(jax.random.key(seed), 36)
    replay = draw_replay(jax.random.fold_in(keys[35], 71), 0)
    model_rows = draw_model_rows(jax.random.fold_in(keys[35], 71), 0)
    requests = draw_requests(jax.random.fold_in(keys[35], 71), 0)
    member_of = set_ends(jax.random.randint(keys[3], (DEVICES * N_DP, CAP), 0, MEMBERS), jax.random.fold_in(keys[3], 1), 0, MEMBERS - 1).astype(jnp.int32)
    model_live = draw_model_live(jax.random.fold_in(keys[35], 71), 0)
    noise = scatter_about(keys[5], (2, BATCH_ALL, ACT), 1.0, 4.0, ((1, 32),), jnp.float32)
    sac_hidden = scatter_about(keys[6], (3, HSAC, HSAC), HSAC ** -0.5, 0.375, ((1, 4),), jnp.float32)
    sac_hidden_mom = scatter_about(keys[7], (3, HSAC, HSAC), (3.0 / BATCH_ALL ** 0.5), 0.21875, ((1, 4),), jnp.float32)
    dyn_hidden = scatter_about(keys[8], (MEMBERS, HDYN, HDYN), HDYN ** -0.5, 0.4375, ((1, 4),), jnp.float32)
    dyn_hidden_mom = scatter_about(keys[9], (MEMBERS, HDYN, HDYN), (0.6 / BATCH_ALL ** 0.5), 0.046875, ((1, 4),), jnp.float32)
    crit_in = scatter_about(keys[10], (2, IN, HSAC), IN ** -0.5, 1.25, (), jnp.float32)
    crit_in_m = scatter_about(keys[11], (2, IN, HSAC), (0.3 / BATCH_ALL ** 0.5), 0.0234375, (), jnp.float32)
    crit_in_v = jnp.clip(jnp.exp(jax.random.uniform(keys[12], (2, IN, HSAC), jnp.float32, math.log(2.4414063659605745e-07), math.log(9.765625463842298e-07))), 2.4414063659605745e-07, 9.765625463842298e-07)
    act_in = scatter_about(keys[13], (OBS, HSAC), OBS ** -0.5, 1.5, (), jnp.float32)
    act_in_m = scatter_about(keys[14], (OBS, HSAC), (0.3 / BATCH_ALL ** 0.5), 0.0234375, (), jnp.float32)
    act_in_v = jnp.clip(jnp.exp(jax.random.uniform(keys[15], (OBS, HSAC), jnp.float32, math.log(2.4414063659605745e-07), math.log(9.765625463842298e-07))), 2.4414063659605745e-07, 9.765625463842298e-07)
    dyn_in = scatter_about(keys[16], (MEMBERS, IN, HDYN), IN ** -0.5, 1.25, (), jnp.float32)
    dyn_in_m = scatter_about(keys[17], (MEMBERS, IN, HDYN), (0.06 / BATCH_ALL ** 0.5), 0.00390625, (), jnp.float32)
    dyn_in_v = jnp.clip(jnp.exp(jax.random.uniform(keys[18], (MEMBERS, IN, HDYN), jnp.float32, math.log(9.765624753299562e-09), math.log(3.906249901319825e-08))), 9.765624753299562e-09, 3.906249901319825e-08)
    crit_out = scatter_about(keys[19], (2, HSAC), HSAC ** -0.5, 0.375, (), jnp.float32)
    crit_out_m = scatter_about(keys[20], (2, HSAC), (0.3 / BATCH_ALL ** 0.5), 0.0234375, (), jnp.float32)
    crit_out_v = jnp.clip(jnp.exp(jax.random.uniform(keys[21], (2, HSAC), jnp.float32, math.log(2.4414063659605745e-07), math.log(9.765625463842298e-07))), 2.4414063659605745e-07, 9.765625463842298e-07)
    act_out = scatter_about(keys[22], (HSAC, 2 * ACT), HSAC ** -0.5, 0.375, (), jnp.float32)
    act_out_m = scatter_about(keys[23], (HSAC, 2 * ACT), (0.3 / BATCH_ALL ** 0.5), 0.0234375, (), jnp.float32)
    act_out_v = jnp.clip(jnp.exp(jax.random.uniform(keys[24], (HSAC, 2 * ACT), jnp.float32, math.log(2.4414063659605745e-07), math.log(9.765625463842298e-07))), 2.4414063659605745e-07, 9.765625463842298e-07)
    dyn_out = scatter_about(keys[25], (MEMBERS, HDYN, DOUT), HDYN ** -0.5, 0.4375, (), jnp.float32)
    dyn_out_m = scatter_about(keys[26], (MEMBERS, HDYN, DOUT), (0.06 / BATCH_ALL ** 0.5), 0.00390625, (), jnp.float32)
    dyn_out_v = jnp.clip(jnp.exp(jax.random.uniform(keys[27], (MEMBERS, HDYN, DOUT), jnp.float32, math.log(9.765624753299562e-09), math.log(3.906249901319825e-08))), 9.765624753299562e-09, 3.906249901319825e-08)
    biases = scatter_about(keys[28], (NB,), 0.1, 1.5, (), jnp.float32)
    biases_m = scatter_about(keys[29], (NB,), (0.3 / BATCH_ALL ** 0.5), 0.0234375, (), jnp.float32)
    biases_v = jnp.clip(jnp.exp(jax.random.uniform(keys[30], (NB,), jnp.float32, math.log(2.4414063659605745e-07), math.log(9.765625463842298e-07))), 2.4414063659605745e-07, 9.765625463842298e-07)
    targ_in = scatter_about(keys[31], (2, IN, HSAC), IN ** -0.5, 1.25, (), jnp.float32)
    targ_hidden = scatter_about(keys[32], (2, HSAC, HSAC), HSAC ** -0.5, 0.375, (), jnp.float32)
    targ_out = scatter_about(keys[33], (2, HSAC), HSAC ** -0.5, 0.375, (), jnp.float32)
    targ_bias = scatter_about(keys[34], (2, 2 * HSAC + 1), 0.1, 1.5, (), jnp.float32)
    return {"replay": replay, "model_rows": model_rows, "requests": requests, "member_of": member_of, "model_live": model_live, "noise": noise, "sac_hidden": sac_hidden, "sac_hidden_mom": sac_hidden_mom, "dyn_hidden": dyn_hidden, "dyn_hidden_mom": dyn_hidden_mom, "crit_in": crit_in, "crit_in_m": crit_in_m, "crit_in_v": crit_in_v, "act_in": act_in, "act_in_m": act_in_m, "act_in_v": act_in_v, "dyn_in": dyn_in, "dyn_in_m": dyn_in_m, "dyn_in_v": dyn_in_v, "crit_out": crit_out, "crit_out_m": crit_out_m, "crit_out_v": crit_out_v, "act_out": act_out, "act_out_m": act_out_m, "act_out_v": act_out_v, "dyn_out": dyn_out, "dyn_out_m": dyn_out_m, "dyn_out_v": dyn_out_v, "biases": biases, "biases_m": biases_m, "biases_v": biases_v, "targ_in": targ_in, "targ_hidden": targ_hidden, "targ_out": targ_out, "targ_bias": targ_bias}


PRECISE = lax.Precision.HIGHEST
DISCOUNT = 0.99
TARGET_ENTROPY = -6.0
BOUND_WEIGHT = 0.01
MOMENTUM = 0.95
MUON_RATE = 0.4
MUON_DECAY = 0.01
ADAM_RATE = 0.1
ADAM_DECAY = 0.01
BETA_FIRST = 0.9
BETA_SECOND = 0.999
COEF_LINEAR = 3.4445
COEF_CUBIC = -4.775
COEF_QUINTIC = 2.0315

@jax.custom_vjp
def low(v):
    return lax.optimization_barrier(v.astype(jnp.bfloat16)).astype(jnp.float32)

@jax.custom_vjp
def low_back(v):
    return v

def low_keep(v):
    return (low(v), None)

def low_pass(kept, grad):
    return (grad,)

def back_keep(v):
    return (v, None)

def back_low(kept, grad):
    return (low(grad),)
low.defvjp(low_keep, low_pass)
low_back.defvjp(back_keep, back_low)

def smooth_gate(value):
    return value * jax.nn.sigmoid(value)

def dense_layer(inputs, weights, offset):
    return low_back(jnp.matmul(low(inputs), low(weights), precision=PRECISE) + offset)

def unpack_biases(vector):
    widths = [2 * HSAC, 2 * HSAC, 2, HSAC, HSAC, 2 * ACT, MEMBERS * HDYN, MEMBERS * HDYN, MEMBERS * 2 * (OBS + 1), OBS + 1, OBS + 1, 1]
    pieces = []
    start = 0
    for width in widths:
        pieces.append(vector[start:start + width])
        start = start + width
    return (pieces[0].reshape(2, HSAC), pieces[1].reshape(2, HSAC), pieces[2], pieces[3], pieces[4], pieces[5], pieces[6].reshape(MEMBERS, HDYN), pieces[7].reshape(MEMBERS, HDYN), pieces[8].reshape(MEMBERS, 2 * (OBS + 1)), pieces[9], pieces[10], pieces[11][0])

def bound_penalty(vector):
    parts = unpack_biases(vector)
    return BOUND_WEIGHT * (jnp.sum(parts[9]) - jnp.sum(parts[10]))

def critic_pair(joined, w_in, w_hidden, w_out, first_bias, second_bias, last_bias):
    layer = smooth_gate(dense_layer(joined, w_in, first_bias[:, None, :]))
    layer = smooth_gate(dense_layer(layer, w_hidden, second_bias[:, None, :]))
    return dense_layer(layer, w_out[:, :, None], last_bias[:, None, None])[:, :, 0]

def policy(states, w_in, w_hidden, w_out, first_bias, second_bias, last_bias, noise_rows):
    layer = smooth_gate(dense_layer(states, w_in, first_bias))
    layer = smooth_gate(dense_layer(layer, w_hidden, second_bias))
    output = dense_layer(layer, w_out, last_bias)
    log_scale = -5.0 + 3.5 * (jnp.tanh(output[:, ACT:]) + 1.0)
    latent = output[:, :ACT] + jnp.exp(log_scale) * noise_rows
    log_prob = lax.optimization_barrier(jnp.sum(-0.5 * noise_rows * noise_rows - log_scale - 0.9189385 - 2.0 * (0.6931472 - latent - jax.nn.softplus(-2.0 * latent)), axis=1))
    return (jnp.tanh(latent), log_prob)

def dynamics_model(inputs, w_in, w_hidden, w_out, first_bias, second_bias, last_bias, upper, lower):
    layer = smooth_gate(dense_layer(inputs, w_in, first_bias[:, None, :]))
    layer = smooth_gate(dense_layer(layer, w_hidden, second_bias[:, None, :]))
    output = dense_layer(layer, w_out, last_bias[:, None, :])
    width = OBS + 1
    log_var = upper - jax.nn.softplus(upper - output[:, :, width:])
    log_var = lower + jax.nn.softplus(log_var - lower)
    return (output[:, :, :width], log_var)

def prepare(params, targets, batch, noise):
    sac_hidden, dyn_hidden, crit_in, act_in, dyn_in, crit_out, act_out, dyn_out, biases = params
    targ_in, targ_hidden, targ_out, targ_bias = targets
    parts = unpack_biases(biases)
    states = batch[:, :OBS]
    following = batch[:, OBS + ACT + 1:2 * OBS + ACT + 1]
    alpha_fixed = jnp.exp(parts[11])
    next_action, next_prob = policy(following, act_in, sac_hidden[2], act_out, parts[3], parts[4], parts[5], noise[1])
    target_values = critic_pair(jnp.concatenate([following, next_action], 1), targ_in, targ_hidden, targ_out, targ_bias[:, :HSAC], targ_bias[:, HSAC:2 * HSAC], targ_bias[:, 2 * HSAC])
    reward = batch[:, OBS + ACT]
    finished = batch[:, 2 * OBS + ACT + 1]
    target_q = reward + DISCOUNT * (1.0 - finished) * (lax.optimization_barrier(jnp.min(target_values, axis=0)) - alpha_fixed * next_prob)
    unused, prob_fixed = policy(states, act_in, sac_hidden[2], act_out, parts[3], parts[4], parts[5], noise[0])
    return (target_q, prob_fixed, alpha_fixed)

def real_pieces(real_rows, centre_in, inv_scale, member_of, filled):
    real_input = (real_rows[:, :OBS + ACT] - centre_in) * inv_scale
    real_target = jnp.concatenate([real_rows[:, OBS + ACT + 1:2 * OBS + ACT + 1] - real_rows[:, :OBS], real_rows[:, OBS + ACT:OBS + ACT + 1]], 1)
    member_weight = (member_of.reshape(-1)[None, :] == jnp.arange(MEMBERS, dtype=jnp.int32)[:, None]).astype(jnp.float32)
    return (real_input, real_target, member_weight * filled[None, :])

def local_terms(params, frozen, batch, weight, real_input, real_target, member_weight, noise_now, target_q, prob_fixed, alpha_fixed):
    sac_hidden, dyn_hidden, crit_in, act_in, dyn_in, crit_out, act_out, dyn_out, biases = params
    parts = unpack_biases(biases)
    fixed_hidden, fixed_in, fixed_out, fixed_biases = frozen
    fixed_parts = unpack_biases(fixed_biases)
    states = batch[:, :OBS]
    values = critic_pair(batch[:, :OBS + ACT], crit_in, sac_hidden[:2], crit_out, parts[0], parts[1], parts[2])
    critic_terms = 0.5 * lax.optimization_barrier(jnp.sum((values - target_q[None, :]) ** 2, axis=0))
    action, log_prob = policy(states, act_in, sac_hidden[2], act_out, parts[3], parts[4], parts[5], noise_now)
    judged = critic_pair(jnp.concatenate([states, action], 1), fixed_in, fixed_hidden, fixed_out, fixed_parts[0], fixed_parts[1], fixed_parts[2])
    actor_terms = alpha_fixed * log_prob - lax.optimization_barrier(jnp.mean(judged, axis=0))
    alpha_terms = -parts[11] * (prob_fixed + TARGET_ENTROPY)
    sac_total = jnp.sum(weight * (critic_terms + actor_terms + alpha_terms))
    centre, log_var = dynamics_model(real_input, dyn_in, dyn_hidden, dyn_out, parts[6], parts[7], parts[8], parts[9], parts[10])
    errors = lax.optimization_barrier(jnp.sum((centre - real_target[None]) ** 2 * jnp.exp(-log_var) + log_var, axis=2))
    return sac_total + jnp.sum(member_weight * errors)

def schulz_step(matrix, gram):
    square = jnp.matmul(gram, gram, precision=PRECISE)
    return COEF_LINEAR * matrix + jnp.matmul(matrix, COEF_CUBIC * gram + COEF_QUINTIC * square, precision=PRECISE)

def newton_schulz(moment):
    matrix = moment / (jnp.sqrt(lax.optimization_barrier(jnp.sum(moment * moment, axis=(1, 2), keepdims=True))) + 1e-07)
    for step in range(NS_ITERS):
        gram = jnp.matmul(jnp.swapaxes(matrix, 1, 2), matrix, precision=PRECISE)
        matrix = schulz_step(matrix, gram)
    return matrix

def muon_weight(weights, direction):
    return weights * (1.0 - MUON_RATE * MUON_DECAY) - MUON_RATE * direction

def adamw_update(weights, first, second, gradient):
    first = BETA_FIRST * first + (1.0 - BETA_FIRST) * gradient
    second = BETA_SECOND * second + (1.0 - BETA_SECOND) * gradient * gradient
    first_hat = first / (1.0 - BETA_FIRST ** STEP)
    second_hat = second / (1.0 - BETA_SECOND ** STEP)
    weights = weights - ADAM_RATE * (first_hat / (jnp.sqrt(second_hat) + 1e-08) + ADAM_DECAY * weights)
    return (weights, first, second)

def reference(replay, model_rows, requests, member_of, model_live, noise, sac_hidden, sac_hidden_mom, dyn_hidden, dyn_hidden_mom, crit_in, crit_in_m, crit_in_v, act_in, act_in_m, act_in_v, dyn_in, dyn_in_m, dyn_in_v, crit_out, crit_out_m, crit_out_v, act_out, act_out_m, act_out_v, dyn_out, dyn_out_m, dyn_out_v, biases, biases_m, biases_v, targ_in, targ_hidden, targ_out, targ_bias):
    inputs = replay[:OBS + ACT]
    centre_in = lax.optimization_barrier(jnp.sum(inputs, axis=1)) / ROWS
    inv_scale = lax.rsqrt(lax.optimization_barrier(jnp.sum(inputs * inputs, axis=1)) / ROWS - centre_in * centre_in + 1e-06)
    devices = N_DP * N_BLK
    asked = requests.reshape(devices, N_DP, CAP)
    device_ids = jnp.arange(devices, dtype=jnp.int32)
    owners = jnp.arange(N_DP, dtype=jnp.int32)[None, :] * N_BLK + (device_ids % N_BLK)[:, None]
    columns = owners[:, :, None] * ROWS_DEV + jnp.maximum(asked, 0)
    real_rows = jnp.take(replay, columns.reshape(-1), axis=1).T
    filled = (requests.reshape(-1) >= 0).astype(jnp.float32)
    batch = jnp.concatenate([real_rows.reshape(devices, N_DP * CAP, FEAT), model_rows.T.reshape(devices, MODEL_DEV, FEAT)], 1).reshape(-1, FEAT)
    weight = jnp.concatenate([filled.reshape(devices, -1), model_live.astype(jnp.float32).reshape(devices, -1)], 1).reshape(-1)
    row_count = jnp.sum(weight)
    params = (sac_hidden, dyn_hidden, crit_in, act_in, dyn_in, crit_out, act_out, dyn_out, biases)
    target_q, prob_fixed, alpha_fixed = prepare(params, (targ_in, targ_hidden, targ_out, targ_bias), batch, noise)
    frozen = (sac_hidden[:2], crit_in, crit_out, biases)
    real_input, real_target, member_weight = real_pieces(real_rows, centre_in, inv_scale, member_of, filled)

    def objective(values):
        total = local_terms(values, frozen, batch, weight, real_input, real_target, member_weight, noise[0], target_q, prob_fixed, alpha_fixed)
        return (total, bound_penalty(values[8]))
    outputs, pull = jax.vjp(objective, params)
    raw = pull((jnp.float32(1.0), row_count))[0]
    grads = [piece / row_count for piece in raw]
    sac_moment = MOMENTUM * sac_hidden_mom + grads[0]
    dyn_moment = MOMENTUM * dyn_hidden_mom + grads[1]
    sac_new = muon_weight(sac_hidden, newton_schulz(sac_moment))
    dyn_new = muon_weight(dyn_hidden, newton_schulz(dyn_moment))
    ci = adamw_update(crit_in, crit_in_m, crit_in_v, grads[2])
    ai = adamw_update(act_in, act_in_m, act_in_v, grads[3])
    di = adamw_update(dyn_in, dyn_in_m, dyn_in_v, grads[4])
    co = adamw_update(crit_out, crit_out_m, crit_out_v, grads[5])
    ao = adamw_update(act_out, act_out_m, act_out_v, grads[6])
    do_out = adamw_update(dyn_out, dyn_out_m, dyn_out_v, grads[7])
    bi = adamw_update(biases, biases_m, biases_v, grads[8])
    return (sac_new, sac_moment, dyn_new, dyn_moment, ci[0], ci[1], ci[2], ai[0], ai[1], ai[2], di[0], di[1], di[2], co[0], co[1], co[2], ao[0], ao[1], ao[2], do_out[0], do_out[1], do_out[2], bi[0], bi[1], bi[2], outputs[0], row_count)
```

```python
import functools
import math

import jax
import jax.numpy as jnp
from jax import lax
from jax.experimental import pallas as pl
from jax.experimental.pallas import tpu as pltpu
from jax.sharding import PartitionSpec as P

OBS = 17
ACT = 6
IN = OBS + ACT
FEAT = 42
HDYN = 200
HSAC = 256
MEMBERS = 7
DOUT = 36
HALF = DOUT // 2
NB = 4639
NS_ITERS = 5
STEP = 10
CAP = 8
TILE = 256

DISCOUNT = 0.99
TARGET_ENTROPY = -6.0
BOUND_WEIGHT = 0.01
MOMENTUM = 0.95
MUON_RATE = 0.4
MUON_DECAY = 0.01
ADAM_RATE = 0.1
ADAM_DECAY = 0.01
BETA_FIRST = 0.9
BETA_SECOND = 0.999
COEF_LINEAR = 3.4445
COEF_CUBIC = -4.775
COEF_QUINTIC = 2.0315

CB1, CB2, CB3, AB1, AB2, AB3 = 0, 512, 1024, 1026, 1282, 1538
DB1, DB2, DB3, MAXLV, MINLV, LOGA = 1550, 2950, 4350, 4602, 4620, 4638

R_IN, R_HEAD, R_OUT, R_MISC, R_SMALL = 0, 72, 88, 96, 128
D_IN, D_OUT, D_B2, D_B3, D_UP, D_LOW, D_LOSS, D_ROWS = 0, 24, 60, 61, 62, 63, 64, 72

F32, BF16 = jnp.float32, jnp.bfloat16
MESH = pl.DeviceIdType.MESH
NN = (((1,), (0,)), ((), ()))
NT = (((1,), (1,)), ((), ()))


def dot(a, b, dims=NN):
    return lax.dot_general(a, b, dims, preferred_element_type=F32)


def rounded(v):
    return v.astype(BF16).astype(F32)


def pieces(v):
    high = v.astype(BF16)
    rest = v - high.astype(F32)
    middle = rest.astype(BF16)
    return high, middle, (rest - middle.astype(F32)).astype(BF16)


def split(v):
    high = v.astype(BF16)
    return high, (v - high.astype(F32)).astype(BF16)


def product(a, b, dims=NN):
    return dot(a[0], b[0], dims) + dot(a[0], b[1], dims) + dot(a[1], b[0], dims)


def softplus(v):
    return jnp.maximum(v, 0.0) + jnp.log1p(jnp.exp(-jnp.abs(v)))


def sigmoid(v):
    return 0.5 + 0.5 * jnp.tanh(0.5 * v)


def gate(half):
    up = 1.0 + jnp.tanh(half)
    value = half * up
    return value, up + value * (2.0 - up)


def rows_of(shape):
    return lax.broadcasted_iota(jnp.int32, shape, 0)


def schulz(ref, steps):
    @pl.loop(0, steps)
    def _(step):
        matrix = ref[...]
        parts = split(matrix)
        gram = product(parts, parts, NT)
        halves = split(gram)
        blend = COEF_CUBIC * gram + COEF_QUINTIC * product(halves, halves)
        ref[...] = COEF_LINEAR * matrix + product(split(blend), parts)


class Layout:
    def __init__(self, mesh, replay, model):
        self.n_dp = mesh.shape["dp"]
        self.n_blk = mesh.shape["blk"]
        self.bits = int(math.log2(self.n_dp))
        self.n_dev = self.n_dp * self.n_blk
        self.replay = replay
        self.model = model
        self.real = self.n_dp * CAP
        self.batch = self.real + model
        self.width = -(-(self.real + 2) // 128) * 128
        self.rows = HSAC // self.n_blk
        self.drows = HDYN // self.n_blk
        self.mat = 64 // self.n_dp
        self.sml = 32 // self.n_dp
        self.chunk = 3 * self.mat + self.sml
        self.split_z = self.chunk % self.n_blk == 0
        self.part = self.chunk // self.n_blk if self.split_z else self.chunk
        self.owners = [self.n_dp - 1 - 2 * k for k in range(3)]


def main_kernel(lay, *refs):
    (
        replay, model, requests, member, live, noise, sac_h, sac_m, dyn_h, dyn_m, crit_in, act_in,
        dyn_in, crit_out, act_out, dyn_out, biases, targ_in, targ_hidden, targ_out, targ_bias,
        sac_g, sac_x, dyn_g, dyn_x, dyn_s, small, count,
        wg, asked, owned, dhg, dmg, smg, bk, xs, nz, w1f, w1t, w1n, w2t, w2h, heads, head_t, head_f,
        rowbuf, cols, headcol, acc_h, acc_w, acc_c, acc_a, acc_m, acc_l, grid, zr, zf, mg, mat,
        grow, xrow, dcols, dacc_h, dacc_w, dacc_o, dacc_m, dacc_b, dacc_l, xt, dmat, dpack, drow_g,
        drow_x, *rest,
    ) = refs
    rs_bufs = rest[: lay.bits]
    (
        s_w, r_w, s_q, r_q, s_p, r_p, s_dh, r_dh, s_dm, r_dm, s_sm, r_sm, s_bz, r_bz, s_bp, r_bp,
        s_rs, r_rs, s_zr, r_zr, s_za, r_za, s_pl, r_pl, s_mg, r_mg, s_ds, r_ds, s_dg, r_dg, s_dx,
        r_dx, s_sg, r_sg, s_sx, r_sx,
    ) = rest[lay.bits :]
    n_dp, n_blk, bits = lay.n_dp, lay.n_blk, lay.bits
    me = lax.axis_index("dp")
    z = lax.axis_index("blk")
    is_dyn = me < MEMBERS
    owner_k = (n_dp - 1 - me) // 2
    is_sac = jnp.logical_and(lax.rem(n_dp - 1 - me, 2) == 0, owner_k < 3)
    sac_k = jnp.minimum(owner_k, 2)
    dyn_e = jnp.minimum(me, MEMBERS - 1)

    def on_plane(src, dst, ssem, rsem, peer):
        return pltpu.make_async_remote_copy(
            src_ref=src, dst_ref=dst, send_sem=ssem, recv_sem=rsem,
            device_id={"dp": peer}, device_id_type=MESH,
        )

    def on_line(src, dst, ssem, rsem, peer):
        return pltpu.make_async_remote_copy(
            src_ref=src, dst_ref=dst, send_sem=ssem, recv_sem=rsem,
            device_id={"blk": peer}, device_id_type=MESH,
        )

    def plane_peers(body):
        @pl.loop(1, n_dp)
        def _(off):
            body(lax.rem(me + off, n_dp))

    def line_peers(body):
        @pl.loop(1, n_blk)
        def _(off):
            body(lax.rem(z + off, n_blk))

    barrier = pltpu.get_barrier_semaphore()
    plane_peers(lambda peer: pl.semaphore_signal(barrier, inc=1, device_id={"dp": peer}, device_id_type=MESH))
    line_peers(lambda peer: pl.semaphore_signal(barrier, inc=1, device_id={"blk": peer}, device_id_type=MESH))
    wg[z] = sac_h[...].astype(BF16)
    pl.semaphore_wait(barrier, n_dp - 1 + n_blk - 1)

    def hidden_copy(owner, part, peer):
        at = (2, 1) if part == 0 else (0, 2)
        view = wg.at[owner, pl.ds(*at)]
        return on_line(view, view, s_w.at[part, peer], r_w.at[part, owner], peer)

    line_peers(lambda peer: hidden_copy(z, 0, peer).start())

    def list_copy(owner, peer):
        return on_plane(requests, asked.at[owner], s_q.at[peer], r_q.at[owner], peer)

    def member_copy(owner, peer):
        return on_plane(member, owned.at[owner], s_p.at[peer], r_p.at[owner], peer)

    plane_peers(lambda peer: list_copy(me, peer).start())
    plane_peers(lambda peer: member_copy(me, peer).start())
    line_peers(lambda peer: hidden_copy(z, 1, peer).start())
    asked[me] = requests[...]
    owned[me] = member[...]

    def dyn_h_copy(owner, peer):
        return on_line(dyn_h.at[dyn_e], dhg.at[owner], s_dh.at[peer], r_dh.at[owner], peer)

    def dyn_m_copy(owner, peer):
        return on_line(dyn_m.at[dyn_e], dmg.at[owner], s_dm.at[peer], r_dm.at[owner], peer)

    def sac_m_copy(owner, peer):
        return on_line(sac_m.at[sac_k], smg.at[owner], s_sm.at[peer], r_sm.at[owner], peer)

    xs[42:56, :] = jnp.zeros((14, lay.batch), F32)
    xs[0:FEAT, lay.real : lay.batch] = model[...]
    xs[42:43, lay.real : lay.batch] = live[...].astype(F32)
    nz[...] = jnp.zeros_like(nz)
    for which in range(2):
        nz[which, 1:7, :] = noise[:, which, :]
    bias = biases
    firsts = [
        (targ_in[:, 0, :], targ_bias[0:1, 0:HSAC]),
        (targ_in[:, 1, :], targ_bias[1:2, 0:HSAC]),
        (crit_in[:, 0, :], bias[:, CB1 : CB1 + HSAC]),
        (crit_in[:, 1, :], bias[:, CB1 + HSAC : CB1 + 2 * HSAC]),
        (act_in[...], bias[:, AB1 : AB1 + HSAC]),
    ]
    w1f[...] = jnp.zeros_like(w1f)
    for net, (weights, offset) in enumerate(firsts):
        w1f[net, 0 : weights.shape[0], :] = rounded(weights)
        for at, piece in enumerate(pieces(offset)):
            w1f[net, IN + at : IN + at + 1, :] = piece.astype(F32)
        w1t[net] = (0.5 * w1f[net].T).astype(BF16)
    for k in range(2):
        w1n[k] = w1f[2 + k, 16:32, :].astype(BF16)
    for net in range(2):
        w2t[net] = (0.5 * rounded(targ_hidden[net])).T.astype(BF16)
    rowbuf[...] = jnp.zeros_like(rowbuf)
    rowbuf[0:1, :] = targ_bias[0:1, HSAC : 2 * HSAC]
    rowbuf[1:2, :] = targ_bias[1:2, HSAC : 2 * HSAC]
    rowbuf[2:3, :] = bias[:, CB2 : CB2 + HSAC]
    rowbuf[3:4, :] = bias[:, CB2 + HSAC : CB2 + 2 * HSAC]
    rowbuf[4:5, :] = bias[:, AB2 : AB2 + HSAC]
    rowbuf[5:7, :] = rounded(crit_out[...])
    cols[...] = 0.5 * rowbuf[...].T
    rowbuf[...] = jnp.zeros_like(rowbuf)
    rowbuf[0:1, 1:7] = bias[:, AB3 : AB3 + ACT]
    rowbuf[0:1, 9:15] = bias[:, AB3 + ACT : AB3 + 2 * ACT]
    headcol[...] = rowbuf[:, 0:128].T
    head_f[...] = jnp.zeros_like(head_f)
    for k in range(2):
        head_f[0:1, :] = targ_out[k : k + 1, :]
        heads[k] = head_f[...].astype(BF16)
        head_f[0:1, :] = crit_out[k : k + 1, :]
        heads[2 + k] = head_f[...].astype(BF16)
    head_f[0:1, :] = jnp.zeros((1, HSAC), F32)
    head_f[1:7, :] = act_out[0:ACT, :]
    head_f[9:15, :] = act_out[ACT : 2 * ACT, :]
    heads[4] = head_f[...].astype(BF16)
    head_t[...] = (0.5 * rounded(head_f[...])).T.astype(BF16)
    for ref in (acc_h, acc_w, acc_c, acc_a, acc_m, acc_l):
        ref[...] = jnp.zeros_like(ref)

    data = replay[...]
    sums = jnp.sum(data[0:24], axis=1, keepdims=True)
    squares = jnp.sum(data[0:24] * data[0:24], axis=1, keepdims=True)
    living = jnp.sum(live[...].astype(F32), axis=1, keepdims=True)

    def wait_lists(peer):
        list_copy(peer, peer).wait_recv()
        member_copy(peer, peer).wait_recv()

    plane_peers(wait_lists)
    spread = (
        lax.rem(lax.broadcasted_iota(jnp.int32, (CAP, lay.real), 1), CAP)
        == lax.broadcasted_iota(jnp.int32, (CAP, lay.real), 0)
    ).astype(F32)
    here = (
        lax.broadcasted_iota(jnp.int32, (n_dp, lay.real), 1) // CAP
        == lax.broadcasted_iota(jnp.int32, (n_dp, lay.real), 0)
    )

    def in_lanes(ref):
        lists = ref[:, me, :].astype(F32)
        wide = lax.dot_general(
            lists, spread, NN, precision=lax.Precision.HIGHEST, preferred_element_type=F32
        )
        return jnp.sum(jnp.where(here, wide, 0.0), axis=0, keepdims=True)

    slots = in_lanes(asked)
    wanted = jnp.maximum(slots, 0.0).astype(jnp.int32)
    hot = (rows_of((lay.replay, lay.real)) == wanted).astype(BF16)
    high, middle, low = pieces(data)
    picked = dot(high, hot) + dot(middle, hot) + dot(low, hot)
    mine = me * n_blk + z
    bk[mine, 0:FEAT, 0 : lay.real] = picked
    bk[mine, 42:43, 0 : lay.real] = (slots >= 0.0).astype(F32)
    bk[mine, 43:44, 0 : lay.real] = in_lanes(owned)
    bk[mine, 44:48, 0 : lay.real] = jnp.zeros((4, lay.real), F32)
    bk[mine, :, lay.real : lay.width] = jnp.zeros((48, lay.width - lay.real), F32)
    bk[mine, 0:24, lay.real : lay.real + 1] = sums
    bk[mine, 0:24, lay.real + 1 : lay.real + 2] = squares
    bk[mine, 24:25, lay.real : lay.real + 1] = living

    def block_line(owner, peer):
        view = bk.at[me * n_blk + owner]
        return on_line(view, view, s_bz.at[peer], r_bz.at[owner], peer)

    def block_plane(owner, peer):
        view = bk.at[pl.ds(owner * n_blk, n_blk)]
        return on_plane(view, view, s_bp.at[peer], r_bp.at[owner], peer)

    line_peers(lambda peer: block_line(z, peer).start())

    @pl.when(is_dyn)
    def _():
        line_peers(lambda peer: dyn_h_copy(z, peer).start())
        line_peers(lambda peer: dyn_m_copy(z, peer).start())

    @pl.when(is_sac)
    def _():
        line_peers(lambda peer: sac_m_copy(z, peer).start())

    def wait_hidden(peer):
        hidden_copy(peer, 0, peer).wait_recv()
        hidden_copy(peer, 1, peer).wait_recv()

    line_peers(wait_hidden)
    for k in range(3):
        for block in range(n_blk):
            w2h[k, block * lay.rows : (block + 1) * lay.rows, :] = (
                0.5 * wg[block, k].astype(F32)
            ).astype(BF16)
        w2t[2 + k] = w2h[k].astype(F32).T.astype(BF16)

    log_alpha = bias[:, LOGA : LOGA + 1]
    alpha = jnp.exp(log_alpha)
    last = [
        targ_bias[0:1, 2 * HSAC : 2 * HSAC + 1],
        targ_bias[1:2, 2 * HSAC : 2 * HSAC + 1],
        bias[:, CB3 : CB3 + 1],
        bias[:, CB3 + 1 : CB3 + 2],
    ]
    n_tiles = lay.batch // TILE

    @pl.loop(0, n_tiles)
    def _(step):
        @pl.when(step == 1)
        def _():
            line_peers(lambda peer: block_line(peer, peer).wait_recv())
            plane_peers(lambda peer: block_plane(me, peer).start())

        @pl.when(step == n_tiles - 1)
        def _():
            plane_peers(lambda peer: block_plane(peer, peer).wait_recv())
            lanes = lax.broadcasted_iota(jnp.int32, (48, lay.width), 1) // CAP

            def gather(owner, total):
                turned = pltpu.roll(
                    bk[owner * n_blk + z], lax.rem((owner - me) * CAP + lay.width, lay.width), axis=1
                )
                return jnp.where(lanes == owner, turned, total)

            own = lax.fori_loop(0, n_dp, gather, jnp.zeros((48, lay.width), F32))
            xs[0:48, 0 : lay.real] = own[:, 0 : lay.real]

        where = pl.ds(pl.multiple_of(lax.rem(step + 1, n_tiles) * TILE, TILE), TILE)
        row32 = rows_of((32, TILE))
        ones3 = jnp.logical_and(row32 >= IN, row32 < IN + 3).astype(F32)
        now_f = jnp.where(row32 < IN, xs[0:32, where], ones3)
        next_f = jnp.where(row32 < OBS, xs[24:56, where], ones3)
        now_in = now_f.astype(BF16)
        reward = xs[23:24, where]
        done = xs[41:42, where]
        weight = xs[42:43, where]
        row8 = rows_of((8, TILE))
        act_rows = jnp.logical_and(row8 >= 1, row8 < 1 + ACT)
        row16 = rows_of((16, TILE))
        ones16 = jnp.ones((16, TILE), BF16)

        def hidden(inputs, net):
            first, slope1 = gate(dot(w1t[net], inputs))
            first = first.astype(BF16)
            second, slope2 = gate(dot(w2t[net], first) + cols[:, net : net + 1])
            return first, slope1, second.astype(BF16), slope2

        def policy(inputs, which):
            first, slope1, second, slope2 = hidden(inputs, 4)
            out = dot(heads[4], second) + headcol[0:16, 0:1]
            bent = jnp.tanh(out[8:16])
            log_scale = -5.0 + 3.5 * (bent + 1.0)
            draw = nz[which, :, where]
            moved = jnp.exp(log_scale) * draw
            latent = out[0:8] + moved
            terms = (
                -0.5 * draw * draw
                - log_scale
                - 0.9189385
                - 2.0 * (0.6931472 - latent - softplus(-2.0 * latent))
            )
            log_prob = jnp.sum(jnp.where(act_rows, terms, 0.0), axis=0, keepdims=True)
            action = jnp.where(act_rows, jnp.tanh(latent), 0.0)
            return action, log_prob, bent, moved, (first, slope1, second, slope2)

        def with_action(inputs, action):
            middle_rows = jnp.where(act_rows, action, inputs[16:24])
            return jnp.concatenate([inputs[0:16], middle_rows, inputs[24:32]], 0).astype(BF16)

        def critic(inputs, net):
            kept = hidden(inputs, net)
            value = dot(heads[net], kept[2])[0:1] + last[net]
            return value, kept

        def add_hidden(k, first, grad):
            acc_h[k] += dot(jnp.concatenate([first, ones16], 0), grad, NT)

        next_action, next_prob, _, _, _ = policy(next_f.astype(BF16), 1)
        aim_in = with_action(next_f, next_action)
        aim = jnp.minimum(critic(aim_in, 0)[0], critic(aim_in, 1)[0])
        target = reward + DISCOUNT * (1.0 - done) * (aim - alpha * next_prob)
        action, log_prob, bent, moved, (a1, da1, a2, da2) = policy(now_in, 0)
        judged_in = with_action(now_f, action)
        loss = alpha * log_prob - log_alpha * (log_prob + TARGET_ENTROPY)
        grad_action = jnp.zeros((8, TILE), F32)
        heads_grad = []
        for k in range(2):
            value, (c1, dc1, c2, dc2) = critic(now_in, 2 + k)
            miss = value - target
            loss += 0.5 * miss * miss
            g3 = rounded(weight * miss)
            g3_rows = jnp.where(row16 == 0, g3, 0.0).astype(BF16)
            heads_grad.append(g3_rows)
            acc_c[k] += dot(g3_rows, c2, NT)
            g2 = ((cols[:, 5 + k : 6 + k] * g3) * dc2).astype(BF16)
            add_hidden(k, c1, g2)
            g1 = (dot(w2h[k], g2) * dc1).astype(BF16)
            acc_w[k] += dot(now_in, g1, NT)
            judged, (_, df1, _, df2) = critic(judged_in, 2 + k)
            loss -= 0.5 * judged
            g2 = ((cols[:, 5 + k : 6 + k] * (-0.5 * weight)) * df2).astype(BF16)
            g1 = (dot(w2h[k], g2) * df1).astype(BF16)
            grad_action += dot(w1n[k], g1)[0:8]
        grad_latent = 2.0 * alpha * weight * action + grad_action * (1.0 - action * action)
        grad_scale = grad_latent * moved - alpha * weight
        grad_bent = grad_scale * 3.5 * (1.0 - bent * bent)
        g3 = jnp.concatenate(
            [jnp.where(act_rows, grad_latent, 0.0), jnp.where(act_rows, grad_bent, 0.0)], 0
        ).astype(BF16)
        acc_a[...] += dot(g3, a2, NT)
        acc_m[...] += dot(ones16, jnp.concatenate([g3] + heads_grad, 0), NT)
        g2 = (dot(head_t[...], g3) * da2).astype(BF16)
        add_hidden(2, a1, g2)
        g1 = (dot(w2h[2], g2) * da1).astype(BF16)
        acc_w[2] += dot(now_in, g1, NT)
        acc_l[0:1, :] += weight * loss
        acc_l[1:2, :] += weight * (log_prob + TARGET_ENTROPY)

    for k in range(3):
        for chunk in range(n_dp):
            tile = chunk * lay.mat
            side, row = tile // 32, tile % 32
            grid[chunk, k * lay.mat : (k + 1) * lay.mat] = acc_h[
                k, row * 8 : (row + lay.mat) * 8, side * 128 : (side + 1) * 128
            ].reshape(lay.mat, 8, 128)

    def put(row, value):
        for at in range(value.shape[0] // 8):
            for side in range(value.shape[1] // 128):
                tile = side * (R_SMALL // 8) + row // 8 + at
                grid[tile // lay.sml, 3 * lay.mat + tile % lay.sml] = value[
                    at * 8 : at * 8 + 8, side * 128 : (side + 1) * 128
                ]

    for k in range(3):
        put(R_IN + 24 * k, acc_w[k, 0:24, :])
    put(R_HEAD, acc_a[...])
    rowbuf[0:1, :] = acc_c[0, 0:1, :]
    rowbuf[1:2, :] = acc_c[1, 0:1, :]
    for k in range(3):
        rowbuf[2 + k : 3 + k, :] = acc_h[k, HSAC : HSAC + 1, :]
    put(R_OUT, rowbuf[...])
    folded = jnp.sum(acc_l[...], axis=1, keepdims=True)
    rowbuf[...] = jnp.zeros_like(rowbuf)
    rowbuf[0:1, 0:48] = acc_m[0:1, :]
    rowbuf[0:1, 64:65] = folded[0:1]
    rowbuf[0:1, 65:66] = folded[1:2]
    put(R_MISC, rowbuf[...])
    put(R_MISC + 8, jnp.zeros((R_SMALL - R_MISC - 8, HSAC), F32))

    core = lax.rem(me, 2)

    def bit(b):
        return lax.rem(me // (1 << b), 2)

    starts, faces, partners = [], [], []
    start = 0
    for s in range(bits):
        if s == 0:
            face, stride = core, 1
        else:
            face = (1 - core) * bit(s) + core * bit(bits - s)
            stride = (1 - core) * (1 << s) + core * (1 << (bits - s))
        starts.append(start)
        faces.append(face)
        partners.append(me + (1 - 2 * face) * stride)
        start = start + face * (n_dp >> (s + 1))
    place = start

    def fold_copy(s):
        half = n_dp >> (s + 1)
        begin = starts[s] + (1 - faces[s]) * half
        return on_plane(grid.at[pl.ds(begin, half)], rs_bufs[s], s_rs.at[s], r_rs.at[s], partners[s])

    def fold_wait(s):
        half = n_dp >> (s + 1)
        begin = starts[s] + faces[s] * half
        fold_copy(s).wait_recv()
        for at in range(half):
            grid[begin + at] += rs_bufs[s][at]

    fold_copy(0).start()

    lane0 = lay.real // 128 * 128

    def add_block(at, carry):
        sides, fills = carry
        return sides + bk[at, 0:32, lane0 : lane0 + 128], fills + bk[at, 40:48, 0 : lay.real]

    sides, fills = lax.fori_loop(
        0, lay.n_dev, add_block, (jnp.zeros((32, 128), F32), jnp.zeros((8, lay.real), F32))
    )
    at = lay.real - lane0
    rows_all = float(lay.replay * lay.n_dev)
    centre = sides[0:24, at : at + 1] / rows_all
    scale = lax.rsqrt(sides[0:24, at + 1 : at + 2] / rows_all - centre * centre + 1e-6)
    total = sides[24:25, at : at + 1] + jnp.sum(fills[2:3, :], axis=1, keepdims=True)
    count[...] = jnp.broadcast_to(total, (8, 128))

    def dyn_bias(start, width):
        row = jnp.zeros((1, width), F32)
        for e in range(MEMBERS):
            row = jnp.where(me == e, bias[:, start + width * e : start + width * (e + 1)], row)
        return row

    @pl.when(is_dyn)
    def _():
        w1f[0] = jnp.zeros((32, HSAC), F32)
        w1f[0, 0:IN, 0:HDYN] = rounded(dyn_in[dyn_e])
        for at, piece in enumerate(pieces(dyn_bias(DB1, HDYN))):
            w1f[0, IN + at : IN + at + 1, 0:HDYN] = piece.astype(F32)
        w1t[0] = (0.5 * w1f[0].T).astype(BF16)
        rowbuf[...] = jnp.zeros_like(rowbuf)
        rowbuf[0:1, 0:HDYN] = dyn_bias(DB2, HDYN)
        head_row = dyn_bias(DB3, DOUT)
        rowbuf[1:2, 0:HALF] = head_row[:, 0:HALF]
        rowbuf[1:2, 24 : 24 + HALF] = head_row[:, HALF:DOUT]
        rowbuf[2:3, 0:HALF] = bias[:, MAXLV : MAXLV + HALF]
        rowbuf[3:4, 0:HALF] = bias[:, MINLV : MINLV + HALF]
        dcols[...] = rowbuf[...].T
        dpack[...] = jnp.zeros_like(dpack)
        dpack[0:HALF, 0:HDYN] = dyn_out[dyn_e, 0:HALF, :]
        dpack[24 : 24 + HALF, 0:HDYN] = dyn_out[dyn_e, HALF:DOUT, :]
        head = dpack[0:48, :].astype(BF16)
        head_back = (0.5 * rounded(dpack[0:48, :])).T.astype(BF16)
        dpack[...] = jnp.zeros_like(dpack)

        def wait_dyn(peer):
            dyn_h_copy(peer, peer).wait_recv()
            dyn_m_copy(peer, peer).wait_recv()

        line_peers(wait_dyn)
        dhg[z] = dyn_h[dyn_e]
        dmg[z] = dyn_m[dyn_e]
        dmat[...] = jnp.zeros_like(dmat)
        for block in range(n_blk):
            dmat[block * lay.drows : (block + 1) * lay.drows, 0:HDYN] = 0.5 * rounded(dhg[block])
        w2h[0] = dmat[...].astype(BF16)
        w2t[0] = dmat[...].T.astype(BF16)
        for ref in (dacc_h, dacc_w, dacc_o, dacc_m, dacc_b, dacc_l):
            ref[...] = jnp.zeros_like(ref)
        per = TILE // lay.real

        @pl.loop(0, lay.n_dev // per)
        def _(tile):
            for at in range(per):
                xt[:, at * lay.real : (at + 1) * lay.real] = bk[tile * per + at, :, 0 : lay.real]
            now = xt[0:24, :]
            later = xt[24:48, :]
            row24 = rows_of((24, TILE))
            scaled = jnp.where(row24 < IN, (now - centre) * scale, 1.0)
            inputs = jnp.concatenate([scaled, (rows_of((8, TILE)) < 2).astype(F32)], 0).astype(BF16)
            ones16 = jnp.ones((16, TILE), BF16)
            first, slope1 = gate(dot(w1t[0], inputs))
            first = first.astype(BF16)
            second, slope2 = gate(dot(w2t[0], first) + 0.5 * dcols[:, 0:1])
            second = second.astype(BF16)
            out = dot(head, second) + dcols[0:48, 1:2]
            used = row24 < HALF
            upper = dcols[0:24, 2:3]
            lower = dcols[0:24, 3:4]
            gap1 = upper - out[24:48]
            gap2 = upper - softplus(gap1) - lower
            log_var = lower + softplus(gap2)
            error = out[0:24] - jnp.where(row24 == OBS, now[23:24], later - now)
            inverse = jnp.exp(-log_var)
            weight = xt[42:43, :] * (xt[43:44, :] == me.astype(F32)).astype(F32)
            spread_term = error * error * inverse
            nll = jnp.sum(jnp.where(used, spread_term + log_var, 0.0), axis=0, keepdims=True)
            dacc_l[0:1, :] += weight * nll
            grad_mu = 2.0 * weight * error * inverse
            grad_lv = weight * (1.0 - spread_term)
            open1 = sigmoid(gap1)
            open2 = sigmoid(gap2)
            grad_lv1 = grad_lv * open2
            dacc_b[0] += jnp.where(used, grad_lv1 * (1.0 - open1), 0.0)
            dacc_b[1] += jnp.where(used, grad_lv * (1.0 - open2), 0.0)
            g3 = jnp.concatenate(
                [jnp.where(used, grad_mu, 0.0), jnp.where(used, grad_lv1 * open1, 0.0)], 0
            ).astype(BF16)
            dacc_o[...] += dot(g3, second, NT)
            dacc_m[...] += dot(ones16, g3, NT)
            g2 = (dot(head_back, g3) * slope2).astype(BF16)
            dacc_h[...] += dot(jnp.concatenate([first, ones16], 0), g2, NT)
            g1 = (dot(w2h[0], g2) * slope1).astype(BF16)
            dacc_w[...] += dot(inputs, g1, NT)

        dpack[D_IN : D_IN + 24, :] = dacc_w[0:24, :]
        dpack[D_OUT : D_OUT + HALF, :] = dacc_o[0:HALF, :]
        dpack[D_OUT + HALF : D_OUT + DOUT, :] = dacc_o[24 : 24 + HALF, :]
        dpack[D_B2 : D_B2 + 1, :] = dacc_h[HSAC : HSAC + 1, :]
        dpack[D_B3 : D_B3 + 1, 0:48] = dacc_m[0:1, :]
        lanes = lax.broadcasted_iota(jnp.int32, (24, 128), 1)
        bound = jnp.where(
            lanes == 0,
            jnp.sum(dacc_b[0], axis=1, keepdims=True),
            jnp.where(lanes == 1, jnp.sum(dacc_b[1], axis=1, keepdims=True), 0.0),
        )
        dpack[D_UP : D_UP + 2, 0:24] = bound.T[0:2, :]
        dpack[D_LOSS : D_LOSS + 1, 0:128] = jnp.broadcast_to(
            jnp.sum(dacc_l[0:1, :], axis=1, keepdims=True), (1, 128)
        )
        dyn_s[dyn_e] = dpack[...]

    def pack_copy(owner, peer):
        at = dyn_s.at[jnp.minimum(owner, MEMBERS - 1)]
        return on_plane(dpack, at, s_ds.at[peer], r_ds.at[owner], peer)

    def dyn_g_copy(owner, peer):
        at = dyn_g.at[jnp.minimum(owner, MEMBERS - 1)]
        return on_plane(drow_g, at, s_dg.at[peer], r_dg.at[owner], peer)

    def dyn_x_copy(owner, peer):
        at = dyn_x.at[jnp.minimum(owner, MEMBERS - 1)]
        return on_plane(drow_x, at, s_dx.at[peer], r_dx.at[owner], peer)

    def line_rows(ref):
        rows = ref[0 : lay.drows, 0:HDYN]
        for block in range(1, n_blk):
            rows = jnp.where(z == block, ref[block * lay.drows : (block + 1) * lay.drows, 0:HDYN], rows)
        return rows

    fold_wait(0)
    if bits > 1:
        fold_copy(1).start()

    @pl.when(is_dyn)
    def _():
        plane_peers(lambda peer: pack_copy(me, peer).start())
        rows = line_rows(dacc_h)
        drow_g[...] = rows
        dyn_g[dyn_e] = rows
        plane_peers(lambda peer: dyn_g_copy(me, peer).start())
        dmat[...] = jnp.zeros_like(dmat)
        for block in range(n_blk):
            at = slice(block * lay.drows, (block + 1) * lay.drows)
            dmat[at, 0:HDYN] = MOMENTUM * dmg[block] + dacc_h[at, 0:HDYN] / total
        moment = dmat[...]
        norm = jnp.sqrt(jnp.sum(jnp.sum(moment * moment, axis=1, keepdims=True), axis=0, keepdims=True))
        dmat[...] = moment / (norm + 1e-7)
        schulz(dmat, 2)

    for s in range(1, bits):
        fold_wait(s)
        if s + 1 < bits:
            fold_copy(s + 1).start()

    def line_first(owner, peer):
        if lay.split_z:
            src = grid.at[place, pl.ds(peer * lay.part, lay.part)]
        else:
            src = grid.at[place]
        return on_line(src, zr.at[owner], s_zr.at[peer], r_zr.at[owner], peer)

    def line_second(owner, peer):
        view = zf.at[pl.ds(owner * lay.part, lay.part)]
        return on_line(view, view, s_za.at[peer], r_za.at[owner], peer)

    line_peers(lambda peer: line_first(z, peer).start())

    @pl.when(is_dyn)
    def _():
        schulz(dmat, NS_ITERS - 2)
        rows = line_rows(dmat)
        drow_x[...] = rows
        dyn_x[dyn_e] = rows
        plane_peers(lambda peer: dyn_x_copy(me, peer).start())

    line_peers(lambda peer: line_first(peer, peer).wait_recv())
    if lay.split_z:
        zr[z] = grid[place, pl.ds(z * lay.part, lay.part)]
    else:
        zr[z] = grid[place]
    whole = zr[0]
    for block in range(1, n_blk):
        whole = whole + zr[block]
    if lay.split_z:
        zf[pl.ds(z * lay.part, lay.part)] = whole
        line_peers(lambda peer: line_second(z, peer).start())
        line_peers(lambda peer: line_second(peer, peer).wait_recv())
    else:
        zf[...] = whole

    def tile_copy(k, owner):
        return on_plane(zf.at[pl.ds(k * lay.mat, lay.mat)], mg.at[place], s_mg.at[k], r_mg.at[place], owner)

    for k in range(3):
        @pl.when(me != lay.owners[k])
        def _():
            tile_copy(k, lay.owners[k]).start()

    def small_copy(at, peer):
        return on_plane(
            zf.at[pl.ds(3 * lay.mat, lay.sml)], small.at[pl.ds(at * lay.sml, lay.sml)],
            s_pl.at[peer], r_pl.at[at], peer,
        )

    plane_peers(lambda peer: small_copy(place, peer).start())
    small[pl.ds(place * lay.sml, lay.sml)] = zf[3 * lay.mat :]

    def sac_g_copy(k, peer):
        src = grow.at[pl.ds(pl.multiple_of(z * lay.rows, lay.rows), lay.rows)]
        return on_plane(src, sac_g.at[k], s_sg.at[peer], r_sg.at[k], peer)

    def sac_x_copy(k, peer):
        src = mat.at[pl.ds(pl.multiple_of(z * lay.rows, lay.rows), lay.rows)]
        return on_plane(src, sac_x.at[k], s_sx.at[peer], r_sx.at[k], peer)

    mine_rows = pl.ds(pl.multiple_of(z * lay.rows, lay.rows), lay.rows)

    @pl.when(is_sac)
    def _():
        line_peers(lambda peer: sac_m_copy(peer, peer).wait_recv())
        smg[z] = sac_m[sac_k]
        mg[place] = zf[pl.ds(sac_k * lay.mat, lay.mat)]

        @pl.loop(1, n_dp)
        def _(off):
            at = lax.rem(place + off, n_dp)
            on_plane(mg.at[at], mg.at[at], s_mg.at[0], r_mg.at[at], me).wait_recv()

        for chunk in range(n_dp):
            tile = chunk * lay.mat
            side, row = tile // 32, tile % 32
            grow[row * 8 : (row + lay.mat) * 8, side * 128 : (side + 1) * 128] = mg[chunk].reshape(
                lay.mat * 8, 128
            )
        sac_g[sac_k] = grow[mine_rows, :]
        plane_peers(lambda peer: sac_g_copy(sac_k, peer).start())
        for block in range(n_blk):
            at = slice(block * lay.rows, (block + 1) * lay.rows)
            mat[at, :] = MOMENTUM * smg[block] + grow[at, :] / total
        moment = mat[...]
        norm = jnp.sqrt(jnp.sum(jnp.sum(moment * moment, axis=1, keepdims=True), axis=0, keepdims=True))
        mat[...] = moment / (norm + 1e-7)
        schulz(mat, NS_ITERS)
        sac_x[sac_k] = mat[mine_rows, :]
        plane_peers(lambda peer: sac_x_copy(sac_k, peer).start())

    @pl.loop(1, n_dp)
    def _(off):
        small_copy(lax.rem(place + off, n_dp), me).wait_recv()

    def from_members(peer):
        @pl.when(peer < MEMBERS)
        def _():
            pack_copy(peer, peer).wait_recv()
            dyn_g_copy(peer, peer).wait_recv()
            dyn_x_copy(peer, peer).wait_recv()

    plane_peers(from_members)
    for k in range(3):
        @pl.when(me != lay.owners[k])
        def _():
            sac_g_copy(k, me).wait_recv()
            sac_x_copy(k, me).wait_recv()

    def sent_on_line(peer):
        hidden_copy(z, 0, peer).wait_send()
        hidden_copy(z, 1, peer).wait_send()
        block_line(z, peer).wait_send()
        line_first(z, peer).wait_send()
        if lay.split_z:
            line_second(z, peer).wait_send()

        @pl.when(is_dyn)
        def _():
            dyn_h_copy(z, peer).wait_send()
            dyn_m_copy(z, peer).wait_send()

        @pl.when(is_sac)
        def _():
            sac_m_copy(z, peer).wait_send()

    line_peers(sent_on_line)

    def sent_on_plane(peer):
        list_copy(me, peer).wait_send()
        member_copy(me, peer).wait_send()
        block_plane(me, peer).wait_send()
        small_copy(place, peer).wait_send()

        @pl.when(is_dyn)
        def _():
            pack_copy(me, peer).wait_send()
            dyn_g_copy(me, peer).wait_send()
            dyn_x_copy(me, peer).wait_send()

        @pl.when(is_sac)
        def _():
            sac_g_copy(sac_k, peer).wait_send()
            sac_x_copy(sac_k, peer).wait_send()

    plane_peers(sent_on_plane)
    for s in range(bits):
        fold_copy(s).wait_send()
    for k in range(3):
        @pl.when(me != lay.owners[k])
        def _():
            tile_copy(k, lay.owners[k]).wait_send()


def adamw(weights, first, second, gradient):
    first = BETA_FIRST * first + (1.0 - BETA_FIRST) * gradient
    second = BETA_SECOND * second + (1.0 - BETA_SECOND) * gradient * gradient
    first_hat = first / (1.0 - BETA_FIRST**STEP)
    second_hat = second / (1.0 - BETA_SECOND**STEP)
    step = first_hat / (jnp.sqrt(second_hat) + 1e-8) + ADAM_DECAY * weights
    return weights - ADAM_RATE * step, first, second


def update_kernel(*refs):
    (
        sac_g, sac_x, dyn_g, dyn_x, dyn_s, small, count, sac_h, sac_m, dyn_h, dyn_m,
        ci, ci_m, ci_v, ai, ai_m, ai_v, di, di_m, di_v, co, co_m, co_v, ao, ao_m, ao_v,
        do, do_m, do_v, bi, bi_m, bi_v,
        sac_new, sac_mom, dyn_new, dyn_mom, ci_n, ci_mn, ci_vn, ai_n, ai_mn, ai_vn, di_n, di_mn,
        di_vn, co_n, co_mn, co_vn, ao_n, ao_mn, ao_vn, do_n, do_mn, do_vn, bi_n, bi_mn, bi_vn,
        loss, counted, bg,
    ) = refs
    total = count[0:1, 0:1]
    sac_mom[...] = MOMENTUM * sac_m[...] + sac_g[...] / total.reshape(1, 1, 1)
    sac_new[...] = sac_h[...] * (1.0 - MUON_RATE * MUON_DECAY) - MUON_RATE * sac_x[...]
    dyn_mom[...] = MOMENTUM * dyn_m[...] + dyn_g[...] / total.reshape(1, 1, 1)
    dyn_new[...] = dyn_h[...] * (1.0 - MUON_RATE * MUON_DECAY) - MUON_RATE * dyn_x[...]

    def rows(row, number):
        sides = []
        for side in range(2):
            at = side * (R_SMALL // 8) + row // 8
            sides.append(small[at : at + -(-number // 8)].reshape(-1, 128))
        return jnp.concatenate(sides, 1)

    def store(outs, at, values):
        for out, value in zip(outs, values):
            out[at] = value

    outs = (ci_n, ci_mn, ci_vn)
    for k in range(2):
        at = (slice(None), k, slice(None))
        grad = rows(R_IN + 24 * k, 24)
        bg[:, CB1 + HSAC * k : CB1 + HSAC * (k + 1)] = grad[IN : IN + 1]
        store(outs, at, adamw(ci[at], ci_m[at], ci_v[at], grad[0:IN] / total))
    grad = rows(R_IN + 48, 24)
    bg[:, AB1 : AB1 + HSAC] = grad[IN : IN + 1]
    store((ai_n, ai_mn, ai_vn), ..., adamw(ai[...], ai_m[...], ai_v[...], grad[0:OBS] / total))
    grad = rows(R_HEAD, 16)
    for at, row in ((slice(0, ACT), slice(1, 1 + ACT)), (slice(ACT, 2 * ACT), slice(9, 9 + ACT))):
        store((ao_n, ao_mn, ao_vn), at, adamw(ao[at], ao_m[at], ao_v[at], grad[row] / total))
    grad = rows(R_OUT, 8)
    store((co_n, co_mn, co_vn), ..., adamw(co[...], co_m[...], co_v[...], grad[0:2] / total))
    bg[:, CB2 : CB2 + HSAC] = grad[2:3]
    bg[:, CB2 + HSAC : CB2 + 2 * HSAC] = grad[3:4]
    bg[:, AB2 : AB2 + HSAC] = grad[4:5]
    grad = rows(R_MISC, 8)
    bg[:, CB3 : CB3 + 1] = grad[0:1, 16:17]
    bg[:, CB3 + 1 : CB3 + 2] = grad[0:1, 32:33]
    bg[:, AB3 : AB3 + ACT] = grad[0:1, 1 : 1 + ACT]
    bg[:, AB3 + ACT : AB3 + 2 * ACT] = grad[0:1, 9 : 9 + ACT]
    bg[:, LOGA : LOGA + 1] = -grad[0:1, 65:66]
    total_loss = grad[0:1, 64:65]
    up = jnp.zeros((1, HALF), F32)
    low = jnp.zeros((1, HALF), F32)
    for e in range(MEMBERS):
        pack = dyn_s[e]
        total_loss = total_loss + pack[D_LOSS : D_LOSS + 1, 0:1]
        up = up + pack[D_UP : D_UP + 1, 0:HALF]
        low = low + pack[D_LOW : D_LOW + 1, 0:HALF]
        bg[:, DB1 + HDYN * e : DB1 + HDYN * (e + 1)] = pack[IN : IN + 1, 0:HDYN]
        bg[:, DB2 + HDYN * e : DB2 + HDYN * (e + 1)] = pack[D_B2 : D_B2 + 1, 0:HDYN]
        bg[:, DB3 + DOUT * e : DB3 + DOUT * e + HALF] = pack[D_B3 : D_B3 + 1, 0:HALF]
        bg[:, DB3 + DOUT * e + HALF : DB3 + DOUT * (e + 1)] = pack[D_B3 : D_B3 + 1, 24 : 24 + HALF]
        grad = pack[0:IN, 0:HDYN] / total
        store((di_n, di_mn, di_vn), e, adamw(di[e], di_m[e], di_v[e], grad))
        grad = pack[D_OUT : D_OUT + DOUT, 0:HDYN] / total
        store((do_n, do_mn, do_vn), e, adamw(do[e], do_m[e], do_v[e], grad))
    bg[:, MAXLV : MAXLV + HALF] = up
    bg[:, MINLV : MINLV + HALF] = low
    lane = lax.broadcasted_iota(jnp.int32, (1, NB), 1)
    bounds = jnp.where(
        jnp.logical_and(lane >= MAXLV, lane < MINLV),
        BOUND_WEIGHT,
        jnp.where(jnp.logical_and(lane >= MINLV, lane < LOGA), -BOUND_WEIGHT, 0.0),
    )
    grad = bg[...] / total + bounds
    store((bi_n, bi_mn, bi_vn), ..., adamw(bi[...], bi_m[...], bi_v[...], grad))
    loss[...] = total_loss
    counted[...] = total


def shards(
    lay, replay, model_rows, requests, member_of, model_live, noise, sac_hidden, sac_hidden_mom,
    dyn_hidden, dyn_hidden_mom, crit_in, crit_in_m, crit_in_v, act_in, act_in_m, act_in_v, dyn_in,
    dyn_in_m, dyn_in_v, crit_out, crit_out_m, crit_out_v, act_out, act_out_m, act_out_v, dyn_out,
    dyn_out_m, dyn_out_v, biases, biases_m, biases_v, targ_in, targ_hidden, targ_out, targ_bias,
):
    n_dp, n_blk, bits = lay.n_dp, lay.n_blk, lay.bits
    spec = pl.BlockSpec(memory_space=pltpu.VMEM)

    def flip(value):
        return jnp.transpose(value, (1, 0, 2))

    def swap(value):
        return jnp.swapaxes(value, -1, -2)

    def row(value):
        return value.reshape(1, -1)

    inputs = (
        replay, model_rows, requests, member_of, row(model_live), jnp.transpose(noise, (2, 0, 1)),
        sac_hidden, sac_hidden_mom, dyn_hidden, dyn_hidden_mom, flip(crit_in), act_in, dyn_in,
        crit_out, swap(act_out), swap(dyn_out), row(biases), flip(targ_in), targ_hidden, targ_out,
        targ_bias,
    )
    shape = jax.ShapeDtypeStruct
    rows, drows = lay.rows, lay.drows
    out_shape = (
        shape((3, rows, HSAC), F32),
        shape((3, rows, HSAC), F32),
        shape((MEMBERS, drows, HDYN), F32),
        shape((MEMBERS, drows, HDYN), F32),
        shape((MEMBERS, D_ROWS, HSAC), F32),
        shape((32, 8, 128), F32),
        shape((8, 128), F32),
    )

    def vm(*dims, kind=F32):
        return pltpu.VMEM(dims, kind)

    def sems(*dims):
        return [pltpu.SemaphoreType.DMA(dims), pltpu.SemaphoreType.DMA(dims)]

    scratch = [
        vm(n_blk, 3, rows, HSAC, kind=BF16),
        vm(n_dp, n_dp, CAP, kind=jnp.int32),
        vm(n_dp, n_dp, CAP, kind=jnp.int32),
        vm(n_blk, drows, HDYN),
        vm(n_blk, drows, HDYN),
        vm(n_blk, rows, HSAC),
        vm(lay.n_dev, 48, lay.width),
        vm(56, lay.batch),
        vm(2, 8, lay.batch),
        vm(5, 32, HSAC),
        vm(5, HSAC, 32, kind=BF16),
        vm(2, 16, HSAC, kind=BF16),
        vm(5, HSAC, HSAC, kind=BF16),
        vm(3, HSAC, HSAC, kind=BF16),
        vm(5, 16, HSAC, kind=BF16),
        vm(HSAC, 16, kind=BF16),
        vm(16, HSAC),
        vm(8, HSAC),
        vm(HSAC, 8),
        vm(128, 8),
        vm(3, HSAC + 16, HSAC),
        vm(3, 32, HSAC),
        vm(2, 16, HSAC),
        vm(16, HSAC),
        vm(16, 48),
        vm(8, TILE),
        vm(n_dp, lay.chunk, 8, 128),
        vm(n_blk, lay.part, 8, 128),
        vm(lay.chunk, 8, 128),
        vm(n_dp, lay.mat, 8, 128),
        vm(HSAC, HSAC),
        vm(HSAC, HSAC),
        vm(8, 128),
        vm(HSAC, 8),
        vm(HSAC + 16, HSAC),
        vm(32, HSAC),
        vm(48, HSAC),
        vm(16, 48),
        vm(2, 24, TILE),
        vm(8, TILE),
        vm(48, TILE),
        vm(HSAC, HSAC),
        vm(D_ROWS, HSAC),
        vm(drows, HDYN),
        vm(drows, HDYN),
    ]
    scratch += [vm(n_dp >> (s + 1), lay.chunk, 8, 128) for s in range(bits)]
    scratch += sems(2, n_blk)
    scratch += sems(n_dp) + sems(n_dp)
    scratch += sems(n_blk) + sems(n_blk) + sems(n_blk)
    scratch += sems(n_blk) + sems(n_dp)
    scratch += sems(bits) + sems(n_blk) + sems(n_blk) + sems(n_dp)
    scratch += [pltpu.SemaphoreType.DMA((3,)), pltpu.SemaphoreType.DMA((n_dp,))]
    scratch += sems(n_dp) + sems(n_dp) + sems(n_dp)
    scratch += 2 * [pltpu.SemaphoreType.DMA((n_dp,)), pltpu.SemaphoreType.DMA((3,))]
    gathered = pl.pallas_call(
        functools.partial(main_kernel, lay),
        out_shape=out_shape,
        in_specs=[spec] * len(inputs),
        out_specs=[spec] * len(out_shape),
        scratch_shapes=scratch,
        compiler_params=pltpu.CompilerParams(
            collective_id=0, has_side_effects=True, vmem_limit_bytes=60 * 2**20
        ),
        name="step",
    )(*inputs)
    params = (
        sac_hidden, sac_hidden_mom, dyn_hidden, dyn_hidden_mom,
        flip(crit_in), flip(crit_in_m), flip(crit_in_v), act_in, act_in_m, act_in_v,
        dyn_in, dyn_in_m, dyn_in_v, crit_out, crit_out_m, crit_out_v,
        swap(act_out), swap(act_out_m), swap(act_out_v),
        swap(dyn_out), swap(dyn_out_m), swap(dyn_out_v), row(biases), row(biases_m), row(biases_v),
    )
    new_shape = [shape(params[i].shape, F32) for i in (0, 1, 2, 3)]
    new_shape += [shape(params[i].shape, F32) for i in range(4, 25)]
    new_shape += [shape((1, 1), F32)] * 2
    out = pl.pallas_call(
        update_kernel,
        out_shape=tuple(new_shape),
        in_specs=[spec] * (len(gathered) + len(params)),
        out_specs=[spec] * len(new_shape),
        scratch_shapes=[vm(1, NB)],
        compiler_params=pltpu.CompilerParams(vmem_limit_bytes=40 * 2**20),
        name="update",
    )(*gathered, *params)
    out = list(out)
    for at in (4, 5, 6):
        out[at] = flip(out[at])
    for at in (16, 17, 18, 19, 20, 21):
        out[at] = swap(out[at])
    for at in (22, 23, 24):
        out[at] = out[at].reshape(-1)
    for at in (25, 26):
        out[at] = out[at].reshape(())
    return tuple(out)


def solution(mesh):
    both = ("dp", "blk")
    sharded = (
        P(None, both), P(None, both), P(both, None), P(both, None), P(both), P(None, both, None),
    )
    hidden = (P(None, "blk", None),) * 4

    def step(replay, model_rows, *others):
        lay = Layout(mesh, replay.shape[1], model_rows.shape[1])
        return shards(lay, replay, model_rows, *others)

    return jax.shard_map(
        step,
        mesh=mesh,
        in_specs=sharded + hidden + (P(),) * 25,
        out_specs=hidden + (P(),) * 23,
        check_vma=False,
    )
```

```python
import functools
import math

import jax
import jax.numpy as jnp
from jax import lax
from jax.experimental import pallas as pl
from jax.experimental.pallas import tpu as pltpu
from jax.sharding import PartitionSpec as P

OBS = 17
ACT = 6
IN = OBS + ACT
FEAT = 42
HDYN = 200
HSAC = 256
MEMBERS = 7
DOUT = 36
HALF = DOUT // 2
NB = 4639
NS_ITERS = 5
STEP = 10
CAP = 8
TILE = 256

DISCOUNT = 0.99
TARGET_ENTROPY = -6.0
BOUND_WEIGHT = 0.01
MOMENTUM = 0.95
MUON_RATE = 0.4
MUON_DECAY = 0.01
ADAM_RATE = 0.1
ADAM_DECAY = 0.01
BETA_FIRST = 0.9
BETA_SECOND = 0.999
COEF_LINEAR = 3.4445
COEF_CUBIC = -4.775
COEF_QUINTIC = 2.0315

CB1, CB2, CB3, AB1, AB2, AB3 = 0, 512, 1024, 1026, 1282, 1538
DB1, DB2, DB3, MAXLV, MINLV, LOGA = 1550, 2950, 4350, 4602, 4620, 4638

R_IN, R_HEAD, R_OUT, R_MISC, R_SMALL = 0, 72, 88, 96, 128
D_IN, D_OUT, D_B2, D_B3, D_UP, D_LOW, D_LOSS, D_ROWS = 0, 24, 60, 61, 62, 63, 64, 72

F32, BF16 = jnp.float32, jnp.bfloat16
MESH = pl.DeviceIdType.MESH
NN = (((1,), (0,)), ((), ()))
NT = (((1,), (1,)), ((), ()))


def dot(a, b, dims=NN):
    return lax.dot_general(a, b, dims, preferred_element_type=F32)


def rounded(v):
    return v.astype(BF16).astype(F32)


def pieces(v):
    high = v.astype(BF16)
    rest = v - high.astype(F32)
    middle = rest.astype(BF16)
    return high, middle, (rest - middle.astype(F32)).astype(BF16)


def split(v):
    high = v.astype(BF16)
    return high, (v - high.astype(F32)).astype(BF16)


def product(a, b, dims=NN):
    return dot(a[0], b[0], dims) + dot(a[0], b[1], dims) + dot(a[1], b[0], dims)


def softplus(v):
    return jnp.maximum(v, 0.0) + jnp.log1p(jnp.exp(-jnp.abs(v)))


def sigmoid(v):
    return 0.5 + 0.5 * jnp.tanh(0.5 * v)


def gate(half):
    up = 1.0 + jnp.tanh(half)
    value = half * up
    return value, up + value * (2.0 - up)


def rows_of(shape):
    return lax.broadcasted_iota(jnp.int32, shape, 0)


def schulz(refs, steps):
    @pl.loop(0, steps)
    def _(step):
        matrices = [ref[...] for ref in refs]
        parts = [split(matrix) for matrix in matrices]
        grams = [product(part, part, NT) for part in parts]
        halves = [split(gram) for gram in grams]
        squares = [product(half, half) for half in halves]
        blends = [
            split(COEF_CUBIC * gram + COEF_QUINTIC * square) for gram, square in zip(grams, squares)
        ]
        moved = [product(blend, part) for blend, part in zip(blends, parts)]
        for ref, matrix, move in zip(refs, matrices, moved):
            ref[...] = COEF_LINEAR * matrix + move


def normalise(ref):
    moment = ref[...]
    norm = jnp.sqrt(jnp.sum(jnp.sum(moment * moment, axis=1, keepdims=True), axis=0, keepdims=True))
    ref[...] = moment / (norm + 1e-7)


class Layout:
    def __init__(self, mesh, replay, model):
        self.n_dp = mesh.shape["dp"]
        self.n_blk = mesh.shape["blk"]
        self.bits = int(math.log2(self.n_dp))
        self.n_dev = self.n_dp * self.n_blk
        self.replay = replay
        self.model = model
        self.real = self.n_dp * CAP
        self.batch = self.real + model
        self.width = -(-(self.real + 2) // 128) * 128
        self.rows = HSAC // self.n_blk
        self.drows = HDYN // self.n_blk
        self.mat = 64 // self.n_dp
        self.sml = 32 // self.n_dp
        self.chunks = (2 * self.mat, self.mat + self.sml)
        self.split_z = all(chunk % self.n_blk == 0 for chunk in self.chunks)
        self.owners = [self.n_dp - 5, self.n_dp - 3, self.n_dp - 1]

    def part(self, group):
        return self.chunks[group] // self.n_blk if self.split_z else self.chunks[group]


def main_kernel(lay, *refs):
    (
        replay, model, requests, member, live, noise, sac_h, sac_m, dyn_h, dyn_m, crit_in, act_in,
        dyn_in, crit_out, act_out, dyn_out, biases, targ_in, targ_hidden, targ_out, targ_bias,
        sac_g, sac_x, dyn_g, dyn_x, dyn_s, small, count,
        wg, asked, owned, dhg, dmg, smg, bk, xs, nz, w1f, w1t, w1n, w2t, w2h, heads, head_t, head_f,
        rowbuf, cols, headcol, acc_h, acc_w, acc_c, acc_a, acc_m, acc_l, grid_c, grid_a, zr_c, zr_a,
        zf_c, zf_a, mg, mat, grow, dcols, dacc_h, dacc_w, dacc_o, dacc_m, dacc_b, dacc_l, xt, dmat,
        dpack, drow_g, drow_x, bias, dhead, dhead_t, *rest,
    ) = refs
    bits = lay.bits
    bufs = (rest[:bits], rest[bits : 2 * bits])
    (
        s_w, r_w, s_q, r_q, s_p, r_p, s_dh, r_dh, s_dm, r_dm, s_sm, r_sm, s_bz, r_bz, s_bo, r_bo,
        s_bp, r_bp, s_rs, r_rs, s_zr, r_zr, s_za, r_za, s_pl, r_pl, s_mg, r_mg, s_ds, r_ds, s_dg,
        r_dg, s_dx, r_dx, f_ds, f_dg, f_dx, s_sg, r_sg, s_sx, r_sx,
    ) = rest[2 * bits :]
    grids, zrs, zfs = (grid_c, grid_a), (zr_c, zr_a), (zf_c, zf_a)
    n_dp, n_blk = lay.n_dp, lay.n_blk
    me = lax.axis_index("dp")
    z = lax.axis_index("blk")
    core = lax.rem(me, 2)
    sibling = me + 1 - 2 * core
    is_dyn = me < MEMBERS
    dyn_e = jnp.minimum(me, MEMBERS - 1)
    is_actor = me == lay.owners[2]
    is_critic = jnp.logical_or(me == lay.owners[0], me == lay.owners[1])
    is_sac = jnp.logical_or(is_actor, is_critic)
    sac_k = jnp.clip((me - lay.owners[0]) // 2, 0, 2)

    def on_plane(src, dst, ssem, rsem, peer):
        return pltpu.make_async_remote_copy(
            src_ref=src, dst_ref=dst, send_sem=ssem, recv_sem=rsem,
            device_id={"dp": peer}, device_id_type=MESH,
        )

    def on_line(src, dst, ssem, rsem, peer):
        return pltpu.make_async_remote_copy(
            src_ref=src, dst_ref=dst, send_sem=ssem, recv_sem=rsem,
            device_id={"blk": peer}, device_id_type=MESH,
        )

    def plane_peers(body):
        @pl.loop(1, n_dp)
        def _(off):
            body(lax.rem(me + off, n_dp))

    def like_peers(body):
        @pl.loop(1, n_dp // 2)
        def _(off):
            body(lax.rem(me + 2 * off, n_dp))

    def line_peers(body):
        @pl.loop(1, n_blk)
        def _(off):
            body(lax.rem(z + off, n_blk))

    barrier = pltpu.get_barrier_semaphore()
    plane_peers(lambda peer: pl.semaphore_signal(barrier, inc=1, device_id={"dp": peer}, device_id_type=MESH))
    line_peers(lambda peer: pl.semaphore_signal(barrier, inc=1, device_id={"blk": peer}, device_id_type=MESH))
    wg[z] = sac_h[...].astype(BF16)
    pl.semaphore_wait(barrier, n_dp - 1 + n_blk - 1)

    def hidden_copy(owner, part, peer):
        at = (2, 1) if part == 0 else (0, 2)
        view = wg.at[owner, pl.ds(*at)]
        return on_line(view, view, s_w.at[part, peer], r_w.at[part, owner], peer)

    line_peers(lambda peer: hidden_copy(z, 0, peer).start())

    def list_copy(owner, peer):
        return on_plane(requests, asked.at[owner], s_q.at[peer], r_q.at[owner], peer)

    def member_copy(owner, peer):
        return on_plane(member, owned.at[owner], s_p.at[peer], r_p.at[owner], peer)

    plane_peers(lambda peer: list_copy(me, peer).start())
    plane_peers(lambda peer: member_copy(me, peer).start())
    line_peers(lambda peer: hidden_copy(z, 1, peer).start())
    asked[me] = requests[...]
    owned[me] = member[...]

    def dyn_h_copy(owner, peer):
        return on_line(dyn_h.at[dyn_e], dhg.at[owner], s_dh.at[peer], r_dh.at[owner], peer)

    def dyn_m_copy(owner, peer):
        return on_line(dyn_m.at[dyn_e], dmg.at[owner], s_dm.at[peer], r_dm.at[owner], peer)

    def sac_m_copy(owner, peer):
        return on_line(sac_m.at[sac_k], smg.at[owner], s_sm.at[peer], r_sm.at[owner], peer)

    alive = live[...].astype(F32).reshape(1, lay.model)
    bias[...] = biases[...].reshape(1, NB)
    xs[42:56, :] = jnp.zeros((14, lay.batch), F32)
    xs[0:FEAT, lay.real : lay.batch] = model[...]
    xs[42:43, lay.real : lay.batch] = alive
    nz[...] = jnp.zeros_like(nz)
    for which in range(2):
        nz[which, 1:7, :] = noise[:, which, :]
    firsts = [
        (targ_in[:, 0, :], targ_bias[0:1, 0:HSAC]),
        (targ_in[:, 1, :], targ_bias[1:2, 0:HSAC]),
        (crit_in[:, 0, :], bias[:, CB1 : CB1 + HSAC]),
        (crit_in[:, 1, :], bias[:, CB1 + HSAC : CB1 + 2 * HSAC]),
        (act_in[...], bias[:, AB1 : AB1 + HSAC]),
    ]
    w1f[...] = jnp.zeros_like(w1f)
    for net, (weights, offset) in enumerate(firsts):
        w1f[net, 0 : weights.shape[0], :] = rounded(weights)
        for at, piece in enumerate(pieces(offset)):
            w1f[net, IN + at : IN + at + 1, :] = piece.astype(F32)
        w1t[net] = (0.5 * w1f[net].T).astype(BF16)
    for k in range(2):
        w1n[k] = w1f[2 + k, 16:32, :].astype(BF16)
    for net in range(2):
        w2t[net] = (0.5 * rounded(targ_hidden[net])).T.astype(BF16)
    rowbuf[...] = jnp.zeros_like(rowbuf)
    rowbuf[0:1, :] = targ_bias[0:1, HSAC : 2 * HSAC]
    rowbuf[1:2, :] = targ_bias[1:2, HSAC : 2 * HSAC]
    rowbuf[2:3, :] = bias[:, CB2 : CB2 + HSAC]
    rowbuf[3:4, :] = bias[:, CB2 + HSAC : CB2 + 2 * HSAC]
    rowbuf[4:5, :] = bias[:, AB2 : AB2 + HSAC]
    rowbuf[5:7, :] = rounded(crit_out[...])
    cols[...] = 0.5 * rowbuf[...].T
    rowbuf[...] = jnp.zeros_like(rowbuf)
    rowbuf[0:1, 1:7] = bias[:, AB3 : AB3 + ACT]
    rowbuf[0:1, 9:15] = bias[:, AB3 + ACT : AB3 + 2 * ACT]
    headcol[...] = rowbuf[:, 0:128].T
    head_f[...] = jnp.zeros_like(head_f)
    for k in range(2):
        head_f[0:1, :] = targ_out[k : k + 1, :]
        heads[k] = head_f[...].astype(BF16)
        head_f[0:1, :] = crit_out[k : k + 1, :]
        heads[2 + k] = head_f[...].astype(BF16)
    head_f[0:1, :] = jnp.zeros((1, HSAC), F32)
    head_f[1:7, :] = act_out[0:ACT, :]
    head_f[9:15, :] = act_out[ACT : 2 * ACT, :]
    heads[4] = head_f[...].astype(BF16)
    head_t[...] = (0.5 * rounded(head_f[...])).T.astype(BF16)
    for ref in (acc_h, acc_w, acc_c, acc_a, acc_m, acc_l):
        ref[...] = jnp.zeros_like(ref)

    data = replay[...]
    sums = jnp.sum(data[0:24], axis=1, keepdims=True)
    squares = jnp.sum(data[0:24] * data[0:24], axis=1, keepdims=True)
    living = jnp.sum(alive, axis=1, keepdims=True)

    def wait_lists(peer):
        list_copy(peer, peer).wait_recv()
        member_copy(peer, peer).wait_recv()

    plane_peers(wait_lists)
    spread = (
        lax.rem(lax.broadcasted_iota(jnp.int32, (CAP, lay.real), 1), CAP)
        == lax.broadcasted_iota(jnp.int32, (CAP, lay.real), 0)
    ).astype(F32)
    here = (
        lax.broadcasted_iota(jnp.int32, (n_dp, lay.real), 1) // CAP
        == lax.broadcasted_iota(jnp.int32, (n_dp, lay.real), 0)
    )

    def in_lanes(ref):
        lists = ref[:, me, :].astype(F32)
        wide = lax.dot_general(
            lists, spread, NN, precision=lax.Precision.HIGHEST, preferred_element_type=F32
        )
        return jnp.sum(jnp.where(here, wide, 0.0), axis=0, keepdims=True)

    slots = in_lanes(asked)
    wanted = jnp.maximum(slots, 0.0).astype(jnp.int32)
    hot = (rows_of((lay.replay, lay.real)) == wanted).astype(BF16)
    high, middle, low = pieces(data)
    picked = dot(high, hot) + dot(middle, hot) + dot(low, hot)
    mine = me * n_blk
    bk[mine, 0:FEAT, 0 : lay.real] = picked
    bk[mine, 42:43, 0 : lay.real] = (slots >= 0.0).astype(F32)
    bk[mine, 43:44, 0 : lay.real] = in_lanes(owned)
    bk[mine, 44:48, 0 : lay.real] = jnp.zeros((4, lay.real), F32)
    bk[mine, :, lay.real : lay.width] = jnp.zeros((48, lay.width - lay.real), F32)
    bk[mine, 0:24, lay.real : lay.real + 1] = sums
    bk[mine, 0:24, lay.real + 1 : lay.real + 2] = squares
    bk[mine, 24:25, lay.real : lay.real + 1] = living

    def slot_of(block):
        line = lax.rem(block, n_blk)
        return block - line + lax.rem(line - z + n_blk, n_blk)

    def block_line(owner, peer):
        slot = me * n_blk + lax.rem(owner - peer + n_blk, n_blk)
        return on_line(bk.at[mine], bk.at[slot], s_bz.at[peer], r_bz.at[owner], peer)

    def block_arrives(owner):
        slot = me * n_blk + lax.rem(owner - z + n_blk, n_blk)
        on_line(bk.at[mine], bk.at[slot], s_bz.at[owner], r_bz.at[owner], owner).wait_recv()

    def block_own(owner, peer):
        view = bk.at[owner * n_blk]
        return on_plane(view, view, s_bo.at[peer], r_bo.at[owner], peer)

    def block_plane(owner, peer):
        view = bk.at[pl.ds(owner * n_blk + 1, n_blk - 1)]
        return on_plane(view, view, s_bp.at[peer], r_bp.at[owner], peer)

    plane_peers(lambda peer: block_own(me, peer).start())
    line_peers(lambda peer: block_line(z, peer).start())

    @pl.when(is_dyn)
    def _():
        line_peers(lambda peer: dyn_h_copy(z, peer).start())
        line_peers(lambda peer: dyn_m_copy(z, peer).start())

    @pl.when(is_sac)
    def _():
        line_peers(lambda peer: sac_m_copy(z, peer).start())

    def wait_hidden(peer):
        hidden_copy(peer, 0, peer).wait_recv()
        hidden_copy(peer, 1, peer).wait_recv()

    line_peers(wait_hidden)
    for k in range(3):
        for block in range(n_blk):
            w2h[k, block * lay.rows : (block + 1) * lay.rows, :] = (
                0.5 * wg[block, k].astype(F32)
            ).astype(BF16)
        w2t[2 + k] = w2h[k].astype(F32).T.astype(BF16)

    log_alpha = bias[:, LOGA : LOGA + 1]
    alpha = jnp.exp(log_alpha)
    last = [
        targ_bias[0:1, 2 * HSAC : 2 * HSAC + 1],
        targ_bias[1:2, 2 * HSAC : 2 * HSAC + 1],
        bias[:, CB3 : CB3 + 1],
        bias[:, CB3 + 1 : CB3 + 2],
    ]
    n_tiles = lay.batch // TILE
    row8 = rows_of((8, TILE))
    act_rows = jnp.logical_and(row8 >= 1, row8 < 1 + ACT)

    def place_of(step):
        return pl.ds(pl.multiple_of(lax.rem(step + 1, n_tiles) * TILE, TILE), TILE)

    def ones16():
        return jnp.ones((16, TILE), BF16)

    def framed(first_row, used, where):
        row32 = rows_of((32, TILE))
        ones3 = jnp.logical_and(row32 >= IN, row32 < IN + 3).astype(F32)
        return jnp.where(row32 < used, xs[first_row : first_row + 32, where], ones3)

    def hidden(inputs, net):
        first, slope1 = gate(dot(w1t[net], inputs))
        first = first.astype(BF16)
        second, slope2 = gate(dot(w2t[net], first) + cols[:, net : net + 1])
        return first, slope1, second.astype(BF16), slope2

    def policy(inputs, which, where):
        first, slope1, second, slope2 = hidden(inputs, 4)
        out = dot(heads[4], second) + headcol[0:16, 0:1]
        bent = jnp.tanh(out[8:16])
        log_scale = -5.0 + 3.5 * (bent + 1.0)
        draw = nz[which, :, where]
        moved = jnp.exp(log_scale) * draw
        latent = out[0:8] + moved
        terms = (
            -0.5 * draw * draw
            - log_scale
            - 0.9189385
            - 2.0 * (0.6931472 - latent - softplus(-2.0 * latent))
        )
        log_prob = jnp.sum(jnp.where(act_rows, terms, 0.0), axis=0, keepdims=True)
        action = jnp.where(act_rows, jnp.tanh(latent), 0.0)
        return action, log_prob, bent, moved, (first, slope1, second, slope2)

    def with_action(inputs, action):
        middle_rows = jnp.where(act_rows, action, inputs[16:24])
        return jnp.concatenate([inputs[0:16], middle_rows, inputs[24:32]], 0).astype(BF16)

    def critic(inputs, net):
        kept = hidden(inputs, net)
        value = dot(heads[net], kept[2])[0:1] + last[net]
        return value, kept

    def add_hidden(k, first, grad):
        acc_h[k] += dot(jnp.concatenate([first, ones16()], 0), grad, NT)

    @pl.loop(0, n_tiles)
    def _(step):
        @pl.when(step == 1)
        def _():
            line_peers(block_arrives)
            plane_peers(lambda peer: block_plane(me, peer).start())

        @pl.when(step == n_tiles - 1)
        def _():
            plane_peers(lambda peer: block_own(peer, peer).wait_recv())
            lanes = lax.broadcasted_iota(jnp.int32, (48, lay.width), 1) // CAP

            def gather(owner, total):
                turned = pltpu.roll(
                    bk[owner * n_blk], lax.rem((owner - me) * CAP + lay.width, lay.width), axis=1
                )
                return jnp.where(lanes == owner, turned, total)

            own = lax.fori_loop(0, n_dp, gather, jnp.zeros((48, lay.width), F32))
            xs[0:48, 0 : lay.real] = own[:, 0 : lay.real]

        where = place_of(step)
        now_in = framed(0, IN, where).astype(BF16)
        next_f = framed(24, OBS, where)
        reward = xs[23:24, where]
        done = xs[41:42, where]
        weight = xs[42:43, where]
        row16 = rows_of((16, TILE))
        next_action, next_prob, _, _, _ = policy(next_f.astype(BF16), 1, where)
        aim_in = with_action(next_f, next_action)
        aim = jnp.minimum(critic(aim_in, 0)[0], critic(aim_in, 1)[0])
        target = reward + DISCOUNT * (1.0 - done) * (aim - alpha * next_prob)
        loss = jnp.zeros((1, TILE), F32)
        heads_grad = []
        for k in range(2):
            value, (c1, dc1, c2, dc2) = critic(now_in, 2 + k)
            miss = value - target
            loss += 0.5 * miss * miss
            g3 = rounded(weight * miss)
            g3_rows = jnp.where(row16 == 0, g3, 0.0).astype(BF16)
            heads_grad.append(g3_rows)
            acc_c[k] += dot(g3_rows, c2, NT)
            g2 = ((cols[:, 5 + k : 6 + k] * g3) * dc2).astype(BF16)
            add_hidden(k, c1, g2)
            g1 = (dot(w2h[k], g2) * dc1).astype(BF16)
            acc_w[k] += dot(now_in, g1, NT)
        acc_m[:, 16:48] += dot(ones16(), jnp.concatenate(heads_grad, 0), NT)
        acc_l[0:1, :] += weight * loss

    def put_matrix(group, k, at):
        for chunk in range(n_dp):
            tile = chunk * lay.mat
            side, row = tile // 32, tile % 32
            grids[group][chunk, at * lay.mat : (at + 1) * lay.mat] = acc_h[
                k, row * 8 : (row + lay.mat) * 8, side * 128 : (side + 1) * 128
            ].reshape(lay.mat, 8, 128)

    def put(row, value):
        for at in range(value.shape[0] // 8):
            for side in range(value.shape[1] // 128):
                tile = side * (R_SMALL // 8) + row // 8 + at
                grid_a[tile // lay.sml, lay.mat + tile % lay.sml] = value[
                    at * 8 : at * 8 + 8, side * 128 : (side + 1) * 128
                ]

    def bit(b):
        return lax.rem(me // (1 << b), 2)

    starts, faces, partners = [], [], []
    start = 0
    for s in range(bits):
        if s == 0:
            face, stride = core, 1
        else:
            face = (1 - core) * bit(s) + core * bit(bits - s)
            stride = (1 - core) * (1 << s) + core * (1 << (bits - s))
        starts.append(start)
        faces.append(face)
        partners.append(me + (1 - 2 * face) * stride)
        start = start + face * (n_dp >> (s + 1))
    place = start

    def fold_copy(group, s):
        half = n_dp >> (s + 1)
        begin = starts[s] + (1 - faces[s]) * half
        return on_plane(
            grids[group].at[pl.ds(begin, half)], bufs[group][s], s_rs.at[group, s], r_rs.at[group, s],
            partners[s],
        )

    def fold_wait(group, s):
        half = n_dp >> (s + 1)
        begin = starts[s] + faces[s] * half
        fold_copy(group, s).wait_recv()
        for at in range(half):
            grids[group][begin + at] += bufs[group][s][at]

    def line_first(group, owner, peer):
        if lay.split_z:
            src = grids[group].at[place, pl.ds(peer * lay.part(group), lay.part(group))]
        else:
            src = grids[group].at[place]
        return on_line(src, zrs[group].at[owner], s_zr.at[group, peer], r_zr.at[group, owner], peer)

    def line_second(group, owner, peer):
        view = zfs[group].at[pl.ds(owner * lay.part(group), lay.part(group))]
        return on_line(view, view, s_za.at[group, peer], r_za.at[group, owner], peer)

    def line_start(group):
        line_peers(lambda peer: line_first(group, z, peer).start())

    def line_sum(group):
        part, zr, zf = lay.part(group), zrs[group], zfs[group]
        line_peers(lambda peer: line_first(group, peer, peer).wait_recv())
        zr[z] = grids[group][place, pl.ds(z * part, part)] if lay.split_z else grids[group][place]
        whole = zr[0]
        for block in range(1, n_blk):
            whole = whole + zr[block]
        if lay.split_z:
            zf[pl.ds(z * part, part)] = whole
            line_peers(lambda peer: line_second(group, z, peer).start())
        else:
            zf[...] = whole

    def line_end(group):
        if lay.split_z:
            line_peers(lambda peer: line_second(group, peer, peer).wait_recv())

    def tile_copy(k, owner):
        src = zfs[k // 2].at[pl.ds((k % 2) * lay.mat, lay.mat)]
        return on_plane(src, mg.at[place], s_mg.at[k], r_mg.at[place], owner)

    def send_tiles(group):
        for k in (0, 1) if group == 0 else (2,):
            @pl.when(me != lay.owners[k])
            def _():
                tile_copy(k, lay.owners[k]).start()

            @pl.when(me == lay.owners[k])
            def _():
                mg[place] = zfs[group][(k % 2) * lay.mat : (k % 2 + 1) * lay.mat]

    def small_copy(at, peer):
        return on_plane(
            zf_a.at[pl.ds(lay.mat, lay.sml)], small.at[pl.ds(at * lay.sml, lay.sml)],
            s_pl.at[peer], r_pl.at[at], peer,
        )

    def chain(group):
        steps = [functools.partial(lambda s: fold_copy(group, s).start(), 0)]

        def fold(s):
            fold_wait(group, s)
            if s + 1 < bits:
                fold_copy(group, s + 1).start()
            else:
                line_start(group)

        steps += [functools.partial(fold, s) for s in range(bits)]
        steps.append(lambda: line_sum(group))

        def finish():
            line_end(group)
            send_tiles(group)
            if group == 1:
                plane_peers(lambda peer: small_copy(place, peer).start())
                small[pl.ds(place * lay.sml, lay.sml)] = zf_a[lay.mat :]

        steps.append(finish)
        return steps

    critic_chain, actor_chain = chain(0), chain(1)
    for k in range(2):
        put_matrix(0, k, k)
    critic_chain[0]()

    inside = min(len(critic_chain) - 1, n_tiles - 1)

    @pl.loop(0, n_tiles)
    def _(step):
        for at in range(inside):
            @pl.when(step == at + 1)
            def _():
                critic_chain[at + 1]()

        where = place_of(step)
        now_f = framed(0, IN, where)
        now_in = now_f.astype(BF16)
        weight = xs[42:43, where]
        action, log_prob, bent, moved, (a1, da1, a2, da2) = policy(now_in, 0, where)
        judged_in = with_action(now_f, action)
        loss = alpha * log_prob - log_alpha * (log_prob + TARGET_ENTROPY)
        grad_action = jnp.zeros((8, TILE), F32)
        for k in range(2):
            judged, (_, df1, _, df2) = critic(judged_in, 2 + k)
            loss -= 0.5 * judged
            g2 = ((cols[:, 5 + k : 6 + k] * (-0.5 * weight)) * df2).astype(BF16)
            g1 = (dot(w2h[k], g2) * df1).astype(BF16)
            grad_action += dot(w1n[k], g1)[0:8]
        grad_latent = 2.0 * alpha * weight * action + grad_action * (1.0 - action * action)
        grad_scale = grad_latent * moved - alpha * weight
        grad_bent = grad_scale * 3.5 * (1.0 - bent * bent)
        g3 = jnp.concatenate(
            [jnp.where(act_rows, grad_latent, 0.0), jnp.where(act_rows, grad_bent, 0.0)], 0
        ).astype(BF16)
        acc_a[...] += dot(g3, a2, NT)
        acc_m[:, 0:16] += dot(ones16(), g3, NT)
        g2 = (dot(head_t[...], g3) * da2).astype(BF16)
        add_hidden(2, a1, g2)
        g1 = (dot(w2h[2], g2) * da1).astype(BF16)
        acc_w[2] += dot(now_in, g1, NT)
        acc_l[0:1, :] += weight * loss
        acc_l[1:2, :] += weight * (log_prob + TARGET_ENTROPY)

    for at in range(inside, len(critic_chain) - 1):
        critic_chain[at + 1]()
    put_matrix(1, 2, 0)
    for k in range(3):
        put(R_IN + 24 * k, acc_w[k, 0:24, :])
    put(R_HEAD, acc_a[...])
    rowbuf[0:1, :] = acc_c[0, 0:1, :]
    rowbuf[1:2, :] = acc_c[1, 0:1, :]
    for k in range(3):
        rowbuf[2 + k : 3 + k, :] = acc_h[k, HSAC : HSAC + 1, :]
    put(R_OUT, rowbuf[...])
    folded = jnp.sum(acc_l[...], axis=1, keepdims=True)
    rowbuf[...] = jnp.zeros_like(rowbuf)
    rowbuf[0:1, 0:48] = acc_m[0:1, :]
    rowbuf[0:1, 64:65] = folded[0:1]
    rowbuf[0:1, 65:66] = folded[1:2]
    put(R_MISC, rowbuf[...])
    put(R_MISC + 8, jnp.zeros((R_SMALL - R_MISC - 8, HSAC), F32))
    actor_chain[0]()

    plane_peers(lambda peer: block_plane(peer, peer).wait_recv())
    lane0 = lay.real // 128 * 128

    def add_block(at, carry):
        sides, fills = carry
        slot = slot_of(at)
        return sides + bk[slot, 0:32, lane0 : lane0 + 128], fills + bk[slot, 40:48, 0 : lay.real]

    sides, fills = lax.fori_loop(
        0, lay.n_dev, add_block, (jnp.zeros((32, 128), F32), jnp.zeros((8, lay.real), F32))
    )
    at = lay.real - lane0
    rows_all = float(lay.replay * lay.n_dev)
    centre = sides[0:24, at : at + 1] / rows_all
    scale = lax.rsqrt(sides[0:24, at + 1 : at + 2] / rows_all - centre * centre + 1e-6)
    total = sides[24:25, at : at + 1] + jnp.sum(fills[2:3, :], axis=1, keepdims=True)
    count[...] = jnp.broadcast_to(total, (8, 128))

    def dyn_bias(start, width):
        row = jnp.zeros((1, width), F32)
        for e in range(MEMBERS):
            row = jnp.where(me == e, bias[:, start + width * e : start + width * (e + 1)], row)
        return row

    @pl.when(is_dyn)
    def _():
        w1f[0] = jnp.zeros((32, HSAC), F32)
        w1f[0, 0:IN, 0:HDYN] = rounded(dyn_in[dyn_e])
        for at, piece in enumerate(pieces(dyn_bias(DB1, HDYN))):
            w1f[0, IN + at : IN + at + 1, 0:HDYN] = piece.astype(F32)
        w1t[0] = (0.5 * w1f[0].T).astype(BF16)
        rowbuf[...] = jnp.zeros_like(rowbuf)
        rowbuf[0:1, 0:HDYN] = dyn_bias(DB2, HDYN)
        head_row = dyn_bias(DB3, DOUT)
        rowbuf[1:2, 0:HALF] = head_row[:, 0:HALF]
        rowbuf[1:2, 24 : 24 + HALF] = head_row[:, HALF:DOUT]
        rowbuf[2:3, 0:HALF] = bias[:, MAXLV : MAXLV + HALF]
        rowbuf[3:4, 0:HALF] = bias[:, MINLV : MINLV + HALF]
        dcols[...] = rowbuf[...].T
        dpack[...] = jnp.zeros_like(dpack)
        dpack[0:HALF, 0:HDYN] = dyn_out[dyn_e, 0:HALF, :]
        dpack[24 : 24 + HALF, 0:HDYN] = dyn_out[dyn_e, HALF:DOUT, :]
        dhead[...] = dpack[0:48, :].astype(BF16)
        dhead_t[...] = (0.5 * rounded(dpack[0:48, :])).T.astype(BF16)
        dpack[...] = jnp.zeros_like(dpack)

        def wait_dyn(peer):
            dyn_h_copy(peer, peer).wait_recv()
            dyn_m_copy(peer, peer).wait_recv()

        line_peers(wait_dyn)
        dhg[z] = dyn_h[dyn_e]
        dmg[z] = dyn_m[dyn_e]
        dmat[...] = jnp.zeros_like(dmat)
        for block in range(n_blk):
            dmat[block * lay.drows : (block + 1) * lay.drows, 0:HDYN] = 0.5 * rounded(dhg[block])
        w2h[0] = dmat[...].astype(BF16)
        w2t[0] = dmat[...].T.astype(BF16)
        for ref in (dacc_h, dacc_w, dacc_o, dacc_m, dacc_b, dacc_l):
            ref[...] = jnp.zeros_like(ref)

    per = TILE // lay.real
    dyn_tiles = lay.n_dev // per
    gap = max(dyn_tiles // (bits + 1), 1)

    @pl.loop(0, dyn_tiles)
    def _(tile):
        for s in range(bits):
            @pl.when(tile == (s + 1) * gap)
            def _():
                actor_chain[s + 1]()

        @pl.when(is_dyn)
        def _():
            for at in range(per):
                slot = slot_of(tile * per + at)
                xt[:, at * lay.real : (at + 1) * lay.real] = bk[slot, :, 0 : lay.real]
            now = xt[0:24, :]
            later = xt[24:48, :]
            row24 = rows_of((24, TILE))
            scaled = jnp.where(row24 < IN, (now - centre) * scale, 1.0)
            inputs = jnp.concatenate([scaled, (row8 < 2).astype(F32)], 0).astype(BF16)
            first, slope1 = gate(dot(w1t[0], inputs))
            first = first.astype(BF16)
            second, slope2 = gate(dot(w2t[0], first) + 0.5 * dcols[:, 0:1])
            second = second.astype(BF16)
            out = dot(dhead[...], second) + dcols[0:48, 1:2]
            used = row24 < HALF
            upper = dcols[0:24, 2:3]
            lower = dcols[0:24, 3:4]
            gap1 = upper - out[24:48]
            gap2 = upper - softplus(gap1) - lower
            log_var = lower + softplus(gap2)
            error = out[0:24] - jnp.where(row24 == OBS, now[23:24], later - now)
            inverse = jnp.exp(-log_var)
            weight = xt[42:43, :] * (xt[43:44, :] == me.astype(F32)).astype(F32)
            spread_term = error * error * inverse
            nll = jnp.sum(jnp.where(used, spread_term + log_var, 0.0), axis=0, keepdims=True)
            dacc_l[0:1, :] += weight * nll
            grad_mu = 2.0 * weight * error * inverse
            grad_lv = weight * (1.0 - spread_term)
            open1 = sigmoid(gap1)
            open2 = sigmoid(gap2)
            grad_lv1 = grad_lv * open2
            dacc_b[0] += jnp.where(used, grad_lv1 * (1.0 - open1), 0.0)
            dacc_b[1] += jnp.where(used, grad_lv * (1.0 - open2), 0.0)
            g3 = jnp.concatenate(
                [jnp.where(used, grad_mu, 0.0), jnp.where(used, grad_lv1 * open1, 0.0)], 0
            ).astype(BF16)
            dacc_o[...] += dot(g3, second, NT)
            dacc_m[...] += dot(ones16(), g3, NT)
            g2 = (dot(dhead_t[...], g3) * slope2).astype(BF16)
            dacc_h[...] += dot(jnp.concatenate([first, ones16()], 0), g2, NT)
            g1 = (dot(w2h[0], g2) * slope1).astype(BF16)
            dacc_w[...] += dot(inputs, g1, NT)

    def pack_copy(src, owner, ssem, peer):
        return on_plane(src, dyn_s.at[owner], ssem, r_ds.at[owner], peer)

    def dyn_g_copy(src, owner, ssem, peer):
        return on_plane(src, dyn_g.at[owner], ssem, r_dg.at[owner], peer)

    def dyn_x_copy(src, owner, ssem, peer):
        return on_plane(src, dyn_x.at[owner], ssem, r_dx.at[owner], peer)

    def give(copy, src, sems):
        like_peers(lambda peer: copy(src, dyn_e, sems.at[peer], peer).start())
        copy(src, dyn_e, sems.at[sibling], sibling).start()

    def given(copy, src, sems):
        like_peers(lambda peer: copy(src, dyn_e, sems.at[peer], peer).wait_send())
        copy(src, dyn_e, sems.at[sibling], sibling).wait_send()

    def from_like(body):
        def member_only(peer):
            @pl.when(peer < MEMBERS)
            def _():
                body(jnp.minimum(peer, MEMBERS - 1))

        like_peers(member_only)

    def hand_on(copy, out, sems):
        def body(owner):
            copy(out.at[owner], owner, sems.at[owner], sibling).wait_recv()
            copy(out.at[owner], owner, sems.at[owner], sibling).start()

        from_like(body)

    def handed_on(copy, out, sems):
        from_like(lambda owner: copy(out.at[owner], owner, sems.at[owner], sibling).wait_send())

    def from_sibling(copy, out, sems):
        @pl.loop(0, n_dp // 2)
        def _(off):
            owner = lax.rem(sibling + 2 * off, n_dp)

            @pl.when(owner < MEMBERS)
            def _():
                at = jnp.minimum(owner, MEMBERS - 1)
                copy(out.at[at], at, sems.at[at], sibling).wait_recv()

    def line_rows(ref):
        rows = ref[0 : lay.drows, 0:HDYN]
        for block in range(1, n_blk):
            rows = jnp.where(z == block, ref[block * lay.drows : (block + 1) * lay.drows, 0:HDYN], rows)
        return rows

    def sac_g_copy(k, peer):
        src = grow.at[pl.ds(pl.multiple_of(z * lay.rows, lay.rows), lay.rows)]
        return on_plane(src, sac_g.at[k], s_sg.at[peer], r_sg.at[k], peer)

    def sac_x_copy(k, peer):
        src = mat.at[pl.ds(pl.multiple_of(z * lay.rows, lay.rows), lay.rows)]
        return on_plane(src, sac_x.at[k], s_sx.at[peer], r_sx.at[k], peer)

    mine_rows = pl.ds(pl.multiple_of(z * lay.rows, lay.rows), lay.rows)

    def take_matrix():
        line_peers(lambda peer: sac_m_copy(peer, peer).wait_recv())
        smg[z] = sac_m[sac_k]

        @pl.loop(1, n_dp)
        def _(off):
            at = lax.rem(place + off, n_dp)
            on_plane(mg.at[at], mg.at[at], s_mg.at[0], r_mg.at[at], me).wait_recv()

        for chunk in range(n_dp):
            tile = chunk * lay.mat
            side, row = tile // 32, tile % 32
            grow[row * 8 : (row + lay.mat) * 8, side * 128 : (side + 1) * 128] = mg[chunk].reshape(
                lay.mat * 8, 128
            )
        sac_g[sac_k] = grow[mine_rows, :]
        plane_peers(lambda peer: sac_g_copy(sac_k, peer).start())
        for block in range(n_blk):
            at = slice(block * lay.rows, (block + 1) * lay.rows)
            mat[at, :] = MOMENTUM * smg[block] + grow[at, :] / total
        normalise(mat)

    @pl.when(is_dyn)
    def _():
        dpack[D_IN : D_IN + 24, :] = dacc_w[0:24, :]
        dpack[D_OUT : D_OUT + HALF, :] = dacc_o[0:HALF, :]
        dpack[D_OUT + HALF : D_OUT + DOUT, :] = dacc_o[24 : 24 + HALF, :]
        dpack[D_B2 : D_B2 + 1, :] = dacc_h[HSAC : HSAC + 1, :]
        dpack[D_B3 : D_B3 + 1, 0:48] = dacc_m[0:1, :]
        lanes = lax.broadcasted_iota(jnp.int32, (24, 128), 1)
        bound = jnp.where(
            lanes == 0,
            jnp.sum(dacc_b[0], axis=1, keepdims=True),
            jnp.where(lanes == 1, jnp.sum(dacc_b[1], axis=1, keepdims=True), 0.0),
        )
        dpack[D_UP : D_UP + 2, 0:24] = bound.T[0:2, :]
        dpack[D_LOSS : D_LOSS + 1, 0:128] = jnp.broadcast_to(
            jnp.sum(dacc_l[0:1, :], axis=1, keepdims=True), (1, 128)
        )
        dyn_s[dyn_e] = dpack[...]
        give(pack_copy, dpack, s_ds)
        rows = line_rows(dacc_h)
        drow_g[...] = rows
        dyn_g[dyn_e] = rows
        give(dyn_g_copy, drow_g, s_dg)
        dmat[...] = jnp.zeros_like(dmat)
        for block in range(n_blk):
            at = slice(block * lay.drows, (block + 1) * lay.drows)
            dmat[at, 0:HDYN] = MOMENTUM * dmg[block] + dacc_h[at, 0:HDYN] / total
        normalise(dmat)

    pl.when(is_critic)(take_matrix)
    if n_dp <= MEMBERS + 1:
        only_dyn = jnp.logical_and(is_dyn, jnp.logical_not(is_critic))
        pairs = [(is_critic, [dmat, mat]), (only_dyn, [dmat])]
    else:
        pairs = [(is_critic, [mat]), (is_dyn, [dmat])]
    for test, matrices in pairs:
        pl.when(test)(functools.partial(schulz, matrices, 2))
    actor_chain[bits + 1]()
    for test, matrices in pairs:
        pl.when(test)(functools.partial(schulz, matrices, 2))
    actor_chain[bits + 2]()
    for test, matrices in pairs:
        pl.when(test)(functools.partial(schulz, matrices, NS_ITERS - 4))

    def send_sac():
        sac_x[sac_k] = mat[mine_rows, :]
        plane_peers(lambda peer: sac_x_copy(sac_k, peer).start())

    @pl.when(is_dyn)
    def _():
        rows = line_rows(dmat)
        drow_x[...] = rows
        dyn_x[dyn_e] = rows
        give(dyn_x_copy, drow_x, s_dx)

    pl.when(is_critic)(send_sac)

    @pl.when(is_actor)
    def _():
        take_matrix()
        schulz([mat], NS_ITERS)
        send_sac()

    hand_on(pack_copy, dyn_s, f_ds)
    hand_on(dyn_g_copy, dyn_g, f_dg)
    hand_on(dyn_x_copy, dyn_x, f_dx)

    @pl.loop(1, n_dp)
    def _(off):
        small_copy(lax.rem(place + off, n_dp), me).wait_recv()

    from_sibling(pack_copy, dyn_s, f_ds)
    from_sibling(dyn_g_copy, dyn_g, f_dg)
    from_sibling(dyn_x_copy, dyn_x, f_dx)
    for k in range(3):
        @pl.when(me != lay.owners[k])
        def _():
            sac_g_copy(k, me).wait_recv()
            sac_x_copy(k, me).wait_recv()

    def sent_on_line(peer):
        hidden_copy(z, 0, peer).wait_send()
        hidden_copy(z, 1, peer).wait_send()
        block_line(z, peer).wait_send()
        for group in range(2):
            line_first(group, z, peer).wait_send()
            if lay.split_z:
                line_second(group, z, peer).wait_send()

        @pl.when(is_dyn)
        def _():
            dyn_h_copy(z, peer).wait_send()
            dyn_m_copy(z, peer).wait_send()

        @pl.when(is_sac)
        def _():
            sac_m_copy(z, peer).wait_send()

    line_peers(sent_on_line)

    def sent_on_plane(peer):
        list_copy(me, peer).wait_send()
        member_copy(me, peer).wait_send()
        block_own(me, peer).wait_send()
        block_plane(me, peer).wait_send()
        small_copy(place, peer).wait_send()

        @pl.when(is_sac)
        def _():
            sac_g_copy(sac_k, peer).wait_send()
            sac_x_copy(sac_k, peer).wait_send()

    plane_peers(sent_on_plane)

    @pl.when(is_dyn)
    def _():
        given(pack_copy, dpack, s_ds)
        given(dyn_g_copy, drow_g, s_dg)
        given(dyn_x_copy, drow_x, s_dx)

    handed_on(pack_copy, dyn_s, f_ds)
    handed_on(dyn_g_copy, dyn_g, f_dg)
    handed_on(dyn_x_copy, dyn_x, f_dx)
    for group in range(2):
        for s in range(bits):
            fold_copy(group, s).wait_send()
    for k in range(3):
        @pl.when(me != lay.owners[k])
        def _():
            tile_copy(k, lay.owners[k]).wait_send()


def adamw(weights, first, second, gradient):
    first = BETA_FIRST * first + (1.0 - BETA_FIRST) * gradient
    second = BETA_SECOND * second + (1.0 - BETA_SECOND) * gradient * gradient
    first_hat = first / (1.0 - BETA_FIRST**STEP)
    second_hat = second / (1.0 - BETA_SECOND**STEP)
    step = first_hat / (jnp.sqrt(second_hat) + 1e-8) + ADAM_DECAY * weights
    return weights - ADAM_RATE * step, first, second


def update_kernel(*refs):
    (
        sac_g, sac_x, dyn_g, dyn_x, dyn_s, small, count, sac_h, sac_m, dyn_h, dyn_m,
        ci, ci_m, ci_v, ai, ai_m, ai_v, di, di_m, di_v, co, co_m, co_v, ao, ao_m, ao_v,
        do, do_m, do_v, bi, bi_m, bi_v,
        sac_new, sac_mom, dyn_new, dyn_mom, ci_n, ci_mn, ci_vn, ai_n, ai_mn, ai_vn, di_n, di_mn,
        di_vn, co_n, co_mn, co_vn, ao_n, ao_mn, ao_vn, do_n, do_mn, do_vn, bi_n, bi_mn, bi_vn,
        loss, counted, bg,
    ) = refs
    total = count[0:1, 0:1]
    sac_mom[...] = MOMENTUM * sac_m[...] + sac_g[...] / total.reshape(1, 1, 1)
    sac_new[...] = sac_h[...] * (1.0 - MUON_RATE * MUON_DECAY) - MUON_RATE * sac_x[...]
    dyn_mom[...] = MOMENTUM * dyn_m[...] + dyn_g[...] / total.reshape(1, 1, 1)
    dyn_new[...] = dyn_h[...] * (1.0 - MUON_RATE * MUON_DECAY) - MUON_RATE * dyn_x[...]

    def rows(row, number):
        sides = []
        for side in range(2):
            at = side * (R_SMALL // 8) + row // 8
            sides.append(small[at : at + -(-number // 8)].reshape(-1, 128))
        return jnp.concatenate(sides, 1)

    def store(outs, at, values):
        for out, value in zip(outs, values):
            out[at] = value

    outs = (ci_n, ci_mn, ci_vn)
    for k in range(2):
        at = (slice(None), k, slice(None))
        grad = rows(R_IN + 24 * k, 24)
        bg[:, CB1 + HSAC * k : CB1 + HSAC * (k + 1)] = grad[IN : IN + 1]
        store(outs, at, adamw(ci[at], ci_m[at], ci_v[at], grad[0:IN] / total))
    grad = rows(R_IN + 48, 24)
    bg[:, AB1 : AB1 + HSAC] = grad[IN : IN + 1]
    store((ai_n, ai_mn, ai_vn), ..., adamw(ai[...], ai_m[...], ai_v[...], grad[0:OBS] / total))
    grad = rows(R_HEAD, 16)
    for at, row in ((slice(0, ACT), slice(1, 1 + ACT)), (slice(ACT, 2 * ACT), slice(9, 9 + ACT))):
        store((ao_n, ao_mn, ao_vn), at, adamw(ao[at], ao_m[at], ao_v[at], grad[row] / total))
    grad = rows(R_OUT, 8)
    store((co_n, co_mn, co_vn), ..., adamw(co[...], co_m[...], co_v[...], grad[0:2] / total))
    bg[:, CB2 : CB2 + HSAC] = grad[2:3]
    bg[:, CB2 + HSAC : CB2 + 2 * HSAC] = grad[3:4]
    bg[:, AB2 : AB2 + HSAC] = grad[4:5]
    grad = rows(R_MISC, 8)
    bg[:, CB3 : CB3 + 1] = grad[0:1, 16:17]
    bg[:, CB3 + 1 : CB3 + 2] = grad[0:1, 32:33]
    bg[:, AB3 : AB3 + ACT] = grad[0:1, 1 : 1 + ACT]
    bg[:, AB3 + ACT : AB3 + 2 * ACT] = grad[0:1, 9 : 9 + ACT]
    bg[:, LOGA : LOGA + 1] = -grad[0:1, 65:66]
    total_loss = grad[0:1, 64:65]
    up = jnp.zeros((1, HALF), F32)
    low = jnp.zeros((1, HALF), F32)
    for e in range(MEMBERS):
        pack = dyn_s[e]
        total_loss = total_loss + pack[D_LOSS : D_LOSS + 1, 0:1]
        up = up + pack[D_UP : D_UP + 1, 0:HALF]
        low = low + pack[D_LOW : D_LOW + 1, 0:HALF]
        bg[:, DB1 + HDYN * e : DB1 + HDYN * (e + 1)] = pack[IN : IN + 1, 0:HDYN]
        bg[:, DB2 + HDYN * e : DB2 + HDYN * (e + 1)] = pack[D_B2 : D_B2 + 1, 0:HDYN]
        bg[:, DB3 + DOUT * e : DB3 + DOUT * e + HALF] = pack[D_B3 : D_B3 + 1, 0:HALF]
        bg[:, DB3 + DOUT * e + HALF : DB3 + DOUT * (e + 1)] = pack[D_B3 : D_B3 + 1, 24 : 24 + HALF]
        grad = pack[0:IN, 0:HDYN] / total
        store((di_n, di_mn, di_vn), e, adamw(di[e], di_m[e], di_v[e], grad))
        grad = pack[D_OUT : D_OUT + DOUT, 0:HDYN] / total
        store((do_n, do_mn, do_vn), e, adamw(do[e], do_m[e], do_v[e], grad))
    bg[:, MAXLV : MAXLV + HALF] = up
    bg[:, MINLV : MINLV + HALF] = low
    lane = lax.broadcasted_iota(jnp.int32, (1, NB), 1)
    bounds = jnp.where(
        jnp.logical_and(lane >= MAXLV, lane < MINLV),
        BOUND_WEIGHT,
        jnp.where(jnp.logical_and(lane >= MINLV, lane < LOGA), -BOUND_WEIGHT, 0.0),
    )
    grad = bg[...] / total + bounds
    flat = [ref[...].reshape(1, NB) for ref in (bi, bi_m, bi_v)]
    store((bi_n, bi_mn, bi_vn), ..., [value.reshape(NB) for value in adamw(*flat, grad)])
    loss[...] = total_loss
    counted[...] = total


def shards(
    lay, replay, model_rows, requests, member_of, model_live, noise, sac_hidden, sac_hidden_mom,
    dyn_hidden, dyn_hidden_mom, crit_in, crit_in_m, crit_in_v, act_in, act_in_m, act_in_v, dyn_in,
    dyn_in_m, dyn_in_v, crit_out, crit_out_m, crit_out_v, act_out, act_out_m, act_out_v, dyn_out,
    dyn_out_m, dyn_out_v, biases, biases_m, biases_v, targ_in, targ_hidden, targ_out, targ_bias,
):
    n_dp, n_blk, bits = lay.n_dp, lay.n_blk, lay.bits
    spec = pl.BlockSpec(memory_space=pltpu.VMEM)

    def flip(value):
        return jnp.transpose(value, (1, 0, 2))

    def swap(value):
        return jnp.swapaxes(value, -1, -2)

    def kept(value):
        return pltpu.with_memory_space_constraint(value, pltpu.VMEM)

    inputs = (
        replay, model_rows, requests, member_of, model_live, jnp.transpose(noise, (2, 0, 1)),
        sac_hidden, sac_hidden_mom, dyn_hidden, dyn_hidden_mom, flip(crit_in), act_in, dyn_in,
        crit_out, swap(act_out), swap(dyn_out), biases, flip(targ_in), targ_hidden, targ_out,
        targ_bias,
    )
    shape = jax.ShapeDtypeStruct
    rows, drows = lay.rows, lay.drows
    out_shape = (
        pltpu.VMEM((3, rows, HSAC), F32),
        pltpu.VMEM((3, rows, HSAC), F32),
        pltpu.VMEM((MEMBERS, drows, HDYN), F32),
        pltpu.VMEM((MEMBERS, drows, HDYN), F32),
        pltpu.VMEM((MEMBERS, D_ROWS, HSAC), F32),
        pltpu.VMEM((32, 8, 128), F32),
        pltpu.VMEM((8, 128), F32),
    )

    def vm(*dims, kind=F32):
        return pltpu.VMEM(dims, kind)

    def sems(*dims):
        return [pltpu.SemaphoreType.DMA(dims), pltpu.SemaphoreType.DMA(dims)]

    scratch = [
        vm(n_blk, 3, rows, HSAC, kind=BF16),
        vm(n_dp, n_dp, CAP, kind=jnp.int32),
        vm(n_dp, n_dp, CAP, kind=jnp.int32),
        vm(n_blk, drows, HDYN),
        vm(n_blk, drows, HDYN),
        vm(n_blk, rows, HSAC),
        vm(lay.n_dev, 48, lay.width),
        vm(56, lay.batch),
        vm(2, 8, lay.batch),
        vm(5, 32, HSAC),
        vm(5, HSAC, 32, kind=BF16),
        vm(2, 16, HSAC, kind=BF16),
        vm(5, HSAC, HSAC, kind=BF16),
        vm(3, HSAC, HSAC, kind=BF16),
        vm(5, 16, HSAC, kind=BF16),
        vm(HSAC, 16, kind=BF16),
        vm(16, HSAC),
        vm(8, HSAC),
        vm(HSAC, 8),
        vm(128, 8),
        vm(3, HSAC + 16, HSAC),
        vm(3, 32, HSAC),
        vm(2, 16, HSAC),
        vm(16, HSAC),
        vm(16, 48),
        vm(8, TILE),
        vm(n_dp, lay.chunks[0], 8, 128),
        vm(n_dp, lay.chunks[1], 8, 128),
        vm(n_blk, lay.part(0), 8, 128),
        vm(n_blk, lay.part(1), 8, 128),
        vm(lay.chunks[0], 8, 128),
        vm(lay.chunks[1], 8, 128),
        vm(n_dp, lay.mat, 8, 128),
        vm(HSAC, HSAC),
        vm(HSAC, HSAC),
        vm(HSAC, 8),
        vm(HSAC + 16, HSAC),
        vm(32, HSAC),
        vm(48, HSAC),
        vm(16, 48),
        vm(2, 24, TILE),
        vm(8, TILE),
        vm(48, TILE),
        vm(HSAC, HSAC),
        vm(D_ROWS, HSAC),
        vm(drows, HDYN),
        vm(drows, HDYN),
        vm(1, NB),
        vm(48, HSAC, kind=BF16),
        vm(HSAC, 48, kind=BF16),
    ]
    scratch += [vm(n_dp >> (s + 1), chunk, 8, 128) for chunk in lay.chunks for s in range(bits)]
    scratch += sems(2, n_blk)
    scratch += sems(n_dp) + sems(n_dp)
    scratch += sems(n_blk) + sems(n_blk) + sems(n_blk)
    scratch += sems(n_blk) + sems(n_dp) + sems(n_dp)
    scratch += sems(2, bits) + sems(2, n_blk) + sems(2, n_blk) + sems(n_dp)
    scratch += [pltpu.SemaphoreType.DMA((3,)), pltpu.SemaphoreType.DMA((n_dp,))]
    scratch += sems(n_dp) + sems(n_dp) + sems(n_dp)
    scratch += 3 * [pltpu.SemaphoreType.DMA((n_dp,))]
    scratch += 2 * [pltpu.SemaphoreType.DMA((n_dp,)), pltpu.SemaphoreType.DMA((3,))]
    varying = 4 * (lay.n_dev * 48 * lay.width + 72 * lay.batch + 48 * lay.replay)
    gathered = pl.pallas_call(
        functools.partial(main_kernel, lay),
        out_shape=out_shape,
        in_specs=[spec] * len(inputs),
        out_specs=[spec] * len(out_shape),
        scratch_shapes=scratch,
        compiler_params=pltpu.CompilerParams(
            collective_id=0, has_side_effects=True, vmem_limit_bytes=14 * 2**20 + 2 * varying
        ),
        name="step",
    )(*[pltpu.with_memory_space_constraint(value, pltpu.HBM) for value in inputs])
    params = (
        sac_hidden, sac_hidden_mom, dyn_hidden, dyn_hidden_mom,
        flip(crit_in), flip(crit_in_m), flip(crit_in_v), act_in, act_in_m, act_in_v,
        dyn_in, dyn_in_m, dyn_in_v, crit_out, crit_out_m, crit_out_v,
        swap(act_out), swap(act_out_m), swap(act_out_v),
        swap(dyn_out), swap(dyn_out_m), swap(dyn_out_v), biases, biases_m, biases_v,
    )
    new_shape = [shape(value.shape, F32) for value in params]
    new_shape += [shape((1, 1), F32)] * 2
    out = pl.pallas_call(
        update_kernel,
        out_shape=tuple(new_shape),
        in_specs=[spec] * (len(gathered) + len(params)),
        out_specs=[spec] * len(new_shape),
        scratch_shapes=[vm(1, NB)],
        compiler_params=pltpu.CompilerParams(vmem_limit_bytes=16 * 2**20),
        name="update",
    )(*[kept(value) for value in gathered], *params)
    out = list(out)
    for at in (4, 5, 6):
        out[at] = flip(out[at])
    for at in (16, 17, 18, 19, 20, 21):
        out[at] = swap(out[at])
    for at in (25, 26):
        out[at] = out[at].reshape(())
    return tuple(out)


def solution(mesh):
    both = ("dp", "blk")
    sharded = (
        P(None, both), P(None, both), P(both, None), P(both, None), P(both), P(None, both, None),
    )
    hidden = (P(None, "blk", None),) * 4

    def step(replay, model_rows, *others):
        lay = Layout(mesh, replay.shape[1], model_rows.shape[1])
        return shards(lay, replay, model_rows, *others)

    return jax.shard_map(
        step,
        mesh=mesh,
        in_specs=sharded + hidden + (P(),) * 25,
        out_specs=hidden + (P(),) * 23,
        check_vma=False,
    )
```

```python
import functools
import math

import jax
import jax.numpy as jnp
from jax import lax
from jax.experimental import pallas as pl
from jax.experimental.pallas import tpu as pltpu
from jax.sharding import PartitionSpec as P

OBS = 17
ACT = 6
IN = OBS + ACT
FEAT = 42
HDYN = 200
HSAC = 256
MEMBERS = 7
DOUT = 36
HALF = DOUT // 2
NB = 4639
NS_ITERS = 5
STEP = 10
CAP = 8
TILE = 256
ROWS = 32

DISCOUNT = 0.99
TARGET_ENTROPY = -6.0
BOUND_WEIGHT = 0.01
MOMENTUM = 0.95
MUON_RATE = 0.4
MUON_DECAY = 0.01
ADAM_RATE = 0.1
ADAM_DECAY = 0.01
BETA_FIRST = 0.9
BETA_SECOND = 0.999
COEF_LINEAR = 3.4445
COEF_CUBIC = -4.775
COEF_QUINTIC = 2.0315

CB1, CB2, CB3, AB1, AB2, AB3 = 0, 512, 1024, 1026, 1282, 1538
DB1, DB2, DB3, MAXLV, MINLV, LOGA = 1550, 2950, 4350, 4602, 4620, 4638

R_IN, R_HEAD, R_OUT, R_MISC, R_SMALL = 0, 72, 88, 96, 128
D_IN, D_OUT, D_B2, D_B3, D_UP, D_LOW, D_LOSS, D_ROWS = 0, 24, 60, 61, 62, 63, 64, 72

F32, BF16 = jnp.float32, jnp.bfloat16
MESH = pl.DeviceIdType.MESH
NN = (((1,), (0,)), ((), ()))
NT = (((1,), (1,)), ((), ()))


def dot(a, b, dims=NN):
    return lax.dot_general(a, b, dims, preferred_element_type=F32)


def rounded(v):
    return v.astype(BF16).astype(F32)


def pieces(v):
    high = v.astype(BF16)
    rest = v - high.astype(F32)
    middle = rest.astype(BF16)
    return high, middle, (rest - middle.astype(F32)).astype(BF16)


def split(v):
    high = v.astype(BF16)
    return high, (v - high.astype(F32)).astype(BF16)


def product(a, b, dims=NN):
    left = jnp.concatenate([a[0], a[0], a[1]], 1)
    return dot(left, jnp.concatenate([b[0], b[1], b[0]], dims[0][1][0]), dims)


def softplus(v):
    return jnp.maximum(v, 0.0) + jnp.log1p(jnp.exp(-jnp.abs(v)))


def sigmoid(v):
    return 0.5 + 0.5 * jnp.tanh(0.5 * v)


def gate(half):
    up = 1.0 + jnp.tanh(half)
    value = half * up
    return value, up + value * (2.0 - up)


def by_rows(body, *arrays):
    done = [
        body(*[array[at : at + ROWS] for array in arrays]) for at in range(0, arrays[0].shape[0], ROWS)
    ]
    return [jnp.concatenate(parts, 0) for parts in zip(*done)]


def twice(column):
    return jnp.concatenate([column] * (TILE // 128), 1)


def gated(half, column=None):
    def body(part, *offset):
        value, slope = gate(part + twice(offset[0]) if offset else part)
        return value.astype(BF16), slope

    return by_rows(body, half, *([] if column is None else [column]))


def sloped(grad, slope):
    return by_rows(lambda part, by: ((part * by).astype(BF16),), grad, slope)[0]


def outer_sloped(column, row, slope):
    return by_rows(lambda part, by: (((twice(part) * row) * by).astype(BF16),), column, slope)[0]


def rows_of(shape):
    return lax.broadcasted_iota(jnp.int32, shape, 0)


def schulz(refs, steps):
    @pl.loop(0, steps)
    def _(step):
        matrices = [ref[...] for ref in refs]
        parts = [split(matrix) for matrix in matrices]
        grams = [product(part, part, NT) for part in parts]
        halves = [split(gram) for gram in grams]
        squares = [product(half, half) for half in halves]
        blends = [
            split(COEF_CUBIC * gram + COEF_QUINTIC * square) for gram, square in zip(grams, squares)
        ]
        moved = [product(blend, part) for blend, part in zip(blends, parts)]
        for ref, matrix, move in zip(refs, matrices, moved):
            ref[...] = COEF_LINEAR * matrix + move


def normalise(ref):
    moment = ref[...]
    norm = jnp.sqrt(jnp.sum(jnp.sum(moment * moment, axis=1, keepdims=True), axis=0, keepdims=True))
    ref[...] = moment / (norm + 1e-7)


class Layout:
    def __init__(self, mesh, replay, model):
        self.n_dp = mesh.shape["dp"]
        self.n_blk = mesh.shape["blk"]
        self.bits = int(math.log2(self.n_dp))
        self.n_dev = self.n_dp * self.n_blk
        self.replay = replay
        self.model = model
        self.real = self.n_dp * CAP
        self.batch = self.real + model
        self.width = -(-(self.real + 2) // 128) * 128
        self.rows = HSAC // self.n_blk
        self.drows = HDYN // self.n_blk
        self.mat = 64 // self.n_dp
        self.sml = 32 // self.n_dp
        self.chunks = (2 * self.mat, self.mat + self.sml)
        self.split_z = all(chunk % self.n_blk == 0 for chunk in self.chunks)
        self.owners = [self.n_dp - 5, self.n_dp - 3, self.n_dp - 1]

    def part(self, group):
        return self.chunks[group] // self.n_blk if self.split_z else self.chunks[group]


def main_kernel(lay, *refs):
    (
        replay, model, requests, member, live, noise, sac_h, sac_m, dyn_h, dyn_m, crit_in, act_in,
        dyn_in, crit_out, act_out, dyn_out, biases, targ_in, targ_hidden, targ_out, targ_bias,
        sac_g, sac_x, dyn_g, dyn_x, dyn_s, small, count,
        wg, asked, owned, dhg, dmg, smg, bk, xs, nz, w1f, w1t, w1n, w2t, w2h, heads, head_t, head_f,
        rowbuf, wide, headcol, acc_h, acc_w, acc_c, acc_a, acc_m, acc_l, grid_c, grid_a, zr_c, zr_a,
        zf_c, zf_a, mg, mat, grow, dcols, dacc_h, dacc_w, dacc_o, dacc_m, dacc_b, dacc_l, xt, dmat,
        dpack, drow_g, drow_x, bias, dhead, dhead_t, *rest,
    ) = refs
    bits = lay.bits
    bufs = (rest[:bits], rest[bits : 2 * bits])
    (
        s_w, r_w, s_q, r_q, s_p, r_p, s_dh, r_dh, s_dm, r_dm, s_sm, r_sm, s_bz, r_bz, s_bo, r_bo,
        s_bp, r_bp, s_rs, r_rs, s_zr, r_zr, s_za, r_za, s_pl, r_pl, s_mg, r_mg, s_ds, r_ds, s_dg,
        r_dg, s_dx, r_dx, f_ds, f_dg, f_dx, s_sg, r_sg, s_sx, r_sx,
    ) = rest[2 * bits :]
    grids, zrs, zfs = (grid_c, grid_a), (zr_c, zr_a), (zf_c, zf_a)
    n_dp, n_blk = lay.n_dp, lay.n_blk
    me = lax.axis_index("dp")
    z = lax.axis_index("blk")
    core = lax.rem(me, 2)
    sibling = me + 1 - 2 * core
    is_dyn = me < MEMBERS
    dyn_e = jnp.minimum(me, MEMBERS - 1)
    is_actor = me == lay.owners[2]
    is_critic = jnp.logical_or(me == lay.owners[0], me == lay.owners[1])
    is_sac = jnp.logical_or(is_actor, is_critic)
    sac_k = jnp.clip((me - lay.owners[0]) // 2, 0, 2)

    def on_plane(src, dst, ssem, rsem, peer):
        return pltpu.make_async_remote_copy(
            src_ref=src, dst_ref=dst, send_sem=ssem, recv_sem=rsem,
            device_id={"dp": peer}, device_id_type=MESH,
        )

    def on_line(src, dst, ssem, rsem, peer):
        return pltpu.make_async_remote_copy(
            src_ref=src, dst_ref=dst, send_sem=ssem, recv_sem=rsem,
            device_id={"blk": peer}, device_id_type=MESH,
        )

    def plane_peers(body):
        @pl.loop(1, n_dp)
        def _(off):
            body(lax.rem(me + off, n_dp))

    def like_peers(body):
        @pl.loop(1, n_dp // 2)
        def _(off):
            body(lax.rem(me + 2 * off, n_dp))

    def line_peers(body):
        @pl.loop(1, n_blk)
        def _(off):
            body(lax.rem(z + off, n_blk))

    barrier = pltpu.get_barrier_semaphore()
    plane_peers(lambda peer: pl.semaphore_signal(barrier, inc=1, device_id={"dp": peer}, device_id_type=MESH))
    line_peers(lambda peer: pl.semaphore_signal(barrier, inc=1, device_id={"blk": peer}, device_id_type=MESH))
    wg[z] = sac_h[...].astype(BF16)
    pl.semaphore_wait(barrier, n_dp - 1 + n_blk - 1)

    def hidden_copy(owner, part, peer):
        at = (2, 1) if part == 0 else (0, 2)
        view = wg.at[owner, pl.ds(*at)]
        return on_line(view, view, s_w.at[part, peer], r_w.at[part, owner], peer)

    line_peers(lambda peer: hidden_copy(z, 0, peer).start())

    def list_copy(owner, peer):
        return on_plane(requests, asked.at[owner], s_q.at[peer], r_q.at[owner], peer)

    def member_copy(owner, peer):
        return on_plane(member, owned.at[owner], s_p.at[peer], r_p.at[owner], peer)

    plane_peers(lambda peer: list_copy(me, peer).start())
    plane_peers(lambda peer: member_copy(me, peer).start())
    line_peers(lambda peer: hidden_copy(z, 1, peer).start())
    asked[me] = requests[...]
    owned[me] = member[...]

    def dyn_h_copy(owner, peer):
        return on_line(dyn_h.at[dyn_e], dhg.at[owner], s_dh.at[peer], r_dh.at[owner], peer)

    def dyn_m_copy(owner, peer):
        return on_line(dyn_m.at[dyn_e], dmg.at[owner], s_dm.at[peer], r_dm.at[owner], peer)

    def sac_m_copy(owner, peer):
        return on_line(sac_m.at[sac_k], smg.at[owner], s_sm.at[peer], r_sm.at[owner], peer)

    alive = live[...].astype(F32).reshape(1, lay.model)
    bias[...] = biases[...].reshape(1, NB)
    xs[42:56, :] = jnp.zeros((14, lay.batch), F32)
    xs[0:FEAT, lay.real : lay.batch] = model[...]
    xs[42:43, lay.real : lay.batch] = alive
    nz[...] = jnp.zeros_like(nz)
    for which in range(2):
        nz[which, 1:7, :] = noise[:, which, :]
    firsts = [
        (targ_in[:, 0, :], targ_bias[0:1, 0:HSAC]),
        (targ_in[:, 1, :], targ_bias[1:2, 0:HSAC]),
        (crit_in[:, 0, :], bias[:, CB1 : CB1 + HSAC]),
        (crit_in[:, 1, :], bias[:, CB1 + HSAC : CB1 + 2 * HSAC]),
        (act_in[...], bias[:, AB1 : AB1 + HSAC]),
    ]
    w1f[...] = jnp.zeros_like(w1f)
    for net, (weights, offset) in enumerate(firsts):
        w1f[net, 0 : weights.shape[0], :] = rounded(weights)
        for at, piece in enumerate(pieces(offset)):
            w1f[net, IN + at : IN + at + 1, :] = piece.astype(F32)
        w1t[net] = (0.5 * w1f[net].T).astype(BF16)
    for k in range(2):
        w1n[k] = w1f[2 + k, 16:32, :].astype(BF16)
    for net in range(2):
        w2t[net] = (0.5 * rounded(targ_hidden[net])).T.astype(BF16)
    rowbuf[...] = jnp.zeros_like(rowbuf)
    rowbuf[0:1, :] = targ_bias[0:1, HSAC : 2 * HSAC]
    rowbuf[1:2, :] = targ_bias[1:2, HSAC : 2 * HSAC]
    rowbuf[2:3, :] = bias[:, CB2 : CB2 + HSAC]
    rowbuf[3:4, :] = bias[:, CB2 + HSAC : CB2 + 2 * HSAC]
    rowbuf[4:5, :] = bias[:, AB2 : AB2 + HSAC]
    rowbuf[5:7, :] = rounded(crit_out[...])
    columns = 0.5 * rowbuf[...].T
    for at in range(7):
        wide[at] = jnp.broadcast_to(columns[:, at : at + 1], (HSAC, 128))
    rowbuf[...] = jnp.zeros_like(rowbuf)
    rowbuf[0:1, 1:7] = bias[:, AB3 : AB3 + ACT]
    rowbuf[0:1, 9:15] = bias[:, AB3 + ACT : AB3 + 2 * ACT]
    headcol[...] = rowbuf[:, 0:128].T
    head_f[...] = jnp.zeros_like(head_f)
    for k in range(2):
        head_f[0:1, :] = targ_out[k : k + 1, :]
        heads[k] = head_f[...].astype(BF16)
        head_f[0:1, :] = crit_out[k : k + 1, :]
        heads[2 + k] = head_f[...].astype(BF16)
    head_f[0:1, :] = jnp.zeros((1, HSAC), F32)
    head_f[1:7, :] = act_out[0:ACT, :]
    head_f[9:15, :] = act_out[ACT : 2 * ACT, :]
    heads[4] = head_f[...].astype(BF16)
    head_t[...] = (0.5 * rounded(head_f[...])).T.astype(BF16)
    for ref in (acc_h, acc_w, acc_c, acc_a, acc_m, acc_l):
        ref[...] = jnp.zeros_like(ref)

    data = replay[...]
    sums = jnp.sum(data[0:24], axis=1, keepdims=True)
    squares = jnp.sum(data[0:24] * data[0:24], axis=1, keepdims=True)
    living = jnp.sum(alive, axis=1, keepdims=True)

    def wait_lists(peer):
        list_copy(peer, peer).wait_recv()
        member_copy(peer, peer).wait_recv()

    plane_peers(wait_lists)
    spread = (
        lax.rem(lax.broadcasted_iota(jnp.int32, (CAP, lay.real), 1), CAP)
        == lax.broadcasted_iota(jnp.int32, (CAP, lay.real), 0)
    ).astype(F32)
    here = (
        lax.broadcasted_iota(jnp.int32, (n_dp, lay.real), 1) // CAP
        == lax.broadcasted_iota(jnp.int32, (n_dp, lay.real), 0)
    )

    def in_lanes(ref):
        lists = ref[:, me, :].astype(F32)
        wide = lax.dot_general(
            lists, spread, NN, precision=lax.Precision.HIGHEST, preferred_element_type=F32
        )
        return jnp.sum(jnp.where(here, wide, 0.0), axis=0, keepdims=True)

    slots = in_lanes(asked)
    wanted = jnp.maximum(slots, 0.0).astype(jnp.int32)
    hot = (rows_of((lay.replay, lay.real)) == wanted).astype(BF16)
    high, middle, low = pieces(data)
    picked = dot(high, hot) + dot(middle, hot) + dot(low, hot)
    mine = me * n_blk
    bk[mine, 0:FEAT, 0 : lay.real] = picked
    bk[mine, 42:43, 0 : lay.real] = (slots >= 0.0).astype(F32)
    bk[mine, 43:44, 0 : lay.real] = in_lanes(owned)
    bk[mine, 44:48, 0 : lay.real] = jnp.zeros((4, lay.real), F32)
    bk[mine, :, lay.real : lay.width] = jnp.zeros((48, lay.width - lay.real), F32)
    bk[mine, 0:24, lay.real : lay.real + 1] = sums
    bk[mine, 0:24, lay.real + 1 : lay.real + 2] = squares
    bk[mine, 24:25, lay.real : lay.real + 1] = living

    def slot_of(block):
        line = lax.rem(block, n_blk)
        return block - line + lax.rem(line - z + n_blk, n_blk)

    def block_line(owner, peer):
        slot = me * n_blk + lax.rem(owner - peer + n_blk, n_blk)
        return on_line(bk.at[mine], bk.at[slot], s_bz.at[peer], r_bz.at[owner], peer)

    def block_arrives(owner):
        slot = me * n_blk + lax.rem(owner - z + n_blk, n_blk)
        on_line(bk.at[mine], bk.at[slot], s_bz.at[owner], r_bz.at[owner], owner).wait_recv()

    def block_own(owner, peer):
        view = bk.at[owner * n_blk]
        return on_plane(view, view, s_bo.at[peer], r_bo.at[owner], peer)

    def block_plane(owner, peer):
        view = bk.at[pl.ds(owner * n_blk + 1, n_blk - 1)]
        return on_plane(view, view, s_bp.at[peer], r_bp.at[owner], peer)

    plane_peers(lambda peer: block_own(me, peer).start())
    line_peers(lambda peer: block_line(z, peer).start())

    @pl.when(is_dyn)
    def _():
        line_peers(lambda peer: dyn_h_copy(z, peer).start())
        line_peers(lambda peer: dyn_m_copy(z, peer).start())

    @pl.when(is_sac)
    def _():
        line_peers(lambda peer: sac_m_copy(z, peer).start())

    def wait_hidden(peer):
        hidden_copy(peer, 0, peer).wait_recv()
        hidden_copy(peer, 1, peer).wait_recv()

    line_peers(wait_hidden)
    for k in range(3):
        for block in range(n_blk):
            w2h[k, block * lay.rows : (block + 1) * lay.rows, :] = (
                0.5 * wg[block, k].astype(F32)
            ).astype(BF16)
        w2t[2 + k] = w2h[k].astype(F32).T.astype(BF16)

    log_alpha = bias[:, LOGA : LOGA + 1]
    alpha = jnp.exp(log_alpha)
    last = [
        targ_bias[0:1, 2 * HSAC : 2 * HSAC + 1],
        targ_bias[1:2, 2 * HSAC : 2 * HSAC + 1],
        bias[:, CB3 : CB3 + 1],
        bias[:, CB3 + 1 : CB3 + 2],
    ]
    n_tiles = lay.batch // TILE
    row8 = rows_of((8, TILE))
    act_rows = jnp.logical_and(row8 >= 1, row8 < 1 + ACT)

    def place_of(step):
        return pl.ds(pl.multiple_of(lax.rem(step + 1, n_tiles) * TILE, TILE), TILE)

    def ones16():
        return jnp.ones((16, TILE), BF16)

    def framed(first_row, used, where):
        row32 = rows_of((32, TILE))
        ones3 = jnp.logical_and(row32 >= IN, row32 < IN + 3).astype(F32)
        return jnp.where(row32 < used, xs[first_row : first_row + 32, where], ones3)

    def hidden(inputs, net):
        first, slope1 = gated(dot(w1t[net], inputs))
        second, slope2 = gated(dot(w2t[net], first), wide[net])
        return first, slope1, second, slope2

    def policy(inputs, which, where):
        first, slope1, second, slope2 = hidden(inputs, 4)
        out = dot(heads[4], second) + headcol[0:16, 0:1]
        bent = jnp.tanh(out[8:16])
        log_scale = -5.0 + 3.5 * (bent + 1.0)
        draw = nz[which, :, where]
        moved = jnp.exp(log_scale) * draw
        latent = out[0:8] + moved
        terms = (
            -0.5 * draw * draw
            - log_scale
            - 0.9189385
            - 2.0 * (0.6931472 - latent - softplus(-2.0 * latent))
        )
        log_prob = jnp.sum(jnp.where(act_rows, terms, 0.0), axis=0, keepdims=True)
        action = jnp.where(act_rows, jnp.tanh(latent), 0.0)
        return action, log_prob, bent, moved, (first, slope1, second, slope2)

    def with_action(inputs, action):
        middle_rows = jnp.where(act_rows, action, inputs[16:24])
        return jnp.concatenate([inputs[0:16], middle_rows, inputs[24:32]], 0).astype(BF16)

    def critic(inputs, net):
        kept = hidden(inputs, net)
        value = dot(heads[net], kept[2])[0:1] + last[net]
        return value, kept

    def add_hidden(k, first, grad):
        acc_h[k] += dot(jnp.concatenate([first, ones16()], 0), grad, NT)

    @pl.loop(0, n_tiles)
    def _(step):
        @pl.when(step == 1)
        def _():
            line_peers(block_arrives)
            plane_peers(lambda peer: block_plane(me, peer).start())

        @pl.when(step == n_tiles - 1)
        def _():
            plane_peers(lambda peer: block_own(peer, peer).wait_recv())
            lanes = lax.broadcasted_iota(jnp.int32, (48, lay.width), 1) // CAP

            def gather(owner, total):
                turned = pltpu.roll(
                    bk[owner * n_blk], lax.rem((owner - me) * CAP + lay.width, lay.width), axis=1
                )
                return jnp.where(lanes == owner, turned, total)

            own = lax.fori_loop(0, n_dp, gather, jnp.zeros((48, lay.width), F32))
            xs[0:48, 0 : lay.real] = own[:, 0 : lay.real]

        where = place_of(step)
        now_in = framed(0, IN, where).astype(BF16)
        next_f = framed(24, OBS, where)
        reward = xs[23:24, where]
        done = xs[41:42, where]
        weight = xs[42:43, where]
        row16 = rows_of((16, TILE))
        next_action, next_prob, _, _, _ = policy(next_f.astype(BF16), 1, where)
        aim_in = with_action(next_f, next_action)
        aim = jnp.minimum(critic(aim_in, 0)[0], critic(aim_in, 1)[0])
        target = reward + DISCOUNT * (1.0 - done) * (aim - alpha * next_prob)
        loss = jnp.zeros((1, TILE), F32)
        heads_grad = []
        for k in range(2):
            value, (c1, dc1, c2, dc2) = critic(now_in, 2 + k)
            miss = value - target
            loss += 0.5 * miss * miss
            g3 = rounded(weight * miss)
            g3_rows = jnp.where(row16 == 0, g3, 0.0).astype(BF16)
            heads_grad.append(g3_rows)
            acc_c[k] += dot(g3_rows, c2, NT)
            g2 = outer_sloped(wide[5 + k], g3, dc2)
            add_hidden(k, c1, g2)
            g1 = sloped(dot(w2h[k], g2), dc1)
            acc_w[k] += dot(now_in, g1, NT)
        acc_m[:, 16:48] += dot(ones16(), jnp.concatenate(heads_grad, 0), NT)
        acc_l[0:1, :] += weight * loss

    def put_matrix(group, k, at):
        for chunk in range(n_dp):
            tile = chunk * lay.mat
            side, row = tile // 32, tile % 32
            grids[group][chunk, at * lay.mat : (at + 1) * lay.mat] = acc_h[
                k, row * 8 : (row + lay.mat) * 8, side * 128 : (side + 1) * 128
            ].reshape(lay.mat, 8, 128)

    def put(row, value):
        for at in range(value.shape[0] // 8):
            for side in range(value.shape[1] // 128):
                tile = side * (R_SMALL // 8) + row // 8 + at
                grid_a[tile // lay.sml, lay.mat + tile % lay.sml] = value[
                    at * 8 : at * 8 + 8, side * 128 : (side + 1) * 128
                ]

    def bit(b):
        return lax.rem(me // (1 << b), 2)

    starts, faces, partners = [], [], []
    start = 0
    for s in range(bits):
        if s == 0:
            face, stride = core, 1
        else:
            face = (1 - core) * bit(s) + core * bit(bits - s)
            stride = (1 - core) * (1 << s) + core * (1 << (bits - s))
        starts.append(start)
        faces.append(face)
        partners.append(me + (1 - 2 * face) * stride)
        start = start + face * (n_dp >> (s + 1))
    place = start

    def fold_copy(group, s):
        half = n_dp >> (s + 1)
        begin = starts[s] + (1 - faces[s]) * half
        return on_plane(
            grids[group].at[pl.ds(begin, half)], bufs[group][s], s_rs.at[group, s], r_rs.at[group, s],
            partners[s],
        )

    def fold_wait(group, s):
        half = n_dp >> (s + 1)
        begin = starts[s] + faces[s] * half
        fold_copy(group, s).wait_recv()
        for at in range(half):
            grids[group][begin + at] += bufs[group][s][at]

    def line_first(group, owner, peer):
        if lay.split_z:
            src = grids[group].at[place, pl.ds(peer * lay.part(group), lay.part(group))]
        else:
            src = grids[group].at[place]
        return on_line(src, zrs[group].at[owner], s_zr.at[group, peer], r_zr.at[group, owner], peer)

    def line_second(group, owner, peer):
        view = zfs[group].at[pl.ds(owner * lay.part(group), lay.part(group))]
        return on_line(view, view, s_za.at[group, peer], r_za.at[group, owner], peer)

    def line_start(group):
        line_peers(lambda peer: line_first(group, z, peer).start())

    def line_sum(group):
        part, zr, zf = lay.part(group), zrs[group], zfs[group]
        line_peers(lambda peer: line_first(group, peer, peer).wait_recv())
        zr[z] = grids[group][place, pl.ds(z * part, part)] if lay.split_z else grids[group][place]
        whole = zr[0]
        for block in range(1, n_blk):
            whole = whole + zr[block]
        if lay.split_z:
            zf[pl.ds(z * part, part)] = whole
            line_peers(lambda peer: line_second(group, z, peer).start())
        else:
            zf[...] = whole

    def line_end(group):
        if lay.split_z:
            line_peers(lambda peer: line_second(group, peer, peer).wait_recv())

    def tile_copy(k, owner):
        src = zfs[k // 2].at[pl.ds((k % 2) * lay.mat, lay.mat)]
        return on_plane(src, mg.at[place], s_mg.at[k], r_mg.at[place], owner)

    def send_tiles(group):
        for k in (0, 1) if group == 0 else (2,):
            @pl.when(me != lay.owners[k])
            def _():
                tile_copy(k, lay.owners[k]).start()

            @pl.when(me == lay.owners[k])
            def _():
                mg[place] = zfs[group][(k % 2) * lay.mat : (k % 2 + 1) * lay.mat]

    def small_copy(at, peer):
        return on_plane(
            zf_a.at[pl.ds(lay.mat, lay.sml)], small.at[pl.ds(at * lay.sml, lay.sml)],
            s_pl.at[peer], r_pl.at[at], peer,
        )

    def chain(group):
        steps = [functools.partial(lambda s: fold_copy(group, s).start(), 0)]

        def fold(s):
            fold_wait(group, s)
            if s + 1 < bits:
                fold_copy(group, s + 1).start()
            else:
                line_start(group)

        steps += [functools.partial(fold, s) for s in range(bits)]
        steps.append(lambda: line_sum(group))

        def finish():
            line_end(group)
            send_tiles(group)
            if group == 1:
                plane_peers(lambda peer: small_copy(place, peer).start())
                small[pl.ds(place * lay.sml, lay.sml)] = zf_a[lay.mat :]

        steps.append(finish)
        return steps

    critic_chain, actor_chain = chain(0), chain(1)
    for k in range(2):
        put_matrix(0, k, k)
    critic_chain[0]()

    inside = min(len(critic_chain) - 1, n_tiles - 1)

    @pl.loop(0, n_tiles)
    def _(step):
        for at in range(inside):
            @pl.when(step == at + 1)
            def _():
                critic_chain[at + 1]()

        where = place_of(step)
        now_f = framed(0, IN, where)
        now_in = now_f.astype(BF16)
        weight = xs[42:43, where]
        action, log_prob, bent, moved, (a1, da1, a2, da2) = policy(now_in, 0, where)
        judged_in = with_action(now_f, action)
        loss = alpha * log_prob - log_alpha * (log_prob + TARGET_ENTROPY)
        grad_action = jnp.zeros((8, TILE), F32)
        for k in range(2):
            judged, (_, df1, _, df2) = critic(judged_in, 2 + k)
            loss -= 0.5 * judged
            g2 = outer_sloped(wide[5 + k], -0.5 * weight, df2)
            g1 = sloped(dot(w2h[k], g2), df1)
            grad_action += dot(w1n[k], g1)[0:8]
        grad_latent = 2.0 * alpha * weight * action + grad_action * (1.0 - action * action)
        grad_scale = grad_latent * moved - alpha * weight
        grad_bent = grad_scale * 3.5 * (1.0 - bent * bent)
        g3 = jnp.concatenate(
            [jnp.where(act_rows, grad_latent, 0.0), jnp.where(act_rows, grad_bent, 0.0)], 0
        ).astype(BF16)
        acc_a[...] += dot(g3, a2, NT)
        acc_m[:, 0:16] += dot(ones16(), g3, NT)
        g2 = sloped(dot(head_t[...], g3), da2)
        add_hidden(2, a1, g2)
        g1 = sloped(dot(w2h[2], g2), da1)
        acc_w[2] += dot(now_in, g1, NT)
        acc_l[0:1, :] += weight * loss
        acc_l[1:2, :] += weight * (log_prob + TARGET_ENTROPY)

    for at in range(inside, len(critic_chain) - 1):
        critic_chain[at + 1]()
    put_matrix(1, 2, 0)
    for k in range(3):
        put(R_IN + 24 * k, acc_w[k, 0:24, :])
    put(R_HEAD, acc_a[...])
    rowbuf[0:1, :] = acc_c[0, 0:1, :]
    rowbuf[1:2, :] = acc_c[1, 0:1, :]
    for k in range(3):
        rowbuf[2 + k : 3 + k, :] = acc_h[k, HSAC : HSAC + 1, :]
    put(R_OUT, rowbuf[...])
    folded = jnp.sum(acc_l[...], axis=1, keepdims=True)
    rowbuf[...] = jnp.zeros_like(rowbuf)
    rowbuf[0:1, 0:48] = acc_m[0:1, :]
    rowbuf[0:1, 64:65] = folded[0:1]
    rowbuf[0:1, 65:66] = folded[1:2]
    put(R_MISC, rowbuf[...])
    put(R_MISC + 8, jnp.zeros((R_SMALL - R_MISC - 8, HSAC), F32))
    actor_chain[0]()

    plane_peers(lambda peer: block_plane(peer, peer).wait_recv())
    lane0 = lay.real // 128 * 128

    def add_block(at, carry):
        sides, fills = carry
        slot = slot_of(at)
        return sides + bk[slot, 0:32, lane0 : lane0 + 128], fills + bk[slot, 40:48, 0 : lay.real]

    sides, fills = lax.fori_loop(
        0, lay.n_dev, add_block, (jnp.zeros((32, 128), F32), jnp.zeros((8, lay.real), F32))
    )
    at = lay.real - lane0
    rows_all = float(lay.replay * lay.n_dev)
    centre = sides[0:24, at : at + 1] / rows_all
    scale = lax.rsqrt(sides[0:24, at + 1 : at + 2] / rows_all - centre * centre + 1e-6)
    total = sides[24:25, at : at + 1] + jnp.sum(fills[2:3, :], axis=1, keepdims=True)
    count[...] = jnp.broadcast_to(total, (8, 128))

    def dyn_bias(start, width):
        row = jnp.zeros((1, width), F32)
        for e in range(MEMBERS):
            row = jnp.where(me == e, bias[:, start + width * e : start + width * (e + 1)], row)
        return row

    @pl.when(is_dyn)
    def _():
        w1f[0] = jnp.zeros((32, HSAC), F32)
        w1f[0, 0:IN, 0:HDYN] = rounded(dyn_in[dyn_e])
        for at, piece in enumerate(pieces(dyn_bias(DB1, HDYN))):
            w1f[0, IN + at : IN + at + 1, 0:HDYN] = piece.astype(F32)
        w1t[0] = (0.5 * w1f[0].T).astype(BF16)
        rowbuf[...] = jnp.zeros_like(rowbuf)
        rowbuf[0:1, 0:HDYN] = dyn_bias(DB2, HDYN)
        head_row = dyn_bias(DB3, DOUT)
        rowbuf[1:2, 0:HALF] = head_row[:, 0:HALF]
        rowbuf[1:2, 24 : 24 + HALF] = head_row[:, HALF:DOUT]
        rowbuf[2:3, 0:HALF] = bias[:, MAXLV : MAXLV + HALF]
        rowbuf[3:4, 0:HALF] = bias[:, MINLV : MINLV + HALF]
        dcols[...] = rowbuf[...].T
        wide[0] = jnp.broadcast_to(0.5 * dcols[:, 0:1], (HSAC, 128))
        dpack[...] = jnp.zeros_like(dpack)
        dpack[0:HALF, 0:HDYN] = dyn_out[dyn_e, 0:HALF, :]
        dpack[24 : 24 + HALF, 0:HDYN] = dyn_out[dyn_e, HALF:DOUT, :]
        dhead[...] = dpack[0:48, :].astype(BF16)
        dhead_t[...] = (0.5 * rounded(dpack[0:48, :])).T.astype(BF16)
        dpack[...] = jnp.zeros_like(dpack)

        def wait_dyn(peer):
            dyn_h_copy(peer, peer).wait_recv()
            dyn_m_copy(peer, peer).wait_recv()

        line_peers(wait_dyn)
        dhg[z] = dyn_h[dyn_e]
        dmg[z] = dyn_m[dyn_e]
        dmat[...] = jnp.zeros_like(dmat)
        for block in range(n_blk):
            dmat[block * lay.drows : (block + 1) * lay.drows, 0:HDYN] = 0.5 * rounded(dhg[block])
        w2h[0] = dmat[...].astype(BF16)
        w2t[0] = dmat[...].T.astype(BF16)
        for ref in (dacc_h, dacc_w, dacc_o, dacc_m, dacc_b, dacc_l):
            ref[...] = jnp.zeros_like(ref)

    per = TILE // lay.real
    dyn_tiles = lay.n_dev // per
    gap = max(dyn_tiles // (bits + 1), 1)

    @pl.loop(0, dyn_tiles)
    def _(tile):
        for s in range(bits):
            @pl.when(tile == (s + 1) * gap)
            def _():
                actor_chain[s + 1]()

        @pl.when(is_dyn)
        def _():
            for at in range(per):
                slot = slot_of(tile * per + at)
                xt[:, at * lay.real : (at + 1) * lay.real] = bk[slot, :, 0 : lay.real]
            now = xt[0:24, :]
            later = xt[24:48, :]
            row24 = rows_of((24, TILE))
            scaled = jnp.where(row24 < IN, (now - centre) * scale, 1.0)
            inputs = jnp.concatenate([scaled, (row8 < 2).astype(F32)], 0).astype(BF16)
            first, slope1 = gated(dot(w1t[0], inputs))
            second, slope2 = gated(dot(w2t[0], first), wide[0])
            out = dot(dhead[...], second) + dcols[0:48, 1:2]
            used = row24 < HALF
            upper = dcols[0:24, 2:3]
            lower = dcols[0:24, 3:4]
            gap1 = upper - out[24:48]
            gap2 = upper - softplus(gap1) - lower
            log_var = lower + softplus(gap2)
            error = out[0:24] - jnp.where(row24 == OBS, now[23:24], later - now)
            inverse = jnp.exp(-log_var)
            weight = xt[42:43, :] * (xt[43:44, :] == me.astype(F32)).astype(F32)
            spread_term = error * error * inverse
            nll = jnp.sum(jnp.where(used, spread_term + log_var, 0.0), axis=0, keepdims=True)
            dacc_l[0:1, :] += weight * nll
            grad_mu = 2.0 * weight * error * inverse
            grad_lv = weight * (1.0 - spread_term)
            open1 = sigmoid(gap1)
            open2 = sigmoid(gap2)
            grad_lv1 = grad_lv * open2
            dacc_b[0] += jnp.where(used, grad_lv1 * (1.0 - open1), 0.0)
            dacc_b[1] += jnp.where(used, grad_lv * (1.0 - open2), 0.0)
            g3 = jnp.concatenate(
                [jnp.where(used, grad_mu, 0.0), jnp.where(used, grad_lv1 * open1, 0.0)], 0
            ).astype(BF16)
            dacc_o[...] += dot(g3, second, NT)
            dacc_m[...] += dot(ones16(), g3, NT)
            g2 = sloped(dot(dhead_t[...], g3), slope2)
            dacc_h[...] += dot(jnp.concatenate([first, ones16()], 0), g2, NT)
            g1 = sloped(dot(w2h[0], g2), slope1)
            dacc_w[...] += dot(inputs, g1, NT)

    def pack_copy(src, owner, ssem, peer):
        return on_plane(src, dyn_s.at[owner], ssem, r_ds.at[owner], peer)

    def dyn_g_copy(src, owner, ssem, peer):
        return on_plane(src, dyn_g.at[owner], ssem, r_dg.at[owner], peer)

    def dyn_x_copy(src, owner, ssem, peer):
        return on_plane(src, dyn_x.at[owner], ssem, r_dx.at[owner], peer)

    def give(copy, src, sems):
        like_peers(lambda peer: copy(src, dyn_e, sems.at[peer], peer).start())
        copy(src, dyn_e, sems.at[sibling], sibling).start()

    def given(copy, src, sems):
        like_peers(lambda peer: copy(src, dyn_e, sems.at[peer], peer).wait_send())
        copy(src, dyn_e, sems.at[sibling], sibling).wait_send()

    def from_like(body):
        def member_only(peer):
            @pl.when(peer < MEMBERS)
            def _():
                body(jnp.minimum(peer, MEMBERS - 1))

        like_peers(member_only)

    def hand_on(copy, out, sems):
        def body(owner):
            copy(out.at[owner], owner, sems.at[owner], sibling).wait_recv()
            copy(out.at[owner], owner, sems.at[owner], sibling).start()

        from_like(body)

    def handed_on(copy, out, sems):
        from_like(lambda owner: copy(out.at[owner], owner, sems.at[owner], sibling).wait_send())

    def from_sibling(copy, out, sems):
        @pl.loop(0, n_dp // 2)
        def _(off):
            owner = lax.rem(sibling + 2 * off, n_dp)

            @pl.when(owner < MEMBERS)
            def _():
                at = jnp.minimum(owner, MEMBERS - 1)
                copy(out.at[at], at, sems.at[at], sibling).wait_recv()

    def line_rows(ref):
        rows = ref[0 : lay.drows, 0:HDYN]
        for block in range(1, n_blk):
            rows = jnp.where(z == block, ref[block * lay.drows : (block + 1) * lay.drows, 0:HDYN], rows)
        return rows

    def sac_g_copy(k, peer):
        src = grow.at[pl.ds(pl.multiple_of(z * lay.rows, lay.rows), lay.rows)]
        return on_plane(src, sac_g.at[k], s_sg.at[peer], r_sg.at[k], peer)

    def sac_x_copy(k, peer):
        src = mat.at[pl.ds(pl.multiple_of(z * lay.rows, lay.rows), lay.rows)]
        return on_plane(src, sac_x.at[k], s_sx.at[peer], r_sx.at[k], peer)

    mine_rows = pl.ds(pl.multiple_of(z * lay.rows, lay.rows), lay.rows)

    def take_matrix():
        line_peers(lambda peer: sac_m_copy(peer, peer).wait_recv())
        smg[z] = sac_m[sac_k]

        @pl.loop(1, n_dp)
        def _(off):
            at = lax.rem(place + off, n_dp)
            on_plane(mg.at[at], mg.at[at], s_mg.at[0], r_mg.at[at], me).wait_recv()

        for chunk in range(n_dp):
            tile = chunk * lay.mat
            side, row = tile // 32, tile % 32
            grow[row * 8 : (row + lay.mat) * 8, side * 128 : (side + 1) * 128] = mg[chunk].reshape(
                lay.mat * 8, 128
            )
        sac_g[sac_k] = grow[mine_rows, :]
        plane_peers(lambda peer: sac_g_copy(sac_k, peer).start())
        for block in range(n_blk):
            at = slice(block * lay.rows, (block + 1) * lay.rows)
            mat[at, :] = MOMENTUM * smg[block] + grow[at, :] / total
        normalise(mat)

    @pl.when(is_dyn)
    def _():
        dpack[D_IN : D_IN + 24, :] = dacc_w[0:24, :]
        dpack[D_OUT : D_OUT + HALF, :] = dacc_o[0:HALF, :]
        dpack[D_OUT + HALF : D_OUT + DOUT, :] = dacc_o[24 : 24 + HALF, :]
        dpack[D_B2 : D_B2 + 1, :] = dacc_h[HSAC : HSAC + 1, :]
        dpack[D_B3 : D_B3 + 1, 0:48] = dacc_m[0:1, :]
        lanes = lax.broadcasted_iota(jnp.int32, (24, 128), 1)
        bound = jnp.where(
            lanes == 0,
            jnp.sum(dacc_b[0], axis=1, keepdims=True),
            jnp.where(lanes == 1, jnp.sum(dacc_b[1], axis=1, keepdims=True), 0.0),
        )
        dpack[D_UP : D_UP + 2, 0:24] = bound.T[0:2, :]
        dpack[D_LOSS : D_LOSS + 1, 0:128] = jnp.broadcast_to(
            jnp.sum(dacc_l[0:1, :], axis=1, keepdims=True), (1, 128)
        )
        dyn_s[dyn_e] = dpack[...]
        give(pack_copy, dpack, s_ds)
        rows = line_rows(dacc_h)
        drow_g[...] = rows
        dyn_g[dyn_e] = rows
        give(dyn_g_copy, drow_g, s_dg)
        dmat[...] = jnp.zeros_like(dmat)
        for block in range(n_blk):
            at = slice(block * lay.drows, (block + 1) * lay.drows)
            dmat[at, 0:HDYN] = MOMENTUM * dmg[block] + dacc_h[at, 0:HDYN] / total
        normalise(dmat)

    pl.when(is_critic)(take_matrix)
    if n_dp <= MEMBERS + 1:
        only_dyn = jnp.logical_and(is_dyn, jnp.logical_not(is_critic))
        pairs = [(is_critic, [dmat, mat]), (only_dyn, [dmat])]
    else:
        pairs = [(is_critic, [mat]), (is_dyn, [dmat])]
    for test, matrices in pairs:
        pl.when(test)(functools.partial(schulz, matrices, 2))
    actor_chain[bits + 1]()
    for test, matrices in pairs:
        pl.when(test)(functools.partial(schulz, matrices, 2))
    actor_chain[bits + 2]()
    for test, matrices in pairs:
        pl.when(test)(functools.partial(schulz, matrices, NS_ITERS - 4))

    def send_sac():
        sac_x[sac_k] = mat[mine_rows, :]
        plane_peers(lambda peer: sac_x_copy(sac_k, peer).start())

    @pl.when(is_dyn)
    def _():
        rows = line_rows(dmat)
        drow_x[...] = rows
        dyn_x[dyn_e] = rows
        give(dyn_x_copy, drow_x, s_dx)

    pl.when(is_critic)(send_sac)

    def sent_on_line(peer):
        hidden_copy(z, 0, peer).wait_send()
        hidden_copy(z, 1, peer).wait_send()
        block_line(z, peer).wait_send()
        for group in range(2):
            line_first(group, z, peer).wait_send()
            if lay.split_z:
                line_second(group, z, peer).wait_send()

        @pl.when(is_dyn)
        def _():
            dyn_h_copy(z, peer).wait_send()
            dyn_m_copy(z, peer).wait_send()

        @pl.when(is_sac)
        def _():
            sac_m_copy(z, peer).wait_send()

    def sent_on_plane(peer):
        list_copy(me, peer).wait_send()
        member_copy(me, peer).wait_send()
        block_own(me, peer).wait_send()
        block_plane(me, peer).wait_send()

    def sent_early():
        line_peers(sent_on_line)
        plane_peers(sent_on_plane)
        for group in range(2):
            for s in range(bits):
                fold_copy(group, s).wait_send()

    @pl.when(is_actor)
    def _():
        sent_early()
        take_matrix()
        schulz([mat], NS_ITERS)
        send_sac()

    pl.when(jnp.logical_not(is_actor))(sent_early)
    hand_on(pack_copy, dyn_s, f_ds)
    hand_on(dyn_g_copy, dyn_g, f_dg)
    hand_on(dyn_x_copy, dyn_x, f_dx)

    @pl.loop(1, n_dp)
    def _(off):
        small_copy(lax.rem(place + off, n_dp), me).wait_recv()

    from_sibling(pack_copy, dyn_s, f_ds)
    from_sibling(dyn_g_copy, dyn_g, f_dg)
    from_sibling(dyn_x_copy, dyn_x, f_dx)
    for k in range(3):
        @pl.when(me != lay.owners[k])
        def _():
            sac_g_copy(k, me).wait_recv()
            sac_x_copy(k, me).wait_recv()

    def sent_late(peer):
        small_copy(place, peer).wait_send()

        @pl.when(is_sac)
        def _():
            sac_g_copy(sac_k, peer).wait_send()
            sac_x_copy(sac_k, peer).wait_send()

    plane_peers(sent_late)

    @pl.when(is_dyn)
    def _():
        given(pack_copy, dpack, s_ds)
        given(dyn_g_copy, drow_g, s_dg)
        given(dyn_x_copy, drow_x, s_dx)

    handed_on(pack_copy, dyn_s, f_ds)
    handed_on(dyn_g_copy, dyn_g, f_dg)
    handed_on(dyn_x_copy, dyn_x, f_dx)
    for k in range(3):
        @pl.when(me != lay.owners[k])
        def _():
            tile_copy(k, lay.owners[k]).wait_send()


def adamw(weights, first, second, gradient):
    first = BETA_FIRST * first + (1.0 - BETA_FIRST) * gradient
    second = BETA_SECOND * second + (1.0 - BETA_SECOND) * gradient * gradient
    first_hat = first / (1.0 - BETA_FIRST**STEP)
    second_hat = second / (1.0 - BETA_SECOND**STEP)
    step = first_hat / (jnp.sqrt(second_hat) + 1e-8) + ADAM_DECAY * weights
    return weights - ADAM_RATE * step, first, second


def update_kernel(*refs):
    (
        sac_g, sac_x, dyn_g, dyn_x, dyn_s, small, count, sac_h, sac_m, dyn_h, dyn_m,
        ci, ci_m, ci_v, ai, ai_m, ai_v, di, di_m, di_v, co, co_m, co_v, ao, ao_m, ao_v,
        do, do_m, do_v, bi, bi_m, bi_v,
        sac_new, sac_mom, dyn_new, dyn_mom, ci_n, ci_mn, ci_vn, ai_n, ai_mn, ai_vn, di_n, di_mn,
        di_vn, co_n, co_mn, co_vn, ao_n, ao_mn, ao_vn, do_n, do_mn, do_vn, bi_n, bi_mn, bi_vn,
        loss, counted, bg,
    ) = refs
    total = count[0:1, 0:1]
    sac_mom[...] = MOMENTUM * sac_m[...] + sac_g[...] / total.reshape(1, 1, 1)
    sac_new[...] = sac_h[...] * (1.0 - MUON_RATE * MUON_DECAY) - MUON_RATE * sac_x[...]
    dyn_mom[...] = MOMENTUM * dyn_m[...] + dyn_g[...] / total.reshape(1, 1, 1)
    dyn_new[...] = dyn_h[...] * (1.0 - MUON_RATE * MUON_DECAY) - MUON_RATE * dyn_x[...]

    def rows(row, number):
        sides = []
        for side in range(2):
            at = side * (R_SMALL // 8) + row // 8
            sides.append(small[at : at + -(-number // 8)].reshape(-1, 128))
        return jnp.concatenate(sides, 1)

    def store(outs, at, values):
        for out, value in zip(outs, values):
            out[at] = value

    outs = (ci_n, ci_mn, ci_vn)
    for k in range(2):
        at = (slice(None), k, slice(None))
        grad = rows(R_IN + 24 * k, 24)
        bg[:, CB1 + HSAC * k : CB1 + HSAC * (k + 1)] = grad[IN : IN + 1]
        store(outs, at, adamw(ci[at], ci_m[at], ci_v[at], grad[0:IN] / total))
    grad = rows(R_IN + 48, 24)
    bg[:, AB1 : AB1 + HSAC] = grad[IN : IN + 1]
    store((ai_n, ai_mn, ai_vn), ..., adamw(ai[...], ai_m[...], ai_v[...], grad[0:OBS] / total))
    grad = rows(R_HEAD, 16)
    for at, row in ((slice(0, ACT), slice(1, 1 + ACT)), (slice(ACT, 2 * ACT), slice(9, 9 + ACT))):
        store((ao_n, ao_mn, ao_vn), at, adamw(ao[at], ao_m[at], ao_v[at], grad[row] / total))
    grad = rows(R_OUT, 8)
    store((co_n, co_mn, co_vn), ..., adamw(co[...], co_m[...], co_v[...], grad[0:2] / total))
    bg[:, CB2 : CB2 + HSAC] = grad[2:3]
    bg[:, CB2 + HSAC : CB2 + 2 * HSAC] = grad[3:4]
    bg[:, AB2 : AB2 + HSAC] = grad[4:5]
    grad = rows(R_MISC, 8)
    bg[:, CB3 : CB3 + 1] = grad[0:1, 16:17]
    bg[:, CB3 + 1 : CB3 + 2] = grad[0:1, 32:33]
    bg[:, AB3 : AB3 + ACT] = grad[0:1, 1 : 1 + ACT]
    bg[:, AB3 + ACT : AB3 + 2 * ACT] = grad[0:1, 9 : 9 + ACT]
    bg[:, LOGA : LOGA + 1] = -grad[0:1, 65:66]
    total_loss = grad[0:1, 64:65]
    up = jnp.zeros((1, HALF), F32)
    low = jnp.zeros((1, HALF), F32)
    for e in range(MEMBERS):
        pack = dyn_s[e]
        total_loss = total_loss + pack[D_LOSS : D_LOSS + 1, 0:1]
        up = up + pack[D_UP : D_UP + 1, 0:HALF]
        low = low + pack[D_LOW : D_LOW + 1, 0:HALF]
        bg[:, DB1 + HDYN * e : DB1 + HDYN * (e + 1)] = pack[IN : IN + 1, 0:HDYN]
        bg[:, DB2 + HDYN * e : DB2 + HDYN * (e + 1)] = pack[D_B2 : D_B2 + 1, 0:HDYN]
        bg[:, DB3 + DOUT * e : DB3 + DOUT * e + HALF] = pack[D_B3 : D_B3 + 1, 0:HALF]
        bg[:, DB3 + DOUT * e + HALF : DB3 + DOUT * (e + 1)] = pack[D_B3 : D_B3 + 1, 24 : 24 + HALF]
        grad = pack[0:IN, 0:HDYN] / total
        store((di_n, di_mn, di_vn), e, adamw(di[e], di_m[e], di_v[e], grad))
        grad = pack[D_OUT : D_OUT + DOUT, 0:HDYN] / total
        store((do_n, do_mn, do_vn), e, adamw(do[e], do_m[e], do_v[e], grad))
    bg[:, MAXLV : MAXLV + HALF] = up
    bg[:, MINLV : MINLV + HALF] = low
    lane = lax.broadcasted_iota(jnp.int32, (1, NB), 1)
    bounds = jnp.where(
        jnp.logical_and(lane >= MAXLV, lane < MINLV),
        BOUND_WEIGHT,
        jnp.where(jnp.logical_and(lane >= MINLV, lane < LOGA), -BOUND_WEIGHT, 0.0),
    )
    grad = bg[...] / total + bounds
    flat = [ref[...].reshape(1, NB) for ref in (bi, bi_m, bi_v)]
    store((bi_n, bi_mn, bi_vn), ..., [value.reshape(NB) for value in adamw(*flat, grad)])
    loss[...] = total_loss
    counted[...] = total


def shards(
    lay, replay, model_rows, requests, member_of, model_live, noise, sac_hidden, sac_hidden_mom,
    dyn_hidden, dyn_hidden_mom, crit_in, crit_in_m, crit_in_v, act_in, act_in_m, act_in_v, dyn_in,
    dyn_in_m, dyn_in_v, crit_out, crit_out_m, crit_out_v, act_out, act_out_m, act_out_v, dyn_out,
    dyn_out_m, dyn_out_v, biases, biases_m, biases_v, targ_in, targ_hidden, targ_out, targ_bias,
):
    n_dp, n_blk, bits = lay.n_dp, lay.n_blk, lay.bits
    spec = pl.BlockSpec(memory_space=pltpu.VMEM)

    def flip(value):
        return jnp.transpose(value, (1, 0, 2))

    def swap(value):
        return jnp.swapaxes(value, -1, -2)

    def kept(value):
        return pltpu.with_memory_space_constraint(value, pltpu.VMEM)

    inputs = (
        replay, model_rows, requests, member_of, model_live, jnp.transpose(noise, (2, 0, 1)),
        sac_hidden, sac_hidden_mom, dyn_hidden, dyn_hidden_mom, flip(crit_in), act_in, dyn_in,
        crit_out, swap(act_out), swap(dyn_out), biases, flip(targ_in), targ_hidden, targ_out,
        targ_bias,
    )
    shape = jax.ShapeDtypeStruct
    rows, drows = lay.rows, lay.drows
    out_shape = (
        pltpu.VMEM((3, rows, HSAC), F32),
        pltpu.VMEM((3, rows, HSAC), F32),
        pltpu.VMEM((MEMBERS, drows, HDYN), F32),
        pltpu.VMEM((MEMBERS, drows, HDYN), F32),
        pltpu.VMEM((MEMBERS, D_ROWS, HSAC), F32),
        pltpu.VMEM((32, 8, 128), F32),
        pltpu.VMEM((8, 128), F32),
    )

    def vm(*dims, kind=F32):
        return pltpu.VMEM(dims, kind)

    def sems(*dims):
        return [pltpu.SemaphoreType.DMA(dims), pltpu.SemaphoreType.DMA(dims)]

    scratch = [
        vm(n_blk, 3, rows, HSAC, kind=BF16),
        vm(n_dp, n_dp, CAP, kind=jnp.int32),
        vm(n_dp, n_dp, CAP, kind=jnp.int32),
        vm(n_blk, drows, HDYN),
        vm(n_blk, drows, HDYN),
        vm(n_blk, rows, HSAC),
        vm(lay.n_dev, 48, lay.width),
        vm(56, lay.batch),
        vm(2, 8, lay.batch),
        vm(5, 32, HSAC),
        vm(5, HSAC, 32, kind=BF16),
        vm(2, 16, HSAC, kind=BF16),
        vm(5, HSAC, HSAC, kind=BF16),
        vm(3, HSAC, HSAC, kind=BF16),
        vm(5, 16, HSAC, kind=BF16),
        vm(HSAC, 16, kind=BF16),
        vm(16, HSAC),
        vm(8, HSAC),
        vm(7, HSAC, 128),
        vm(128, 8),
        vm(3, HSAC + 16, HSAC),
        vm(3, 32, HSAC),
        vm(2, 16, HSAC),
        vm(16, HSAC),
        vm(16, 48),
        vm(8, TILE),
        vm(n_dp, lay.chunks[0], 8, 128),
        vm(n_dp, lay.chunks[1], 8, 128),
        vm(n_blk, lay.part(0), 8, 128),
        vm(n_blk, lay.part(1), 8, 128),
        vm(lay.chunks[0], 8, 128),
        vm(lay.chunks[1], 8, 128),
        vm(n_dp, lay.mat, 8, 128),
        vm(HSAC, HSAC),
        vm(HSAC, HSAC),
        vm(HSAC, 8),
        vm(HSAC + 16, HSAC),
        vm(32, HSAC),
        vm(48, HSAC),
        vm(16, 48),
        vm(2, 24, TILE),
        vm(8, TILE),
        vm(48, TILE),
        vm(HSAC, HSAC),
        vm(D_ROWS, HSAC),
        vm(drows, HDYN),
        vm(drows, HDYN),
        vm(1, NB),
        vm(48, HSAC, kind=BF16),
        vm(HSAC, 48, kind=BF16),
    ]
    scratch += [vm(n_dp >> (s + 1), chunk, 8, 128) for chunk in lay.chunks for s in range(bits)]
    scratch += sems(2, n_blk)
    scratch += sems(n_dp) + sems(n_dp)
    scratch += sems(n_blk) + sems(n_blk) + sems(n_blk)
    scratch += sems(n_blk) + sems(n_dp) + sems(n_dp)
    scratch += sems(2, bits) + sems(2, n_blk) + sems(2, n_blk) + sems(n_dp)
    scratch += [pltpu.SemaphoreType.DMA((3,)), pltpu.SemaphoreType.DMA((n_dp,))]
    scratch += sems(n_dp) + sems(n_dp) + sems(n_dp)
    scratch += 3 * [pltpu.SemaphoreType.DMA((n_dp,))]
    scratch += 2 * [pltpu.SemaphoreType.DMA((n_dp,)), pltpu.SemaphoreType.DMA((3,))]
    varying = 4 * (lay.n_dev * 48 * lay.width + 72 * lay.batch + 48 * lay.replay)
    gathered = pl.pallas_call(
        functools.partial(main_kernel, lay),
        out_shape=out_shape,
        in_specs=[spec] * len(inputs),
        out_specs=[spec] * len(out_shape),
        scratch_shapes=scratch,
        compiler_params=pltpu.CompilerParams(
            collective_id=0, has_side_effects=True, vmem_limit_bytes=14 * 2**20 + 2 * varying
        ),
        name="step",
    )(*[pltpu.with_memory_space_constraint(value, pltpu.HBM) for value in inputs])
    params = (
        sac_hidden, sac_hidden_mom, dyn_hidden, dyn_hidden_mom,
        flip(crit_in), flip(crit_in_m), flip(crit_in_v), act_in, act_in_m, act_in_v,
        dyn_in, dyn_in_m, dyn_in_v, crit_out, crit_out_m, crit_out_v,
        swap(act_out), swap(act_out_m), swap(act_out_v),
        swap(dyn_out), swap(dyn_out_m), swap(dyn_out_v), biases, biases_m, biases_v,
    )
    new_shape = [shape(value.shape, F32) for value in params]
    new_shape += [shape((1, 1), F32)] * 2
    out = pl.pallas_call(
        update_kernel,
        out_shape=tuple(new_shape),
        in_specs=[spec] * (len(gathered) + len(params)),
        out_specs=[spec] * len(new_shape),
        scratch_shapes=[vm(1, NB)],
        compiler_params=pltpu.CompilerParams(vmem_limit_bytes=16 * 2**20),
        name="update",
    )(*[kept(value) for value in gathered], *params)
    out = list(out)
    for at in (4, 5, 6):
        out[at] = flip(out[at])
    for at in (16, 17, 18, 19, 20, 21):
        out[at] = swap(out[at])
    for at in (25, 26):
        out[at] = out[at].reshape(())
    return tuple(out)


def solution(mesh):
    both = ("dp", "blk")
    sharded = (
        P(None, both), P(None, both), P(both, None), P(both, None), P(both), P(None, both, None),
    )
    hidden = (P(None, "blk", None),) * 4

    def step(replay, model_rows, *others):
        lay = Layout(mesh, replay.shape[1], model_rows.shape[1])
        return shards(lay, replay, model_rows, *others)

    return jax.shard_map(
        step,
        mesh=mesh,
        in_specs=sharded + hidden + (P(),) * 25,
        out_specs=hidden + (P(),) * 23,
        check_vma=False,
    )
```

```python
import functools
import math

import jax
import jax.numpy as jnp
from jax import lax
from jax.experimental import pallas as pl
from jax.experimental.pallas import tpu as pltpu
from jax.sharding import PartitionSpec as P

OBS = 17
ACT = 6
IN = OBS + ACT
FEAT = 42
HDYN = 200
HSAC = 256
MEMBERS = 7
DOUT = 36
HALF = DOUT // 2
NB = 4639
NS_ITERS = 5
STEP = 10
CAP = 8
TILE = 256
ROWS = 32

DISCOUNT = 0.99
TARGET_ENTROPY = -6.0
BOUND_WEIGHT = 0.01
MOMENTUM = 0.95
MUON_RATE = 0.4
MUON_DECAY = 0.01
ADAM_RATE = 0.1
ADAM_DECAY = 0.01
BETA_FIRST = 0.9
BETA_SECOND = 0.999
COEF_LINEAR = 3.4445
COEF_CUBIC = -4.775
COEF_QUINTIC = 2.0315

CB1, CB2, CB3, AB1, AB2, AB3 = 0, 512, 1024, 1026, 1282, 1538
DB1, DB2, DB3, MAXLV, MINLV, LOGA = 1550, 2950, 4350, 4602, 4620, 4638

R_IN, R_HEAD, R_OUT, R_MISC, R_SMALL = 0, 72, 88, 96, 128
D_IN, D_OUT, D_B2, D_B3, D_UP, D_LOW, D_LOSS, D_HID, D_ROWS = 0, 24, 60, 61, 62, 63, 64, 72, 128

F32, BF16 = jnp.float32, jnp.bfloat16
MESH = pl.DeviceIdType.MESH
NN = (((1,), (0,)), ((), ()))
NT = (((1,), (1,)), ((), ()))


def dot(a, b, dims=NN):
    return lax.dot_general(a, b, dims, preferred_element_type=F32)


def rounded(v):
    return v.astype(BF16).astype(F32)


def pieces(v):
    high = v.astype(BF16)
    rest = v - high.astype(F32)
    middle = rest.astype(BF16)
    return high, middle, (rest - middle.astype(F32)).astype(BF16)


def split(v):
    high = v.astype(BF16)
    return high, (v - high.astype(F32)).astype(BF16)


def product(a, b, dims=NN):
    left = jnp.concatenate([a[0], a[0], a[1]], 1)
    return dot(left, jnp.concatenate([b[0], b[1], b[0]], dims[0][1][0]), dims)


def softplus(v):
    return jnp.maximum(v, 0.0) + jnp.log1p(jnp.exp(-jnp.abs(v)))


def sigmoid(v):
    return 0.5 + 0.5 * jnp.tanh(0.5 * v)


def gate(half):
    up = 1.0 + jnp.tanh(half)
    value = half * up
    return value, up + value * (2.0 - up)


def by_rows(body, *arrays):
    done = [
        body(*[array[at : at + ROWS] for array in arrays]) for at in range(0, arrays[0].shape[0], ROWS)
    ]
    return [jnp.concatenate(parts, 0) for parts in zip(*done)]


def twice(column):
    return jnp.concatenate([column] * (TILE // 128), 1)


def gated(half, column=None):
    def body(part, *offset):
        value, slope = gate(part + twice(offset[0]) if offset else part)
        return value.astype(BF16), slope

    return by_rows(body, half, *([] if column is None else [column]))


def sloped(grad, slope):
    return by_rows(lambda part, by: ((part * by).astype(BF16),), grad, slope)[0]


def outer_sloped(column, row, slope):
    return by_rows(lambda part, by: (((twice(part) * row) * by).astype(BF16),), column, slope)[0]


def rows_of(shape):
    return lax.broadcasted_iota(jnp.int32, shape, 0)


def schulz(refs, steps):
    @pl.loop(0, steps)
    def _(step):
        matrices = [ref[...] for ref in refs]
        parts = [split(matrix) for matrix in matrices]
        grams = [product(part, part, NT) for part in parts]
        halves = [split(gram) for gram in grams]
        squares = [product(half, half) for half in halves]
        blends = [
            split(COEF_CUBIC * gram + COEF_QUINTIC * square) for gram, square in zip(grams, squares)
        ]
        moved = [product(blend, part) for blend, part in zip(blends, parts)]
        for ref, matrix, move in zip(refs, matrices, moved):
            ref[...] = COEF_LINEAR * matrix + move


def normalise(ref):
    moment = ref[...]
    norm = jnp.sqrt(jnp.sum(jnp.sum(moment * moment, axis=1, keepdims=True), axis=0, keepdims=True))
    ref[...] = moment / (norm + 1e-7)


class Layout:
    def __init__(self, mesh, replay, model):
        self.n_dp = mesh.shape["dp"]
        self.n_blk = mesh.shape["blk"]
        self.bits = int(math.log2(self.n_dp))
        self.n_dev = self.n_dp * self.n_blk
        self.replay = replay
        self.model = model
        self.real = self.n_dp * CAP
        self.batch = self.real + model
        self.width = -(-(self.real + 2) // 128) * 128
        self.rows = HSAC // self.n_blk
        self.drows = HDYN // self.n_blk
        self.mat = 64 // self.n_dp
        self.sml = 32 // self.n_dp
        self.chunks = (2 * self.mat, self.mat + self.sml)
        self.split_z = all(chunk % self.n_blk == 0 for chunk in self.chunks)
        self.owners = [self.n_dp - 5, self.n_dp - 3, self.n_dp - 1]

        groups = [("fold", g, s) for g in range(2) for s in range(self.bits)]
        groups += [(name, g) for name in ("first", "second") for g in range(2)]
        common = ["hidden", "hidden on", "lists", "own", "line", "plane", "dyn h", "dyn m", "sac m", "small"]
        common += groups
        kinds = [(name, kind) for name in ("pack", "x") for kind in ("own", "on")]
        sent = common + [("tiles", k) for k in range(3)] + kinds
        self.sent = {name: at for at, name in enumerate(sent)}
        self.sent["sac g"] = len(sent)
        self.sent["sac x"] = len(sent) + self.n_dp
        self.departures = len(sent) + 2 * self.n_dp
        self.here, self.arrivals = {}, 0
        for name in common + ["tiles", ("pack", "sibling"), ("x", "sibling")]:
            self.here[name] = self.arrivals
            self.arrivals += 1
        for name, number in (("sac g", 3), ("sac x", 3), (("pack", "like"), MEMBERS), (("x", "like"), MEMBERS)):
            self.here[name] = self.arrivals
            self.arrivals += number

    def part(self, group):
        return self.chunks[group] // self.n_blk if self.split_z else self.chunks[group]


def main_kernel(lay, *refs):
    (
        replay, model, requests, member, live, noise, sac_h, sac_m, dyn_h, dyn_m, crit_in, act_in,
        dyn_in, crit_out, act_out, dyn_out, biases, targ_in, targ_hidden, targ_out, targ_bias,
        sac_g, sac_x, dyn_x, dyn_s, small, count,
        wg, lists, asked, dhg, dmg, smg, bk, xs, nz, w1f, w1t, w1n, w2t, w2h, heads, head_t, head_f,
        rowbuf, wide, headcol, acc_h, acc_w, acc_c, acc_a, acc_m, acc_l, grid_c, grid_a, zr_c, zr_a,
        zf_c, zf_a, mg, mat, grow, dcols, dacc_h, dacc_w, dacc_o, dacc_m, dacc_b, dacc_l, xt, dmat,
        dpack, drow_x, bias, dhead, dhead_t, *rest,
    ) = refs
    bits = lay.bits
    bufs = (rest[:bits], rest[bits : 2 * bits])
    send, recv = rest[2 * bits :]
    sent, here_at = lay.sent, lay.here
    grids, zrs, zfs = (grid_c, grid_a), (zr_c, zr_a), (zf_c, zf_a)
    n_dp, n_blk = lay.n_dp, lay.n_blk
    me = lax.axis_index("dp")
    z = lax.axis_index("blk")
    core = lax.rem(me, 2)
    sibling = me + 1 - 2 * core
    is_dyn = me < MEMBERS
    dyn_e = jnp.minimum(me, MEMBERS - 1)
    is_actor = me == lay.owners[2]
    is_critic = jnp.logical_or(me == lay.owners[0], me == lay.owners[1])
    is_sac = jnp.logical_or(is_actor, is_critic)
    sac_k = jnp.clip((me - lay.owners[0]) // 2, 0, 2)

    def on_plane(src, dst, ssem, rsem, peer):
        return pltpu.make_async_remote_copy(
            src_ref=src, dst_ref=dst, send_sem=ssem, recv_sem=rsem,
            device_id={"dp": peer}, device_id_type=MESH,
        )

    def on_line(src, dst, ssem, rsem, peer):
        return pltpu.make_async_remote_copy(
            src_ref=src, dst_ref=dst, send_sem=ssem, recv_sem=rsem,
            device_id={"blk": peer}, device_id_type=MESH,
        )

    def over(number, body):
        if number <= 8:
            for off in range(1, number):
                body(off)
        else:
            pl.loop(1, number)(body)

    def plane_peers(body):
        over(n_dp, lambda off: body(lax.rem(me + off, n_dp)))

    def like_peers(body):
        over(n_dp // 2, lambda off: body(lax.rem(me + 2 * off, n_dp)))

    def line_peers(body):
        over(n_blk, lambda off: body(lax.rem(z + off, n_blk)))

    def has_sent(view, name):
        at = send.at[sent[name]]
        on_plane(view, view, at, at, sibling).wait_send()

    def has_come(view, name):
        at = recv.at[here_at[name]]
        on_plane(view, view, at, at, sibling).wait_recv()

    barrier = pltpu.get_barrier_semaphore()
    plane_peers(lambda peer: pl.semaphore_signal(barrier, inc=1, device_id={"dp": peer}, device_id_type=MESH))
    line_peers(lambda peer: pl.semaphore_signal(barrier, inc=1, device_id={"blk": peer}, device_id_type=MESH))
    wg[0] = sac_h[...].astype(BF16)
    lists[0] = requests[...]
    lists[1] = member[...]
    pl.semaphore_wait(barrier, n_dp - 1 + n_blk - 1)

    half_rows = pl.ds(pl.multiple_of(core * (lay.rows // 2), lay.rows // 2), lay.rows // 2)

    def slot_from(owner, at):
        return lax.rem(owner - at + n_blk, n_blk)

    def hidden_copy(peer):
        src = wg.at[0, :, half_rows]
        dst = wg.at[slot_from(z, peer), :, half_rows]
        return on_line(src, dst, send.at[sent["hidden"]], recv.at[here_at["hidden"]], peer)

    def hidden_on():
        view = wg.at[pl.ds(1, n_blk - 1), :, half_rows]
        return on_plane(view, view, send.at[sent["hidden on"]], recv.at[here_at["hidden on"]], sibling)

    def list_copy(peer):
        return on_plane(lists, asked.at[me], send.at[sent["lists"]], recv.at[here_at["lists"]], peer)

    line_peers(lambda peer: hidden_copy(peer).start())
    plane_peers(lambda peer: list_copy(peer).start())
    asked[me] = lists[...]

    def dyn_h_copy(peer):
        return on_line(dyn_h.at[dyn_e], dhg.at[z], send.at[sent["dyn h"]], recv.at[here_at["dyn h"]], peer)

    def dyn_m_copy(peer):
        return on_line(dyn_m.at[dyn_e], dmg.at[z], send.at[sent["dyn m"]], recv.at[here_at["dyn m"]], peer)

    def sac_m_copy(peer):
        return on_line(sac_m.at[sac_k], smg.at[z], send.at[sent["sac m"]], recv.at[here_at["sac m"]], peer)

    alive = live[...].astype(F32).reshape(1, lay.model)
    bias[...] = biases[...].reshape(1, NB)
    xs[42:56, :] = jnp.zeros((14, lay.batch), F32)
    xs[0:FEAT, lay.real : lay.batch] = model[...]
    xs[42:43, lay.real : lay.batch] = alive
    nz[...] = jnp.zeros_like(nz)
    for which in range(2):
        nz[which, 1:7, :] = noise[:, which, :]
    firsts = [
        (targ_in[:, 0, :], targ_bias[0:1, 0:HSAC]),
        (targ_in[:, 1, :], targ_bias[1:2, 0:HSAC]),
        (crit_in[:, 0, :], bias[:, CB1 : CB1 + HSAC]),
        (crit_in[:, 1, :], bias[:, CB1 + HSAC : CB1 + 2 * HSAC]),
        (act_in[...], bias[:, AB1 : AB1 + HSAC]),
    ]
    w1f[...] = jnp.zeros_like(w1f)
    for net, (weights, offset) in enumerate(firsts):
        w1f[net, 0 : weights.shape[0], :] = rounded(weights)
        for at, piece in enumerate(pieces(offset)):
            w1f[net, IN + at : IN + at + 1, :] = piece.astype(F32)
        w1t[net] = (0.5 * w1f[net].T).astype(BF16)
    for k in range(2):
        w1n[k] = w1f[2 + k, 16:32, :].astype(BF16)
    for net in range(2):
        w2t[net] = (0.5 * rounded(targ_hidden[net])).T.astype(BF16)
    rowbuf[...] = jnp.zeros_like(rowbuf)
    rowbuf[0:1, :] = targ_bias[0:1, HSAC : 2 * HSAC]
    rowbuf[1:2, :] = targ_bias[1:2, HSAC : 2 * HSAC]
    rowbuf[2:3, :] = bias[:, CB2 : CB2 + HSAC]
    rowbuf[3:4, :] = bias[:, CB2 + HSAC : CB2 + 2 * HSAC]
    rowbuf[4:5, :] = bias[:, AB2 : AB2 + HSAC]
    rowbuf[5:7, :] = rounded(crit_out[...])
    columns = 0.5 * rowbuf[...].T
    for at in range(7):
        wide[at] = jnp.broadcast_to(columns[:, at : at + 1], (HSAC, 128))
    rowbuf[...] = jnp.zeros_like(rowbuf)
    rowbuf[0:1, 1:7] = bias[:, AB3 : AB3 + ACT]
    rowbuf[0:1, 9:15] = bias[:, AB3 + ACT : AB3 + 2 * ACT]
    headcol[...] = rowbuf[:, 0:128].T
    head_f[...] = jnp.zeros_like(head_f)
    for k in range(2):
        head_f[0:1, :] = targ_out[k : k + 1, :]
        heads[k] = head_f[...].astype(BF16)
        head_f[0:1, :] = crit_out[k : k + 1, :]
        heads[2 + k] = head_f[...].astype(BF16)
    head_f[0:1, :] = jnp.zeros((1, HSAC), F32)
    head_f[1:7, :] = act_out[0:ACT, :]
    head_f[9:15, :] = act_out[ACT : 2 * ACT, :]
    heads[4] = head_f[...].astype(BF16)
    head_t[...] = (0.5 * rounded(head_f[...])).T.astype(BF16)
    for ref in (acc_h, acc_w, acc_c, acc_a, acc_m, acc_l):
        ref[...] = jnp.zeros_like(ref)

    data = replay[...]
    sums = jnp.sum(data[0:24], axis=1, keepdims=True)
    squares = jnp.sum(data[0:24] * data[0:24], axis=1, keepdims=True)
    living = jnp.sum(alive, axis=1, keepdims=True)

    has_come(asked.at[pl.ds(0, n_dp - 1)], "lists")
    spread = (
        lax.rem(lax.broadcasted_iota(jnp.int32, (CAP, lay.real), 1), CAP)
        == lax.broadcasted_iota(jnp.int32, (CAP, lay.real), 0)
    ).astype(F32)
    here = (
        lax.broadcasted_iota(jnp.int32, (n_dp, lay.real), 1) // CAP
        == lax.broadcasted_iota(jnp.int32, (n_dp, lay.real), 0)
    )

    def in_lanes(which):
        values = asked[:, which, me, :].astype(F32)
        wide = lax.dot_general(
            values, spread, NN, precision=lax.Precision.HIGHEST, preferred_element_type=F32
        )
        return jnp.sum(jnp.where(here, wide, 0.0), axis=0, keepdims=True)

    slots = in_lanes(0)
    wanted = jnp.maximum(slots, 0.0).astype(jnp.int32)
    hot = (rows_of((lay.replay, lay.real)) == wanted).astype(BF16)
    high, middle, low = pieces(data)
    picked = dot(high, hot) + dot(middle, hot) + dot(low, hot)
    mine = me * n_blk
    bk[mine, 0:FEAT, 0 : lay.real] = picked
    bk[mine, 42:43, 0 : lay.real] = (slots >= 0.0).astype(F32)
    bk[mine, 43:44, 0 : lay.real] = in_lanes(1)
    bk[mine, 44:48, 0 : lay.real] = jnp.zeros((4, lay.real), F32)
    bk[mine, :, lay.real : lay.width] = jnp.zeros((48, lay.width - lay.real), F32)
    bk[mine, 0:24, lay.real : lay.real + 1] = sums
    bk[mine, 0:24, lay.real + 1 : lay.real + 2] = squares
    bk[mine, 24:25, lay.real : lay.real + 1] = living

    def slot_of(block):
        line = lax.rem(block, n_blk)
        return block - line + slot_from(line, z)

    def block_line(peer):
        dst = bk.at[me * n_blk + slot_from(z, peer)]
        return on_line(bk.at[mine], dst, send.at[sent["line"]], recv.at[here_at["line"]], peer)

    def block_own(peer):
        view = bk.at[mine]
        return on_plane(view, view, send.at[sent["own"]], recv.at[here_at["own"]], peer)

    def block_plane(peer):
        view = bk.at[pl.ds(mine + 1, n_blk - 1)]
        return on_plane(view, view, send.at[sent["plane"]], recv.at[here_at["plane"]], peer)

    plane_peers(lambda peer: block_own(peer).start())
    line_peers(lambda peer: block_line(peer).start())
    has_come(wg.at[pl.ds(0, n_blk - 1), :, half_rows], "hidden")
    hidden_on().start()

    @pl.when(is_dyn)
    def _():
        line_peers(lambda peer: dyn_h_copy(peer).start())
        line_peers(lambda peer: dyn_m_copy(peer).start())

    @pl.when(is_sac)
    def _():
        line_peers(lambda peer: sac_m_copy(peer).start())

    has_come(wg.at[pl.ds(0, n_blk - 1), :, half_rows], "hidden on")
    for k in range(3):
        for block in range(n_blk):
            w2h[k, block * lay.rows : (block + 1) * lay.rows, :] = (
                0.5 * wg[slot_from(block, z), k].astype(F32)
            ).astype(BF16)
        w2t[2 + k] = w2h[k].astype(F32).T.astype(BF16)

    log_alpha = bias[:, LOGA : LOGA + 1]
    alpha = jnp.exp(log_alpha)
    last = [
        targ_bias[0:1, 2 * HSAC : 2 * HSAC + 1],
        targ_bias[1:2, 2 * HSAC : 2 * HSAC + 1],
        bias[:, CB3 : CB3 + 1],
        bias[:, CB3 + 1 : CB3 + 2],
    ]
    n_tiles = lay.batch // TILE
    row8 = rows_of((8, TILE))
    act_rows = jnp.logical_and(row8 >= 1, row8 < 1 + ACT)

    def place_of(step):
        return pl.ds(pl.multiple_of(lax.rem(step + 1, n_tiles) * TILE, TILE), TILE)

    def ones16():
        return jnp.ones((16, TILE), BF16)

    def framed(first_row, used, where):
        row32 = rows_of((32, TILE))
        ones3 = jnp.logical_and(row32 >= IN, row32 < IN + 3).astype(F32)
        return jnp.where(row32 < used, xs[first_row : first_row + 32, where], ones3)

    def hidden(inputs, net):
        first, slope1 = gated(dot(w1t[net], inputs))
        second, slope2 = gated(dot(w2t[net], first), wide[net])
        return first, slope1, second, slope2

    def policy(inputs, which, where):
        first, slope1, second, slope2 = hidden(inputs, 4)
        out = dot(heads[4], second) + headcol[0:16, 0:1]
        bent = jnp.tanh(out[8:16])
        log_scale = -5.0 + 3.5 * (bent + 1.0)
        draw = nz[which, :, where]
        moved = jnp.exp(log_scale) * draw
        latent = out[0:8] + moved
        terms = (
            -0.5 * draw * draw
            - log_scale
            - 0.9189385
            - 2.0 * (0.6931472 - latent - softplus(-2.0 * latent))
        )
        log_prob = jnp.sum(jnp.where(act_rows, terms, 0.0), axis=0, keepdims=True)
        action = jnp.where(act_rows, jnp.tanh(latent), 0.0)
        return action, log_prob, bent, moved, (first, slope1, second, slope2)

    def with_action(inputs, action):
        middle_rows = jnp.where(act_rows, action, inputs[16:24])
        return jnp.concatenate([inputs[0:16], middle_rows, inputs[24:32]], 0).astype(BF16)

    def critic(inputs, net):
        kept = hidden(inputs, net)
        value = dot(heads[net], kept[2])[0:1] + last[net]
        return value, kept

    def add_hidden(k, first, grad):
        acc_h[k] += dot(jnp.concatenate([first, ones16()], 0), grad, NT)

    @pl.loop(0, n_tiles)
    def _(step):
        @pl.when(step == 1)
        def _():
            has_come(bk.at[pl.ds(0, n_blk - 1)], "line")
            plane_peers(lambda peer: block_plane(peer).start())

        @pl.when(step == n_tiles - 1)
        def _():
            has_come(bk.at[pl.ds(0, n_dp - 1)], "own")
            lanes = lax.broadcasted_iota(jnp.int32, (48, lay.width), 1) // CAP

            def gather(owner, total):
                turned = pltpu.roll(
                    bk[owner * n_blk], lax.rem((owner - me) * CAP + lay.width, lay.width), axis=1
                )
                return jnp.where(lanes == owner, turned, total)

            own = lax.fori_loop(0, n_dp, gather, jnp.zeros((48, lay.width), F32))
            xs[0:48, 0 : lay.real] = own[:, 0 : lay.real]

        where = place_of(step)
        now_in = framed(0, IN, where).astype(BF16)
        next_f = framed(24, OBS, where)
        reward = xs[23:24, where]
        done = xs[41:42, where]
        weight = xs[42:43, where]
        row16 = rows_of((16, TILE))
        next_action, next_prob, _, _, _ = policy(next_f.astype(BF16), 1, where)
        aim_in = with_action(next_f, next_action)
        aim = jnp.minimum(critic(aim_in, 0)[0], critic(aim_in, 1)[0])
        target = reward + DISCOUNT * (1.0 - done) * (aim - alpha * next_prob)
        loss = jnp.zeros((1, TILE), F32)
        heads_grad = []
        for k in range(2):
            value, (c1, dc1, c2, dc2) = critic(now_in, 2 + k)
            miss = value - target
            loss += 0.5 * miss * miss
            g3 = rounded(weight * miss)
            g3_rows = jnp.where(row16 == 0, g3, 0.0).astype(BF16)
            heads_grad.append(g3_rows)
            acc_c[k] += dot(g3_rows, c2, NT)
            g2 = outer_sloped(wide[5 + k], g3, dc2)
            add_hidden(k, c1, g2)
            g1 = sloped(dot(w2h[k], g2), dc1)
            acc_w[k] += dot(now_in, g1, NT)
        acc_m[:, 16:48] += dot(ones16(), jnp.concatenate(heads_grad, 0), NT)
        acc_l[0:1, :] += weight * loss

    def put_matrix(group, k, at):
        for chunk in range(n_dp):
            tile = chunk * lay.mat
            side, row = tile // 32, tile % 32
            grids[group][chunk, at * lay.mat : (at + 1) * lay.mat] = acc_h[
                k, row * 8 : (row + lay.mat) * 8, side * 128 : (side + 1) * 128
            ].reshape(lay.mat, 8, 128)

    def put(row, value):
        for at in range(value.shape[0] // 8):
            for side in range(value.shape[1] // 128):
                tile = side * (R_SMALL // 8) + row // 8 + at
                grid_a[tile // lay.sml, lay.mat + tile % lay.sml] = value[
                    at * 8 : at * 8 + 8, side * 128 : (side + 1) * 128
                ]

    def bit(b):
        return lax.rem(me // (1 << b), 2)

    starts, faces, partners = [], [], []
    start = 0
    for s in range(bits):
        if s == 0:
            face, stride = core, 1
        else:
            face = (1 - core) * bit(s) + core * bit(bits - s)
            stride = (1 - core) * (1 << s) + core * (1 << (bits - s))
        starts.append(start)
        faces.append(face)
        partners.append(me + (1 - 2 * face) * stride)
        start = start + face * (n_dp >> (s + 1))
    place = start

    def fold_copy(group, s):
        half = n_dp >> (s + 1)
        begin = starts[s] + (1 - faces[s]) * half
        return on_plane(
            grids[group].at[pl.ds(begin, half)], bufs[group][s], send.at[sent["fold", group, s]],
            recv.at[here_at["fold", group, s]], partners[s],
        )

    def fold_wait(group, s):
        half = n_dp >> (s + 1)
        begin = starts[s] + faces[s] * half
        fold_copy(group, s).wait_recv()
        for at in range(half):
            grids[group][begin + at] += bufs[group][s][at]

    def line_first(group, peer):
        if lay.split_z:
            src = grids[group].at[place, pl.ds(peer * lay.part(group), lay.part(group))]
        else:
            src = grids[group].at[place]
        name = ("first", group)
        return on_line(src, zrs[group].at[z], send.at[sent[name]], recv.at[here_at[name]], peer)

    def line_second(group, peer):
        view = zfs[group].at[pl.ds(z * lay.part(group), lay.part(group))]
        name = ("second", group)
        return on_line(view, view, send.at[sent[name]], recv.at[here_at[name]], peer)

    def firsts_of(group):
        return zrs[group].at[pl.ds(0, n_blk - 1)]

    def seconds_of(group):
        return zfs[group].at[pl.ds(0, (n_blk - 1) * lay.part(group))]

    def line_start(group):
        line_peers(lambda peer: line_first(group, peer).start())

    def line_sum(group):
        part, zr, zf = lay.part(group), zrs[group], zfs[group]
        has_come(firsts_of(group), ("first", group))
        zr[z] = grids[group][place, pl.ds(z * part, part)] if lay.split_z else grids[group][place]
        whole = zr[0]
        for block in range(1, n_blk):
            whole = whole + zr[block]
        if lay.split_z:
            zf[pl.ds(z * part, part)] = whole
            line_peers(lambda peer: line_second(group, peer).start())
        else:
            zf[...] = whole

    def line_end(group):
        if lay.split_z:
            has_come(seconds_of(group), ("second", group))

    def tile_copy(k, owner):
        src = zfs[k // 2].at[pl.ds((k % 2) * lay.mat, lay.mat)]
        return on_plane(src, mg.at[place], send.at[sent["tiles", k]], recv.at[here_at["tiles"]], owner)

    def send_tiles(group):
        for k in (0, 1) if group == 0 else (2,):
            @pl.when(me != lay.owners[k])
            def _():
                tile_copy(k, lay.owners[k]).start()

            @pl.when(me == lay.owners[k])
            def _():
                mg[place] = zfs[group][(k % 2) * lay.mat : (k % 2 + 1) * lay.mat]

    def small_copy(peer):
        return on_plane(
            zf_a.at[pl.ds(lay.mat, lay.sml)], small.at[pl.ds(place * lay.sml, lay.sml)],
            send.at[sent["small"]], recv.at[here_at["small"]], peer,
        )

    def chain(group):
        steps = [functools.partial(lambda s: fold_copy(group, s).start(), 0)]

        def fold(s):
            fold_wait(group, s)
            if s + 1 < bits:
                fold_copy(group, s + 1).start()
            else:
                line_start(group)

        steps += [functools.partial(fold, s) for s in range(bits)]
        steps.append(lambda: line_sum(group))

        def finish():
            line_end(group)
            send_tiles(group)
            if group == 1:
                plane_peers(lambda peer: small_copy(peer).start())
                small[pl.ds(place * lay.sml, lay.sml)] = zf_a[lay.mat :]

        steps.append(finish)
        return steps

    critic_chain, actor_chain = chain(0), chain(1)
    for k in range(2):
        put_matrix(0, k, k)
    critic_chain[0]()

    inside = min(len(critic_chain) - 1, n_tiles - 1)

    @pl.loop(0, n_tiles)
    def _(step):
        for at in range(inside):
            @pl.when(step == at + 1)
            def _():
                critic_chain[at + 1]()

        where = place_of(step)
        now_f = framed(0, IN, where)
        now_in = now_f.astype(BF16)
        weight = xs[42:43, where]
        action, log_prob, bent, moved, (a1, da1, a2, da2) = policy(now_in, 0, where)
        judged_in = with_action(now_f, action)
        loss = alpha * log_prob - log_alpha * (log_prob + TARGET_ENTROPY)
        grad_action = jnp.zeros((8, TILE), F32)
        for k in range(2):
            judged, (_, df1, _, df2) = critic(judged_in, 2 + k)
            loss -= 0.5 * judged
            g2 = outer_sloped(wide[5 + k], -0.5 * weight, df2)
            g1 = sloped(dot(w2h[k], g2), df1)
            grad_action += dot(w1n[k], g1)[0:8]
        grad_latent = 2.0 * alpha * weight * action + grad_action * (1.0 - action * action)
        grad_scale = grad_latent * moved - alpha * weight
        grad_bent = grad_scale * 3.5 * (1.0 - bent * bent)
        g3 = jnp.concatenate(
            [jnp.where(act_rows, grad_latent, 0.0), jnp.where(act_rows, grad_bent, 0.0)], 0
        ).astype(BF16)
        acc_a[...] += dot(g3, a2, NT)
        acc_m[:, 0:16] += dot(ones16(), g3, NT)
        g2 = sloped(dot(head_t[...], g3), da2)
        add_hidden(2, a1, g2)
        g1 = sloped(dot(w2h[2], g2), da1)
        acc_w[2] += dot(now_in, g1, NT)
        acc_l[0:1, :] += weight * loss
        acc_l[1:2, :] += weight * (log_prob + TARGET_ENTROPY)

    for at in range(inside, len(critic_chain) - 1):
        critic_chain[at + 1]()
    put_matrix(1, 2, 0)
    for k in range(3):
        put(R_IN + 24 * k, acc_w[k, 0:24, :])
    put(R_HEAD, acc_a[...])
    rowbuf[0:1, :] = acc_c[0, 0:1, :]
    rowbuf[1:2, :] = acc_c[1, 0:1, :]
    for k in range(3):
        rowbuf[2 + k : 3 + k, :] = acc_h[k, HSAC : HSAC + 1, :]
    put(R_OUT, rowbuf[...])
    folded = jnp.sum(acc_l[...], axis=1, keepdims=True)
    rowbuf[...] = jnp.zeros_like(rowbuf)
    rowbuf[0:1, 0:48] = acc_m[0:1, :]
    rowbuf[0:1, 64:65] = folded[0:1]
    rowbuf[0:1, 65:66] = folded[1:2]
    put(R_MISC, rowbuf[...])
    put(R_MISC + 8, jnp.zeros((R_SMALL - R_MISC - 8, HSAC), F32))
    actor_chain[0]()

    has_come(bk.at[pl.ds(0, (n_dp - 1) * (n_blk - 1))], "plane")
    lane0 = lay.real // 128 * 128

    def add_block(at, carry):
        sides, fills = carry
        slot = slot_of(at)
        return sides + bk[slot, 0:32, lane0 : lane0 + 128], fills + bk[slot, 40:48, 0 : lay.real]

    sides, fills = lax.fori_loop(
        0, lay.n_dev, add_block, (jnp.zeros((32, 128), F32), jnp.zeros((8, lay.real), F32))
    )
    at = lay.real - lane0
    rows_all = float(lay.replay * lay.n_dev)
    centre = sides[0:24, at : at + 1] / rows_all
    scale = lax.rsqrt(sides[0:24, at + 1 : at + 2] / rows_all - centre * centre + 1e-6)
    total = sides[24:25, at : at + 1] + jnp.sum(fills[2:3, :], axis=1, keepdims=True)
    count[...] = jnp.broadcast_to(total, (8, 128))

    def dyn_bias(start, width):
        row = jnp.zeros((1, width), F32)
        for e in range(MEMBERS):
            row = jnp.where(me == e, bias[:, start + width * e : start + width * (e + 1)], row)
        return row

    @pl.when(is_dyn)
    def _():
        w1f[0] = jnp.zeros((32, HSAC), F32)
        w1f[0, 0:IN, 0:HDYN] = rounded(dyn_in[dyn_e])
        for at, piece in enumerate(pieces(dyn_bias(DB1, HDYN))):
            w1f[0, IN + at : IN + at + 1, 0:HDYN] = piece.astype(F32)
        w1t[0] = (0.5 * w1f[0].T).astype(BF16)
        rowbuf[...] = jnp.zeros_like(rowbuf)
        rowbuf[0:1, 0:HDYN] = dyn_bias(DB2, HDYN)
        head_row = dyn_bias(DB3, DOUT)
        rowbuf[1:2, 0:HALF] = head_row[:, 0:HALF]
        rowbuf[1:2, 24 : 24 + HALF] = head_row[:, HALF:DOUT]
        rowbuf[2:3, 0:HALF] = bias[:, MAXLV : MAXLV + HALF]
        rowbuf[3:4, 0:HALF] = bias[:, MINLV : MINLV + HALF]
        dcols[...] = rowbuf[...].T
        wide[0] = jnp.broadcast_to(0.5 * dcols[:, 0:1], (HSAC, 128))
        dpack[...] = jnp.zeros_like(dpack)
        dpack[0:HALF, 0:HDYN] = dyn_out[dyn_e, 0:HALF, :]
        dpack[24 : 24 + HALF, 0:HDYN] = dyn_out[dyn_e, HALF:DOUT, :]
        dhead[...] = dpack[0:48, :].astype(BF16)
        dhead_t[...] = (0.5 * rounded(dpack[0:48, :])).T.astype(BF16)
        dpack[...] = jnp.zeros_like(dpack)

        has_come(dhg.at[pl.ds(0, n_blk - 1)], "dyn h")
        has_come(dmg.at[pl.ds(0, n_blk - 1)], "dyn m")
        dhg[z] = dyn_h[dyn_e]
        dmg[z] = dyn_m[dyn_e]
        dmat[...] = jnp.zeros_like(dmat)
        for block in range(n_blk):
            dmat[block * lay.drows : (block + 1) * lay.drows, 0:HDYN] = 0.5 * rounded(dhg[block])
        w2h[0] = dmat[...].astype(BF16)
        w2t[0] = dmat[...].T.astype(BF16)
        for ref in (dacc_h, dacc_w, dacc_o, dacc_m, dacc_b, dacc_l):
            ref[...] = jnp.zeros_like(ref)

    per = TILE // lay.real
    dyn_tiles = lay.n_dev // per
    gap = max(dyn_tiles // (bits + 1), 1)

    @pl.loop(0, dyn_tiles)
    def _(tile):
        for s in range(bits):
            @pl.when(tile == (s + 1) * gap)
            def _():
                actor_chain[s + 1]()

        @pl.when(is_dyn)
        def _():
            for at in range(per):
                slot = slot_of(tile * per + at)
                xt[:, at * lay.real : (at + 1) * lay.real] = bk[slot, :, 0 : lay.real]
            now = xt[0:24, :]
            later = xt[24:48, :]
            row24 = rows_of((24, TILE))
            scaled = jnp.where(row24 < IN, (now - centre) * scale, 1.0)
            inputs = jnp.concatenate([scaled, (row8 < 2).astype(F32)], 0).astype(BF16)
            first, slope1 = gated(dot(w1t[0], inputs))
            second, slope2 = gated(dot(w2t[0], first), wide[0])
            out = dot(dhead[...], second) + dcols[0:48, 1:2]
            used = row24 < HALF
            upper = dcols[0:24, 2:3]
            lower = dcols[0:24, 3:4]
            gap1 = upper - out[24:48]
            gap2 = upper - softplus(gap1) - lower
            log_var = lower + softplus(gap2)
            error = out[0:24] - jnp.where(row24 == OBS, now[23:24], later - now)
            inverse = jnp.exp(-log_var)
            weight = xt[42:43, :] * (xt[43:44, :] == me.astype(F32)).astype(F32)
            spread_term = error * error * inverse
            nll = jnp.sum(jnp.where(used, spread_term + log_var, 0.0), axis=0, keepdims=True)
            dacc_l[0:1, :] += weight * nll
            grad_mu = 2.0 * weight * error * inverse
            grad_lv = weight * (1.0 - spread_term)
            open1 = sigmoid(gap1)
            open2 = sigmoid(gap2)
            grad_lv1 = grad_lv * open2
            dacc_b[0] += jnp.where(used, grad_lv1 * (1.0 - open1), 0.0)
            dacc_b[1] += jnp.where(used, grad_lv * (1.0 - open2), 0.0)
            g3 = jnp.concatenate(
                [jnp.where(used, grad_mu, 0.0), jnp.where(used, grad_lv1 * open1, 0.0)], 0
            ).astype(BF16)
            dacc_o[...] += dot(g3, second, NT)
            dacc_m[...] += dot(ones16(), g3, NT)
            g2 = sloped(dot(dhead_t[...], g3), slope2)
            dacc_h[...] += dot(jnp.concatenate([first, ones16()], 0), g2, NT)
            g1 = sloped(dot(w2h[0], g2), slope1)
            dacc_w[...] += dot(inputs, g1, NT)

    out_of = {"pack": dyn_s, "x": dyn_x}

    def member_copy(name, src, owner, kind, sem, peer):
        return on_plane(src, out_of[name].at[owner], send.at[sent[name, kind]], recv.at[sem], peer)

    def give(name, src):
        like_peers(
            lambda peer: member_copy(name, src, dyn_e, "own", here_at[name, "like"] + dyn_e, peer).start()
        )
        member_copy(name, src, dyn_e, "own", here_at[name, "sibling"], sibling).start()

    def hand_on(name):
        def body(peer):
            @pl.when(peer < MEMBERS)
            def _():
                owner = jnp.minimum(peer, MEMBERS - 1)
                view = out_of[name].at[owner]
                member_copy(name, view, owner, "on", here_at[name, "like"] + owner, sibling).wait_recv()
                member_copy(name, view, owner, "on", here_at[name, "sibling"], sibling).start()

        like_peers(body)

    even, odd = (MEMBERS + 1) // 2, MEMBERS // 2
    handed = even - core * (even - odd) - jnp.where(is_dyn, 1, 0)

    def from_sibling(name):
        for side, number in ((0, odd), (1, even)):
            @pl.when(core == side)
            def _():
                has_come(out_of[name].at[pl.ds(0, number)], (name, "sibling"))

    def gave(name):
        @pl.when(is_dyn)
        def _():
            for begin in range(0, n_dp // 2, MEMBERS):
                number = min(MEMBERS, n_dp // 2 - begin)
                has_sent(out_of[name].at[pl.ds(0, number)], (name, "own"))

        for number in (even, even - 1, even - 2):
            @pl.when(handed == number)
            def _():
                has_sent(out_of[name].at[pl.ds(0, number)], (name, "on"))

    def line_rows(ref):
        rows = ref[0 : lay.drows, 0:HDYN]
        for block in range(1, n_blk):
            rows = jnp.where(z == block, ref[block * lay.drows : (block + 1) * lay.drows, 0:HDYN], rows)
        return rows

    def sac_g_copy(k, peer):
        src = grow.at[pl.ds(pl.multiple_of(z * lay.rows, lay.rows), lay.rows)]
        return on_plane(src, sac_g.at[k], send.at[sent["sac g"] + peer], recv.at[here_at["sac g"] + k], peer)

    def sac_x_copy(k, peer):
        src = mat.at[pl.ds(pl.multiple_of(z * lay.rows, lay.rows), lay.rows)]
        return on_plane(src, sac_x.at[k], send.at[sent["sac x"] + peer], recv.at[here_at["sac x"] + k], peer)

    mine_rows = pl.ds(pl.multiple_of(z * lay.rows, lay.rows), lay.rows)

    def take_matrix():
        has_come(smg.at[pl.ds(0, n_blk - 1)], "sac m")
        smg[z] = sac_m[sac_k]
        has_come(mg.at[pl.ds(0, n_dp - 1)], "tiles")
        for chunk in range(n_dp):
            tile = chunk * lay.mat
            side, row = tile // 32, tile % 32
            grow[row * 8 : (row + lay.mat) * 8, side * 128 : (side + 1) * 128] = mg[chunk].reshape(
                lay.mat * 8, 128
            )
        sac_g[sac_k] = grow[mine_rows, :]
        plane_peers(lambda peer: sac_g_copy(sac_k, peer).start())
        for block in range(n_blk):
            at = slice(block * lay.rows, (block + 1) * lay.rows)
            mat[at, :] = MOMENTUM * smg[block] + grow[at, :] / total
        normalise(mat)

    @pl.when(is_dyn)
    def _():
        dpack[D_IN : D_IN + 24, :] = dacc_w[0:24, :]
        dpack[D_OUT : D_OUT + HALF, :] = dacc_o[0:HALF, :]
        dpack[D_OUT + HALF : D_OUT + DOUT, :] = dacc_o[24 : 24 + HALF, :]
        dpack[D_B2 : D_B2 + 1, :] = dacc_h[HSAC : HSAC + 1, :]
        dpack[D_B3 : D_B3 + 1, 0:48] = dacc_m[0:1, :]
        lanes = lax.broadcasted_iota(jnp.int32, (24, 128), 1)
        bound = jnp.where(
            lanes == 0,
            jnp.sum(dacc_b[0], axis=1, keepdims=True),
            jnp.where(lanes == 1, jnp.sum(dacc_b[1], axis=1, keepdims=True), 0.0),
        )
        dpack[D_UP : D_UP + 2, 0:24] = bound.T[0:2, :]
        dpack[D_LOSS : D_LOSS + 1, 0:128] = jnp.broadcast_to(
            jnp.sum(dacc_l[0:1, :], axis=1, keepdims=True), (1, 128)
        )
        dpack[D_HID : D_HID + lay.drows, 0:HDYN] = line_rows(dacc_h)
        dyn_s[dyn_e] = dpack[...]
        give("pack", dpack)
        dmat[...] = jnp.zeros_like(dmat)
        for block in range(n_blk):
            at = slice(block * lay.drows, (block + 1) * lay.drows)
            dmat[at, 0:HDYN] = MOMENTUM * dmg[block] + dacc_h[at, 0:HDYN] / total
        normalise(dmat)

    pl.when(is_critic)(take_matrix)
    if n_dp <= MEMBERS + 1:
        only_dyn = jnp.logical_and(is_dyn, jnp.logical_not(is_critic))
        pairs = [(is_critic, [dmat, mat]), (only_dyn, [dmat])]
    else:
        pairs = [(is_critic, [mat]), (is_dyn, [dmat])]
    for test, matrices in pairs:
        pl.when(test)(functools.partial(schulz, matrices, 2))
    actor_chain[bits + 1]()
    for test, matrices in pairs:
        pl.when(test)(functools.partial(schulz, matrices, 2))
    actor_chain[bits + 2]()
    for test, matrices in pairs:
        pl.when(test)(functools.partial(schulz, matrices, NS_ITERS - 4))

    def send_sac():
        sac_x[sac_k] = mat[mine_rows, :]
        plane_peers(lambda peer: sac_x_copy(sac_k, peer).start())

    @pl.when(is_dyn)
    def _():
        rows = line_rows(dmat)
        drow_x[...] = rows
        dyn_x[dyn_e] = rows
        give("x", drow_x)

    pl.when(is_critic)(send_sac)

    def sent_early():
        has_sent(wg.at[pl.ds(0, n_blk - 1), :, half_rows], "hidden")
        has_sent(wg.at[pl.ds(0, n_blk - 1), :, half_rows], "hidden on")
        has_sent(asked.at[pl.ds(0, n_dp - 1)], "lists")
        has_sent(bk.at[pl.ds(0, n_dp - 1)], "own")
        has_sent(bk.at[pl.ds(0, n_blk - 1)], "line")
        has_sent(bk.at[pl.ds(0, (n_dp - 1) * (n_blk - 1))], "plane")

        @pl.when(is_dyn)
        def _():
            has_sent(dhg.at[pl.ds(0, n_blk - 1)], "dyn h")
            has_sent(dmg.at[pl.ds(0, n_blk - 1)], "dyn m")

        @pl.when(is_sac)
        def _():
            has_sent(smg.at[pl.ds(0, n_blk - 1)], "sac m")

        for group in range(2):
            for s in range(bits):
                fold_copy(group, s).wait_send()
            has_sent(firsts_of(group), ("first", group))
            if lay.split_z:
                has_sent(seconds_of(group), ("second", group))

    @pl.when(is_actor)
    def _():
        sent_early()
        take_matrix()
        schulz([mat], NS_ITERS)
        send_sac()

    pl.when(jnp.logical_not(is_actor))(sent_early)
    hand_on("pack")
    hand_on("x")
    has_come(small.at[pl.ds(0, (n_dp - 1) * lay.sml)], "small")
    from_sibling("pack")
    from_sibling("x")
    for k in range(3):
        @pl.when(me != lay.owners[k])
        def _():
            sac_g_copy(k, me).wait_recv()
            sac_x_copy(k, me).wait_recv()

    has_sent(small.at[pl.ds(0, (n_dp - 1) * lay.sml)], "small")
    gave("pack")
    gave("x")
    for k in range(3):
        @pl.when(me != lay.owners[k])
        def _():
            tile_copy(k, lay.owners[k]).wait_send()

    @pl.when(is_sac)
    def _():
        plane_peers(lambda peer: sac_g_copy(sac_k, peer).wait_send())
        plane_peers(lambda peer: sac_x_copy(sac_k, peer).wait_send())


def adamw(weights, first, second, gradient):
    first = BETA_FIRST * first + (1.0 - BETA_FIRST) * gradient
    second = BETA_SECOND * second + (1.0 - BETA_SECOND) * gradient * gradient
    first_hat = first / (1.0 - BETA_FIRST**STEP)
    second_hat = second / (1.0 - BETA_SECOND**STEP)
    step = first_hat / (jnp.sqrt(second_hat) + 1e-8) + ADAM_DECAY * weights
    return weights - ADAM_RATE * step, first, second


def update_kernel(*refs):
    (
        sac_g, sac_x, dyn_x, dyn_s, small, count, sac_h, sac_m, dyn_h, dyn_m,
        ci, ci_m, ci_v, ai, ai_m, ai_v, di, di_m, di_v, co, co_m, co_v, ao, ao_m, ao_v,
        do, do_m, do_v, bi, bi_m, bi_v,
        sac_new, sac_mom, dyn_new, dyn_mom, ci_n, ci_mn, ci_vn, ai_n, ai_mn, ai_vn, di_n, di_mn,
        di_vn, co_n, co_mn, co_vn, ao_n, ao_mn, ao_vn, do_n, do_mn, do_vn, bi_n, bi_mn, bi_vn,
        loss, counted, bg,
    ) = refs
    total = count[0:1, 0:1]
    sac_mom[...] = MOMENTUM * sac_m[...] + sac_g[...] / total.reshape(1, 1, 1)
    sac_new[...] = sac_h[...] * (1.0 - MUON_RATE * MUON_DECAY) - MUON_RATE * sac_x[...]
    dyn_rows = dyn_s[:, D_HID : D_HID + dyn_m.shape[1], 0:HDYN]
    dyn_mom[...] = MOMENTUM * dyn_m[...] + dyn_rows / total.reshape(1, 1, 1)
    dyn_new[...] = dyn_h[...] * (1.0 - MUON_RATE * MUON_DECAY) - MUON_RATE * dyn_x[...]

    def rows(row, number):
        sides = []
        for side in range(2):
            at = side * (R_SMALL // 8) + row // 8
            sides.append(small[at : at + -(-number // 8)].reshape(-1, 128))
        return jnp.concatenate(sides, 1)

    def store(outs, at, values):
        for out, value in zip(outs, values):
            out[at] = value

    outs = (ci_n, ci_mn, ci_vn)
    for k in range(2):
        at = (slice(None), k, slice(None))
        grad = rows(R_IN + 24 * k, 24)
        bg[:, CB1 + HSAC * k : CB1 + HSAC * (k + 1)] = grad[IN : IN + 1]
        store(outs, at, adamw(ci[at], ci_m[at], ci_v[at], grad[0:IN] / total))
    grad = rows(R_IN + 48, 24)
    bg[:, AB1 : AB1 + HSAC] = grad[IN : IN + 1]
    store((ai_n, ai_mn, ai_vn), ..., adamw(ai[...], ai_m[...], ai_v[...], grad[0:OBS] / total))
    grad = rows(R_HEAD, 16)
    for at, row in ((slice(0, ACT), slice(1, 1 + ACT)), (slice(ACT, 2 * ACT), slice(9, 9 + ACT))):
        store((ao_n, ao_mn, ao_vn), at, adamw(ao[at], ao_m[at], ao_v[at], grad[row] / total))
    grad = rows(R_OUT, 8)
    store((co_n, co_mn, co_vn), ..., adamw(co[...], co_m[...], co_v[...], grad[0:2] / total))
    bg[:, CB2 : CB2 + HSAC] = grad[2:3]
    bg[:, CB2 + HSAC : CB2 + 2 * HSAC] = grad[3:4]
    bg[:, AB2 : AB2 + HSAC] = grad[4:5]
    grad = rows(R_MISC, 8)
    bg[:, CB3 : CB3 + 1] = grad[0:1, 16:17]
    bg[:, CB3 + 1 : CB3 + 2] = grad[0:1, 32:33]
    bg[:, AB3 : AB3 + ACT] = grad[0:1, 1 : 1 + ACT]
    bg[:, AB3 + ACT : AB3 + 2 * ACT] = grad[0:1, 9 : 9 + ACT]
    bg[:, LOGA : LOGA + 1] = -grad[0:1, 65:66]
    total_loss = grad[0:1, 64:65]
    up = jnp.zeros((1, HALF), F32)
    low = jnp.zeros((1, HALF), F32)
    for e in range(MEMBERS):
        pack = dyn_s[e]
        total_loss = total_loss + pack[D_LOSS : D_LOSS + 1, 0:1]
        up = up + pack[D_UP : D_UP + 1, 0:HALF]
        low = low + pack[D_LOW : D_LOW + 1, 0:HALF]
        bg[:, DB1 + HDYN * e : DB1 + HDYN * (e + 1)] = pack[IN : IN + 1, 0:HDYN]
        bg[:, DB2 + HDYN * e : DB2 + HDYN * (e + 1)] = pack[D_B2 : D_B2 + 1, 0:HDYN]
        bg[:, DB3 + DOUT * e : DB3 + DOUT * e + HALF] = pack[D_B3 : D_B3 + 1, 0:HALF]
        bg[:, DB3 + DOUT * e + HALF : DB3 + DOUT * (e + 1)] = pack[D_B3 : D_B3 + 1, 24 : 24 + HALF]
        grad = pack[0:IN, 0:HDYN] / total
        store((di_n, di_mn, di_vn), e, adamw(di[e], di_m[e], di_v[e], grad))
        grad = pack[D_OUT : D_OUT + DOUT, 0:HDYN] / total
        store((do_n, do_mn, do_vn), e, adamw(do[e], do_m[e], do_v[e], grad))
    bg[:, MAXLV : MAXLV + HALF] = up
    bg[:, MINLV : MINLV + HALF] = low
    lane = lax.broadcasted_iota(jnp.int32, (1, NB), 1)
    bounds = jnp.where(
        jnp.logical_and(lane >= MAXLV, lane < MINLV),
        BOUND_WEIGHT,
        jnp.where(jnp.logical_and(lane >= MINLV, lane < LOGA), -BOUND_WEIGHT, 0.0),
    )
    grad = bg[...] / total + bounds
    flat = [ref[...].reshape(1, NB) for ref in (bi, bi_m, bi_v)]
    store((bi_n, bi_mn, bi_vn), ..., [value.reshape(NB) for value in adamw(*flat, grad)])
    loss[...] = total_loss
    counted[...] = total


def shards(
    lay, replay, model_rows, requests, member_of, model_live, noise, sac_hidden, sac_hidden_mom,
    dyn_hidden, dyn_hidden_mom, crit_in, crit_in_m, crit_in_v, act_in, act_in_m, act_in_v, dyn_in,
    dyn_in_m, dyn_in_v, crit_out, crit_out_m, crit_out_v, act_out, act_out_m, act_out_v, dyn_out,
    dyn_out_m, dyn_out_v, biases, biases_m, biases_v, targ_in, targ_hidden, targ_out, targ_bias,
):
    n_dp, n_blk, bits = lay.n_dp, lay.n_blk, lay.bits
    spec = pl.BlockSpec(memory_space=pltpu.VMEM)

    def flip(value):
        return jnp.transpose(value, (1, 0, 2))

    def swap(value):
        return jnp.swapaxes(value, -1, -2)

    def kept(value):
        return pltpu.with_memory_space_constraint(value, pltpu.VMEM)

    inputs = (
        replay, model_rows, requests, member_of, model_live, jnp.transpose(noise, (2, 0, 1)),
        sac_hidden, sac_hidden_mom, dyn_hidden, dyn_hidden_mom, flip(crit_in), act_in, dyn_in,
        crit_out, swap(act_out), swap(dyn_out), biases, flip(targ_in), targ_hidden, targ_out,
        targ_bias,
    )
    shape = jax.ShapeDtypeStruct
    rows, drows = lay.rows, lay.drows
    out_shape = (
        pltpu.VMEM((3, rows, HSAC), F32),
        pltpu.VMEM((3, rows, HSAC), F32),
        pltpu.VMEM((MEMBERS, drows, HDYN), F32),
        pltpu.VMEM((MEMBERS, D_ROWS, HSAC), F32),
        pltpu.VMEM((32, 8, 128), F32),
        pltpu.VMEM((8, 128), F32),
    )

    def vm(*dims, kind=F32):
        return pltpu.VMEM(dims, kind)

    scratch = [
        vm(n_blk, 3, rows, HSAC, kind=BF16),
        vm(2, n_dp, CAP, kind=jnp.int32),
        vm(n_dp, 2, n_dp, CAP, kind=jnp.int32),
        vm(n_blk, drows, HDYN),
        vm(n_blk, drows, HDYN),
        vm(n_blk, rows, HSAC),
        vm(lay.n_dev, 48, lay.width),
        vm(56, lay.batch),
        vm(2, 8, lay.batch),
        vm(5, 32, HSAC),
        vm(5, HSAC, 32, kind=BF16),
        vm(2, 16, HSAC, kind=BF16),
        vm(5, HSAC, HSAC, kind=BF16),
        vm(3, HSAC, HSAC, kind=BF16),
        vm(5, 16, HSAC, kind=BF16),
        vm(HSAC, 16, kind=BF16),
        vm(16, HSAC),
        vm(8, HSAC),
        vm(7, HSAC, 128),
        vm(128, 8),
        vm(3, HSAC + 16, HSAC),
        vm(3, 32, HSAC),
        vm(2, 16, HSAC),
        vm(16, HSAC),
        vm(16, 48),
        vm(8, TILE),
        vm(n_dp, lay.chunks[0], 8, 128),
        vm(n_dp, lay.chunks[1], 8, 128),
        vm(n_blk, lay.part(0), 8, 128),
        vm(n_blk, lay.part(1), 8, 128),
        vm(lay.chunks[0], 8, 128),
        vm(lay.chunks[1], 8, 128),
        vm(n_dp, lay.mat, 8, 128),
        vm(HSAC, HSAC),
        vm(HSAC, HSAC),
        vm(HSAC, 8),
        vm(HSAC + 16, HSAC),
        vm(32, HSAC),
        vm(48, HSAC),
        vm(16, 48),
        vm(2, 24, TILE),
        vm(8, TILE),
        vm(48, TILE),
        vm(HSAC, HSAC),
        vm(D_ROWS, HSAC),
        vm(drows, HDYN),
        vm(1, NB),
        vm(48, HSAC, kind=BF16),
        vm(HSAC, 48, kind=BF16),
    ]
    scratch += [vm(n_dp >> (s + 1), chunk, 8, 128) for chunk in lay.chunks for s in range(bits)]
    scratch += [pltpu.SemaphoreType.DMA((lay.departures,)), pltpu.SemaphoreType.DMA((lay.arrivals,))]
    varying = 4 * (lay.n_dev * 48 * lay.width + 72 * lay.batch + 48 * lay.replay)
    gathered = pl.pallas_call(
        functools.partial(main_kernel, lay),
        out_shape=out_shape,
        in_specs=[spec] * len(inputs),
        out_specs=[spec] * len(out_shape),
        scratch_shapes=scratch,
        compiler_params=pltpu.CompilerParams(
            collective_id=0, has_side_effects=True, vmem_limit_bytes=14 * 2**20 + 2 * varying
        ),
        name="step",
    )(*[pltpu.with_memory_space_constraint(value, pltpu.HBM) for value in inputs])
    params = (
        sac_hidden, sac_hidden_mom, dyn_hidden, dyn_hidden_mom,
        flip(crit_in), flip(crit_in_m), flip(crit_in_v), act_in, act_in_m, act_in_v,
        dyn_in, dyn_in_m, dyn_in_v, crit_out, crit_out_m, crit_out_v,
        swap(act_out), swap(act_out_m), swap(act_out_v),
        swap(dyn_out), swap(dyn_out_m), swap(dyn_out_v), biases, biases_m, biases_v,
    )
    new_shape = [shape(value.shape, F32) for value in params]
    new_shape += [shape((1, 1), F32)] * 2
    out = pl.pallas_call(
        update_kernel,
        out_shape=tuple(new_shape),
        in_specs=[spec] * (len(gathered) + len(params)),
        out_specs=[spec] * len(new_shape),
        scratch_shapes=[vm(1, NB)],
        compiler_params=pltpu.CompilerParams(vmem_limit_bytes=16 * 2**20),
        name="update",
    )(*[kept(value) for value in gathered], *params)
    out = list(out)
    for at in (4, 5, 6):
        out[at] = flip(out[at])
    for at in (16, 17, 18, 19, 20, 21):
        out[at] = swap(out[at])
    for at in (25, 26):
        out[at] = out[at].reshape(())
    return tuple(out)


def solution(mesh):
    both = ("dp", "blk")
    sharded = (
        P(None, both), P(None, both), P(both, None), P(both, None), P(both), P(None, both, None),
    )
    hidden = (P(None, "blk", None),) * 4

    def step(replay, model_rows, *others):
        lay = Layout(mesh, replay.shape[1], model_rows.shape[1])
        return shards(lay, replay, model_rows, *others)

    return jax.shard_map(
        step,
        mesh=mesh,
        in_specs=sharded + hidden + (P(),) * 25,
        out_specs=hidden + (P(),) * 23,
        check_vma=False,
    )
```

```python
import functools
import math

import jax
import jax.numpy as jnp
from jax import lax
from jax.experimental import pallas as pl
from jax.experimental.pallas import tpu as pltpu
from jax.sharding import PartitionSpec as P

OBS = 17
ACT = 6
IN = OBS + ACT
FEAT = 42
HDYN = 200
HSAC = 256
MEMBERS = 7
DOUT = 36
HALF = DOUT // 2
NB = 4639
NS_ITERS = 5
STEP = 10
CAP = 8
TILE = 640
DYN_TILE = 512
ROWS = 32

DISCOUNT = 0.99
TARGET_ENTROPY = -6.0
BOUND_WEIGHT = 0.01
MOMENTUM = 0.95
MUON_RATE = 0.4
MUON_DECAY = 0.01
ADAM_RATE = 0.1
ADAM_DECAY = 0.01
BETA_FIRST = 0.9
BETA_SECOND = 0.999
COEF_LINEAR = 3.4445
COEF_CUBIC = -4.775
COEF_QUINTIC = 2.0315

CB1, CB2, CB3, AB1, AB2, AB3 = 0, 512, 1024, 1026, 1282, 1538
DB1, DB2, DB3, MAXLV, MINLV, LOGA = 1550, 2950, 4350, 4602, 4620, 4638

R_IN, R_HEAD, R_OUT, R_MISC, R_SMALL = 0, 72, 88, 96, 128
D_IN, D_OUT, D_B2, D_B3, D_UP, D_LOW, D_LOSS, D_HID, D_ROWS = 0, 24, 60, 61, 62, 63, 64, 72, 128

F32, BF16 = jnp.float32, jnp.bfloat16
MESH = pl.DeviceIdType.MESH
NN = (((1,), (0,)), ((), ()))
NT = (((1,), (1,)), ((), ()))


def dot(a, b, dims=NN):
    return lax.dot_general(a, b, dims, preferred_element_type=F32)


def rounded(v):
    return v.astype(BF16).astype(F32)


def pieces(v):
    high = v.astype(BF16)
    rest = v - high.astype(F32)
    middle = rest.astype(BF16)
    return high, middle, (rest - middle.astype(F32)).astype(BF16)


def split(v):
    high = v.astype(BF16)
    return high, (v - high.astype(F32)).astype(BF16)


def product(a, b, dims=NN):
    left = jnp.concatenate([a[0], a[0], a[1]], 1)
    right = jnp.concatenate([b[0], b[1], b[0]], dims[0][1][0])
    half = left.shape[0] // 2
    return jnp.concatenate([dot(left[:half], right, dims), dot(left[half:], right, dims)], 0)


def softplus(v):
    return jnp.maximum(v, 0.0) + jnp.log1p(jnp.exp(-jnp.abs(v)))


def sigmoid(v):
    return 0.5 + 0.5 * jnp.tanh(0.5 * v)


def gate(half):
    up = 1.0 + jnp.tanh(half)
    value = half * up
    return value, up + value * (2.0 - up)


def by_rows(body, *arrays):
    done = [
        body(*[array[at : at + ROWS] for array in arrays]) for at in range(0, arrays[0].shape[0], ROWS)
    ]
    return [jnp.concatenate(parts, 0) for parts in zip(*done)]


def spread_to(column, width):
    return jnp.concatenate([column] * (width // 128), 1)


def gated(half, column=None):
    def body(part, *offset):
        value, slope = gate(part + spread_to(offset[0], part.shape[1]) if offset else part)
        return value.astype(BF16), slope

    return by_rows(body, half, *([] if column is None else [column]))


def sloped(grad, slope):
    return by_rows(lambda part, by: ((part * by).astype(BF16),), grad, slope)[0]


def outer_sloped(column, row, slope):
    return by_rows(lambda part, by: (((spread_to(part, by.shape[1]) * row) * by).astype(BF16),), column, slope)[0]


def rows_of(shape):
    return lax.broadcasted_iota(jnp.int32, shape, 0)


def schulz(refs, steps, before=None):
    @pl.loop(0, steps)
    def _(step):
        if before is not None:
            before(step)
        matrices = [ref[...] for ref in refs]
        parts = [split(matrix) for matrix in matrices]
        grams = [product(part, part, NT) for part in parts]
        halves = [split(gram) for gram in grams]
        squares = [product(half, half) for half in halves]
        blends = [
            split(COEF_CUBIC * gram + COEF_QUINTIC * square) for gram, square in zip(grams, squares)
        ]
        moved = [product(blend, part) for blend, part in zip(blends, parts)]
        for ref, matrix, move in zip(refs, matrices, moved):
            ref[...] = COEF_LINEAR * matrix + move


def normalise(ref):
    moment = ref[...]
    norm = jnp.sqrt(jnp.sum(jnp.sum(moment * moment, axis=1, keepdims=True), axis=0, keepdims=True))
    ref[...] = moment / (norm + 1e-7)


class Layout:
    def __init__(self, mesh, replay, model):
        self.n_dp = mesh.shape["dp"]
        self.n_blk = mesh.shape["blk"]
        self.bits = int(math.log2(self.n_dp))
        self.n_dev = self.n_dp * self.n_blk
        self.replay = replay
        self.model = model
        self.real = self.n_dp * CAP
        self.batch = self.real + model
        self.width = -(-(self.real + 2) // 128) * 128
        self.rows = HSAC // self.n_blk
        self.drows = HDYN // self.n_blk
        self.mat = 64 // self.n_dp
        self.sml = 32 // self.n_dp
        self.chunks = (2 * self.mat, self.mat + self.sml)
        self.split_z = all(chunk % self.n_blk == 0 for chunk in self.chunks)
        self.owners = [self.n_dp - 5, self.n_dp - 3, self.n_dp - 1]

        groups = [("fold", g, s) for g in range(2) for s in range(self.bits)]
        groups += [(name, g) for name in ("first", "second") for g in range(2)]
        common = ["hidden", "hidden on", "lists", "own", "line", "plane", "dyn h", "dyn m", "sac m", "small"]
        common += groups
        kinds = [(name, kind) for name in ("pack", "x") for kind in ("own", "on")]
        sent = common + [("tiles", k) for k in range(3)] + kinds
        self.sent = {name: at for at, name in enumerate(sent)}
        self.sent["sac g"] = len(sent)
        self.sent["sac x"] = len(sent) + self.n_dp
        self.departures = len(sent) + 2 * self.n_dp
        self.here, self.arrivals = {}, 0
        for name in common + ["tiles", ("pack", "sibling"), ("x", "sibling")]:
            self.here[name] = self.arrivals
            self.arrivals += 1
        for name, number in (("sac g", 3), ("sac x", 3), (("pack", "like"), MEMBERS), (("x", "like"), MEMBERS)):
            self.here[name] = self.arrivals
            self.arrivals += number

    def part(self, group):
        return self.chunks[group] // self.n_blk if self.split_z else self.chunks[group]


def main_kernel(lay, *refs):
    (
        replay, model, requests, member, live, noise, sac_h, sac_m, dyn_h, dyn_m, crit_in, act_in,
        dyn_in, crit_out, act_out, dyn_out, biases, targ_in, targ_hidden, targ_out, targ_bias,
        sac_g, sac_x, dyn_x, dyn_s, small, count,
        wg, lists, asked, dhg, dmg, smg, bk, xs, nz, w1f, w1t, w1n, w2t, w2h, heads, head_t, head_f,
        rowbuf, wide, headcol, acc_h, acc_w, acc_c, acc_a, acc_m, acc_l, grid_c, grid_a, zr_c, zr_a,
        zf_c, zf_a, mg, mat, grow, dcols, dacc_h, dacc_w, dacc_o, dacc_m, dacc_b, dacc_l, xt, dmat,
        dpack, drow_x, bias, dhead, dhead_t, *rest,
    ) = refs
    bits = lay.bits
    bufs = (rest[:bits], rest[bits : 2 * bits])
    send, recv = rest[2 * bits :]
    sent, here_at = lay.sent, lay.here
    grids, zrs, zfs = (grid_c, grid_a), (zr_c, zr_a), (zf_c, zf_a)
    n_dp, n_blk = lay.n_dp, lay.n_blk
    me = lax.axis_index("dp")
    z = lax.axis_index("blk")
    core = lax.rem(me, 2)
    sibling = me + 1 - 2 * core
    is_dyn = me < MEMBERS
    dyn_e = jnp.minimum(me, MEMBERS - 1)
    is_actor = me == lay.owners[2]
    is_critic = jnp.logical_or(me == lay.owners[0], me == lay.owners[1])
    is_sac = jnp.logical_or(is_actor, is_critic)
    sac_k = jnp.clip((me - lay.owners[0]) // 2, 0, 2)

    def on_plane(src, dst, ssem, rsem, peer):
        return pltpu.make_async_remote_copy(
            src_ref=src, dst_ref=dst, send_sem=ssem, recv_sem=rsem,
            device_id={"dp": peer}, device_id_type=MESH,
        )

    def on_line(src, dst, ssem, rsem, peer):
        return pltpu.make_async_remote_copy(
            src_ref=src, dst_ref=dst, send_sem=ssem, recv_sem=rsem,
            device_id={"blk": peer}, device_id_type=MESH,
        )

    def over(number, body):
        if number <= 8:
            for off in range(1, number):
                body(off)
        else:
            pl.loop(1, number)(body)

    def plane_peers(body):
        over(n_dp, lambda off: body(lax.rem(me + off, n_dp)))

    def like_peers(body):
        over(n_dp // 2, lambda off: body(lax.rem(me + 2 * off, n_dp)))

    def line_peers(body):
        over(n_blk, lambda off: body(lax.rem(z + off, n_blk)))

    def has_sent(view, name):
        at = send.at[sent[name]]
        on_plane(view, view, at, at, sibling).wait_send()

    def has_come(view, name):
        at = recv.at[here_at[name]]
        on_plane(view, view, at, at, sibling).wait_recv()

    barrier = pltpu.get_barrier_semaphore()
    plane_peers(lambda peer: pl.semaphore_signal(barrier, inc=1, device_id={"dp": peer}, device_id_type=MESH))
    line_peers(lambda peer: pl.semaphore_signal(barrier, inc=1, device_id={"blk": peer}, device_id_type=MESH))
    wg[0] = sac_h[...].astype(BF16)
    lists[0] = requests[...]
    lists[1] = member[...]
    pl.semaphore_wait(barrier, n_dp - 1 + n_blk - 1)

    half_rows = pl.ds(pl.multiple_of(core * (lay.rows // 2), lay.rows // 2), lay.rows // 2)

    def slot_from(owner, at):
        return lax.rem(owner - at + n_blk, n_blk)

    def hidden_copy(peer):
        src = wg.at[0, :, half_rows]
        dst = wg.at[slot_from(z, peer), :, half_rows]
        return on_line(src, dst, send.at[sent["hidden"]], recv.at[here_at["hidden"]], peer)

    def hidden_on():
        view = wg.at[pl.ds(1, n_blk - 1), :, half_rows]
        return on_plane(view, view, send.at[sent["hidden on"]], recv.at[here_at["hidden on"]], sibling)

    def list_copy(peer):
        return on_plane(lists, asked.at[me], send.at[sent["lists"]], recv.at[here_at["lists"]], peer)

    line_peers(lambda peer: hidden_copy(peer).start())
    plane_peers(lambda peer: list_copy(peer).start())
    asked[me] = lists[...]

    def dyn_h_copy(peer):
        return on_line(dyn_h.at[dyn_e], dhg.at[z], send.at[sent["dyn h"]], recv.at[here_at["dyn h"]], peer)

    def dyn_m_copy(peer):
        return on_line(dyn_m.at[dyn_e], dmg.at[z], send.at[sent["dyn m"]], recv.at[here_at["dyn m"]], peer)

    def sac_m_copy(peer):
        return on_line(sac_m.at[sac_k], smg.at[z], send.at[sent["sac m"]], recv.at[here_at["sac m"]], peer)

    alive = live[...].astype(F32).reshape(1, lay.model)
    bias[...] = biases[...].reshape(1, NB)
    xs[42:56, :] = jnp.zeros((14, lay.batch), F32)
    xs[0:FEAT, lay.real : lay.batch] = model[...]
    xs[42:43, lay.real : lay.batch] = alive
    nz[...] = jnp.zeros_like(nz)
    for which in range(2):
        nz[which, 1:7, :] = noise[:, which, :]
    firsts = [
        (targ_in[:, 0, :], targ_bias[0:1, 0:HSAC]),
        (targ_in[:, 1, :], targ_bias[1:2, 0:HSAC]),
        (crit_in[:, 0, :], bias[:, CB1 : CB1 + HSAC]),
        (crit_in[:, 1, :], bias[:, CB1 + HSAC : CB1 + 2 * HSAC]),
        (act_in[...], bias[:, AB1 : AB1 + HSAC]),
    ]
    w1f[...] = jnp.zeros_like(w1f)
    for net, (weights, offset) in enumerate(firsts):
        w1f[net, 0 : weights.shape[0], :] = rounded(weights)
        for at, piece in enumerate(pieces(offset)):
            w1f[net, IN + at : IN + at + 1, :] = piece.astype(F32)
        w1t[net] = (0.5 * w1f[net].T).astype(BF16)
    for k in range(2):
        w1n[k] = w1f[2 + k, 16:32, :].astype(BF16)
    for net in range(2):
        w2t[net] = (0.5 * rounded(targ_hidden[net])).T.astype(BF16)
    has_come(wg.at[pl.ds(0, n_blk - 1), :, half_rows], "hidden")
    hidden_on().start()

    rowbuf[...] = jnp.zeros_like(rowbuf)
    rowbuf[0:1, :] = targ_bias[0:1, HSAC : 2 * HSAC]
    rowbuf[1:2, :] = targ_bias[1:2, HSAC : 2 * HSAC]
    rowbuf[2:3, :] = bias[:, CB2 : CB2 + HSAC]
    rowbuf[3:4, :] = bias[:, CB2 + HSAC : CB2 + 2 * HSAC]
    rowbuf[4:5, :] = bias[:, AB2 : AB2 + HSAC]
    rowbuf[5:7, :] = rounded(crit_out[...])
    columns = 0.5 * rowbuf[...].T
    for at in range(7):
        wide[at] = jnp.broadcast_to(columns[:, at : at + 1], (HSAC, 128))
    rowbuf[...] = jnp.zeros_like(rowbuf)
    rowbuf[0:1, 1:7] = bias[:, AB3 : AB3 + ACT]
    rowbuf[0:1, 9:15] = bias[:, AB3 + ACT : AB3 + 2 * ACT]
    headcol[...] = rowbuf[:, 0:128].T
    head_f[...] = jnp.zeros_like(head_f)
    for k in range(2):
        head_f[0:1, :] = targ_out[k : k + 1, :]
        heads[k] = head_f[...].astype(BF16)
        head_f[0:1, :] = crit_out[k : k + 1, :]
        heads[2 + k] = head_f[...].astype(BF16)
    head_f[0:1, :] = jnp.zeros((1, HSAC), F32)
    head_f[1:7, :] = act_out[0:ACT, :]
    head_f[9:15, :] = act_out[ACT : 2 * ACT, :]
    heads[4] = head_f[...].astype(BF16)
    head_t[...] = (0.5 * rounded(head_f[...])).T.astype(BF16)
    for ref in (acc_h, acc_w, acc_c, acc_a, acc_m, acc_l):
        ref[...] = jnp.zeros_like(ref)

    data = replay[...]
    sums = jnp.sum(data[0:24], axis=1, keepdims=True)
    squares = jnp.sum(data[0:24] * data[0:24], axis=1, keepdims=True)
    living = jnp.sum(alive, axis=1, keepdims=True)

    has_come(asked.at[pl.ds(0, n_dp - 1)], "lists")
    spread = (
        lax.rem(lax.broadcasted_iota(jnp.int32, (CAP, lay.real), 1), CAP)
        == lax.broadcasted_iota(jnp.int32, (CAP, lay.real), 0)
    ).astype(F32)
    here = (
        lax.broadcasted_iota(jnp.int32, (n_dp, lay.real), 1) // CAP
        == lax.broadcasted_iota(jnp.int32, (n_dp, lay.real), 0)
    )

    def in_lanes(which):
        values = asked[:, which, me, :].astype(F32)
        wide = lax.dot_general(
            values, spread, NN, precision=lax.Precision.HIGHEST, preferred_element_type=F32
        )
        return jnp.sum(jnp.where(here, wide, 0.0), axis=0, keepdims=True)

    slots = in_lanes(0)
    wanted = jnp.maximum(slots, 0.0).astype(jnp.int32)
    hot = (rows_of((lay.replay, lay.real)) == wanted).astype(BF16)
    high, middle, low = pieces(data)
    picked = dot(high, hot) + dot(middle, hot) + dot(low, hot)
    mine = me * n_blk
    bk[mine, 0:FEAT, 0 : lay.real] = picked
    bk[mine, 42:43, 0 : lay.real] = (slots >= 0.0).astype(F32)
    bk[mine, 43:44, 0 : lay.real] = in_lanes(1)
    bk[mine, 44:48, 0 : lay.real] = jnp.zeros((4, lay.real), F32)
    bk[mine, :, lay.real : lay.width] = jnp.zeros((48, lay.width - lay.real), F32)
    bk[mine, 0:24, lay.real : lay.real + 1] = sums
    bk[mine, 0:24, lay.real + 1 : lay.real + 2] = squares
    bk[mine, 24:25, lay.real : lay.real + 1] = living

    def slot_of(block):
        line = lax.rem(block, n_blk)
        return block - line + slot_from(line, z)

    def block_line(peer):
        dst = bk.at[me * n_blk + slot_from(z, peer)]
        return on_line(bk.at[mine], dst, send.at[sent["line"]], recv.at[here_at["line"]], peer)

    def block_own(peer):
        view = bk.at[mine]
        return on_plane(view, view, send.at[sent["own"]], recv.at[here_at["own"]], peer)

    def block_plane(peer):
        view = bk.at[pl.ds(mine + 1, n_blk - 1)]
        return on_plane(view, view, send.at[sent["plane"]], recv.at[here_at["plane"]], peer)

    plane_peers(lambda peer: block_own(peer).start())
    line_peers(lambda peer: block_line(peer).start())

    @pl.when(is_dyn)
    def _():
        line_peers(lambda peer: dyn_h_copy(peer).start())
        line_peers(lambda peer: dyn_m_copy(peer).start())

    @pl.when(is_sac)
    def _():
        line_peers(lambda peer: sac_m_copy(peer).start())

    has_come(wg.at[pl.ds(0, n_blk - 1), :, half_rows], "hidden on")
    for k in range(3):
        for block in range(n_blk):
            w2h[k, block * lay.rows : (block + 1) * lay.rows, :] = (
                0.5 * wg[slot_from(block, z), k].astype(F32)
            ).astype(BF16)
        w2t[2 + k] = w2h[k].astype(F32).T.astype(BF16)

    log_alpha = bias[:, LOGA : LOGA + 1]
    alpha = jnp.exp(log_alpha)
    last = [
        targ_bias[0:1, 2 * HSAC : 2 * HSAC + 1],
        targ_bias[1:2, 2 * HSAC : 2 * HSAC + 1],
        bias[:, CB3 : CB3 + 1],
        bias[:, CB3 + 1 : CB3 + 2],
    ]
    n_tiles = lay.batch // TILE
    row8 = rows_of((8, TILE))
    act_rows = jnp.logical_and(row8 >= 1, row8 < 1 + ACT)

    def place_of(step):
        return pl.ds(pl.multiple_of(lax.rem(step + 1, n_tiles) * TILE, TILE), TILE)

    def ones16(width=TILE):
        return jnp.ones((16, width), BF16)

    def framed(first_row, used, where):
        row32 = rows_of((32, TILE))
        ones3 = jnp.logical_and(row32 >= IN, row32 < IN + 3).astype(F32)
        return jnp.where(row32 < used, xs[first_row : first_row + 32, where], ones3)

    def hidden(inputs, net):
        first, slope1 = gated(dot(w1t[net], inputs))
        second, slope2 = gated(dot(w2t[net], first), wide[net])
        return first, slope1, second, slope2

    def policy(inputs, which, where):
        first, slope1, second, slope2 = hidden(inputs, 4)
        out = dot(heads[4], second) + headcol[0:16, 0:1]
        bent = jnp.tanh(out[8:16])
        log_scale = -5.0 + 3.5 * (bent + 1.0)
        draw = nz[which, :, where]
        moved = jnp.exp(log_scale) * draw
        latent = out[0:8] + moved
        terms = (
            -0.5 * draw * draw
            - log_scale
            - 0.9189385
            - 2.0 * (0.6931472 - latent - softplus(-2.0 * latent))
        )
        log_prob = jnp.sum(jnp.where(act_rows, terms, 0.0), axis=0, keepdims=True)
        action = jnp.where(act_rows, jnp.tanh(latent), 0.0)
        return action, log_prob, bent, moved, (first, slope1, second, slope2)

    def with_action(inputs, action):
        middle_rows = jnp.where(act_rows, action, inputs[16:24])
        return jnp.concatenate([inputs[0:16], middle_rows, inputs[24:32]], 0).astype(BF16)

    def critic(inputs, net):
        kept = hidden(inputs, net)
        value = dot(heads[net], kept[2])[0:1] + last[net]
        return value, kept

    def add_hidden(k, first, grad):
        acc_h[k] += dot(jnp.concatenate([first, ones16()], 0), grad, NT)

    @pl.loop(0, n_tiles)
    def _(step):
        @pl.when(step == 1)
        def _():
            has_come(bk.at[pl.ds(0, n_blk - 1)], "line")
            plane_peers(lambda peer: block_plane(peer).start())

        @pl.when(step == n_tiles - 1)
        def _():
            has_come(bk.at[pl.ds(0, n_dp - 1)], "own")
            lanes = lax.broadcasted_iota(jnp.int32, (48, lay.width), 1) // CAP

            def gather(owner, total):
                turned = pltpu.roll(
                    bk[owner * n_blk], lax.rem((owner - me) * CAP + lay.width, lay.width), axis=1
                )
                return jnp.where(lanes == owner, turned, total)

            own = lax.fori_loop(0, n_dp, gather, jnp.zeros((48, lay.width), F32))
            xs[0:48, 0 : lay.real] = own[:, 0 : lay.real]

        where = place_of(step)
        now_in = framed(0, IN, where).astype(BF16)
        next_f = framed(24, OBS, where)
        reward = xs[23:24, where]
        done = xs[41:42, where]
        weight = xs[42:43, where]
        row16 = rows_of((16, TILE))
        next_action, next_prob, _, _, _ = policy(next_f.astype(BF16), 1, where)
        aim_in = with_action(next_f, next_action)
        aim = jnp.minimum(critic(aim_in, 0)[0], critic(aim_in, 1)[0])
        target = reward + DISCOUNT * (1.0 - done) * (aim - alpha * next_prob)
        loss = jnp.zeros((1, TILE), F32)
        heads_grad = []
        for k in range(2):
            value, (c1, dc1, c2, dc2) = critic(now_in, 2 + k)
            miss = value - target
            loss += 0.5 * miss * miss
            g3 = rounded(weight * miss)
            g3_rows = jnp.where(row16 == 0, g3, 0.0).astype(BF16)
            heads_grad.append(g3_rows)
            acc_c[k] += dot(g3_rows, c2, NT)
            g2 = outer_sloped(wide[5 + k], g3, dc2)
            add_hidden(k, c1, g2)
            g1 = sloped(dot(w2h[k], g2), dc1)
            acc_w[k] += dot(now_in, g1, NT)
        acc_m[:, 16:48] += dot(ones16(), jnp.concatenate(heads_grad, 0), NT)
        acc_l[0:1, :] += weight * loss

    def put_matrix(group, k, at):
        for chunk in range(n_dp):
            tile = chunk * lay.mat
            side, row = tile // 32, tile % 32
            grids[group][chunk, at * lay.mat : (at + 1) * lay.mat] = acc_h[
                k, row * 8 : (row + lay.mat) * 8, side * 128 : (side + 1) * 128
            ].reshape(lay.mat, 8, 128)

    def put(row, value):
        for at in range(value.shape[0] // 8):
            for side in range(value.shape[1] // 128):
                tile = side * (R_SMALL // 8) + row // 8 + at
                grid_a[tile // lay.sml, lay.mat + tile % lay.sml] = value[
                    at * 8 : at * 8 + 8, side * 128 : (side + 1) * 128
                ]

    def bit(b):
        return lax.rem(me // (1 << b), 2)

    starts, faces, partners = [], [], []
    start = 0
    for s in range(bits):
        if s == 0:
            face, stride = core, 1
        else:
            face = (1 - core) * bit(s) + core * bit(bits - s)
            stride = (1 - core) * (1 << s) + core * (1 << (bits - s))
        starts.append(start)
        faces.append(face)
        partners.append(me + (1 - 2 * face) * stride)
        start = start + face * (n_dp >> (s + 1))
    place = start

    def fold_copy(group, s):
        half = n_dp >> (s + 1)
        begin = starts[s] + (1 - faces[s]) * half
        return on_plane(
            grids[group].at[pl.ds(begin, half)], bufs[group][s], send.at[sent["fold", group, s]],
            recv.at[here_at["fold", group, s]], partners[s],
        )

    def fold_wait(group, s):
        half = n_dp >> (s + 1)
        begin = starts[s] + faces[s] * half
        fold_copy(group, s).wait_recv()
        for at in range(half):
            grids[group][begin + at] += bufs[group][s][at]

    def line_first(group, peer):
        if lay.split_z:
            src = grids[group].at[place, pl.ds(peer * lay.part(group), lay.part(group))]
        else:
            src = grids[group].at[place]
        name = ("first", group)
        return on_line(src, zrs[group].at[z], send.at[sent[name]], recv.at[here_at[name]], peer)

    def line_second(group, peer):
        view = zfs[group].at[pl.ds(z * lay.part(group), lay.part(group))]
        name = ("second", group)
        return on_line(view, view, send.at[sent[name]], recv.at[here_at[name]], peer)

    def firsts_of(group):
        return zrs[group].at[pl.ds(0, n_blk - 1)]

    def seconds_of(group):
        return zfs[group].at[pl.ds(0, (n_blk - 1) * lay.part(group))]

    def line_start(group):
        line_peers(lambda peer: line_first(group, peer).start())

    def line_sum(group):
        part, zr, zf = lay.part(group), zrs[group], zfs[group]
        has_come(firsts_of(group), ("first", group))
        zr[z] = grids[group][place, pl.ds(z * part, part)] if lay.split_z else grids[group][place]
        whole = zr[0]
        for block in range(1, n_blk):
            whole = whole + zr[block]
        if lay.split_z:
            zf[pl.ds(z * part, part)] = whole
            line_peers(lambda peer: line_second(group, peer).start())
        else:
            zf[...] = whole

    def line_end(group):
        if lay.split_z:
            has_come(seconds_of(group), ("second", group))

    def tile_copy(k, owner):
        src = zfs[k // 2].at[pl.ds((k % 2) * lay.mat, lay.mat)]
        return on_plane(src, mg.at[place], send.at[sent["tiles", k]], recv.at[here_at["tiles"]], owner)

    def send_tiles(group):
        for k in (0, 1) if group == 0 else (2,):
            @pl.when(me != lay.owners[k])
            def _():
                tile_copy(k, lay.owners[k]).start()

            @pl.when(me == lay.owners[k])
            def _():
                mg[place] = zfs[group][(k % 2) * lay.mat : (k % 2 + 1) * lay.mat]

    def small_copy(peer):
        return on_plane(
            zf_a.at[pl.ds(lay.mat, lay.sml)], small.at[pl.ds(place * lay.sml, lay.sml)],
            send.at[sent["small"]], recv.at[here_at["small"]], peer,
        )

    def chain(group):
        steps = [functools.partial(lambda s: fold_copy(group, s).start(), 0)]

        def fold(s):
            fold_wait(group, s)
            if s + 1 < bits:
                fold_copy(group, s + 1).start()
            else:
                line_start(group)

        steps += [functools.partial(fold, s) for s in range(bits)]
        steps.append(lambda: line_sum(group))

        def finish():
            line_end(group)
            send_tiles(group)
            if group == 1:
                plane_peers(lambda peer: small_copy(peer).start())
                small[pl.ds(place * lay.sml, lay.sml)] = zf_a[lay.mat :]

        steps.append(finish)
        return steps

    critic_chain, actor_chain = chain(0), chain(1)
    per = DYN_TILE // lay.real
    dyn_tiles = lay.n_dev // per
    inside = min(bits + 2, n_tiles - 1)
    in_actor = {step: [critic_chain[step]] for step in range(1, inside + 1)}
    in_dyn = {}
    for at, event in enumerate(critic_chain[inside + 1 :]):
        in_dyn.setdefault(min(at, dyn_tiles - 1), []).append(event)
    for at in range(1, bits + 1):
        in_dyn.setdefault(min(at, dyn_tiles - 1), []).append(actor_chain[at])

    def take(slots, step):
        for at, events in slots.items():
            @pl.when(step == at)
            def _():
                for event in events:
                    event()

    for k in range(2):
        put_matrix(0, k, k)
    critic_chain[0]()

    @pl.loop(0, n_tiles)
    def _(step):
        take(in_actor, step)
        where = place_of(step)
        now_f = framed(0, IN, where)
        now_in = now_f.astype(BF16)
        weight = xs[42:43, where]
        action, log_prob, bent, moved, (a1, da1, a2, da2) = policy(now_in, 0, where)
        judged_in = with_action(now_f, action)
        loss = alpha * log_prob - log_alpha * (log_prob + TARGET_ENTROPY)
        grad_action = jnp.zeros((8, TILE), F32)
        for k in range(2):
            judged, (_, df1, _, df2) = critic(judged_in, 2 + k)
            loss -= 0.5 * judged
            g2 = outer_sloped(wide[5 + k], -0.5 * weight, df2)
            g1 = sloped(dot(w2h[k], g2), df1)
            grad_action += dot(w1n[k], g1)[0:8]
        grad_latent = 2.0 * alpha * weight * action + grad_action * (1.0 - action * action)
        grad_scale = grad_latent * moved - alpha * weight
        grad_bent = grad_scale * 3.5 * (1.0 - bent * bent)
        g3 = jnp.concatenate(
            [jnp.where(act_rows, grad_latent, 0.0), jnp.where(act_rows, grad_bent, 0.0)], 0
        ).astype(BF16)
        acc_a[...] += dot(g3, a2, NT)
        acc_m[:, 0:16] += dot(ones16(), g3, NT)
        g2 = sloped(dot(head_t[...], g3), da2)
        add_hidden(2, a1, g2)
        g1 = sloped(dot(w2h[2], g2), da1)
        acc_w[2] += dot(now_in, g1, NT)
        acc_l[0:1, :] += weight * loss
        acc_l[1:2, :] += weight * (log_prob + TARGET_ENTROPY)

    put_matrix(1, 2, 0)
    for k in range(3):
        put(R_IN + 24 * k, acc_w[k, 0:24, :])
    put(R_HEAD, acc_a[...])
    rowbuf[0:1, :] = acc_c[0, 0:1, :]
    rowbuf[1:2, :] = acc_c[1, 0:1, :]
    for k in range(3):
        rowbuf[2 + k : 3 + k, :] = acc_h[k, HSAC : HSAC + 1, :]
    put(R_OUT, rowbuf[...])
    folded = jnp.sum(acc_l[...], axis=1, keepdims=True)
    rowbuf[...] = jnp.zeros_like(rowbuf)
    rowbuf[0:1, 0:48] = acc_m[0:1, :]
    rowbuf[0:1, 64:65] = folded[0:1]
    rowbuf[0:1, 65:66] = folded[1:2]
    put(R_MISC, rowbuf[...])
    put(R_MISC + 8, jnp.zeros((R_SMALL - R_MISC - 8, HSAC), F32))
    actor_chain[0]()

    has_come(bk.at[pl.ds(0, (n_dp - 1) * (n_blk - 1))], "plane")
    lane0 = lay.real // 128 * 128

    def add_block(at, carry):
        sides, fills = carry
        slot = slot_of(at)
        return sides + bk[slot, 0:32, lane0 : lane0 + 128], fills + bk[slot, 40:48, 0 : lay.real]

    sides, fills = lax.fori_loop(
        0, lay.n_dev, add_block, (jnp.zeros((32, 128), F32), jnp.zeros((8, lay.real), F32))
    )
    at = lay.real - lane0
    rows_all = float(lay.replay * lay.n_dev)
    centre = sides[0:24, at : at + 1] / rows_all
    scale = lax.rsqrt(sides[0:24, at + 1 : at + 2] / rows_all - centre * centre + 1e-6)
    total = sides[24:25, at : at + 1] + jnp.sum(fills[2:3, :], axis=1, keepdims=True)
    count[...] = jnp.broadcast_to(total, (8, 128))

    def dyn_bias(start, width):
        row = jnp.zeros((1, width), F32)
        for e in range(MEMBERS):
            row = jnp.where(me == e, bias[:, start + width * e : start + width * (e + 1)], row)
        return row

    @pl.when(is_dyn)
    def _():
        w1f[0] = jnp.zeros((32, HSAC), F32)
        w1f[0, 0:IN, 0:HDYN] = rounded(dyn_in[dyn_e])
        for at, piece in enumerate(pieces(dyn_bias(DB1, HDYN))):
            w1f[0, IN + at : IN + at + 1, 0:HDYN] = piece.astype(F32)
        w1t[0] = (0.5 * w1f[0].T).astype(BF16)
        rowbuf[...] = jnp.zeros_like(rowbuf)
        rowbuf[0:1, 0:HDYN] = dyn_bias(DB2, HDYN)
        head_row = dyn_bias(DB3, DOUT)
        rowbuf[1:2, 0:HALF] = head_row[:, 0:HALF]
        rowbuf[1:2, 24 : 24 + HALF] = head_row[:, HALF:DOUT]
        rowbuf[2:3, 0:HALF] = bias[:, MAXLV : MAXLV + HALF]
        rowbuf[3:4, 0:HALF] = bias[:, MINLV : MINLV + HALF]
        dcols[...] = rowbuf[...].T
        wide[0] = jnp.broadcast_to(0.5 * dcols[:, 0:1], (HSAC, 128))
        dpack[...] = jnp.zeros_like(dpack)
        dpack[0:HALF, 0:HDYN] = dyn_out[dyn_e, 0:HALF, :]
        dpack[24 : 24 + HALF, 0:HDYN] = dyn_out[dyn_e, HALF:DOUT, :]
        dhead[...] = dpack[0:48, :].astype(BF16)
        dhead_t[...] = (0.5 * rounded(dpack[0:48, :])).T.astype(BF16)
        dpack[...] = jnp.zeros_like(dpack)

        has_come(dhg.at[pl.ds(0, n_blk - 1)], "dyn h")
        has_come(dmg.at[pl.ds(0, n_blk - 1)], "dyn m")
        dhg[z] = dyn_h[dyn_e]
        dmg[z] = dyn_m[dyn_e]
        dmat[...] = jnp.zeros_like(dmat)
        for block in range(n_blk):
            dmat[block * lay.drows : (block + 1) * lay.drows, 0:HDYN] = 0.5 * rounded(dhg[block])
        w2h[0] = dmat[...].astype(BF16)
        w2t[0] = dmat[...].T.astype(BF16)
        for ref in (dacc_h, dacc_w, dacc_o, dacc_m, dacc_b, dacc_l):
            ref[...] = jnp.zeros_like(ref)

    @pl.loop(0, dyn_tiles)
    def _(tile):
        take(in_dyn, tile)

        @pl.when(is_dyn)
        def _():
            for at in range(per):
                slot = slot_of(tile * per + at)
                xt[:, at * lay.real : (at + 1) * lay.real] = bk[slot, :, 0 : lay.real]
            now = xt[0:24, :]
            later = xt[24:48, :]
            row24 = rows_of((24, DYN_TILE))
            scaled = jnp.where(row24 < IN, (now - centre) * scale, 1.0)
            inputs = jnp.concatenate([scaled, (rows_of((8, DYN_TILE)) < 2).astype(F32)], 0).astype(BF16)
            first, slope1 = gated(dot(w1t[0], inputs))
            second, slope2 = gated(dot(w2t[0], first), wide[0])
            out = dot(dhead[...], second) + dcols[0:48, 1:2]
            used = row24 < HALF
            upper = dcols[0:24, 2:3]
            lower = dcols[0:24, 3:4]
            gap1 = upper - out[24:48]
            gap2 = upper - softplus(gap1) - lower
            log_var = lower + softplus(gap2)
            error = out[0:24] - jnp.where(row24 == OBS, now[23:24], later - now)
            inverse = jnp.exp(-log_var)
            weight = xt[42:43, :] * (xt[43:44, :] == me.astype(F32)).astype(F32)
            spread_term = error * error * inverse
            nll = jnp.sum(jnp.where(used, spread_term + log_var, 0.0), axis=0, keepdims=True)
            dacc_l[0:1, :] += weight * nll
            grad_mu = 2.0 * weight * error * inverse
            grad_lv = weight * (1.0 - spread_term)
            open1 = sigmoid(gap1)
            open2 = sigmoid(gap2)
            grad_lv1 = grad_lv * open2
            dacc_b[0] += jnp.where(used, grad_lv1 * (1.0 - open1), 0.0)
            dacc_b[1] += jnp.where(used, grad_lv * (1.0 - open2), 0.0)
            g3 = jnp.concatenate(
                [jnp.where(used, grad_mu, 0.0), jnp.where(used, grad_lv1 * open1, 0.0)], 0
            ).astype(BF16)
            dacc_o[...] += dot(g3, second, NT)
            dacc_m[...] += dot(ones16(DYN_TILE), g3, NT)
            g2 = sloped(dot(dhead_t[...], g3), slope2)
            dacc_h[...] += dot(jnp.concatenate([first, ones16(DYN_TILE)], 0), g2, NT)
            g1 = sloped(dot(w2h[0], g2), slope1)
            dacc_w[...] += dot(inputs, g1, NT)

    out_of = {"pack": dyn_s, "x": dyn_x}

    def member_copy(name, src, owner, kind, sem, peer):
        return on_plane(src, out_of[name].at[owner], send.at[sent[name, kind]], recv.at[sem], peer)

    def give(name, src):
        like_peers(
            lambda peer: member_copy(name, src, dyn_e, "own", here_at[name, "like"] + dyn_e, peer).start()
        )
        member_copy(name, src, dyn_e, "own", here_at[name, "sibling"], sibling).start()

    def hand_on(name):
        def body(peer):
            @pl.when(peer < MEMBERS)
            def _():
                owner = jnp.minimum(peer, MEMBERS - 1)
                view = out_of[name].at[owner]
                member_copy(name, view, owner, "on", here_at[name, "like"] + owner, sibling).wait_recv()
                member_copy(name, view, owner, "on", here_at[name, "sibling"], sibling).start()

        like_peers(body)

    even, odd = (MEMBERS + 1) // 2, MEMBERS // 2
    handed = even - core * (even - odd) - jnp.where(is_dyn, 1, 0)

    def from_sibling(name):
        for side, number in ((0, odd), (1, even)):
            @pl.when(core == side)
            def _():
                has_come(out_of[name].at[pl.ds(0, number)], (name, "sibling"))

    def gave(name):
        @pl.when(is_dyn)
        def _():
            for begin in range(0, n_dp // 2, MEMBERS):
                number = min(MEMBERS, n_dp // 2 - begin)
                has_sent(out_of[name].at[pl.ds(0, number)], (name, "own"))

        for number in (even, even - 1, even - 2):
            @pl.when(handed == number)
            def _():
                has_sent(out_of[name].at[pl.ds(0, number)], (name, "on"))

    def line_rows(ref):
        rows = ref[0 : lay.drows, 0:HDYN]
        for block in range(1, n_blk):
            rows = jnp.where(z == block, ref[block * lay.drows : (block + 1) * lay.drows, 0:HDYN], rows)
        return rows

    def sac_g_copy(k, peer):
        src = grow.at[pl.ds(pl.multiple_of(z * lay.rows, lay.rows), lay.rows)]
        return on_plane(src, sac_g.at[k], send.at[sent["sac g"] + peer], recv.at[here_at["sac g"] + k], peer)

    def sac_x_copy(k, peer):
        src = mat.at[pl.ds(pl.multiple_of(z * lay.rows, lay.rows), lay.rows)]
        return on_plane(src, sac_x.at[k], send.at[sent["sac x"] + peer], recv.at[here_at["sac x"] + k], peer)

    mine_rows = pl.ds(pl.multiple_of(z * lay.rows, lay.rows), lay.rows)

    def take_matrix():
        has_come(smg.at[pl.ds(0, n_blk - 1)], "sac m")
        smg[z] = sac_m[sac_k]
        has_come(mg.at[pl.ds(0, n_dp - 1)], "tiles")
        for chunk in range(n_dp):
            tile = chunk * lay.mat
            side, row = tile // 32, tile % 32
            grow[row * 8 : (row + lay.mat) * 8, side * 128 : (side + 1) * 128] = mg[chunk].reshape(
                lay.mat * 8, 128
            )
        sac_g[sac_k] = grow[mine_rows, :]
        plane_peers(lambda peer: sac_g_copy(sac_k, peer).start())
        for block in range(n_blk):
            at = slice(block * lay.rows, (block + 1) * lay.rows)
            mat[at, :] = MOMENTUM * smg[block] + grow[at, :] / total
        normalise(mat)

    actor_chain[bits + 1]()

    @pl.when(is_dyn)
    def _():
        dpack[D_IN : D_IN + 24, :] = dacc_w[0:24, :]
        dpack[D_OUT : D_OUT + HALF, :] = dacc_o[0:HALF, :]
        dpack[D_OUT + HALF : D_OUT + DOUT, :] = dacc_o[24 : 24 + HALF, :]
        dpack[D_B2 : D_B2 + 1, :] = dacc_h[HSAC : HSAC + 1, :]
        dpack[D_B3 : D_B3 + 1, 0:48] = dacc_m[0:1, :]
        lanes = lax.broadcasted_iota(jnp.int32, (24, 128), 1)
        bound = jnp.where(
            lanes == 0,
            jnp.sum(dacc_b[0], axis=1, keepdims=True),
            jnp.where(lanes == 1, jnp.sum(dacc_b[1], axis=1, keepdims=True), 0.0),
        )
        dpack[D_UP : D_UP + 2, 0:24] = bound.T[0:2, :]
        dpack[D_LOSS : D_LOSS + 1, 0:128] = jnp.broadcast_to(
            jnp.sum(dacc_l[0:1, :], axis=1, keepdims=True), (1, 128)
        )
        dpack[D_HID : D_HID + lay.drows, 0:HDYN] = line_rows(dacc_h)
        dyn_s[dyn_e] = dpack[...]
        give("pack", dpack)
        dmat[...] = jnp.zeros_like(dmat)
        for block in range(n_blk):
            at = slice(block * lay.drows, (block + 1) * lay.drows)
            dmat[at, 0:HDYN] = MOMENTUM * dmg[block] + dacc_h[at, 0:HDYN] / total
        normalise(dmat)

    pl.when(is_critic)(take_matrix)
    if n_dp <= MEMBERS + 1:
        only_dyn = jnp.logical_and(is_dyn, jnp.logical_not(is_critic))
        pairs = [(is_critic, [dmat, mat]), (only_dyn, [dmat])]
    else:
        pairs = [(is_critic, [mat]), (is_dyn, [dmat])]
    def sum_end(step):
        pl.when(step == 2)(actor_chain[bits + 2])

    for test, matrices in pairs:
        pl.when(test)(functools.partial(schulz, matrices, NS_ITERS, sum_end))
    if n_dp <= MEMBERS + 1:
        pl.when(is_actor)(actor_chain[bits + 2])
    else:
        pl.when(jnp.logical_not(jnp.logical_or(is_critic, is_dyn)))(actor_chain[bits + 2])

    def send_sac():
        sac_x[sac_k] = mat[mine_rows, :]
        plane_peers(lambda peer: sac_x_copy(sac_k, peer).start())

    @pl.when(is_dyn)
    def _():
        rows = line_rows(dmat)
        drow_x[...] = rows
        dyn_x[dyn_e] = rows
        give("x", drow_x)

    pl.when(is_critic)(send_sac)

    def sent_early():
        has_sent(wg.at[pl.ds(0, n_blk - 1), :, half_rows], "hidden")
        has_sent(wg.at[pl.ds(0, n_blk - 1), :, half_rows], "hidden on")
        has_sent(asked.at[pl.ds(0, n_dp - 1)], "lists")
        has_sent(bk.at[pl.ds(0, n_dp - 1)], "own")
        has_sent(bk.at[pl.ds(0, n_blk - 1)], "line")
        has_sent(bk.at[pl.ds(0, (n_dp - 1) * (n_blk - 1))], "plane")

        @pl.when(is_dyn)
        def _():
            has_sent(dhg.at[pl.ds(0, n_blk - 1)], "dyn h")
            has_sent(dmg.at[pl.ds(0, n_blk - 1)], "dyn m")

        @pl.when(is_sac)
        def _():
            has_sent(smg.at[pl.ds(0, n_blk - 1)], "sac m")

        for group in range(2):
            for s in range(bits):
                fold_copy(group, s).wait_send()
            has_sent(firsts_of(group), ("first", group))
            if lay.split_z:
                has_sent(seconds_of(group), ("second", group))

    @pl.when(is_actor)
    def _():
        sent_early()
        take_matrix()
        schulz([mat], NS_ITERS)
        send_sac()

    pl.when(jnp.logical_not(is_actor))(sent_early)
    hand_on("pack")
    hand_on("x")
    has_come(small.at[pl.ds(0, (n_dp - 1) * lay.sml)], "small")
    from_sibling("pack")
    from_sibling("x")
    for k in range(3):
        @pl.when(me != lay.owners[k])
        def _():
            sac_g_copy(k, me).wait_recv()
            sac_x_copy(k, me).wait_recv()

    has_sent(small.at[pl.ds(0, (n_dp - 1) * lay.sml)], "small")
    gave("pack")
    gave("x")
    for k in range(3):
        @pl.when(me != lay.owners[k])
        def _():
            tile_copy(k, lay.owners[k]).wait_send()

    @pl.when(is_sac)
    def _():
        plane_peers(lambda peer: sac_g_copy(sac_k, peer).wait_send())
        plane_peers(lambda peer: sac_x_copy(sac_k, peer).wait_send())


def adamw(weights, first, second, gradient):
    first = BETA_FIRST * first + (1.0 - BETA_FIRST) * gradient
    second = BETA_SECOND * second + (1.0 - BETA_SECOND) * gradient * gradient
    first_hat = first / (1.0 - BETA_FIRST**STEP)
    second_hat = second / (1.0 - BETA_SECOND**STEP)
    step = first_hat / (jnp.sqrt(second_hat) + 1e-8) + ADAM_DECAY * weights
    return weights - ADAM_RATE * step, first, second


def update_kernel(*refs):
    (
        sac_g, sac_x, dyn_x, dyn_s, small, count, sac_h, sac_m, dyn_h, dyn_m,
        ci, ci_m, ci_v, ai, ai_m, ai_v, di, di_m, di_v, co, co_m, co_v, ao, ao_m, ao_v,
        do, do_m, do_v, bi, bi_m, bi_v,
        sac_new, sac_mom, dyn_new, dyn_mom, ci_n, ci_mn, ci_vn, ai_n, ai_mn, ai_vn, di_n, di_mn,
        di_vn, co_n, co_mn, co_vn, ao_n, ao_mn, ao_vn, do_n, do_mn, do_vn, bi_n, bi_mn, bi_vn,
        loss, counted, bg,
    ) = refs
    total = count[0:1, 0:1]
    sac_mom[...] = MOMENTUM * sac_m[...] + sac_g[...] / total.reshape(1, 1, 1)
    sac_new[...] = sac_h[...] * (1.0 - MUON_RATE * MUON_DECAY) - MUON_RATE * sac_x[...]
    dyn_rows = dyn_s[:, D_HID : D_HID + dyn_m.shape[1], 0:HDYN]
    dyn_mom[...] = MOMENTUM * dyn_m[...] + dyn_rows / total.reshape(1, 1, 1)
    dyn_new[...] = dyn_h[...] * (1.0 - MUON_RATE * MUON_DECAY) - MUON_RATE * dyn_x[...]

    def rows(row, number):
        sides = []
        for side in range(2):
            at = side * (R_SMALL // 8) + row // 8
            sides.append(small[at : at + -(-number // 8)].reshape(-1, 128))
        return jnp.concatenate(sides, 1)

    def store(outs, at, values):
        for out, value in zip(outs, values):
            out[at] = value

    outs = (ci_n, ci_mn, ci_vn)
    for k in range(2):
        at = (slice(None), k, slice(None))
        grad = rows(R_IN + 24 * k, 24)
        bg[:, CB1 + HSAC * k : CB1 + HSAC * (k + 1)] = grad[IN : IN + 1]
        store(outs, at, adamw(ci[at], ci_m[at], ci_v[at], grad[0:IN] / total))
    grad = rows(R_IN + 48, 24)
    bg[:, AB1 : AB1 + HSAC] = grad[IN : IN + 1]
    store((ai_n, ai_mn, ai_vn), ..., adamw(ai[...], ai_m[...], ai_v[...], grad[0:OBS] / total))
    grad = rows(R_HEAD, 16)
    for at, row in ((slice(0, ACT), slice(1, 1 + ACT)), (slice(ACT, 2 * ACT), slice(9, 9 + ACT))):
        store((ao_n, ao_mn, ao_vn), at, adamw(ao[at], ao_m[at], ao_v[at], grad[row] / total))
    grad = rows(R_OUT, 8)
    store((co_n, co_mn, co_vn), ..., adamw(co[...], co_m[...], co_v[...], grad[0:2] / total))
    bg[:, CB2 : CB2 + HSAC] = grad[2:3]
    bg[:, CB2 + HSAC : CB2 + 2 * HSAC] = grad[3:4]
    bg[:, AB2 : AB2 + HSAC] = grad[4:5]
    grad = rows(R_MISC, 8)
    bg[:, CB3 : CB3 + 1] = grad[0:1, 16:17]
    bg[:, CB3 + 1 : CB3 + 2] = grad[0:1, 32:33]
    bg[:, AB3 : AB3 + ACT] = grad[0:1, 1 : 1 + ACT]
    bg[:, AB3 + ACT : AB3 + 2 * ACT] = grad[0:1, 9 : 9 + ACT]
    bg[:, LOGA : LOGA + 1] = -grad[0:1, 65:66]
    total_loss = grad[0:1, 64:65]
    up = jnp.zeros((1, HALF), F32)
    low = jnp.zeros((1, HALF), F32)
    for e in range(MEMBERS):
        pack = dyn_s[e]
        total_loss = total_loss + pack[D_LOSS : D_LOSS + 1, 0:1]
        up = up + pack[D_UP : D_UP + 1, 0:HALF]
        low = low + pack[D_LOW : D_LOW + 1, 0:HALF]
        bg[:, DB1 + HDYN * e : DB1 + HDYN * (e + 1)] = pack[IN : IN + 1, 0:HDYN]
        bg[:, DB2 + HDYN * e : DB2 + HDYN * (e + 1)] = pack[D_B2 : D_B2 + 1, 0:HDYN]
        bg[:, DB3 + DOUT * e : DB3 + DOUT * e + HALF] = pack[D_B3 : D_B3 + 1, 0:HALF]
        bg[:, DB3 + DOUT * e + HALF : DB3 + DOUT * (e + 1)] = pack[D_B3 : D_B3 + 1, 24 : 24 + HALF]
        grad = pack[0:IN, 0:HDYN] / total
        store((di_n, di_mn, di_vn), e, adamw(di[e], di_m[e], di_v[e], grad))
        grad = pack[D_OUT : D_OUT + DOUT, 0:HDYN] / total
        store((do_n, do_mn, do_vn), e, adamw(do[e], do_m[e], do_v[e], grad))
    bg[:, MAXLV : MAXLV + HALF] = up
    bg[:, MINLV : MINLV + HALF] = low
    lane = lax.broadcasted_iota(jnp.int32, (1, NB), 1)
    bounds = jnp.where(
        jnp.logical_and(lane >= MAXLV, lane < MINLV),
        BOUND_WEIGHT,
        jnp.where(jnp.logical_and(lane >= MINLV, lane < LOGA), -BOUND_WEIGHT, 0.0),
    )
    grad = bg[...] / total + bounds
    flat = [ref[...].reshape(1, NB) for ref in (bi, bi_m, bi_v)]
    store((bi_n, bi_mn, bi_vn), ..., [value.reshape(NB) for value in adamw(*flat, grad)])
    loss[...] = total_loss
    counted[...] = total


def shards(
    lay, replay, model_rows, requests, member_of, model_live, noise, sac_hidden, sac_hidden_mom,
    dyn_hidden, dyn_hidden_mom, crit_in, crit_in_m, crit_in_v, act_in, act_in_m, act_in_v, dyn_in,
    dyn_in_m, dyn_in_v, crit_out, crit_out_m, crit_out_v, act_out, act_out_m, act_out_v, dyn_out,
    dyn_out_m, dyn_out_v, biases, biases_m, biases_v, targ_in, targ_hidden, targ_out, targ_bias,
):
    n_dp, n_blk, bits = lay.n_dp, lay.n_blk, lay.bits
    spec = pl.BlockSpec(memory_space=pltpu.VMEM)

    def flip(value):
        return jnp.transpose(value, (1, 0, 2))

    def swap(value):
        return jnp.swapaxes(value, -1, -2)

    def kept(value):
        return pltpu.with_memory_space_constraint(value, pltpu.VMEM)

    inputs = (
        replay, model_rows, requests, member_of, model_live, jnp.transpose(noise, (2, 0, 1)),
        sac_hidden, sac_hidden_mom, dyn_hidden, dyn_hidden_mom, flip(crit_in), act_in, dyn_in,
        crit_out, swap(act_out), swap(dyn_out), biases, flip(targ_in), targ_hidden, targ_out,
        targ_bias,
    )
    shape = jax.ShapeDtypeStruct
    rows, drows = lay.rows, lay.drows
    out_shape = (
        pltpu.VMEM((3, rows, HSAC), F32),
        pltpu.VMEM((3, rows, HSAC), F32),
        pltpu.VMEM((MEMBERS, drows, HDYN), F32),
        pltpu.VMEM((MEMBERS, D_ROWS, HSAC), F32),
        pltpu.VMEM((32, 8, 128), F32),
        pltpu.VMEM((8, 128), F32),
    )

    def vm(*dims, kind=F32):
        return pltpu.VMEM(dims, kind)

    scratch = [
        vm(n_blk, 3, rows, HSAC, kind=BF16),
        vm(2, n_dp, CAP, kind=jnp.int32),
        vm(n_dp, 2, n_dp, CAP, kind=jnp.int32),
        vm(n_blk, drows, HDYN),
        vm(n_blk, drows, HDYN),
        vm(n_blk, rows, HSAC),
        vm(lay.n_dev, 48, lay.width),
        vm(56, lay.batch),
        vm(2, 8, lay.batch),
        vm(5, 32, HSAC),
        vm(5, HSAC, 32, kind=BF16),
        vm(2, 16, HSAC, kind=BF16),
        vm(5, HSAC, HSAC, kind=BF16),
        vm(3, HSAC, HSAC, kind=BF16),
        vm(5, 16, HSAC, kind=BF16),
        vm(HSAC, 16, kind=BF16),
        vm(16, HSAC),
        vm(8, HSAC),
        vm(7, HSAC, 128),
        vm(128, 8),
        vm(3, HSAC + 16, HSAC),
        vm(3, 32, HSAC),
        vm(2, 16, HSAC),
        vm(16, HSAC),
        vm(16, 48),
        vm(8, TILE),
        vm(n_dp, lay.chunks[0], 8, 128),
        vm(n_dp, lay.chunks[1], 8, 128),
        vm(n_blk, lay.part(0), 8, 128),
        vm(n_blk, lay.part(1), 8, 128),
        vm(lay.chunks[0], 8, 128),
        vm(lay.chunks[1], 8, 128),
        vm(n_dp, lay.mat, 8, 128),
        vm(HSAC, HSAC),
        vm(HSAC, HSAC),
        vm(HSAC, 8),
        vm(HSAC + 16, HSAC),
        vm(32, HSAC),
        vm(48, HSAC),
        vm(16, 48),
        vm(2, 24, DYN_TILE),
        vm(8, DYN_TILE),
        vm(48, DYN_TILE),
        vm(HSAC, HSAC),
        vm(D_ROWS, HSAC),
        vm(drows, HDYN),
        vm(1, NB),
        vm(48, HSAC, kind=BF16),
        vm(HSAC, 48, kind=BF16),
    ]
    scratch += [vm(n_dp >> (s + 1), chunk, 8, 128) for chunk in lay.chunks for s in range(bits)]
    scratch += [pltpu.SemaphoreType.DMA((lay.departures,)), pltpu.SemaphoreType.DMA((lay.arrivals,))]
    varying = 4 * (lay.n_dev * 48 * lay.width + 72 * lay.batch + 48 * lay.replay)
    gathered = pl.pallas_call(
        functools.partial(main_kernel, lay),
        out_shape=out_shape,
        in_specs=[spec] * len(inputs),
        out_specs=[spec] * len(out_shape),
        scratch_shapes=scratch,
        compiler_params=pltpu.CompilerParams(
            collective_id=0, has_side_effects=True, vmem_limit_bytes=26 * 2**20 + varying
        ),
        name="step",
    )(*[pltpu.with_memory_space_constraint(value, pltpu.HBM) for value in inputs])
    params = (
        sac_hidden, sac_hidden_mom, dyn_hidden, dyn_hidden_mom,
        flip(crit_in), flip(crit_in_m), flip(crit_in_v), act_in, act_in_m, act_in_v,
        dyn_in, dyn_in_m, dyn_in_v, crit_out, crit_out_m, crit_out_v,
        swap(act_out), swap(act_out_m), swap(act_out_v),
        swap(dyn_out), swap(dyn_out_m), swap(dyn_out_v), biases, biases_m, biases_v,
    )
    new_shape = [shape(value.shape, F32) for value in params]
    new_shape += [shape((1, 1), F32)] * 2
    out = pl.pallas_call(
        update_kernel,
        out_shape=tuple(new_shape),
        in_specs=[spec] * (len(gathered) + len(params)),
        out_specs=[spec] * len(new_shape),
        scratch_shapes=[vm(1, NB)],
        compiler_params=pltpu.CompilerParams(vmem_limit_bytes=16 * 2**20),
        name="update",
    )(*[kept(value) for value in gathered], *params)
    out = list(out)
    for at in (4, 5, 6):
        out[at] = flip(out[at])
    for at in (16, 17, 18, 19, 20, 21):
        out[at] = swap(out[at])
    for at in (25, 26):
        out[at] = out[at].reshape(())
    return tuple(out)


def solution(mesh):
    both = ("dp", "blk")
    sharded = (
        P(None, both), P(None, both), P(both, None), P(both, None), P(both), P(None, both, None),
    )
    hidden = (P(None, "blk", None),) * 4

    def step(replay, model_rows, *others):
        lay = Layout(mesh, replay.shape[1], model_rows.shape[1])
        return shards(lay, replay, model_rows, *others)

    return jax.shard_map(
        step,
        mesh=mesh,
        in_specs=sharded + hidden + (P(),) * 25,
        out_specs=hidden + (P(),) * 23,
        check_vma=False,
    )
```

```python
import functools

import jax
import jax.numpy as jnp
from jax import lax
from jax.experimental import pallas as pl
from jax.experimental.pallas import tpu as pltpu
from jax.sharding import PartitionSpec as P

OBS = 17
ACT = 6
IN = OBS + ACT
FEAT = 42
HDYN = 200
HSAC = 256
MEMBERS = 7
DOUT = 36
HALF = DOUT // 2
NB = 4639
NS_ITERS = 5
STEP = 10
CAP = 8
TILE = 640
DYN_TILE = 512
ROWS = 32

DISCOUNT = 0.99
TARGET_ENTROPY = -6.0
BOUND_WEIGHT = 0.01
MOMENTUM = 0.95
MUON_RATE = 0.4
MUON_DECAY = 0.01
ADAM_RATE = 0.1
ADAM_DECAY = 0.01
BETA_FIRST = 0.9
BETA_SECOND = 0.999
COEF_LINEAR = 3.4445
COEF_CUBIC = -4.775
COEF_QUINTIC = 2.0315

CB1, CB2, CB3, AB1, AB2, AB3 = 0, 512, 1024, 1026, 1282, 1538
DB1, DB2, DB3, MAXLV, MINLV, LOGA = 1550, 2950, 4350, 4602, 4620, 4638

R_IN, R_HEAD, R_OUT, R_MISC, R_SMALL = 0, 72, 88, 96, 128
D_IN, D_OUT, D_B2, D_B3, D_UP, D_LOW, D_LOSS, D_HID, D_ROWS = 0, 24, 60, 61, 62, 63, 64, 72, 128

F32, BF16 = jnp.float32, jnp.bfloat16
MESH = pl.DeviceIdType.MESH
NN = (((1,), (0,)), ((), ()))
NT = (((1,), (1,)), ((), ()))


def dot(a, b, dims=NN):
    return lax.dot_general(a, b, dims, preferred_element_type=F32)


def rounded(v):
    return v.astype(BF16).astype(F32)


def pieces(v):
    high = v.astype(BF16)
    rest = v - high.astype(F32)
    middle = rest.astype(BF16)
    return high, middle, (rest - middle.astype(F32)).astype(BF16)


def split(v):
    high = v.astype(BF16)
    return high, (v - high.astype(F32)).astype(BF16)


def product(a, b, dims=NN):
    left = jnp.concatenate([a[0], a[0], a[1]], 1)
    right = jnp.concatenate([b[0], b[1], b[0]], dims[0][1][0])
    half = left.shape[0] // 2
    return jnp.concatenate([dot(left[:half], right, dims), dot(left[half:], right, dims)], 0)


def softplus(v):
    return jnp.maximum(v, 0.0) + jnp.log1p(jnp.exp(-jnp.abs(v)))


def sigmoid(v):
    return 0.5 + 0.5 * jnp.tanh(0.5 * v)


def gate(half):
    up = 1.0 + jnp.tanh(half)
    value = half * up
    return value, up + value * (2.0 - up)


def by_rows(body, *arrays):
    done = [
        body(*[array[at : at + ROWS] for array in arrays]) for at in range(0, arrays[0].shape[0], ROWS)
    ]
    return [jnp.concatenate(parts, 0) for parts in zip(*done)]


def spread_to(column, width):
    return jnp.concatenate([column] * (width // 128), 1)


def gated(half, column=None):
    def body(part, *offset):
        value, slope = gate(part + spread_to(offset[0], part.shape[1]) if offset else part)
        return value.astype(BF16), slope

    return by_rows(body, half, *([] if column is None else [column]))


def sloped(grad, slope):
    return by_rows(lambda part, by: ((part * by).astype(BF16),), grad, slope)[0]


def outer_sloped(column, row, slope):
    return by_rows(lambda part, by: (((spread_to(part, by.shape[1]) * row) * by).astype(BF16),), column, slope)[0]


def rows_of(shape):
    return lax.broadcasted_iota(jnp.int32, shape, 0)


def schulz(refs, steps, before=None):
    @pl.loop(0, steps)
    def _(step):
        if before is not None:
            before(step)
        matrices = [ref[...] for ref in refs]
        parts = [split(matrix) for matrix in matrices]
        grams = [product(part, part, NT) for part in parts]
        halves = [split(gram) for gram in grams]
        squares = [product(half, half) for half in halves]
        blends = [
            split(COEF_CUBIC * gram + COEF_QUINTIC * square) for gram, square in zip(grams, squares)
        ]
        moved = [product(blend, part) for blend, part in zip(blends, parts)]
        for ref, matrix, move in zip(refs, matrices, moved):
            ref[...] = COEF_LINEAR * matrix + move


def normalise(ref):
    moment = ref[...]
    norm = jnp.sqrt(jnp.sum(jnp.sum(moment * moment, axis=1, keepdims=True), axis=0, keepdims=True))
    ref[...] = moment / (norm + 1e-7)


class Layout:
    def __init__(self, mesh, replay, model):
        self.n_dp = mesh.shape["dp"]
        self.n_blk = mesh.shape["blk"]
        self.n_dev = self.n_dp * self.n_blk
        self.replay = replay
        self.model = model
        self.real = self.n_dp * CAP
        self.batch = self.real + model
        self.width = -(-(self.real + 2) // 128) * 128
        self.rows = HSAC // self.n_blk
        self.drows = HDYN // self.n_blk
        self.mat = 64 // self.n_dp
        self.sml = 32 // self.n_dp
        self.chunks = (2 * self.mat, self.mat + self.sml)
        self.owner = self.n_dp - 1

        groups = [("plane sum", g) for g in range(2)] + [("line sum", g) for g in range(3)]
        common = ["hidden", "hidden on", "lists", "own", "line", "plane", "dyn h", "dyn m", "sac m", "small"]
        common += groups
        kinds = [(name, kind) for name in ("pack", "x") for kind in ("own", "on")]
        sent = common + [("tiles", k) for k in range(3)] + kinds
        self.sent = {name: at for at, name in enumerate(sent)}
        self.departures = len(sent)
        for k in range(3):
            for name in ("sac g", "sac x"):
                self.sent[name, k] = self.departures
                self.departures += self.n_dp
        self.here, self.arrivals = {}, 0
        tiles = [("tiles", k) for k in range(3)]
        for name in common + tiles + [("pack", "sibling"), ("x", "sibling")]:
            self.here[name] = self.arrivals
            self.arrivals += 1
        for name, number in (("sac g", 3), ("sac x", 3), (("pack", "like"), MEMBERS), (("x", "like"), MEMBERS)):
            self.here[name] = self.arrivals
            self.arrivals += number


def main_kernel(lay, *refs):
    (
        replay, model, requests, member, live, noise, sac_h, sac_m, dyn_h, dyn_m, crit_in, act_in,
        dyn_in, crit_out, act_out, dyn_out, biases, targ_in, targ_hidden, targ_out, targ_bias,
        sac_g, sac_x, dyn_x, dyn_s, small, count,
        wg, lists, asked, dhg, dmg, smg, bk, xs, nz, w1f, w1t, w1n, w2t, w2h, heads, head_t, head_f,
        rowbuf, wide, headcol, acc_h, acc_w, acc_c, acc_a, acc_m, acc_l, grid_c, grid_a, from_c, from_a,
        zr_c, zr_a, zf_c, zf_a, sum_c, sum_a, mg, mat, grow, dcols, dacc_h, dacc_w, dacc_o, dacc_m, dacc_b, dacc_l, xt, dmat,
        dpack, drow_x, bias, dhead, dhead_t, *rest,
    ) = refs
    send, recv = rest
    sent, here_at = lay.sent, lay.here
    grids, froms, zrs, zfs = (grid_c, grid_a), (from_c, from_a), (zr_c, zr_a), (zf_c, zf_a)
    n_dp, n_blk = lay.n_dp, lay.n_blk
    me = lax.axis_index("dp")
    z = lax.axis_index("blk")
    core = lax.rem(me, 2)
    sibling = me + 1 - 2 * core
    is_dyn = me < MEMBERS
    dyn_e = jnp.minimum(me, MEMBERS - 1)
    is_owner = me == lay.owner

    def on_plane(src, dst, ssem, rsem, peer):
        return pltpu.make_async_remote_copy(
            src_ref=src, dst_ref=dst, send_sem=ssem, recv_sem=rsem,
            device_id={"dp": peer}, device_id_type=MESH,
        )

    def on_line(src, dst, ssem, rsem, peer):
        return pltpu.make_async_remote_copy(
            src_ref=src, dst_ref=dst, send_sem=ssem, recv_sem=rsem,
            device_id={"blk": peer}, device_id_type=MESH,
        )

    def over(number, body):
        if number <= 8:
            for off in range(1, number):
                body(off)
        else:
            pl.loop(1, number)(body)

    def plane_peers(body):
        over(n_dp, lambda off: body(lax.rem(me + off, n_dp)))

    def like_peers(body):
        over(n_dp // 2, lambda off: body(lax.rem(me + 2 * off, n_dp)))

    def line_peers(body):
        over(n_blk, lambda off: body(lax.rem(z + off, n_blk)))

    def has_sent(view, name):
        at = send.at[sent[name]]
        on_plane(view, view, at, at, sibling).wait_send()

    def has_come(view, name):
        at = recv.at[here_at[name]]
        on_plane(view, view, at, at, sibling).wait_recv()

    barrier = pltpu.get_barrier_semaphore()
    plane_peers(lambda peer: pl.semaphore_signal(barrier, inc=1, device_id={"dp": peer}, device_id_type=MESH))
    line_peers(lambda peer: pl.semaphore_signal(barrier, inc=1, device_id={"blk": peer}, device_id_type=MESH))
    wg[0] = sac_h[...].astype(BF16)
    lists[0] = requests[...]
    lists[1] = member[...]
    pl.semaphore_wait(barrier, n_dp - 1 + n_blk - 1)

    half_rows = pl.ds(pl.multiple_of(core * (lay.rows // 2), lay.rows // 2), lay.rows // 2)

    def slot_from(owner, at):
        return lax.rem(owner - at + n_blk, n_blk)

    def hidden_copy(peer):
        src = wg.at[0, :, half_rows]
        dst = wg.at[slot_from(z, peer), :, half_rows]
        return on_line(src, dst, send.at[sent["hidden"]], recv.at[here_at["hidden"]], peer)

    def hidden_on():
        view = wg.at[pl.ds(1, n_blk - 1), :, half_rows]
        return on_plane(view, view, send.at[sent["hidden on"]], recv.at[here_at["hidden on"]], sibling)

    def list_copy(peer):
        return on_plane(lists, asked.at[me], send.at[sent["lists"]], recv.at[here_at["lists"]], peer)

    line_peers(lambda peer: hidden_copy(peer).start())
    plane_peers(lambda peer: list_copy(peer).start())
    asked[me] = lists[...]

    def dyn_h_copy(peer):
        return on_line(dyn_h.at[dyn_e], dhg.at[z], send.at[sent["dyn h"]], recv.at[here_at["dyn h"]], peer)

    def dyn_m_copy(peer):
        return on_line(dyn_m.at[dyn_e], dmg.at[z], send.at[sent["dyn m"]], recv.at[here_at["dyn m"]], peer)

    def sac_m_copy(peer):
        return on_line(sac_m, smg.at[z], send.at[sent["sac m"]], recv.at[here_at["sac m"]], peer)

    alive = live[...].astype(F32).reshape(1, lay.model)
    bias[...] = biases[...].reshape(1, NB)
    xs[42:56, :] = jnp.zeros((14, lay.batch), F32)
    xs[0:FEAT, lay.real : lay.batch] = model[...]
    xs[42:43, lay.real : lay.batch] = alive
    nz[...] = jnp.zeros_like(nz)
    for which in range(2):
        nz[which, 1:7, :] = noise[:, which, :]
    firsts = [
        (targ_in[:, 0, :], targ_bias[0:1, 0:HSAC]),
        (targ_in[:, 1, :], targ_bias[1:2, 0:HSAC]),
        (crit_in[:, 0, :], bias[:, CB1 : CB1 + HSAC]),
        (crit_in[:, 1, :], bias[:, CB1 + HSAC : CB1 + 2 * HSAC]),
        (act_in[...], bias[:, AB1 : AB1 + HSAC]),
    ]
    w1f[...] = jnp.zeros_like(w1f)
    for net, (weights, offset) in enumerate(firsts):
        w1f[net, 0 : weights.shape[0], :] = rounded(weights)
        for at, piece in enumerate(pieces(offset)):
            w1f[net, IN + at : IN + at + 1, :] = piece.astype(F32)
        w1t[net] = (0.5 * w1f[net].T).astype(BF16)
    for k in range(2):
        w1n[k] = w1f[2 + k, 16:32, :].astype(BF16)
    for net in range(2):
        w2t[net] = (0.5 * rounded(targ_hidden[net])).T.astype(BF16)
    has_come(wg.at[pl.ds(0, n_blk - 1), :, half_rows], "hidden")
    hidden_on().start()

    rowbuf[...] = jnp.zeros_like(rowbuf)
    rowbuf[0:1, :] = targ_bias[0:1, HSAC : 2 * HSAC]
    rowbuf[1:2, :] = targ_bias[1:2, HSAC : 2 * HSAC]
    rowbuf[2:3, :] = bias[:, CB2 : CB2 + HSAC]
    rowbuf[3:4, :] = bias[:, CB2 + HSAC : CB2 + 2 * HSAC]
    rowbuf[4:5, :] = bias[:, AB2 : AB2 + HSAC]
    rowbuf[5:7, :] = rounded(crit_out[...])
    columns = 0.5 * rowbuf[...].T
    for at in range(7):
        wide[at] = jnp.broadcast_to(columns[:, at : at + 1], (HSAC, 128))
    rowbuf[...] = jnp.zeros_like(rowbuf)
    rowbuf[0:1, 1:7] = bias[:, AB3 : AB3 + ACT]
    rowbuf[0:1, 9:15] = bias[:, AB3 + ACT : AB3 + 2 * ACT]
    headcol[...] = rowbuf[:, 0:128].T
    head_f[...] = jnp.zeros_like(head_f)
    for k in range(2):
        head_f[0:1, :] = targ_out[k : k + 1, :]
        heads[k] = head_f[...].astype(BF16)
        head_f[0:1, :] = crit_out[k : k + 1, :]
        heads[2 + k] = head_f[...].astype(BF16)
    head_f[0:1, :] = jnp.zeros((1, HSAC), F32)
    head_f[1:7, :] = act_out[0:ACT, :]
    head_f[9:15, :] = act_out[ACT : 2 * ACT, :]
    heads[4] = head_f[...].astype(BF16)
    head_t[...] = (0.5 * rounded(head_f[...])).T.astype(BF16)
    for ref in (acc_h, acc_w, acc_c, acc_a, acc_m, acc_l):
        ref[...] = jnp.zeros_like(ref)

    data = replay[...]
    sums = jnp.sum(data[0:24], axis=1, keepdims=True)
    squares = jnp.sum(data[0:24] * data[0:24], axis=1, keepdims=True)
    living = jnp.sum(alive, axis=1, keepdims=True)

    has_come(asked.at[pl.ds(0, n_dp - 1)], "lists")
    spread = (
        lax.rem(lax.broadcasted_iota(jnp.int32, (CAP, lay.real), 1), CAP)
        == lax.broadcasted_iota(jnp.int32, (CAP, lay.real), 0)
    ).astype(F32)
    here = (
        lax.broadcasted_iota(jnp.int32, (n_dp, lay.real), 1) // CAP
        == lax.broadcasted_iota(jnp.int32, (n_dp, lay.real), 0)
    )

    def in_lanes(which):
        values = asked[:, which, me, :].astype(F32)
        wide = lax.dot_general(
            values, spread, NN, precision=lax.Precision.HIGHEST, preferred_element_type=F32
        )
        return jnp.sum(jnp.where(here, wide, 0.0), axis=0, keepdims=True)

    slots = in_lanes(0)
    wanted = jnp.maximum(slots, 0.0).astype(jnp.int32)
    hot = (rows_of((lay.replay, lay.real)) == wanted).astype(BF16)
    high, middle, low = pieces(data)
    picked = dot(high, hot) + dot(middle, hot) + dot(low, hot)
    mine = me * n_blk
    bk[mine, 0:FEAT, 0 : lay.real] = picked
    bk[mine, 42:43, 0 : lay.real] = (slots >= 0.0).astype(F32)
    bk[mine, 43:44, 0 : lay.real] = in_lanes(1)
    bk[mine, 44:48, 0 : lay.real] = jnp.zeros((4, lay.real), F32)
    bk[mine, :, lay.real : lay.width] = jnp.zeros((48, lay.width - lay.real), F32)
    bk[mine, 0:24, lay.real : lay.real + 1] = sums
    bk[mine, 0:24, lay.real + 1 : lay.real + 2] = squares
    bk[mine, 24:25, lay.real : lay.real + 1] = living

    def slot_of(block):
        line = lax.rem(block, n_blk)
        return block - line + slot_from(line, z)

    def block_line(peer):
        dst = bk.at[me * n_blk + slot_from(z, peer)]
        return on_line(bk.at[mine], dst, send.at[sent["line"]], recv.at[here_at["line"]], peer)

    def block_own(peer):
        view = bk.at[mine]
        return on_plane(view, view, send.at[sent["own"]], recv.at[here_at["own"]], peer)

    def block_plane(peer):
        view = bk.at[pl.ds(mine + 1, n_blk - 1)]
        return on_plane(view, view, send.at[sent["plane"]], recv.at[here_at["plane"]], peer)

    plane_peers(lambda peer: block_own(peer).start())
    line_peers(lambda peer: block_line(peer).start())

    @pl.when(is_dyn)
    def _():
        line_peers(lambda peer: dyn_h_copy(peer).start())
        line_peers(lambda peer: dyn_m_copy(peer).start())

    @pl.when(is_owner)
    def _():
        line_peers(lambda peer: sac_m_copy(peer).start())

    has_come(wg.at[pl.ds(0, n_blk - 1), :, half_rows], "hidden on")
    for k in range(3):
        for block in range(n_blk):
            w2h[k, block * lay.rows : (block + 1) * lay.rows, :] = (
                0.5 * wg[slot_from(block, z), k].astype(F32)
            ).astype(BF16)
        w2t[2 + k] = w2h[k].astype(F32).T.astype(BF16)

    log_alpha = bias[:, LOGA : LOGA + 1]
    alpha = jnp.exp(log_alpha)
    last = [
        targ_bias[0:1, 2 * HSAC : 2 * HSAC + 1],
        targ_bias[1:2, 2 * HSAC : 2 * HSAC + 1],
        bias[:, CB3 : CB3 + 1],
        bias[:, CB3 + 1 : CB3 + 2],
    ]
    n_tiles = lay.batch // TILE
    row8 = rows_of((8, TILE))
    act_rows = jnp.logical_and(row8 >= 1, row8 < 1 + ACT)

    def place_of(step):
        return pl.ds(pl.multiple_of(lax.rem(step + 1, n_tiles) * TILE, TILE), TILE)

    def ones16(width=TILE):
        return jnp.ones((16, width), BF16)

    def framed(first_row, used, where):
        row32 = rows_of((32, TILE))
        ones3 = jnp.logical_and(row32 >= IN, row32 < IN + 3).astype(F32)
        return jnp.where(row32 < used, xs[first_row : first_row + 32, where], ones3)

    def hidden(inputs, net):
        first, slope1 = gated(dot(w1t[net], inputs))
        second, slope2 = gated(dot(w2t[net], first), wide[net])
        return first, slope1, second, slope2

    def policy(inputs, which, where):
        first, slope1, second, slope2 = hidden(inputs, 4)
        out = dot(heads[4], second) + headcol[0:16, 0:1]
        bent = jnp.tanh(out[8:16])
        log_scale = -5.0 + 3.5 * (bent + 1.0)
        draw = nz[which, :, where]
        moved = jnp.exp(log_scale) * draw
        latent = out[0:8] + moved
        terms = (
            -0.5 * draw * draw
            - log_scale
            - 0.9189385
            - 2.0 * (0.6931472 - latent - softplus(-2.0 * latent))
        )
        log_prob = jnp.sum(jnp.where(act_rows, terms, 0.0), axis=0, keepdims=True)
        action = jnp.where(act_rows, jnp.tanh(latent), 0.0)
        return action, log_prob, bent, moved, (first, slope1, second, slope2)

    def with_action(inputs, action):
        middle_rows = jnp.where(act_rows, action, inputs[16:24])
        return jnp.concatenate([inputs[0:16], middle_rows, inputs[24:32]], 0).astype(BF16)

    def critic(inputs, net):
        kept = hidden(inputs, net)
        value = dot(heads[net], kept[2])[0:1] + last[net]
        return value, kept

    def add_hidden(k, first, grad):
        acc_h[k] += dot(jnp.concatenate([first, ones16()], 0), grad, NT)

    @pl.loop(0, n_tiles)
    def _(step):
        @pl.when(step == 1)
        def _():
            has_come(bk.at[pl.ds(0, n_blk - 1)], "line")
            plane_peers(lambda peer: block_plane(peer).start())

        @pl.when(step == n_tiles - 1)
        def _():
            has_come(bk.at[pl.ds(0, n_dp - 1)], "own")
            lanes = lax.broadcasted_iota(jnp.int32, (48, lay.width), 1) // CAP

            def gather(owner, total):
                turned = pltpu.roll(
                    bk[owner * n_blk], lax.rem((owner - me) * CAP + lay.width, lay.width), axis=1
                )
                return jnp.where(lanes == owner, turned, total)

            own = lax.fori_loop(0, n_dp, gather, jnp.zeros((48, lay.width), F32))
            xs[0:48, 0 : lay.real] = own[:, 0 : lay.real]

        where = place_of(step)
        now_in = framed(0, IN, where).astype(BF16)
        next_f = framed(24, OBS, where)
        reward = xs[23:24, where]
        done = xs[41:42, where]
        weight = xs[42:43, where]
        row16 = rows_of((16, TILE))
        next_action, next_prob, _, _, _ = policy(next_f.astype(BF16), 1, where)
        aim_in = with_action(next_f, next_action)
        aim = jnp.minimum(critic(aim_in, 0)[0], critic(aim_in, 1)[0])
        target = reward + DISCOUNT * (1.0 - done) * (aim - alpha * next_prob)
        loss = jnp.zeros((1, TILE), F32)
        heads_grad = []
        for k in range(2):
            value, (c1, dc1, c2, dc2) = critic(now_in, 2 + k)
            miss = value - target
            loss += 0.5 * miss * miss
            g3 = rounded(weight * miss)
            g3_rows = jnp.where(row16 == 0, g3, 0.0).astype(BF16)
            heads_grad.append(g3_rows)
            acc_c[k] += dot(g3_rows, c2, NT)
            g2 = outer_sloped(wide[5 + k], g3, dc2)
            add_hidden(k, c1, g2)
            g1 = sloped(dot(w2h[k], g2), dc1)
            acc_w[k] += dot(now_in, g1, NT)
        acc_m[:, 16:48] += dot(ones16(), jnp.concatenate(heads_grad, 0), NT)
        acc_l[0:1, :] += weight * loss

    def put_matrix(group, k, at):
        for chunk in range(n_dp):
            tile = chunk * lay.mat
            side, row = tile // 32, tile % 32
            grids[group][chunk, at * lay.mat : (at + 1) * lay.mat] = acc_h[
                k, row * 8 : (row + lay.mat) * 8, side * 128 : (side + 1) * 128
            ].reshape(lay.mat, 8, 128)

    def put(row, value):
        for at in range(value.shape[0] // 8):
            for side in range(value.shape[1] // 128):
                tile = side * (R_SMALL // 8) + row // 8 + at
                grid_a[tile // lay.sml, lay.mat + tile % lay.sml] = value[
                    at * 8 : at * 8 + 8, side * 128 : (side + 1) * 128
                ]

    def plane_sum(group, peer):
        name = ("plane sum", group)
        return on_plane(
            grids[group].at[peer], froms[group].at[me], send.at[sent[name]], recv.at[here_at[name]], peer
        )

    def line_part(part):
        group = min(part, 1)
        tiles = (pl.ds(0, 2 * lay.mat), pl.ds(0, lay.mat), pl.ds(lay.mat, lay.sml))[part]
        return group, tiles

    def line_sum(part, peer):
        group, tiles = line_part(part)
        name = ("line sum", part)
        src, dst = zfs[group].at[tiles], zrs[group].at[z, tiles]
        return on_line(src, dst, send.at[sent[name]], recv.at[here_at[name]], peer)

    def line_bytes(part):
        group, tiles = line_part(part)
        return zrs[group].at[pl.ds(0, n_blk - 1), tiles]

    def fold_plane(group):
        has_come(froms[group].at[pl.ds(0, n_dp - 1)], ("plane sum", group))
        froms[group][me] = grids[group][me]
        whole = froms[group][0]
        for at in range(1, n_dp):
            whole = whole + froms[group][at]
        zfs[group][...] = whole
        for part in (0,) if group == 0 else (1, 2):
            line_peers(lambda peer: line_sum(part, peer).start())

    def tile_copy(k):
        src = (sum_c, sum_a)[k // 2].at[pl.ds((k % 2) * lay.mat, lay.mat)]
        return on_plane(src, mg.at[k, me], send.at[sent["tiles", k]], recv.at[here_at["tiles", k]], lay.owner)

    def small_copy(peer):
        return on_plane(
            sum_a.at[pl.ds(lay.mat, lay.sml)], small.at[pl.ds(me * lay.sml, lay.sml)],
            send.at[sent["small"]], recv.at[here_at["small"]], peer,
        )

    def fold_end(part):
        group, tiles = line_part(part)
        has_come(line_bytes(part), ("line sum", part))
        zrs[group][z, tiles] = zfs[group][tiles]
        whole = zrs[group][0, tiles]
        for block in range(1, n_blk):
            whole = whole + zrs[group][block, tiles]
        (sum_c, sum_a)[group][tiles] = whole
        for k in ((0, 1), (2,), ())[part]:
            pl.when(jnp.logical_not(is_owner))(tile_copy(k).start)

            @pl.when(is_owner)
            def _():
                mg[k, me] = (sum_c, sum_a)[group][(k % 2) * lay.mat : (k % 2 + 1) * lay.mat]

        if part == 2:
            plane_peers(lambda peer: small_copy(peer).start())
            small[pl.ds(me * lay.sml, lay.sml)] = sum_a[lay.mat :]

    def chain(group):
        def end():
            for part in (0,) if group == 0 else (1, 2):
                fold_end(part)

        return [
            lambda: plane_peers(lambda peer: plane_sum(group, peer).start()),
            lambda: fold_plane(group),
            end,
        ]

    critic_chain, actor_chain = chain(0), chain(1)
    per = DYN_TILE // lay.real
    dyn_tiles = lay.n_dev // per
    in_actor, in_dyn = {}, {}
    if n_tiles > 1:
        in_actor[1] = [critic_chain[1]]
        in_dyn[0] = [critic_chain[2]]
    else:
        in_dyn[0] = [critic_chain[1]]
        in_dyn[min(1, dyn_tiles - 1)] = [critic_chain[2]]
    in_dyn.setdefault(dyn_tiles - 1, []).append(actor_chain[1])

    def take(slots, step):
        for at, events in slots.items():
            @pl.when(step == at)
            def _():
                for event in events:
                    event()

    for k in range(2):
        put_matrix(0, k, k)
    critic_chain[0]()

    @pl.loop(0, n_tiles)
    def _(step):
        take(in_actor, step)
        where = place_of(step)
        now_f = framed(0, IN, where)
        now_in = now_f.astype(BF16)
        weight = xs[42:43, where]
        action, log_prob, bent, moved, (a1, da1, a2, da2) = policy(now_in, 0, where)
        judged_in = with_action(now_f, action)
        loss = alpha * log_prob - log_alpha * (log_prob + TARGET_ENTROPY)
        grad_action = jnp.zeros((8, TILE), F32)
        for k in range(2):
            judged, (_, df1, _, df2) = critic(judged_in, 2 + k)
            loss -= 0.5 * judged
            g2 = outer_sloped(wide[5 + k], -0.5 * weight, df2)
            g1 = sloped(dot(w2h[k], g2), df1)
            grad_action += dot(w1n[k], g1)[0:8]
        grad_latent = 2.0 * alpha * weight * action + grad_action * (1.0 - action * action)
        grad_scale = grad_latent * moved - alpha * weight
        grad_bent = grad_scale * 3.5 * (1.0 - bent * bent)
        g3 = jnp.concatenate(
            [jnp.where(act_rows, grad_latent, 0.0), jnp.where(act_rows, grad_bent, 0.0)], 0
        ).astype(BF16)
        acc_a[...] += dot(g3, a2, NT)
        acc_m[:, 0:16] += dot(ones16(), g3, NT)
        g2 = sloped(dot(head_t[...], g3), da2)
        add_hidden(2, a1, g2)
        g1 = sloped(dot(w2h[2], g2), da1)
        acc_w[2] += dot(now_in, g1, NT)
        acc_l[0:1, :] += weight * loss
        acc_l[1:2, :] += weight * (log_prob + TARGET_ENTROPY)

    put_matrix(1, 2, 0)
    for k in range(3):
        put(R_IN + 24 * k, acc_w[k, 0:24, :])
    put(R_HEAD, acc_a[...])
    rowbuf[0:1, :] = acc_c[0, 0:1, :]
    rowbuf[1:2, :] = acc_c[1, 0:1, :]
    for k in range(3):
        rowbuf[2 + k : 3 + k, :] = acc_h[k, HSAC : HSAC + 1, :]
    put(R_OUT, rowbuf[...])
    folded = jnp.sum(acc_l[...], axis=1, keepdims=True)
    rowbuf[...] = jnp.zeros_like(rowbuf)
    rowbuf[0:1, 0:48] = acc_m[0:1, :]
    rowbuf[0:1, 64:65] = folded[0:1]
    rowbuf[0:1, 65:66] = folded[1:2]
    put(R_MISC, rowbuf[...])
    put(R_MISC + 8, jnp.zeros((R_SMALL - R_MISC - 8, HSAC), F32))
    actor_chain[0]()

    has_come(bk.at[pl.ds(0, (n_dp - 1) * (n_blk - 1))], "plane")
    lane0 = lay.real // 128 * 128

    def add_block(at, carry):
        sides, fills = carry
        slot = slot_of(at)
        return sides + bk[slot, 0:32, lane0 : lane0 + 128], fills + bk[slot, 40:48, 0 : lay.real]

    sides, fills = lax.fori_loop(
        0, lay.n_dev, add_block, (jnp.zeros((32, 128), F32), jnp.zeros((8, lay.real), F32))
    )
    at = lay.real - lane0
    rows_all = float(lay.replay * lay.n_dev)
    centre = sides[0:24, at : at + 1] / rows_all
    scale = lax.rsqrt(sides[0:24, at + 1 : at + 2] / rows_all - centre * centre + 1e-6)
    total = sides[24:25, at : at + 1] + jnp.sum(fills[2:3, :], axis=1, keepdims=True)
    count[...] = jnp.broadcast_to(total, (8, 128))

    def dyn_bias(start, width):
        row = jnp.zeros((1, width), F32)
        for e in range(MEMBERS):
            row = jnp.where(me == e, bias[:, start + width * e : start + width * (e + 1)], row)
        return row

    @pl.when(is_dyn)
    def _():
        w1f[0] = jnp.zeros((32, HSAC), F32)
        w1f[0, 0:IN, 0:HDYN] = rounded(dyn_in[dyn_e])
        for at, piece in enumerate(pieces(dyn_bias(DB1, HDYN))):
            w1f[0, IN + at : IN + at + 1, 0:HDYN] = piece.astype(F32)
        w1t[0] = (0.5 * w1f[0].T).astype(BF16)
        rowbuf[...] = jnp.zeros_like(rowbuf)
        rowbuf[0:1, 0:HDYN] = dyn_bias(DB2, HDYN)
        head_row = dyn_bias(DB3, DOUT)
        rowbuf[1:2, 0:HALF] = head_row[:, 0:HALF]
        rowbuf[1:2, 24 : 24 + HALF] = head_row[:, HALF:DOUT]
        rowbuf[2:3, 0:HALF] = bias[:, MAXLV : MAXLV + HALF]
        rowbuf[3:4, 0:HALF] = bias[:, MINLV : MINLV + HALF]
        dcols[...] = rowbuf[...].T
        wide[0] = jnp.broadcast_to(0.5 * dcols[:, 0:1], (HSAC, 128))
        dpack[...] = jnp.zeros_like(dpack)
        dpack[0:HALF, 0:HDYN] = dyn_out[dyn_e, 0:HALF, :]
        dpack[24 : 24 + HALF, 0:HDYN] = dyn_out[dyn_e, HALF:DOUT, :]
        dhead[...] = dpack[0:48, :].astype(BF16)
        dhead_t[...] = (0.5 * rounded(dpack[0:48, :])).T.astype(BF16)
        dpack[...] = jnp.zeros_like(dpack)

        has_come(dhg.at[pl.ds(0, n_blk - 1)], "dyn h")
        has_come(dmg.at[pl.ds(0, n_blk - 1)], "dyn m")
        dhg[z] = dyn_h[dyn_e]
        dmg[z] = dyn_m[dyn_e]
        dmat[...] = jnp.zeros_like(dmat)
        for block in range(n_blk):
            dmat[block * lay.drows : (block + 1) * lay.drows, 0:HDYN] = 0.5 * rounded(dhg[block])
        w2h[0] = dmat[...].astype(BF16)
        w2t[0] = dmat[...].T.astype(BF16)
        for ref in (dacc_h, dacc_w, dacc_o, dacc_m, dacc_b, dacc_l):
            ref[...] = jnp.zeros_like(ref)

    @pl.loop(0, dyn_tiles)
    def _(tile):
        take(in_dyn, tile)

        @pl.when(is_dyn)
        def _():
            for at in range(per):
                slot = slot_of(tile * per + at)
                xt[:, at * lay.real : (at + 1) * lay.real] = bk[slot, :, 0 : lay.real]
            now = xt[0:24, :]
            later = xt[24:48, :]
            row24 = rows_of((24, DYN_TILE))
            scaled = jnp.where(row24 < IN, (now - centre) * scale, 1.0)
            inputs = jnp.concatenate([scaled, (rows_of((8, DYN_TILE)) < 2).astype(F32)], 0).astype(BF16)
            first, slope1 = gated(dot(w1t[0], inputs))
            second, slope2 = gated(dot(w2t[0], first), wide[0])
            out = dot(dhead[...], second) + dcols[0:48, 1:2]
            used = row24 < HALF
            upper = dcols[0:24, 2:3]
            lower = dcols[0:24, 3:4]
            gap1 = upper - out[24:48]
            gap2 = upper - softplus(gap1) - lower
            log_var = lower + softplus(gap2)
            error = out[0:24] - jnp.where(row24 == OBS, now[23:24], later - now)
            inverse = jnp.exp(-log_var)
            weight = xt[42:43, :] * (xt[43:44, :] == me.astype(F32)).astype(F32)
            spread_term = error * error * inverse
            nll = jnp.sum(jnp.where(used, spread_term + log_var, 0.0), axis=0, keepdims=True)
            dacc_l[0:1, :] += weight * nll
            grad_mu = 2.0 * weight * error * inverse
            grad_lv = weight * (1.0 - spread_term)
            open1 = sigmoid(gap1)
            open2 = sigmoid(gap2)
            grad_lv1 = grad_lv * open2
            dacc_b[0] += jnp.where(used, grad_lv1 * (1.0 - open1), 0.0)
            dacc_b[1] += jnp.where(used, grad_lv * (1.0 - open2), 0.0)
            g3 = jnp.concatenate(
                [jnp.where(used, grad_mu, 0.0), jnp.where(used, grad_lv1 * open1, 0.0)], 0
            ).astype(BF16)
            dacc_o[...] += dot(g3, second, NT)
            dacc_m[...] += dot(ones16(DYN_TILE), g3, NT)
            g2 = sloped(dot(dhead_t[...], g3), slope2)
            dacc_h[...] += dot(jnp.concatenate([first, ones16(DYN_TILE)], 0), g2, NT)
            g1 = sloped(dot(w2h[0], g2), slope1)
            dacc_w[...] += dot(inputs, g1, NT)

    out_of = {"pack": dyn_s, "x": dyn_x}

    def member_copy(name, src, owner, kind, sem, peer):
        return on_plane(src, out_of[name].at[owner], send.at[sent[name, kind]], recv.at[sem], peer)

    def give(name, src):
        like_peers(
            lambda peer: member_copy(name, src, dyn_e, "own", here_at[name, "like"] + dyn_e, peer).start()
        )
        member_copy(name, src, dyn_e, "own", here_at[name, "sibling"], sibling).start()

    def hand_on(name):
        def body(peer):
            @pl.when(peer < MEMBERS)
            def _():
                owner = jnp.minimum(peer, MEMBERS - 1)
                view = out_of[name].at[owner]
                member_copy(name, view, owner, "on", here_at[name, "like"] + owner, sibling).wait_recv()
                member_copy(name, view, owner, "on", here_at[name, "sibling"], sibling).start()

        like_peers(body)

    even, odd = (MEMBERS + 1) // 2, MEMBERS // 2
    handed = even - core * (even - odd) - jnp.where(is_dyn, 1, 0)

    def from_sibling(name):
        for side, number in ((0, odd), (1, even)):
            @pl.when(core == side)
            def _():
                has_come(out_of[name].at[pl.ds(0, number)], (name, "sibling"))

    def gave(name):
        @pl.when(is_dyn)
        def _():
            for begin in range(0, n_dp // 2, MEMBERS):
                number = min(MEMBERS, n_dp // 2 - begin)
                has_sent(out_of[name].at[pl.ds(0, number)], (name, "own"))

        for number in (even, even - 1, even - 2):
            @pl.when(handed == number)
            def _():
                has_sent(out_of[name].at[pl.ds(0, number)], (name, "on"))

    def line_rows(ref):
        rows = ref[0 : lay.drows, 0:HDYN]
        for block in range(1, n_blk):
            rows = jnp.where(z == block, ref[block * lay.drows : (block + 1) * lay.drows, 0:HDYN], rows)
        return rows

    def sac_g_copy(k, peer):
        return on_plane(grow.at[k, mine_rows], sac_g.at[k], send.at[sent["sac g", k] + peer], recv.at[here_at["sac g"] + k], peer)

    def sac_x_copy(k, peer):
        return on_plane(mat.at[k, mine_rows], sac_x.at[k], send.at[sent["sac x", k] + peer], recv.at[here_at["sac x"] + k], peer)

    mine_rows = pl.ds(pl.multiple_of(z * lay.rows, lay.rows), lay.rows)

    def take_matrix(k):
        has_come(mg.at[k, pl.ds(0, n_dp - 1)], ("tiles", k))
        for chunk in range(n_dp):
            tile = chunk * lay.mat
            side, row = tile // 32, tile % 32
            at = slice(row * 8, (row + lay.mat) * 8)
            grow[k, at, side * 128 : (side + 1) * 128] = mg[k, chunk].reshape(lay.mat * 8, 128)
        sac_g[k] = grow[k, mine_rows, :]
        plane_peers(lambda peer: sac_g_copy(k, peer).start())
        for block in range(n_blk):
            at = slice(block * lay.rows, (block + 1) * lay.rows)
            mat[k, at, :] = MOMENTUM * smg[block, k] + grow[k, at, :] / total
        normalise(mat.at[k])

    @pl.when(is_dyn)
    def _():
        dpack[D_IN : D_IN + 24, :] = dacc_w[0:24, :]
        dpack[D_OUT : D_OUT + HALF, :] = dacc_o[0:HALF, :]
        dpack[D_OUT + HALF : D_OUT + DOUT, :] = dacc_o[24 : 24 + HALF, :]
        dpack[D_B2 : D_B2 + 1, :] = dacc_h[HSAC : HSAC + 1, :]
        dpack[D_B3 : D_B3 + 1, 0:48] = dacc_m[0:1, :]
        lanes = lax.broadcasted_iota(jnp.int32, (24, 128), 1)
        bound = jnp.where(
            lanes == 0,
            jnp.sum(dacc_b[0], axis=1, keepdims=True),
            jnp.where(lanes == 1, jnp.sum(dacc_b[1], axis=1, keepdims=True), 0.0),
        )
        dpack[D_UP : D_UP + 2, 0:24] = bound.T[0:2, :]
        dpack[D_LOSS : D_LOSS + 1, 0:128] = jnp.broadcast_to(
            jnp.sum(dacc_l[0:1, :], axis=1, keepdims=True), (1, 128)
        )
        dpack[D_HID : D_HID + lay.drows, 0:HDYN] = line_rows(dacc_h)
        dyn_s[dyn_e] = dpack[...]
        give("pack", dpack)
        dmat[...] = jnp.zeros_like(dmat)
        for block in range(n_blk):
            at = slice(block * lay.drows, (block + 1) * lay.drows)
            dmat[at, 0:HDYN] = MOMENTUM * dmg[block] + dacc_h[at, 0:HDYN] / total
        normalise(dmat)

    def send_sac(k):
        sac_x[k] = mat[k, mine_rows, :]
        plane_peers(lambda peer: sac_x_copy(k, peer).start())

    def sum_end(step):
        pl.when(step == NS_ITERS - 2)(actor_chain[2])

    @pl.when(is_dyn)
    def _():
        schulz([dmat], NS_ITERS, sum_end)
        rows = line_rows(dmat)
        drow_x[...] = rows
        dyn_x[dyn_e] = rows
        give("x", drow_x)

    @pl.when(is_owner)
    def _():
        has_come(smg.at[pl.ds(0, n_blk - 1)], "sac m")
        smg[z] = sac_m[...]
        for k in range(2):
            take_matrix(k)
        schulz([mat.at[0], mat.at[1]], NS_ITERS, sum_end)
        for k in range(2):
            send_sac(k)

    if n_dp > MEMBERS + 1:
        pl.when(jnp.logical_not(jnp.logical_or(is_dyn, is_owner)))(actor_chain[2])

    def sent_early():
        has_sent(wg.at[pl.ds(0, n_blk - 1), :, half_rows], "hidden")
        has_sent(wg.at[pl.ds(0, n_blk - 1), :, half_rows], "hidden on")
        has_sent(asked.at[pl.ds(0, n_dp - 1)], "lists")
        has_sent(bk.at[pl.ds(0, n_dp - 1)], "own")
        has_sent(bk.at[pl.ds(0, n_blk - 1)], "line")
        has_sent(bk.at[pl.ds(0, (n_dp - 1) * (n_blk - 1))], "plane")

        @pl.when(is_dyn)
        def _():
            has_sent(dhg.at[pl.ds(0, n_blk - 1)], "dyn h")
            has_sent(dmg.at[pl.ds(0, n_blk - 1)], "dyn m")

        @pl.when(is_owner)
        def _():
            has_sent(smg.at[pl.ds(0, n_blk - 1)], "sac m")

        for group in range(2):
            has_sent(froms[group].at[pl.ds(0, n_dp - 1)], ("plane sum", group))
        for part in range(3):
            has_sent(line_bytes(part), ("line sum", part))

    @pl.when(is_owner)
    def _():
        take_matrix(2)
        schulz([mat.at[2]], NS_ITERS)
        send_sac(2)

    sent_early()
    hand_on("pack")
    hand_on("x")
    has_come(small.at[pl.ds(0, (n_dp - 1) * lay.sml)], "small")
    from_sibling("pack")
    from_sibling("x")

    @pl.when(jnp.logical_not(is_owner))
    def _():
        for k in range(3):
            sac_g_copy(k, sibling).wait_recv()
            sac_x_copy(k, sibling).wait_recv()

    has_sent(small.at[pl.ds(0, (n_dp - 1) * lay.sml)], "small")
    gave("pack")
    gave("x")

    @pl.when(jnp.logical_not(is_owner))
    def _():
        for k in range(3):
            tile_copy(k).wait_send()

    @pl.when(is_owner)
    def _():
        for k in range(3):
            plane_peers(lambda peer: sac_g_copy(k, peer).wait_send())
            plane_peers(lambda peer: sac_x_copy(k, peer).wait_send())


def adamw(weights, first, second, gradient):
    first = BETA_FIRST * first + (1.0 - BETA_FIRST) * gradient
    second = BETA_SECOND * second + (1.0 - BETA_SECOND) * gradient * gradient
    first_hat = first / (1.0 - BETA_FIRST**STEP)
    second_hat = second / (1.0 - BETA_SECOND**STEP)
    step = first_hat / (jnp.sqrt(second_hat) + 1e-8) + ADAM_DECAY * weights
    return weights - ADAM_RATE * step, first, second


def update_kernel(*refs):
    (
        sac_g, sac_x, dyn_x, dyn_s, small, count, sac_h, sac_m, dyn_h, dyn_m,
        ci, ci_m, ci_v, ai, ai_m, ai_v, di, di_m, di_v, co, co_m, co_v, ao, ao_m, ao_v,
        do, do_m, do_v, bi, bi_m, bi_v,
        sac_new, sac_mom, dyn_new, dyn_mom, ci_n, ci_mn, ci_vn, ai_n, ai_mn, ai_vn, di_n, di_mn,
        di_vn, co_n, co_mn, co_vn, ao_n, ao_mn, ao_vn, do_n, do_mn, do_vn, bi_n, bi_mn, bi_vn,
        loss, counted, bg,
    ) = refs
    total = count[0:1, 0:1]
    sac_mom[...] = MOMENTUM * sac_m[...] + sac_g[...] / total.reshape(1, 1, 1)
    sac_new[...] = sac_h[...] * (1.0 - MUON_RATE * MUON_DECAY) - MUON_RATE * sac_x[...]
    dyn_rows = dyn_s[:, D_HID : D_HID + dyn_m.shape[1], 0:HDYN]
    dyn_mom[...] = MOMENTUM * dyn_m[...] + dyn_rows / total.reshape(1, 1, 1)
    dyn_new[...] = dyn_h[...] * (1.0 - MUON_RATE * MUON_DECAY) - MUON_RATE * dyn_x[...]

    def rows(row, number):
        sides = []
        for side in range(2):
            at = side * (R_SMALL // 8) + row // 8
            sides.append(small[at : at + -(-number // 8)].reshape(-1, 128))
        return jnp.concatenate(sides, 1)

    def store(outs, at, values):
        for out, value in zip(outs, values):
            out[at] = value

    outs = (ci_n, ci_mn, ci_vn)
    for k in range(2):
        at = (slice(None), k, slice(None))
        grad = rows(R_IN + 24 * k, 24)
        bg[:, CB1 + HSAC * k : CB1 + HSAC * (k + 1)] = grad[IN : IN + 1]
        store(outs, at, adamw(ci[at], ci_m[at], ci_v[at], grad[0:IN] / total))
    grad = rows(R_IN + 48, 24)
    bg[:, AB1 : AB1 + HSAC] = grad[IN : IN + 1]
    store((ai_n, ai_mn, ai_vn), ..., adamw(ai[...], ai_m[...], ai_v[...], grad[0:OBS] / total))
    grad = rows(R_HEAD, 16)
    for at, row in ((slice(0, ACT), slice(1, 1 + ACT)), (slice(ACT, 2 * ACT), slice(9, 9 + ACT))):
        store((ao_n, ao_mn, ao_vn), at, adamw(ao[at], ao_m[at], ao_v[at], grad[row] / total))
    grad = rows(R_OUT, 8)
    store((co_n, co_mn, co_vn), ..., adamw(co[...], co_m[...], co_v[...], grad[0:2] / total))
    bg[:, CB2 : CB2 + HSAC] = grad[2:3]
    bg[:, CB2 + HSAC : CB2 + 2 * HSAC] = grad[3:4]
    bg[:, AB2 : AB2 + HSAC] = grad[4:5]
    grad = rows(R_MISC, 8)
    bg[:, CB3 : CB3 + 1] = grad[0:1, 16:17]
    bg[:, CB3 + 1 : CB3 + 2] = grad[0:1, 32:33]
    bg[:, AB3 : AB3 + ACT] = grad[0:1, 1 : 1 + ACT]
    bg[:, AB3 + ACT : AB3 + 2 * ACT] = grad[0:1, 9 : 9 + ACT]
    bg[:, LOGA : LOGA + 1] = -grad[0:1, 65:66]
    total_loss = grad[0:1, 64:65]
    up = jnp.zeros((1, HALF), F32)
    low = jnp.zeros((1, HALF), F32)
    for e in range(MEMBERS):
        pack = dyn_s[e]
        total_loss = total_loss + pack[D_LOSS : D_LOSS + 1, 0:1]
        up = up + pack[D_UP : D_UP + 1, 0:HALF]
        low = low + pack[D_LOW : D_LOW + 1, 0:HALF]
        bg[:, DB1 + HDYN * e : DB1 + HDYN * (e + 1)] = pack[IN : IN + 1, 0:HDYN]
        bg[:, DB2 + HDYN * e : DB2 + HDYN * (e + 1)] = pack[D_B2 : D_B2 + 1, 0:HDYN]
        bg[:, DB3 + DOUT * e : DB3 + DOUT * e + HALF] = pack[D_B3 : D_B3 + 1, 0:HALF]
        bg[:, DB3 + DOUT * e + HALF : DB3 + DOUT * (e + 1)] = pack[D_B3 : D_B3 + 1, 24 : 24 + HALF]
        grad = pack[0:IN, 0:HDYN] / total
        store((di_n, di_mn, di_vn), e, adamw(di[e], di_m[e], di_v[e], grad))
        grad = pack[D_OUT : D_OUT + DOUT, 0:HDYN] / total
        store((do_n, do_mn, do_vn), e, adamw(do[e], do_m[e], do_v[e], grad))
    bg[:, MAXLV : MAXLV + HALF] = up
    bg[:, MINLV : MINLV + HALF] = low
    lane = lax.broadcasted_iota(jnp.int32, (1, NB), 1)
    bounds = jnp.where(
        jnp.logical_and(lane >= MAXLV, lane < MINLV),
        BOUND_WEIGHT,
        jnp.where(jnp.logical_and(lane >= MINLV, lane < LOGA), -BOUND_WEIGHT, 0.0),
    )
    grad = bg[...] / total + bounds
    flat = [ref[...].reshape(1, NB) for ref in (bi, bi_m, bi_v)]
    store((bi_n, bi_mn, bi_vn), ..., [value.reshape(NB) for value in adamw(*flat, grad)])
    loss[...] = total_loss
    counted[...] = total


def shards(
    lay, replay, model_rows, requests, member_of, model_live, noise, sac_hidden, sac_hidden_mom,
    dyn_hidden, dyn_hidden_mom, crit_in, crit_in_m, crit_in_v, act_in, act_in_m, act_in_v, dyn_in,
    dyn_in_m, dyn_in_v, crit_out, crit_out_m, crit_out_v, act_out, act_out_m, act_out_v, dyn_out,
    dyn_out_m, dyn_out_v, biases, biases_m, biases_v, targ_in, targ_hidden, targ_out, targ_bias,
):
    n_dp, n_blk = lay.n_dp, lay.n_blk
    spec = pl.BlockSpec(memory_space=pltpu.VMEM)

    def flip(value):
        return jnp.transpose(value, (1, 0, 2))

    def swap(value):
        return jnp.swapaxes(value, -1, -2)

    def kept(value):
        return pltpu.with_memory_space_constraint(value, pltpu.VMEM)

    inputs = (
        replay, model_rows, requests, member_of, model_live, jnp.transpose(noise, (2, 0, 1)),
        sac_hidden, sac_hidden_mom, dyn_hidden, dyn_hidden_mom, flip(crit_in), act_in, dyn_in,
        crit_out, swap(act_out), swap(dyn_out), biases, flip(targ_in), targ_hidden, targ_out,
        targ_bias,
    )
    shape = jax.ShapeDtypeStruct
    rows, drows = lay.rows, lay.drows
    out_shape = (
        pltpu.VMEM((3, rows, HSAC), F32),
        pltpu.VMEM((3, rows, HSAC), F32),
        pltpu.VMEM((MEMBERS, drows, HDYN), F32),
        pltpu.VMEM((MEMBERS, D_ROWS, HSAC), F32),
        pltpu.VMEM((32, 8, 128), F32),
        pltpu.VMEM((8, 128), F32),
    )

    def vm(*dims, kind=F32):
        return pltpu.VMEM(dims, kind)

    scratch = [
        vm(n_blk, 3, rows, HSAC, kind=BF16),
        vm(2, n_dp, CAP, kind=jnp.int32),
        vm(n_dp, 2, n_dp, CAP, kind=jnp.int32),
        vm(n_blk, drows, HDYN),
        vm(n_blk, drows, HDYN),
        vm(n_blk, 3, rows, HSAC),
        vm(lay.n_dev, 48, lay.width),
        vm(56, lay.batch),
        vm(2, 8, lay.batch),
        vm(5, 32, HSAC),
        vm(5, HSAC, 32, kind=BF16),
        vm(2, 16, HSAC, kind=BF16),
        vm(5, HSAC, HSAC, kind=BF16),
        vm(3, HSAC, HSAC, kind=BF16),
        vm(5, 16, HSAC, kind=BF16),
        vm(HSAC, 16, kind=BF16),
        vm(16, HSAC),
        vm(8, HSAC),
        vm(7, HSAC, 128),
        vm(128, 8),
        vm(3, HSAC + 16, HSAC),
        vm(3, 32, HSAC),
        vm(2, 16, HSAC),
        vm(16, HSAC),
        vm(16, 48),
        vm(8, TILE),
        vm(n_dp, lay.chunks[0], 8, 128),
        vm(n_dp, lay.chunks[1], 8, 128),
        vm(n_dp, lay.chunks[0], 8, 128),
        vm(n_dp, lay.chunks[1], 8, 128),
        vm(n_blk, lay.chunks[0], 8, 128),
        vm(n_blk, lay.chunks[1], 8, 128),
        vm(lay.chunks[0], 8, 128),
        vm(lay.chunks[1], 8, 128),
        vm(lay.chunks[0], 8, 128),
        vm(lay.chunks[1], 8, 128),
        vm(3, n_dp, lay.mat, 8, 128),
        vm(3, HSAC, HSAC),
        vm(3, HSAC, HSAC),
        vm(HSAC, 8),
        vm(HSAC + 16, HSAC),
        vm(32, HSAC),
        vm(48, HSAC),
        vm(16, 48),
        vm(2, 24, DYN_TILE),
        vm(8, DYN_TILE),
        vm(48, DYN_TILE),
        vm(HSAC, HSAC),
        vm(D_ROWS, HSAC),
        vm(drows, HDYN),
        vm(1, NB),
        vm(48, HSAC, kind=BF16),
        vm(HSAC, 48, kind=BF16),
    ]
    scratch += [pltpu.SemaphoreType.DMA((lay.departures,)), pltpu.SemaphoreType.DMA((lay.arrivals,))]
    varying = 4 * (lay.n_dev * 48 * lay.width + 72 * lay.batch + 48 * lay.replay)
    gathered = pl.pallas_call(
        functools.partial(main_kernel, lay),
        out_shape=out_shape,
        in_specs=[spec] * len(inputs),
        out_specs=[spec] * len(out_shape),
        scratch_shapes=scratch,
        compiler_params=pltpu.CompilerParams(
            collective_id=0, has_side_effects=True, vmem_limit_bytes=26 * 2**20 + varying
        ),
        name="step",
    )(*[pltpu.with_memory_space_constraint(value, pltpu.HBM) for value in inputs])
    params = (
        sac_hidden, sac_hidden_mom, dyn_hidden, dyn_hidden_mom,
        flip(crit_in), flip(crit_in_m), flip(crit_in_v), act_in, act_in_m, act_in_v,
        dyn_in, dyn_in_m, dyn_in_v, crit_out, crit_out_m, crit_out_v,
        swap(act_out), swap(act_out_m), swap(act_out_v),
        swap(dyn_out), swap(dyn_out_m), swap(dyn_out_v), biases, biases_m, biases_v,
    )
    new_shape = [shape(value.shape, F32) for value in params]
    new_shape += [shape((1, 1), F32)] * 2
    out = pl.pallas_call(
        update_kernel,
        out_shape=tuple(new_shape),
        in_specs=[spec] * (len(gathered) + len(params)),
        out_specs=[spec] * len(new_shape),
        scratch_shapes=[vm(1, NB)],
        compiler_params=pltpu.CompilerParams(vmem_limit_bytes=16 * 2**20),
        name="update",
    )(*[kept(value) for value in gathered], *params)
    out = list(out)
    for at in (4, 5, 6):
        out[at] = flip(out[at])
    for at in (16, 17, 18, 19, 20, 21):
        out[at] = swap(out[at])
    for at in (25, 26):
        out[at] = out[at].reshape(())
    return tuple(out)


def solution(mesh):
    both = ("dp", "blk")
    sharded = (
        P(None, both), P(None, both), P(both, None), P(both, None), P(both), P(None, both, None),
    )
    hidden = (P(None, "blk", None),) * 4

    def step(replay, model_rows, *others):
        lay = Layout(mesh, replay.shape[1], model_rows.shape[1])
        return shards(lay, replay, model_rows, *others)

    return jax.shard_map(
        step,
        mesh=mesh,
        in_specs=sharded + hidden + (P(),) * 25,
        out_specs=hidden + (P(),) * 23,
        check_vma=False,
    )
```

```python
import functools

import jax
import jax.numpy as jnp
from jax import lax
from jax.experimental import pallas as pl
from jax.experimental.pallas import tpu as pltpu
from jax.sharding import PartitionSpec as P

OBS = 17
ACT = 6
IN = OBS + ACT
FEAT = 42
HDYN = 200
HSAC = 256
MEMBERS = 7
DOUT = 36
HALF = DOUT // 2
NB = 4639
NS_ITERS = 5
STEP = 10
CAP = 8
TILE = 640
DYN_TILE = 512
ROWS = 32

DISCOUNT = 0.99
TARGET_ENTROPY = -6.0
BOUND_WEIGHT = 0.01
MOMENTUM = 0.95
MUON_RATE = 0.4
MUON_DECAY = 0.01
ADAM_RATE = 0.1
ADAM_DECAY = 0.01
BETA_FIRST = 0.9
BETA_SECOND = 0.999
COEF_LINEAR = 3.4445
COEF_CUBIC = -4.775
COEF_QUINTIC = 2.0315

CB1, CB2, CB3, AB1, AB2, AB3 = 0, 512, 1024, 1026, 1282, 1538
DB1, DB2, DB3, MAXLV, MINLV, LOGA = 1550, 2950, 4350, 4602, 4620, 4638

R_IN, R_HEAD, R_OUT, R_MISC, R_SMALL = 0, 72, 88, 96, 128
D_IN, D_OUT, D_B2, D_B3, D_UP, D_LOW, D_LOSS, D_HID, D_ROWS = 0, 24, 60, 61, 62, 63, 64, 72, 128

F32, BF16 = jnp.float32, jnp.bfloat16
MESH = pl.DeviceIdType.MESH
NN = (((1,), (0,)), ((), ()))
NT = (((1,), (1,)), ((), ()))


def dot(a, b, dims=NN):
    return lax.dot_general(a, b, dims, preferred_element_type=F32)


def rounded(v):
    return v.astype(BF16).astype(F32)


def pieces(v):
    high = v.astype(BF16)
    rest = v - high.astype(F32)
    middle = rest.astype(BF16)
    return high, middle, (rest - middle.astype(F32)).astype(BF16)


def split(v):
    high = v.astype(BF16)
    return high, (v - high.astype(F32)).astype(BF16)


def product(a, b, dims=NN):
    left = jnp.concatenate([a[0], a[0], a[1]], 1)
    right = jnp.concatenate([b[0], b[1], b[0]], dims[0][1][0])
    half = left.shape[0] // 2
    return jnp.concatenate([dot(left[:half], right, dims), dot(left[half:], right, dims)], 0)


def softplus(v):
    return jnp.maximum(v, 0.0) + jnp.log1p(jnp.exp(-jnp.abs(v)))


def sigmoid(v):
    return 0.5 + 0.5 * jnp.tanh(0.5 * v)


def gate(half):
    up = 1.0 + jnp.tanh(half)
    value = half * up
    return value, up + value * (2.0 - up)


def by_rows(body, *arrays):
    done = [
        body(*[array[at : at + ROWS] for array in arrays]) for at in range(0, arrays[0].shape[0], ROWS)
    ]
    return [jnp.concatenate(parts, 0) for parts in zip(*done)]


def spread_to(column, width):
    return jnp.concatenate([column] * (width // 128), 1)


def gated(half, column=None):
    def body(part, *offset):
        value, slope = gate(part + spread_to(offset[0], part.shape[1]) if offset else part)
        return value.astype(BF16), slope

    return by_rows(body, half, *([] if column is None else [column]))


def sloped(grad, slope):
    return by_rows(lambda part, by: ((part * by).astype(BF16),), grad, slope)[0]


def outer_sloped(column, row, slope):
    return by_rows(lambda part, by: (((spread_to(part, by.shape[1]) * row) * by).astype(BF16),), column, slope)[0]


def rows_of(shape):
    return lax.broadcasted_iota(jnp.int32, shape, 0)


def schulz(refs, steps, before=None):
    @pl.loop(0, steps)
    def _(step):
        if before is not None:
            before(step)
        matrices = [ref[...] for ref in refs]
        parts = [split(matrix) for matrix in matrices]
        grams = [product(part, part, NT) for part in parts]
        halves = [split(gram) for gram in grams]
        squares = [product(half, half) for half in halves]
        blends = [
            split(COEF_CUBIC * gram + COEF_QUINTIC * square) for gram, square in zip(grams, squares)
        ]
        moved = [product(blend, part) for blend, part in zip(blends, parts)]
        for ref, matrix, move in zip(refs, matrices, moved):
            ref[...] = COEF_LINEAR * matrix + move


def normalise(ref):
    moment = ref[...]
    norm = jnp.sqrt(jnp.sum(jnp.sum(moment * moment, axis=1, keepdims=True), axis=0, keepdims=True))
    ref[...] = moment / (norm + 1e-7)


class Layout:
    def __init__(self, mesh, replay, model):
        self.n_dp = mesh.shape["dp"]
        self.n_blk = mesh.shape["blk"]
        self.n_dev = self.n_dp * self.n_blk
        self.replay = replay
        self.model = model
        self.real = self.n_dp * CAP
        self.batch = self.real + model
        self.width = -(-(self.real + 2) // 128) * 128
        self.rows = HSAC // self.n_blk
        self.drows = HDYN // self.n_blk
        self.mat = 64 // self.n_dp
        self.sml = 32 // self.n_dp
        self.chunks = (2 * self.mat, self.mat + self.sml)
        self.owner = self.n_dp - 1

        groups = [("plane sum", g) for g in range(2)] + [("line sum", g) for g in range(3)]
        common = ["hidden", "hidden on", "lists", "own", "line", "plane", "dyn h", "dyn m", "small"]
        common += groups + ["sac g c", "sac g a"]
        kinds = [(name, kind) for name in ("pack", "x") for kind in ("own", "on")]
        sent = common + [("tiles", k) for k in range(3)] + kinds
        self.sent = {name: at for at, name in enumerate(sent)}
        self.departures = len(sent)
        for name in ("sac x c", "sac x a"):
            self.sent[name] = self.departures
            self.departures += self.n_dp
        self.here, self.arrivals = {}, 0
        tiles = [("tiles", k) for k in range(3)]
        tiles += ["sac x c", "sac x a", ("pack", "sibling"), ("x", "sibling")]
        for name in common + tiles:
            self.here[name] = self.arrivals
            self.arrivals += 1
        for name in ("pack", "x"):
            self.here[name, "like"] = self.arrivals
            self.arrivals += MEMBERS
        self.keepers = 2 * (self.rows // 8) // self.mat


def main_kernel(lay, *refs):
    (
        replay, model, requests, member, live, noise, sac_h, sac_m, dyn_h, dyn_m, crit_in, act_in,
        dyn_in, crit_out, act_out, dyn_out, biases, targ_in, targ_hidden, targ_out, targ_bias,
        sac_g, sac_x, dyn_x, dyn_s, small, count,
        wg, lists, asked, dhg, dmg, bk, xs, nz, w1f, w1t, w1n, w2t, w2h, heads, head_t, head_f,
        rowbuf, wide, headcol, acc_h, acc_w, acc_c, acc_a, acc_m, acc_l, grid_c, grid_a, from_c, from_a,
        zr_c, zr_a, zf_c, zf_a, sum_c, sum_a, mg, mat, dcols, dacc_h, dacc_w, dacc_o, dacc_m, dacc_b, dacc_l, xt, dmat,
        dpack, drow_x, bias, dhead, dhead_t, *rest,
    ) = refs
    send, recv = rest
    sent, here_at = lay.sent, lay.here
    grids, froms, zrs, zfs = (grid_c, grid_a), (from_c, from_a), (zr_c, zr_a), (zf_c, zf_a)
    n_dp, n_blk = lay.n_dp, lay.n_blk
    me = lax.axis_index("dp")
    z = lax.axis_index("blk")
    core = lax.rem(me, 2)
    sibling = me + 1 - 2 * core
    is_dyn = me < MEMBERS
    dyn_e = jnp.minimum(me, MEMBERS - 1)
    is_owner = me == lay.owner

    def on_plane(src, dst, ssem, rsem, peer):
        return pltpu.make_async_remote_copy(
            src_ref=src, dst_ref=dst, send_sem=ssem, recv_sem=rsem,
            device_id={"dp": peer}, device_id_type=MESH,
        )

    def on_line(src, dst, ssem, rsem, peer):
        return pltpu.make_async_remote_copy(
            src_ref=src, dst_ref=dst, send_sem=ssem, recv_sem=rsem,
            device_id={"blk": peer}, device_id_type=MESH,
        )

    def over(number, body):
        if number <= 8:
            for off in range(1, number):
                body(off)
        else:
            pl.loop(1, number)(body)

    def plane_peers(body):
        over(n_dp, lambda off: body(lax.rem(me + off, n_dp)))

    def like_peers(body):
        over(n_dp // 2, lambda off: body(lax.rem(me + 2 * off, n_dp)))

    def line_peers(body):
        over(n_blk, lambda off: body(lax.rem(z + off, n_blk)))

    def has_sent(view, name):
        at = send.at[sent[name]]
        on_plane(view, view, at, at, sibling).wait_send()

    def has_come(view, name):
        at = recv.at[here_at[name]]
        on_plane(view, view, at, at, sibling).wait_recv()

    barrier = pltpu.get_barrier_semaphore()
    plane_peers(lambda peer: pl.semaphore_signal(barrier, inc=1, device_id={"dp": peer}, device_id_type=MESH))
    line_peers(lambda peer: pl.semaphore_signal(barrier, inc=1, device_id={"blk": peer}, device_id_type=MESH))
    wg[0] = sac_h[...].astype(BF16)
    lists[0] = requests[...]
    lists[1] = member[...]
    pl.semaphore_wait(barrier, n_dp - 1 + n_blk - 1)

    half_rows = pl.ds(pl.multiple_of(core * (lay.rows // 2), lay.rows // 2), lay.rows // 2)

    def slot_from(owner, at):
        return lax.rem(owner - at + n_blk, n_blk)

    def hidden_copy(peer):
        src = wg.at[0, :, half_rows]
        dst = wg.at[slot_from(z, peer), :, half_rows]
        return on_line(src, dst, send.at[sent["hidden"]], recv.at[here_at["hidden"]], peer)

    def hidden_on():
        view = wg.at[pl.ds(1, n_blk - 1), :, half_rows]
        return on_plane(view, view, send.at[sent["hidden on"]], recv.at[here_at["hidden on"]], sibling)

    def list_copy(peer):
        return on_plane(lists, asked.at[me], send.at[sent["lists"]], recv.at[here_at["lists"]], peer)

    line_peers(lambda peer: hidden_copy(peer).start())
    plane_peers(lambda peer: list_copy(peer).start())
    asked[me] = lists[...]

    def dyn_h_copy(peer):
        return on_line(dyn_h.at[dyn_e], dhg.at[z], send.at[sent["dyn h"]], recv.at[here_at["dyn h"]], peer)

    def dyn_m_copy(peer):
        return on_line(dyn_m.at[dyn_e], dmg.at[z], send.at[sent["dyn m"]], recv.at[here_at["dyn m"]], peer)

    alive = live[...].astype(F32).reshape(1, lay.model)
    bias[...] = biases[...].reshape(1, NB)
    xs[42:56, :] = jnp.zeros((14, lay.batch), F32)
    xs[0:FEAT, lay.real : lay.batch] = model[...]
    xs[42:43, lay.real : lay.batch] = alive
    nz[...] = jnp.zeros_like(nz)
    for which in range(2):
        nz[which, 1:7, :] = noise[:, which, :]
    firsts = [
        (targ_in[:, 0, :], targ_bias[0:1, 0:HSAC]),
        (targ_in[:, 1, :], targ_bias[1:2, 0:HSAC]),
        (crit_in[:, 0, :], bias[:, CB1 : CB1 + HSAC]),
        (crit_in[:, 1, :], bias[:, CB1 + HSAC : CB1 + 2 * HSAC]),
        (act_in[...], bias[:, AB1 : AB1 + HSAC]),
    ]
    w1f[...] = jnp.zeros_like(w1f)
    for net, (weights, offset) in enumerate(firsts):
        w1f[net, 0 : weights.shape[0], :] = rounded(weights)
        for at, piece in enumerate(pieces(offset)):
            w1f[net, IN + at : IN + at + 1, :] = piece.astype(F32)
        w1t[net] = (0.5 * w1f[net].T).astype(BF16)
    for k in range(2):
        w1n[k] = w1f[2 + k, 16:32, :].astype(BF16)
    for net in range(2):
        w2t[net] = (0.5 * rounded(targ_hidden[net])).T.astype(BF16)
    has_come(wg.at[pl.ds(0, n_blk - 1), :, half_rows], "hidden")
    hidden_on().start()

    rowbuf[...] = jnp.zeros_like(rowbuf)
    rowbuf[0:1, :] = targ_bias[0:1, HSAC : 2 * HSAC]
    rowbuf[1:2, :] = targ_bias[1:2, HSAC : 2 * HSAC]
    rowbuf[2:3, :] = bias[:, CB2 : CB2 + HSAC]
    rowbuf[3:4, :] = bias[:, CB2 + HSAC : CB2 + 2 * HSAC]
    rowbuf[4:5, :] = bias[:, AB2 : AB2 + HSAC]
    rowbuf[5:7, :] = rounded(crit_out[...])
    columns = 0.5 * rowbuf[...].T
    for at in range(7):
        wide[at] = jnp.broadcast_to(columns[:, at : at + 1], (HSAC, 128))
    rowbuf[...] = jnp.zeros_like(rowbuf)
    rowbuf[0:1, 1:7] = bias[:, AB3 : AB3 + ACT]
    rowbuf[0:1, 9:15] = bias[:, AB3 + ACT : AB3 + 2 * ACT]
    headcol[...] = rowbuf[:, 0:128].T
    head_f[...] = jnp.zeros_like(head_f)
    for k in range(2):
        head_f[0:1, :] = targ_out[k : k + 1, :]
        heads[k] = head_f[...].astype(BF16)
        head_f[0:1, :] = crit_out[k : k + 1, :]
        heads[2 + k] = head_f[...].astype(BF16)
    head_f[0:1, :] = jnp.zeros((1, HSAC), F32)
    head_f[1:7, :] = act_out[0:ACT, :]
    head_f[9:15, :] = act_out[ACT : 2 * ACT, :]
    heads[4] = head_f[...].astype(BF16)
    head_t[...] = (0.5 * rounded(head_f[...])).T.astype(BF16)
    for ref in (acc_h, acc_w, acc_c, acc_a, acc_m, acc_l):
        ref[...] = jnp.zeros_like(ref)

    data = replay[...]
    sums = jnp.sum(data[0:24], axis=1, keepdims=True)
    squares = jnp.sum(data[0:24] * data[0:24], axis=1, keepdims=True)
    living = jnp.sum(alive, axis=1, keepdims=True)

    has_come(asked.at[pl.ds(0, n_dp - 1)], "lists")
    spread = (
        lax.rem(lax.broadcasted_iota(jnp.int32, (CAP, lay.real), 1), CAP)
        == lax.broadcasted_iota(jnp.int32, (CAP, lay.real), 0)
    ).astype(F32)
    here = (
        lax.broadcasted_iota(jnp.int32, (n_dp, lay.real), 1) // CAP
        == lax.broadcasted_iota(jnp.int32, (n_dp, lay.real), 0)
    )

    def in_lanes(which):
        values = asked[:, which, me, :].astype(F32)
        wide = lax.dot_general(
            values, spread, NN, precision=lax.Precision.HIGHEST, preferred_element_type=F32
        )
        return jnp.sum(jnp.where(here, wide, 0.0), axis=0, keepdims=True)

    slots = in_lanes(0)
    wanted = jnp.maximum(slots, 0.0).astype(jnp.int32)
    hot = (rows_of((lay.replay, lay.real)) == wanted).astype(BF16)
    high, middle, low = pieces(data)
    picked = dot(high, hot) + dot(middle, hot) + dot(low, hot)
    mine = me * n_blk
    bk[mine, 0:FEAT, 0 : lay.real] = picked
    bk[mine, 42:43, 0 : lay.real] = (slots >= 0.0).astype(F32)
    bk[mine, 43:44, 0 : lay.real] = in_lanes(1)
    bk[mine, 44:48, 0 : lay.real] = jnp.zeros((4, lay.real), F32)
    bk[mine, :, lay.real : lay.width] = jnp.zeros((48, lay.width - lay.real), F32)
    bk[mine, 0:24, lay.real : lay.real + 1] = sums
    bk[mine, 0:24, lay.real + 1 : lay.real + 2] = squares
    bk[mine, 24:25, lay.real : lay.real + 1] = living

    def slot_of(block):
        line = lax.rem(block, n_blk)
        return block - line + slot_from(line, z)

    def block_line(peer):
        dst = bk.at[me * n_blk + slot_from(z, peer)]
        return on_line(bk.at[mine], dst, send.at[sent["line"]], recv.at[here_at["line"]], peer)

    def block_own(peer):
        view = bk.at[mine]
        return on_plane(view, view, send.at[sent["own"]], recv.at[here_at["own"]], peer)

    def block_plane(peer):
        view = bk.at[pl.ds(mine + 1, n_blk - 1)]
        return on_plane(view, view, send.at[sent["plane"]], recv.at[here_at["plane"]], peer)

    plane_peers(lambda peer: block_own(peer).start())
    line_peers(lambda peer: block_line(peer).start())

    @pl.when(is_dyn)
    def _():
        line_peers(lambda peer: dyn_h_copy(peer).start())
        line_peers(lambda peer: dyn_m_copy(peer).start())

    has_come(wg.at[pl.ds(0, n_blk - 1), :, half_rows], "hidden on")
    for k in range(3):
        for block in range(n_blk):
            w2h[k, block * lay.rows : (block + 1) * lay.rows, :] = (
                0.5 * wg[slot_from(block, z), k].astype(F32)
            ).astype(BF16)
        w2t[2 + k] = w2h[k].astype(F32).T.astype(BF16)

    log_alpha = bias[:, LOGA : LOGA + 1]
    alpha = jnp.exp(log_alpha)
    last = [
        targ_bias[0:1, 2 * HSAC : 2 * HSAC + 1],
        targ_bias[1:2, 2 * HSAC : 2 * HSAC + 1],
        bias[:, CB3 : CB3 + 1],
        bias[:, CB3 + 1 : CB3 + 2],
    ]
    n_tiles = lay.batch // TILE
    row8 = rows_of((8, TILE))
    act_rows = jnp.logical_and(row8 >= 1, row8 < 1 + ACT)

    def place_of(step):
        return pl.ds(pl.multiple_of(lax.rem(step + 1, n_tiles) * TILE, TILE), TILE)

    def ones16(width=TILE):
        return jnp.ones((16, width), BF16)

    def framed(first_row, used, where):
        row32 = rows_of((32, TILE))
        ones3 = jnp.logical_and(row32 >= IN, row32 < IN + 3).astype(F32)
        return jnp.where(row32 < used, xs[first_row : first_row + 32, where], ones3)

    def hidden(inputs, net):
        first, slope1 = gated(dot(w1t[net], inputs))
        second, slope2 = gated(dot(w2t[net], first), wide[net])
        return first, slope1, second, slope2

    def policy(inputs, which, where):
        first, slope1, second, slope2 = hidden(inputs, 4)
        out = dot(heads[4], second) + headcol[0:16, 0:1]
        bent = jnp.tanh(out[8:16])
        log_scale = -5.0 + 3.5 * (bent + 1.0)
        draw = nz[which, :, where]
        moved = jnp.exp(log_scale) * draw
        latent = out[0:8] + moved
        terms = (
            -0.5 * draw * draw
            - log_scale
            - 0.9189385
            - 2.0 * (0.6931472 - latent - softplus(-2.0 * latent))
        )
        log_prob = jnp.sum(jnp.where(act_rows, terms, 0.0), axis=0, keepdims=True)
        action = jnp.where(act_rows, jnp.tanh(latent), 0.0)
        return action, log_prob, bent, moved, (first, slope1, second, slope2)

    def with_action(inputs, action):
        middle_rows = jnp.where(act_rows, action, inputs[16:24])
        return jnp.concatenate([inputs[0:16], middle_rows, inputs[24:32]], 0).astype(BF16)

    def critic(inputs, net):
        kept = hidden(inputs, net)
        value = dot(heads[net], kept[2])[0:1] + last[net]
        return value, kept

    def add_hidden(k, first, grad):
        acc_h[k] += dot(jnp.concatenate([first, ones16()], 0), grad, NT)

    has_come(bk.at[pl.ds(0, n_blk - 1)], "line")
    plane_peers(lambda peer: block_plane(peer).start())

    @pl.loop(0, n_tiles)
    def _(step):
        @pl.when(step == n_tiles - 1)
        def _():
            has_come(bk.at[pl.ds(0, n_dp - 1)], "own")
            lanes = lax.broadcasted_iota(jnp.int32, (48, lay.width), 1) // CAP

            def gather(owner, total):
                turned = pltpu.roll(
                    bk[owner * n_blk], lax.rem((owner - me) * CAP + lay.width, lay.width), axis=1
                )
                return jnp.where(lanes == owner, turned, total)

            own = lax.fori_loop(0, n_dp, gather, jnp.zeros((48, lay.width), F32))
            xs[0:48, 0 : lay.real] = own[:, 0 : lay.real]

        where = place_of(step)
        now_in = framed(0, IN, where).astype(BF16)
        next_f = framed(24, OBS, where)
        reward = xs[23:24, where]
        done = xs[41:42, where]
        weight = xs[42:43, where]
        row16 = rows_of((16, TILE))
        next_action, next_prob, _, _, _ = policy(next_f.astype(BF16), 1, where)
        aim_in = with_action(next_f, next_action)
        aim = jnp.minimum(critic(aim_in, 0)[0], critic(aim_in, 1)[0])
        target = reward + DISCOUNT * (1.0 - done) * (aim - alpha * next_prob)
        loss = jnp.zeros((1, TILE), F32)
        heads_grad = []
        for k in range(2):
            value, (c1, dc1, c2, dc2) = critic(now_in, 2 + k)
            miss = value - target
            loss += 0.5 * miss * miss
            g3 = rounded(weight * miss)
            g3_rows = jnp.where(row16 == 0, g3, 0.0).astype(BF16)
            heads_grad.append(g3_rows)
            acc_c[k] += dot(g3_rows, c2, NT)
            g2 = outer_sloped(wide[5 + k], g3, dc2)
            add_hidden(k, c1, g2)
            g1 = sloped(dot(w2h[k], g2), dc1)
            acc_w[k] += dot(now_in, g1, NT)
        acc_m[:, 16:48] += dot(ones16(), jnp.concatenate(heads_grad, 0), NT)
        acc_l[0:1, :] += weight * loss

    def put_matrix(group, k, at):
        for chunk in range(n_dp):
            tile = chunk * lay.mat
            side, row = tile // 32, tile % 32
            grids[group][chunk, at * lay.mat : (at + 1) * lay.mat] = acc_h[
                k, row * 8 : (row + lay.mat) * 8, side * 128 : (side + 1) * 128
            ].reshape(lay.mat, 8, 128)

    def put(row, value):
        for at in range(value.shape[0] // 8):
            for side in range(value.shape[1] // 128):
                tile = side * (R_SMALL // 8) + row // 8 + at
                grid_a[tile // lay.sml, lay.mat + tile % lay.sml] = value[
                    at * 8 : at * 8 + 8, side * 128 : (side + 1) * 128
                ]

    def plane_sum(group, peer):
        name = ("plane sum", group)
        return on_plane(
            grids[group].at[peer], froms[group].at[me], send.at[sent[name]], recv.at[here_at[name]], peer
        )

    def line_part(part):
        group = min(part, 1)
        tiles = (pl.ds(0, 2 * lay.mat), pl.ds(0, lay.mat), pl.ds(lay.mat, lay.sml))[part]
        return group, tiles

    def line_sum(part, peer):
        group, tiles = line_part(part)
        name = ("line sum", part)
        src, dst = zfs[group].at[tiles], zrs[group].at[z, tiles]
        return on_line(src, dst, send.at[sent[name]], recv.at[here_at[name]], peer)

    def line_bytes(part):
        group, tiles = line_part(part)
        return zrs[group].at[pl.ds(0, n_blk - 1), tiles]

    first_tile = me * lay.mat
    side = first_tile // 32
    row_tile = lax.rem(first_tile, 32)
    keeper_z = row_tile * 8 // lay.rows
    local_tile = row_tile - keeper_z * (lay.rows // 8)
    is_keeper = z == keeper_z

    def fold_plane(group):
        has_come(froms[group].at[pl.ds(0, n_dp - 1)], ("plane sum", group))
        froms[group][me] = grids[group][me]
        whole = froms[group][0]
        for at in range(1, n_dp):
            whole = whole + froms[group][at]
        zfs[group][...] = whole

        @pl.when(is_keeper)
        def _():
            held_rows = pl.ds(pl.multiple_of(local_tile * 8, 8), lay.mat * 8)
            held_lanes = pl.ds(pl.multiple_of(side * 128, 128), 128)
            for at, k in enumerate(((0, 1), (2,))[group]):
                old = sac_m[k, held_rows, held_lanes].reshape(lay.mat, 8, 128)
                zfs[group][at * lay.mat : (at + 1) * lay.mat] += (MOMENTUM * total).reshape(1, 1, 1) * old

        for part in (0,) if group == 0 else (1, 2):
            line_peers(lambda peer: line_sum(part, peer).start())

    def tile_copy(k):
        src = (sum_c, sum_a)[k // 2].at[pl.ds((k % 2) * lay.mat, lay.mat)]
        return on_plane(src, mg.at[k, me], send.at[sent["tiles", k]], recv.at[here_at["tiles", k]], lay.owner)

    def small_copy(peer):
        return on_plane(
            sum_a.at[pl.ds(lay.mat, lay.sml)], small.at[pl.ds(me * lay.sml, lay.sml)],
            send.at[sent["small"]], recv.at[here_at["small"]], peer,
        )

    def keep_copy(part, peer):
        ks = pl.ds(2 * part, 2 - part)
        view = sac_g.at[side, ks, pl.ds(local_tile, lay.mat)]
        name = ("sac g c", "sac g a")[part]
        return on_plane(view, view, send.at[sent[name]], recv.at[here_at[name]], peer)

    def kept_bytes(part, number):
        return froms[0].at[pl.ds(0, number)] if part == 0 else mg.at[0, pl.ds(0, number)]

    def fold_end(part):
        group, tiles = line_part(part)
        has_come(line_bytes(part), ("line sum", part))
        zrs[group][z, tiles] = zfs[group][tiles]
        whole = zrs[group][0, tiles]
        for block in range(1, n_blk):
            whole = whole + zrs[group][block, tiles]
        (sum_c, sum_a)[group][tiles] = whole
        for k in ((0, 1), (2,), ())[part]:
            pl.when(jnp.logical_not(is_owner))(tile_copy(k).start)

            @pl.when(is_owner)
            def _():
                mg[k, me] = (sum_c, sum_a)[group][(k % 2) * lay.mat : (k % 2 + 1) * lay.mat]

        if part < 2:
            @pl.when(is_keeper)
            def _():
                for at, k in enumerate(((0, 1), (2,))[part]):
                    sac_g[side, k, pl.ds(local_tile, lay.mat)] = whole[at * lay.mat : (at + 1) * lay.mat]
                plane_peers(lambda peer: keep_copy(part, peer).start())

        if part == 2:
            plane_peers(lambda peer: small_copy(peer).start())
            small[pl.ds(me * lay.sml, lay.sml)] = sum_a[lay.mat :]

    def chain(group):
        def end():
            for part in (0,) if group == 0 else (1, 2):
                fold_end(part)

        return [
            lambda: plane_peers(lambda peer: plane_sum(group, peer).start()),
            lambda: fold_plane(group),
            end,
        ]

    critic_chain, actor_chain = chain(0), chain(1)
    per = DYN_TILE // lay.real
    dyn_tiles = lay.n_dev // per
    in_actor, in_dyn = {}, {}
    if n_tiles > 1:
        in_actor[1] = [critic_chain[1]]
        in_dyn[0] = [critic_chain[2]]
    else:
        in_dyn[0] = [critic_chain[1]]
        in_dyn[min(1, dyn_tiles - 1)] = [critic_chain[2]]
    in_dyn.setdefault(dyn_tiles - 1, []).append(actor_chain[1])

    def take(slots, step):
        for at, events in slots.items():
            @pl.when(step == at)
            def _():
                for event in events:
                    event()

    for k in range(2):
        put_matrix(0, k, k)
    critic_chain[0]()

    has_come(bk.at[pl.ds(0, (n_dp - 1) * (n_blk - 1))], "plane")
    lane0 = lay.real // 128 * 128

    def add_block(at, carry):
        sides, fills = carry
        slot = slot_of(at)
        return sides + bk[slot, 0:32, lane0 : lane0 + 128], fills + bk[slot, 40:48, 0 : lay.real]

    sides, fills = lax.fori_loop(
        0, lay.n_dev, add_block, (jnp.zeros((32, 128), F32), jnp.zeros((8, lay.real), F32))
    )
    at = lay.real - lane0
    rows_all = float(lay.replay * lay.n_dev)
    centre = sides[0:24, at : at + 1] / rows_all
    scale = lax.rsqrt(sides[0:24, at + 1 : at + 2] / rows_all - centre * centre + 1e-6)
    total = sides[24:25, at : at + 1] + jnp.sum(fills[2:3, :], axis=1, keepdims=True)
    count[...] = jnp.broadcast_to(total, (8, 128))

    @pl.loop(0, n_tiles)
    def _(step):
        take(in_actor, step)
        where = place_of(step)
        now_f = framed(0, IN, where)
        now_in = now_f.astype(BF16)
        weight = xs[42:43, where]
        action, log_prob, bent, moved, (a1, da1, a2, da2) = policy(now_in, 0, where)
        judged_in = with_action(now_f, action)
        loss = alpha * log_prob - log_alpha * (log_prob + TARGET_ENTROPY)
        grad_action = jnp.zeros((8, TILE), F32)
        for k in range(2):
            judged, (_, df1, _, df2) = critic(judged_in, 2 + k)
            loss -= 0.5 * judged
            g2 = outer_sloped(wide[5 + k], -0.5 * weight, df2)
            g1 = sloped(dot(w2h[k], g2), df1)
            grad_action += dot(w1n[k], g1)[0:8]
        grad_latent = 2.0 * alpha * weight * action + grad_action * (1.0 - action * action)
        grad_scale = grad_latent * moved - alpha * weight
        grad_bent = grad_scale * 3.5 * (1.0 - bent * bent)
        g3 = jnp.concatenate(
            [jnp.where(act_rows, grad_latent, 0.0), jnp.where(act_rows, grad_bent, 0.0)], 0
        ).astype(BF16)
        acc_a[...] += dot(g3, a2, NT)
        acc_m[:, 0:16] += dot(ones16(), g3, NT)
        g2 = sloped(dot(head_t[...], g3), da2)
        add_hidden(2, a1, g2)
        g1 = sloped(dot(w2h[2], g2), da1)
        acc_w[2] += dot(now_in, g1, NT)
        acc_l[0:1, :] += weight * loss
        acc_l[1:2, :] += weight * (log_prob + TARGET_ENTROPY)

    put_matrix(1, 2, 0)
    for k in range(3):
        put(R_IN + 24 * k, acc_w[k, 0:24, :])
    put(R_HEAD, acc_a[...])
    rowbuf[0:1, :] = acc_c[0, 0:1, :]
    rowbuf[1:2, :] = acc_c[1, 0:1, :]
    for k in range(3):
        rowbuf[2 + k : 3 + k, :] = acc_h[k, HSAC : HSAC + 1, :]
    put(R_OUT, rowbuf[...])
    folded = jnp.sum(acc_l[...], axis=1, keepdims=True)
    rowbuf[...] = jnp.zeros_like(rowbuf)
    rowbuf[0:1, 0:48] = acc_m[0:1, :]
    rowbuf[0:1, 64:65] = folded[0:1]
    rowbuf[0:1, 65:66] = folded[1:2]
    put(R_MISC, rowbuf[...])
    put(R_MISC + 8, jnp.zeros((R_SMALL - R_MISC - 8, HSAC), F32))
    actor_chain[0]()

    def dyn_bias(start, width):
        row = jnp.zeros((1, width), F32)
        for e in range(MEMBERS):
            row = jnp.where(me == e, bias[:, start + width * e : start + width * (e + 1)], row)
        return row

    @pl.when(is_dyn)
    def _():
        w1f[0] = jnp.zeros((32, HSAC), F32)
        w1f[0, 0:IN, 0:HDYN] = rounded(dyn_in[dyn_e])
        for at, piece in enumerate(pieces(dyn_bias(DB1, HDYN))):
            w1f[0, IN + at : IN + at + 1, 0:HDYN] = piece.astype(F32)
        w1t[0] = (0.5 * w1f[0].T).astype(BF16)
        rowbuf[...] = jnp.zeros_like(rowbuf)
        rowbuf[0:1, 0:HDYN] = dyn_bias(DB2, HDYN)
        head_row = dyn_bias(DB3, DOUT)
        rowbuf[1:2, 0:HALF] = head_row[:, 0:HALF]
        rowbuf[1:2, 24 : 24 + HALF] = head_row[:, HALF:DOUT]
        rowbuf[2:3, 0:HALF] = bias[:, MAXLV : MAXLV + HALF]
        rowbuf[3:4, 0:HALF] = bias[:, MINLV : MINLV + HALF]
        dcols[...] = rowbuf[...].T
        wide[0] = jnp.broadcast_to(0.5 * dcols[:, 0:1], (HSAC, 128))
        dpack[...] = jnp.zeros_like(dpack)
        dpack[0:HALF, 0:HDYN] = dyn_out[dyn_e, 0:HALF, :]
        dpack[24 : 24 + HALF, 0:HDYN] = dyn_out[dyn_e, HALF:DOUT, :]
        dhead[...] = dpack[0:48, :].astype(BF16)
        dhead_t[...] = (0.5 * rounded(dpack[0:48, :])).T.astype(BF16)
        dpack[...] = jnp.zeros_like(dpack)

        has_come(dhg.at[pl.ds(0, n_blk - 1)], "dyn h")
        has_come(dmg.at[pl.ds(0, n_blk - 1)], "dyn m")
        dhg[z] = dyn_h[dyn_e]
        dmg[z] = dyn_m[dyn_e]
        dmat[...] = jnp.zeros_like(dmat)
        for block in range(n_blk):
            dmat[block * lay.drows : (block + 1) * lay.drows, 0:HDYN] = 0.5 * rounded(dhg[block])
        w2h[0] = dmat[...].astype(BF16)
        w2t[0] = dmat[...].T.astype(BF16)
        for ref in (dacc_h, dacc_w, dacc_o, dacc_m, dacc_b, dacc_l):
            ref[...] = jnp.zeros_like(ref)

    @pl.loop(0, dyn_tiles)
    def _(tile):
        take(in_dyn, tile)

        @pl.when(is_dyn)
        def _():
            for at in range(per):
                slot = slot_of(tile * per + at)
                xt[:, at * lay.real : (at + 1) * lay.real] = bk[slot, :, 0 : lay.real]
            now = xt[0:24, :]
            later = xt[24:48, :]
            row24 = rows_of((24, DYN_TILE))
            scaled = jnp.where(row24 < IN, (now - centre) * scale, 1.0)
            inputs = jnp.concatenate([scaled, (rows_of((8, DYN_TILE)) < 2).astype(F32)], 0).astype(BF16)
            first, slope1 = gated(dot(w1t[0], inputs))
            second, slope2 = gated(dot(w2t[0], first), wide[0])
            out = dot(dhead[...], second) + dcols[0:48, 1:2]
            used = row24 < HALF
            upper = dcols[0:24, 2:3]
            lower = dcols[0:24, 3:4]
            gap1 = upper - out[24:48]
            gap2 = upper - softplus(gap1) - lower
            log_var = lower + softplus(gap2)
            error = out[0:24] - jnp.where(row24 == OBS, now[23:24], later - now)
            inverse = jnp.exp(-log_var)
            weight = xt[42:43, :] * (xt[43:44, :] == me.astype(F32)).astype(F32)
            spread_term = error * error * inverse
            nll = jnp.sum(jnp.where(used, spread_term + log_var, 0.0), axis=0, keepdims=True)
            dacc_l[0:1, :] += weight * nll
            grad_mu = 2.0 * weight * error * inverse
            grad_lv = weight * (1.0 - spread_term)
            open1 = sigmoid(gap1)
            open2 = sigmoid(gap2)
            grad_lv1 = grad_lv * open2
            dacc_b[0] += jnp.where(used, grad_lv1 * (1.0 - open1), 0.0)
            dacc_b[1] += jnp.where(used, grad_lv * (1.0 - open2), 0.0)
            g3 = jnp.concatenate(
                [jnp.where(used, grad_mu, 0.0), jnp.where(used, grad_lv1 * open1, 0.0)], 0
            ).astype(BF16)
            dacc_o[...] += dot(g3, second, NT)
            dacc_m[...] += dot(ones16(DYN_TILE), g3, NT)
            g2 = sloped(dot(dhead_t[...], g3), slope2)
            dacc_h[...] += dot(jnp.concatenate([first, ones16(DYN_TILE)], 0), g2, NT)
            g1 = sloped(dot(w2h[0], g2), slope1)
            dacc_w[...] += dot(inputs, g1, NT)

    out_of = {"pack": dyn_s, "x": dyn_x}

    def member_copy(name, src, owner, kind, sem, peer):
        return on_plane(src, out_of[name].at[owner], send.at[sent[name, kind]], recv.at[sem], peer)

    def give(name, src):
        like_peers(
            lambda peer: member_copy(name, src, dyn_e, "own", here_at[name, "like"] + dyn_e, peer).start()
        )
        member_copy(name, src, dyn_e, "own", here_at[name, "sibling"], sibling).start()

    def hand_on(name):
        def body(peer):
            @pl.when(peer < MEMBERS)
            def _():
                owner = jnp.minimum(peer, MEMBERS - 1)
                view = out_of[name].at[owner]
                member_copy(name, view, owner, "on", here_at[name, "like"] + owner, sibling).wait_recv()
                member_copy(name, view, owner, "on", here_at[name, "sibling"], sibling).start()

        like_peers(body)

    even, odd = (MEMBERS + 1) // 2, MEMBERS // 2
    handed = even - core * (even - odd) - jnp.where(is_dyn, 1, 0)

    def from_sibling(name):
        for side, number in ((0, odd), (1, even)):
            @pl.when(core == side)
            def _():
                has_come(out_of[name].at[pl.ds(0, number)], (name, "sibling"))

    def gave(name):
        @pl.when(is_dyn)
        def _():
            for begin in range(0, n_dp // 2, MEMBERS):
                number = min(MEMBERS, n_dp // 2 - begin)
                has_sent(out_of[name].at[pl.ds(0, number)], (name, "own"))

        for number in (even, even - 1, even - 2):
            @pl.when(handed == number)
            def _():
                has_sent(out_of[name].at[pl.ds(0, number)], (name, "on"))

    def line_rows(ref):
        rows = ref[0 : lay.drows, 0:HDYN]
        for block in range(1, n_blk):
            rows = jnp.where(z == block, ref[block * lay.drows : (block + 1) * lay.drows, 0:HDYN], rows)
        return rows

    def sac_x_copy(part, src, peer):
        name = ("sac x c", "sac x a")[part]
        dst = sac_x.at[pl.ds(2 * part, 2 - part)]
        return on_plane(src, dst, send.at[sent[name] + peer], recv.at[here_at[name]], peer)

    mine_rows = pl.ds(pl.multiple_of(z * lay.rows, lay.rows), lay.rows)

    def take_matrix(k):
        has_come(mg.at[k, pl.ds(0, n_dp - 1)], ("tiles", k))
        for chunk in range(n_dp):
            tile = chunk * lay.mat
            half, row = tile // 32, tile % 32
            at = slice(row * 8, (row + lay.mat) * 8)
            piece = mg[k, chunk].reshape(lay.mat * 8, 128)
            mat[k, at, half * 128 : (half + 1) * 128] = piece / total
        normalise(mat.at[k])

    @pl.when(is_dyn)
    def _():
        dpack[D_IN : D_IN + 24, :] = dacc_w[0:24, :]
        dpack[D_OUT : D_OUT + HALF, :] = dacc_o[0:HALF, :]
        dpack[D_OUT + HALF : D_OUT + DOUT, :] = dacc_o[24 : 24 + HALF, :]
        dpack[D_B2 : D_B2 + 1, :] = dacc_h[HSAC : HSAC + 1, :]
        dpack[D_B3 : D_B3 + 1, 0:48] = dacc_m[0:1, :]
        lanes = lax.broadcasted_iota(jnp.int32, (24, 128), 1)
        bound = jnp.where(
            lanes == 0,
            jnp.sum(dacc_b[0], axis=1, keepdims=True),
            jnp.where(lanes == 1, jnp.sum(dacc_b[1], axis=1, keepdims=True), 0.0),
        )
        dpack[D_UP : D_UP + 2, 0:24] = bound.T[0:2, :]
        dpack[D_LOSS : D_LOSS + 1, 0:128] = jnp.broadcast_to(
            jnp.sum(dacc_l[0:1, :], axis=1, keepdims=True), (1, 128)
        )
        dpack[D_HID : D_HID + lay.drows, 0:HDYN] = line_rows(dacc_h)
        dyn_s[dyn_e] = dpack[...]
        give("pack", dpack)
        dmat[...] = jnp.zeros_like(dmat)
        for block in range(n_blk):
            at = slice(block * lay.drows, (block + 1) * lay.drows)
            dmat[at, 0:HDYN] = MOMENTUM * dmg[block] + dacc_h[at, 0:HDYN] / total
        normalise(dmat)

    def own_x(part):
        return mat.at[pl.ds(2 * part, 2 - part), mine_rows]

    def passed_x(part):
        return sac_x.at[pl.ds(2 * part, 2 - part)]

    def send_sac(part):
        for k in ((0, 1), (2,))[part]:
            sac_x[k] = mat[k, mine_rows, :]
        like_peers(lambda peer: sac_x_copy(part, own_x(part), peer).start())
        sac_x_copy(part, own_x(part), sibling).start()

    passes_x = jnp.logical_and(core == lay.owner % 2, jnp.logical_not(is_owner))

    def receive_sac(part):
        pl.when(jnp.logical_not(is_owner))(sac_x_copy(part, passed_x(part), sibling).wait_recv)
        pl.when(passes_x)(sac_x_copy(part, passed_x(part), sibling).start)

    def sum_end(step):
        pl.when(step == NS_ITERS - 2)(actor_chain[2])

    @pl.when(is_dyn)
    def _():
        schulz([dmat], NS_ITERS, sum_end)
        rows = line_rows(dmat)
        drow_x[...] = rows
        dyn_x[dyn_e] = rows
        give("x", drow_x)

    @pl.when(is_owner)
    def _():
        for k in range(2):
            take_matrix(k)
        schulz([mat.at[0], mat.at[1]], NS_ITERS, sum_end)
        send_sac(0)

    if n_dp > MEMBERS + 1:
        pl.when(jnp.logical_not(jnp.logical_or(is_dyn, is_owner)))(actor_chain[2])

    def sent_early():
        has_sent(wg.at[pl.ds(0, n_blk - 1), :, half_rows], "hidden")
        has_sent(wg.at[pl.ds(0, n_blk - 1), :, half_rows], "hidden on")
        has_sent(asked.at[pl.ds(0, n_dp - 1)], "lists")
        has_sent(bk.at[pl.ds(0, n_dp - 1)], "own")
        has_sent(bk.at[pl.ds(0, n_blk - 1)], "line")
        has_sent(bk.at[pl.ds(0, (n_dp - 1) * (n_blk - 1))], "plane")

        @pl.when(is_dyn)
        def _():
            has_sent(dhg.at[pl.ds(0, n_blk - 1)], "dyn h")
            has_sent(dmg.at[pl.ds(0, n_blk - 1)], "dyn m")

        for group in range(2):
            has_sent(froms[group].at[pl.ds(0, n_dp - 1)], ("plane sum", group))
        for part in range(3):
            has_sent(line_bytes(part), ("line sum", part))

    @pl.when(is_owner)
    def _():
        take_matrix(2)
        schulz([mat.at[2]], NS_ITERS)
        send_sac(1)

    sent_early()
    hand_on("pack")
    receive_sac(0)
    hand_on("x")
    has_come(small.at[pl.ds(0, (n_dp - 1) * lay.sml)], "small")
    for part in range(2):
        for number, test in ((lay.keepers - 1, is_keeper), (lay.keepers, jnp.logical_not(is_keeper))):
            pl.when(test)(
                functools.partial(has_come, kept_bytes(part, number), ("sac g c", "sac g a")[part])
            )
    from_sibling("pack")
    from_sibling("x")
    receive_sac(1)

    has_sent(small.at[pl.ds(0, (n_dp - 1) * lay.sml)], "small")
    gave("pack")
    gave("x")

    @pl.when(jnp.logical_not(is_owner))
    def _():
        for k in range(3):
            tile_copy(k).wait_send()

    @pl.when(is_keeper)
    def _():
        for part in range(2):
            has_sent(kept_bytes(part, n_dp - 1), ("sac g c", "sac g a")[part])

    for part in range(2):
        @pl.when(is_owner)
        def _():
            like_peers(lambda peer: sac_x_copy(part, own_x(part), peer).wait_send())

        pl.when(is_owner)(sac_x_copy(part, own_x(part), sibling).wait_send)
        pl.when(passes_x)(sac_x_copy(part, passed_x(part), sibling).wait_send)


def adamw(weights, first, second, gradient):
    first = BETA_FIRST * first + (1.0 - BETA_FIRST) * gradient
    second = BETA_SECOND * second + (1.0 - BETA_SECOND) * gradient * gradient
    first_hat = first / (1.0 - BETA_FIRST**STEP)
    second_hat = second / (1.0 - BETA_SECOND**STEP)
    step = first_hat / (jnp.sqrt(second_hat) + 1e-8) + ADAM_DECAY * weights
    return weights - ADAM_RATE * step, first, second


def update_kernel(*refs):
    (
        sac_g, sac_x, dyn_x, dyn_s, small, count, sac_h, dyn_h, dyn_m,
        ci, ci_m, ci_v, ai, ai_m, ai_v, di, di_m, di_v, co, co_m, co_v, ao, ao_m, ao_v,
        do, do_m, do_v, bi, bi_m, bi_v,
        sac_new, sac_mom, dyn_new, dyn_mom, ci_n, ci_mn, ci_vn, ai_n, ai_mn, ai_vn, di_n, di_mn,
        di_vn, co_n, co_mn, co_vn, ao_n, ao_mn, ao_vn, do_n, do_mn, do_vn, bi_n, bi_mn, bi_vn,
        loss, counted, bg,
    ) = refs
    total = count[0:1, 0:1]
    for k in range(3):
        for side in range(2):
            tiles = sac_g[side, k].reshape(sac_mom.shape[1], 128)
            sac_mom[k, :, side * 128 : (side + 1) * 128] = tiles / total
    sac_new[...] = sac_h[...] * (1.0 - MUON_RATE * MUON_DECAY) - MUON_RATE * sac_x[...]
    dyn_rows = dyn_s[:, D_HID : D_HID + dyn_m.shape[1], 0:HDYN]
    dyn_mom[...] = MOMENTUM * dyn_m[...] + dyn_rows / total.reshape(1, 1, 1)
    dyn_new[...] = dyn_h[...] * (1.0 - MUON_RATE * MUON_DECAY) - MUON_RATE * dyn_x[...]

    def rows(row, number):
        sides = []
        for side in range(2):
            at = side * (R_SMALL // 8) + row // 8
            sides.append(small[at : at + -(-number // 8)].reshape(-1, 128))
        return jnp.concatenate(sides, 1)

    def store(outs, at, values):
        for out, value in zip(outs, values):
            out[at] = value

    outs = (ci_n, ci_mn, ci_vn)
    for k in range(2):
        at = (slice(None), k, slice(None))
        grad = rows(R_IN + 24 * k, 24)
        bg[:, CB1 + HSAC * k : CB1 + HSAC * (k + 1)] = grad[IN : IN + 1]
        store(outs, at, adamw(ci[at], ci_m[at], ci_v[at], grad[0:IN] / total))
    grad = rows(R_IN + 48, 24)
    bg[:, AB1 : AB1 + HSAC] = grad[IN : IN + 1]
    store((ai_n, ai_mn, ai_vn), ..., adamw(ai[...], ai_m[...], ai_v[...], grad[0:OBS] / total))
    grad = rows(R_HEAD, 16)
    for at, row in ((slice(0, ACT), slice(1, 1 + ACT)), (slice(ACT, 2 * ACT), slice(9, 9 + ACT))):
        store((ao_n, ao_mn, ao_vn), at, adamw(ao[at], ao_m[at], ao_v[at], grad[row] / total))
    grad = rows(R_OUT, 8)
    store((co_n, co_mn, co_vn), ..., adamw(co[...], co_m[...], co_v[...], grad[0:2] / total))
    bg[:, CB2 : CB2 + HSAC] = grad[2:3]
    bg[:, CB2 + HSAC : CB2 + 2 * HSAC] = grad[3:4]
    bg[:, AB2 : AB2 + HSAC] = grad[4:5]
    grad = rows(R_MISC, 8)
    bg[:, CB3 : CB3 + 1] = grad[0:1, 16:17]
    bg[:, CB3 + 1 : CB3 + 2] = grad[0:1, 32:33]
    bg[:, AB3 : AB3 + ACT] = grad[0:1, 1 : 1 + ACT]
    bg[:, AB3 + ACT : AB3 + 2 * ACT] = grad[0:1, 9 : 9 + ACT]
    bg[:, LOGA : LOGA + 1] = -grad[0:1, 65:66]
    total_loss = grad[0:1, 64:65]
    up = jnp.zeros((1, HALF), F32)
    low = jnp.zeros((1, HALF), F32)
    for e in range(MEMBERS):
        pack = dyn_s[e]
        total_loss = total_loss + pack[D_LOSS : D_LOSS + 1, 0:1]
        up = up + pack[D_UP : D_UP + 1, 0:HALF]
        low = low + pack[D_LOW : D_LOW + 1, 0:HALF]
        bg[:, DB1 + HDYN * e : DB1 + HDYN * (e + 1)] = pack[IN : IN + 1, 0:HDYN]
        bg[:, DB2 + HDYN * e : DB2 + HDYN * (e + 1)] = pack[D_B2 : D_B2 + 1, 0:HDYN]
        bg[:, DB3 + DOUT * e : DB3 + DOUT * e + HALF] = pack[D_B3 : D_B3 + 1, 0:HALF]
        bg[:, DB3 + DOUT * e + HALF : DB3 + DOUT * (e + 1)] = pack[D_B3 : D_B3 + 1, 24 : 24 + HALF]
        grad = pack[0:IN, 0:HDYN] / total
        store((di_n, di_mn, di_vn), e, adamw(di[e], di_m[e], di_v[e], grad))
        grad = pack[D_OUT : D_OUT + DOUT, 0:HDYN] / total
        store((do_n, do_mn, do_vn), e, adamw(do[e], do_m[e], do_v[e], grad))
    bg[:, MAXLV : MAXLV + HALF] = up
    bg[:, MINLV : MINLV + HALF] = low
    lane = lax.broadcasted_iota(jnp.int32, (1, NB), 1)
    bounds = jnp.where(
        jnp.logical_and(lane >= MAXLV, lane < MINLV),
        BOUND_WEIGHT,
        jnp.where(jnp.logical_and(lane >= MINLV, lane < LOGA), -BOUND_WEIGHT, 0.0),
    )
    grad = bg[...] / total + bounds
    flat = [ref[...].reshape(1, NB) for ref in (bi, bi_m, bi_v)]
    store((bi_n, bi_mn, bi_vn), ..., [value.reshape(NB) for value in adamw(*flat, grad)])
    loss[...] = total_loss
    counted[...] = total


def shards(
    lay, replay, model_rows, requests, member_of, model_live, noise, sac_hidden, sac_hidden_mom,
    dyn_hidden, dyn_hidden_mom, crit_in, crit_in_m, crit_in_v, act_in, act_in_m, act_in_v, dyn_in,
    dyn_in_m, dyn_in_v, crit_out, crit_out_m, crit_out_v, act_out, act_out_m, act_out_v, dyn_out,
    dyn_out_m, dyn_out_v, biases, biases_m, biases_v, targ_in, targ_hidden, targ_out, targ_bias,
):
    n_dp, n_blk = lay.n_dp, lay.n_blk
    spec = pl.BlockSpec(memory_space=pltpu.VMEM)

    def flip(value):
        return jnp.transpose(value, (1, 0, 2))

    def swap(value):
        return jnp.swapaxes(value, -1, -2)

    def kept(value):
        return pltpu.with_memory_space_constraint(value, pltpu.VMEM)

    inputs = (
        replay, model_rows, requests, member_of, model_live, jnp.transpose(noise, (2, 0, 1)),
        sac_hidden, sac_hidden_mom, dyn_hidden, dyn_hidden_mom, flip(crit_in), act_in, dyn_in,
        crit_out, swap(act_out), swap(dyn_out), biases, flip(targ_in), targ_hidden, targ_out,
        targ_bias,
    )
    shape = jax.ShapeDtypeStruct
    rows, drows = lay.rows, lay.drows
    out_shape = (
        pltpu.VMEM((2, 3, rows // 8, 8, 128), F32),
        pltpu.VMEM((3, rows, HSAC), F32),
        pltpu.VMEM((MEMBERS, drows, HDYN), F32),
        pltpu.VMEM((MEMBERS, D_ROWS, HSAC), F32),
        pltpu.VMEM((32, 8, 128), F32),
        pltpu.VMEM((8, 128), F32),
    )

    def vm(*dims, kind=F32):
        return pltpu.VMEM(dims, kind)

    scratch = [
        vm(n_blk, 3, rows, HSAC, kind=BF16),
        vm(2, n_dp, CAP, kind=jnp.int32),
        vm(n_dp, 2, n_dp, CAP, kind=jnp.int32),
        vm(n_blk, drows, HDYN),
        vm(n_blk, drows, HDYN),
        vm(lay.n_dev, 48, lay.width),
        vm(56, lay.batch),
        vm(2, 8, lay.batch),
        vm(5, 32, HSAC),
        vm(5, HSAC, 32, kind=BF16),
        vm(2, 16, HSAC, kind=BF16),
        vm(5, HSAC, HSAC, kind=BF16),
        vm(3, HSAC, HSAC, kind=BF16),
        vm(5, 16, HSAC, kind=BF16),
        vm(HSAC, 16, kind=BF16),
        vm(16, HSAC),
        vm(8, HSAC),
        vm(7, HSAC, 128),
        vm(128, 8),
        vm(3, HSAC + 16, HSAC),
        vm(3, 32, HSAC),
        vm(2, 16, HSAC),
        vm(16, HSAC),
        vm(16, 48),
        vm(8, TILE),
        vm(n_dp, lay.chunks[0], 8, 128),
        vm(n_dp, lay.chunks[1], 8, 128),
        vm(n_dp, lay.chunks[0], 8, 128),
        vm(n_dp, lay.chunks[1], 8, 128),
        vm(n_blk, lay.chunks[0], 8, 128),
        vm(n_blk, lay.chunks[1], 8, 128),
        vm(lay.chunks[0], 8, 128),
        vm(lay.chunks[1], 8, 128),
        vm(lay.chunks[0], 8, 128),
        vm(lay.chunks[1], 8, 128),
        vm(3, n_dp, lay.mat, 8, 128),
        vm(3, HSAC, HSAC),
        vm(HSAC, 8),
        vm(HSAC + 16, HSAC),
        vm(32, HSAC),
        vm(48, HSAC),
        vm(16, 48),
        vm(2, 24, DYN_TILE),
        vm(8, DYN_TILE),
        vm(48, DYN_TILE),
        vm(HSAC, HSAC),
        vm(D_ROWS, HSAC),
        vm(drows, HDYN),
        vm(1, NB),
        vm(48, HSAC, kind=BF16),
        vm(HSAC, 48, kind=BF16),
    ]
    scratch += [pltpu.SemaphoreType.DMA((lay.departures,)), pltpu.SemaphoreType.DMA((lay.arrivals,))]
    varying = 4 * (lay.n_dev * 48 * lay.width + 72 * lay.batch + 48 * lay.replay)
    gathered = pl.pallas_call(
        functools.partial(main_kernel, lay),
        out_shape=out_shape,
        in_specs=[spec] * len(inputs),
        out_specs=[spec] * len(out_shape),
        scratch_shapes=scratch,
        compiler_params=pltpu.CompilerParams(
            collective_id=0, has_side_effects=True, vmem_limit_bytes=26 * 2**20 + varying
        ),
        name="step",
    )(*[pltpu.with_memory_space_constraint(value, pltpu.HBM) for value in inputs])
    params = (
        sac_hidden, dyn_hidden, dyn_hidden_mom,
        flip(crit_in), flip(crit_in_m), flip(crit_in_v), act_in, act_in_m, act_in_v,
        dyn_in, dyn_in_m, dyn_in_v, crit_out, crit_out_m, crit_out_v,
        swap(act_out), swap(act_out_m), swap(act_out_v),
        swap(dyn_out), swap(dyn_out_m), swap(dyn_out_v), biases, biases_m, biases_v,
    )
    new_shape = [shape(sac_hidden.shape, F32)] + [shape(value.shape, F32) for value in params]
    new_shape += [shape((1, 1), F32)] * 2
    out = pl.pallas_call(
        update_kernel,
        out_shape=tuple(new_shape),
        in_specs=[spec] * (len(gathered) + len(params)),
        out_specs=[spec] * len(new_shape),
        scratch_shapes=[vm(1, NB)],
        compiler_params=pltpu.CompilerParams(vmem_limit_bytes=16 * 2**20),
        name="update",
    )(*[kept(value) for value in gathered], *params)
    out = list(out)
    for at in (4, 5, 6):
        out[at] = flip(out[at])
    for at in (16, 17, 18, 19, 20, 21):
        out[at] = swap(out[at])
    for at in (25, 26):
        out[at] = out[at].reshape(())
    return tuple(out)


def solution(mesh):
    both = ("dp", "blk")
    sharded = (
        P(None, both), P(None, both), P(both, None), P(both, None), P(both), P(None, both, None),
    )
    hidden = (P(None, "blk", None),) * 4

    def step(replay, model_rows, *others):
        lay = Layout(mesh, replay.shape[1], model_rows.shape[1])
        return shards(lay, replay, model_rows, *others)

    return jax.shard_map(
        step,
        mesh=mesh,
        in_specs=sharded + hidden + (P(),) * 25,
        out_specs=hidden + (P(),) * 23,
        check_vma=False,
    )
```

```python
import functools

import jax
import jax.numpy as jnp
from jax import lax
from jax.experimental import pallas as pl
from jax.experimental.pallas import tpu as pltpu
from jax.sharding import PartitionSpec as P

OBS = 17
ACT = 6
IN = OBS + ACT
FEAT = 42
HDYN = 200
HSAC = 256
MEMBERS = 7
DOUT = 36
HALF = DOUT // 2
NB = 4639
NS_ITERS = 5
STEP = 10
CAP = 8
CRITIC_TILE = 1280
ACTOR_TILE = 640
DYN_TILE = 512
ROWS = 32

DISCOUNT = 0.99
TARGET_ENTROPY = -6.0
BOUND_WEIGHT = 0.01
MOMENTUM = 0.95
MUON_RATE = 0.4
MUON_DECAY = 0.01
ADAM_RATE = 0.1
ADAM_DECAY = 0.01
BETA_FIRST = 0.9
BETA_SECOND = 0.999
COEF_LINEAR = 3.4445
COEF_CUBIC = -4.775
COEF_QUINTIC = 2.0315

CB1, CB2, CB3, AB1, AB2, AB3 = 0, 512, 1024, 1026, 1282, 1538
DB1, DB2, DB3, MAXLV, MINLV, LOGA = 1550, 2950, 4350, 4602, 4620, 4638

R_IN, R_HEAD, R_OUT, R_MISC, R_SMALL = 0, 72, 88, 96, 128
D_IN, D_OUT, D_B2, D_B3, D_UP, D_LOW, D_LOSS, D_HID, D_ROWS = 0, 24, 60, 61, 62, 63, 64, 72, 128

F32, BF16 = jnp.float32, jnp.bfloat16
MESH = pl.DeviceIdType.MESH
NN = (((1,), (0,)), ((), ()))
NT = (((1,), (1,)), ((), ()))


def dot(a, b, dims=NN):
    return lax.dot_general(a, b, dims, preferred_element_type=F32)


def rounded(v):
    return v.astype(BF16).astype(F32)


def pieces(v):
    high = v.astype(BF16)
    rest = v - high.astype(F32)
    middle = rest.astype(BF16)
    return high, middle, (rest - middle.astype(F32)).astype(BF16)


def split(v):
    high = v.astype(BF16)
    return high, (v - high.astype(F32)).astype(BF16)


def product(a, b, dims=NN):
    left = jnp.concatenate([a[0], a[0], a[1]], 1)
    right = jnp.concatenate([b[0], b[1], b[0]], dims[0][1][0])
    half = left.shape[0] // 2
    return jnp.concatenate([dot(left[:half], right, dims), dot(left[half:], right, dims)], 0)


def softplus(v):
    return jnp.maximum(v, 0.0) + jnp.log1p(jnp.exp(-jnp.abs(v)))


def sigmoid(v):
    return 0.5 + 0.5 * jnp.tanh(0.5 * v)


def gate(half):
    up = 1.0 + jnp.tanh(half)
    value = half * up
    return value, up + value * (2.0 - up)


def by_rows(body, *arrays):
    done = [
        body(*[array[at : at + ROWS] for array in arrays]) for at in range(0, arrays[0].shape[0], ROWS)
    ]
    return [jnp.concatenate(parts, 0) for parts in zip(*done)]


def spread_to(column, width):
    return jnp.concatenate([column] * (width // 128), 1)


def gated(half, column=None):
    def body(part, *offset):
        value, slope = gate(part + spread_to(offset[0], part.shape[1]) if offset else part)
        return value.astype(BF16), slope

    return by_rows(body, half, *([] if column is None else [column]))


def sloped(grad, slope):
    return by_rows(lambda part, by: ((part * by).astype(BF16),), grad, slope)[0]


def outer_sloped(column, row, slope):
    return by_rows(lambda part, by: (((spread_to(part, by.shape[1]) * row) * by).astype(BF16),), column, slope)[0]


def rows_of(shape):
    return lax.broadcasted_iota(jnp.int32, shape, 0)


def schulz(refs, steps, before=None):
    @pl.loop(0, steps)
    def _(step):
        if before is not None:
            before(step)
        matrices = [ref[...] for ref in refs]
        parts = [split(matrix) for matrix in matrices]
        grams = [product(part, part, NT) for part in parts]
        halves = [split(gram) for gram in grams]
        squares = [product(half, half) for half in halves]
        blends = [
            split(COEF_CUBIC * gram + COEF_QUINTIC * square) for gram, square in zip(grams, squares)
        ]
        moved = [product(blend, part) for blend, part in zip(blends, parts)]
        for ref, matrix, move in zip(refs, matrices, moved):
            ref[...] = COEF_LINEAR * matrix + move


def normalise(ref):
    moment = ref[...]
    norm = jnp.sqrt(jnp.sum(jnp.sum(moment * moment, axis=1, keepdims=True), axis=0, keepdims=True))
    ref[...] = moment / (norm + 1e-7)


class Layout:
    def __init__(self, mesh, replay, model):
        self.n_dp = mesh.shape["dp"]
        self.n_blk = mesh.shape["blk"]
        self.n_dev = self.n_dp * self.n_blk
        self.replay = replay
        self.model = model
        self.real = self.n_dp * CAP
        self.batch = self.real + model
        self.width = -(-(self.real + 2) // 128) * 128
        self.rows = HSAC // self.n_blk
        self.drows = HDYN // self.n_blk
        self.mat = 64 // self.n_dp
        self.sml = 32 // self.n_dp
        self.chunks = (2 * self.mat, self.mat + self.sml)
        self.owner = self.n_dp - 1

        groups = [("plane sum", g) for g in range(2)] + [("line sum", g) for g in range(3)]
        common = ["hidden", "hidden on", "lists", "own", "line", "plane", "dyn h", "dyn m", "small"]
        common += groups + ["sac g"]
        kinds = [(name, kind) for name in ("pack", "x") for kind in ("own", "on")]
        sent = common + [("tiles", k) for k in range(3)] + kinds
        self.sent = {name: at for at, name in enumerate(sent)}
        self.departures = len(sent)
        self.sent["sac x"] = self.departures
        self.departures += self.n_dp
        self.here, self.arrivals = {}, 0
        tiles = [("tiles", k) for k in range(3)]
        tiles += ["sac x", ("pack", "sibling"), ("x", "sibling")]
        for name in common + tiles:
            self.here[name] = self.arrivals
            self.arrivals += 1
        for name in ("pack", "x"):
            self.here[name, "like"] = self.arrivals
            self.arrivals += MEMBERS
        self.keepers = 2 * (self.rows // 8) // self.mat


def main_kernel(lay, *refs):
    (
        replay, model, requests, member, live, noise, sac_h, sac_m, dyn_h, dyn_m, crit_in, act_in,
        dyn_in, crit_out, act_out, dyn_out, biases, targ_in, targ_hidden, targ_out, targ_bias,
        sac_g, sac_x, dyn_x, dyn_s, small, count,
        wg, lists, asked, dhg, dmg, bk, xs, nz, w1f, w1t, w1n, w2t, w2h, heads, head_t, head_f,
        rowbuf, wide, headcol, acc_h, acc_w, acc_c, acc_a, acc_m, acc_l, grid_c, grid_a, from_c, from_a,
        zr_c, zr_a, zf_c, zf_a, sum_c, sum_a, mg, mat, dcols, dacc_h, dacc_w, dacc_o, dacc_m, dacc_b, dacc_l, xt, dmat,
        dpack, drow_x, bias, dhead, dhead_t, *rest,
    ) = refs
    send, recv = rest
    sent, here_at = lay.sent, lay.here
    grids, froms, zrs, zfs = (grid_c, grid_a), (from_c, from_a), (zr_c, zr_a), (zf_c, zf_a)
    n_dp, n_blk = lay.n_dp, lay.n_blk
    me = lax.axis_index("dp")
    z = lax.axis_index("blk")
    core = lax.rem(me, 2)
    sibling = me + 1 - 2 * core
    is_dyn = me < MEMBERS
    dyn_e = jnp.minimum(me, MEMBERS - 1)
    is_owner = me == lay.owner

    def on_plane(src, dst, ssem, rsem, peer):
        return pltpu.make_async_remote_copy(
            src_ref=src, dst_ref=dst, send_sem=ssem, recv_sem=rsem,
            device_id={"dp": peer}, device_id_type=MESH,
        )

    def on_line(src, dst, ssem, rsem, peer):
        return pltpu.make_async_remote_copy(
            src_ref=src, dst_ref=dst, send_sem=ssem, recv_sem=rsem,
            device_id={"blk": peer}, device_id_type=MESH,
        )

    def over(number, body):
        if number <= 8:
            for off in range(1, number):
                body(off)
        else:
            pl.loop(1, number)(body)

    def plane_peers(body):
        over(n_dp, lambda off: body(lax.rem(me + off, n_dp)))

    def like_peers(body):
        over(n_dp // 2, lambda off: body(lax.rem(me + 2 * off, n_dp)))

    def line_peers(body):
        over(n_blk, lambda off: body(lax.rem(z + off, n_blk)))

    def has_sent(view, name):
        at = send.at[sent[name]]
        on_plane(view, view, at, at, sibling).wait_send()

    def has_come(view, name):
        at = recv.at[here_at[name]]
        on_plane(view, view, at, at, sibling).wait_recv()

    barrier = pltpu.get_barrier_semaphore()
    plane_peers(lambda peer: pl.semaphore_signal(barrier, inc=1, device_id={"dp": peer}, device_id_type=MESH))
    line_peers(lambda peer: pl.semaphore_signal(barrier, inc=1, device_id={"blk": peer}, device_id_type=MESH))
    wg[0] = sac_h[...].astype(BF16)
    lists[0] = requests[...]
    lists[1] = member[...]
    pl.semaphore_wait(barrier, n_dp - 1 + n_blk - 1)

    half_rows = pl.ds(pl.multiple_of(core * (lay.rows // 2), lay.rows // 2), lay.rows // 2)

    def slot_from(owner, at):
        return lax.rem(owner - at + n_blk, n_blk)

    def hidden_copy(peer):
        src = wg.at[0, :, half_rows]
        dst = wg.at[slot_from(z, peer), :, half_rows]
        return on_line(src, dst, send.at[sent["hidden"]], recv.at[here_at["hidden"]], peer)

    def hidden_on():
        view = wg.at[pl.ds(1, n_blk - 1), :, half_rows]
        return on_plane(view, view, send.at[sent["hidden on"]], recv.at[here_at["hidden on"]], sibling)

    def list_copy(peer):
        return on_plane(lists, asked.at[me], send.at[sent["lists"]], recv.at[here_at["lists"]], peer)

    line_peers(lambda peer: hidden_copy(peer).start())
    plane_peers(lambda peer: list_copy(peer).start())
    asked[me] = lists[...]

    def dyn_h_copy(peer):
        return on_line(dyn_h.at[dyn_e], dhg.at[z], send.at[sent["dyn h"]], recv.at[here_at["dyn h"]], peer)

    def dyn_m_copy(peer):
        return on_line(dyn_m.at[dyn_e], dmg.at[z], send.at[sent["dyn m"]], recv.at[here_at["dyn m"]], peer)

    alive = live[...].astype(F32).reshape(1, lay.model)
    bias[...] = biases[...].reshape(1, NB)
    xs[42:56, :] = jnp.zeros((14, lay.batch), F32)
    xs[0:FEAT, lay.real : lay.batch] = model[...]
    xs[42:43, lay.real : lay.batch] = alive
    nz[...] = jnp.zeros_like(nz)
    for which in range(2):
        nz[which, 1:7, :] = noise[:, which, :]
    firsts = [
        (targ_in[:, 0, :], targ_bias[0:1, 0:HSAC]),
        (targ_in[:, 1, :], targ_bias[1:2, 0:HSAC]),
        (crit_in[:, 0, :], bias[:, CB1 : CB1 + HSAC]),
        (crit_in[:, 1, :], bias[:, CB1 + HSAC : CB1 + 2 * HSAC]),
        (act_in[...], bias[:, AB1 : AB1 + HSAC]),
    ]
    w1f[...] = jnp.zeros_like(w1f)
    for net, (weights, offset) in enumerate(firsts):
        w1f[net, 0 : weights.shape[0], :] = rounded(weights)
        for at, piece in enumerate(pieces(offset)):
            w1f[net, IN + at : IN + at + 1, :] = piece.astype(F32)
        w1t[net] = (0.5 * w1f[net].T).astype(BF16)
    for k in range(2):
        w1n[k] = w1f[2 + k, 16:32, :].astype(BF16)
    for net in range(2):
        w2t[net] = (0.5 * rounded(targ_hidden[net])).T.astype(BF16)
    has_come(wg.at[pl.ds(0, n_blk - 1), :, half_rows], "hidden")
    hidden_on().start()

    rowbuf[...] = jnp.zeros_like(rowbuf)
    rowbuf[0:1, :] = targ_bias[0:1, HSAC : 2 * HSAC]
    rowbuf[1:2, :] = targ_bias[1:2, HSAC : 2 * HSAC]
    rowbuf[2:3, :] = bias[:, CB2 : CB2 + HSAC]
    rowbuf[3:4, :] = bias[:, CB2 + HSAC : CB2 + 2 * HSAC]
    rowbuf[4:5, :] = bias[:, AB2 : AB2 + HSAC]
    rowbuf[5:7, :] = rounded(crit_out[...])
    columns = 0.5 * rowbuf[...].T
    for at in range(7):
        wide[at] = jnp.broadcast_to(columns[:, at : at + 1], (HSAC, 128))
    rowbuf[...] = jnp.zeros_like(rowbuf)
    rowbuf[0:1, 1:7] = bias[:, AB3 : AB3 + ACT]
    rowbuf[0:1, 9:15] = bias[:, AB3 + ACT : AB3 + 2 * ACT]
    headcol[...] = rowbuf[:, 0:128].T
    head_f[...] = jnp.zeros_like(head_f)
    for k in range(2):
        head_f[0:1, :] = targ_out[k : k + 1, :]
        heads[k] = head_f[...].astype(BF16)
        head_f[0:1, :] = crit_out[k : k + 1, :]
        heads[2 + k] = head_f[...].astype(BF16)
    head_f[0:1, :] = jnp.zeros((1, HSAC), F32)
    head_f[1:7, :] = act_out[0:ACT, :]
    head_f[9:15, :] = act_out[ACT : 2 * ACT, :]
    heads[4] = head_f[...].astype(BF16)
    head_t[...] = (0.5 * rounded(head_f[...])).T.astype(BF16)
    for ref in (acc_h, acc_w, acc_c, acc_a, acc_m, acc_l):
        ref[...] = jnp.zeros_like(ref)

    data = replay[...]
    sums = jnp.sum(data[0:24], axis=1, keepdims=True)
    squares = jnp.sum(data[0:24] * data[0:24], axis=1, keepdims=True)
    living = jnp.sum(alive, axis=1, keepdims=True)

    has_come(asked.at[pl.ds(0, n_dp - 1)], "lists")
    spread = (
        lax.rem(lax.broadcasted_iota(jnp.int32, (CAP, lay.real), 1), CAP)
        == lax.broadcasted_iota(jnp.int32, (CAP, lay.real), 0)
    ).astype(F32)
    here = (
        lax.broadcasted_iota(jnp.int32, (n_dp, lay.real), 1) // CAP
        == lax.broadcasted_iota(jnp.int32, (n_dp, lay.real), 0)
    )

    def in_lanes(which):
        values = asked[:, which, me, :].astype(F32)
        wide = lax.dot_general(
            values, spread, NN, precision=lax.Precision.HIGHEST, preferred_element_type=F32
        )
        return jnp.sum(jnp.where(here, wide, 0.0), axis=0, keepdims=True)

    slots = in_lanes(0)
    wanted = jnp.maximum(slots, 0.0).astype(jnp.int32)
    hot = (rows_of((lay.replay, lay.real)) == wanted).astype(BF16)
    high, middle, low = pieces(data)
    picked = dot(high, hot) + dot(middle, hot) + dot(low, hot)
    mine = me * n_blk
    bk[mine, 0:FEAT, 0 : lay.real] = picked
    bk[mine, 42:43, 0 : lay.real] = (slots >= 0.0).astype(F32)
    bk[mine, 43:44, 0 : lay.real] = in_lanes(1)
    bk[mine, 44:48, 0 : lay.real] = jnp.zeros((4, lay.real), F32)
    bk[mine, :, lay.real : lay.width] = jnp.zeros((48, lay.width - lay.real), F32)
    bk[mine, 0:24, lay.real : lay.real + 1] = sums
    bk[mine, 0:24, lay.real + 1 : lay.real + 2] = squares
    bk[mine, 24:25, lay.real : lay.real + 1] = living

    def slot_of(block):
        line = lax.rem(block, n_blk)
        return block - line + slot_from(line, z)

    def block_line(peer):
        dst = bk.at[me * n_blk + slot_from(z, peer)]
        return on_line(bk.at[mine], dst, send.at[sent["line"]], recv.at[here_at["line"]], peer)

    def block_own(peer):
        view = bk.at[mine]
        return on_plane(view, view, send.at[sent["own"]], recv.at[here_at["own"]], peer)

    def block_plane(peer):
        view = bk.at[pl.ds(mine + 1, n_blk - 1)]
        return on_plane(view, view, send.at[sent["plane"]], recv.at[here_at["plane"]], peer)

    plane_peers(lambda peer: block_own(peer).start())
    line_peers(lambda peer: block_line(peer).start())

    @pl.when(is_dyn)
    def _():
        line_peers(lambda peer: dyn_h_copy(peer).start())
        line_peers(lambda peer: dyn_m_copy(peer).start())

    has_come(wg.at[pl.ds(0, n_blk - 1), :, half_rows], "hidden on")
    for k in range(3):
        for block in range(n_blk):
            w2h[k, block * lay.rows : (block + 1) * lay.rows, :] = (
                0.5 * wg[slot_from(block, z), k].astype(F32)
            ).astype(BF16)
        w2t[2 + k] = w2h[k].astype(F32).T.astype(BF16)

    log_alpha = bias[:, LOGA : LOGA + 1]
    alpha = jnp.exp(log_alpha)
    last = [
        targ_bias[0:1, 2 * HSAC : 2 * HSAC + 1],
        targ_bias[1:2, 2 * HSAC : 2 * HSAC + 1],
        bias[:, CB3 : CB3 + 1],
        bias[:, CB3 + 1 : CB3 + 2],
    ]
    critic_tiles = lay.batch // CRITIC_TILE
    actor_tiles = lay.batch // ACTOR_TILE

    def act_rows(width):
        row8 = rows_of((8, width))
        return jnp.logical_and(row8 >= 1, row8 < 1 + ACT)

    def place_of(step, width):
        return pl.ds(pl.multiple_of(lax.rem(step + 1, lay.batch // width) * width, width), width)

    def ones16(width):
        return jnp.ones((16, width), BF16)

    def framed(first_row, used, where):
        row32 = rows_of((32, where.size))
        ones3 = jnp.logical_and(row32 >= IN, row32 < IN + 3).astype(F32)
        return jnp.where(row32 < used, xs[first_row : first_row + 32, where], ones3)

    def hidden(inputs, net):
        first, slope1 = gated(dot(w1t[net], inputs))
        second, slope2 = gated(dot(w2t[net], first), wide[net])
        return first, slope1, second, slope2

    def policy(inputs, which, where):
        first, slope1, second, slope2 = hidden(inputs, 4)
        out = dot(heads[4], second) + headcol[0:16, 0:1]
        bent = jnp.tanh(out[8:16])
        log_scale = -5.0 + 3.5 * (bent + 1.0)
        draw = nz[which, :, where]
        moved = jnp.exp(log_scale) * draw
        latent = out[0:8] + moved
        terms = (
            -0.5 * draw * draw
            - log_scale
            - 0.9189385
            - 2.0 * (0.6931472 - latent - softplus(-2.0 * latent))
        )
        used = act_rows(where.size)
        log_prob = jnp.sum(jnp.where(used, terms, 0.0), axis=0, keepdims=True)
        action = jnp.where(used, jnp.tanh(latent), 0.0)
        return action, log_prob, bent, moved, (first, slope1, second, slope2)

    def with_action(inputs, action):
        middle_rows = jnp.where(act_rows(action.shape[1]), action, inputs[16:24])
        return jnp.concatenate([inputs[0:16], middle_rows, inputs[24:32]], 0).astype(BF16)

    def critic(inputs, net):
        kept = hidden(inputs, net)
        value = dot(heads[net], kept[2])[0:1] + last[net]
        return value, kept

    def add_hidden(k, first, grad):
        acc_h[k] += dot(jnp.concatenate([first, ones16(grad.shape[1])], 0), grad, NT)

    has_come(bk.at[pl.ds(0, n_blk - 1)], "line")
    plane_peers(lambda peer: block_plane(peer).start())

    @pl.loop(0, critic_tiles)
    def _(step):
        @pl.when(step == critic_tiles - 1)
        def _():
            has_come(bk.at[pl.ds(0, n_dp - 1)], "own")
            lanes = lax.broadcasted_iota(jnp.int32, (48, lay.width), 1) // CAP

            def gather(owner, total):
                turned = pltpu.roll(
                    bk[owner * n_blk], lax.rem((owner - me) * CAP + lay.width, lay.width), axis=1
                )
                return jnp.where(lanes == owner, turned, total)

            own = lax.fori_loop(0, n_dp, gather, jnp.zeros((48, lay.width), F32))
            xs[0:48, 0 : lay.real] = own[:, 0 : lay.real]

        where = place_of(step, CRITIC_TILE)
        now_in = framed(0, IN, where).astype(BF16)
        next_f = framed(24, OBS, where)
        reward = xs[23:24, where]
        done = xs[41:42, where]
        weight = xs[42:43, where]
        row16 = rows_of((16, CRITIC_TILE))
        next_action, next_prob, _, _, _ = policy(next_f.astype(BF16), 1, where)
        aim_in = with_action(next_f, next_action)
        aim = jnp.minimum(critic(aim_in, 0)[0], critic(aim_in, 1)[0])
        target = reward + DISCOUNT * (1.0 - done) * (aim - alpha * next_prob)
        loss = jnp.zeros((1, CRITIC_TILE), F32)
        heads_grad = []
        for k in range(2):
            value, (c1, dc1, c2, dc2) = critic(now_in, 2 + k)
            miss = value - target
            loss += 0.5 * miss * miss
            g3 = rounded(weight * miss)
            g3_rows = jnp.where(row16 == 0, g3, 0.0).astype(BF16)
            heads_grad.append(g3_rows)
            acc_c[k] += dot(g3_rows, c2, NT)
            g2 = outer_sloped(wide[5 + k], g3, dc2)
            add_hidden(k, c1, g2)
            g1 = sloped(dot(w2h[k], g2), dc1)
            acc_w[k] += dot(now_in, g1, NT)
        acc_m[:, 16:48] += dot(ones16(CRITIC_TILE), jnp.concatenate(heads_grad, 0), NT)
        acc_l[0:1, 0:CRITIC_TILE] += weight * loss

    def put_matrix(group, k, at):
        for chunk in range(n_dp):
            tile = chunk * lay.mat
            side, row = tile // 32, tile % 32
            grids[group][chunk, at * lay.mat : (at + 1) * lay.mat] = acc_h[
                k, row * 8 : (row + lay.mat) * 8, side * 128 : (side + 1) * 128
            ].reshape(lay.mat, 8, 128)

    def put(row, value):
        for at in range(value.shape[0] // 8):
            for side in range(value.shape[1] // 128):
                tile = side * (R_SMALL // 8) + row // 8 + at
                grid_a[tile // lay.sml, lay.mat + tile % lay.sml] = value[
                    at * 8 : at * 8 + 8, side * 128 : (side + 1) * 128
                ]

    def plane_sum(group, peer):
        name = ("plane sum", group)
        return on_plane(
            grids[group].at[peer], froms[group].at[me], send.at[sent[name]], recv.at[here_at[name]], peer
        )

    def line_part(part):
        group = min(part, 1)
        tiles = (pl.ds(0, 2 * lay.mat), pl.ds(0, lay.mat), pl.ds(lay.mat, lay.sml))[part]
        return group, tiles

    def line_sum(part, peer):
        group, tiles = line_part(part)
        name = ("line sum", part)
        src, dst = zfs[group].at[tiles], zrs[group].at[z, tiles]
        return on_line(src, dst, send.at[sent[name]], recv.at[here_at[name]], peer)

    def line_bytes(part):
        group, tiles = line_part(part)
        return zrs[group].at[pl.ds(0, n_blk - 1), tiles]

    first_tile = me * lay.mat
    side = first_tile // 32
    row_tile = lax.rem(first_tile, 32)
    keeper_z = row_tile * 8 // lay.rows
    local_tile = row_tile - keeper_z * (lay.rows // 8)
    is_keeper = z == keeper_z

    def fold_plane(group):
        has_come(froms[group].at[pl.ds(0, n_dp - 1)], ("plane sum", group))
        froms[group][me] = grids[group][me]
        whole = froms[group][0]
        for at in range(1, n_dp):
            whole = whole + froms[group][at]
        zfs[group][...] = whole

        @pl.when(is_keeper)
        def _():
            held_rows = pl.ds(pl.multiple_of(local_tile * 8, 8), lay.mat * 8)
            held_lanes = pl.ds(pl.multiple_of(side * 128, 128), 128)
            for at, k in enumerate(((0, 1), (2,))[group]):
                old = sac_m[k, held_rows, held_lanes].reshape(lay.mat, 8, 128)
                zfs[group][at * lay.mat : (at + 1) * lay.mat] += (MOMENTUM * total).reshape(1, 1, 1) * old

        for part in (0,) if group == 0 else (1, 2):
            line_peers(lambda peer: line_sum(part, peer).start())

    def tile_copy(k, peer):
        src = (sum_c, sum_a)[k // 2].at[pl.ds((k % 2) * lay.mat, lay.mat)]
        return on_plane(src, mg.at[k, me], send.at[sent["tiles", k]], recv.at[here_at["tiles", k]], peer)

    def small_copy(peer):
        return on_plane(
            sum_a.at[pl.ds(lay.mat, lay.sml)], small.at[pl.ds(me * lay.sml, lay.sml)],
            send.at[sent["small"]], recv.at[here_at["small"]], peer,
        )

    def keep_copy(peer):
        view = sac_g.at[side, pl.ds(0, 2), pl.ds(local_tile, lay.mat)]
        return on_plane(view, view, send.at[sent["sac g"]], recv.at[here_at["sac g"]], peer)

    def kept_bytes(number):
        return froms[0].at[pl.ds(0, number)]

    def fold_end(part):
        group, tiles = line_part(part)
        has_come(line_bytes(part), ("line sum", part))
        zrs[group][z, tiles] = zfs[group][tiles]
        whole = zrs[group][0, tiles]
        for block in range(1, n_blk):
            whole = whole + zrs[group][block, tiles]
        (sum_c, sum_a)[group][tiles] = whole
        if part == 0:
            for k in range(2):
                pl.when(jnp.logical_not(is_owner))(tile_copy(k, lay.owner).start)

                @pl.when(is_owner)
                def _():
                    mg[k, me] = whole[k * lay.mat : (k + 1) * lay.mat]

            @pl.when(is_keeper)
            def _():
                for k in range(2):
                    sac_g[side, k, pl.ds(local_tile, lay.mat)] = whole[k * lay.mat : (k + 1) * lay.mat]
                plane_peers(lambda peer: keep_copy(peer).start())

        if part == 1:
            plane_peers(lambda peer: tile_copy(2, peer).start())
            mg[2, me] = whole

        if part == 2:
            plane_peers(lambda peer: small_copy(peer).start())
            small[pl.ds(me * lay.sml, lay.sml)] = sum_a[lay.mat :]

    def chain(group):
        def end():
            for part in (0,) if group == 0 else (1, 2):
                fold_end(part)

        return [
            lambda: plane_peers(lambda peer: plane_sum(group, peer).start()),
            lambda: fold_plane(group),
            end,
        ]

    critic_chain, actor_chain = chain(0), chain(1)
    per = DYN_TILE // lay.real
    dyn_tiles = lay.n_dev // per
    in_actor, in_dyn = {}, {}
    if actor_tiles > 1:
        in_actor[1] = [critic_chain[1]]
        in_dyn[0] = [critic_chain[2]]
    else:
        in_dyn[0] = [critic_chain[1]]
        in_dyn[min(1, dyn_tiles - 1)] = [critic_chain[2]]
    in_dyn.setdefault(dyn_tiles - 1, []).append(actor_chain[1])

    def take(slots, step):
        for at, events in slots.items():
            @pl.when(step == at)
            def _():
                for event in events:
                    event()

    for k in range(2):
        put_matrix(0, k, k)
    critic_chain[0]()

    has_come(bk.at[pl.ds(0, (n_dp - 1) * (n_blk - 1))], "plane")
    lane0 = lay.real // 128 * 128

    def add_block(at, carry):
        sides, fills = carry
        slot = slot_of(at)
        return sides + bk[slot, 0:32, lane0 : lane0 + 128], fills + bk[slot, 40:48, 0 : lay.real]

    sides, fills = lax.fori_loop(
        0, lay.n_dev, add_block, (jnp.zeros((32, 128), F32), jnp.zeros((8, lay.real), F32))
    )
    at = lay.real - lane0
    rows_all = float(lay.replay * lay.n_dev)
    centre = sides[0:24, at : at + 1] / rows_all
    scale = lax.rsqrt(sides[0:24, at + 1 : at + 2] / rows_all - centre * centre + 1e-6)
    total = sides[24:25, at : at + 1] + jnp.sum(fills[2:3, :], axis=1, keepdims=True)
    count[...] = jnp.broadcast_to(total, (8, 128))

    @pl.loop(0, actor_tiles)
    def _(step):
        take(in_actor, step)
        where = place_of(step, ACTOR_TILE)
        now_f = framed(0, IN, where)
        now_in = now_f.astype(BF16)
        weight = xs[42:43, where]
        action, log_prob, bent, moved, (a1, da1, a2, da2) = policy(now_in, 0, where)
        judged_in = with_action(now_f, action)
        loss = alpha * log_prob - log_alpha * (log_prob + TARGET_ENTROPY)
        grad_action = jnp.zeros((8, ACTOR_TILE), F32)
        used = act_rows(ACTOR_TILE)
        for k in range(2):
            judged, (_, df1, _, df2) = critic(judged_in, 2 + k)
            loss -= 0.5 * judged
            g2 = outer_sloped(wide[5 + k], -0.5 * weight, df2)
            g1 = sloped(dot(w2h[k], g2), df1)
            grad_action += dot(w1n[k], g1)[0:8]
        grad_latent = 2.0 * alpha * weight * action + grad_action * (1.0 - action * action)
        grad_scale = grad_latent * moved - alpha * weight
        grad_bent = grad_scale * 3.5 * (1.0 - bent * bent)
        g3 = jnp.concatenate(
            [jnp.where(used, grad_latent, 0.0), jnp.where(used, grad_bent, 0.0)], 0
        ).astype(BF16)
        acc_a[...] += dot(g3, a2, NT)
        acc_m[:, 0:16] += dot(ones16(ACTOR_TILE), g3, NT)
        g2 = sloped(dot(head_t[...], g3), da2)
        add_hidden(2, a1, g2)
        g1 = sloped(dot(w2h[2], g2), da1)
        acc_w[2] += dot(now_in, g1, NT)
        acc_l[1:2, 0:ACTOR_TILE] += weight * loss
        acc_l[2:3, 0:ACTOR_TILE] += weight * (log_prob + TARGET_ENTROPY)

    put_matrix(1, 2, 0)
    for k in range(3):
        put(R_IN + 24 * k, acc_w[k, 0:24, :])
    put(R_HEAD, acc_a[...])
    rowbuf[0:1, :] = acc_c[0, 0:1, :]
    rowbuf[1:2, :] = acc_c[1, 0:1, :]
    for k in range(3):
        rowbuf[2 + k : 3 + k, :] = acc_h[k, HSAC : HSAC + 1, :]
    put(R_OUT, rowbuf[...])
    folded = jnp.sum(acc_l[...], axis=1, keepdims=True)
    rowbuf[...] = jnp.zeros_like(rowbuf)
    rowbuf[0:1, 0:48] = acc_m[0:1, :]
    rowbuf[0:1, 64:65] = folded[0:1] + folded[1:2]
    rowbuf[0:1, 65:66] = folded[2:3]
    put(R_MISC, rowbuf[...])
    put(R_MISC + 8, jnp.zeros((R_SMALL - R_MISC - 8, HSAC), F32))
    actor_chain[0]()

    def dyn_bias(start, width):
        row = jnp.zeros((1, width), F32)
        for e in range(MEMBERS):
            row = jnp.where(me == e, bias[:, start + width * e : start + width * (e + 1)], row)
        return row

    @pl.when(is_dyn)
    def _():
        w1f[0] = jnp.zeros((32, HSAC), F32)
        w1f[0, 0:IN, 0:HDYN] = rounded(dyn_in[dyn_e])
        for at, piece in enumerate(pieces(dyn_bias(DB1, HDYN))):
            w1f[0, IN + at : IN + at + 1, 0:HDYN] = piece.astype(F32)
        w1t[0] = (0.5 * w1f[0].T).astype(BF16)
        rowbuf[...] = jnp.zeros_like(rowbuf)
        rowbuf[0:1, 0:HDYN] = dyn_bias(DB2, HDYN)
        head_row = dyn_bias(DB3, DOUT)
        rowbuf[1:2, 0:HALF] = head_row[:, 0:HALF]
        rowbuf[1:2, 24 : 24 + HALF] = head_row[:, HALF:DOUT]
        rowbuf[2:3, 0:HALF] = bias[:, MAXLV : MAXLV + HALF]
        rowbuf[3:4, 0:HALF] = bias[:, MINLV : MINLV + HALF]
        dcols[...] = rowbuf[...].T
        wide[0] = jnp.broadcast_to(0.5 * dcols[:, 0:1], (HSAC, 128))
        dpack[...] = jnp.zeros_like(dpack)
        dpack[0:HALF, 0:HDYN] = dyn_out[dyn_e, 0:HALF, :]
        dpack[24 : 24 + HALF, 0:HDYN] = dyn_out[dyn_e, HALF:DOUT, :]
        dhead[...] = dpack[0:48, :].astype(BF16)
        dhead_t[...] = (0.5 * rounded(dpack[0:48, :])).T.astype(BF16)
        dpack[...] = jnp.zeros_like(dpack)

        has_come(dhg.at[pl.ds(0, n_blk - 1)], "dyn h")
        has_come(dmg.at[pl.ds(0, n_blk - 1)], "dyn m")
        dhg[z] = dyn_h[dyn_e]
        dmg[z] = dyn_m[dyn_e]
        dmat[...] = jnp.zeros_like(dmat)
        for block in range(n_blk):
            dmat[block * lay.drows : (block + 1) * lay.drows, 0:HDYN] = 0.5 * rounded(dhg[block])
        w2h[0] = dmat[...].astype(BF16)
        w2t[0] = dmat[...].T.astype(BF16)
        for ref in (dacc_h, dacc_w, dacc_o, dacc_m, dacc_b, dacc_l):
            ref[...] = jnp.zeros_like(ref)

    @pl.loop(0, dyn_tiles)
    def _(tile):
        take(in_dyn, tile)

        @pl.when(is_dyn)
        def _():
            for at in range(per):
                slot = slot_of(tile * per + at)
                xt[:, at * lay.real : (at + 1) * lay.real] = bk[slot, :, 0 : lay.real]
            now = xt[0:24, :]
            later = xt[24:48, :]
            row24 = rows_of((24, DYN_TILE))
            scaled = jnp.where(row24 < IN, (now - centre) * scale, 1.0)
            inputs = jnp.concatenate([scaled, (rows_of((8, DYN_TILE)) < 2).astype(F32)], 0).astype(BF16)
            first, slope1 = gated(dot(w1t[0], inputs))
            second, slope2 = gated(dot(w2t[0], first), wide[0])
            out = dot(dhead[...], second) + dcols[0:48, 1:2]
            used = row24 < HALF
            upper = dcols[0:24, 2:3]
            lower = dcols[0:24, 3:4]
            gap1 = upper - out[24:48]
            gap2 = upper - softplus(gap1) - lower
            log_var = lower + softplus(gap2)
            error = out[0:24] - jnp.where(row24 == OBS, now[23:24], later - now)
            inverse = jnp.exp(-log_var)
            weight = xt[42:43, :] * (xt[43:44, :] == me.astype(F32)).astype(F32)
            spread_term = error * error * inverse
            nll = jnp.sum(jnp.where(used, spread_term + log_var, 0.0), axis=0, keepdims=True)
            dacc_l[0:1, :] += weight * nll
            grad_mu = 2.0 * weight * error * inverse
            grad_lv = weight * (1.0 - spread_term)
            open1 = sigmoid(gap1)
            open2 = sigmoid(gap2)
            grad_lv1 = grad_lv * open2
            dacc_b[0] += jnp.where(used, grad_lv1 * (1.0 - open1), 0.0)
            dacc_b[1] += jnp.where(used, grad_lv * (1.0 - open2), 0.0)
            g3 = jnp.concatenate(
                [jnp.where(used, grad_mu, 0.0), jnp.where(used, grad_lv1 * open1, 0.0)], 0
            ).astype(BF16)
            dacc_o[...] += dot(g3, second, NT)
            dacc_m[...] += dot(ones16(DYN_TILE), g3, NT)
            g2 = sloped(dot(dhead_t[...], g3), slope2)
            dacc_h[...] += dot(jnp.concatenate([first, ones16(DYN_TILE)], 0), g2, NT)
            g1 = sloped(dot(w2h[0], g2), slope1)
            dacc_w[...] += dot(inputs, g1, NT)

    out_of = {"pack": dyn_s, "x": dyn_x}

    def member_copy(name, src, owner, kind, sem, peer):
        return on_plane(src, out_of[name].at[owner], send.at[sent[name, kind]], recv.at[sem], peer)

    def give(name, src):
        like_peers(
            lambda peer: member_copy(name, src, dyn_e, "own", here_at[name, "like"] + dyn_e, peer).start()
        )
        member_copy(name, src, dyn_e, "own", here_at[name, "sibling"], sibling).start()

    def hand_on(name):
        def body(peer):
            @pl.when(peer < MEMBERS)
            def _():
                owner = jnp.minimum(peer, MEMBERS - 1)
                view = out_of[name].at[owner]
                member_copy(name, view, owner, "on", here_at[name, "like"] + owner, sibling).wait_recv()
                member_copy(name, view, owner, "on", here_at[name, "sibling"], sibling).start()

        like_peers(body)

    even, odd = (MEMBERS + 1) // 2, MEMBERS // 2
    handed = even - core * (even - odd) - jnp.where(is_dyn, 1, 0)

    def from_sibling(name):
        for side, number in ((0, odd), (1, even)):
            @pl.when(core == side)
            def _():
                has_come(out_of[name].at[pl.ds(0, number)], (name, "sibling"))

    def gave(name):
        @pl.when(is_dyn)
        def _():
            for begin in range(0, n_dp // 2, MEMBERS):
                number = min(MEMBERS, n_dp // 2 - begin)
                has_sent(out_of[name].at[pl.ds(0, number)], (name, "own"))

        for number in (even, even - 1, even - 2):
            @pl.when(handed == number)
            def _():
                has_sent(out_of[name].at[pl.ds(0, number)], (name, "on"))

    def line_rows(ref):
        rows = ref[0 : lay.drows, 0:HDYN]
        for block in range(1, n_blk):
            rows = jnp.where(z == block, ref[block * lay.drows : (block + 1) * lay.drows, 0:HDYN], rows)
        return rows

    def sac_x_copy(src, peer):
        dst = sac_x.at[pl.ds(0, 2)]
        return on_plane(src, dst, send.at[sent["sac x"] + peer], recv.at[here_at["sac x"]], peer)

    mine_rows = pl.ds(pl.multiple_of(z * lay.rows, lay.rows), lay.rows)

    def take_matrix(k):
        has_come(mg.at[k, pl.ds(0, n_dp - 1)], ("tiles", k))
        for chunk in range(n_dp):
            tile = chunk * lay.mat
            half, row = tile // 32, tile % 32
            at = slice(row * 8, (row + lay.mat) * 8)
            piece = mg[k, chunk].reshape(lay.mat * 8, 128)
            mat[k, at, half * 128 : (half + 1) * 128] = piece / total
        normalise(mat.at[k])

    @pl.when(is_dyn)
    def _():
        dpack[D_IN : D_IN + 24, :] = dacc_w[0:24, :]
        dpack[D_OUT : D_OUT + HALF, :] = dacc_o[0:HALF, :]
        dpack[D_OUT + HALF : D_OUT + DOUT, :] = dacc_o[24 : 24 + HALF, :]
        dpack[D_B2 : D_B2 + 1, :] = dacc_h[HSAC : HSAC + 1, :]
        dpack[D_B3 : D_B3 + 1, 0:48] = dacc_m[0:1, :]
        lanes = lax.broadcasted_iota(jnp.int32, (24, 128), 1)
        bound = jnp.where(
            lanes == 0,
            jnp.sum(dacc_b[0], axis=1, keepdims=True),
            jnp.where(lanes == 1, jnp.sum(dacc_b[1], axis=1, keepdims=True), 0.0),
        )
        dpack[D_UP : D_UP + 2, 0:24] = bound.T[0:2, :]
        dpack[D_LOSS : D_LOSS + 1, 0:128] = jnp.broadcast_to(
            jnp.sum(dacc_l[0:1, :], axis=1, keepdims=True), (1, 128)
        )
        dpack[D_HID : D_HID + lay.drows, 0:HDYN] = line_rows(dacc_h)
        dyn_s[dyn_e] = dpack[...]
        give("pack", dpack)
        dmat[...] = jnp.zeros_like(dmat)
        for block in range(n_blk):
            at = slice(block * lay.drows, (block + 1) * lay.drows)
            dmat[at, 0:HDYN] = MOMENTUM * dmg[block] + dacc_h[at, 0:HDYN] / total
        normalise(dmat)

    own_x, passed_x = mat.at[pl.ds(0, 2), mine_rows], sac_x.at[pl.ds(0, 2)]
    passes_x = jnp.logical_and(core == lay.owner % 2, jnp.logical_not(is_owner))

    def sum_end(step):
        pl.when(step == NS_ITERS - 2)(actor_chain[2])

    @pl.when(is_dyn)
    def _():
        schulz([dmat], NS_ITERS, sum_end)
        rows = line_rows(dmat)
        drow_x[...] = rows
        dyn_x[dyn_e] = rows
        give("x", drow_x)

    @pl.when(is_owner)
    def _():
        for k in range(2):
            take_matrix(k)
        schulz([mat.at[0], mat.at[1]], NS_ITERS, sum_end)
        for k in range(2):
            sac_x[k] = mat[k, mine_rows, :]
        like_peers(lambda peer: sac_x_copy(own_x, peer).start())
        sac_x_copy(own_x, sibling).start()

    if n_dp > MEMBERS + 1:
        pl.when(jnp.logical_not(jnp.logical_or(is_dyn, is_owner)))(actor_chain[2])

    def sent_early():
        has_sent(wg.at[pl.ds(0, n_blk - 1), :, half_rows], "hidden")
        has_sent(wg.at[pl.ds(0, n_blk - 1), :, half_rows], "hidden on")
        has_sent(asked.at[pl.ds(0, n_dp - 1)], "lists")
        has_sent(bk.at[pl.ds(0, n_dp - 1)], "own")
        has_sent(bk.at[pl.ds(0, n_blk - 1)], "line")
        has_sent(bk.at[pl.ds(0, (n_dp - 1) * (n_blk - 1))], "plane")

        @pl.when(is_dyn)
        def _():
            has_sent(dhg.at[pl.ds(0, n_blk - 1)], "dyn h")
            has_sent(dmg.at[pl.ds(0, n_blk - 1)], "dyn m")

        for group in range(2):
            has_sent(froms[group].at[pl.ds(0, n_dp - 1)], ("plane sum", group))
        for part in range(3):
            has_sent(line_bytes(part), ("line sum", part))

    def pass_on(step):
        @pl.when(step == 2)
        def _():
            hand_on("pack")
            hand_on("x")
            pl.when(jnp.logical_not(is_owner))(sac_x_copy(passed_x, sibling).wait_recv)
            pl.when(passes_x)(sac_x_copy(passed_x, sibling).start)

    take_matrix(2)
    for half in range(2):
        for piece in range(lay.rows // 8 // lay.mat):
            chunk = (half * 32 + z * (lay.rows // 8)) // lay.mat + piece
            sac_g[half, 2, piece * lay.mat : (piece + 1) * lay.mat] = mg[2, chunk]
    schulz([mat.at[2]], NS_ITERS, pass_on)
    sac_x[2] = mat[2, mine_rows, :]

    sent_early()
    has_come(small.at[pl.ds(0, (n_dp - 1) * lay.sml)], "small")
    for number, test in ((lay.keepers - 1, is_keeper), (lay.keepers, jnp.logical_not(is_keeper))):
        pl.when(test)(functools.partial(has_come, kept_bytes(number), "sac g"))
    from_sibling("pack")
    from_sibling("x")

    has_sent(small.at[pl.ds(0, (n_dp - 1) * lay.sml)], "small")
    gave("pack")
    gave("x")

    has_sent(mg.at[2, pl.ds(0, n_dp - 1)], ("tiles", 2))

    @pl.when(jnp.logical_not(is_owner))
    def _():
        for k in range(2):
            tile_copy(k, sibling).wait_send()

    pl.when(is_keeper)(functools.partial(has_sent, kept_bytes(n_dp - 1), "sac g"))

    @pl.when(is_owner)
    def _():
        like_peers(lambda peer: sac_x_copy(own_x, peer).wait_send())
        sac_x_copy(own_x, sibling).wait_send()

    pl.when(passes_x)(sac_x_copy(passed_x, sibling).wait_send)


def adamw(weights, first, second, gradient):
    first = BETA_FIRST * first + (1.0 - BETA_FIRST) * gradient
    second = BETA_SECOND * second + (1.0 - BETA_SECOND) * gradient * gradient
    first_hat = first / (1.0 - BETA_FIRST**STEP)
    second_hat = second / (1.0 - BETA_SECOND**STEP)
    step = first_hat / (jnp.sqrt(second_hat) + 1e-8) + ADAM_DECAY * weights
    return weights - ADAM_RATE * step, first, second


def update_kernel(*refs):
    (
        sac_g, sac_x, dyn_x, dyn_s, small, count, sac_h, dyn_h, dyn_m,
        ci, ci_m, ci_v, ai, ai_m, ai_v, di, di_m, di_v, co, co_m, co_v, ao, ao_m, ao_v,
        do, do_m, do_v, bi, bi_m, bi_v,
        sac_new, sac_mom, dyn_new, dyn_mom, ci_n, ci_mn, ci_vn, ai_n, ai_mn, ai_vn, di_n, di_mn,
        di_vn, co_n, co_mn, co_vn, ao_n, ao_mn, ao_vn, do_n, do_mn, do_vn, bi_n, bi_mn, bi_vn,
        loss, counted, bg,
    ) = refs
    total = count[0:1, 0:1]
    for k in range(3):
        for side in range(2):
            tiles = sac_g[side, k].reshape(sac_mom.shape[1], 128)
            sac_mom[k, :, side * 128 : (side + 1) * 128] = tiles / total
    sac_new[...] = sac_h[...] * (1.0 - MUON_RATE * MUON_DECAY) - MUON_RATE * sac_x[...]
    dyn_rows = dyn_s[:, D_HID : D_HID + dyn_m.shape[1], 0:HDYN]
    dyn_mom[...] = MOMENTUM * dyn_m[...] + dyn_rows / total.reshape(1, 1, 1)
    dyn_new[...] = dyn_h[...] * (1.0 - MUON_RATE * MUON_DECAY) - MUON_RATE * dyn_x[...]

    def rows(row, number):
        sides = []
        for side in range(2):
            at = side * (R_SMALL // 8) + row // 8
            sides.append(small[at : at + -(-number // 8)].reshape(-1, 128))
        return jnp.concatenate(sides, 1)

    def store(outs, at, values):
        for out, value in zip(outs, values):
            out[at] = value

    outs = (ci_n, ci_mn, ci_vn)
    for k in range(2):
        at = (slice(None), k, slice(None))
        grad = rows(R_IN + 24 * k, 24)
        bg[:, CB1 + HSAC * k : CB1 + HSAC * (k + 1)] = grad[IN : IN + 1]
        store(outs, at, adamw(ci[at], ci_m[at], ci_v[at], grad[0:IN] / total))
    grad = rows(R_IN + 48, 24)
    bg[:, AB1 : AB1 + HSAC] = grad[IN : IN + 1]
    store((ai_n, ai_mn, ai_vn), ..., adamw(ai[...], ai_m[...], ai_v[...], grad[0:OBS] / total))
    grad = rows(R_HEAD, 16)
    for at, row in ((slice(0, ACT), slice(1, 1 + ACT)), (slice(ACT, 2 * ACT), slice(9, 9 + ACT))):
        store((ao_n, ao_mn, ao_vn), at, adamw(ao[at], ao_m[at], ao_v[at], grad[row] / total))
    grad = rows(R_OUT, 8)
    store((co_n, co_mn, co_vn), ..., adamw(co[...], co_m[...], co_v[...], grad[0:2] / total))
    bg[:, CB2 : CB2 + HSAC] = grad[2:3]
    bg[:, CB2 + HSAC : CB2 + 2 * HSAC] = grad[3:4]
    bg[:, AB2 : AB2 + HSAC] = grad[4:5]
    grad = rows(R_MISC, 8)
    bg[:, CB3 : CB3 + 1] = grad[0:1, 16:17]
    bg[:, CB3 + 1 : CB3 + 2] = grad[0:1, 32:33]
    bg[:, AB3 : AB3 + ACT] = grad[0:1, 1 : 1 + ACT]
    bg[:, AB3 + ACT : AB3 + 2 * ACT] = grad[0:1, 9 : 9 + ACT]
    bg[:, LOGA : LOGA + 1] = -grad[0:1, 65:66]
    total_loss = grad[0:1, 64:65]
    up = jnp.zeros((1, HALF), F32)
    low = jnp.zeros((1, HALF), F32)
    for e in range(MEMBERS):
        pack = dyn_s[e]
        total_loss = total_loss + pack[D_LOSS : D_LOSS + 1, 0:1]
        up = up + pack[D_UP : D_UP + 1, 0:HALF]
        low = low + pack[D_LOW : D_LOW + 1, 0:HALF]
        bg[:, DB1 + HDYN * e : DB1 + HDYN * (e + 1)] = pack[IN : IN + 1, 0:HDYN]
        bg[:, DB2 + HDYN * e : DB2 + HDYN * (e + 1)] = pack[D_B2 : D_B2 + 1, 0:HDYN]
        bg[:, DB3 + DOUT * e : DB3 + DOUT * e + HALF] = pack[D_B3 : D_B3 + 1, 0:HALF]
        bg[:, DB3 + DOUT * e + HALF : DB3 + DOUT * (e + 1)] = pack[D_B3 : D_B3 + 1, 24 : 24 + HALF]
        grad = pack[0:IN, 0:HDYN] / total
        store((di_n, di_mn, di_vn), e, adamw(di[e], di_m[e], di_v[e], grad))
        grad = pack[D_OUT : D_OUT + DOUT, 0:HDYN] / total
        store((do_n, do_mn, do_vn), e, adamw(do[e], do_m[e], do_v[e], grad))
    bg[:, MAXLV : MAXLV + HALF] = up
    bg[:, MINLV : MINLV + HALF] = low
    lane = lax.broadcasted_iota(jnp.int32, (1, NB), 1)
    bounds = jnp.where(
        jnp.logical_and(lane >= MAXLV, lane < MINLV),
        BOUND_WEIGHT,
        jnp.where(jnp.logical_and(lane >= MINLV, lane < LOGA), -BOUND_WEIGHT, 0.0),
    )
    grad = bg[...] / total + bounds
    flat = [ref[...].reshape(1, NB) for ref in (bi, bi_m, bi_v)]
    store((bi_n, bi_mn, bi_vn), ..., [value.reshape(NB) for value in adamw(*flat, grad)])
    loss[...] = total_loss
    counted[...] = total


def shards(
    lay, replay, model_rows, requests, member_of, model_live, noise, sac_hidden, sac_hidden_mom,
    dyn_hidden, dyn_hidden_mom, crit_in, crit_in_m, crit_in_v, act_in, act_in_m, act_in_v, dyn_in,
    dyn_in_m, dyn_in_v, crit_out, crit_out_m, crit_out_v, act_out, act_out_m, act_out_v, dyn_out,
    dyn_out_m, dyn_out_v, biases, biases_m, biases_v, targ_in, targ_hidden, targ_out, targ_bias,
):
    n_dp, n_blk = lay.n_dp, lay.n_blk
    spec = pl.BlockSpec(memory_space=pltpu.VMEM)

    def flip(value):
        return jnp.transpose(value, (1, 0, 2))

    def swap(value):
        return jnp.swapaxes(value, -1, -2)

    def kept(value):
        return pltpu.with_memory_space_constraint(value, pltpu.VMEM)

    inputs = (
        replay, model_rows, requests, member_of, model_live, jnp.transpose(noise, (2, 0, 1)),
        sac_hidden, sac_hidden_mom, dyn_hidden, dyn_hidden_mom, flip(crit_in), act_in, dyn_in,
        crit_out, swap(act_out), swap(dyn_out), biases, flip(targ_in), targ_hidden, targ_out,
        targ_bias,
    )
    shape = jax.ShapeDtypeStruct
    rows, drows = lay.rows, lay.drows
    out_shape = (
        pltpu.VMEM((2, 3, rows // 8, 8, 128), F32),
        pltpu.VMEM((3, rows, HSAC), F32),
        pltpu.VMEM((MEMBERS, drows, HDYN), F32),
        pltpu.VMEM((MEMBERS, D_ROWS, HSAC), F32),
        pltpu.VMEM((32, 8, 128), F32),
        pltpu.VMEM((8, 128), F32),
    )

    def vm(*dims, kind=F32):
        return pltpu.VMEM(dims, kind)

    scratch = [
        vm(n_blk, 3, rows, HSAC, kind=BF16),
        vm(2, n_dp, CAP, kind=jnp.int32),
        vm(n_dp, 2, n_dp, CAP, kind=jnp.int32),
        vm(n_blk, drows, HDYN),
        vm(n_blk, drows, HDYN),
        vm(lay.n_dev, 48, lay.width),
        vm(56, lay.batch),
        vm(2, 8, lay.batch),
        vm(5, 32, HSAC),
        vm(5, HSAC, 32, kind=BF16),
        vm(2, 16, HSAC, kind=BF16),
        vm(5, HSAC, HSAC, kind=BF16),
        vm(3, HSAC, HSAC, kind=BF16),
        vm(5, 16, HSAC, kind=BF16),
        vm(HSAC, 16, kind=BF16),
        vm(16, HSAC),
        vm(8, HSAC),
        vm(7, HSAC, 128),
        vm(128, 8),
        vm(3, HSAC + 16, HSAC),
        vm(3, 32, HSAC),
        vm(2, 16, HSAC),
        vm(16, HSAC),
        vm(16, 48),
        vm(8, max(CRITIC_TILE, ACTOR_TILE)),
        vm(n_dp, lay.chunks[0], 8, 128),
        vm(n_dp, lay.chunks[1], 8, 128),
        vm(n_dp, lay.chunks[0], 8, 128),
        vm(n_dp, lay.chunks[1], 8, 128),
        vm(n_blk, lay.chunks[0], 8, 128),
        vm(n_blk, lay.chunks[1], 8, 128),
        vm(lay.chunks[0], 8, 128),
        vm(lay.chunks[1], 8, 128),
        vm(lay.chunks[0], 8, 128),
        vm(lay.chunks[1], 8, 128),
        vm(3, n_dp, lay.mat, 8, 128),
        vm(3, HSAC, HSAC),
        vm(HSAC, 8),
        vm(HSAC + 16, HSAC),
        vm(32, HSAC),
        vm(48, HSAC),
        vm(16, 48),
        vm(2, 24, DYN_TILE),
        vm(8, DYN_TILE),
        vm(48, DYN_TILE),
        vm(HSAC, HSAC),
        vm(D_ROWS, HSAC),
        vm(drows, HDYN),
        vm(1, NB),
        vm(48, HSAC, kind=BF16),
        vm(HSAC, 48, kind=BF16),
    ]
    scratch += [pltpu.SemaphoreType.DMA((lay.departures,)), pltpu.SemaphoreType.DMA((lay.arrivals,))]
    varying = 4 * (lay.n_dev * 48 * lay.width + 72 * lay.batch + 48 * lay.replay)
    gathered = pl.pallas_call(
        functools.partial(main_kernel, lay),
        out_shape=out_shape,
        in_specs=[spec] * len(inputs),
        out_specs=[spec] * len(out_shape),
        scratch_shapes=scratch,
        compiler_params=pltpu.CompilerParams(
            collective_id=0, has_side_effects=True, vmem_limit_bytes=26 * 2**20 + varying
        ),
        name="step",
    )(*[pltpu.with_memory_space_constraint(value, pltpu.HBM) for value in inputs])
    params = (
        sac_hidden, dyn_hidden, dyn_hidden_mom,
        flip(crit_in), flip(crit_in_m), flip(crit_in_v), act_in, act_in_m, act_in_v,
        dyn_in, dyn_in_m, dyn_in_v, crit_out, crit_out_m, crit_out_v,
        swap(act_out), swap(act_out_m), swap(act_out_v),
        swap(dyn_out), swap(dyn_out_m), swap(dyn_out_v), biases, biases_m, biases_v,
    )
    new_shape = [shape(sac_hidden.shape, F32)] + [shape(value.shape, F32) for value in params]
    new_shape += [shape((1, 1), F32)] * 2
    out = pl.pallas_call(
        update_kernel,
        out_shape=tuple(new_shape),
        in_specs=[spec] * (len(gathered) + len(params)),
        out_specs=[spec] * len(new_shape),
        scratch_shapes=[vm(1, NB)],
        compiler_params=pltpu.CompilerParams(vmem_limit_bytes=16 * 2**20),
        name="update",
    )(*[kept(value) for value in gathered], *params)
    out = list(out)
    for at in (4, 5, 6):
        out[at] = flip(out[at])
    for at in (16, 17, 18, 19, 20, 21):
        out[at] = swap(out[at])
    for at in (25, 26):
        out[at] = out[at].reshape(())
    return tuple(out)


def solution(mesh):
    both = ("dp", "blk")
    sharded = (
        P(None, both), P(None, both), P(both, None), P(both, None), P(both), P(None, both, None),
    )
    hidden = (P(None, "blk", None),) * 4

    def step(replay, model_rows, *others):
        lay = Layout(mesh, replay.shape[1], model_rows.shape[1])
        return shards(lay, replay, model_rows, *others)

    return jax.shard_map(
        step,
        mesh=mesh,
        in_specs=sharded + hidden + (P(),) * 25,
        out_specs=hidden + (P(),) * 23,
        check_vma=False,
    )
```

```python
import functools

import jax
import jax.numpy as jnp
from jax import lax
from jax.experimental import pallas as pl
from jax.experimental.pallas import tpu as pltpu
from jax.sharding import PartitionSpec as P

OBS = 17
ACT = 6
IN = OBS + ACT
FEAT = 42
HDYN = 200
HSAC = 256
MEMBERS = 7
DOUT = 36
HALF = DOUT // 2
NB = 4639
NS_ITERS = 5
STEP = 10
CAP = 8
CRITIC_TILE = 1280
ACTOR_TILE = 640
DYN_TILE = 512
ROWS = 32

DISCOUNT = 0.99
TARGET_ENTROPY = -6.0
BOUND_WEIGHT = 0.01
MOMENTUM = 0.95
MUON_RATE = 0.4
MUON_DECAY = 0.01
ADAM_RATE = 0.1
ADAM_DECAY = 0.01
BETA_FIRST = 0.9
BETA_SECOND = 0.999
COEF_LINEAR = 3.4445
COEF_CUBIC = -4.775
COEF_QUINTIC = 2.0315

CB1, CB2, CB3, AB1, AB2, AB3 = 0, 512, 1024, 1026, 1282, 1538
DB1, DB2, DB3, MAXLV, MINLV, LOGA = 1550, 2950, 4350, 4602, 4620, 4638

R_IN, R_HEAD, R_OUT, R_MISC, R_SMALL = 0, 72, 88, 96, 128
D_IN, D_OUT, D_B2, D_B3, D_UP, D_LOW, D_LOSS, D_HID, D_ROWS = 0, 24, 60, 61, 62, 63, 64, 72, 128

F32, BF16 = jnp.float32, jnp.bfloat16
MESH = pl.DeviceIdType.MESH
NN = (((1,), (0,)), ((), ()))
NT = (((1,), (1,)), ((), ()))


def dot(a, b, dims=NN):
    return lax.dot_general(a, b, dims, preferred_element_type=F32)


def rounded(v):
    return v.astype(BF16).astype(F32)


def pieces(v):
    high = v.astype(BF16)
    rest = v - high.astype(F32)
    middle = rest.astype(BF16)
    return high, middle, (rest - middle.astype(F32)).astype(BF16)


def split(v):
    high = v.astype(BF16)
    return high, (v - high.astype(F32)).astype(BF16)


def product(a, b, dims=NN):
    left = jnp.concatenate([a[0], a[0], a[1]], 1)
    right = jnp.concatenate([b[0], b[1], b[0]], dims[0][1][0])
    half = left.shape[0] // 2
    return jnp.concatenate([dot(left[:half], right, dims), dot(left[half:], right, dims)], 0)


def softplus(v):
    return jnp.maximum(v, 0.0) + jnp.log1p(jnp.exp(-jnp.abs(v)))


def sigmoid(v):
    return 0.5 + 0.5 * jnp.tanh(0.5 * v)


def gate(half):
    up = 1.0 + jnp.tanh(half)
    value = half * up
    return value, up + value * (2.0 - up)


def by_rows(body, *arrays):
    done = [
        body(*[array[at : at + ROWS] for array in arrays]) for at in range(0, arrays[0].shape[0], ROWS)
    ]
    return [jnp.concatenate(parts, 0) for parts in zip(*done)]


def spread_to(column, width):
    return jnp.concatenate([column] * (width // 128), 1)


def gated(half, column=None):
    def body(part, *offset):
        value, slope = gate(part + spread_to(offset[0], part.shape[1]) if offset else part)
        return value.astype(BF16), slope

    return by_rows(body, half, *([] if column is None else [column]))


def sloped(grad, slope):
    return by_rows(lambda part, by: ((part * by).astype(BF16),), grad, slope)[0]


def outer_sloped(column, row, slope):
    return by_rows(lambda part, by: (((spread_to(part, by.shape[1]) * row) * by).astype(BF16),), column, slope)[0]


def rows_of(shape):
    return lax.broadcasted_iota(jnp.int32, shape, 0)


def schulz(refs, steps, before=None):
    @pl.loop(0, steps)
    def _(step):
        if before is not None:
            before(step)
        matrices = [ref[...] for ref in refs]
        parts = [split(matrix) for matrix in matrices]
        grams = [product(part, part, NT) for part in parts]
        halves = [split(gram) for gram in grams]
        squares = [product(half, half) for half in halves]
        blends = [
            split(COEF_CUBIC * gram + COEF_QUINTIC * square) for gram, square in zip(grams, squares)
        ]
        moved = [product(blend, part) for blend, part in zip(blends, parts)]
        for ref, matrix, move in zip(refs, matrices, moved):
            ref[...] = COEF_LINEAR * matrix + move


def normalise(ref):
    moment = ref[...]
    norm = jnp.sqrt(jnp.sum(jnp.sum(moment * moment, axis=1, keepdims=True), axis=0, keepdims=True))
    ref[...] = moment / (norm + 1e-7)


class Layout:
    def __init__(self, mesh, replay, model):
        self.n_dp = mesh.shape["dp"]
        self.n_blk = mesh.shape["blk"]
        self.n_dev = self.n_dp * self.n_blk
        self.replay = replay
        self.model = model
        self.real = self.n_dp * CAP
        self.batch = self.real + model
        self.width = -(-(self.real + 2) // 128) * 128
        self.rows = HSAC // self.n_blk
        self.drows = HDYN // self.n_blk
        self.mat = 64 // self.n_dp
        self.sml = 32 // self.n_dp
        self.chunks = (self.mat, self.mat, self.mat + self.sml)
        self.owner = self.n_dp - 1

        groups = [("plane sum", g) for g in range(3)] + [("line sum", g) for g in range(4)]
        common = ["hidden", "hidden on", "lists", "own", "line", "plane", "dyn h", "dyn m", "small"]
        common += groups + [("sac g", k) for k in range(2)]
        kinds = [(name, kind) for name in ("pack", "x") for kind in ("own", "on")]
        sent = common + [("tiles", k) for k in range(3)] + kinds
        self.sent = {name: at for at, name in enumerate(sent)}
        self.departures = len(sent)
        for k in range(2):
            self.sent["sac x", k] = self.departures
            self.departures += self.n_dp
        self.here, self.arrivals = {}, 0
        tiles = [("tiles", k) for k in range(3)]
        tiles += [("sac x", 0), ("sac x", 1), ("pack", "sibling"), ("x", "sibling")]
        for name in common + tiles:
            self.here[name] = self.arrivals
            self.arrivals += 1
        for name in ("pack", "x"):
            self.here[name, "like"] = self.arrivals
            self.arrivals += MEMBERS
        self.keepers = 2 * (self.rows // 8) // self.mat


def main_kernel(lay, *refs):
    (
        replay, model, requests, member, live, noise, sac_h, sac_m, dyn_h, dyn_m, crit_in, act_in,
        dyn_in, crit_out, act_out, dyn_out, biases, targ_in, targ_hidden, targ_out, targ_bias,
        sac_g, sac_x, dyn_x, dyn_s, small, count,
        wg, lists, asked, dhg, dmg, bk, xs, nz, w1f, w1t, w1n, w2t, w2h, heads, head_t, head_f,
        rowbuf, wide, headcol, acc_h, acc_w, acc_c, acc_a, acc_m, acc_l, grid_0, grid_1, grid_a, from_0, from_1,
        from_a, zr_0, zr_1, zr_a, zf_0, zf_1, zf_a, sum_0, sum_1, sum_a, ys, mg, mat, dcols, dacc_h, dacc_w, dacc_o, dacc_m, dacc_b, dacc_l, xt, dmat,
        dpack, drow_x, bias, dhead, dhead_t, *rest,
    ) = refs
    send, recv = rest
    sent, here_at = lay.sent, lay.here
    grids, froms = (grid_0, grid_1, grid_a), (from_0, from_1, from_a)
    zrs, zfs, totals = (zr_0, zr_1, zr_a), (zf_0, zf_1, zf_a), (sum_0, sum_1, sum_a)
    n_dp, n_blk = lay.n_dp, lay.n_blk
    me = lax.axis_index("dp")
    z = lax.axis_index("blk")
    core = lax.rem(me, 2)
    sibling = me + 1 - 2 * core
    is_dyn = me < MEMBERS
    dyn_e = jnp.minimum(me, MEMBERS - 1)
    is_owner = me == lay.owner

    def on_plane(src, dst, ssem, rsem, peer):
        return pltpu.make_async_remote_copy(
            src_ref=src, dst_ref=dst, send_sem=ssem, recv_sem=rsem,
            device_id={"dp": peer}, device_id_type=MESH,
        )

    def on_line(src, dst, ssem, rsem, peer):
        return pltpu.make_async_remote_copy(
            src_ref=src, dst_ref=dst, send_sem=ssem, recv_sem=rsem,
            device_id={"blk": peer}, device_id_type=MESH,
        )

    def over(number, body):
        if number <= 8:
            for off in range(1, number):
                body(off)
        else:
            pl.loop(1, number)(body)

    def plane_peers(body):
        over(n_dp, lambda off: body(lax.rem(me + off, n_dp)))

    def like_peers(body):
        over(n_dp // 2, lambda off: body(lax.rem(me + 2 * off, n_dp)))

    def line_peers(body):
        over(n_blk, lambda off: body(lax.rem(z + off, n_blk)))

    def has_sent(view, name):
        at = send.at[sent[name]]
        on_plane(view, view, at, at, sibling).wait_send()

    def has_come(view, name):
        at = recv.at[here_at[name]]
        on_plane(view, view, at, at, sibling).wait_recv()

    barrier = pltpu.get_barrier_semaphore()
    plane_peers(lambda peer: pl.semaphore_signal(barrier, inc=1, device_id={"dp": peer}, device_id_type=MESH))
    line_peers(lambda peer: pl.semaphore_signal(barrier, inc=1, device_id={"blk": peer}, device_id_type=MESH))
    wg[0] = sac_h[...].astype(BF16)
    lists[0] = requests[...]
    lists[1] = member[...]
    pl.semaphore_wait(barrier, n_dp - 1 + n_blk - 1)

    half_rows = pl.ds(pl.multiple_of(core * (lay.rows // 2), lay.rows // 2), lay.rows // 2)

    def slot_from(owner, at):
        return lax.rem(owner - at + n_blk, n_blk)

    def hidden_copy(peer):
        src = wg.at[0, :, half_rows]
        dst = wg.at[slot_from(z, peer), :, half_rows]
        return on_line(src, dst, send.at[sent["hidden"]], recv.at[here_at["hidden"]], peer)

    def hidden_on():
        view = wg.at[pl.ds(1, n_blk - 1), :, half_rows]
        return on_plane(view, view, send.at[sent["hidden on"]], recv.at[here_at["hidden on"]], sibling)

    def list_copy(peer):
        return on_plane(lists, asked.at[me], send.at[sent["lists"]], recv.at[here_at["lists"]], peer)

    line_peers(lambda peer: hidden_copy(peer).start())
    plane_peers(lambda peer: list_copy(peer).start())
    asked[me] = lists[...]

    def dyn_h_copy(peer):
        return on_line(dyn_h.at[dyn_e], dhg.at[z], send.at[sent["dyn h"]], recv.at[here_at["dyn h"]], peer)

    def dyn_m_copy(peer):
        return on_line(dyn_m.at[dyn_e], dmg.at[z], send.at[sent["dyn m"]], recv.at[here_at["dyn m"]], peer)

    alive = live[...].astype(F32).reshape(1, lay.model)
    bias[...] = biases[...].reshape(1, NB)
    xs[42:56, :] = jnp.zeros((14, lay.batch), F32)
    xs[0:FEAT, lay.real : lay.batch] = model[...]
    xs[42:43, lay.real : lay.batch] = alive
    nz[...] = jnp.zeros_like(nz)
    for which in range(2):
        nz[which, 1:7, :] = noise[:, which, :]
    firsts = [
        (targ_in[:, 0, :], targ_bias[0:1, 0:HSAC]),
        (targ_in[:, 1, :], targ_bias[1:2, 0:HSAC]),
        (crit_in[:, 0, :], bias[:, CB1 : CB1 + HSAC]),
        (crit_in[:, 1, :], bias[:, CB1 + HSAC : CB1 + 2 * HSAC]),
        (act_in[...], bias[:, AB1 : AB1 + HSAC]),
    ]
    w1f[...] = jnp.zeros_like(w1f)
    for net, (weights, offset) in enumerate(firsts):
        w1f[net, 0 : weights.shape[0], :] = rounded(weights)
        for at, piece in enumerate(pieces(offset)):
            w1f[net, IN + at : IN + at + 1, :] = piece.astype(F32)
        w1t[net] = (0.5 * w1f[net].T).astype(BF16)
    for k in range(2):
        w1n[k] = w1f[2 + k, 16:32, :].astype(BF16)
    for net in range(2):
        w2t[net] = (0.5 * rounded(targ_hidden[net])).T.astype(BF16)
    has_come(wg.at[pl.ds(0, n_blk - 1), :, half_rows], "hidden")
    hidden_on().start()

    rowbuf[...] = jnp.zeros_like(rowbuf)
    rowbuf[0:1, :] = targ_bias[0:1, HSAC : 2 * HSAC]
    rowbuf[1:2, :] = targ_bias[1:2, HSAC : 2 * HSAC]
    rowbuf[2:3, :] = bias[:, CB2 : CB2 + HSAC]
    rowbuf[3:4, :] = bias[:, CB2 + HSAC : CB2 + 2 * HSAC]
    rowbuf[4:5, :] = bias[:, AB2 : AB2 + HSAC]
    rowbuf[5:7, :] = rounded(crit_out[...])
    columns = 0.5 * rowbuf[...].T
    for at in range(7):
        wide[at] = jnp.broadcast_to(columns[:, at : at + 1], (HSAC, 128))
    rowbuf[...] = jnp.zeros_like(rowbuf)
    rowbuf[0:1, 1:7] = bias[:, AB3 : AB3 + ACT]
    rowbuf[0:1, 9:15] = bias[:, AB3 + ACT : AB3 + 2 * ACT]
    headcol[...] = rowbuf[:, 0:128].T
    head_f[...] = jnp.zeros_like(head_f)
    for k in range(2):
        head_f[0:1, :] = targ_out[k : k + 1, :]
        heads[k] = head_f[...].astype(BF16)
        head_f[0:1, :] = crit_out[k : k + 1, :]
        heads[2 + k] = head_f[...].astype(BF16)
    head_f[0:1, :] = jnp.zeros((1, HSAC), F32)
    head_f[1:7, :] = act_out[0:ACT, :]
    head_f[9:15, :] = act_out[ACT : 2 * ACT, :]
    heads[4] = head_f[...].astype(BF16)
    head_t[...] = (0.5 * rounded(head_f[...])).T.astype(BF16)
    for ref in (acc_h, acc_w, acc_c, acc_a, acc_m, acc_l):
        ref[...] = jnp.zeros_like(ref)

    data = replay[...]
    sums = jnp.sum(data[0:24], axis=1, keepdims=True)
    squares = jnp.sum(data[0:24] * data[0:24], axis=1, keepdims=True)
    living = jnp.sum(alive, axis=1, keepdims=True)

    has_come(asked.at[pl.ds(0, n_dp - 1)], "lists")
    spread = (
        lax.rem(lax.broadcasted_iota(jnp.int32, (CAP, lay.real), 1), CAP)
        == lax.broadcasted_iota(jnp.int32, (CAP, lay.real), 0)
    ).astype(F32)
    here = (
        lax.broadcasted_iota(jnp.int32, (n_dp, lay.real), 1) // CAP
        == lax.broadcasted_iota(jnp.int32, (n_dp, lay.real), 0)
    )

    def in_lanes(which):
        values = asked[:, which, me, :].astype(F32)
        wide = lax.dot_general(
            values, spread, NN, precision=lax.Precision.HIGHEST, preferred_element_type=F32
        )
        return jnp.sum(jnp.where(here, wide, 0.0), axis=0, keepdims=True)

    slots = in_lanes(0)
    wanted = jnp.maximum(slots, 0.0).astype(jnp.int32)
    hot = (rows_of((lay.replay, lay.real)) == wanted).astype(BF16)
    padded = jnp.concatenate([data[0:40], jnp.zeros((8, lay.replay), F32)], 0)
    tail = jnp.concatenate([data[40:FEAT], jnp.zeros((14, lay.replay), F32)], 0)
    parts = [jnp.concatenate(pair, 0) for pair in zip(pieces(padded), pieces(tail))]
    chosen = dot(jnp.concatenate(parts, 0), hot)
    chosen = chosen[0:64] + chosen[64:128] + chosen[128:192]
    mine = me * n_blk
    bk[mine, 0:40, 0 : lay.real] = chosen[0:40]
    bk[mine, 40:FEAT, 0 : lay.real] = chosen[48:50]
    bk[mine, 42:43, 0 : lay.real] = (slots >= 0.0).astype(F32)
    bk[mine, 43:44, 0 : lay.real] = in_lanes(1)
    bk[mine, 44:48, 0 : lay.real] = jnp.zeros((4, lay.real), F32)
    bk[mine, :, lay.real : lay.width] = jnp.zeros((48, lay.width - lay.real), F32)
    bk[mine, 0:24, lay.real : lay.real + 1] = sums
    bk[mine, 0:24, lay.real + 1 : lay.real + 2] = squares
    bk[mine, 24:25, lay.real : lay.real + 1] = living

    def slot_of(block):
        line = lax.rem(block, n_blk)
        return block - line + slot_from(line, z)

    def block_line(peer):
        dst = bk.at[me * n_blk + slot_from(z, peer)]
        return on_line(bk.at[mine], dst, send.at[sent["line"]], recv.at[here_at["line"]], peer)

    def block_own(peer):
        view = bk.at[mine]
        return on_plane(view, view, send.at[sent["own"]], recv.at[here_at["own"]], peer)

    def block_plane(peer):
        view = bk.at[pl.ds(mine + 1, n_blk - 1)]
        return on_plane(view, view, send.at[sent["plane"]], recv.at[here_at["plane"]], peer)

    plane_peers(lambda peer: block_own(peer).start())
    line_peers(lambda peer: block_line(peer).start())

    @pl.when(is_dyn)
    def _():
        line_peers(lambda peer: dyn_h_copy(peer).start())
        line_peers(lambda peer: dyn_m_copy(peer).start())

    has_come(wg.at[pl.ds(0, n_blk - 1), :, half_rows], "hidden on")
    for k in range(3):
        for block in range(n_blk):
            w2h[k, block * lay.rows : (block + 1) * lay.rows, :] = (
                0.5 * wg[slot_from(block, z), k].astype(F32)
            ).astype(BF16)
        w2t[2 + k] = w2h[k].astype(F32).T.astype(BF16)

    log_alpha = bias[:, LOGA : LOGA + 1]
    alpha = jnp.exp(log_alpha)
    last = [
        targ_bias[0:1, 2 * HSAC : 2 * HSAC + 1],
        targ_bias[1:2, 2 * HSAC : 2 * HSAC + 1],
        bias[:, CB3 : CB3 + 1],
        bias[:, CB3 + 1 : CB3 + 2],
    ]
    critic_tiles = lay.batch // CRITIC_TILE
    actor_tiles = lay.batch // ACTOR_TILE

    def act_rows(width):
        row8 = rows_of((8, width))
        return jnp.logical_and(row8 >= 1, row8 < 1 + ACT)

    def place_of(step, width):
        return pl.ds(pl.multiple_of(lax.rem(step + 1, lay.batch // width) * width, width), width)

    def ones16(width):
        return jnp.ones((16, width), BF16)

    def framed(first_row, used, where):
        row32 = rows_of((32, where.size))
        ones3 = jnp.logical_and(row32 >= IN, row32 < IN + 3).astype(F32)
        return jnp.where(row32 < used, xs[first_row : first_row + 32, where], ones3)

    def hidden(inputs, net):
        first, slope1 = gated(dot(w1t[net], inputs))
        second, slope2 = gated(dot(w2t[net], first), wide[net])
        return first, slope1, second, slope2

    def policy(inputs, which, where):
        first, slope1, second, slope2 = hidden(inputs, 4)
        out = dot(heads[4], second) + headcol[0:16, 0:1]
        bent = jnp.tanh(out[8:16])
        log_scale = -5.0 + 3.5 * (bent + 1.0)
        draw = nz[which, :, where]
        moved = jnp.exp(log_scale) * draw
        latent = out[0:8] + moved
        terms = (
            -0.5 * draw * draw
            - log_scale
            - 0.9189385
            - 2.0 * (0.6931472 - latent - softplus(-2.0 * latent))
        )
        used = act_rows(where.size)
        log_prob = jnp.sum(jnp.where(used, terms, 0.0), axis=0, keepdims=True)
        action = jnp.where(used, jnp.tanh(latent), 0.0)
        return action, log_prob, bent, moved, (first, slope1, second, slope2)

    def with_action(inputs, action):
        middle_rows = jnp.where(act_rows(action.shape[1]), action, inputs[16:24])
        return jnp.concatenate([inputs[0:16], middle_rows, inputs[24:32]], 0).astype(BF16)

    def critic(inputs, net):
        kept = hidden(inputs, net)
        value = dot(heads[net], kept[2])[0:1] + last[net]
        return value, kept

    def add_hidden(k, first, grad):
        acc_h[k] += dot(jnp.concatenate([first, ones16(grad.shape[1])], 0), grad, NT)

    has_come(bk.at[pl.ds(0, n_blk - 1)], "line")
    plane_peers(lambda peer: block_plane(peer).start())

    def critic_pass(k, now_in, where, target):
        weight = xs[42:43, where]
        value, (c1, dc1, c2, dc2) = critic(now_in, 2 + k)
        miss = value - target
        g3 = rounded(weight * miss)
        g3_rows = jnp.where(rows_of((16, CRITIC_TILE)) == 0, g3, 0.0).astype(BF16)
        acc_c[k] += dot(g3_rows, c2, NT)
        acc_m[:, 16 + 16 * k : 32 + 16 * k] += dot(ones16(CRITIC_TILE), g3_rows, NT)
        g2 = outer_sloped(wide[5 + k], g3, dc2)
        add_hidden(k, c1, g2)
        g1 = sloped(dot(w2h[k], g2), dc1)
        acc_w[k] += dot(now_in, g1, NT)
        acc_l[0:1, 0:CRITIC_TILE] += weight * (0.5 * miss * miss)

    @pl.loop(0, critic_tiles)
    def _(step):
        @pl.when(step == critic_tiles - 1)
        def _():
            has_come(bk.at[pl.ds(0, n_dp - 1)], "own")
            lanes = lax.broadcasted_iota(jnp.int32, (48, lay.width), 1) // CAP

            def gather(owner, total):
                turned = pltpu.roll(
                    bk[owner * n_blk], lax.rem((owner - me) * CAP + lay.width, lay.width), axis=1
                )
                return jnp.where(lanes == owner, turned, total)

            own = lax.fori_loop(0, n_dp, gather, jnp.zeros((48, lay.width), F32))
            xs[0:48, 0 : lay.real] = own[:, 0 : lay.real]

        where = place_of(step, CRITIC_TILE)
        now_in = framed(0, IN, where).astype(BF16)
        next_f = framed(24, OBS, where)
        reward = xs[23:24, where]
        done = xs[41:42, where]
        next_action, next_prob, _, _, _ = policy(next_f.astype(BF16), 1, where)
        aim_in = with_action(next_f, next_action)
        aim = jnp.minimum(critic(aim_in, 0)[0], critic(aim_in, 1)[0])
        target = reward + DISCOUNT * (1.0 - done) * (aim - alpha * next_prob)
        ys[0:1, where] = target
        critic_pass(0, now_in, where, target)

    def put_matrix(k):
        for chunk in range(n_dp):
            tile = chunk * lay.mat
            side, row = tile // 32, tile % 32
            grids[k][chunk, 0 : lay.mat] = acc_h[
                k, row * 8 : (row + lay.mat) * 8, side * 128 : (side + 1) * 128
            ].reshape(lay.mat, 8, 128)

    def put(row, value):
        for at in range(value.shape[0] // 8):
            for side in range(value.shape[1] // 128):
                tile = side * (R_SMALL // 8) + row // 8 + at
                grid_a[tile // lay.sml, lay.mat + tile % lay.sml] = value[
                    at * 8 : at * 8 + 8, side * 128 : (side + 1) * 128
                ]

    def plane_sum(group, peer):
        name = ("plane sum", group)
        return on_plane(
            grids[group].at[peer], froms[group].at[me], send.at[sent[name]], recv.at[here_at[name]], peer
        )

    def line_part(part):
        return min(part, 2), pl.ds(lay.mat, lay.sml) if part == 3 else pl.ds(0, lay.mat)

    def line_sum(part, peer):
        group, tiles = line_part(part)
        name = ("line sum", part)
        src, dst = zfs[group].at[tiles], zrs[group].at[z, tiles]
        return on_line(src, dst, send.at[sent[name]], recv.at[here_at[name]], peer)

    def line_bytes(part):
        group, tiles = line_part(part)
        return zrs[group].at[pl.ds(0, n_blk - 1), tiles]

    first_tile = me * lay.mat
    side = first_tile // 32
    row_tile = lax.rem(first_tile, 32)
    keeper_z = row_tile * 8 // lay.rows
    local_tile = row_tile - keeper_z * (lay.rows // 8)
    is_keeper = z == keeper_z

    def fold_plane(group):
        has_come(froms[group].at[pl.ds(0, n_dp - 1)], ("plane sum", group))
        froms[group][me] = grids[group][me]
        whole = froms[group][0]
        for at in range(1, n_dp):
            whole = whole + froms[group][at]
        zfs[group][...] = whole

        @pl.when(is_keeper)
        def _():
            held_rows = pl.ds(pl.multiple_of(local_tile * 8, 8), lay.mat * 8)
            held_lanes = pl.ds(pl.multiple_of(side * 128, 128), 128)
            old = sac_m[group, held_rows, held_lanes].reshape(lay.mat, 8, 128)
            zfs[group][0 : lay.mat] += (MOMENTUM * total).reshape(1, 1, 1) * old

        for part in (2, 3) if group == 2 else (group,):
            line_peers(lambda peer: line_sum(part, peer).start())

    def tile_copy(k, peer):
        return on_plane(totals[k].at[pl.ds(0, lay.mat)], mg.at[k, me], send.at[sent["tiles", k]], recv.at[here_at["tiles", k]], peer)

    def small_copy(peer):
        return on_plane(
            sum_a.at[pl.ds(lay.mat, lay.sml)], small.at[pl.ds(me * lay.sml, lay.sml)],
            send.at[sent["small"]], recv.at[here_at["small"]], peer,
        )

    def keep_copy(k, peer):
        view = sac_g.at[side, k, pl.ds(local_tile, lay.mat)]
        return on_plane(view, view, send.at[sent["sac g", k]], recv.at[here_at["sac g", k]], peer)

    def kept_bytes(number):
        return froms[0].at[pl.ds(0, number)]

    def fold_end(part):
        group, tiles = line_part(part)
        has_come(line_bytes(part), ("line sum", part))
        zrs[group][z, tiles] = zfs[group][tiles]
        whole = zrs[group][0, tiles]
        for block in range(1, n_blk):
            whole = whole + zrs[group][block, tiles]
        totals[group][tiles] = whole
        if part < 2:
            pl.when(jnp.logical_not(is_owner))(tile_copy(part, lay.owner).start)

            @pl.when(is_owner)
            def _():
                mg[part, me] = whole

            @pl.when(is_keeper)
            def _():
                sac_g[side, part, pl.ds(local_tile, lay.mat)] = whole
                plane_peers(lambda peer: keep_copy(part, peer).start())

        if part == 2:
            plane_peers(lambda peer: tile_copy(2, peer).start())
            mg[2, me] = whole

        if part == 3:
            plane_peers(lambda peer: small_copy(peer).start())
            small[pl.ds(me * lay.sml, lay.sml)] = sum_a[lay.mat :]

    def chain(group):
        def end():
            for part in (2, 3) if group == 2 else (group,):
                fold_end(part)

        return [
            lambda: plane_peers(lambda peer: plane_sum(group, peer).start()),
            lambda: fold_plane(group),
            end,
        ]

    chains = [chain(group) for group in range(3)]
    per = DYN_TILE // lay.real
    dyn_tiles = lay.n_dev // per
    in_actor = {actor_tiles - 1: [chains[0][1]]} if actor_tiles > 1 else {}
    after_actor = [chains[1][1]] if actor_tiles > 1 else [chains[0][1], chains[1][1]]
    in_dyn = {}
    in_dyn.setdefault(min(1, dyn_tiles - 1), []).append(chains[0][2])
    in_dyn.setdefault(dyn_tiles - 1, []).append(chains[1][2])

    def take(slots, step):
        for at, events in slots.items():
            @pl.when(step == at)
            def _():
                for event in events:
                    event()

    put_matrix(0)
    chains[0][0]()

    @pl.loop(0, critic_tiles)
    def _(step):
        where = place_of(step, CRITIC_TILE)
        critic_pass(1, framed(0, IN, where).astype(BF16), where, ys[0:1, where])

    put_matrix(1)
    chains[1][0]()

    has_come(bk.at[pl.ds(0, (n_dp - 1) * (n_blk - 1))], "plane")
    lane0 = lay.real // 128 * 128

    def add_block(at, carry):
        sides, fills = carry
        slot = slot_of(at)
        return sides + bk[slot, 0:32, lane0 : lane0 + 128], fills + bk[slot, 40:48, 0 : lay.real]

    sides, fills = lax.fori_loop(
        0, lay.n_dev, add_block, (jnp.zeros((32, 128), F32), jnp.zeros((8, lay.real), F32))
    )
    at = lay.real - lane0
    rows_all = float(lay.replay * lay.n_dev)
    centre = sides[0:24, at : at + 1] / rows_all
    scale = lax.rsqrt(sides[0:24, at + 1 : at + 2] / rows_all - centre * centre + 1e-6)
    total = sides[24:25, at : at + 1] + jnp.sum(fills[2:3, :], axis=1, keepdims=True)
    count[...] = jnp.broadcast_to(total, (8, 128))

    @pl.loop(0, actor_tiles)
    def _(step):
        take(in_actor, step)
        where = place_of(step, ACTOR_TILE)
        now_f = framed(0, IN, where)
        now_in = now_f.astype(BF16)
        weight = xs[42:43, where]
        action, log_prob, bent, moved, (a1, da1, a2, da2) = policy(now_in, 0, where)
        judged_in = with_action(now_f, action)
        loss = alpha * log_prob - log_alpha * (log_prob + TARGET_ENTROPY)
        grad_action = jnp.zeros((8, ACTOR_TILE), F32)
        used = act_rows(ACTOR_TILE)
        for k in range(2):
            judged, (_, df1, _, df2) = critic(judged_in, 2 + k)
            loss -= 0.5 * judged
            g2 = outer_sloped(wide[5 + k], -0.5 * weight, df2)
            g1 = sloped(dot(w2h[k], g2), df1)
            grad_action += dot(w1n[k], g1)[0:8]
        grad_latent = 2.0 * alpha * weight * action + grad_action * (1.0 - action * action)
        grad_scale = grad_latent * moved - alpha * weight
        grad_bent = grad_scale * 3.5 * (1.0 - bent * bent)
        g3 = jnp.concatenate(
            [jnp.where(used, grad_latent, 0.0), jnp.where(used, grad_bent, 0.0)], 0
        ).astype(BF16)
        acc_a[...] += dot(g3, a2, NT)
        acc_m[:, 0:16] += dot(ones16(ACTOR_TILE), g3, NT)
        g2 = sloped(dot(head_t[...], g3), da2)
        add_hidden(2, a1, g2)
        g1 = sloped(dot(w2h[2], g2), da1)
        acc_w[2] += dot(now_in, g1, NT)
        acc_l[1:2, 0:ACTOR_TILE] += weight * loss
        acc_l[2:3, 0:ACTOR_TILE] += weight * (log_prob + TARGET_ENTROPY)

    put_matrix(2)
    for k in range(3):
        put(R_IN + 24 * k, acc_w[k, 0:24, :])
    put(R_HEAD, acc_a[...])
    rowbuf[0:1, :] = acc_c[0, 0:1, :]
    rowbuf[1:2, :] = acc_c[1, 0:1, :]
    for k in range(3):
        rowbuf[2 + k : 3 + k, :] = acc_h[k, HSAC : HSAC + 1, :]
    put(R_OUT, rowbuf[...])
    folded = jnp.sum(acc_l[...], axis=1, keepdims=True)
    rowbuf[...] = jnp.zeros_like(rowbuf)
    rowbuf[0:1, 0:48] = acc_m[0:1, :]
    rowbuf[0:1, 64:65] = folded[0:1] + folded[1:2]
    rowbuf[0:1, 65:66] = folded[2:3]
    put(R_MISC, rowbuf[...])
    put(R_MISC + 8, jnp.zeros((R_SMALL - R_MISC - 8, HSAC), F32))
    chains[2][0]()
    for event in after_actor:
        event()

    def dyn_bias(start, width):
        row = jnp.zeros((1, width), F32)
        for e in range(MEMBERS):
            row = jnp.where(me == e, bias[:, start + width * e : start + width * (e + 1)], row)
        return row

    @pl.when(is_dyn)
    def _():
        w1f[0] = jnp.zeros((32, HSAC), F32)
        w1f[0, 0:IN, 0:HDYN] = rounded(dyn_in[dyn_e])
        for at, piece in enumerate(pieces(dyn_bias(DB1, HDYN))):
            w1f[0, IN + at : IN + at + 1, 0:HDYN] = piece.astype(F32)
        w1t[0] = (0.5 * w1f[0].T).astype(BF16)
        rowbuf[...] = jnp.zeros_like(rowbuf)
        rowbuf[0:1, 0:HDYN] = dyn_bias(DB2, HDYN)
        head_row = dyn_bias(DB3, DOUT)
        rowbuf[1:2, 0:HALF] = head_row[:, 0:HALF]
        rowbuf[1:2, 24 : 24 + HALF] = head_row[:, HALF:DOUT]
        rowbuf[2:3, 0:HALF] = bias[:, MAXLV : MAXLV + HALF]
        rowbuf[3:4, 0:HALF] = bias[:, MINLV : MINLV + HALF]
        dcols[...] = rowbuf[...].T
        wide[0] = jnp.broadcast_to(0.5 * dcols[:, 0:1], (HSAC, 128))
        dpack[...] = jnp.zeros_like(dpack)
        dpack[0:HALF, 0:HDYN] = dyn_out[dyn_e, 0:HALF, :]
        dpack[24 : 24 + HALF, 0:HDYN] = dyn_out[dyn_e, HALF:DOUT, :]
        dhead[...] = dpack[0:48, :].astype(BF16)
        dhead_t[...] = (0.5 * rounded(dpack[0:48, :])).T.astype(BF16)
        dpack[...] = jnp.zeros_like(dpack)

        has_come(dhg.at[pl.ds(0, n_blk - 1)], "dyn h")
        has_come(dmg.at[pl.ds(0, n_blk - 1)], "dyn m")
        dhg[z] = dyn_h[dyn_e]
        dmg[z] = dyn_m[dyn_e]
        dmat[...] = jnp.zeros_like(dmat)
        for block in range(n_blk):
            dmat[block * lay.drows : (block + 1) * lay.drows, 0:HDYN] = 0.5 * rounded(dhg[block])
        w2h[0] = dmat[...].astype(BF16)
        w2t[0] = dmat[...].T.astype(BF16)
        for ref in (dacc_h, dacc_w, dacc_o, dacc_m, dacc_b, dacc_l):
            ref[...] = jnp.zeros_like(ref)

    @pl.loop(0, dyn_tiles)
    def _(tile):
        take(in_dyn, tile)

        @pl.when(is_dyn)
        def _():
            for at in range(per):
                slot = slot_of(tile * per + at)
                xt[:, at * lay.real : (at + 1) * lay.real] = bk[slot, :, 0 : lay.real]
            now = xt[0:24, :]
            later = xt[24:48, :]
            row24 = rows_of((24, DYN_TILE))
            scaled = jnp.where(row24 < IN, (now - centre) * scale, 1.0)
            inputs = jnp.concatenate([scaled, (rows_of((8, DYN_TILE)) < 2).astype(F32)], 0).astype(BF16)
            first, slope1 = gated(dot(w1t[0], inputs))
            second, slope2 = gated(dot(w2t[0], first), wide[0])
            out = dot(dhead[...], second) + dcols[0:48, 1:2]
            used = row24 < HALF
            upper = dcols[0:24, 2:3]
            lower = dcols[0:24, 3:4]
            gap1 = upper - out[24:48]
            gap2 = upper - softplus(gap1) - lower
            log_var = lower + softplus(gap2)
            error = out[0:24] - jnp.where(row24 == OBS, now[23:24], later - now)
            inverse = jnp.exp(-log_var)
            weight = xt[42:43, :] * (xt[43:44, :] == me.astype(F32)).astype(F32)
            spread_term = error * error * inverse
            nll = jnp.sum(jnp.where(used, spread_term + log_var, 0.0), axis=0, keepdims=True)
            dacc_l[0:1, :] += weight * nll
            grad_mu = 2.0 * weight * error * inverse
            grad_lv = weight * (1.0 - spread_term)
            open1 = sigmoid(gap1)
            open2 = sigmoid(gap2)
            grad_lv1 = grad_lv * open2
            dacc_b[0] += jnp.where(used, grad_lv1 * (1.0 - open1), 0.0)
            dacc_b[1] += jnp.where(used, grad_lv * (1.0 - open2), 0.0)
            g3 = jnp.concatenate(
                [jnp.where(used, grad_mu, 0.0), jnp.where(used, grad_lv1 * open1, 0.0)], 0
            ).astype(BF16)
            dacc_o[...] += dot(g3, second, NT)
            dacc_m[...] += dot(ones16(DYN_TILE), g3, NT)
            g2 = sloped(dot(dhead_t[...], g3), slope2)
            dacc_h[...] += dot(jnp.concatenate([first, ones16(DYN_TILE)], 0), g2, NT)
            g1 = sloped(dot(w2h[0], g2), slope1)
            dacc_w[...] += dot(inputs, g1, NT)

    out_of = {"pack": dyn_s, "x": dyn_x}

    def member_copy(name, src, owner, kind, sem, peer):
        return on_plane(src, out_of[name].at[owner], send.at[sent[name, kind]], recv.at[sem], peer)

    def give(name, src):
        like_peers(
            lambda peer: member_copy(name, src, dyn_e, "own", here_at[name, "like"] + dyn_e, peer).start()
        )
        member_copy(name, src, dyn_e, "own", here_at[name, "sibling"], sibling).start()

    def hand_on(name):
        def body(peer):
            @pl.when(peer < MEMBERS)
            def _():
                owner = jnp.minimum(peer, MEMBERS - 1)
                view = out_of[name].at[owner]
                member_copy(name, view, owner, "on", here_at[name, "like"] + owner, sibling).wait_recv()
                member_copy(name, view, owner, "on", here_at[name, "sibling"], sibling).start()

        like_peers(body)

    even, odd = (MEMBERS + 1) // 2, MEMBERS // 2
    handed = even - core * (even - odd) - jnp.where(is_dyn, 1, 0)

    def from_sibling(name):
        for side, number in ((0, odd), (1, even)):
            @pl.when(core == side)
            def _():
                has_come(out_of[name].at[pl.ds(0, number)], (name, "sibling"))

    def gave(name):
        @pl.when(is_dyn)
        def _():
            for begin in range(0, n_dp // 2, MEMBERS):
                number = min(MEMBERS, n_dp // 2 - begin)
                has_sent(out_of[name].at[pl.ds(0, number)], (name, "own"))

        for number in (even, even - 1, even - 2):
            @pl.when(handed == number)
            def _():
                has_sent(out_of[name].at[pl.ds(0, number)], (name, "on"))

    def line_rows(ref):
        rows = ref[0 : lay.drows, 0:HDYN]
        for block in range(1, n_blk):
            rows = jnp.where(z == block, ref[block * lay.drows : (block + 1) * lay.drows, 0:HDYN], rows)
        return rows

    def sac_x_copy(k, src, peer):
        name = ("sac x", k)
        return on_plane(src, sac_x.at[k], send.at[sent[name] + peer], recv.at[here_at[name]], peer)

    mine_rows = pl.ds(pl.multiple_of(z * lay.rows, lay.rows), lay.rows)

    def take_matrix(k):
        has_come(mg.at[k, pl.ds(0, n_dp - 1)], ("tiles", k))
        for chunk in range(n_dp):
            tile = chunk * lay.mat
            half, row = tile // 32, tile % 32
            at = slice(row * 8, (row + lay.mat) * 8)
            piece = mg[k, chunk].reshape(lay.mat * 8, 128)
            mat[k, at, half * 128 : (half + 1) * 128] = piece / total
        normalise(mat.at[k])

    chains[2][1]()

    @pl.when(is_dyn)
    def _():
        dpack[D_IN : D_IN + 24, :] = dacc_w[0:24, :]
        dpack[D_OUT : D_OUT + HALF, :] = dacc_o[0:HALF, :]
        dpack[D_OUT + HALF : D_OUT + DOUT, :] = dacc_o[24 : 24 + HALF, :]
        dpack[D_B2 : D_B2 + 1, :] = dacc_h[HSAC : HSAC + 1, :]
        dpack[D_B3 : D_B3 + 1, 0:48] = dacc_m[0:1, :]
        lanes = lax.broadcasted_iota(jnp.int32, (24, 128), 1)
        bound = jnp.where(
            lanes == 0,
            jnp.sum(dacc_b[0], axis=1, keepdims=True),
            jnp.where(lanes == 1, jnp.sum(dacc_b[1], axis=1, keepdims=True), 0.0),
        )
        dpack[D_UP : D_UP + 2, 0:24] = bound.T[0:2, :]
        dpack[D_LOSS : D_LOSS + 1, 0:128] = jnp.broadcast_to(
            jnp.sum(dacc_l[0:1, :], axis=1, keepdims=True), (1, 128)
        )
        dpack[D_HID : D_HID + lay.drows, 0:HDYN] = line_rows(dacc_h)
        dyn_s[dyn_e] = dpack[...]
        give("pack", dpack)
        dmat[...] = jnp.zeros_like(dmat)
        for block in range(n_blk):
            at = slice(block * lay.drows, (block + 1) * lay.drows)
            dmat[at, 0:HDYN] = MOMENTUM * dmg[block] + dacc_h[at, 0:HDYN] / total
        normalise(dmat)

    def own_x(k):
        return mat.at[k, mine_rows]

    passes_x = jnp.logical_and(core == lay.owner % 2, jnp.logical_not(is_owner))

    def sum_end(step):
        pl.when(step == NS_ITERS - 1)(chains[2][2])

    @pl.when(is_dyn)
    def _():
        schulz([dmat], NS_ITERS, sum_end)
        rows = line_rows(dmat)
        drow_x[...] = rows
        dyn_x[dyn_e] = rows
        give("x", drow_x)

    @pl.when(is_owner)
    def _():
        for k in range(2):
            take_matrix(k)
            schulz([mat.at[k]], NS_ITERS, sum_end if k == 1 else None)
            sac_x[k] = mat[k, mine_rows, :]
            like_peers(lambda peer: sac_x_copy(k, own_x(k), peer).start())
            sac_x_copy(k, own_x(k), sibling).start()

    if n_dp > MEMBERS + 1:
        pl.when(jnp.logical_not(jnp.logical_or(is_dyn, is_owner)))(chains[2][2])

    def sent_early():
        has_sent(wg.at[pl.ds(0, n_blk - 1), :, half_rows], "hidden")
        has_sent(wg.at[pl.ds(0, n_blk - 1), :, half_rows], "hidden on")
        has_sent(asked.at[pl.ds(0, n_dp - 1)], "lists")
        has_sent(bk.at[pl.ds(0, n_dp - 1)], "own")
        has_sent(bk.at[pl.ds(0, n_blk - 1)], "line")
        has_sent(bk.at[pl.ds(0, (n_dp - 1) * (n_blk - 1))], "plane")

        @pl.when(is_dyn)
        def _():
            has_sent(dhg.at[pl.ds(0, n_blk - 1)], "dyn h")
            has_sent(dmg.at[pl.ds(0, n_blk - 1)], "dyn m")

        for group in range(3):
            has_sent(froms[group].at[pl.ds(0, n_dp - 1)], ("plane sum", group))
        for part in range(4):
            has_sent(line_bytes(part), ("line sum", part))

    def pass_on(step):
        @pl.when(step == 2)
        def _():
            hand_on("pack")
            hand_on("x")
            for k in range(2):
                pl.when(jnp.logical_not(is_owner))(sac_x_copy(k, sac_x.at[k], sibling).wait_recv)
                pl.when(passes_x)(sac_x_copy(k, sac_x.at[k], sibling).start)

    take_matrix(2)
    for half in range(2):
        for piece in range(lay.rows // 8 // lay.mat):
            chunk = (half * 32 + z * (lay.rows // 8)) // lay.mat + piece
            sac_g[half, 2, piece * lay.mat : (piece + 1) * lay.mat] = mg[2, chunk]
    schulz([mat.at[2]], NS_ITERS, pass_on)
    sac_x[2] = mat[2, mine_rows, :]

    sent_early()
    has_come(small.at[pl.ds(0, (n_dp - 1) * lay.sml)], "small")
    for number, test in ((lay.keepers - 1, is_keeper), (lay.keepers, jnp.logical_not(is_keeper))):
        for k in range(2):
            pl.when(test)(functools.partial(has_come, kept_bytes(number), ("sac g", k)))
    from_sibling("pack")
    from_sibling("x")

    has_sent(small.at[pl.ds(0, (n_dp - 1) * lay.sml)], "small")
    gave("pack")
    gave("x")

    has_sent(mg.at[2, pl.ds(0, n_dp - 1)], ("tiles", 2))

    @pl.when(jnp.logical_not(is_owner))
    def _():
        for k in range(2):
            tile_copy(k, sibling).wait_send()

    for k in range(2):
        pl.when(is_keeper)(functools.partial(has_sent, kept_bytes(n_dp - 1), ("sac g", k)))

    for k in range(2):
        @pl.when(is_owner)
        def _():
            like_peers(lambda peer: sac_x_copy(k, own_x(k), peer).wait_send())
            sac_x_copy(k, own_x(k), sibling).wait_send()

        pl.when(passes_x)(sac_x_copy(k, sac_x.at[k], sibling).wait_send)


def adamw(weights, first, second, gradient):
    first = BETA_FIRST * first + (1.0 - BETA_FIRST) * gradient
    second = BETA_SECOND * second + (1.0 - BETA_SECOND) * gradient * gradient
    first_hat = first / (1.0 - BETA_FIRST**STEP)
    second_hat = second / (1.0 - BETA_SECOND**STEP)
    step = first_hat / (jnp.sqrt(second_hat) + 1e-8) + ADAM_DECAY * weights
    return weights - ADAM_RATE * step, first, second


def update_kernel(*refs):
    (
        sac_g, sac_x, dyn_x, dyn_s, small, count, sac_h, dyn_h, dyn_m,
        ci, ci_m, ci_v, ai, ai_m, ai_v, di, di_m, di_v, co, co_m, co_v, ao, ao_m, ao_v,
        do, do_m, do_v, bi, bi_m, bi_v,
        sac_new, sac_mom, dyn_new, dyn_mom, ci_n, ci_mn, ci_vn, ai_n, ai_mn, ai_vn, di_n, di_mn,
        di_vn, co_n, co_mn, co_vn, ao_n, ao_mn, ao_vn, do_n, do_mn, do_vn, bi_n, bi_mn, bi_vn,
        loss, counted, bg,
    ) = refs
    total = count[0:1, 0:1]
    for k in range(3):
        for side in range(2):
            tiles = sac_g[side, k].reshape(sac_mom.shape[1], 128)
            sac_mom[k, :, side * 128 : (side + 1) * 128] = tiles / total
    sac_new[...] = sac_h[...] * (1.0 - MUON_RATE * MUON_DECAY) - MUON_RATE * sac_x[...]
    dyn_rows = dyn_s[:, D_HID : D_HID + dyn_m.shape[1], 0:HDYN]
    dyn_mom[...] = MOMENTUM * dyn_m[...] + dyn_rows / total.reshape(1, 1, 1)
    dyn_new[...] = dyn_h[...] * (1.0 - MUON_RATE * MUON_DECAY) - MUON_RATE * dyn_x[...]

    def rows(row, number):
        sides = []
        for side in range(2):
            at = side * (R_SMALL // 8) + row // 8
            sides.append(small[at : at + -(-number // 8)].reshape(-1, 128))
        return jnp.concatenate(sides, 1)

    def store(outs, at, values):
        for out, value in zip(outs, values):
            out[at] = value

    outs = (ci_n, ci_mn, ci_vn)
    for k in range(2):
        at = (slice(None), k, slice(None))
        grad = rows(R_IN + 24 * k, 24)
        bg[:, CB1 + HSAC * k : CB1 + HSAC * (k + 1)] = grad[IN : IN + 1]
        store(outs, at, adamw(ci[at], ci_m[at], ci_v[at], grad[0:IN] / total))
    grad = rows(R_IN + 48, 24)
    bg[:, AB1 : AB1 + HSAC] = grad[IN : IN + 1]
    store((ai_n, ai_mn, ai_vn), ..., adamw(ai[...], ai_m[...], ai_v[...], grad[0:OBS] / total))
    grad = rows(R_HEAD, 16)
    for at, row in ((slice(0, ACT), slice(1, 1 + ACT)), (slice(ACT, 2 * ACT), slice(9, 9 + ACT))):
        store((ao_n, ao_mn, ao_vn), at, adamw(ao[at], ao_m[at], ao_v[at], grad[row] / total))
    grad = rows(R_OUT, 8)
    store((co_n, co_mn, co_vn), ..., adamw(co[...], co_m[...], co_v[...], grad[0:2] / total))
    bg[:, CB2 : CB2 + HSAC] = grad[2:3]
    bg[:, CB2 + HSAC : CB2 + 2 * HSAC] = grad[3:4]
    bg[:, AB2 : AB2 + HSAC] = grad[4:5]
    grad = rows(R_MISC, 8)
    bg[:, CB3 : CB3 + 1] = grad[0:1, 16:17]
    bg[:, CB3 + 1 : CB3 + 2] = grad[0:1, 32:33]
    bg[:, AB3 : AB3 + ACT] = grad[0:1, 1 : 1 + ACT]
    bg[:, AB3 + ACT : AB3 + 2 * ACT] = grad[0:1, 9 : 9 + ACT]
    bg[:, LOGA : LOGA + 1] = -grad[0:1, 65:66]
    total_loss = grad[0:1, 64:65]
    up = jnp.zeros((1, HALF), F32)
    low = jnp.zeros((1, HALF), F32)
    for e in range(MEMBERS):
        pack = dyn_s[e]
        total_loss = total_loss + pack[D_LOSS : D_LOSS + 1, 0:1]
        up = up + pack[D_UP : D_UP + 1, 0:HALF]
        low = low + pack[D_LOW : D_LOW + 1, 0:HALF]
        bg[:, DB1 + HDYN * e : DB1 + HDYN * (e + 1)] = pack[IN : IN + 1, 0:HDYN]
        bg[:, DB2 + HDYN * e : DB2 + HDYN * (e + 1)] = pack[D_B2 : D_B2 + 1, 0:HDYN]
        bg[:, DB3 + DOUT * e : DB3 + DOUT * e + HALF] = pack[D_B3 : D_B3 + 1, 0:HALF]
        bg[:, DB3 + DOUT * e + HALF : DB3 + DOUT * (e + 1)] = pack[D_B3 : D_B3 + 1, 24 : 24 + HALF]
        grad = pack[0:IN, 0:HDYN] / total
        store((di_n, di_mn, di_vn), e, adamw(di[e], di_m[e], di_v[e], grad))
        grad = pack[D_OUT : D_OUT + DOUT, 0:HDYN] / total
        store((do_n, do_mn, do_vn), e, adamw(do[e], do_m[e], do_v[e], grad))
    bg[:, MAXLV : MAXLV + HALF] = up
    bg[:, MINLV : MINLV + HALF] = low
    lane = lax.broadcasted_iota(jnp.int32, (1, NB), 1)
    bounds = jnp.where(
        jnp.logical_and(lane >= MAXLV, lane < MINLV),
        BOUND_WEIGHT,
        jnp.where(jnp.logical_and(lane >= MINLV, lane < LOGA), -BOUND_WEIGHT, 0.0),
    )
    grad = bg[...] / total + bounds
    flat = [ref[...].reshape(1, NB) for ref in (bi, bi_m, bi_v)]
    store((bi_n, bi_mn, bi_vn), ..., [value.reshape(NB) for value in adamw(*flat, grad)])
    loss[...] = total_loss
    counted[...] = total


def shards(
    lay, replay, model_rows, requests, member_of, model_live, noise, sac_hidden, sac_hidden_mom,
    dyn_hidden, dyn_hidden_mom, crit_in, crit_in_m, crit_in_v, act_in, act_in_m, act_in_v, dyn_in,
    dyn_in_m, dyn_in_v, crit_out, crit_out_m, crit_out_v, act_out, act_out_m, act_out_v, dyn_out,
    dyn_out_m, dyn_out_v, biases, biases_m, biases_v, targ_in, targ_hidden, targ_out, targ_bias,
):
    n_dp, n_blk = lay.n_dp, lay.n_blk
    spec = pl.BlockSpec(memory_space=pltpu.VMEM)

    def flip(value):
        return jnp.transpose(value, (1, 0, 2))

    def swap(value):
        return jnp.swapaxes(value, -1, -2)

    def kept(value):
        return pltpu.with_memory_space_constraint(value, pltpu.VMEM)

    inputs = (
        replay, model_rows, requests, member_of, model_live, jnp.transpose(noise, (2, 0, 1)),
        sac_hidden, sac_hidden_mom, dyn_hidden, dyn_hidden_mom, flip(crit_in), act_in, dyn_in,
        crit_out, swap(act_out), swap(dyn_out), biases, flip(targ_in), targ_hidden, targ_out,
        targ_bias,
    )
    shape = jax.ShapeDtypeStruct
    rows, drows = lay.rows, lay.drows
    out_shape = (
        pltpu.VMEM((2, 3, rows // 8, 8, 128), F32),
        pltpu.VMEM((3, rows, HSAC), F32),
        pltpu.VMEM((MEMBERS, drows, HDYN), F32),
        pltpu.VMEM((MEMBERS, D_ROWS, HSAC), F32),
        pltpu.VMEM((32, 8, 128), F32),
        pltpu.VMEM((8, 128), F32),
    )

    def vm(*dims, kind=F32):
        return pltpu.VMEM(dims, kind)

    scratch = [
        vm(n_blk, 3, rows, HSAC, kind=BF16),
        vm(2, n_dp, CAP, kind=jnp.int32),
        vm(n_dp, 2, n_dp, CAP, kind=jnp.int32),
        vm(n_blk, drows, HDYN),
        vm(n_blk, drows, HDYN),
        vm(lay.n_dev, 48, lay.width),
        vm(56, lay.batch),
        vm(2, 8, lay.batch),
        vm(5, 32, HSAC),
        vm(5, HSAC, 32, kind=BF16),
        vm(2, 16, HSAC, kind=BF16),
        vm(5, HSAC, HSAC, kind=BF16),
        vm(3, HSAC, HSAC, kind=BF16),
        vm(5, 16, HSAC, kind=BF16),
        vm(HSAC, 16, kind=BF16),
        vm(16, HSAC),
        vm(8, HSAC),
        vm(7, HSAC, 128),
        vm(128, 8),
        vm(3, HSAC + 16, HSAC),
        vm(3, 32, HSAC),
        vm(2, 16, HSAC),
        vm(16, HSAC),
        vm(16, 48),
        vm(8, max(CRITIC_TILE, ACTOR_TILE)),
        *[vm(n_dp, chunk, 8, 128) for chunk in lay.chunks],
        *[vm(n_dp, chunk, 8, 128) for chunk in lay.chunks],
        *[vm(n_blk, chunk, 8, 128) for chunk in lay.chunks],
        *[vm(chunk, 8, 128) for chunk in lay.chunks],
        *[vm(chunk, 8, 128) for chunk in lay.chunks],
        vm(8, lay.batch),
        vm(3, n_dp, lay.mat, 8, 128),
        vm(3, HSAC, HSAC),
        vm(HSAC, 8),
        vm(HSAC + 16, HSAC),
        vm(32, HSAC),
        vm(48, HSAC),
        vm(16, 48),
        vm(2, 24, DYN_TILE),
        vm(8, DYN_TILE),
        vm(48, DYN_TILE),
        vm(HSAC, HSAC),
        vm(D_ROWS, HSAC),
        vm(drows, HDYN),
        vm(1, NB),
        vm(48, HSAC, kind=BF16),
        vm(HSAC, 48, kind=BF16),
    ]
    scratch += [pltpu.SemaphoreType.DMA((lay.departures,)), pltpu.SemaphoreType.DMA((lay.arrivals,))]
    varying = 4 * (lay.n_dev * 48 * lay.width + 72 * lay.batch + 48 * lay.replay)
    gathered = pl.pallas_call(
        functools.partial(main_kernel, lay),
        out_shape=out_shape,
        in_specs=[spec] * len(inputs),
        out_specs=[spec] * len(out_shape),
        scratch_shapes=scratch,
        compiler_params=pltpu.CompilerParams(
            collective_id=0, has_side_effects=True, vmem_limit_bytes=26 * 2**20 + varying
        ),
        name="step",
    )(*[pltpu.with_memory_space_constraint(value, pltpu.HBM) for value in inputs])
    params = (
        sac_hidden, dyn_hidden, dyn_hidden_mom,
        flip(crit_in), flip(crit_in_m), flip(crit_in_v), act_in, act_in_m, act_in_v,
        dyn_in, dyn_in_m, dyn_in_v, crit_out, crit_out_m, crit_out_v,
        swap(act_out), swap(act_out_m), swap(act_out_v),
        swap(dyn_out), swap(dyn_out_m), swap(dyn_out_v), biases, biases_m, biases_v,
    )
    new_shape = [shape(sac_hidden.shape, F32)] + [shape(value.shape, F32) for value in params]
    new_shape += [shape((1, 1), F32)] * 2
    out = pl.pallas_call(
        update_kernel,
        out_shape=tuple(new_shape),
        in_specs=[spec] * (len(gathered) + len(params)),
        out_specs=[spec] * len(new_shape),
        scratch_shapes=[vm(1, NB)],
        compiler_params=pltpu.CompilerParams(vmem_limit_bytes=16 * 2**20),
        name="update",
    )(*[kept(value) for value in gathered], *params)
    out = list(out)
    for at in (4, 5, 6):
        out[at] = flip(out[at])
    for at in (16, 17, 18, 19, 20, 21):
        out[at] = swap(out[at])
    for at in (25, 26):
        out[at] = out[at].reshape(())
    return tuple(out)


def solution(mesh):
    both = ("dp", "blk")
    sharded = (
        P(None, both), P(None, both), P(both, None), P(both, None), P(both), P(None, both, None),
    )
    hidden = (P(None, "blk", None),) * 4

    def step(replay, model_rows, *others):
        lay = Layout(mesh, replay.shape[1], model_rows.shape[1])
        return shards(lay, replay, model_rows, *others)

    return jax.shard_map(
        step,
        mesh=mesh,
        in_specs=sharded + hidden + (P(),) * 25,
        out_specs=hidden + (P(),) * 23,
        check_vma=False,
    )
```

```python
import functools

import jax
import jax.numpy as jnp
from jax import lax
from jax.experimental import pallas as pl
from jax.experimental.pallas import tpu as pltpu
from jax.sharding import PartitionSpec as P

OBS = 17
ACT = 6
IN = OBS + ACT
FEAT = 42
HDYN = 200
HSAC = 256
MEMBERS = 7
DOUT = 36
HALF = DOUT // 2
NB = 4639
NS_ITERS = 5
STEP = 10
CAP = 8
CRITIC_TILE = 1280
ACTOR_TILE = 640
DYN_TILE = 512
ROWS = 32

DISCOUNT = 0.99
TARGET_ENTROPY = -6.0
BOUND_WEIGHT = 0.01
MOMENTUM = 0.95
MUON_RATE = 0.4
MUON_DECAY = 0.01
ADAM_RATE = 0.1
ADAM_DECAY = 0.01
BETA_FIRST = 0.9
BETA_SECOND = 0.999
COEF_LINEAR = 3.4445
COEF_CUBIC = -4.775
COEF_QUINTIC = 2.0315

CB1, CB2, CB3, AB1, AB2, AB3 = 0, 512, 1024, 1026, 1282, 1538
DB1, DB2, DB3, MAXLV, MINLV, LOGA = 1550, 2950, 4350, 4602, 4620, 4638

R_IN, R_HEAD, R_OUT, R_MISC, R_SMALL = 0, 72, 88, 96, 128
D_IN, D_OUT, D_B2, D_B3, D_UP, D_LOW, D_LOSS, D_HID, D_ROWS = 0, 24, 60, 61, 62, 63, 64, 72, 128

F32, BF16 = jnp.float32, jnp.bfloat16
MESH = pl.DeviceIdType.MESH
NN = (((1,), (0,)), ((), ()))
NT = (((1,), (1,)), ((), ()))


def dot(a, b, dims=NN):
    return lax.dot_general(a, b, dims, preferred_element_type=F32)


def rounded(v):
    return v.astype(BF16).astype(F32)


def pieces(v):
    high = v.astype(BF16)
    rest = v - high.astype(F32)
    middle = rest.astype(BF16)
    return high, middle, (rest - middle.astype(F32)).astype(BF16)


def split(v):
    high = v.astype(BF16)
    return high, (v - high.astype(F32)).astype(BF16)


def product(a, b, dims=NN):
    left = jnp.concatenate([a[0], a[0], a[1]], 1)
    right = jnp.concatenate([b[0], b[1], b[0]], dims[0][1][0])
    half = left.shape[0] // 2
    return jnp.concatenate([dot(left[:half], right, dims), dot(left[half:], right, dims)], 0)


def softplus(v):
    return jnp.maximum(v, 0.0) + jnp.log1p(jnp.exp(-jnp.abs(v)))


def sigmoid(v):
    return 0.5 + 0.5 * jnp.tanh(0.5 * v)


def gate(half):
    up = 1.0 + jnp.tanh(half)
    value = half * up
    return value, up + value * (2.0 - up)


def by_rows(body, *arrays):
    done = [
        body(*[array[at : at + ROWS] for array in arrays]) for at in range(0, arrays[0].shape[0], ROWS)
    ]
    return [jnp.concatenate(parts, 0) for parts in zip(*done)]


def spread_to(column, width):
    return jnp.concatenate([column] * (width // 128), 1)


def gated(half, column=None):
    def body(part, *offset):
        value, slope = gate(part + spread_to(offset[0], part.shape[1]) if offset else part)
        return value.astype(BF16), slope

    return by_rows(body, half, *([] if column is None else [column]))


def sloped(grad, slope):
    return by_rows(lambda part, by: ((part * by).astype(BF16),), grad, slope)[0]


def outer_sloped(column, row, slope):
    return by_rows(lambda part, by: (((spread_to(part, by.shape[1]) * row) * by).astype(BF16),), column, slope)[0]


def rows_of(shape):
    return lax.broadcasted_iota(jnp.int32, shape, 0)


def schulz(refs, steps, before=None):
    @pl.loop(0, steps)
    def _(step):
        if before is not None:
            before(step)
        matrices = [ref[...] for ref in refs]
        parts = [split(matrix) for matrix in matrices]
        grams = [product(part, part, NT) for part in parts]
        halves = [split(gram) for gram in grams]
        squares = [product(half, half) for half in halves]
        blends = [
            split(COEF_CUBIC * gram + COEF_QUINTIC * square) for gram, square in zip(grams, squares)
        ]
        moved = [product(blend, part) for blend, part in zip(blends, parts)]
        for ref, matrix, move in zip(refs, matrices, moved):
            ref[...] = COEF_LINEAR * matrix + move


def normalise(ref):
    moment = ref[...]
    norm = jnp.sqrt(jnp.sum(jnp.sum(moment * moment, axis=1, keepdims=True), axis=0, keepdims=True))
    ref[...] = moment / (norm + 1e-7)


class Layout:
    def __init__(self, mesh, replay, model):
        self.n_dp = mesh.shape["dp"]
        self.n_blk = mesh.shape["blk"]
        self.n_dev = self.n_dp * self.n_blk
        self.replay = replay
        self.model = model
        self.real = self.n_dp * CAP
        self.batch = self.real + model
        self.width = -(-(self.real + 2) // 128) * 128
        self.rows = HSAC // self.n_blk
        self.drows = HDYN // self.n_blk
        self.mat = 64 // self.n_dp
        self.sml = 32 // self.n_dp
        self.chunks = (self.mat, self.mat + self.sml, self.mat)
        groups = [("plane sum", g) for g in range(3)] + [("line sum", g) for g in range(4)]
        common = ["hidden", "hidden on", "lists", "own", "line", "plane", "dyn h", "dyn m", "small"]
        common += groups
        kinds = [(name, kind) for name in ("pack", "x") for kind in ("own", "on")]
        sent = common + [("tiles", k) for k in range(3)] + kinds
        self.sent = {name: at for at, name in enumerate(sent)}
        self.departures = len(sent)
        self.here, self.arrivals = {}, 0
        tiles = [("tiles", k) for k in range(3)]
        tiles += [("pack", "sibling"), ("x", "sibling")]
        for name in common + tiles:
            self.here[name] = self.arrivals
            self.arrivals += 1
        for name in ("pack", "x"):
            self.here[name, "like"] = self.arrivals
            self.arrivals += MEMBERS


def main_kernel(lay, *refs):
    (
        replay, model, requests, member, live, noise, sac_h, sac_m, dyn_h, dyn_m, crit_in, act_in,
        dyn_in, crit_out, act_out, dyn_out, biases, targ_in, targ_hidden, targ_out, targ_bias,
        sac_g, sac_x, dyn_x, dyn_s, small, count,
        wg, lists, asked, dhg, dmg, bk, xs, nz, ys, w1f, w1t, w1n, w2t, w2h, heads, head_t, head_f,
        rowbuf, wide, headcol, acc_h, acc_w, acc_c, acc_a, acc_m, acc_l, grid_0, grid_1, grid_2, from_0, from_1,
        from_2, zr_0, zr_1, zr_2, zf_0, zf_1, zf_2, sum_0, sum_1, sum_2, mg, mat, dcols, dacc_h, dacc_w, dacc_o, dacc_m, dacc_b, dacc_l, xt, dmat,
        dpack, drow_x, bias, dhead, dhead_t, *rest,
    ) = refs
    send, recv = rest
    sent, here_at = lay.sent, lay.here
    grids, froms = (grid_0, grid_1, grid_2), (from_0, from_1, from_2)
    zrs, zfs, totals = (zr_0, zr_1, zr_2), (zf_0, zf_1, zf_2), (sum_0, sum_1, sum_2)
    n_dp, n_blk = lay.n_dp, lay.n_blk
    me = lax.axis_index("dp")
    z = lax.axis_index("blk")
    core = lax.rem(me, 2)
    sibling = me + 1 - 2 * core
    is_dyn = me < MEMBERS
    dyn_e = jnp.minimum(me, MEMBERS - 1)

    def on_plane(src, dst, ssem, rsem, peer):
        return pltpu.make_async_remote_copy(
            src_ref=src, dst_ref=dst, send_sem=ssem, recv_sem=rsem,
            device_id={"dp": peer}, device_id_type=MESH,
        )

    def on_line(src, dst, ssem, rsem, peer):
        return pltpu.make_async_remote_copy(
            src_ref=src, dst_ref=dst, send_sem=ssem, recv_sem=rsem,
            device_id={"blk": peer}, device_id_type=MESH,
        )

    def over(number, body):
        if number <= 8:
            for off in range(1, number):
                body(off)
        else:
            pl.loop(1, number)(body)

    def plane_peers(body):
        over(n_dp, lambda off: body(lax.rem(me + off, n_dp)))

    def like_peers(body):
        over(n_dp // 2, lambda off: body(lax.rem(me + 2 * off, n_dp)))

    def line_peers(body):
        over(n_blk, lambda off: body(lax.rem(z + off, n_blk)))

    def has_sent(view, name):
        at = send.at[sent[name]]
        on_plane(view, view, at, at, sibling).wait_send()

    def has_come(view, name):
        at = recv.at[here_at[name]]
        on_plane(view, view, at, at, sibling).wait_recv()

    barrier = pltpu.get_barrier_semaphore()
    plane_peers(lambda peer: pl.semaphore_signal(barrier, inc=1, device_id={"dp": peer}, device_id_type=MESH))
    line_peers(lambda peer: pl.semaphore_signal(barrier, inc=1, device_id={"blk": peer}, device_id_type=MESH))
    wg[0] = sac_h[...].astype(BF16)
    lists[0] = requests[...]
    lists[1] = member[...]
    pl.semaphore_wait(barrier, n_dp - 1 + n_blk - 1)

    half_rows = pl.ds(pl.multiple_of(core * (lay.rows // 2), lay.rows // 2), lay.rows // 2)

    def slot_from(owner, at):
        return lax.rem(owner - at + n_blk, n_blk)

    def hidden_copy(peer):
        src = wg.at[0, :, half_rows]
        dst = wg.at[slot_from(z, peer), :, half_rows]
        return on_line(src, dst, send.at[sent["hidden"]], recv.at[here_at["hidden"]], peer)

    def hidden_on():
        view = wg.at[pl.ds(1, n_blk - 1), :, half_rows]
        return on_plane(view, view, send.at[sent["hidden on"]], recv.at[here_at["hidden on"]], sibling)

    def list_copy(peer):
        return on_plane(lists, asked.at[me], send.at[sent["lists"]], recv.at[here_at["lists"]], peer)

    line_peers(lambda peer: hidden_copy(peer).start())
    plane_peers(lambda peer: list_copy(peer).start())
    asked[me] = lists[...]

    def dyn_h_copy(peer):
        return on_line(dyn_h.at[dyn_e], dhg.at[z], send.at[sent["dyn h"]], recv.at[here_at["dyn h"]], peer)

    def dyn_m_copy(peer):
        return on_line(dyn_m.at[dyn_e], dmg.at[z], send.at[sent["dyn m"]], recv.at[here_at["dyn m"]], peer)

    alive = live[...].astype(F32).reshape(1, lay.model)
    data = replay[...]
    sums = jnp.sum(data[0:24], axis=1, keepdims=True)
    squares = jnp.sum(data[0:24] * data[0:24], axis=1, keepdims=True)
    living = jnp.sum(alive, axis=1, keepdims=True)

    has_come(asked.at[pl.ds(0, n_dp - 1)], "lists")
    spread = (
        lax.rem(lax.broadcasted_iota(jnp.int32, (CAP, lay.real), 1), CAP)
        == lax.broadcasted_iota(jnp.int32, (CAP, lay.real), 0)
    ).astype(F32)
    here = (
        lax.broadcasted_iota(jnp.int32, (n_dp, lay.real), 1) // CAP
        == lax.broadcasted_iota(jnp.int32, (n_dp, lay.real), 0)
    )

    def in_lanes(which):
        values = asked[:, which, me, :].astype(F32)
        wide = lax.dot_general(
            values, spread, NN, precision=lax.Precision.HIGHEST, preferred_element_type=F32
        )
        return jnp.sum(jnp.where(here, wide, 0.0), axis=0, keepdims=True)

    slots = in_lanes(0)
    wanted = jnp.maximum(slots, 0.0).astype(jnp.int32)
    hot = (rows_of((lay.replay, lay.real)) == wanted).astype(BF16)
    padded = jnp.concatenate([data[0:40], jnp.zeros((8, lay.replay), F32)], 0)
    tail = jnp.concatenate([data[40:FEAT], jnp.zeros((14, lay.replay), F32)], 0)
    parts = [jnp.concatenate(pair, 0) for pair in zip(pieces(padded), pieces(tail))]
    chosen = dot(jnp.concatenate(parts, 0), hot)
    chosen = chosen[0:64] + chosen[64:128] + chosen[128:192]
    mine = me * n_blk
    bk[mine, 0:40, 0 : lay.real] = chosen[0:40]
    bk[mine, 40:FEAT, 0 : lay.real] = chosen[48:50]
    bk[mine, 42:43, 0 : lay.real] = (slots >= 0.0).astype(F32)
    bk[mine, 43:44, 0 : lay.real] = in_lanes(1)
    bk[mine, 44:48, 0 : lay.real] = jnp.zeros((4, lay.real), F32)
    bk[mine, :, lay.real : lay.width] = jnp.zeros((48, lay.width - lay.real), F32)
    bk[mine, 0:24, lay.real : lay.real + 1] = sums
    bk[mine, 0:24, lay.real + 1 : lay.real + 2] = squares
    bk[mine, 24:25, lay.real : lay.real + 1] = living

    def slot_of(block):
        line = lax.rem(block, n_blk)
        return block - line + slot_from(line, z)

    def block_line(peer):
        dst = bk.at[me * n_blk + slot_from(z, peer)]
        return on_line(bk.at[mine], dst, send.at[sent["line"]], recv.at[here_at["line"]], peer)

    def block_own(peer):
        view = bk.at[mine]
        return on_plane(view, view, send.at[sent["own"]], recv.at[here_at["own"]], peer)

    def block_plane(peer):
        view = bk.at[pl.ds(mine + 1, n_blk - 1)]
        return on_plane(view, view, send.at[sent["plane"]], recv.at[here_at["plane"]], peer)

    plane_peers(lambda peer: block_own(peer).start())
    line_peers(lambda peer: block_line(peer).start())

    @pl.when(is_dyn)
    def _():
        line_peers(lambda peer: dyn_h_copy(peer).start())
        line_peers(lambda peer: dyn_m_copy(peer).start())

    bias[...] = biases[...].reshape(1, NB)
    xs[42:56, :] = jnp.zeros((14, lay.batch), F32)
    xs[0:FEAT, lay.real : lay.batch] = model[...]
    xs[42:43, lay.real : lay.batch] = alive
    nz[...] = jnp.zeros_like(nz)
    for which in range(2):
        nz[which, 1:7, :] = noise[:, which, :]
    firsts = [
        (targ_in[:, 0, :], targ_bias[0:1, 0:HSAC]),
        (targ_in[:, 1, :], targ_bias[1:2, 0:HSAC]),
        (crit_in[:, 0, :], bias[:, CB1 : CB1 + HSAC]),
        (crit_in[:, 1, :], bias[:, CB1 + HSAC : CB1 + 2 * HSAC]),
        (act_in[...], bias[:, AB1 : AB1 + HSAC]),
    ]
    w1f[...] = jnp.zeros_like(w1f)
    for net, (weights, offset) in enumerate(firsts):
        w1f[net, 0 : weights.shape[0], :] = rounded(weights)
        for at, piece in enumerate(pieces(offset)):
            w1f[net, IN + at : IN + at + 1, :] = piece.astype(F32)
        w1t[net] = (0.5 * w1f[net].T).astype(BF16)
    for k in range(2):
        w1n[k] = w1f[2 + k, 16:32, :].astype(BF16)
    for net in range(2):
        w2t[net] = (0.5 * rounded(targ_hidden[net])).T.astype(BF16)
    has_come(wg.at[pl.ds(0, n_blk - 1), :, half_rows], "hidden")
    hidden_on().start()

    rowbuf[...] = jnp.zeros_like(rowbuf)
    rowbuf[0:1, :] = targ_bias[0:1, HSAC : 2 * HSAC]
    rowbuf[1:2, :] = targ_bias[1:2, HSAC : 2 * HSAC]
    rowbuf[2:3, :] = bias[:, CB2 : CB2 + HSAC]
    rowbuf[3:4, :] = bias[:, CB2 + HSAC : CB2 + 2 * HSAC]
    rowbuf[4:5, :] = bias[:, AB2 : AB2 + HSAC]
    rowbuf[5:7, :] = rounded(crit_out[...])
    columns = 0.5 * rowbuf[...].T
    for at in range(7):
        wide[at] = jnp.broadcast_to(columns[:, at : at + 1], (HSAC, 128))
    rowbuf[...] = jnp.zeros_like(rowbuf)
    rowbuf[0:1, 1:7] = bias[:, AB3 : AB3 + ACT]
    rowbuf[0:1, 9:15] = bias[:, AB3 + ACT : AB3 + 2 * ACT]
    headcol[...] = rowbuf[:, 0:128].T
    head_f[...] = jnp.zeros_like(head_f)
    for k in range(2):
        head_f[0:1, :] = targ_out[k : k + 1, :]
        heads[k] = head_f[...].astype(BF16)
        head_f[0:1, :] = crit_out[k : k + 1, :]
        heads[2 + k] = head_f[...].astype(BF16)
    head_f[0:1, :] = jnp.zeros((1, HSAC), F32)
    head_f[1:7, :] = act_out[0:ACT, :]
    head_f[9:15, :] = act_out[ACT : 2 * ACT, :]
    heads[4] = head_f[...].astype(BF16)
    head_t[...] = (0.5 * rounded(head_f[...])).T.astype(BF16)
    for ref in (acc_h, acc_w, acc_c, acc_a, acc_m, acc_l):
        ref[...] = jnp.zeros_like(ref)

    has_come(wg.at[pl.ds(0, n_blk - 1), :, half_rows], "hidden on")
    for k in range(3):
        for block in range(n_blk):
            w2h[k, block * lay.rows : (block + 1) * lay.rows, :] = (
                0.5 * wg[slot_from(block, z), k].astype(F32)
            ).astype(BF16)
        w2t[2 + k] = w2h[k].astype(F32).T.astype(BF16)

    log_alpha = bias[:, LOGA : LOGA + 1]
    alpha = jnp.exp(log_alpha)
    last = [
        targ_bias[0:1, 2 * HSAC : 2 * HSAC + 1],
        targ_bias[1:2, 2 * HSAC : 2 * HSAC + 1],
        bias[:, CB3 : CB3 + 1],
        bias[:, CB3 + 1 : CB3 + 2],
    ]
    critic_tiles = lay.batch // CRITIC_TILE
    actor_tiles = lay.batch // ACTOR_TILE

    def act_rows(width):
        row8 = rows_of((8, width))
        return jnp.logical_and(row8 >= 1, row8 < 1 + ACT)

    def place_of(step, width):
        return pl.ds(pl.multiple_of(lax.rem(step + 1, lay.batch // width) * width, width), width)

    def ones16(width):
        return jnp.ones((16, width), BF16)

    def framed(first_row, used, where):
        row32 = rows_of((32, where.size))
        ones3 = jnp.logical_and(row32 >= IN, row32 < IN + 3).astype(F32)
        return jnp.where(row32 < used, xs[first_row : first_row + 32, where], ones3)

    def hidden(inputs, net):
        first, slope1 = gated(dot(w1t[net], inputs))
        second, slope2 = gated(dot(w2t[net], first), wide[net])
        return first, slope1, second, slope2

    def policy(inputs, which, where):
        first, slope1, second, slope2 = hidden(inputs, 4)
        out = dot(heads[4], second) + headcol[0:16, 0:1]
        bent = jnp.tanh(out[8:16])
        log_scale = -5.0 + 3.5 * (bent + 1.0)
        draw = nz[which, :, where]
        moved = jnp.exp(log_scale) * draw
        latent = out[0:8] + moved
        terms = (
            -0.5 * draw * draw
            - log_scale
            - 0.9189385
            - 2.0 * (0.6931472 - latent - softplus(-2.0 * latent))
        )
        used = act_rows(where.size)
        log_prob = jnp.sum(jnp.where(used, terms, 0.0), axis=0, keepdims=True)
        action = jnp.where(used, jnp.tanh(latent), 0.0)
        return action, log_prob, bent, moved, (first, slope1, second, slope2)

    def with_action(inputs, action):
        middle_rows = jnp.where(act_rows(action.shape[1]), action, inputs[16:24])
        return jnp.concatenate([inputs[0:16], middle_rows, inputs[24:32]], 0).astype(BF16)

    def critic(inputs, net):
        kept = hidden(inputs, net)
        value = dot(heads[net], kept[2])[0:1] + last[net]
        return value, kept

    def add_hidden(k, first, grad):
        acc_h[k] += dot(jnp.concatenate([first, ones16(grad.shape[1])], 0), grad, NT)

    has_come(bk.at[pl.ds(0, n_blk - 1)], "line")
    plane_peers(lambda peer: block_plane(peer).start())

    def critic_pass(k, now_in, where, target):
        weight = xs[42:43, where]
        value, (c1, dc1, c2, dc2) = critic(now_in, 2 + k)
        miss = value - target
        g3 = rounded(weight * miss)
        g3_rows = jnp.where(rows_of((16, CRITIC_TILE)) == 0, g3, 0.0).astype(BF16)
        acc_c[k] += dot(g3_rows, c2, NT)
        acc_m[:, 16 + 16 * k : 32 + 16 * k] += dot(ones16(CRITIC_TILE), g3_rows, NT)
        g2 = outer_sloped(wide[5 + k], g3, dc2)
        add_hidden(k, c1, g2)
        g1 = sloped(dot(w2h[k], g2), dc1)
        acc_w[k] += dot(now_in, g1, NT)
        acc_l[0:1, 0:CRITIC_TILE] += weight * (0.5 * miss * miss)

    def put_matrix(k):
        for chunk in range(n_dp):
            tile = chunk * lay.mat
            side, row = tile // 32, tile % 32
            grids[k][chunk, 0 : lay.mat] = acc_h[
                k, row * 8 : (row + lay.mat) * 8, side * 128 : (side + 1) * 128
            ].reshape(lay.mat, 8, 128)

    def put(row, value):
        for at in range(value.shape[0] // 8):
            for side in range(value.shape[1] // 128):
                tile = side * (R_SMALL // 8) + row // 8 + at
                grid_1[tile // lay.sml, lay.mat + tile % lay.sml] = value[
                    at * 8 : at * 8 + 8, side * 128 : (side + 1) * 128
                ]

    def plane_sum(group, peer):
        name = ("plane sum", group)
        return on_plane(
            grids[group].at[peer], froms[group].at[me], send.at[sent[name]], recv.at[here_at[name]], peer
        )

    def line_part(part):
        return (1, pl.ds(lay.mat, lay.sml)) if part == 3 else (part, pl.ds(0, lay.mat))

    def line_sum(part, peer):
        group, tiles = line_part(part)
        name = ("line sum", part)
        src, dst = zfs[group].at[tiles], zrs[group].at[z, tiles]
        return on_line(src, dst, send.at[sent[name]], recv.at[here_at[name]], peer)

    def line_bytes(part):
        group, tiles = line_part(part)
        return zrs[group].at[pl.ds(0, n_blk - 1), tiles]

    first_tile = me * lay.mat
    side = first_tile // 32
    row_tile = lax.rem(first_tile, 32)
    keeper_z = row_tile * 8 // lay.rows
    local_tile = row_tile - keeper_z * (lay.rows // 8)

    def fold_plane(group):
        has_come(froms[group].at[pl.ds(0, n_dp - 1)], ("plane sum", group))
        froms[group][me] = grids[group][me]
        whole = froms[group][0]
        for at in range(1, n_dp):
            whole = whole + froms[group][at]
        zfs[group][...] = whole

        @pl.when(z == keeper_z)
        def _():
            held_rows = pl.ds(pl.multiple_of(local_tile * 8, 8), lay.mat * 8)
            held_lanes = pl.ds(pl.multiple_of(side * 128, 128), 128)
            old = sac_m[group, held_rows, held_lanes].reshape(lay.mat, 8, 128)
            zfs[group][0 : lay.mat] += (MOMENTUM * count[0:1, 0:1]).reshape(1, 1, 1) * old

        for part in (1, 3) if group == 1 else (group,):
            line_peers(lambda peer: line_sum(part, peer).start())

    def tile_copy(k, peer):
        name = ("tiles", k)
        src = totals[k].at[pl.ds(0, lay.mat)]
        return on_plane(src, mg.at[k, me], send.at[sent[name]], recv.at[here_at[name]], peer)

    def small_copy(peer):
        return on_plane(
            sum_1.at[pl.ds(lay.mat, lay.sml)], small.at[pl.ds(me * lay.sml, lay.sml)],
            send.at[sent["small"]], recv.at[here_at["small"]], peer,
        )

    def fold_end(part):
        group, tiles = line_part(part)
        has_come(line_bytes(part), ("line sum", part))
        zrs[group][z, tiles] = zfs[group][tiles]
        whole = zrs[group][0, tiles]
        for block in range(1, n_blk):
            whole = whole + zrs[group][block, tiles]
        totals[group][tiles] = whole
        if part == 3:
            plane_peers(lambda peer: small_copy(peer).start())
            small[pl.ds(me * lay.sml, lay.sml)] = whole
        else:
            plane_peers(lambda peer: tile_copy(part, peer).start())
            mg[part, me] = whole

    def chain(group):
        def end():
            for part in (1, 3) if group == 1 else (group,):
                fold_end(part)

        return [
            lambda: plane_peers(lambda peer: plane_sum(group, peer).start()),
            lambda: fold_plane(group),
            end,
        ]

    chains = [chain(group) for group in range(3)]
    per = DYN_TILE // lay.real
    dyn_tiles = lay.n_dev // per

    def take(slots, step):
        for at, events in slots.items():
            @pl.when(step == at)
            def _():
                for event in events:
                    event()

    @pl.loop(0, actor_tiles)
    def _(step):
        @pl.when(step == actor_tiles - 1)
        def _():
            has_come(bk.at[pl.ds(0, n_dp - 1)], "own")
            lanes = lax.broadcasted_iota(jnp.int32, (48, lay.width), 1) // CAP

            def gather(owner, total):
                turned = pltpu.roll(
                    bk[owner * n_blk], lax.rem((owner - me) * CAP + lay.width, lay.width), axis=1
                )
                return jnp.where(lanes == owner, turned, total)

            own = lax.fori_loop(0, n_dp, gather, jnp.zeros((48, lay.width), F32))
            xs[0:48, 0 : lay.real] = own[:, 0 : lay.real]

        where = place_of(step, ACTOR_TILE)
        now_f = framed(0, IN, where)
        now_in = now_f.astype(BF16)
        weight = xs[42:43, where]
        action, log_prob, bent, moved, (a1, da1, a2, da2) = policy(now_in, 0, where)
        judged_in = with_action(now_f, action)
        loss = alpha * log_prob - log_alpha * (log_prob + TARGET_ENTROPY)
        grad_action = jnp.zeros((8, ACTOR_TILE), F32)
        used = act_rows(ACTOR_TILE)
        for k in range(2):
            judged, (_, df1, _, df2) = critic(judged_in, 2 + k)
            loss -= 0.5 * judged
            g2 = outer_sloped(wide[5 + k], -0.5 * weight, df2)
            g1 = sloped(dot(w2h[k], g2), df1)
            grad_action += dot(w1n[k], g1)[0:8]
        grad_latent = 2.0 * alpha * weight * action + grad_action * (1.0 - action * action)
        grad_scale = grad_latent * moved - alpha * weight
        grad_bent = grad_scale * 3.5 * (1.0 - bent * bent)
        g3 = jnp.concatenate(
            [jnp.where(used, grad_latent, 0.0), jnp.where(used, grad_bent, 0.0)], 0
        ).astype(BF16)
        acc_a[...] += dot(g3, a2, NT)
        acc_m[:, 0:16] += dot(ones16(ACTOR_TILE), g3, NT)
        g2 = sloped(dot(head_t[...], g3), da2)
        add_hidden(2, a1, g2)
        g1 = sloped(dot(w2h[2], g2), da1)
        acc_w[2] += dot(now_in, g1, NT)
        acc_l[1:2, 0:ACTOR_TILE] += weight * loss
        acc_l[2:3, 0:ACTOR_TILE] += weight * (log_prob + TARGET_ENTROPY)

    put_matrix(2)
    chains[2][0]()

    @pl.loop(0, critic_tiles)
    def _(step):
        where = place_of(step, CRITIC_TILE)
        now_in = framed(0, IN, where).astype(BF16)
        next_f = framed(24, OBS, where)
        reward = xs[23:24, where]
        done = xs[41:42, where]
        next_action, next_prob, _, _, _ = policy(next_f.astype(BF16), 1, where)
        aim_in = with_action(next_f, next_action)
        aim = jnp.minimum(critic(aim_in, 0)[0], critic(aim_in, 1)[0])
        target = reward + DISCOUNT * (1.0 - done) * (aim - alpha * next_prob)
        ys[0:1, where] = target
        critic_pass(0, now_in, where, target)

    put_matrix(0)
    chains[0][0]()

    has_come(bk.at[pl.ds(0, (n_dp - 1) * (n_blk - 1))], "plane")
    lane0 = lay.real // 128 * 128

    def add_block(at, carry):
        sides, fills = carry
        slot = slot_of(at)
        return sides + bk[slot, 0:32, lane0 : lane0 + 128], fills + bk[slot, 40:48, 0 : lay.real]

    sides, fills = lax.fori_loop(
        0, lay.n_dev, add_block, (jnp.zeros((32, 128), F32), jnp.zeros((8, lay.real), F32))
    )
    at = lay.real - lane0
    rows_all = float(lay.replay * lay.n_dev)
    centre = sides[0:24, at : at + 1] / rows_all
    scale = lax.rsqrt(sides[0:24, at + 1 : at + 2] / rows_all - centre * centre + 1e-6)
    total = sides[24:25, at : at + 1] + jnp.sum(fills[2:3, :], axis=1, keepdims=True)
    count[...] = jnp.broadcast_to(total, (8, 128))

    chains[2][1]()

    @pl.loop(0, critic_tiles)
    def _(step):
        where = place_of(step, CRITIC_TILE)
        critic_pass(1, framed(0, IN, where).astype(BF16), where, ys[0:1, where])

    put_matrix(1)
    for k in range(3):
        put(R_IN + 24 * k, acc_w[k, 0:24, :])
    put(R_HEAD, acc_a[...])
    rowbuf[0:1, :] = acc_c[0, 0:1, :]
    rowbuf[1:2, :] = acc_c[1, 0:1, :]
    for k in range(3):
        rowbuf[2 + k : 3 + k, :] = acc_h[k, HSAC : HSAC + 1, :]
    put(R_OUT, rowbuf[...])
    folded = jnp.sum(acc_l[...], axis=1, keepdims=True)
    rowbuf[...] = jnp.zeros_like(rowbuf)
    rowbuf[0:1, 0:48] = acc_m[0:1, :]
    rowbuf[0:1, 64:65] = folded[0:1] + folded[1:2]
    rowbuf[0:1, 65:66] = folded[2:3]
    put(R_MISC, rowbuf[...])
    put(R_MISC + 8, jnp.zeros((R_SMALL - R_MISC - 8, HSAC), F32))
    chains[1][0]()

    def dyn_bias(start, width):
        row = jnp.zeros((1, width), F32)
        for e in range(MEMBERS):
            row = jnp.where(me == e, bias[:, start + width * e : start + width * (e + 1)], row)
        return row

    @pl.when(is_dyn)
    def _():
        w1f[0] = jnp.zeros((32, HSAC), F32)
        w1f[0, 0:IN, 0:HDYN] = rounded(dyn_in[dyn_e])
        for at, piece in enumerate(pieces(dyn_bias(DB1, HDYN))):
            w1f[0, IN + at : IN + at + 1, 0:HDYN] = piece.astype(F32)
        w1t[0] = (0.5 * w1f[0].T).astype(BF16)
        rowbuf[...] = jnp.zeros_like(rowbuf)
        rowbuf[0:1, 0:HDYN] = dyn_bias(DB2, HDYN)
        head_row = dyn_bias(DB3, DOUT)
        rowbuf[1:2, 0:HALF] = head_row[:, 0:HALF]
        rowbuf[1:2, 24 : 24 + HALF] = head_row[:, HALF:DOUT]
        rowbuf[2:3, 0:HALF] = bias[:, MAXLV : MAXLV + HALF]
        rowbuf[3:4, 0:HALF] = bias[:, MINLV : MINLV + HALF]
        dcols[...] = rowbuf[...].T
        wide[0] = jnp.broadcast_to(0.5 * dcols[:, 0:1], (HSAC, 128))
        dpack[...] = jnp.zeros_like(dpack)
        dpack[0:HALF, 0:HDYN] = dyn_out[dyn_e, 0:HALF, :]
        dpack[24 : 24 + HALF, 0:HDYN] = dyn_out[dyn_e, HALF:DOUT, :]
        dhead[...] = dpack[0:48, :].astype(BF16)
        dhead_t[...] = (0.5 * rounded(dpack[0:48, :])).T.astype(BF16)
        dpack[...] = jnp.zeros_like(dpack)

        has_come(dhg.at[pl.ds(0, n_blk - 1)], "dyn h")
        has_come(dmg.at[pl.ds(0, n_blk - 1)], "dyn m")
        dhg[z] = dyn_h[dyn_e]
        dmg[z] = dyn_m[dyn_e]
        dmat[...] = jnp.zeros_like(dmat)
        for block in range(n_blk):
            dmat[block * lay.drows : (block + 1) * lay.drows, 0:HDYN] = 0.5 * rounded(dhg[block])
        w2h[0] = dmat[...].astype(BF16)
        w2t[0] = dmat[...].T.astype(BF16)
        for ref in (dacc_h, dacc_w, dacc_o, dacc_m, dacc_b, dacc_l):
            ref[...] = jnp.zeros_like(ref)

    in_dyn = {}
    for at, event in ((1, chains[2][2]), (1, chains[0][1]), (dyn_tiles - 1, chains[1][1])):
        in_dyn.setdefault(min(at, dyn_tiles - 1), []).append(event)

    @pl.loop(0, dyn_tiles)
    def _(tile):
        take(in_dyn, tile)

        @pl.when(is_dyn)
        def _():
            for at in range(per):
                slot = slot_of(tile * per + at)
                xt[:, at * lay.real : (at + 1) * lay.real] = bk[slot, :, 0 : lay.real]
            now = xt[0:24, :]
            later = xt[24:48, :]
            row24 = rows_of((24, DYN_TILE))
            scaled = jnp.where(row24 < IN, (now - centre) * scale, 1.0)
            inputs = jnp.concatenate([scaled, (rows_of((8, DYN_TILE)) < 2).astype(F32)], 0).astype(BF16)
            first, slope1 = gated(dot(w1t[0], inputs))
            second, slope2 = gated(dot(w2t[0], first), wide[0])
            out = dot(dhead[...], second) + dcols[0:48, 1:2]
            used = row24 < HALF
            upper = dcols[0:24, 2:3]
            lower = dcols[0:24, 3:4]
            gap1 = upper - out[24:48]
            gap2 = upper - softplus(gap1) - lower
            log_var = lower + softplus(gap2)
            error = out[0:24] - jnp.where(row24 == OBS, now[23:24], later - now)
            inverse = jnp.exp(-log_var)
            weight = xt[42:43, :] * (xt[43:44, :] == me.astype(F32)).astype(F32)
            spread_term = error * error * inverse
            nll = jnp.sum(jnp.where(used, spread_term + log_var, 0.0), axis=0, keepdims=True)
            dacc_l[0:1, :] += weight * nll
            grad_mu = 2.0 * weight * error * inverse
            grad_lv = weight * (1.0 - spread_term)
            open1 = sigmoid(gap1)
            open2 = sigmoid(gap2)
            grad_lv1 = grad_lv * open2
            dacc_b[0] += jnp.where(used, grad_lv1 * (1.0 - open1), 0.0)
            dacc_b[1] += jnp.where(used, grad_lv * (1.0 - open2), 0.0)
            g3 = jnp.concatenate(
                [jnp.where(used, grad_mu, 0.0), jnp.where(used, grad_lv1 * open1, 0.0)], 0
            ).astype(BF16)
            dacc_o[...] += dot(g3, second, NT)
            dacc_m[...] += dot(ones16(DYN_TILE), g3, NT)
            g2 = sloped(dot(dhead_t[...], g3), slope2)
            dacc_h[...] += dot(jnp.concatenate([first, ones16(DYN_TILE)], 0), g2, NT)
            g1 = sloped(dot(w2h[0], g2), slope1)
            dacc_w[...] += dot(inputs, g1, NT)

    out_of = {"pack": dyn_s, "x": dyn_x}

    def member_copy(name, src, owner, kind, sem, peer):
        return on_plane(src, out_of[name].at[owner], send.at[sent[name, kind]], recv.at[sem], peer)

    def give(name, src):
        like_peers(
            lambda peer: member_copy(name, src, dyn_e, "own", here_at[name, "like"] + dyn_e, peer).start()
        )
        member_copy(name, src, dyn_e, "own", here_at[name, "sibling"], sibling).start()

    def hand_on(name):
        def body(peer):
            @pl.when(peer < MEMBERS)
            def _():
                owner = jnp.minimum(peer, MEMBERS - 1)
                view = out_of[name].at[owner]
                member_copy(name, view, owner, "on", here_at[name, "like"] + owner, sibling).wait_recv()
                member_copy(name, view, owner, "on", here_at[name, "sibling"], sibling).start()

        like_peers(body)

    even, odd = (MEMBERS + 1) // 2, MEMBERS // 2
    handed = even - core * (even - odd) - jnp.where(is_dyn, 1, 0)

    def from_sibling(name):
        for side, number in ((0, odd), (1, even)):
            @pl.when(core == side)
            def _():
                has_come(out_of[name].at[pl.ds(0, number)], (name, "sibling"))

    def gave(name):
        @pl.when(is_dyn)
        def _():
            for begin in range(0, n_dp // 2, MEMBERS):
                number = min(MEMBERS, n_dp // 2 - begin)
                has_sent(out_of[name].at[pl.ds(0, number)], (name, "own"))

        for number in (even, even - 1, even - 2):
            @pl.when(handed == number)
            def _():
                has_sent(out_of[name].at[pl.ds(0, number)], (name, "on"))

    def line_rows(ref):
        rows = ref[0 : lay.drows, 0:HDYN]
        for block in range(1, n_blk):
            rows = jnp.where(z == block, ref[block * lay.drows : (block + 1) * lay.drows, 0:HDYN], rows)
        return rows

    mine_rows = pl.ds(pl.multiple_of(z * lay.rows, lay.rows), lay.rows)

    def take_matrix(k):
        has_come(mg.at[k, pl.ds(0, n_dp - 1)], ("tiles", k))
        for chunk in range(n_dp):
            tile = chunk * lay.mat
            half, row = tile // 32, tile % 32
            at = slice(row * 8, (row + lay.mat) * 8)
            piece = mg[k, chunk].reshape(lay.mat * 8, 128)
            mat[k, at, half * 128 : (half + 1) * 128] = piece / total
        normalise(mat.at[k])

    chains[0][2]()

    @pl.when(is_dyn)
    def _():
        dpack[D_IN : D_IN + 24, :] = dacc_w[0:24, :]
        dpack[D_OUT : D_OUT + HALF, :] = dacc_o[0:HALF, :]
        dpack[D_OUT + HALF : D_OUT + DOUT, :] = dacc_o[24 : 24 + HALF, :]
        dpack[D_B2 : D_B2 + 1, :] = dacc_h[HSAC : HSAC + 1, :]
        dpack[D_B3 : D_B3 + 1, 0:48] = dacc_m[0:1, :]
        lanes = lax.broadcasted_iota(jnp.int32, (24, 128), 1)
        bound = jnp.where(
            lanes == 0,
            jnp.sum(dacc_b[0], axis=1, keepdims=True),
            jnp.where(lanes == 1, jnp.sum(dacc_b[1], axis=1, keepdims=True), 0.0),
        )
        dpack[D_UP : D_UP + 2, 0:24] = bound.T[0:2, :]
        dpack[D_LOSS : D_LOSS + 1, 0:128] = jnp.broadcast_to(
            jnp.sum(dacc_l[0:1, :], axis=1, keepdims=True), (1, 128)
        )
        dpack[D_HID : D_HID + lay.drows, 0:HDYN] = line_rows(dacc_h)
        dyn_s[dyn_e] = dpack[...]
        give("pack", dpack)
        dmat[...] = jnp.zeros_like(dmat)
        for block in range(n_blk):
            at = slice(block * lay.drows, (block + 1) * lay.drows)
            dmat[at, 0:HDYN] = MOMENTUM * dmg[block] + dacc_h[at, 0:HDYN] / total
        normalise(dmat)

    def sum_end(step):
        pl.when(step == 2)(chains[1][2])

    take_matrix(2)

    @pl.when(is_dyn)
    def _():
        schulz([dmat, mat.at[2]], NS_ITERS, sum_end)
        rows = line_rows(dmat)
        drow_x[...] = rows
        dyn_x[dyn_e] = rows
        give("x", drow_x)

    @pl.when(jnp.logical_not(is_dyn))
    def _():
        schulz([mat.at[2]], NS_ITERS, sum_end)

    def sent_early():
        has_sent(wg.at[pl.ds(0, n_blk - 1), :, half_rows], "hidden")
        has_sent(wg.at[pl.ds(0, n_blk - 1), :, half_rows], "hidden on")
        has_sent(asked.at[pl.ds(0, n_dp - 1)], "lists")
        has_sent(bk.at[pl.ds(0, n_dp - 1)], "own")
        has_sent(bk.at[pl.ds(0, n_blk - 1)], "line")
        has_sent(bk.at[pl.ds(0, (n_dp - 1) * (n_blk - 1))], "plane")

        @pl.when(is_dyn)
        def _():
            has_sent(dhg.at[pl.ds(0, n_blk - 1)], "dyn h")
            has_sent(dmg.at[pl.ds(0, n_blk - 1)], "dyn m")

        for group in range(3):
            has_sent(froms[group].at[pl.ds(0, n_dp - 1)], ("plane sum", group))
        for part in range(4):
            has_sent(line_bytes(part), ("line sum", part))

    def pass_on(step):
        pl.when(step == 2)(functools.partial(hand_on, "pack"))
        pl.when(step == NS_ITERS - 1)(functools.partial(hand_on, "x"))

    for k in range(2):
        take_matrix(k)
    schulz([mat.at[0], mat.at[1]], NS_ITERS, pass_on)
    for k in range(3):
        sac_x[k] = mat[k, mine_rows, :]
        for half in range(2):
            for piece in range(lay.rows // 8 // lay.mat):
                chunk = (half * 32 + z * (lay.rows // 8)) // lay.mat + piece
                sac_g[half, k, piece * lay.mat : (piece + 1) * lay.mat] = mg[k, chunk]

    sent_early()
    has_come(small.at[pl.ds(0, (n_dp - 1) * lay.sml)], "small")
    from_sibling("pack")
    from_sibling("x")

    has_sent(small.at[pl.ds(0, (n_dp - 1) * lay.sml)], "small")
    gave("pack")
    gave("x")

    for k in range(3):
        has_sent(mg.at[k, pl.ds(0, n_dp - 1)], ("tiles", k))


def adamw(weights, first, second, gradient):
    first = BETA_FIRST * first + (1.0 - BETA_FIRST) * gradient
    second = BETA_SECOND * second + (1.0 - BETA_SECOND) * gradient * gradient
    first_hat = first / (1.0 - BETA_FIRST**STEP)
    second_hat = second / (1.0 - BETA_SECOND**STEP)
    step = first_hat / (jnp.sqrt(second_hat) + 1e-8) + ADAM_DECAY * weights
    return weights - ADAM_RATE * step, first, second


def update_kernel(*refs):
    (
        sac_g, sac_x, dyn_x, dyn_s, small, count, sac_h, dyn_h, dyn_m,
        ci, ci_m, ci_v, ai, ai_m, ai_v, di, di_m, di_v, co, co_m, co_v, ao, ao_m, ao_v,
        do, do_m, do_v, bi, bi_m, bi_v,
        sac_new, sac_mom, dyn_new, dyn_mom, ci_n, ci_mn, ci_vn, ai_n, ai_mn, ai_vn, di_n, di_mn,
        di_vn, co_n, co_mn, co_vn, ao_n, ao_mn, ao_vn, do_n, do_mn, do_vn, bi_n, bi_mn, bi_vn,
        loss, counted, bg,
    ) = refs
    total = count[0:1, 0:1]
    for k in range(3):
        for side in range(2):
            tiles = sac_g[side, k].reshape(sac_mom.shape[1], 128)
            sac_mom[k, :, side * 128 : (side + 1) * 128] = tiles / total
    sac_new[...] = sac_h[...] * (1.0 - MUON_RATE * MUON_DECAY) - MUON_RATE * sac_x[...]
    dyn_rows = dyn_s[:, D_HID : D_HID + dyn_m.shape[1], 0:HDYN]
    dyn_mom[...] = MOMENTUM * dyn_m[...] + dyn_rows / total.reshape(1, 1, 1)
    dyn_new[...] = dyn_h[...] * (1.0 - MUON_RATE * MUON_DECAY) - MUON_RATE * dyn_x[...]

    def rows(row, number):
        sides = []
        for side in range(2):
            at = side * (R_SMALL // 8) + row // 8
            sides.append(small[at : at + -(-number // 8)].reshape(-1, 128))
        return jnp.concatenate(sides, 1)

    def store(outs, at, values):
        for out, value in zip(outs, values):
            out[at] = value

    outs = (ci_n, ci_mn, ci_vn)
    for k in range(2):
        at = (slice(None), k, slice(None))
        grad = rows(R_IN + 24 * k, 24)
        bg[:, CB1 + HSAC * k : CB1 + HSAC * (k + 1)] = grad[IN : IN + 1]
        store(outs, at, adamw(ci[at], ci_m[at], ci_v[at], grad[0:IN] / total))
    grad = rows(R_IN + 48, 24)
    bg[:, AB1 : AB1 + HSAC] = grad[IN : IN + 1]
    store((ai_n, ai_mn, ai_vn), ..., adamw(ai[...], ai_m[...], ai_v[...], grad[0:OBS] / total))
    grad = rows(R_HEAD, 16)
    for at, row in ((slice(0, ACT), slice(1, 1 + ACT)), (slice(ACT, 2 * ACT), slice(9, 9 + ACT))):
        store((ao_n, ao_mn, ao_vn), at, adamw(ao[at], ao_m[at], ao_v[at], grad[row] / total))
    grad = rows(R_OUT, 8)
    store((co_n, co_mn, co_vn), ..., adamw(co[...], co_m[...], co_v[...], grad[0:2] / total))
    bg[:, CB2 : CB2 + HSAC] = grad[2:3]
    bg[:, CB2 + HSAC : CB2 + 2 * HSAC] = grad[3:4]
    bg[:, AB2 : AB2 + HSAC] = grad[4:5]
    grad = rows(R_MISC, 8)
    bg[:, CB3 : CB3 + 1] = grad[0:1, 16:17]
    bg[:, CB3 + 1 : CB3 + 2] = grad[0:1, 32:33]
    bg[:, AB3 : AB3 + ACT] = grad[0:1, 1 : 1 + ACT]
    bg[:, AB3 + ACT : AB3 + 2 * ACT] = grad[0:1, 9 : 9 + ACT]
    bg[:, LOGA : LOGA + 1] = -grad[0:1, 65:66]
    total_loss = grad[0:1, 64:65]
    up = jnp.zeros((1, HALF), F32)
    low = jnp.zeros((1, HALF), F32)
    for e in range(MEMBERS):
        pack = dyn_s[e]
        total_loss = total_loss + pack[D_LOSS : D_LOSS + 1, 0:1]
        up = up + pack[D_UP : D_UP + 1, 0:HALF]
        low = low + pack[D_LOW : D_LOW + 1, 0:HALF]
        bg[:, DB1 + HDYN * e : DB1 + HDYN * (e + 1)] = pack[IN : IN + 1, 0:HDYN]
        bg[:, DB2 + HDYN * e : DB2 + HDYN * (e + 1)] = pack[D_B2 : D_B2 + 1, 0:HDYN]
        bg[:, DB3 + DOUT * e : DB3 + DOUT * e + HALF] = pack[D_B3 : D_B3 + 1, 0:HALF]
        bg[:, DB3 + DOUT * e + HALF : DB3 + DOUT * (e + 1)] = pack[D_B3 : D_B3 + 1, 24 : 24 + HALF]
        grad = pack[0:IN, 0:HDYN] / total
        store((di_n, di_mn, di_vn), e, adamw(di[e], di_m[e], di_v[e], grad))
        grad = pack[D_OUT : D_OUT + DOUT, 0:HDYN] / total
        store((do_n, do_mn, do_vn), e, adamw(do[e], do_m[e], do_v[e], grad))
    bg[:, MAXLV : MAXLV + HALF] = up
    bg[:, MINLV : MINLV + HALF] = low
    lane = lax.broadcasted_iota(jnp.int32, (1, NB), 1)
    bounds = jnp.where(
        jnp.logical_and(lane >= MAXLV, lane < MINLV),
        BOUND_WEIGHT,
        jnp.where(jnp.logical_and(lane >= MINLV, lane < LOGA), -BOUND_WEIGHT, 0.0),
    )
    grad = bg[...] / total + bounds
    flat = [ref[...].reshape(1, NB) for ref in (bi, bi_m, bi_v)]
    store((bi_n, bi_mn, bi_vn), ..., [value.reshape(NB) for value in adamw(*flat, grad)])
    loss[...] = total_loss
    counted[...] = total


def shards(
    lay, replay, model_rows, requests, member_of, model_live, noise, sac_hidden, sac_hidden_mom,
    dyn_hidden, dyn_hidden_mom, crit_in, crit_in_m, crit_in_v, act_in, act_in_m, act_in_v, dyn_in,
    dyn_in_m, dyn_in_v, crit_out, crit_out_m, crit_out_v, act_out, act_out_m, act_out_v, dyn_out,
    dyn_out_m, dyn_out_v, biases, biases_m, biases_v, targ_in, targ_hidden, targ_out, targ_bias,
):
    n_dp, n_blk = lay.n_dp, lay.n_blk
    spec = pl.BlockSpec(memory_space=pltpu.VMEM)

    def flip(value):
        return jnp.transpose(value, (1, 0, 2))

    def swap(value):
        return jnp.swapaxes(value, -1, -2)

    def kept(value):
        return pltpu.with_memory_space_constraint(value, pltpu.VMEM)

    inputs = (
        replay, model_rows, requests, member_of, model_live, jnp.transpose(noise, (2, 0, 1)),
        sac_hidden, sac_hidden_mom, dyn_hidden, dyn_hidden_mom, flip(crit_in), act_in, dyn_in,
        crit_out, swap(act_out), swap(dyn_out), biases, flip(targ_in), targ_hidden, targ_out,
        targ_bias,
    )
    shape = jax.ShapeDtypeStruct
    rows, drows = lay.rows, lay.drows
    out_shape = (
        pltpu.VMEM((2, 3, rows // 8, 8, 128), F32),
        pltpu.VMEM((3, rows, HSAC), F32),
        pltpu.VMEM((MEMBERS, drows, HDYN), F32),
        pltpu.VMEM((MEMBERS, D_ROWS, HSAC), F32),
        pltpu.VMEM((32, 8, 128), F32),
        pltpu.VMEM((8, 128), F32),
    )

    def vm(*dims, kind=F32):
        return pltpu.VMEM(dims, kind)

    scratch = [
        vm(n_blk, 3, rows, HSAC, kind=BF16),
        vm(2, n_dp, CAP, kind=jnp.int32),
        vm(n_dp, 2, n_dp, CAP, kind=jnp.int32),
        vm(n_blk, drows, HDYN),
        vm(n_blk, drows, HDYN),
        vm(lay.n_dev, 48, lay.width),
        vm(56, lay.batch),
        vm(2, 8, lay.batch),
        vm(8, lay.batch),
        vm(5, 32, HSAC),
        vm(5, HSAC, 32, kind=BF16),
        vm(2, 16, HSAC, kind=BF16),
        vm(5, HSAC, HSAC, kind=BF16),
        vm(3, HSAC, HSAC, kind=BF16),
        vm(5, 16, HSAC, kind=BF16),
        vm(HSAC, 16, kind=BF16),
        vm(16, HSAC),
        vm(8, HSAC),
        vm(7, HSAC, 128),
        vm(128, 8),
        vm(3, HSAC + 16, HSAC),
        vm(3, 32, HSAC),
        vm(2, 16, HSAC),
        vm(16, HSAC),
        vm(16, 48),
        vm(8, max(CRITIC_TILE, ACTOR_TILE)),
        *[vm(n_dp, chunk, 8, 128) for chunk in lay.chunks],
        *[vm(n_dp, chunk, 8, 128) for chunk in lay.chunks],
        *[vm(n_blk, chunk, 8, 128) for chunk in lay.chunks],
        *[vm(chunk, 8, 128) for chunk in lay.chunks],
        *[vm(chunk, 8, 128) for chunk in lay.chunks],
        vm(3, n_dp, lay.mat, 8, 128),
        vm(3, HSAC, HSAC),
        vm(HSAC, 8),
        vm(HSAC + 16, HSAC),
        vm(32, HSAC),
        vm(48, HSAC),
        vm(16, 48),
        vm(2, 24, DYN_TILE),
        vm(8, DYN_TILE),
        vm(48, DYN_TILE),
        vm(HSAC, HSAC),
        vm(D_ROWS, HSAC),
        vm(drows, HDYN),
        vm(1, NB),
        vm(48, HSAC, kind=BF16),
        vm(HSAC, 48, kind=BF16),
    ]
    scratch += [pltpu.SemaphoreType.DMA((lay.departures,)), pltpu.SemaphoreType.DMA((lay.arrivals,))]
    varying = 4 * (lay.n_dev * 48 * lay.width + 72 * lay.batch + 48 * lay.replay)
    gathered = pl.pallas_call(
        functools.partial(main_kernel, lay),
        out_shape=out_shape,
        in_specs=[spec] * len(inputs),
        out_specs=[spec] * len(out_shape),
        scratch_shapes=scratch,
        compiler_params=pltpu.CompilerParams(
            collective_id=0, has_side_effects=True, vmem_limit_bytes=26 * 2**20 + varying
        ),
        name="step",
    )(*[pltpu.with_memory_space_constraint(value, pltpu.HBM) for value in inputs])
    params = (
        sac_hidden, dyn_hidden, dyn_hidden_mom,
        flip(crit_in), flip(crit_in_m), flip(crit_in_v), act_in, act_in_m, act_in_v,
        dyn_in, dyn_in_m, dyn_in_v, crit_out, crit_out_m, crit_out_v,
        swap(act_out), swap(act_out_m), swap(act_out_v),
        swap(dyn_out), swap(dyn_out_m), swap(dyn_out_v), biases, biases_m, biases_v,
    )
    new_shape = [shape(sac_hidden.shape, F32)] + [shape(value.shape, F32) for value in params]
    new_shape += [shape((1, 1), F32)] * 2
    out = pl.pallas_call(
        update_kernel,
        out_shape=tuple(new_shape),
        in_specs=[spec] * (len(gathered) + len(params)),
        out_specs=[spec] * len(new_shape),
        scratch_shapes=[vm(1, NB)],
        compiler_params=pltpu.CompilerParams(vmem_limit_bytes=16 * 2**20),
        name="update",
    )(*[kept(value) for value in gathered], *params)
    out = list(out)
    for at in (4, 5, 6):
        out[at] = flip(out[at])
    for at in (16, 17, 18, 19, 20, 21):
        out[at] = swap(out[at])
    for at in (25, 26):
        out[at] = out[at].reshape(())
    return tuple(out)


def solution(mesh):
    both = ("dp", "blk")
    sharded = (
        P(None, both), P(None, both), P(both, None), P(both, None), P(both), P(None, both, None),
    )
    hidden = (P(None, "blk", None),) * 4

    def step(replay, model_rows, *others):
        lay = Layout(mesh, replay.shape[1], model_rows.shape[1])
        return shards(lay, replay, model_rows, *others)

    return jax.shard_map(
        step,
        mesh=mesh,
        in_specs=sharded + hidden + (P(),) * 25,
        out_specs=hidden + (P(),) * 23,
        check_vma=False,
    )
```

```python
import functools

import jax
import jax.numpy as jnp
from jax import lax
from jax.experimental import pallas as pl
from jax.experimental.pallas import tpu as pltpu
from jax.sharding import PartitionSpec as P

OBS = 17
ACT = 6
IN = OBS + ACT
FEAT = 42
HDYN = 200
HSAC = 256
MEMBERS = 7
DOUT = 36
HALF = DOUT // 2
NB = 4639
NS_ITERS = 5
STEP = 10
CAP = 8
CRITIC_TILE = 640
ACTOR_TILE = 640
DYN_TILE = 512
ROWS = 32

DISCOUNT = 0.99
TARGET_ENTROPY = -6.0
BOUND_WEIGHT = 0.01
MOMENTUM = 0.95
MUON_RATE = 0.4
MUON_DECAY = 0.01
ADAM_RATE = 0.1
ADAM_DECAY = 0.01
BETA_FIRST = 0.9
BETA_SECOND = 0.999
COEF_LINEAR = 3.4445
COEF_CUBIC = -4.775
COEF_QUINTIC = 2.0315

CB1, CB2, CB3, AB1, AB2, AB3 = 0, 512, 1024, 1026, 1282, 1538
DB1, DB2, DB3, MAXLV, MINLV, LOGA = 1550, 2950, 4350, 4602, 4620, 4638

R_IN, R_HEAD, R_OUT, R_MISC, R_SMALL = 0, 72, 88, 96, 128
D_IN, D_OUT, D_B2, D_B3, D_UP, D_LOW, D_LOSS, D_HID, D_ROWS = 0, 24, 60, 61, 62, 63, 64, 72, 128

F32, BF16 = jnp.float32, jnp.bfloat16
MESH = pl.DeviceIdType.MESH
NN = (((1,), (0,)), ((), ()))
NT = (((1,), (1,)), ((), ()))


def dot(a, b, dims=NN):
    return lax.dot_general(a, b, dims, preferred_element_type=F32)


def rounded(v):
    return v.astype(BF16).astype(F32)


def pieces(v):
    high = v.astype(BF16)
    rest = v - high.astype(F32)
    middle = rest.astype(BF16)
    return high, middle, (rest - middle.astype(F32)).astype(BF16)


def split(v):
    high = v.astype(BF16)
    return high, (v - high.astype(F32)).astype(BF16)


def product(a, b, dims=NN):
    left = jnp.concatenate([a[0], a[0], a[1]], 1)
    right = jnp.concatenate([b[0], b[1], b[0]], dims[0][1][0])
    half = left.shape[0] // 2
    return jnp.concatenate([dot(left[:half], right, dims), dot(left[half:], right, dims)], 0)


def softplus(v):
    return jnp.maximum(v, 0.0) + jnp.log1p(jnp.exp(-jnp.abs(v)))


def sigmoid(v):
    return 0.5 + 0.5 * jnp.tanh(0.5 * v)


def gate(half):
    up = 1.0 + jnp.tanh(half)
    value = half * up
    return value, up + value * (2.0 - up)


def by_rows(body, *arrays):
    done = [
        body(*[array[at : at + ROWS] for array in arrays]) for at in range(0, arrays[0].shape[0], ROWS)
    ]
    return [jnp.concatenate(parts, 0) for parts in zip(*done)]


def spread_to(column, width):
    return jnp.concatenate([column] * (width // 128), 1)


def gated(half, column=None):
    def body(part, *offset):
        value, slope = gate(part + spread_to(offset[0], part.shape[1]) if offset else part)
        return value.astype(BF16), slope

    return by_rows(body, half, *([] if column is None else [column]))


def sloped(grad, slope):
    return by_rows(lambda part, by: ((part * by).astype(BF16),), grad, slope)[0]


def outer_sloped(column, row, slope):
    return by_rows(lambda part, by: (((spread_to(part, by.shape[1]) * row) * by).astype(BF16),), column, slope)[0]


def rows_of(shape):
    return lax.broadcasted_iota(jnp.int32, shape, 0)


def schulz(refs, steps, before=None):
    @pl.loop(0, steps)
    def _(step):
        if before is not None:
            before(step)
        matrices = [ref[...] for ref in refs]
        parts = [split(matrix) for matrix in matrices]
        grams = [product(part, part, NT) for part in parts]
        halves = [split(gram) for gram in grams]
        squares = [product(half, half) for half in halves]
        blends = [
            split(COEF_CUBIC * gram + COEF_QUINTIC * square) for gram, square in zip(grams, squares)
        ]
        moved = [product(blend, part) for blend, part in zip(blends, parts)]
        for ref, matrix, move in zip(refs, matrices, moved):
            ref[...] = COEF_LINEAR * matrix + move


def normalise(ref):
    moment = ref[...]
    norm = jnp.sqrt(jnp.sum(jnp.sum(moment * moment, axis=1, keepdims=True), axis=0, keepdims=True))
    ref[...] = moment / (norm + 1e-7)


class Layout:
    def __init__(self, mesh, replay, model):
        self.n_dp = mesh.shape["dp"]
        self.half = self.n_dp // 2
        self.n_blk = mesh.shape["blk"]
        self.n_dev = self.n_dp * self.n_blk
        self.replay = replay
        self.model = model
        self.real = self.n_dp * CAP
        self.batch = self.real + model
        self.width = -(-(self.real + 2) // 128) * 128
        self.rows = HSAC // self.n_blk
        self.drows = HDYN // self.n_blk
        self.mat = 64 // self.n_dp
        self.sml = 32 // self.n_dp
        self.chunks = (self.mat, self.mat + self.sml, self.mat)
        groups = [(name, g) for name in ("core sum", "plane sum") for g in range(3)]
        groups += [("line sum", g) for g in range(4)]
        common = ["hidden", "hidden on", "lists", "own", "line", "plane", "dyn h", "dyn m", "small", "small on"]
        common += groups
        kinds = [(name, kind) for name in ("pack", "x") for kind in ("own", "on")]
        tiles = [(name, k) for name in ("tiles", "tiles on") for k in range(3)]
        sent = common + tiles + kinds
        self.sent = {name: at for at, name in enumerate(sent)}
        self.departures = len(sent)
        self.here, self.arrivals = {}, 0
        tiles += [("pack", "sibling"), ("x", "sibling")]
        for name in common + tiles:
            self.here[name] = self.arrivals
            self.arrivals += 1
        for name in ("pack", "x"):
            self.here[name, "like"] = self.arrivals
            self.arrivals += MEMBERS


def main_kernel(lay, *refs):
    (
        replay, model, requests, member, live, noise, sac_h, sac_m, dyn_h, dyn_m, crit_in, act_in,
        dyn_in, crit_out, act_out, dyn_out, biases, targ_in, targ_hidden, targ_out, targ_bias,
        sac_g, sac_x, dyn_x, dyn_s, small, count,
        wg, lists, asked, dhg, dmg, bk, xs, nz, ys, w1f, w1t, w1n, w2t, w2h, heads, head_t, head_f,
        rowbuf, wide, headcol, acc_h, acc_w, acc_c, acc_a, acc_m, acc_l, grid_0, grid_1, grid_2, core_0, core_1,
        core_2, from_0, from_1, from_2, zr_0, zr_1, zr_2, zf_0, zf_1, zf_2, sum_0, sum_1, sum_2, mg, mat, dcols, dacc_h, dacc_w, dacc_o, dacc_m, dacc_b, dacc_l, xt, dmat,
        dpack, drow_x, bias, dhead, dhead_t, *rest,
    ) = refs
    send, recv = rest
    sent, here_at = lay.sent, lay.here
    grids, cores, froms = (grid_0, grid_1, grid_2), (core_0, core_1, core_2), (from_0, from_1, from_2)
    zrs, zfs, totals = (zr_0, zr_1, zr_2), (zf_0, zf_1, zf_2), (sum_0, sum_1, sum_2)
    n_dp, n_blk = lay.n_dp, lay.n_blk
    me = lax.axis_index("dp")
    z = lax.axis_index("blk")
    core, like = lax.rem(me, 2), me // 2
    sibling = me + 1 - 2 * core
    is_dyn = me < MEMBERS
    dyn_e = jnp.minimum(me, MEMBERS - 1)

    def on_plane(src, dst, ssem, rsem, peer):
        return pltpu.make_async_remote_copy(
            src_ref=src, dst_ref=dst, send_sem=ssem, recv_sem=rsem,
            device_id={"dp": peer}, device_id_type=MESH,
        )

    def on_line(src, dst, ssem, rsem, peer):
        return pltpu.make_async_remote_copy(
            src_ref=src, dst_ref=dst, send_sem=ssem, recv_sem=rsem,
            device_id={"blk": peer}, device_id_type=MESH,
        )

    def over(number, body):
        if number <= 8:
            for off in range(1, number):
                body(off)
        else:
            pl.loop(1, number)(body)

    def plane_peers(body):
        over(n_dp, lambda off: body(lax.rem(me + off, n_dp)))

    def like_peers(body):
        over(n_dp // 2, lambda off: body(lax.rem(me + 2 * off, n_dp)))

    def line_peers(body):
        over(n_blk, lambda off: body(lax.rem(z + off, n_blk)))

    def has_sent(view, name):
        at = send.at[sent[name]]
        on_plane(view, view, at, at, sibling).wait_send()

    def has_come(view, name):
        at = recv.at[here_at[name]]
        on_plane(view, view, at, at, sibling).wait_recv()

    barrier = pltpu.get_barrier_semaphore()
    plane_peers(lambda peer: pl.semaphore_signal(barrier, inc=1, device_id={"dp": peer}, device_id_type=MESH))
    line_peers(lambda peer: pl.semaphore_signal(barrier, inc=1, device_id={"blk": peer}, device_id_type=MESH))
    wg[0] = sac_h[...].astype(BF16)
    lists[0] = requests[...]
    lists[1] = member[...]
    pl.semaphore_wait(barrier, n_dp - 1 + n_blk - 1)

    half_rows = pl.ds(pl.multiple_of(core * (lay.rows // 2), lay.rows // 2), lay.rows // 2)

    def slot_from(owner, at):
        return lax.rem(owner - at + n_blk, n_blk)

    def hidden_copy(peer):
        src = wg.at[0, :, half_rows]
        dst = wg.at[slot_from(z, peer), :, half_rows]
        return on_line(src, dst, send.at[sent["hidden"]], recv.at[here_at["hidden"]], peer)

    def hidden_on():
        view = wg.at[pl.ds(1, n_blk - 1), :, half_rows]
        return on_plane(view, view, send.at[sent["hidden on"]], recv.at[here_at["hidden on"]], sibling)

    def list_copy(peer):
        return on_plane(lists, asked.at[me], send.at[sent["lists"]], recv.at[here_at["lists"]], peer)

    line_peers(lambda peer: hidden_copy(peer).start())
    plane_peers(lambda peer: list_copy(peer).start())
    asked[me] = lists[...]

    def dyn_h_copy(peer):
        return on_line(dyn_h.at[dyn_e], dhg.at[z], send.at[sent["dyn h"]], recv.at[here_at["dyn h"]], peer)

    def dyn_m_copy(peer):
        return on_line(dyn_m.at[dyn_e], dmg.at[z], send.at[sent["dyn m"]], recv.at[here_at["dyn m"]], peer)

    alive = live[...].astype(F32).reshape(1, lay.model)
    data = replay[...]
    sums = jnp.sum(data[0:24], axis=1, keepdims=True)
    squares = jnp.sum(data[0:24] * data[0:24], axis=1, keepdims=True)
    living = jnp.sum(alive, axis=1, keepdims=True)

    has_come(asked.at[pl.ds(0, n_dp - 1)], "lists")
    spread = (
        lax.rem(lax.broadcasted_iota(jnp.int32, (CAP, lay.real), 1), CAP)
        == lax.broadcasted_iota(jnp.int32, (CAP, lay.real), 0)
    ).astype(F32)
    here = (
        lax.broadcasted_iota(jnp.int32, (n_dp, lay.real), 1) // CAP
        == lax.broadcasted_iota(jnp.int32, (n_dp, lay.real), 0)
    )

    def in_lanes(which):
        values = asked[:, which, me, :].astype(F32)
        wide = lax.dot_general(
            values, spread, NN, precision=lax.Precision.HIGHEST, preferred_element_type=F32
        )
        return jnp.sum(jnp.where(here, wide, 0.0), axis=0, keepdims=True)

    slots = in_lanes(0)
    wanted = jnp.maximum(slots, 0.0).astype(jnp.int32)
    hot = (rows_of((lay.replay, lay.real)) == wanted).astype(BF16)
    padded = jnp.concatenate([data[0:40], jnp.zeros((8, lay.replay), F32)], 0)
    tail = jnp.concatenate([data[40:FEAT], jnp.zeros((14, lay.replay), F32)], 0)
    parts = [jnp.concatenate(pair, 0) for pair in zip(pieces(padded), pieces(tail))]
    chosen = dot(jnp.concatenate(parts, 0), hot)
    chosen = chosen[0:64] + chosen[64:128] + chosen[128:192]
    mine = me * n_blk
    bk[mine, 0:40, 0 : lay.real] = chosen[0:40]
    bk[mine, 40:FEAT, 0 : lay.real] = chosen[48:50]
    bk[mine, 42:43, 0 : lay.real] = (slots >= 0.0).astype(F32)
    bk[mine, 43:44, 0 : lay.real] = in_lanes(1)
    bk[mine, 44:48, 0 : lay.real] = jnp.zeros((4, lay.real), F32)
    bk[mine, :, lay.real : lay.width] = jnp.zeros((48, lay.width - lay.real), F32)
    bk[mine, 0:24, lay.real : lay.real + 1] = sums
    bk[mine, 0:24, lay.real + 1 : lay.real + 2] = squares
    bk[mine, 24:25, lay.real : lay.real + 1] = living

    def slot_of(block):
        line = lax.rem(block, n_blk)
        return block - line + slot_from(line, z)

    def block_line(peer):
        dst = bk.at[me * n_blk + slot_from(z, peer)]
        return on_line(bk.at[mine], dst, send.at[sent["line"]], recv.at[here_at["line"]], peer)

    def block_own(peer):
        view = bk.at[mine]
        return on_plane(view, view, send.at[sent["own"]], recv.at[here_at["own"]], peer)

    def block_plane(peer):
        view = bk.at[pl.ds(mine + 1, n_blk - 1)]
        return on_plane(view, view, send.at[sent["plane"]], recv.at[here_at["plane"]], peer)

    plane_peers(lambda peer: block_own(peer).start())
    line_peers(lambda peer: block_line(peer).start())

    @pl.when(is_dyn)
    def _():
        line_peers(lambda peer: dyn_h_copy(peer).start())
        line_peers(lambda peer: dyn_m_copy(peer).start())

    bias[...] = biases[...].reshape(1, NB)
    xs[42:56, :] = jnp.zeros((14, lay.batch), F32)
    xs[0:FEAT, lay.real : lay.batch] = model[...]
    xs[42:43, lay.real : lay.batch] = alive
    nz[...] = jnp.zeros_like(nz)
    for which in range(2):
        nz[which, 1:7, :] = noise[:, which, :]
    firsts = [
        (targ_in[:, 0, :], targ_bias[0:1, 0:HSAC]),
        (targ_in[:, 1, :], targ_bias[1:2, 0:HSAC]),
        (crit_in[:, 0, :], bias[:, CB1 : CB1 + HSAC]),
        (crit_in[:, 1, :], bias[:, CB1 + HSAC : CB1 + 2 * HSAC]),
        (act_in[...], bias[:, AB1 : AB1 + HSAC]),
    ]
    w1f[...] = jnp.zeros_like(w1f)
    for net, (weights, offset) in enumerate(firsts):
        w1f[net, 0 : weights.shape[0], :] = rounded(weights)
        for at, piece in enumerate(pieces(offset)):
            w1f[net, IN + at : IN + at + 1, :] = piece.astype(F32)
        w1t[net] = (0.5 * w1f[net].T).astype(BF16)
    for k in range(2):
        w1n[k] = w1f[2 + k, 16:32, :].astype(BF16)
    for net in range(2):
        w2t[net] = (0.5 * rounded(targ_hidden[net])).T.astype(BF16)
    has_come(wg.at[pl.ds(0, n_blk - 1), :, half_rows], "hidden")
    hidden_on().start()

    rowbuf[...] = jnp.zeros_like(rowbuf)
    rowbuf[0:1, :] = targ_bias[0:1, HSAC : 2 * HSAC]
    rowbuf[1:2, :] = targ_bias[1:2, HSAC : 2 * HSAC]
    rowbuf[2:3, :] = bias[:, CB2 : CB2 + HSAC]
    rowbuf[3:4, :] = bias[:, CB2 + HSAC : CB2 + 2 * HSAC]
    rowbuf[4:5, :] = bias[:, AB2 : AB2 + HSAC]
    rowbuf[5:7, :] = rounded(crit_out[...])
    columns = 0.5 * rowbuf[...].T
    for at in range(7):
        wide[at] = jnp.broadcast_to(columns[:, at : at + 1], (HSAC, 128))
    rowbuf[...] = jnp.zeros_like(rowbuf)
    rowbuf[0:1, 1:7] = bias[:, AB3 : AB3 + ACT]
    rowbuf[0:1, 9:15] = bias[:, AB3 + ACT : AB3 + 2 * ACT]
    headcol[...] = rowbuf[:, 0:128].T
    head_f[...] = jnp.zeros_like(head_f)
    for k in range(2):
        head_f[0:1, :] = targ_out[k : k + 1, :]
        heads[k] = head_f[...].astype(BF16)
        head_f[0:1, :] = crit_out[k : k + 1, :]
        heads[2 + k] = head_f[...].astype(BF16)
    head_f[0:1, :] = jnp.zeros((1, HSAC), F32)
    head_f[1:7, :] = act_out[0:ACT, :]
    head_f[9:15, :] = act_out[ACT : 2 * ACT, :]
    heads[4] = head_f[...].astype(BF16)
    head_t[...] = (0.5 * rounded(head_f[...])).T.astype(BF16)
    for ref in (acc_h, acc_w, acc_c, acc_a, acc_m, acc_l):
        ref[...] = jnp.zeros_like(ref)

    has_come(wg.at[pl.ds(0, n_blk - 1), :, half_rows], "hidden on")
    for k in range(3):
        for block in range(n_blk):
            w2h[k, block * lay.rows : (block + 1) * lay.rows, :] = (
                0.5 * wg[slot_from(block, z), k].astype(F32)
            ).astype(BF16)
        w2t[2 + k] = w2h[k].astype(F32).T.astype(BF16)

    log_alpha = bias[:, LOGA : LOGA + 1]
    alpha = jnp.exp(log_alpha)
    last = [
        targ_bias[0:1, 2 * HSAC : 2 * HSAC + 1],
        targ_bias[1:2, 2 * HSAC : 2 * HSAC + 1],
        bias[:, CB3 : CB3 + 1],
        bias[:, CB3 + 1 : CB3 + 2],
    ]
    critic_tiles = lay.batch // CRITIC_TILE
    actor_tiles = lay.batch // ACTOR_TILE

    def act_rows(width):
        row8 = rows_of((8, width))
        return jnp.logical_and(row8 >= 1, row8 < 1 + ACT)

    def place_of(step, width):
        return pl.ds(pl.multiple_of(lax.rem(step + 1, lay.batch // width) * width, width), width)

    def ones16(width):
        return jnp.ones((16, width), BF16)

    def framed(first_row, used, where):
        row32 = rows_of((32, where.size))
        ones3 = jnp.logical_and(row32 >= IN, row32 < IN + 3).astype(F32)
        return jnp.where(row32 < used, xs[first_row : first_row + 32, where], ones3)

    def hidden(inputs, net):
        first, slope1 = gated(dot(w1t[net], inputs))
        second, slope2 = gated(dot(w2t[net], first), wide[net])
        return first, slope1, second, slope2

    def policy(inputs, which, where):
        first, slope1, second, slope2 = hidden(inputs, 4)
        out = dot(heads[4], second) + headcol[0:16, 0:1]
        bent = jnp.tanh(out[8:16])
        log_scale = -5.0 + 3.5 * (bent + 1.0)
        draw = nz[which, :, where]
        moved = jnp.exp(log_scale) * draw
        latent = out[0:8] + moved
        terms = (
            -0.5 * draw * draw
            - log_scale
            - 0.9189385
            - 2.0 * (0.6931472 - latent - softplus(-2.0 * latent))
        )
        used = act_rows(where.size)
        log_prob = jnp.sum(jnp.where(used, terms, 0.0), axis=0, keepdims=True)
        action = jnp.where(used, jnp.tanh(latent), 0.0)
        return action, log_prob, bent, moved, (first, slope1, second, slope2)

    def with_action(inputs, action):
        middle_rows = jnp.where(act_rows(action.shape[1]), action, inputs[16:24])
        return jnp.concatenate([inputs[0:16], middle_rows, inputs[24:32]], 0).astype(BF16)

    def critic(inputs, net):
        kept = hidden(inputs, net)
        value = dot(heads[net], kept[2])[0:1] + last[net]
        return value, kept

    def add_hidden(k, first, grad):
        acc_h[k] += dot(jnp.concatenate([first, ones16(grad.shape[1])], 0), grad, NT)

    has_come(bk.at[pl.ds(0, n_blk - 1)], "line")
    plane_peers(lambda peer: block_plane(peer).start())

    def critic_pass(k, now_in, where, target):
        weight = xs[42:43, where]
        value, (c1, dc1, c2, dc2) = critic(now_in, 2 + k)
        miss = value - target
        g3 = rounded(weight * miss)
        g3_rows = jnp.where(rows_of((16, CRITIC_TILE)) == 0, g3, 0.0).astype(BF16)
        acc_c[k] += dot(g3_rows, c2, NT)
        acc_m[:, 16 + 16 * k : 32 + 16 * k] += dot(ones16(CRITIC_TILE), g3_rows, NT)
        g2 = outer_sloped(wide[5 + k], g3, dc2)
        add_hidden(k, c1, g2)
        g1 = sloped(dot(w2h[k], g2), dc1)
        acc_w[k] += dot(now_in, g1, NT)
        acc_l[0:1, 0:CRITIC_TILE] += weight * (0.5 * miss * miss)

    def put_matrix(k):
        for chunk in range(n_dp):
            tile = chunk * lay.mat
            side, row = tile // 32, tile % 32
            grids[k][chunk % 2, chunk // 2, 0 : lay.mat] = acc_h[
                k, row * 8 : (row + lay.mat) * 8, side * 128 : (side + 1) * 128
            ].reshape(lay.mat, 8, 128)

    def put(row, value):
        for at in range(value.shape[0] // 8):
            for side in range(value.shape[1] // 128):
                tile = side * (R_SMALL // 8) + row // 8 + at
                chunk = tile // lay.sml
                grid_1[chunk % 2, chunk // 2, lay.mat + tile % lay.sml] = value[
                    at * 8 : at * 8 + 8, side * 128 : (side + 1) * 128
                ]

    def core_sum(group):
        name = ("core sum", group)
        return on_plane(
            grids[group].at[1 - core], cores[group], send.at[sent[name]], recv.at[here_at[name]], sibling
        )

    def plane_sum(group, peer):
        name = ("plane sum", group)
        return on_plane(
            cores[group].at[peer // 2], froms[group].at[like], send.at[sent[name]], recv.at[here_at[name]], peer
        )

    def fold_core(group):
        core_sum(group).wait_recv()
        cores[group][...] += grids[group][core]
        like_peers(lambda peer: plane_sum(group, peer).start())

    def line_part(part):
        return (1, pl.ds(lay.mat, lay.sml)) if part == 3 else (part, pl.ds(0, lay.mat))

    def line_sum(part, peer):
        group, tiles = line_part(part)
        name = ("line sum", part)
        src, dst = zfs[group].at[tiles], zrs[group].at[z, tiles]
        return on_line(src, dst, send.at[sent[name]], recv.at[here_at[name]], peer)

    def line_bytes(part):
        group, tiles = line_part(part)
        return zrs[group].at[pl.ds(0, n_blk - 1), tiles]

    first_tile = me * lay.mat
    side = first_tile // 32
    row_tile = lax.rem(first_tile, 32)
    keeper_z = row_tile * 8 // lay.rows
    local_tile = row_tile - keeper_z * (lay.rows // 8)

    def fold_plane(group):
        has_come(froms[group].at[pl.ds(0, lay.half - 1)], ("plane sum", group))
        froms[group][like] = cores[group][like]
        whole = froms[group][0]
        for at in range(1, lay.half):
            whole = whole + froms[group][at]
        zfs[group][...] = whole

        @pl.when(z == keeper_z)
        def _():
            held_rows = pl.ds(pl.multiple_of(local_tile * 8, 8), lay.mat * 8)
            held_lanes = pl.ds(pl.multiple_of(side * 128, 128), 128)
            old = sac_m[group, held_rows, held_lanes].reshape(lay.mat, 8, 128)
            zfs[group][0 : lay.mat] += (MOMENTUM * count[0:1, 0:1]).reshape(1, 1, 1) * old

        for part in (1, 3) if group == 1 else (group,):
            line_peers(lambda peer: line_sum(part, peer).start())

    def tile_copy(k, peer):
        name = ("tiles", k)
        src = totals[k].at[pl.ds(0, lay.mat)]
        return on_plane(src, mg.at[k, core, like], send.at[sent[name]], recv.at[here_at[name]], peer)

    def tiles_on(k):
        name = ("tiles on", k)
        view = mg.at[k, core]
        return on_plane(view, view, send.at[sent[name]], recv.at[here_at[name]], sibling)

    small_at = (core * lay.half + like) * lay.sml

    def small_copy(peer):
        return on_plane(
            sum_1.at[pl.ds(lay.mat, lay.sml)], small.at[pl.ds(small_at, lay.sml)],
            send.at[sent["small"]], recv.at[here_at["small"]], peer,
        )

    def small_on():
        view = small.at[pl.ds(core * lay.half * lay.sml, lay.half * lay.sml)]
        return on_plane(view, view, send.at[sent["small on"]], recv.at[here_at["small on"]], sibling)

    def fold_end(part):
        group, tiles = line_part(part)
        has_come(line_bytes(part), ("line sum", part))
        zrs[group][z, tiles] = zfs[group][tiles]
        whole = zrs[group][0, tiles]
        for block in range(1, n_blk):
            whole = whole + zrs[group][block, tiles]
        totals[group][tiles] = whole
        if part == 3:
            like_peers(lambda peer: small_copy(peer).start())
            small[pl.ds(small_at, lay.sml)] = whole
        else:
            like_peers(lambda peer: tile_copy(part, peer).start())
            mg[part, core, like] = whole

    def chain(group):
        def end():
            for part in (1, 3) if group == 1 else (group,):
                fold_end(part)

        def turn():
            has_come(mg.at[group, 0, pl.ds(0, lay.half - 1)], ("tiles", group))
            tiles_on(group).start()
            if group == 1:
                has_come(small.at[pl.ds(0, (lay.half - 1) * lay.sml)], "small")
                small_on().start()

        return [
            lambda: core_sum(group).start(),
            lambda: fold_core(group),
            lambda: fold_plane(group),
            end,
            turn,
        ]

    chains = [chain(group) for group in range(3)]
    per = DYN_TILE // lay.real
    dyn_tiles = lay.n_dev // per

    def take(slots, step):
        for at, events in slots.items():
            @pl.when(step == at)
            def _():
                for event in events:
                    event()

    @pl.loop(0, actor_tiles)
    def _(step):
        @pl.when(step == actor_tiles - 1)
        def _():
            has_come(bk.at[pl.ds(0, n_dp - 1)], "own")
            lanes = lax.broadcasted_iota(jnp.int32, (48, lay.width), 1) // CAP

            def gather(owner, total):
                turned = pltpu.roll(
                    bk[owner * n_blk], lax.rem((owner - me) * CAP + lay.width, lay.width), axis=1
                )
                return jnp.where(lanes == owner, turned, total)

            own = lax.fori_loop(0, n_dp, gather, jnp.zeros((48, lay.width), F32))
            xs[0:48, 0 : lay.real] = own[:, 0 : lay.real]

        where = place_of(step, ACTOR_TILE)
        now_f = framed(0, IN, where)
        now_in = now_f.astype(BF16)
        weight = xs[42:43, where]
        action, log_prob, bent, moved, (a1, da1, a2, da2) = policy(now_in, 0, where)
        judged_in = with_action(now_f, action)
        loss = alpha * log_prob - log_alpha * (log_prob + TARGET_ENTROPY)
        grad_action = jnp.zeros((8, ACTOR_TILE), F32)
        used = act_rows(ACTOR_TILE)
        for k in range(2):
            judged, (_, df1, _, df2) = critic(judged_in, 2 + k)
            loss -= 0.5 * judged
            g2 = outer_sloped(wide[5 + k], -0.5 * weight, df2)
            g1 = sloped(dot(w2h[k], g2), df1)
            grad_action += dot(w1n[k], g1)[0:8]
        grad_latent = 2.0 * alpha * weight * action + grad_action * (1.0 - action * action)
        grad_scale = grad_latent * moved - alpha * weight
        grad_bent = grad_scale * 3.5 * (1.0 - bent * bent)
        g3 = jnp.concatenate(
            [jnp.where(used, grad_latent, 0.0), jnp.where(used, grad_bent, 0.0)], 0
        ).astype(BF16)
        acc_a[...] += dot(g3, a2, NT)
        acc_m[:, 0:16] += dot(ones16(ACTOR_TILE), g3, NT)
        g2 = sloped(dot(head_t[...], g3), da2)
        add_hidden(2, a1, g2)
        g1 = sloped(dot(w2h[2], g2), da1)
        acc_w[2] += dot(now_in, g1, NT)
        acc_l[1:2, 0:ACTOR_TILE] += weight * loss
        acc_l[2:3, 0:ACTOR_TILE] += weight * (log_prob + TARGET_ENTROPY)

    put_matrix(2)
    chains[2][0]()

    @pl.loop(0, critic_tiles)
    def _(step):
        if critic_tiles > 1:
            take({1: [chains[2][1]]}, step)

        where = place_of(step, CRITIC_TILE)
        now_in = framed(0, IN, where).astype(BF16)
        next_f = framed(24, OBS, where)
        reward = xs[23:24, where]
        done = xs[41:42, where]
        next_action, next_prob, _, _, _ = policy(next_f.astype(BF16), 1, where)
        aim_in = with_action(next_f, next_action)
        aim = jnp.minimum(critic(aim_in, 0)[0], critic(aim_in, 1)[0])
        target = reward + DISCOUNT * (1.0 - done) * (aim - alpha * next_prob)
        ys[0:1, where] = target
        critic_pass(0, now_in, where, target)

    put_matrix(0)
    chains[0][0]()
    if critic_tiles == 1:
        chains[2][1]()

    has_come(bk.at[pl.ds(0, (n_dp - 1) * (n_blk - 1))], "plane")
    lane0 = lay.real // 128 * 128

    def add_block(at, carry):
        sides, fills = carry
        slot = slot_of(at)
        return sides + bk[slot, 0:32, lane0 : lane0 + 128], fills + bk[slot, 40:48, 0 : lay.real]

    sides, fills = lax.fori_loop(
        0, lay.n_dev, add_block, (jnp.zeros((32, 128), F32), jnp.zeros((8, lay.real), F32))
    )
    at = lay.real - lane0
    rows_all = float(lay.replay * lay.n_dev)
    centre = sides[0:24, at : at + 1] / rows_all
    scale = lax.rsqrt(sides[0:24, at + 1 : at + 2] / rows_all - centre * centre + 1e-6)
    total = sides[24:25, at : at + 1] + jnp.sum(fills[2:3, :], axis=1, keepdims=True)
    count[...] = jnp.broadcast_to(total, (8, 128))

    @pl.loop(0, critic_tiles)
    def _(step):
        take({critic_tiles - 1: [chains[0][1], chains[2][2]]}, step)
        where = place_of(step, CRITIC_TILE)
        critic_pass(1, framed(0, IN, where).astype(BF16), where, ys[0:1, where])

    put_matrix(1)
    for k in range(3):
        put(R_IN + 24 * k, acc_w[k, 0:24, :])
    put(R_HEAD, acc_a[...])
    rowbuf[0:1, :] = acc_c[0, 0:1, :]
    rowbuf[1:2, :] = acc_c[1, 0:1, :]
    for k in range(3):
        rowbuf[2 + k : 3 + k, :] = acc_h[k, HSAC : HSAC + 1, :]
    put(R_OUT, rowbuf[...])
    folded = jnp.sum(acc_l[...], axis=1, keepdims=True)
    rowbuf[...] = jnp.zeros_like(rowbuf)
    rowbuf[0:1, 0:48] = acc_m[0:1, :]
    rowbuf[0:1, 64:65] = folded[0:1] + folded[1:2]
    rowbuf[0:1, 65:66] = folded[2:3]
    put(R_MISC, rowbuf[...])
    put(R_MISC + 8, jnp.zeros((R_SMALL - R_MISC - 8, HSAC), F32))
    chains[1][0]()

    def dyn_bias(start, width):
        row = jnp.zeros((1, width), F32)
        for e in range(MEMBERS):
            row = jnp.where(me == e, bias[:, start + width * e : start + width * (e + 1)], row)
        return row

    @pl.when(is_dyn)
    def _():
        w1f[0] = jnp.zeros((32, HSAC), F32)
        w1f[0, 0:IN, 0:HDYN] = rounded(dyn_in[dyn_e])
        for at, piece in enumerate(pieces(dyn_bias(DB1, HDYN))):
            w1f[0, IN + at : IN + at + 1, 0:HDYN] = piece.astype(F32)
        w1t[0] = (0.5 * w1f[0].T).astype(BF16)
        rowbuf[...] = jnp.zeros_like(rowbuf)
        rowbuf[0:1, 0:HDYN] = dyn_bias(DB2, HDYN)
        head_row = dyn_bias(DB3, DOUT)
        rowbuf[1:2, 0:HALF] = head_row[:, 0:HALF]
        rowbuf[1:2, 24 : 24 + HALF] = head_row[:, HALF:DOUT]
        rowbuf[2:3, 0:HALF] = bias[:, MAXLV : MAXLV + HALF]
        rowbuf[3:4, 0:HALF] = bias[:, MINLV : MINLV + HALF]
        dcols[...] = rowbuf[...].T
        wide[0] = jnp.broadcast_to(0.5 * dcols[:, 0:1], (HSAC, 128))
        dpack[...] = jnp.zeros_like(dpack)
        dpack[0:HALF, 0:HDYN] = dyn_out[dyn_e, 0:HALF, :]
        dpack[24 : 24 + HALF, 0:HDYN] = dyn_out[dyn_e, HALF:DOUT, :]
        dhead[...] = dpack[0:48, :].astype(BF16)
        dhead_t[...] = (0.5 * rounded(dpack[0:48, :])).T.astype(BF16)
        dpack[...] = jnp.zeros_like(dpack)

        has_come(dhg.at[pl.ds(0, n_blk - 1)], "dyn h")
        has_come(dmg.at[pl.ds(0, n_blk - 1)], "dyn m")
        dhg[z] = dyn_h[dyn_e]
        dmg[z] = dyn_m[dyn_e]
        dmat[...] = jnp.zeros_like(dmat)
        for block in range(n_blk):
            dmat[block * lay.drows : (block + 1) * lay.drows, 0:HDYN] = 0.5 * rounded(dhg[block])
        w2h[0] = dmat[...].astype(BF16)
        w2t[0] = dmat[...].T.astype(BF16)
        for ref in (dacc_h, dacc_w, dacc_o, dacc_m, dacc_b, dacc_l):
            ref[...] = jnp.zeros_like(ref)

    in_dyn = {}
    for at, event in (
        (1, chains[0][2]), (1, chains[1][1]), (2, chains[2][3]), (dyn_tiles - 1, chains[1][2]),
    ):
        in_dyn.setdefault(min(at, dyn_tiles - 1), []).append(event)

    @pl.loop(0, dyn_tiles)
    def _(tile):
        take(in_dyn, tile)

        @pl.when(is_dyn)
        def _():
            for at in range(per):
                slot = slot_of(tile * per + at)
                xt[:, at * lay.real : (at + 1) * lay.real] = bk[slot, :, 0 : lay.real]
            now = xt[0:24, :]
            later = xt[24:48, :]
            row24 = rows_of((24, DYN_TILE))
            scaled = jnp.where(row24 < IN, (now - centre) * scale, 1.0)
            inputs = jnp.concatenate([scaled, (rows_of((8, DYN_TILE)) < 2).astype(F32)], 0).astype(BF16)
            first, slope1 = gated(dot(w1t[0], inputs))
            second, slope2 = gated(dot(w2t[0], first), wide[0])
            out = dot(dhead[...], second) + dcols[0:48, 1:2]
            used = row24 < HALF
            upper = dcols[0:24, 2:3]
            lower = dcols[0:24, 3:4]
            gap1 = upper - out[24:48]
            gap2 = upper - softplus(gap1) - lower
            log_var = lower + softplus(gap2)
            error = out[0:24] - jnp.where(row24 == OBS, now[23:24], later - now)
            inverse = jnp.exp(-log_var)
            weight = xt[42:43, :] * (xt[43:44, :] == me.astype(F32)).astype(F32)
            spread_term = error * error * inverse
            nll = jnp.sum(jnp.where(used, spread_term + log_var, 0.0), axis=0, keepdims=True)
            dacc_l[0:1, :] += weight * nll
            grad_mu = 2.0 * weight * error * inverse
            grad_lv = weight * (1.0 - spread_term)
            open1 = sigmoid(gap1)
            open2 = sigmoid(gap2)
            grad_lv1 = grad_lv * open2
            dacc_b[0] += jnp.where(used, grad_lv1 * (1.0 - open1), 0.0)
            dacc_b[1] += jnp.where(used, grad_lv * (1.0 - open2), 0.0)
            g3 = jnp.concatenate(
                [jnp.where(used, grad_mu, 0.0), jnp.where(used, grad_lv1 * open1, 0.0)], 0
            ).astype(BF16)
            dacc_o[...] += dot(g3, second, NT)
            dacc_m[...] += dot(ones16(DYN_TILE), g3, NT)
            g2 = sloped(dot(dhead_t[...], g3), slope2)
            dacc_h[...] += dot(jnp.concatenate([first, ones16(DYN_TILE)], 0), g2, NT)
            g1 = sloped(dot(w2h[0], g2), slope1)
            dacc_w[...] += dot(inputs, g1, NT)

    out_of = {"pack": dyn_s, "x": dyn_x}

    def member_copy(name, src, owner, kind, sem, peer):
        return on_plane(src, out_of[name].at[owner], send.at[sent[name, kind]], recv.at[sem], peer)

    def give(name, src):
        like_peers(
            lambda peer: member_copy(name, src, dyn_e, "own", here_at[name, "like"] + dyn_e, peer).start()
        )
        member_copy(name, src, dyn_e, "own", here_at[name, "sibling"], sibling).start()

    def hand_on(name):
        def body(peer):
            @pl.when(peer < MEMBERS)
            def _():
                owner = jnp.minimum(peer, MEMBERS - 1)
                view = out_of[name].at[owner]
                member_copy(name, view, owner, "on", here_at[name, "like"] + owner, sibling).wait_recv()
                member_copy(name, view, owner, "on", here_at[name, "sibling"], sibling).start()

        like_peers(body)

    even, odd = (MEMBERS + 1) // 2, MEMBERS // 2
    handed = even - core * (even - odd) - jnp.where(is_dyn, 1, 0)

    def from_sibling(name):
        for side, number in ((0, odd), (1, even)):
            @pl.when(core == side)
            def _():
                has_come(out_of[name].at[pl.ds(0, number)], (name, "sibling"))

    def gave(name):
        @pl.when(is_dyn)
        def _():
            for begin in range(0, n_dp // 2, MEMBERS):
                number = min(MEMBERS, n_dp // 2 - begin)
                has_sent(out_of[name].at[pl.ds(0, number)], (name, "own"))

        for number in (even, even - 1, even - 2):
            @pl.when(handed == number)
            def _():
                has_sent(out_of[name].at[pl.ds(0, number)], (name, "on"))

    def line_rows(ref):
        rows = ref[0 : lay.drows, 0:HDYN]
        for block in range(1, n_blk):
            rows = jnp.where(z == block, ref[block * lay.drows : (block + 1) * lay.drows, 0:HDYN], rows)
        return rows

    mine_rows = pl.ds(pl.multiple_of(z * lay.rows, lay.rows), lay.rows)

    def take_matrix(k):
        tiles_on(k).wait_recv()
        for chunk in range(n_dp):
            tile = chunk * lay.mat
            half, row = tile // 32, tile % 32
            at = slice(row * 8, (row + lay.mat) * 8)
            piece = mg[k, chunk % 2, chunk // 2].reshape(lay.mat * 8, 128)
            mat[k, at, half * 128 : (half + 1) * 128] = piece / total
        normalise(mat.at[k])

    chains[2][4]()
    chains[0][3]()

    @pl.when(is_dyn)
    def _():
        dpack[D_IN : D_IN + 24, :] = dacc_w[0:24, :]
        dpack[D_OUT : D_OUT + HALF, :] = dacc_o[0:HALF, :]
        dpack[D_OUT + HALF : D_OUT + DOUT, :] = dacc_o[24 : 24 + HALF, :]
        dpack[D_B2 : D_B2 + 1, :] = dacc_h[HSAC : HSAC + 1, :]
        dpack[D_B3 : D_B3 + 1, 0:48] = dacc_m[0:1, :]
        lanes = lax.broadcasted_iota(jnp.int32, (24, 128), 1)
        bound = jnp.where(
            lanes == 0,
            jnp.sum(dacc_b[0], axis=1, keepdims=True),
            jnp.where(lanes == 1, jnp.sum(dacc_b[1], axis=1, keepdims=True), 0.0),
        )
        dpack[D_UP : D_UP + 2, 0:24] = bound.T[0:2, :]
        dpack[D_LOSS : D_LOSS + 1, 0:128] = jnp.broadcast_to(
            jnp.sum(dacc_l[0:1, :], axis=1, keepdims=True), (1, 128)
        )
        dpack[D_HID : D_HID + lay.drows, 0:HDYN] = line_rows(dacc_h)
        dyn_s[dyn_e] = dpack[...]
        give("pack", dpack)
        dmat[...] = jnp.zeros_like(dmat)
        for block in range(n_blk):
            at = slice(block * lay.drows, (block + 1) * lay.drows)
            dmat[at, 0:HDYN] = MOMENTUM * dmg[block] + dacc_h[at, 0:HDYN] / total
        normalise(dmat)

    def sum_end(step):
        @pl.when(step == 3)
        def _():
            chains[0][4]()
            chains[1][3]()

    take_matrix(2)

    @pl.when(is_dyn)
    def _():
        schulz([dmat, mat.at[2]], NS_ITERS, sum_end)
        rows = line_rows(dmat)
        drow_x[...] = rows
        dyn_x[dyn_e] = rows
        give("x", drow_x)

    @pl.when(jnp.logical_not(is_dyn))
    def _():
        schulz([mat.at[2]], NS_ITERS, sum_end)

    def sent_early():
        has_sent(wg.at[pl.ds(0, n_blk - 1), :, half_rows], "hidden")
        has_sent(wg.at[pl.ds(0, n_blk - 1), :, half_rows], "hidden on")
        has_sent(asked.at[pl.ds(0, n_dp - 1)], "lists")
        has_sent(bk.at[pl.ds(0, n_dp - 1)], "own")
        has_sent(bk.at[pl.ds(0, n_blk - 1)], "line")
        has_sent(bk.at[pl.ds(0, (n_dp - 1) * (n_blk - 1))], "plane")

        @pl.when(is_dyn)
        def _():
            has_sent(dhg.at[pl.ds(0, n_blk - 1)], "dyn h")
            has_sent(dmg.at[pl.ds(0, n_blk - 1)], "dyn m")

        for group in range(3):
            core_sum(group).wait_send()
            has_sent(froms[group].at[pl.ds(0, lay.half - 1)], ("plane sum", group))
        for part in range(4):
            has_sent(line_bytes(part), ("line sum", part))

    def pass_on(step):
        pl.when(step == 2)(functools.partial(hand_on, "pack"))
        pl.when(step == NS_ITERS - 1)(functools.partial(hand_on, "x"))

    chains[1][4]()
    for k in range(2):
        take_matrix(k)
    schulz([mat.at[0], mat.at[1]], NS_ITERS, pass_on)
    for k in range(3):
        sac_x[k] = mat[k, mine_rows, :]
        for half in range(2):
            for piece in range(lay.rows // 8 // lay.mat):
                chunk = (half * 32 + z * (lay.rows // 8)) // lay.mat + piece
                kept = mg[k, lax.rem(chunk, 2), chunk // 2]
                sac_g[half, k, piece * lay.mat : (piece + 1) * lay.mat] = kept

    sent_early()
    small_on().wait_recv()
    from_sibling("pack")
    from_sibling("x")

    has_sent(small.at[pl.ds(0, (lay.half - 1) * lay.sml)], "small")
    small_on().wait_send()
    gave("pack")
    gave("x")

    for k in range(3):
        has_sent(mg.at[k, 0, pl.ds(0, lay.half - 1)], ("tiles", k))
        tiles_on(k).wait_send()


def adamw(weights, first, second, gradient):
    first = BETA_FIRST * first + (1.0 - BETA_FIRST) * gradient
    second = BETA_SECOND * second + (1.0 - BETA_SECOND) * gradient * gradient
    first_hat = first / (1.0 - BETA_FIRST**STEP)
    second_hat = second / (1.0 - BETA_SECOND**STEP)
    step = first_hat / (jnp.sqrt(second_hat) + 1e-8) + ADAM_DECAY * weights
    return weights - ADAM_RATE * step, first, second


def update_kernel(lay, *refs):
    (
        sac_g, sac_x, dyn_x, dyn_s, small, count, sac_h, dyn_h, dyn_m,
        ci, ci_m, ci_v, ai, ai_m, ai_v, di, di_m, di_v, co, co_m, co_v, ao, ao_m, ao_v,
        do, do_m, do_v, bi, bi_m, bi_v,
        sac_new, sac_mom, dyn_new, dyn_mom, ci_n, ci_mn, ci_vn, ai_n, ai_mn, ai_vn, di_n, di_mn,
        di_vn, co_n, co_mn, co_vn, ao_n, ao_mn, ao_vn, do_n, do_mn, do_vn, bi_n, bi_mn, bi_vn,
        loss, counted, bg,
    ) = refs
    total = count[0:1, 0:1]
    for k in range(3):
        for side in range(2):
            tiles = sac_g[side, k].reshape(sac_mom.shape[1], 128)
            sac_mom[k, :, side * 128 : (side + 1) * 128] = tiles / total
    sac_new[...] = sac_h[...] * (1.0 - MUON_RATE * MUON_DECAY) - MUON_RATE * sac_x[...]
    dyn_rows = dyn_s[:, D_HID : D_HID + dyn_m.shape[1], 0:HDYN]
    dyn_mom[...] = MOMENTUM * dyn_m[...] + dyn_rows / total.reshape(1, 1, 1)
    dyn_new[...] = dyn_h[...] * (1.0 - MUON_RATE * MUON_DECAY) - MUON_RATE * dyn_x[...]

    def rows(row, number):
        def tile(at):
            chunk = at // lay.sml
            return small[(chunk % 2 * lay.half + chunk // 2) * lay.sml + at % lay.sml]

        sides = []
        for side in range(2):
            at = side * (R_SMALL // 8) + row // 8
            sides.append(jnp.concatenate([tile(at + more) for more in range(-(-number // 8))], 0))
        return jnp.concatenate(sides, 1)

    def store(outs, at, values):
        for out, value in zip(outs, values):
            out[at] = value

    outs = (ci_n, ci_mn, ci_vn)
    for k in range(2):
        at = (slice(None), k, slice(None))
        grad = rows(R_IN + 24 * k, 24)
        bg[:, CB1 + HSAC * k : CB1 + HSAC * (k + 1)] = grad[IN : IN + 1]
        store(outs, at, adamw(ci[at], ci_m[at], ci_v[at], grad[0:IN] / total))
    grad = rows(R_IN + 48, 24)
    bg[:, AB1 : AB1 + HSAC] = grad[IN : IN + 1]
    store((ai_n, ai_mn, ai_vn), ..., adamw(ai[...], ai_m[...], ai_v[...], grad[0:OBS] / total))
    grad = rows(R_HEAD, 16)
    for at, row in ((slice(0, ACT), slice(1, 1 + ACT)), (slice(ACT, 2 * ACT), slice(9, 9 + ACT))):
        store((ao_n, ao_mn, ao_vn), at, adamw(ao[at], ao_m[at], ao_v[at], grad[row] / total))
    grad = rows(R_OUT, 8)
    store((co_n, co_mn, co_vn), ..., adamw(co[...], co_m[...], co_v[...], grad[0:2] / total))
    bg[:, CB2 : CB2 + HSAC] = grad[2:3]
    bg[:, CB2 + HSAC : CB2 + 2 * HSAC] = grad[3:4]
    bg[:, AB2 : AB2 + HSAC] = grad[4:5]
    grad = rows(R_MISC, 8)
    bg[:, CB3 : CB3 + 1] = grad[0:1, 16:17]
    bg[:, CB3 + 1 : CB3 + 2] = grad[0:1, 32:33]
    bg[:, AB3 : AB3 + ACT] = grad[0:1, 1 : 1 + ACT]
    bg[:, AB3 + ACT : AB3 + 2 * ACT] = grad[0:1, 9 : 9 + ACT]
    bg[:, LOGA : LOGA + 1] = -grad[0:1, 65:66]
    total_loss = grad[0:1, 64:65]
    up = jnp.zeros((1, HALF), F32)
    low = jnp.zeros((1, HALF), F32)
    for e in range(MEMBERS):
        pack = dyn_s[e]
        total_loss = total_loss + pack[D_LOSS : D_LOSS + 1, 0:1]
        up = up + pack[D_UP : D_UP + 1, 0:HALF]
        low = low + pack[D_LOW : D_LOW + 1, 0:HALF]
        bg[:, DB1 + HDYN * e : DB1 + HDYN * (e + 1)] = pack[IN : IN + 1, 0:HDYN]
        bg[:, DB2 + HDYN * e : DB2 + HDYN * (e + 1)] = pack[D_B2 : D_B2 + 1, 0:HDYN]
        bg[:, DB3 + DOUT * e : DB3 + DOUT * e + HALF] = pack[D_B3 : D_B3 + 1, 0:HALF]
        bg[:, DB3 + DOUT * e + HALF : DB3 + DOUT * (e + 1)] = pack[D_B3 : D_B3 + 1, 24 : 24 + HALF]
        grad = pack[0:IN, 0:HDYN] / total
        store((di_n, di_mn, di_vn), e, adamw(di[e], di_m[e], di_v[e], grad))
        grad = pack[D_OUT : D_OUT + DOUT, 0:HDYN] / total
        store((do_n, do_mn, do_vn), e, adamw(do[e], do_m[e], do_v[e], grad))
    bg[:, MAXLV : MAXLV + HALF] = up
    bg[:, MINLV : MINLV + HALF] = low
    lane = lax.broadcasted_iota(jnp.int32, (1, NB), 1)
    bounds = jnp.where(
        jnp.logical_and(lane >= MAXLV, lane < MINLV),
        BOUND_WEIGHT,
        jnp.where(jnp.logical_and(lane >= MINLV, lane < LOGA), -BOUND_WEIGHT, 0.0),
    )
    grad = bg[...] / total + bounds
    flat = [ref[...].reshape(1, NB) for ref in (bi, bi_m, bi_v)]
    store((bi_n, bi_mn, bi_vn), ..., [value.reshape(NB) for value in adamw(*flat, grad)])
    loss[...] = total_loss
    counted[...] = total


def shards(
    lay, replay, model_rows, requests, member_of, model_live, noise, sac_hidden, sac_hidden_mom,
    dyn_hidden, dyn_hidden_mom, crit_in, crit_in_m, crit_in_v, act_in, act_in_m, act_in_v, dyn_in,
    dyn_in_m, dyn_in_v, crit_out, crit_out_m, crit_out_v, act_out, act_out_m, act_out_v, dyn_out,
    dyn_out_m, dyn_out_v, biases, biases_m, biases_v, targ_in, targ_hidden, targ_out, targ_bias,
):
    n_dp, n_blk = lay.n_dp, lay.n_blk
    spec = pl.BlockSpec(memory_space=pltpu.VMEM)

    def flip(value):
        return jnp.transpose(value, (1, 0, 2))

    def swap(value):
        return jnp.swapaxes(value, -1, -2)

    def kept(value):
        return pltpu.with_memory_space_constraint(value, pltpu.VMEM)

    inputs = (
        replay, model_rows, requests, member_of, model_live, jnp.transpose(noise, (2, 0, 1)),
        sac_hidden, sac_hidden_mom, dyn_hidden, dyn_hidden_mom, flip(crit_in), act_in, dyn_in,
        crit_out, swap(act_out), swap(dyn_out), biases, flip(targ_in), targ_hidden, targ_out,
        targ_bias,
    )
    shape = jax.ShapeDtypeStruct
    rows, drows = lay.rows, lay.drows
    out_shape = (
        pltpu.VMEM((2, 3, rows // 8, 8, 128), F32),
        pltpu.VMEM((3, rows, HSAC), F32),
        pltpu.VMEM((MEMBERS, drows, HDYN), F32),
        pltpu.VMEM((MEMBERS, D_ROWS, HSAC), F32),
        pltpu.VMEM((32, 8, 128), F32),
        pltpu.VMEM((8, 128), F32),
    )

    def vm(*dims, kind=F32):
        return pltpu.VMEM(dims, kind)

    scratch = [
        vm(n_blk, 3, rows, HSAC, kind=BF16),
        vm(2, n_dp, CAP, kind=jnp.int32),
        vm(n_dp, 2, n_dp, CAP, kind=jnp.int32),
        vm(n_blk, drows, HDYN),
        vm(n_blk, drows, HDYN),
        vm(lay.n_dev, 48, lay.width),
        vm(56, lay.batch),
        vm(2, 8, lay.batch),
        vm(8, lay.batch),
        vm(5, 32, HSAC),
        vm(5, HSAC, 32, kind=BF16),
        vm(2, 16, HSAC, kind=BF16),
        vm(5, HSAC, HSAC, kind=BF16),
        vm(3, HSAC, HSAC, kind=BF16),
        vm(5, 16, HSAC, kind=BF16),
        vm(HSAC, 16, kind=BF16),
        vm(16, HSAC),
        vm(8, HSAC),
        vm(7, HSAC, 128),
        vm(128, 8),
        vm(3, HSAC + 16, HSAC),
        vm(3, 32, HSAC),
        vm(2, 16, HSAC),
        vm(16, HSAC),
        vm(16, 48),
        vm(8, max(CRITIC_TILE, ACTOR_TILE)),
        *[vm(2, lay.half, chunk, 8, 128) for chunk in lay.chunks],
        *[vm(lay.half, chunk, 8, 128) for chunk in lay.chunks],
        *[vm(lay.half, chunk, 8, 128) for chunk in lay.chunks],
        *[vm(n_blk, chunk, 8, 128) for chunk in lay.chunks],
        *[vm(chunk, 8, 128) for chunk in lay.chunks],
        *[vm(chunk, 8, 128) for chunk in lay.chunks],
        vm(3, 2, lay.half, lay.mat, 8, 128),
        vm(3, HSAC, HSAC),
        vm(HSAC, 8),
        vm(HSAC + 16, HSAC),
        vm(32, HSAC),
        vm(48, HSAC),
        vm(16, 48),
        vm(2, 24, DYN_TILE),
        vm(8, DYN_TILE),
        vm(48, DYN_TILE),
        vm(HSAC, HSAC),
        vm(D_ROWS, HSAC),
        vm(drows, HDYN),
        vm(1, NB),
        vm(48, HSAC, kind=BF16),
        vm(HSAC, 48, kind=BF16),
    ]
    scratch += [pltpu.SemaphoreType.DMA((lay.departures,)), pltpu.SemaphoreType.DMA((lay.arrivals,))]
    varying = 4 * (lay.n_dev * 48 * lay.width + 72 * lay.batch + 48 * lay.replay)
    gathered = pl.pallas_call(
        functools.partial(main_kernel, lay),
        out_shape=out_shape,
        in_specs=[spec] * len(inputs),
        out_specs=[spec] * len(out_shape),
        scratch_shapes=scratch,
        compiler_params=pltpu.CompilerParams(
            collective_id=0, has_side_effects=True, vmem_limit_bytes=26 * 2**20 + varying
        ),
        name="step",
    )(*[pltpu.with_memory_space_constraint(value, pltpu.HBM) for value in inputs])
    params = (
        sac_hidden, dyn_hidden, dyn_hidden_mom,
        flip(crit_in), flip(crit_in_m), flip(crit_in_v), act_in, act_in_m, act_in_v,
        dyn_in, dyn_in_m, dyn_in_v, crit_out, crit_out_m, crit_out_v,
        swap(act_out), swap(act_out_m), swap(act_out_v),
        swap(dyn_out), swap(dyn_out_m), swap(dyn_out_v), biases, biases_m, biases_v,
    )
    new_shape = [shape(sac_hidden.shape, F32)] + [shape(value.shape, F32) for value in params]
    new_shape += [shape((1, 1), F32)] * 2
    out = pl.pallas_call(
        functools.partial(update_kernel, lay),
        out_shape=tuple(new_shape),
        in_specs=[spec] * (len(gathered) + len(params)),
        out_specs=[spec] * len(new_shape),
        scratch_shapes=[vm(1, NB)],
        compiler_params=pltpu.CompilerParams(vmem_limit_bytes=16 * 2**20),
        name="update",
    )(*[kept(value) for value in gathered], *params)
    out = list(out)
    for at in (4, 5, 6):
        out[at] = flip(out[at])
    for at in (16, 17, 18, 19, 20, 21):
        out[at] = swap(out[at])
    for at in (25, 26):
        out[at] = out[at].reshape(())
    return tuple(out)


def solution(mesh):
    both = ("dp", "blk")
    sharded = (
        P(None, both), P(None, both), P(both, None), P(both, None), P(both), P(None, both, None),
    )
    hidden = (P(None, "blk", None),) * 4

    def step(replay, model_rows, *others):
        lay = Layout(mesh, replay.shape[1], model_rows.shape[1])
        return shards(lay, replay, model_rows, *others)

    return jax.shard_map(
        step,
        mesh=mesh,
        in_specs=sharded + hidden + (P(),) * 25,
        out_specs=hidden + (P(),) * 23,
        check_vma=False,
    )
```

```python
import functools

import jax
import jax.numpy as jnp
from jax import lax
from jax.experimental import pallas as pl
from jax.experimental.pallas import tpu as pltpu
from jax.sharding import PartitionSpec as P

OBS = 17
ACT = 6
IN = OBS + ACT
FEAT = 42
HDYN = 200
HSAC = 256
MEMBERS = 7
DOUT = 36
HALF = DOUT // 2
NB = 4639
NS_ITERS = 5
STEP = 10
CAP = 8
CRITIC_TILE = 640
ACTOR_TILE = 640
DYN_TILE = 512
ROWS = 32

DISCOUNT = 0.99
TARGET_ENTROPY = -6.0
BOUND_WEIGHT = 0.01
MOMENTUM = 0.95
MUON_RATE = 0.4
MUON_DECAY = 0.01
ADAM_RATE = 0.1
ADAM_DECAY = 0.01
BETA_FIRST = 0.9
BETA_SECOND = 0.999
COEF_LINEAR = 3.4445
COEF_CUBIC = -4.775
COEF_QUINTIC = 2.0315

CB1, CB2, CB3, AB1, AB2, AB3 = 0, 512, 1024, 1026, 1282, 1538
DB1, DB2, DB3, MAXLV, MINLV, LOGA = 1550, 2950, 4350, 4602, 4620, 4638

R_IN, R_HEAD, R_OUT, R_MISC, R_SMALL = 0, 72, 88, 96, 128
D_IN, D_OUT, D_B2, D_B3, D_UP, D_LOW, D_LOSS, D_HID, D_ROWS = 0, 24, 60, 61, 62, 63, 64, 72, 128

F32, BF16 = jnp.float32, jnp.bfloat16
MESH = pl.DeviceIdType.MESH
NN = (((1,), (0,)), ((), ()))
NT = (((1,), (1,)), ((), ()))


def dot(a, b, dims=NN):
    return lax.dot_general(a, b, dims, preferred_element_type=F32)


def rounded(v):
    return v.astype(BF16).astype(F32)


def pieces(v):
    high = v.astype(BF16)
    rest = v - high.astype(F32)
    middle = rest.astype(BF16)
    return high, middle, (rest - middle.astype(F32)).astype(BF16)


def split(v):
    high = v.astype(BF16)
    return high, (v - high.astype(F32)).astype(BF16)


def product(a, b, dims=NN):
    left = jnp.concatenate([a[0], a[0], a[1]], 1)
    right = jnp.concatenate([b[0], b[1], b[0]], dims[0][1][0])
    half = left.shape[0] // 2
    return jnp.concatenate([dot(left[:half], right, dims), dot(left[half:], right, dims)], 0)


def softplus(v):
    return jnp.maximum(v, 0.0) + jnp.log1p(jnp.exp(-jnp.abs(v)))


def sigmoid(v):
    return 0.5 + 0.5 * jnp.tanh(0.5 * v)


def gate(half):
    up = 1.0 + jnp.tanh(half)
    value = half * up
    return value, up + value * (2.0 - up)


def by_rows(body, *arrays):
    done = [
        body(*[array[at : at + ROWS] for array in arrays]) for at in range(0, arrays[0].shape[0], ROWS)
    ]
    return [jnp.concatenate(parts, 0) for parts in zip(*done)]


def spread_to(column, width):
    return jnp.concatenate([column] * (width // 128), 1)


def gated(half, column=None):
    def body(part, *offset):
        value, slope = gate(part + spread_to(offset[0], part.shape[1]) if offset else part)
        return value.astype(BF16), slope

    return by_rows(body, half, *([] if column is None else [column]))


def sloped(grad, slope):
    return by_rows(lambda part, by: ((part * by).astype(BF16),), grad, slope)[0]


def outer_sloped(column, row, slope):
    return by_rows(lambda part, by: (((spread_to(part, by.shape[1]) * row) * by).astype(BF16),), column, slope)[0]


def rows_of(shape):
    return lax.broadcasted_iota(jnp.int32, shape, 0)


def schulz(refs, steps, before=None):
    @pl.loop(0, steps)
    def _(step):
        if before is not None:
            before(step)
        matrices = [ref[...] for ref in refs]
        parts = [split(matrix) for matrix in matrices]
        grams = [product(part, part, NT) for part in parts]
        halves = [split(gram) for gram in grams]
        squares = [product(half, half) for half in halves]
        blends = [
            split(COEF_CUBIC * gram + COEF_QUINTIC * square) for gram, square in zip(grams, squares)
        ]
        moved = [product(blend, part) for blend, part in zip(blends, parts)]
        for ref, matrix, move in zip(refs, matrices, moved):
            ref[...] = COEF_LINEAR * matrix + move


def normalise(ref):
    moment = ref[...]
    norm = jnp.sqrt(jnp.sum(jnp.sum(moment * moment, axis=1, keepdims=True), axis=0, keepdims=True))
    ref[...] = moment / (norm + 1e-7)


class Layout:
    def __init__(self, mesh, replay, model):
        self.n_dp = mesh.shape["dp"]
        self.half = self.n_dp // 2
        self.n_blk = mesh.shape["blk"]
        self.n_dev = self.n_dp * self.n_blk
        self.replay = replay
        self.model = model
        self.real = self.n_dp * CAP
        self.batch = self.real + model
        self.width = -(-(self.real + 2) // 128) * 128
        self.rows = HSAC // self.n_blk
        self.drows = HDYN // self.n_blk
        self.mat = 64 // self.n_dp
        self.sml = 32 // self.n_dp
        self.chunks = (self.mat, self.mat + self.sml, self.mat)
        self.owners = (self.n_dp - 3, self.n_dp - 1, self.n_dp - 1)
        self.keepers = 2 * (self.rows // 8) // self.mat
        groups = [(name, g) for name in ("core sum", "plane sum") for g in range(3)]
        groups += [("line sum", g) for g in range(4)]
        common = ["hidden", "hidden on", "lists", "own", "line", "plane", "dyn h", "dyn m", "small", "small on"]
        common += groups
        kinds = [(name, kind) for name in ("pack", "x") for kind in ("own", "on")]
        tiles = [(name, k) for name in ("tiles", "sac g") for k in range(3)]
        sent = common + tiles + kinds
        self.sent = {name: at for at, name in enumerate(sent)}
        self.departures = len(sent)
        for k in range(3):
            self.sent["sac x", k] = self.departures
            self.departures += self.n_dp
        self.here, self.arrivals = {}, 0
        tiles += [("sac x", k) for k in range(3)]
        tiles += [("pack", "sibling"), ("x", "sibling")]
        for name in common + tiles:
            self.here[name] = self.arrivals
            self.arrivals += 1
        for name in ("pack", "x"):
            self.here[name, "like"] = self.arrivals
            self.arrivals += MEMBERS


def main_kernel(lay, *refs):
    (
        replay, model, requests, member, live, noise, sac_h, sac_m, dyn_h, dyn_m, crit_in, act_in,
        dyn_in, crit_out, act_out, dyn_out, biases, targ_in, targ_hidden, targ_out, targ_bias,
        sac_g, sac_x, dyn_x, dyn_s, small, count,
        wg, lists, asked, dhg, dmg, bk, xs, nz, ys, w1f, w1t, w1n, w2t, w2h, heads, head_t, head_f,
        rowbuf, wide, headcol, acc_h, acc_w, acc_c, acc_a, acc_m, acc_l, grid_0, grid_1, grid_2, core_0, core_1,
        core_2, from_0, from_1, from_2, zr_0, zr_1, zr_2, zf_0, zf_1, zf_2, sum_0, sum_1, sum_2, mg, mat, dcols, dacc_h, dacc_w, dacc_o, dacc_m, dacc_b, dacc_l, xt, dmat,
        dpack, drow_x, bias, dhead, dhead_t, *rest,
    ) = refs
    send, recv = rest
    sent, here_at = lay.sent, lay.here
    grids, cores, froms = (grid_0, grid_1, grid_2), (core_0, core_1, core_2), (from_0, from_1, from_2)
    zrs, zfs, totals = (zr_0, zr_1, zr_2), (zf_0, zf_1, zf_2), (sum_0, sum_1, sum_2)
    n_dp, n_blk = lay.n_dp, lay.n_blk
    me = lax.axis_index("dp")
    z = lax.axis_index("blk")
    core, like = lax.rem(me, 2), me // 2
    sibling = me + 1 - 2 * core
    is_dyn = me < MEMBERS
    dyn_e = jnp.minimum(me, MEMBERS - 1)

    def on_plane(src, dst, ssem, rsem, peer):
        return pltpu.make_async_remote_copy(
            src_ref=src, dst_ref=dst, send_sem=ssem, recv_sem=rsem,
            device_id={"dp": peer}, device_id_type=MESH,
        )

    def on_line(src, dst, ssem, rsem, peer):
        return pltpu.make_async_remote_copy(
            src_ref=src, dst_ref=dst, send_sem=ssem, recv_sem=rsem,
            device_id={"blk": peer}, device_id_type=MESH,
        )

    def over(number, body):
        if number <= 8:
            for off in range(1, number):
                body(off)
        else:
            pl.loop(1, number)(body)

    def plane_peers(body):
        over(n_dp, lambda off: body(lax.rem(me + off, n_dp)))

    def like_peers(body):
        over(n_dp // 2, lambda off: body(lax.rem(me + 2 * off, n_dp)))

    def line_peers(body):
        over(n_blk, lambda off: body(lax.rem(z + off, n_blk)))

    def has_sent(view, name):
        at = send.at[sent[name]]
        on_plane(view, view, at, at, sibling).wait_send()

    def has_come(view, name):
        at = recv.at[here_at[name]]
        on_plane(view, view, at, at, sibling).wait_recv()

    barrier = pltpu.get_barrier_semaphore()
    plane_peers(lambda peer: pl.semaphore_signal(barrier, inc=1, device_id={"dp": peer}, device_id_type=MESH))
    line_peers(lambda peer: pl.semaphore_signal(barrier, inc=1, device_id={"blk": peer}, device_id_type=MESH))
    wg[0] = sac_h[...].astype(BF16)
    lists[0] = requests[...]
    lists[1] = member[...]
    pl.semaphore_wait(barrier, n_dp - 1 + n_blk - 1)

    half_rows = pl.ds(pl.multiple_of(core * (lay.rows // 2), lay.rows // 2), lay.rows // 2)

    def slot_from(owner, at):
        return lax.rem(owner - at + n_blk, n_blk)

    def hidden_copy(peer):
        src = wg.at[0, :, half_rows]
        dst = wg.at[slot_from(z, peer), :, half_rows]
        return on_line(src, dst, send.at[sent["hidden"]], recv.at[here_at["hidden"]], peer)

    def hidden_on():
        view = wg.at[pl.ds(1, n_blk - 1), :, half_rows]
        return on_plane(view, view, send.at[sent["hidden on"]], recv.at[here_at["hidden on"]], sibling)

    def list_copy(peer):
        return on_plane(lists, asked.at[me], send.at[sent["lists"]], recv.at[here_at["lists"]], peer)

    line_peers(lambda peer: hidden_copy(peer).start())
    plane_peers(lambda peer: list_copy(peer).start())
    asked[me] = lists[...]

    def dyn_h_copy(peer):
        return on_line(dyn_h.at[dyn_e], dhg.at[z], send.at[sent["dyn h"]], recv.at[here_at["dyn h"]], peer)

    def dyn_m_copy(peer):
        return on_line(dyn_m.at[dyn_e], dmg.at[z], send.at[sent["dyn m"]], recv.at[here_at["dyn m"]], peer)

    alive = live[...].astype(F32).reshape(1, lay.model)
    data = replay[...]
    sums = jnp.sum(data[0:24], axis=1, keepdims=True)
    squares = jnp.sum(data[0:24] * data[0:24], axis=1, keepdims=True)
    living = jnp.sum(alive, axis=1, keepdims=True)

    has_come(asked.at[pl.ds(0, n_dp - 1)], "lists")
    spread = (
        lax.rem(lax.broadcasted_iota(jnp.int32, (CAP, lay.real), 1), CAP)
        == lax.broadcasted_iota(jnp.int32, (CAP, lay.real), 0)
    ).astype(F32)
    here = (
        lax.broadcasted_iota(jnp.int32, (n_dp, lay.real), 1) // CAP
        == lax.broadcasted_iota(jnp.int32, (n_dp, lay.real), 0)
    )

    def in_lanes(which):
        values = asked[:, which, me, :].astype(F32)
        wide = lax.dot_general(
            values, spread, NN, precision=lax.Precision.HIGHEST, preferred_element_type=F32
        )
        return jnp.sum(jnp.where(here, wide, 0.0), axis=0, keepdims=True)

    slots = in_lanes(0)
    wanted = jnp.maximum(slots, 0.0).astype(jnp.int32)
    hot = (rows_of((lay.replay, lay.real)) == wanted).astype(BF16)
    padded = jnp.concatenate([data[0:40], jnp.zeros((8, lay.replay), F32)], 0)
    tail = jnp.concatenate([data[40:FEAT], jnp.zeros((14, lay.replay), F32)], 0)
    parts = [jnp.concatenate(pair, 0) for pair in zip(pieces(padded), pieces(tail))]
    chosen = dot(jnp.concatenate(parts, 0), hot)
    chosen = chosen[0:64] + chosen[64:128] + chosen[128:192]
    mine = me * n_blk
    bk[mine, 0:40, 0 : lay.real] = chosen[0:40]
    bk[mine, 40:FEAT, 0 : lay.real] = chosen[48:50]
    bk[mine, 42:43, 0 : lay.real] = (slots >= 0.0).astype(F32)
    bk[mine, 43:44, 0 : lay.real] = in_lanes(1)
    bk[mine, 44:48, 0 : lay.real] = jnp.zeros((4, lay.real), F32)
    bk[mine, :, lay.real : lay.width] = jnp.zeros((48, lay.width - lay.real), F32)
    bk[mine, 0:24, lay.real : lay.real + 1] = sums
    bk[mine, 0:24, lay.real + 1 : lay.real + 2] = squares
    bk[mine, 24:25, lay.real : lay.real + 1] = living

    def slot_of(block):
        line = lax.rem(block, n_blk)
        return block - line + slot_from(line, z)

    def block_line(peer):
        dst = bk.at[me * n_blk + slot_from(z, peer)]
        return on_line(bk.at[mine], dst, send.at[sent["line"]], recv.at[here_at["line"]], peer)

    def block_own(peer):
        view = bk.at[mine]
        return on_plane(view, view, send.at[sent["own"]], recv.at[here_at["own"]], peer)

    def block_plane(peer):
        view = bk.at[pl.ds(mine + 1, n_blk - 1)]
        return on_plane(view, view, send.at[sent["plane"]], recv.at[here_at["plane"]], peer)

    plane_peers(lambda peer: block_own(peer).start())
    line_peers(lambda peer: block_line(peer).start())

    @pl.when(is_dyn)
    def _():
        line_peers(lambda peer: dyn_h_copy(peer).start())
        line_peers(lambda peer: dyn_m_copy(peer).start())

    bias[...] = biases[...].reshape(1, NB)
    xs[42:56, :] = jnp.zeros((14, lay.batch), F32)
    xs[0:FEAT, lay.real : lay.batch] = model[...]
    xs[42:43, lay.real : lay.batch] = alive
    nz[...] = jnp.zeros_like(nz)
    for which in range(2):
        nz[which, 1:7, :] = noise[:, which, :]
    firsts = [
        (targ_in[:, 0, :], targ_bias[0:1, 0:HSAC]),
        (targ_in[:, 1, :], targ_bias[1:2, 0:HSAC]),
        (crit_in[:, 0, :], bias[:, CB1 : CB1 + HSAC]),
        (crit_in[:, 1, :], bias[:, CB1 + HSAC : CB1 + 2 * HSAC]),
        (act_in[...], bias[:, AB1 : AB1 + HSAC]),
    ]
    w1f[...] = jnp.zeros_like(w1f)
    for net, (weights, offset) in enumerate(firsts):
        w1f[net, 0 : weights.shape[0], :] = rounded(weights)
        for at, piece in enumerate(pieces(offset)):
            w1f[net, IN + at : IN + at + 1, :] = piece.astype(F32)
        w1t[net] = (0.5 * w1f[net].T).astype(BF16)
    for k in range(2):
        w1n[k] = w1f[2 + k, 16:32, :].astype(BF16)
    for net in range(2):
        w2t[net] = (0.5 * rounded(targ_hidden[net])).T.astype(BF16)
    has_come(wg.at[pl.ds(0, n_blk - 1), :, half_rows], "hidden")
    hidden_on().start()

    rowbuf[...] = jnp.zeros_like(rowbuf)
    rowbuf[0:1, :] = targ_bias[0:1, HSAC : 2 * HSAC]
    rowbuf[1:2, :] = targ_bias[1:2, HSAC : 2 * HSAC]
    rowbuf[2:3, :] = bias[:, CB2 : CB2 + HSAC]
    rowbuf[3:4, :] = bias[:, CB2 + HSAC : CB2 + 2 * HSAC]
    rowbuf[4:5, :] = bias[:, AB2 : AB2 + HSAC]
    rowbuf[5:7, :] = rounded(crit_out[...])
    columns = 0.5 * rowbuf[...].T
    for at in range(7):
        wide[at] = jnp.broadcast_to(columns[:, at : at + 1], (HSAC, 128))
    rowbuf[...] = jnp.zeros_like(rowbuf)
    rowbuf[0:1, 1:7] = bias[:, AB3 : AB3 + ACT]
    rowbuf[0:1, 9:15] = bias[:, AB3 + ACT : AB3 + 2 * ACT]
    headcol[...] = rowbuf[:, 0:128].T
    head_f[...] = jnp.zeros_like(head_f)
    for k in range(2):
        head_f[0:1, :] = targ_out[k : k + 1, :]
        heads[k] = head_f[...].astype(BF16)
        head_f[0:1, :] = crit_out[k : k + 1, :]
        heads[2 + k] = head_f[...].astype(BF16)
    head_f[0:1, :] = jnp.zeros((1, HSAC), F32)
    head_f[1:7, :] = act_out[0:ACT, :]
    head_f[9:15, :] = act_out[ACT : 2 * ACT, :]
    heads[4] = head_f[...].astype(BF16)
    head_t[...] = (0.5 * rounded(head_f[...])).T.astype(BF16)
    for ref in (acc_h, acc_w, acc_c, acc_a, acc_m, acc_l):
        ref[...] = jnp.zeros_like(ref)

    has_come(wg.at[pl.ds(0, n_blk - 1), :, half_rows], "hidden on")
    for k in range(3):
        for block in range(n_blk):
            w2h[k, block * lay.rows : (block + 1) * lay.rows, :] = (
                0.5 * wg[slot_from(block, z), k].astype(F32)
            ).astype(BF16)
        w2t[2 + k] = w2h[k].astype(F32).T.astype(BF16)

    log_alpha = bias[:, LOGA : LOGA + 1]
    alpha = jnp.exp(log_alpha)
    last = [
        targ_bias[0:1, 2 * HSAC : 2 * HSAC + 1],
        targ_bias[1:2, 2 * HSAC : 2 * HSAC + 1],
        bias[:, CB3 : CB3 + 1],
        bias[:, CB3 + 1 : CB3 + 2],
    ]
    critic_tiles = lay.batch // CRITIC_TILE
    actor_tiles = lay.batch // ACTOR_TILE

    def act_rows(width):
        row8 = rows_of((8, width))
        return jnp.logical_and(row8 >= 1, row8 < 1 + ACT)

    def place_of(step, width):
        return pl.ds(pl.multiple_of(lax.rem(step + 1, lay.batch // width) * width, width), width)

    def ones16(width):
        return jnp.ones((16, width), BF16)

    def framed(first_row, used, where):
        row32 = rows_of((32, where.size))
        ones3 = jnp.logical_and(row32 >= IN, row32 < IN + 3).astype(F32)
        return jnp.where(row32 < used, xs[first_row : first_row + 32, where], ones3)

    def hidden(inputs, net):
        first, slope1 = gated(dot(w1t[net], inputs))
        second, slope2 = gated(dot(w2t[net], first), wide[net])
        return first, slope1, second, slope2

    def policy(inputs, which, where):
        first, slope1, second, slope2 = hidden(inputs, 4)
        out = dot(heads[4], second) + headcol[0:16, 0:1]
        bent = jnp.tanh(out[8:16])
        log_scale = -5.0 + 3.5 * (bent + 1.0)
        draw = nz[which, :, where]
        moved = jnp.exp(log_scale) * draw
        latent = out[0:8] + moved
        terms = (
            -0.5 * draw * draw
            - log_scale
            - 0.9189385
            - 2.0 * (0.6931472 - latent - softplus(-2.0 * latent))
        )
        used = act_rows(where.size)
        log_prob = jnp.sum(jnp.where(used, terms, 0.0), axis=0, keepdims=True)
        action = jnp.where(used, jnp.tanh(latent), 0.0)
        return action, log_prob, bent, moved, (first, slope1, second, slope2)

    def with_action(inputs, action):
        middle_rows = jnp.where(act_rows(action.shape[1]), action, inputs[16:24])
        return jnp.concatenate([inputs[0:16], middle_rows, inputs[24:32]], 0).astype(BF16)

    def critic(inputs, net):
        kept = hidden(inputs, net)
        value = dot(heads[net], kept[2])[0:1] + last[net]
        return value, kept

    def add_hidden(k, first, grad):
        acc_h[k] += dot(jnp.concatenate([first, ones16(grad.shape[1])], 0), grad, NT)

    has_come(bk.at[pl.ds(0, n_blk - 1)], "line")
    plane_peers(lambda peer: block_plane(peer).start())

    def critic_pass(k, now_in, where, target):
        weight = xs[42:43, where]
        value, (c1, dc1, c2, dc2) = critic(now_in, 2 + k)
        miss = value - target
        g3 = rounded(weight * miss)
        g3_rows = jnp.where(rows_of((16, CRITIC_TILE)) == 0, g3, 0.0).astype(BF16)
        acc_c[k] += dot(g3_rows, c2, NT)
        acc_m[:, 16 + 16 * k : 32 + 16 * k] += dot(ones16(CRITIC_TILE), g3_rows, NT)
        g2 = outer_sloped(wide[5 + k], g3, dc2)
        add_hidden(k, c1, g2)
        g1 = sloped(dot(w2h[k], g2), dc1)
        acc_w[k] += dot(now_in, g1, NT)
        acc_l[0:1, 0:CRITIC_TILE] += weight * (0.5 * miss * miss)

    def put_matrix(k):
        for chunk in range(n_dp):
            tile = chunk * lay.mat
            side, row = tile // 32, tile % 32
            grids[k][chunk % 2, chunk // 2, 0 : lay.mat] = acc_h[
                k, row * 8 : (row + lay.mat) * 8, side * 128 : (side + 1) * 128
            ].reshape(lay.mat, 8, 128)

    def put(row, value):
        for at in range(value.shape[0] // 8):
            for side in range(value.shape[1] // 128):
                tile = side * (R_SMALL // 8) + row // 8 + at
                chunk = tile // lay.sml
                grid_1[chunk % 2, chunk // 2, lay.mat + tile % lay.sml] = value[
                    at * 8 : at * 8 + 8, side * 128 : (side + 1) * 128
                ]

    def core_sum(group):
        name = ("core sum", group)
        return on_plane(
            grids[group].at[1 - core], cores[group], send.at[sent[name]], recv.at[here_at[name]], sibling
        )

    def plane_sum(group, peer):
        name = ("plane sum", group)
        return on_plane(
            cores[group].at[peer // 2], froms[group].at[like], send.at[sent[name]], recv.at[here_at[name]], peer
        )

    def fold_core(group):
        core_sum(group).wait_recv()
        cores[group][...] += grids[group][core]
        like_peers(lambda peer: plane_sum(group, peer).start())

    def line_part(part):
        return (1, pl.ds(lay.mat, lay.sml)) if part == 3 else (part, pl.ds(0, lay.mat))

    def line_sum(part, peer):
        group, tiles = line_part(part)
        name = ("line sum", part)
        src, dst = zfs[group].at[tiles], zrs[group].at[z, tiles]
        return on_line(src, dst, send.at[sent[name]], recv.at[here_at[name]], peer)

    def line_bytes(part):
        group, tiles = line_part(part)
        return zrs[group].at[pl.ds(0, n_blk - 1), tiles]

    first_tile = me * lay.mat
    side = first_tile // 32
    row_tile = lax.rem(first_tile, 32)
    keeper_z = row_tile * 8 // lay.rows
    local_tile = row_tile - keeper_z * (lay.rows // 8)

    def fold_plane(group):
        has_come(froms[group].at[pl.ds(0, lay.half - 1)], ("plane sum", group))
        froms[group][like] = cores[group][like]
        whole = froms[group][0]
        for at in range(1, lay.half):
            whole = whole + froms[group][at]
        zfs[group][...] = whole

        @pl.when(z == keeper_z)
        def _():
            held_rows = pl.ds(pl.multiple_of(local_tile * 8, 8), lay.mat * 8)
            held_lanes = pl.ds(pl.multiple_of(side * 128, 128), 128)
            old = sac_m[group, held_rows, held_lanes].reshape(lay.mat, 8, 128)
            zfs[group][0 : lay.mat] += (MOMENTUM * count[0:1, 0:1]).reshape(1, 1, 1) * old

        for part in (1, 3) if group == 1 else (group,):
            line_peers(lambda peer: line_sum(part, peer).start())

    def tile_copy(k):
        name, owner = ("tiles", k), lay.owners[k]
        src = totals[k].at[pl.ds(0, lay.mat)]
        return on_plane(src, mg.at[k, me], send.at[sent[name]], recv.at[here_at[name]], owner)

    def keep_copy(k, peer):
        name = ("sac g", k)
        view = sac_g.at[side, k, pl.ds(local_tile, lay.mat)]
        return on_plane(view, view, send.at[sent[name]], recv.at[here_at[name]], peer)

    def kept_bytes(number):
        return mg.at[0, pl.ds(0, number)]

    small_at = (core * lay.half + like) * lay.sml

    def small_copy(peer):
        return on_plane(
            sum_1.at[pl.ds(lay.mat, lay.sml)], small.at[pl.ds(small_at, lay.sml)],
            send.at[sent["small"]], recv.at[here_at["small"]], peer,
        )

    def small_on():
        view = small.at[pl.ds(core * lay.half * lay.sml, lay.half * lay.sml)]
        return on_plane(view, view, send.at[sent["small on"]], recv.at[here_at["small on"]], sibling)

    def fold_end(part):
        group, tiles = line_part(part)
        has_come(line_bytes(part), ("line sum", part))
        zrs[group][z, tiles] = zfs[group][tiles]
        whole = zrs[group][0, tiles]
        for block in range(1, n_blk):
            whole = whole + zrs[group][block, tiles]
        totals[group][tiles] = whole
        if part == 3:
            like_peers(lambda peer: small_copy(peer).start())
            small[pl.ds(small_at, lay.sml)] = whole
        else:
            pl.when(me != lay.owners[part])(tile_copy(part).start)

            @pl.when(me == lay.owners[part])
            def _():
                mg[part, me] = whole

            @pl.when(z == keeper_z)
            def _():
                sac_g[side, part, pl.ds(local_tile, lay.mat)] = whole
                plane_peers(lambda peer: keep_copy(part, peer).start())

    def chain(group):
        def end():
            for part in (1, 3) if group == 1 else (group,):
                fold_end(part)

        def turn():
            has_come(small.at[pl.ds(0, (lay.half - 1) * lay.sml)], "small")
            small_on().start()

        return [
            lambda: core_sum(group).start(),
            lambda: fold_core(group),
            lambda: fold_plane(group),
            end,
            turn,
        ]

    chains = [chain(group) for group in range(3)]
    per = DYN_TILE // lay.real
    dyn_tiles = lay.n_dev // per

    def take(slots, step):
        for at, events in slots.items():
            @pl.when(step == at)
            def _():
                for event in events:
                    event()

    @pl.loop(0, actor_tiles)
    def _(step):
        @pl.when(step == actor_tiles - 1)
        def _():
            has_come(bk.at[pl.ds(0, n_dp - 1)], "own")
            lanes = lax.broadcasted_iota(jnp.int32, (48, lay.width), 1) // CAP

            def gather(owner, total):
                turned = pltpu.roll(
                    bk[owner * n_blk], lax.rem((owner - me) * CAP + lay.width, lay.width), axis=1
                )
                return jnp.where(lanes == owner, turned, total)

            own = lax.fori_loop(0, n_dp, gather, jnp.zeros((48, lay.width), F32))
            xs[0:48, 0 : lay.real] = own[:, 0 : lay.real]

        where = place_of(step, ACTOR_TILE)
        now_f = framed(0, IN, where)
        now_in = now_f.astype(BF16)
        weight = xs[42:43, where]
        action, log_prob, bent, moved, (a1, da1, a2, da2) = policy(now_in, 0, where)
        judged_in = with_action(now_f, action)
        loss = alpha * log_prob - log_alpha * (log_prob + TARGET_ENTROPY)
        grad_action = jnp.zeros((8, ACTOR_TILE), F32)
        used = act_rows(ACTOR_TILE)
        for k in range(2):
            judged, (_, df1, _, df2) = critic(judged_in, 2 + k)
            loss -= 0.5 * judged
            g2 = outer_sloped(wide[5 + k], -0.5 * weight, df2)
            g1 = sloped(dot(w2h[k], g2), df1)
            grad_action += dot(w1n[k], g1)[0:8]
        grad_latent = 2.0 * alpha * weight * action + grad_action * (1.0 - action * action)
        grad_scale = grad_latent * moved - alpha * weight
        grad_bent = grad_scale * 3.5 * (1.0 - bent * bent)
        g3 = jnp.concatenate(
            [jnp.where(used, grad_latent, 0.0), jnp.where(used, grad_bent, 0.0)], 0
        ).astype(BF16)
        acc_a[...] += dot(g3, a2, NT)
        acc_m[:, 0:16] += dot(ones16(ACTOR_TILE), g3, NT)
        g2 = sloped(dot(head_t[...], g3), da2)
        add_hidden(2, a1, g2)
        g1 = sloped(dot(w2h[2], g2), da1)
        acc_w[2] += dot(now_in, g1, NT)
        acc_l[1:2, 0:ACTOR_TILE] += weight * loss
        acc_l[2:3, 0:ACTOR_TILE] += weight * (log_prob + TARGET_ENTROPY)

    put_matrix(2)
    chains[2][0]()

    @pl.loop(0, critic_tiles)
    def _(step):
        if critic_tiles > 1:
            take({1: [chains[2][1]]}, step)

        where = place_of(step, CRITIC_TILE)
        now_in = framed(0, IN, where).astype(BF16)
        next_f = framed(24, OBS, where)
        reward = xs[23:24, where]
        done = xs[41:42, where]
        next_action, next_prob, _, _, _ = policy(next_f.astype(BF16), 1, where)
        aim_in = with_action(next_f, next_action)
        aim = jnp.minimum(critic(aim_in, 0)[0], critic(aim_in, 1)[0])
        target = reward + DISCOUNT * (1.0 - done) * (aim - alpha * next_prob)
        ys[0:1, where] = target
        critic_pass(0, now_in, where, target)

    put_matrix(0)
    chains[0][0]()
    if critic_tiles == 1:
        chains[2][1]()

    has_come(bk.at[pl.ds(0, (n_dp - 1) * (n_blk - 1))], "plane")
    lane0 = lay.real // 128 * 128

    def add_block(at, carry):
        sides, fills = carry
        slot = slot_of(at)
        return sides + bk[slot, 0:32, lane0 : lane0 + 128], fills + bk[slot, 40:48, 0 : lay.real]

    sides, fills = lax.fori_loop(
        0, lay.n_dev, add_block, (jnp.zeros((32, 128), F32), jnp.zeros((8, lay.real), F32))
    )
    at = lay.real - lane0
    rows_all = float(lay.replay * lay.n_dev)
    centre = sides[0:24, at : at + 1] / rows_all
    scale = lax.rsqrt(sides[0:24, at + 1 : at + 2] / rows_all - centre * centre + 1e-6)
    total = sides[24:25, at : at + 1] + jnp.sum(fills[2:3, :], axis=1, keepdims=True)
    count[...] = jnp.broadcast_to(total, (8, 128))

    @pl.loop(0, critic_tiles)
    def _(step):
        take({critic_tiles - 1: [chains[0][1], chains[2][2]]}, step)
        where = place_of(step, CRITIC_TILE)
        critic_pass(1, framed(0, IN, where).astype(BF16), where, ys[0:1, where])

    put_matrix(1)
    for k in range(3):
        put(R_IN + 24 * k, acc_w[k, 0:24, :])
    put(R_HEAD, acc_a[...])
    rowbuf[0:1, :] = acc_c[0, 0:1, :]
    rowbuf[1:2, :] = acc_c[1, 0:1, :]
    for k in range(3):
        rowbuf[2 + k : 3 + k, :] = acc_h[k, HSAC : HSAC + 1, :]
    put(R_OUT, rowbuf[...])
    folded = jnp.sum(acc_l[...], axis=1, keepdims=True)
    rowbuf[...] = jnp.zeros_like(rowbuf)
    rowbuf[0:1, 0:48] = acc_m[0:1, :]
    rowbuf[0:1, 64:65] = folded[0:1] + folded[1:2]
    rowbuf[0:1, 65:66] = folded[2:3]
    put(R_MISC, rowbuf[...])
    put(R_MISC + 8, jnp.zeros((R_SMALL - R_MISC - 8, HSAC), F32))
    chains[1][0]()

    def dyn_bias(start, width):
        row = jnp.zeros((1, width), F32)
        for e in range(MEMBERS):
            row = jnp.where(me == e, bias[:, start + width * e : start + width * (e + 1)], row)
        return row

    @pl.when(is_dyn)
    def _():
        w1f[0] = jnp.zeros((32, HSAC), F32)
        w1f[0, 0:IN, 0:HDYN] = rounded(dyn_in[dyn_e])
        for at, piece in enumerate(pieces(dyn_bias(DB1, HDYN))):
            w1f[0, IN + at : IN + at + 1, 0:HDYN] = piece.astype(F32)
        w1t[0] = (0.5 * w1f[0].T).astype(BF16)
        rowbuf[...] = jnp.zeros_like(rowbuf)
        rowbuf[0:1, 0:HDYN] = dyn_bias(DB2, HDYN)
        head_row = dyn_bias(DB3, DOUT)
        rowbuf[1:2, 0:HALF] = head_row[:, 0:HALF]
        rowbuf[1:2, 24 : 24 + HALF] = head_row[:, HALF:DOUT]
        rowbuf[2:3, 0:HALF] = bias[:, MAXLV : MAXLV + HALF]
        rowbuf[3:4, 0:HALF] = bias[:, MINLV : MINLV + HALF]
        dcols[...] = rowbuf[...].T
        wide[0] = jnp.broadcast_to(0.5 * dcols[:, 0:1], (HSAC, 128))
        dpack[...] = jnp.zeros_like(dpack)
        dpack[0:HALF, 0:HDYN] = dyn_out[dyn_e, 0:HALF, :]
        dpack[24 : 24 + HALF, 0:HDYN] = dyn_out[dyn_e, HALF:DOUT, :]
        dhead[...] = dpack[0:48, :].astype(BF16)
        dhead_t[...] = (0.5 * rounded(dpack[0:48, :])).T.astype(BF16)
        dpack[...] = jnp.zeros_like(dpack)

        has_come(dhg.at[pl.ds(0, n_blk - 1)], "dyn h")
        has_come(dmg.at[pl.ds(0, n_blk - 1)], "dyn m")
        dhg[z] = dyn_h[dyn_e]
        dmg[z] = dyn_m[dyn_e]
        dmat[...] = jnp.zeros_like(dmat)
        for block in range(n_blk):
            dmat[block * lay.drows : (block + 1) * lay.drows, 0:HDYN] = 0.5 * rounded(dhg[block])
        w2h[0] = dmat[...].astype(BF16)
        w2t[0] = dmat[...].T.astype(BF16)
        for ref in (dacc_h, dacc_w, dacc_o, dacc_m, dacc_b, dacc_l):
            ref[...] = jnp.zeros_like(ref)

    in_dyn = {}
    for at, event in (
        (1, chains[0][2]), (1, chains[1][1]), (2, chains[2][3]), (dyn_tiles - 1, chains[1][2]),
    ):
        in_dyn.setdefault(min(at, dyn_tiles - 1), []).append(event)

    @pl.loop(0, dyn_tiles)
    def _(tile):
        take(in_dyn, tile)

        @pl.when(is_dyn)
        def _():
            for at in range(per):
                slot = slot_of(tile * per + at)
                xt[:, at * lay.real : (at + 1) * lay.real] = bk[slot, :, 0 : lay.real]
            now = xt[0:24, :]
            later = xt[24:48, :]
            row24 = rows_of((24, DYN_TILE))
            scaled = jnp.where(row24 < IN, (now - centre) * scale, 1.0)
            inputs = jnp.concatenate([scaled, (rows_of((8, DYN_TILE)) < 2).astype(F32)], 0).astype(BF16)
            first, slope1 = gated(dot(w1t[0], inputs))
            second, slope2 = gated(dot(w2t[0], first), wide[0])
            out = dot(dhead[...], second) + dcols[0:48, 1:2]
            used = row24 < HALF
            upper = dcols[0:24, 2:3]
            lower = dcols[0:24, 3:4]
            gap1 = upper - out[24:48]
            gap2 = upper - softplus(gap1) - lower
            log_var = lower + softplus(gap2)
            error = out[0:24] - jnp.where(row24 == OBS, now[23:24], later - now)
            inverse = jnp.exp(-log_var)
            weight = xt[42:43, :] * (xt[43:44, :] == me.astype(F32)).astype(F32)
            spread_term = error * error * inverse
            nll = jnp.sum(jnp.where(used, spread_term + log_var, 0.0), axis=0, keepdims=True)
            dacc_l[0:1, :] += weight * nll
            grad_mu = 2.0 * weight * error * inverse
            grad_lv = weight * (1.0 - spread_term)
            open1 = sigmoid(gap1)
            open2 = sigmoid(gap2)
            grad_lv1 = grad_lv * open2
            dacc_b[0] += jnp.where(used, grad_lv1 * (1.0 - open1), 0.0)
            dacc_b[1] += jnp.where(used, grad_lv * (1.0 - open2), 0.0)
            g3 = jnp.concatenate(
                [jnp.where(used, grad_mu, 0.0), jnp.where(used, grad_lv1 * open1, 0.0)], 0
            ).astype(BF16)
            dacc_o[...] += dot(g3, second, NT)
            dacc_m[...] += dot(ones16(DYN_TILE), g3, NT)
            g2 = sloped(dot(dhead_t[...], g3), slope2)
            dacc_h[...] += dot(jnp.concatenate([first, ones16(DYN_TILE)], 0), g2, NT)
            g1 = sloped(dot(w2h[0], g2), slope1)
            dacc_w[...] += dot(inputs, g1, NT)

    out_of = {"pack": dyn_s, "x": dyn_x}

    def member_copy(name, src, owner, kind, sem, peer):
        return on_plane(src, out_of[name].at[owner], send.at[sent[name, kind]], recv.at[sem], peer)

    def give(name, src):
        like_peers(
            lambda peer: member_copy(name, src, dyn_e, "own", here_at[name, "like"] + dyn_e, peer).start()
        )
        member_copy(name, src, dyn_e, "own", here_at[name, "sibling"], sibling).start()

    def hand_on(name):
        def body(peer):
            @pl.when(peer < MEMBERS)
            def _():
                owner = jnp.minimum(peer, MEMBERS - 1)
                view = out_of[name].at[owner]
                member_copy(name, view, owner, "on", here_at[name, "like"] + owner, sibling).wait_recv()
                member_copy(name, view, owner, "on", here_at[name, "sibling"], sibling).start()

        like_peers(body)

    even, odd = (MEMBERS + 1) // 2, MEMBERS // 2
    handed = even - core * (even - odd) - jnp.where(is_dyn, 1, 0)

    def from_sibling(name):
        for side, number in ((0, odd), (1, even)):
            @pl.when(core == side)
            def _():
                has_come(out_of[name].at[pl.ds(0, number)], (name, "sibling"))

    def gave(name):
        @pl.when(is_dyn)
        def _():
            for begin in range(0, n_dp // 2, MEMBERS):
                number = min(MEMBERS, n_dp // 2 - begin)
                has_sent(out_of[name].at[pl.ds(0, number)], (name, "own"))

        for number in (even, even - 1, even - 2):
            @pl.when(handed == number)
            def _():
                has_sent(out_of[name].at[pl.ds(0, number)], (name, "on"))

    def line_rows(ref):
        rows = ref[0 : lay.drows, 0:HDYN]
        for block in range(1, n_blk):
            rows = jnp.where(z == block, ref[block * lay.drows : (block + 1) * lay.drows, 0:HDYN], rows)
        return rows

    mine_rows = pl.ds(pl.multiple_of(z * lay.rows, lay.rows), lay.rows)

    def take_matrix(k):
        has_come(mg.at[k, pl.ds(0, n_dp - 1)], ("tiles", k))
        for chunk in range(n_dp):
            tile = chunk * lay.mat
            half, row = tile // 32, tile % 32
            at = slice(row * 8, (row + lay.mat) * 8)
            piece = mg[k, chunk].reshape(lay.mat * 8, 128)
            mat[k, at, half * 128 : (half + 1) * 128] = piece / total
        normalise(mat.at[k])

    chains[0][3]()

    @pl.when(is_dyn)
    def _():
        dpack[D_IN : D_IN + 24, :] = dacc_w[0:24, :]
        dpack[D_OUT : D_OUT + HALF, :] = dacc_o[0:HALF, :]
        dpack[D_OUT + HALF : D_OUT + DOUT, :] = dacc_o[24 : 24 + HALF, :]
        dpack[D_B2 : D_B2 + 1, :] = dacc_h[HSAC : HSAC + 1, :]
        dpack[D_B3 : D_B3 + 1, 0:48] = dacc_m[0:1, :]
        lanes = lax.broadcasted_iota(jnp.int32, (24, 128), 1)
        bound = jnp.where(
            lanes == 0,
            jnp.sum(dacc_b[0], axis=1, keepdims=True),
            jnp.where(lanes == 1, jnp.sum(dacc_b[1], axis=1, keepdims=True), 0.0),
        )
        dpack[D_UP : D_UP + 2, 0:24] = bound.T[0:2, :]
        dpack[D_LOSS : D_LOSS + 1, 0:128] = jnp.broadcast_to(
            jnp.sum(dacc_l[0:1, :], axis=1, keepdims=True), (1, 128)
        )
        dpack[D_HID : D_HID + lay.drows, 0:HDYN] = line_rows(dacc_h)
        dyn_s[dyn_e] = dpack[...]
        give("pack", dpack)
        dmat[...] = jnp.zeros_like(dmat)
        for block in range(n_blk):
            at = slice(block * lay.drows, (block + 1) * lay.drows)
            dmat[at, 0:HDYN] = MOMENTUM * dmg[block] + dacc_h[at, 0:HDYN] / total
        normalise(dmat)

    def sac_x_copy(k, src, peer):
        name = ("sac x", k)
        return on_plane(src, sac_x.at[k], send.at[sent[name] + peer], recv.at[here_at[name]], peer)

    def own_x(k):
        return mat.at[k, mine_rows]

    def passes_x(k):
        return jnp.logical_and(core == lay.owners[k] % 2, me != lay.owners[k])

    def receive_sac(k):
        pl.when(me != lay.owners[k])(sac_x_copy(k, sac_x.at[k], sibling).wait_recv)
        pl.when(passes_x(k))(sac_x_copy(k, sac_x.at[k], sibling).start)

    def own_matrix(k, before):
        take_matrix(k)
        schulz([mat.at[k]], NS_ITERS, before)
        sac_x[k] = mat[k, mine_rows, :]
        like_peers(lambda peer: sac_x_copy(k, own_x(k), peer).start())
        sac_x_copy(k, own_x(k), sibling).start()

    def sum_end(step):
        pl.when(step == 2)(chains[1][3])
        pl.when(step == NS_ITERS - 1)(chains[1][4])

    def pass_on(step):
        pl.when(step == 2)(functools.partial(hand_on, "pack"))
        pl.when(step == NS_ITERS - 1)(functools.partial(hand_on, "x"))

    @pl.when(is_dyn)
    def _():
        schulz([dmat], NS_ITERS, sum_end)
        rows = line_rows(dmat)
        drow_x[...] = rows
        dyn_x[dyn_e] = rows
        give("x", drow_x)

    if lay.owners[0] >= MEMBERS:
        @pl.when(jnp.logical_not(jnp.logical_or(is_dyn, me == lay.owners[1])))
        def _():
            chains[1][3]()
            chains[1][4]()

    pl.when(me == lay.owners[0])(functools.partial(own_matrix, 0, pass_on))

    @pl.when(me == lay.owners[1])
    def _():
        own_matrix(2, sum_end)
        own_matrix(1, pass_on)

    @pl.when(jnp.logical_and(me != lay.owners[0], me != lay.owners[1]))
    def _():
        hand_on("pack")
        hand_on("x")

    def sent_early():
        has_sent(wg.at[pl.ds(0, n_blk - 1), :, half_rows], "hidden")
        has_sent(wg.at[pl.ds(0, n_blk - 1), :, half_rows], "hidden on")
        has_sent(asked.at[pl.ds(0, n_dp - 1)], "lists")
        has_sent(bk.at[pl.ds(0, n_dp - 1)], "own")
        has_sent(bk.at[pl.ds(0, n_blk - 1)], "line")
        has_sent(bk.at[pl.ds(0, (n_dp - 1) * (n_blk - 1))], "plane")

        @pl.when(is_dyn)
        def _():
            has_sent(dhg.at[pl.ds(0, n_blk - 1)], "dyn h")
            has_sent(dmg.at[pl.ds(0, n_blk - 1)], "dyn m")

        for group in range(3):
            core_sum(group).wait_send()
            has_sent(froms[group].at[pl.ds(0, lay.half - 1)], ("plane sum", group))
        for part in range(4):
            has_sent(line_bytes(part), ("line sum", part))

    sent_early()
    for k in (2, 0, 1):
        receive_sac(k)

    small_on().wait_recv()
    for number, test in ((lay.keepers - 1, z == keeper_z), (lay.keepers, z != keeper_z)):
        for k in range(3):
            pl.when(test)(functools.partial(has_come, kept_bytes(number), ("sac g", k)))

    from_sibling("pack")
    from_sibling("x")

    has_sent(small.at[pl.ds(0, (lay.half - 1) * lay.sml)], "small")
    small_on().wait_send()
    gave("pack")
    gave("x")

    for k in range(3):
        pl.when(me != lay.owners[k])(tile_copy(k).wait_send)
        pl.when(z == keeper_z)(functools.partial(has_sent, kept_bytes(n_dp - 1), ("sac g", k)))
        pl.when(passes_x(k))(sac_x_copy(k, sac_x.at[k], sibling).wait_send)

        @pl.when(me == lay.owners[k])
        def _():
            like_peers(lambda peer: sac_x_copy(k, own_x(k), peer).wait_send())
            sac_x_copy(k, own_x(k), sibling).wait_send()


def adamw(weights, first, second, gradient):
    first = BETA_FIRST * first + (1.0 - BETA_FIRST) * gradient
    second = BETA_SECOND * second + (1.0 - BETA_SECOND) * gradient * gradient
    first_hat = first / (1.0 - BETA_FIRST**STEP)
    second_hat = second / (1.0 - BETA_SECOND**STEP)
    step = first_hat / (jnp.sqrt(second_hat) + 1e-8) + ADAM_DECAY * weights
    return weights - ADAM_RATE * step, first, second


def update_kernel(lay, *refs):
    (
        sac_g, sac_x, dyn_x, dyn_s, small, count, sac_h, dyn_h, dyn_m,
        ci, ci_m, ci_v, ai, ai_m, ai_v, di, di_m, di_v, co, co_m, co_v, ao, ao_m, ao_v,
        do, do_m, do_v, bi, bi_m, bi_v,
        sac_new, sac_mom, dyn_new, dyn_mom, ci_n, ci_mn, ci_vn, ai_n, ai_mn, ai_vn, di_n, di_mn,
        di_vn, co_n, co_mn, co_vn, ao_n, ao_mn, ao_vn, do_n, do_mn, do_vn, bi_n, bi_mn, bi_vn,
        loss, counted, bg,
    ) = refs
    total = count[0:1, 0:1]
    for k in range(3):
        for side in range(2):
            tiles = sac_g[side, k].reshape(sac_mom.shape[1], 128)
            sac_mom[k, :, side * 128 : (side + 1) * 128] = tiles / total
    sac_new[...] = sac_h[...] * (1.0 - MUON_RATE * MUON_DECAY) - MUON_RATE * sac_x[...]
    dyn_rows = dyn_s[:, D_HID : D_HID + dyn_m.shape[1], 0:HDYN]
    dyn_mom[...] = MOMENTUM * dyn_m[...] + dyn_rows / total.reshape(1, 1, 1)
    dyn_new[...] = dyn_h[...] * (1.0 - MUON_RATE * MUON_DECAY) - MUON_RATE * dyn_x[...]

    def rows(row, number):
        def tile(at):
            chunk = at // lay.sml
            return small[(chunk % 2 * lay.half + chunk // 2) * lay.sml + at % lay.sml]

        sides = []
        for side in range(2):
            at = side * (R_SMALL // 8) + row // 8
            sides.append(jnp.concatenate([tile(at + more) for more in range(-(-number // 8))], 0))
        return jnp.concatenate(sides, 1)

    def store(outs, at, values):
        for out, value in zip(outs, values):
            out[at] = value

    outs = (ci_n, ci_mn, ci_vn)
    for k in range(2):
        at = (slice(None), k, slice(None))
        grad = rows(R_IN + 24 * k, 24)
        bg[:, CB1 + HSAC * k : CB1 + HSAC * (k + 1)] = grad[IN : IN + 1]
        store(outs, at, adamw(ci[at], ci_m[at], ci_v[at], grad[0:IN] / total))
    grad = rows(R_IN + 48, 24)
    bg[:, AB1 : AB1 + HSAC] = grad[IN : IN + 1]
    store((ai_n, ai_mn, ai_vn), ..., adamw(ai[...], ai_m[...], ai_v[...], grad[0:OBS] / total))
    grad = rows(R_HEAD, 16)
    for at, row in ((slice(0, ACT), slice(1, 1 + ACT)), (slice(ACT, 2 * ACT), slice(9, 9 + ACT))):
        store((ao_n, ao_mn, ao_vn), at, adamw(ao[at], ao_m[at], ao_v[at], grad[row] / total))
    grad = rows(R_OUT, 8)
    store((co_n, co_mn, co_vn), ..., adamw(co[...], co_m[...], co_v[...], grad[0:2] / total))
    bg[:, CB2 : CB2 + HSAC] = grad[2:3]
    bg[:, CB2 + HSAC : CB2 + 2 * HSAC] = grad[3:4]
    bg[:, AB2 : AB2 + HSAC] = grad[4:5]
    grad = rows(R_MISC, 8)
    bg[:, CB3 : CB3 + 1] = grad[0:1, 16:17]
    bg[:, CB3 + 1 : CB3 + 2] = grad[0:1, 32:33]
    bg[:, AB3 : AB3 + ACT] = grad[0:1, 1 : 1 + ACT]
    bg[:, AB3 + ACT : AB3 + 2 * ACT] = grad[0:1, 9 : 9 + ACT]
    bg[:, LOGA : LOGA + 1] = -grad[0:1, 65:66]
    total_loss = grad[0:1, 64:65]
    up = jnp.zeros((1, HALF), F32)
    low = jnp.zeros((1, HALF), F32)
    for e in range(MEMBERS):
        pack = dyn_s[e]
        total_loss = total_loss + pack[D_LOSS : D_LOSS + 1, 0:1]
        up = up + pack[D_UP : D_UP + 1, 0:HALF]
        low = low + pack[D_LOW : D_LOW + 1, 0:HALF]
        bg[:, DB1 + HDYN * e : DB1 + HDYN * (e + 1)] = pack[IN : IN + 1, 0:HDYN]
        bg[:, DB2 + HDYN * e : DB2 + HDYN * (e + 1)] = pack[D_B2 : D_B2 + 1, 0:HDYN]
        bg[:, DB3 + DOUT * e : DB3 + DOUT * e + HALF] = pack[D_B3 : D_B3 + 1, 0:HALF]
        bg[:, DB3 + DOUT * e + HALF : DB3 + DOUT * (e + 1)] = pack[D_B3 : D_B3 + 1, 24 : 24 + HALF]
        grad = pack[0:IN, 0:HDYN] / total
        store((di_n, di_mn, di_vn), e, adamw(di[e], di_m[e], di_v[e], grad))
        grad = pack[D_OUT : D_OUT + DOUT, 0:HDYN] / total
        store((do_n, do_mn, do_vn), e, adamw(do[e], do_m[e], do_v[e], grad))
    bg[:, MAXLV : MAXLV + HALF] = up
    bg[:, MINLV : MINLV + HALF] = low
    lane = lax.broadcasted_iota(jnp.int32, (1, NB), 1)
    bounds = jnp.where(
        jnp.logical_and(lane >= MAXLV, lane < MINLV),
        BOUND_WEIGHT,
        jnp.where(jnp.logical_and(lane >= MINLV, lane < LOGA), -BOUND_WEIGHT, 0.0),
    )
    grad = bg[...] / total + bounds
    flat = [ref[...].reshape(1, NB) for ref in (bi, bi_m, bi_v)]
    store((bi_n, bi_mn, bi_vn), ..., [value.reshape(NB) for value in adamw(*flat, grad)])
    loss[...] = total_loss
    counted[...] = total


def shards(
    lay, replay, model_rows, requests, member_of, model_live, noise, sac_hidden, sac_hidden_mom,
    dyn_hidden, dyn_hidden_mom, crit_in, crit_in_m, crit_in_v, act_in, act_in_m, act_in_v, dyn_in,
    dyn_in_m, dyn_in_v, crit_out, crit_out_m, crit_out_v, act_out, act_out_m, act_out_v, dyn_out,
    dyn_out_m, dyn_out_v, biases, biases_m, biases_v, targ_in, targ_hidden, targ_out, targ_bias,
):
    n_dp, n_blk = lay.n_dp, lay.n_blk
    spec = pl.BlockSpec(memory_space=pltpu.VMEM)

    def flip(value):
        return jnp.transpose(value, (1, 0, 2))

    def swap(value):
        return jnp.swapaxes(value, -1, -2)

    def kept(value):
        return pltpu.with_memory_space_constraint(value, pltpu.VMEM)

    inputs = (
        replay, model_rows, requests, member_of, model_live, jnp.transpose(noise, (2, 0, 1)),
        sac_hidden, sac_hidden_mom, dyn_hidden, dyn_hidden_mom, flip(crit_in), act_in, dyn_in,
        crit_out, swap(act_out), swap(dyn_out), biases, flip(targ_in), targ_hidden, targ_out,
        targ_bias,
    )
    shape = jax.ShapeDtypeStruct
    rows, drows = lay.rows, lay.drows
    out_shape = (
        pltpu.VMEM((2, 3, rows // 8, 8, 128), F32),
        pltpu.VMEM((3, rows, HSAC), F32),
        pltpu.VMEM((MEMBERS, drows, HDYN), F32),
        pltpu.VMEM((MEMBERS, D_ROWS, HSAC), F32),
        pltpu.VMEM((32, 8, 128), F32),
        pltpu.VMEM((8, 128), F32),
    )

    def vm(*dims, kind=F32):
        return pltpu.VMEM(dims, kind)

    scratch = [
        vm(n_blk, 3, rows, HSAC, kind=BF16),
        vm(2, n_dp, CAP, kind=jnp.int32),
        vm(n_dp, 2, n_dp, CAP, kind=jnp.int32),
        vm(n_blk, drows, HDYN),
        vm(n_blk, drows, HDYN),
        vm(lay.n_dev, 48, lay.width),
        vm(56, lay.batch),
        vm(2, 8, lay.batch),
        vm(8, lay.batch),
        vm(5, 32, HSAC),
        vm(5, HSAC, 32, kind=BF16),
        vm(2, 16, HSAC, kind=BF16),
        vm(5, HSAC, HSAC, kind=BF16),
        vm(3, HSAC, HSAC, kind=BF16),
        vm(5, 16, HSAC, kind=BF16),
        vm(HSAC, 16, kind=BF16),
        vm(16, HSAC),
        vm(8, HSAC),
        vm(7, HSAC, 128),
        vm(128, 8),
        vm(3, HSAC + 16, HSAC),
        vm(3, 32, HSAC),
        vm(2, 16, HSAC),
        vm(16, HSAC),
        vm(16, 48),
        vm(8, max(CRITIC_TILE, ACTOR_TILE)),
        *[vm(2, lay.half, chunk, 8, 128) for chunk in lay.chunks],
        *[vm(lay.half, chunk, 8, 128) for chunk in lay.chunks],
        *[vm(lay.half, chunk, 8, 128) for chunk in lay.chunks],
        *[vm(n_blk, chunk, 8, 128) for chunk in lay.chunks],
        *[vm(chunk, 8, 128) for chunk in lay.chunks],
        *[vm(chunk, 8, 128) for chunk in lay.chunks],
        vm(3, n_dp, lay.mat, 8, 128),
        vm(3, HSAC, HSAC),
        vm(HSAC, 8),
        vm(HSAC + 16, HSAC),
        vm(32, HSAC),
        vm(48, HSAC),
        vm(16, 48),
        vm(2, 24, DYN_TILE),
        vm(8, DYN_TILE),
        vm(48, DYN_TILE),
        vm(HSAC, HSAC),
        vm(D_ROWS, HSAC),
        vm(drows, HDYN),
        vm(1, NB),
        vm(48, HSAC, kind=BF16),
        vm(HSAC, 48, kind=BF16),
    ]
    scratch += [pltpu.SemaphoreType.DMA((lay.departures,)), pltpu.SemaphoreType.DMA((lay.arrivals,))]
    varying = 4 * (lay.n_dev * 48 * lay.width + 72 * lay.batch + 48 * lay.replay)
    gathered = pl.pallas_call(
        functools.partial(main_kernel, lay),
        out_shape=out_shape,
        in_specs=[spec] * len(inputs),
        out_specs=[spec] * len(out_shape),
        scratch_shapes=scratch,
        compiler_params=pltpu.CompilerParams(
            collective_id=0, has_side_effects=True, vmem_limit_bytes=26 * 2**20 + varying
        ),
        name="step",
    )(*[pltpu.with_memory_space_constraint(value, pltpu.HBM) for value in inputs])
    params = (
        sac_hidden, dyn_hidden, dyn_hidden_mom,
        flip(crit_in), flip(crit_in_m), flip(crit_in_v), act_in, act_in_m, act_in_v,
        dyn_in, dyn_in_m, dyn_in_v, crit_out, crit_out_m, crit_out_v,
        swap(act_out), swap(act_out_m), swap(act_out_v),
        swap(dyn_out), swap(dyn_out_m), swap(dyn_out_v), biases, biases_m, biases_v,
    )
    new_shape = [shape(sac_hidden.shape, F32)] + [shape(value.shape, F32) for value in params]
    new_shape += [shape((1, 1), F32)] * 2
    out = pl.pallas_call(
        functools.partial(update_kernel, lay),
        out_shape=tuple(new_shape),
        in_specs=[spec] * (len(gathered) + len(params)),
        out_specs=[spec] * len(new_shape),
        scratch_shapes=[vm(1, NB)],
        compiler_params=pltpu.CompilerParams(vmem_limit_bytes=16 * 2**20),
        name="update",
    )(*[kept(value) for value in gathered], *params)
    out = list(out)
    for at in (4, 5, 6):
        out[at] = flip(out[at])
    for at in (16, 17, 18, 19, 20, 21):
        out[at] = swap(out[at])
    for at in (25, 26):
        out[at] = out[at].reshape(())
    return tuple(out)


def solution(mesh):
    both = ("dp", "blk")
    sharded = (
        P(None, both), P(None, both), P(both, None), P(both, None), P(both), P(None, both, None),
    )
    hidden = (P(None, "blk", None),) * 4

    def step(replay, model_rows, *others):
        lay = Layout(mesh, replay.shape[1], model_rows.shape[1])
        return shards(lay, replay, model_rows, *others)

    return jax.shard_map(
        step,
        mesh=mesh,
        in_specs=sharded + hidden + (P(),) * 25,
        out_specs=hidden + (P(),) * 23,
        check_vma=False,
    )
```

```python
import functools

import jax
import jax.numpy as jnp
from jax import lax
from jax.experimental import pallas as pl
from jax.experimental.pallas import tpu as pltpu
from jax.sharding import PartitionSpec as P

OBS = 17
ACT = 6
IN = OBS + ACT
FEAT = 42
HDYN = 200
HSAC = 256
MEMBERS = 7
DOUT = 36
HALF = DOUT // 2
NB = 4639
NS_ITERS = 5
STEP = 10
CAP = 8
CRITIC_TILE = 640
ACTOR_TILE = 640
DYN_TILE = 512
ROWS = 32

DISCOUNT = 0.99
TARGET_ENTROPY = -6.0
BOUND_WEIGHT = 0.01
MOMENTUM = 0.95
MUON_RATE = 0.4
MUON_DECAY = 0.01
ADAM_RATE = 0.1
ADAM_DECAY = 0.01
BETA_FIRST = 0.9
BETA_SECOND = 0.999
COEF_LINEAR = 3.4445
COEF_CUBIC = -4.775
COEF_QUINTIC = 2.0315

CB1, CB2, CB3, AB1, AB2, AB3 = 0, 512, 1024, 1026, 1282, 1538
DB1, DB2, DB3, MAXLV, MINLV, LOGA = 1550, 2950, 4350, 4602, 4620, 4638

R_IN, R_HEAD, R_OUT, R_MISC, R_SMALL = 0, 72, 88, 96, 128
D_IN, D_OUT, D_B2, D_B3, D_UP, D_LOW, D_LOSS, D_HID, D_ROWS = 0, 24, 60, 61, 62, 63, 64, 72, 128

F32, BF16 = jnp.float32, jnp.bfloat16
MESH = pl.DeviceIdType.MESH
NN = (((1,), (0,)), ((), ()))
NT = (((1,), (1,)), ((), ()))


def dot(a, b, dims=NN):
    return lax.dot_general(a, b, dims, preferred_element_type=F32)


def rounded(v):
    return v.astype(BF16).astype(F32)


def pieces(v):
    high = v.astype(BF16)
    rest = v - high.astype(F32)
    middle = rest.astype(BF16)
    return high, middle, (rest - middle.astype(F32)).astype(BF16)


def split(v):
    high = v.astype(BF16)
    return high, (v - high.astype(F32)).astype(BF16)


def product(a, b, dims=NN):
    left = jnp.concatenate([a[0], a[0], a[1]], 1)
    right = jnp.concatenate([b[0], b[1], b[0]], dims[0][1][0])
    half = left.shape[0] // 2
    return jnp.concatenate([dot(left[:half], right, dims), dot(left[half:], right, dims)], 0)


def softplus(v):
    return jnp.maximum(v, 0.0) + jnp.log1p(jnp.exp(-jnp.abs(v)))


def sigmoid(v):
    return 0.5 + 0.5 * jnp.tanh(0.5 * v)


def gate(half):
    up = 1.0 + jnp.tanh(half)
    value = half * up
    return value, up + value * (2.0 - up)


def by_rows(body, *arrays):
    done = [
        body(*[array[at : at + ROWS] for array in arrays]) for at in range(0, arrays[0].shape[0], ROWS)
    ]
    return [jnp.concatenate(parts, 0) for parts in zip(*done)]


def spread_to(column, width):
    return jnp.concatenate([column] * (width // 128), 1)


def gated(half, column=None):
    def body(part, *offset):
        value, slope = gate(part + spread_to(offset[0], part.shape[1]) if offset else part)
        return value.astype(BF16), slope

    return by_rows(body, half, *([] if column is None else [column]))


def sloped(grad, slope):
    return by_rows(lambda part, by: ((part * by).astype(BF16),), grad, slope)[0]


def outer_sloped(column, row, slope):
    return by_rows(lambda part, by: (((spread_to(part, by.shape[1]) * row) * by).astype(BF16),), column, slope)[0]


def rows_of(shape):
    return lax.broadcasted_iota(jnp.int32, shape, 0)


def schulz(refs, steps, before=None):
    @pl.loop(0, steps)
    def _(step):
        if before is not None:
            before(step)
        matrices = [ref[...] for ref in refs]
        parts = [split(matrix) for matrix in matrices]
        grams = [product(part, part, NT) for part in parts]
        halves = [split(gram) for gram in grams]
        squares = [product(half, half) for half in halves]
        blends = [
            split(COEF_CUBIC * gram + COEF_QUINTIC * square) for gram, square in zip(grams, squares)
        ]
        moved = [product(blend, part) for blend, part in zip(blends, parts)]
        for ref, matrix, move in zip(refs, matrices, moved):
            ref[...] = COEF_LINEAR * matrix + move


def normalise(ref):
    moment = ref[...]
    norm = jnp.sqrt(jnp.sum(jnp.sum(moment * moment, axis=1, keepdims=True), axis=0, keepdims=True))
    ref[...] = moment / (norm + 1e-7)


class Layout:
    def __init__(self, mesh, replay, model):
        self.n_dp = mesh.shape["dp"]
        self.half = self.n_dp // 2
        self.n_blk = mesh.shape["blk"]
        self.n_dev = self.n_dp * self.n_blk
        self.replay = replay
        self.model = model
        self.real = self.n_dp * CAP
        self.batch = self.real + model
        self.width = -(-(self.real + 2) // 128) * 128
        self.rows = HSAC // self.n_blk
        self.drows = HDYN // self.n_blk
        self.mat = 64 // self.n_dp
        self.sml = 32 // self.n_dp
        self.chunks = (self.mat, self.mat + self.sml, self.mat)
        groups = [(name, g) for name in ("core sum", "plane sum") for g in range(3)]
        groups += [("line sum", g) for g in range(4)]
        common = ["hidden", "hidden on", "lists", "own", "line", "plane", "dyn h", "dyn m", "small", "small on"]
        common += groups
        kinds = [(name, kind) for name in ("pack", "x") for kind in ("own", "on")]
        tiles = [(name, k) for name in ("tiles", "tiles on") for k in range(3)]
        sent = common + tiles + kinds
        self.sent = {name: at for at, name in enumerate(sent)}
        self.departures = len(sent)
        self.here, self.arrivals = {}, 0
        tiles += [("pack", "sibling"), ("x", "sibling")]
        for name in common + tiles:
            self.here[name] = self.arrivals
            self.arrivals += 1
        for name in ("pack", "x"):
            self.here[name, "like"] = self.arrivals
            self.arrivals += MEMBERS


OPERANDS = 23
FIRST, SECOND = 3, 16


def main_kernel(lay, *refs):
    n_in = OPERANDS
    sources, held = refs[:n_in], refs[n_in : 2 * n_in]
    (
        sac_h, requests, member, replay, live, model, noise, biases, targ_in, crit_in, act_in, targ_bias,
        targ_hidden, crit_out, targ_out, act_out, dyn_h, dyn_m, crit_out_m, crit_out_v, sac_m, dyn_in, dyn_out,
    ) = held
    loads = refs[2 * n_in]
    refs = refs[2 * n_in + 1 :]
    (
        sac_g, sac_x, dyn_x, dyn_s, small, count, crit_rows,
        wg, lists, asked, dhg, dmg, bk, xs, nz, ys, w1f, w1t, w1n, w2t, w2h, heads, head_t, head_f,
        rowbuf, wide, headcol, acc_h, acc_w, acc_c, acc_a, acc_m, acc_l, grid_0, grid_1, grid_2, core_0, core_1,
        core_2, from_0, from_1, from_2, zr_0, zr_1, zr_2, zf_0, zf_1, zf_2, sum_0, sum_1, sum_2, mg, mat, dcols, dacc_h, dacc_w, dacc_o, dacc_m, dacc_b, dacc_l, xt, dmat,
        dpack, drow_x, bias, dhead, dhead_t, *rest,
    ) = refs
    send, recv = rest
    sent, here_at = lay.sent, lay.here
    grids, cores, froms = (grid_0, grid_1, grid_2), (core_0, core_1, core_2), (from_0, from_1, from_2)
    zrs, zfs, totals = (zr_0, zr_1, zr_2), (zf_0, zf_1, zf_2), (sum_0, sum_1, sum_2)
    n_dp, n_blk = lay.n_dp, lay.n_blk
    me = lax.axis_index("dp")
    z = lax.axis_index("blk")
    core, like = lax.rem(me, 2), me // 2
    sibling = me + 1 - 2 * core
    is_dyn = me < MEMBERS
    dyn_e = jnp.minimum(me, MEMBERS - 1)

    def on_plane(src, dst, ssem, rsem, peer):
        return pltpu.make_async_remote_copy(
            src_ref=src, dst_ref=dst, send_sem=ssem, recv_sem=rsem,
            device_id={"dp": peer}, device_id_type=MESH,
        )

    def on_line(src, dst, ssem, rsem, peer):
        return pltpu.make_async_remote_copy(
            src_ref=src, dst_ref=dst, send_sem=ssem, recv_sem=rsem,
            device_id={"blk": peer}, device_id_type=MESH,
        )

    def over(number, body):
        if number <= 8:
            for off in range(1, number):
                body(off)
        else:
            pl.loop(1, number)(body)

    def plane_peers(body):
        over(n_dp, lambda off: body(lax.rem(me + off, n_dp)))

    def like_peers(body):
        over(n_dp // 2, lambda off: body(lax.rem(me + 2 * off, n_dp)))

    def line_peers(body):
        over(n_blk, lambda off: body(lax.rem(z + off, n_blk)))

    def has_sent(view, name):
        at = send.at[sent[name]]
        on_plane(view, view, at, at, sibling).wait_send()

    def has_come(view, name):
        at = recv.at[here_at[name]]
        on_plane(view, view, at, at, sibling).wait_recv()

    copies = [
        pltpu.make_async_copy(src, dst, loads.at[at]) for at, (src, dst) in enumerate(zip(sources, held))
    ]

    def arrived(begin, end):
        for copy in copies[begin:end]:
            copy.wait()

    barrier = pltpu.get_barrier_semaphore()
    plane_peers(lambda peer: pl.semaphore_signal(barrier, inc=1, device_id={"dp": peer}, device_id_type=MESH))
    line_peers(lambda peer: pl.semaphore_signal(barrier, inc=1, device_id={"blk": peer}, device_id_type=MESH))
    for copy in copies:
        copy.start()
    arrived(0, FIRST)
    wg[0] = sac_h[...].astype(BF16)
    lists[0] = requests[...]
    lists[1] = member[...]
    pl.semaphore_wait(barrier, n_dp - 1 + n_blk - 1)

    half_rows = pl.ds(pl.multiple_of(core * (lay.rows // 2), lay.rows // 2), lay.rows // 2)

    def slot_from(owner, at):
        return lax.rem(owner - at + n_blk, n_blk)

    def hidden_copy(peer):
        src = wg.at[0, :, half_rows]
        dst = wg.at[slot_from(z, peer), :, half_rows]
        return on_line(src, dst, send.at[sent["hidden"]], recv.at[here_at["hidden"]], peer)

    def hidden_on():
        view = wg.at[pl.ds(1, n_blk - 1), :, half_rows]
        return on_plane(view, view, send.at[sent["hidden on"]], recv.at[here_at["hidden on"]], sibling)

    def list_copy(peer):
        return on_plane(lists, asked.at[me], send.at[sent["lists"]], recv.at[here_at["lists"]], peer)

    line_peers(lambda peer: hidden_copy(peer).start())
    plane_peers(lambda peer: list_copy(peer).start())
    asked[me] = lists[...]

    def dyn_h_copy(peer):
        return on_line(dyn_h.at[dyn_e], dhg.at[z], send.at[sent["dyn h"]], recv.at[here_at["dyn h"]], peer)

    def dyn_m_copy(peer):
        return on_line(dyn_m.at[dyn_e], dmg.at[z], send.at[sent["dyn m"]], recv.at[here_at["dyn m"]], peer)

    arrived(FIRST, SECOND)
    alive = live[...].astype(F32).reshape(1, lay.model)
    data = replay[...]
    sums = jnp.sum(data[0:24], axis=1, keepdims=True)
    squares = jnp.sum(data[0:24] * data[0:24], axis=1, keepdims=True)
    living = jnp.sum(alive, axis=1, keepdims=True)

    has_come(asked.at[pl.ds(0, n_dp - 1)], "lists")
    spread = (
        lax.rem(lax.broadcasted_iota(jnp.int32, (CAP, lay.real), 1), CAP)
        == lax.broadcasted_iota(jnp.int32, (CAP, lay.real), 0)
    ).astype(F32)
    here = (
        lax.broadcasted_iota(jnp.int32, (n_dp, lay.real), 1) // CAP
        == lax.broadcasted_iota(jnp.int32, (n_dp, lay.real), 0)
    )

    def in_lanes(which):
        values = asked[:, which, me, :].astype(F32)
        wide = lax.dot_general(
            values, spread, NN, precision=lax.Precision.HIGHEST, preferred_element_type=F32
        )
        return jnp.sum(jnp.where(here, wide, 0.0), axis=0, keepdims=True)

    slots = in_lanes(0)
    wanted = jnp.maximum(slots, 0.0).astype(jnp.int32)
    hot = (rows_of((lay.replay, lay.real)) == wanted).astype(BF16)
    padded = jnp.concatenate([data, jnp.zeros((48 - FEAT, lay.replay), F32)], 0)
    chosen = dot(jnp.concatenate(pieces(padded), 0), hot)
    chosen = chosen[0:48] + chosen[48:96] + chosen[96:144]
    mine = me * n_blk
    bk[mine, 0:FEAT, 0 : lay.real] = chosen[0:FEAT]
    bk[mine, 42:43, 0 : lay.real] = (slots >= 0.0).astype(F32)
    bk[mine, 43:44, 0 : lay.real] = in_lanes(1)
    bk[mine, 44:48, 0 : lay.real] = jnp.zeros((4, lay.real), F32)
    bk[mine, :, lay.real : lay.width] = jnp.zeros((48, lay.width - lay.real), F32)
    bk[mine, 0:24, lay.real : lay.real + 1] = sums
    bk[mine, 0:24, lay.real + 1 : lay.real + 2] = squares
    bk[mine, 24:25, lay.real : lay.real + 1] = living

    def slot_of(block):
        line = lax.rem(block, n_blk)
        return block - line + slot_from(line, z)

    def block_line(peer):
        dst = bk.at[me * n_blk + slot_from(z, peer)]
        return on_line(bk.at[mine], dst, send.at[sent["line"]], recv.at[here_at["line"]], peer)

    def block_own(peer):
        view = bk.at[mine]
        return on_plane(view, view, send.at[sent["own"]], recv.at[here_at["own"]], peer)

    def block_plane(peer):
        view = bk.at[pl.ds(mine + 1, n_blk - 1)]
        return on_plane(view, view, send.at[sent["plane"]], recv.at[here_at["plane"]], peer)

    plane_peers(lambda peer: block_own(peer).start())
    line_peers(lambda peer: block_line(peer).start())

    arrived(SECOND, n_in)
    crit_rows[0:2, :] = crit_out[...]
    crit_rows[2:4, :] = crit_out_m[...]
    crit_rows[4:6, :] = crit_out_v[...]
    crit_rows[6:8, :] = jnp.zeros((2, HSAC), F32)

    @pl.when(is_dyn)
    def _():
        line_peers(lambda peer: dyn_h_copy(peer).start())
        line_peers(lambda peer: dyn_m_copy(peer).start())

    bias[...] = biases[...].reshape(1, NB)
    xs[42:56, :] = jnp.zeros((14, lay.batch), F32)
    xs[0:FEAT, lay.real : lay.batch] = model[...]
    xs[42:43, lay.real : lay.batch] = alive
    nz[...] = jnp.zeros_like(nz)
    for which in range(2):
        nz[which, 1:7, :] = noise[:, which, :]
    firsts = [
        (targ_in[:, 0, :], targ_bias[0:1, 0:HSAC]),
        (targ_in[:, 1, :], targ_bias[1:2, 0:HSAC]),
        (crit_in[:, 0, :], bias[:, CB1 : CB1 + HSAC]),
        (crit_in[:, 1, :], bias[:, CB1 + HSAC : CB1 + 2 * HSAC]),
        (act_in[...], bias[:, AB1 : AB1 + HSAC]),
    ]
    w1f[...] = jnp.zeros_like(w1f)
    for net, (weights, offset) in enumerate(firsts):
        w1f[net, 0 : weights.shape[0], :] = rounded(weights)
        for at, piece in enumerate(pieces(offset)):
            w1f[net, IN + at : IN + at + 1, :] = piece.astype(F32)
        w1t[net] = (0.5 * w1f[net].T).astype(BF16)
    for k in range(2):
        w1n[k] = w1f[2 + k, 16:32, :].astype(BF16)
    for net in range(2):
        w2t[net] = (0.5 * rounded(targ_hidden[net])).T.astype(BF16)
    has_come(wg.at[pl.ds(0, n_blk - 1), :, half_rows], "hidden")
    hidden_on().start()

    rowbuf[...] = jnp.zeros_like(rowbuf)
    rowbuf[0:1, :] = targ_bias[0:1, HSAC : 2 * HSAC]
    rowbuf[1:2, :] = targ_bias[1:2, HSAC : 2 * HSAC]
    rowbuf[2:3, :] = bias[:, CB2 : CB2 + HSAC]
    rowbuf[3:4, :] = bias[:, CB2 + HSAC : CB2 + 2 * HSAC]
    rowbuf[4:5, :] = bias[:, AB2 : AB2 + HSAC]
    rowbuf[5:7, :] = rounded(crit_out[...])
    columns = 0.5 * rowbuf[...].T
    for at in range(7):
        wide[at] = jnp.broadcast_to(columns[:, at : at + 1], (HSAC, 128))
    rowbuf[...] = jnp.zeros_like(rowbuf)
    rowbuf[0:1, 1:7] = bias[:, AB3 : AB3 + ACT]
    rowbuf[0:1, 9:15] = bias[:, AB3 + ACT : AB3 + 2 * ACT]
    headcol[...] = rowbuf[:, 0:128].T
    head_f[...] = jnp.zeros_like(head_f)
    for k in range(2):
        head_f[0:1, :] = targ_out[k : k + 1, :]
        heads[k] = head_f[...].astype(BF16)
        head_f[0:1, :] = crit_out[k : k + 1, :]
        heads[2 + k] = head_f[...].astype(BF16)
    head_f[0:1, :] = jnp.zeros((1, HSAC), F32)
    head_f[1:7, :] = act_out[0:ACT, :]
    head_f[9:15, :] = act_out[ACT : 2 * ACT, :]
    heads[4] = head_f[...].astype(BF16)
    head_t[...] = (0.5 * rounded(head_f[...])).T.astype(BF16)
    for ref in (acc_h, acc_w, acc_c, acc_a, acc_m, acc_l):
        ref[...] = jnp.zeros_like(ref)

    has_come(wg.at[pl.ds(0, n_blk - 1), :, half_rows], "hidden on")
    for k in range(3):
        for block in range(n_blk):
            w2h[k, block * lay.rows : (block + 1) * lay.rows, :] = (
                0.5 * wg[slot_from(block, z), k].astype(F32)
            ).astype(BF16)
        w2t[2 + k] = w2h[k].astype(F32).T.astype(BF16)

    log_alpha = bias[:, LOGA : LOGA + 1]
    alpha = jnp.exp(log_alpha)
    last = [
        targ_bias[0:1, 2 * HSAC : 2 * HSAC + 1],
        targ_bias[1:2, 2 * HSAC : 2 * HSAC + 1],
        bias[:, CB3 : CB3 + 1],
        bias[:, CB3 + 1 : CB3 + 2],
    ]
    critic_tiles = lay.batch // CRITIC_TILE
    actor_tiles = lay.batch // ACTOR_TILE

    def act_rows(width):
        row8 = rows_of((8, width))
        return jnp.logical_and(row8 >= 1, row8 < 1 + ACT)

    def place_of(step, width):
        return pl.ds(pl.multiple_of(lax.rem(step + 1, lay.batch // width) * width, width), width)

    def ones16(width):
        return jnp.ones((16, width), BF16)

    def framed(first_row, used, where):
        row32 = rows_of((32, where.size))
        ones3 = jnp.logical_and(row32 >= IN, row32 < IN + 3).astype(F32)
        return jnp.where(row32 < used, xs[first_row : first_row + 32, where], ones3)

    def hidden(inputs, net):
        first, slope1 = gated(dot(w1t[net], inputs))
        second, slope2 = gated(dot(w2t[net], first), wide[net])
        return first, slope1, second, slope2

    def policy(inputs, which, where):
        first, slope1, second, slope2 = hidden(inputs, 4)
        out = dot(heads[4], second) + headcol[0:16, 0:1]
        bent = jnp.tanh(out[8:16])
        log_scale = -5.0 + 3.5 * (bent + 1.0)
        draw = nz[which, :, where]
        moved = jnp.exp(log_scale) * draw
        latent = out[0:8] + moved
        terms = (
            -0.5 * draw * draw
            - log_scale
            - 0.9189385
            - 2.0 * (0.6931472 - latent - softplus(-2.0 * latent))
        )
        used = act_rows(where.size)
        log_prob = jnp.sum(jnp.where(used, terms, 0.0), axis=0, keepdims=True)
        action = jnp.where(used, jnp.tanh(latent), 0.0)
        return action, log_prob, bent, moved, (first, slope1, second, slope2)

    def with_action(inputs, action):
        middle_rows = jnp.where(act_rows(action.shape[1]), action, inputs[16:24])
        return jnp.concatenate([inputs[0:16], middle_rows, inputs[24:32]], 0).astype(BF16)

    def critic(inputs, net):
        kept = hidden(inputs, net)
        value = dot(heads[net], kept[2])[0:1] + last[net]
        return value, kept

    def add_hidden(k, first, grad):
        acc_h[k] += dot(jnp.concatenate([first, ones16(grad.shape[1])], 0), grad, NT)

    has_come(bk.at[pl.ds(0, n_blk - 1)], "line")
    plane_peers(lambda peer: block_plane(peer).start())

    def critic_pass(k, now_in, where, target):
        weight = xs[42:43, where]
        value, (c1, dc1, c2, dc2) = critic(now_in, 2 + k)
        miss = value - target
        g3 = rounded(weight * miss)
        g3_rows = jnp.where(rows_of((16, CRITIC_TILE)) == 0, g3, 0.0).astype(BF16)
        acc_c[k] += dot(g3_rows, c2, NT)
        acc_m[:, 16 + 16 * k : 32 + 16 * k] += dot(ones16(CRITIC_TILE), g3_rows, NT)
        g2 = outer_sloped(wide[5 + k], g3, dc2)
        add_hidden(k, c1, g2)
        g1 = sloped(dot(w2h[k], g2), dc1)
        acc_w[k] += dot(now_in, g1, NT)
        acc_l[0:1, 0:CRITIC_TILE] += weight * (0.5 * miss * miss)

    def put_matrix(k):
        for chunk in range(n_dp):
            tile = chunk * lay.mat
            side, row = tile // 32, tile % 32
            grids[k][chunk % 2, chunk // 2, 0 : lay.mat] = acc_h[
                k, row * 8 : (row + lay.mat) * 8, side * 128 : (side + 1) * 128
            ].reshape(lay.mat, 8, 128)

    def put(row, value):
        for at in range(value.shape[0] // 8):
            for side in range(value.shape[1] // 128):
                tile = side * (R_SMALL // 8) + row // 8 + at
                chunk = tile // lay.sml
                grid_1[chunk % 2, chunk // 2, lay.mat + tile % lay.sml] = value[
                    at * 8 : at * 8 + 8, side * 128 : (side + 1) * 128
                ]

    def core_sum(group):
        name = ("core sum", group)
        return on_plane(
            grids[group].at[1 - core], cores[group], send.at[sent[name]], recv.at[here_at[name]], sibling
        )

    def plane_sum(group, peer):
        name = ("plane sum", group)
        return on_plane(
            cores[group].at[peer // 2], froms[group].at[like], send.at[sent[name]], recv.at[here_at[name]], peer
        )

    def fold_core(group):
        core_sum(group).wait_recv()
        cores[group][...] += grids[group][core]
        like_peers(lambda peer: plane_sum(group, peer).start())

    def line_part(part):
        return (1, pl.ds(lay.mat, lay.sml)) if part == 3 else (part, pl.ds(0, lay.mat))

    def line_sum(part, peer):
        group, tiles = line_part(part)
        name = ("line sum", part)
        src, dst = zfs[group].at[tiles], zrs[group].at[z, tiles]
        return on_line(src, dst, send.at[sent[name]], recv.at[here_at[name]], peer)

    def line_bytes(part):
        group, tiles = line_part(part)
        return zrs[group].at[pl.ds(0, n_blk - 1), tiles]

    first_tile = me * lay.mat
    side = first_tile // 32
    row_tile = lax.rem(first_tile, 32)
    keeper_z = row_tile * 8 // lay.rows
    local_tile = row_tile - keeper_z * (lay.rows // 8)

    def fold_plane(group):
        has_come(froms[group].at[pl.ds(0, lay.half - 1)], ("plane sum", group))
        froms[group][like] = cores[group][like]
        whole = froms[group][0]
        for at in range(1, lay.half):
            whole = whole + froms[group][at]
        zfs[group][...] = whole

        @pl.when(z == keeper_z)
        def _():
            held_rows = pl.ds(pl.multiple_of(local_tile * 8, 8), lay.mat * 8)
            held_lanes = pl.ds(pl.multiple_of(side * 128, 128), 128)
            old = sac_m[group, held_rows, held_lanes].reshape(lay.mat, 8, 128)
            zfs[group][0 : lay.mat] += (MOMENTUM * count[0:1, 0:1]).reshape(1, 1, 1) * old

        for part in (1, 3) if group == 1 else (group,):
            line_peers(lambda peer: line_sum(part, peer).start())

    def tile_copy(k, peer):
        name = ("tiles", k)
        src = totals[k].at[pl.ds(0, lay.mat)]
        return on_plane(src, mg.at[k, core, like], send.at[sent[name]], recv.at[here_at[name]], peer)

    def tiles_on(k):
        name = ("tiles on", k)
        view = mg.at[k, core]
        return on_plane(view, view, send.at[sent[name]], recv.at[here_at[name]], sibling)

    small_at = (core * lay.half + like) * lay.sml

    def small_copy(peer):
        return on_plane(
            sum_1.at[pl.ds(lay.mat, lay.sml)], small.at[pl.ds(small_at, lay.sml)],
            send.at[sent["small"]], recv.at[here_at["small"]], peer,
        )

    def small_on():
        view = small.at[pl.ds(core * lay.half * lay.sml, lay.half * lay.sml)]
        return on_plane(view, view, send.at[sent["small on"]], recv.at[here_at["small on"]], sibling)

    def fold_end(part):
        group, tiles = line_part(part)
        has_come(line_bytes(part), ("line sum", part))
        zrs[group][z, tiles] = zfs[group][tiles]
        whole = zrs[group][0, tiles]
        for block in range(1, n_blk):
            whole = whole + zrs[group][block, tiles]
        totals[group][tiles] = whole
        if part == 3:
            like_peers(lambda peer: small_copy(peer).start())
            small[pl.ds(small_at, lay.sml)] = whole
        else:
            like_peers(lambda peer: tile_copy(part, peer).start())
            mg[part, core, like] = whole

    def chain(group):
        def end():
            for part in (1, 3) if group == 1 else (group,):
                fold_end(part)

        def turn():
            has_come(mg.at[group, 0, pl.ds(0, lay.half - 1)], ("tiles", group))
            tiles_on(group).start()
            if group == 1:
                has_come(small.at[pl.ds(0, (lay.half - 1) * lay.sml)], "small")
                small_on().start()

        return [
            lambda: core_sum(group).start(),
            lambda: fold_core(group),
            lambda: fold_plane(group),
            end,
            turn,
        ]

    chains = [chain(group) for group in range(3)]
    per = DYN_TILE // lay.real
    dyn_tiles = lay.n_dev // per

    def take(slots, step):
        for at, events in slots.items():
            @pl.when(step == at)
            def _():
                for event in events:
                    event()

    @pl.loop(0, actor_tiles)
    def _(step):
        @pl.when(step == actor_tiles - 1)
        def _():
            has_come(bk.at[pl.ds(0, n_dp - 1)], "own")
            lanes = lax.broadcasted_iota(jnp.int32, (48, lay.width), 1) // CAP

            def gather(owner, total):
                turned = pltpu.roll(
                    bk[owner * n_blk], lax.rem((owner - me) * CAP + lay.width, lay.width), axis=1
                )
                return jnp.where(lanes == owner, turned, total)

            own = lax.fori_loop(0, n_dp, gather, jnp.zeros((48, lay.width), F32))
            xs[0:48, 0 : lay.real] = own[:, 0 : lay.real]

        where = place_of(step, ACTOR_TILE)
        now_f = framed(0, IN, where)
        now_in = now_f.astype(BF16)
        weight = xs[42:43, where]
        action, log_prob, bent, moved, (a1, da1, a2, da2) = policy(now_in, 0, where)
        judged_in = with_action(now_f, action)
        loss = alpha * log_prob - log_alpha * (log_prob + TARGET_ENTROPY)
        grad_action = jnp.zeros((8, ACTOR_TILE), F32)
        used = act_rows(ACTOR_TILE)
        for k in range(2):
            judged, (_, df1, _, df2) = critic(judged_in, 2 + k)
            loss -= 0.5 * judged
            g2 = outer_sloped(wide[5 + k], -0.5 * weight, df2)
            g1 = sloped(dot(w2h[k], g2), df1)
            grad_action += dot(w1n[k], g1)[0:8]
        grad_latent = 2.0 * alpha * weight * action + grad_action * (1.0 - action * action)
        grad_scale = grad_latent * moved - alpha * weight
        grad_bent = grad_scale * 3.5 * (1.0 - bent * bent)
        g3 = jnp.concatenate(
            [jnp.where(used, grad_latent, 0.0), jnp.where(used, grad_bent, 0.0)], 0
        ).astype(BF16)
        acc_a[...] += dot(g3, a2, NT)
        acc_m[:, 0:16] += dot(ones16(ACTOR_TILE), g3, NT)
        g2 = sloped(dot(head_t[...], g3), da2)
        add_hidden(2, a1, g2)
        g1 = sloped(dot(w2h[2], g2), da1)
        acc_w[2] += dot(now_in, g1, NT)
        acc_l[1:2, 0:ACTOR_TILE] += weight * loss
        acc_l[2:3, 0:ACTOR_TILE] += weight * (log_prob + TARGET_ENTROPY)

    put_matrix(2)
    chains[2][0]()

    @pl.loop(0, critic_tiles)
    def _(step):
        if critic_tiles > 1:
            take({1: [chains[2][1]]}, step)

        where = place_of(step, CRITIC_TILE)
        now_in = framed(0, IN, where).astype(BF16)
        next_f = framed(24, OBS, where)
        reward = xs[23:24, where]
        done = xs[41:42, where]
        next_action, next_prob, _, _, _ = policy(next_f.astype(BF16), 1, where)
        aim_in = with_action(next_f, next_action)
        aim = jnp.minimum(critic(aim_in, 0)[0], critic(aim_in, 1)[0])
        target = reward + DISCOUNT * (1.0 - done) * (aim - alpha * next_prob)
        ys[0:1, where] = target
        critic_pass(0, now_in, where, target)

    put_matrix(0)
    chains[0][0]()
    if critic_tiles == 1:
        chains[2][1]()

    has_come(bk.at[pl.ds(0, (n_dp - 1) * (n_blk - 1))], "plane")
    lane0 = lay.real // 128 * 128

    def add_block(at, carry):
        sides, fills = carry
        slot = slot_of(at)
        return sides + bk[slot, 0:32, lane0 : lane0 + 128], fills + bk[slot, 40:48, 0 : lay.real]

    sides, fills = lax.fori_loop(
        0, lay.n_dev, add_block, (jnp.zeros((32, 128), F32), jnp.zeros((8, lay.real), F32))
    )
    at = lay.real - lane0
    rows_all = float(lay.replay * lay.n_dev)
    centre = sides[0:24, at : at + 1] / rows_all
    scale = lax.rsqrt(sides[0:24, at + 1 : at + 2] / rows_all - centre * centre + 1e-6)
    total = sides[24:25, at : at + 1] + jnp.sum(fills[2:3, :], axis=1, keepdims=True)
    count[...] = jnp.broadcast_to(total, (8, 128))

    @pl.loop(0, critic_tiles)
    def _(step):
        take({critic_tiles - 1: [chains[0][1], chains[2][2]]}, step)
        where = place_of(step, CRITIC_TILE)
        critic_pass(1, framed(0, IN, where).astype(BF16), where, ys[0:1, where])

    put_matrix(1)
    for k in range(3):
        put(R_IN + 24 * k, acc_w[k, 0:24, :])
    put(R_HEAD, acc_a[...])
    rowbuf[0:1, :] = acc_c[0, 0:1, :]
    rowbuf[1:2, :] = acc_c[1, 0:1, :]
    for k in range(3):
        rowbuf[2 + k : 3 + k, :] = acc_h[k, HSAC : HSAC + 1, :]
    put(R_OUT, rowbuf[...])
    folded = jnp.sum(acc_l[...], axis=1, keepdims=True)
    rowbuf[...] = jnp.zeros_like(rowbuf)
    rowbuf[0:1, 0:48] = acc_m[0:1, :]
    rowbuf[0:1, 64:65] = folded[0:1] + folded[1:2]
    rowbuf[0:1, 65:66] = folded[2:3]
    put(R_MISC, rowbuf[...])
    put(R_MISC + 8, jnp.zeros((R_SMALL - R_MISC - 8, HSAC), F32))
    chains[1][0]()

    def dyn_bias(start, width):
        row = jnp.zeros((1, width), F32)
        for e in range(MEMBERS):
            row = jnp.where(me == e, bias[:, start + width * e : start + width * (e + 1)], row)
        return row

    @pl.when(is_dyn)
    def _():
        w1f[0] = jnp.zeros((32, HSAC), F32)
        w1f[0, 0:IN, 0:HDYN] = rounded(dyn_in[dyn_e])
        for at, piece in enumerate(pieces(dyn_bias(DB1, HDYN))):
            w1f[0, IN + at : IN + at + 1, 0:HDYN] = piece.astype(F32)
        w1t[0] = (0.5 * w1f[0].T).astype(BF16)
        rowbuf[...] = jnp.zeros_like(rowbuf)
        rowbuf[0:1, 0:HDYN] = dyn_bias(DB2, HDYN)
        head_row = dyn_bias(DB3, DOUT)
        rowbuf[1:2, 0:HALF] = head_row[:, 0:HALF]
        rowbuf[1:2, 24 : 24 + HALF] = head_row[:, HALF:DOUT]
        rowbuf[2:3, 0:HALF] = bias[:, MAXLV : MAXLV + HALF]
        rowbuf[3:4, 0:HALF] = bias[:, MINLV : MINLV + HALF]
        dcols[...] = rowbuf[...].T
        wide[0] = jnp.broadcast_to(0.5 * dcols[:, 0:1], (HSAC, 128))
        dpack[...] = jnp.zeros_like(dpack)
        dpack[0:HALF, 0:HDYN] = dyn_out[dyn_e, 0:HALF, :]
        dpack[24 : 24 + HALF, 0:HDYN] = dyn_out[dyn_e, HALF:DOUT, :]
        dhead[...] = dpack[0:48, :].astype(BF16)
        dhead_t[...] = (0.5 * rounded(dpack[0:48, :])).T.astype(BF16)
        dpack[...] = jnp.zeros_like(dpack)

        has_come(dhg.at[pl.ds(0, n_blk - 1)], "dyn h")
        has_come(dmg.at[pl.ds(0, n_blk - 1)], "dyn m")
        dhg[z] = dyn_h[dyn_e]
        dmg[z] = dyn_m[dyn_e]
        dmat[...] = jnp.zeros_like(dmat)
        for block in range(n_blk):
            dmat[block * lay.drows : (block + 1) * lay.drows, 0:HDYN] = 0.5 * rounded(dhg[block])
        w2h[0] = dmat[...].astype(BF16)
        w2t[0] = dmat[...].T.astype(BF16)
        for ref in (dacc_h, dacc_w, dacc_o, dacc_m, dacc_b, dacc_l):
            ref[...] = jnp.zeros_like(ref)

    in_dyn = {}
    for at, event in (
        (1, chains[0][2]), (1, chains[1][1]), (2, chains[2][3]), (dyn_tiles - 1, chains[1][2]),
    ):
        in_dyn.setdefault(min(at, dyn_tiles - 1), []).append(event)

    @pl.loop(0, dyn_tiles)
    def _(tile):
        take(in_dyn, tile)

        @pl.when(is_dyn)
        def _():
            for at in range(per):
                slot = slot_of(tile * per + at)
                xt[:, at * lay.real : (at + 1) * lay.real] = bk[slot, :, 0 : lay.real]
            now = xt[0:24, :]
            later = xt[24:48, :]
            row24 = rows_of((24, DYN_TILE))
            scaled = jnp.where(row24 < IN, (now - centre) * scale, 1.0)
            inputs = jnp.concatenate([scaled, (rows_of((8, DYN_TILE)) < 2).astype(F32)], 0).astype(BF16)
            first, slope1 = gated(dot(w1t[0], inputs))
            second, slope2 = gated(dot(w2t[0], first), wide[0])
            out = dot(dhead[...], second) + dcols[0:48, 1:2]
            used = row24 < HALF
            upper = dcols[0:24, 2:3]
            lower = dcols[0:24, 3:4]
            gap1 = upper - out[24:48]
            gap2 = upper - softplus(gap1) - lower
            log_var = lower + softplus(gap2)
            error = out[0:24] - jnp.where(row24 == OBS, now[23:24], later - now)
            inverse = jnp.exp(-log_var)
            weight = xt[42:43, :] * (xt[43:44, :] == me.astype(F32)).astype(F32)
            spread_term = error * error * inverse
            nll = jnp.sum(jnp.where(used, spread_term + log_var, 0.0), axis=0, keepdims=True)
            dacc_l[0:1, :] += weight * nll
            grad_mu = 2.0 * weight * error * inverse
            grad_lv = weight * (1.0 - spread_term)
            open1 = sigmoid(gap1)
            open2 = sigmoid(gap2)
            grad_lv1 = grad_lv * open2
            dacc_b[0] += jnp.where(used, grad_lv1 * (1.0 - open1), 0.0)
            dacc_b[1] += jnp.where(used, grad_lv * (1.0 - open2), 0.0)
            g3 = jnp.concatenate(
                [jnp.where(used, grad_mu, 0.0), jnp.where(used, grad_lv1 * open1, 0.0)], 0
            ).astype(BF16)
            dacc_o[...] += dot(g3, second, NT)
            dacc_m[...] += dot(ones16(DYN_TILE), g3, NT)
            g2 = sloped(dot(dhead_t[...], g3), slope2)
            dacc_h[...] += dot(jnp.concatenate([first, ones16(DYN_TILE)], 0), g2, NT)
            g1 = sloped(dot(w2h[0], g2), slope1)
            dacc_w[...] += dot(inputs, g1, NT)

    out_of = {"pack": dyn_s, "x": dyn_x}

    def member_copy(name, src, owner, kind, sem, peer):
        return on_plane(src, out_of[name].at[owner], send.at[sent[name, kind]], recv.at[sem], peer)

    def give(name, src):
        like_peers(
            lambda peer: member_copy(name, src, dyn_e, "own", here_at[name, "like"] + dyn_e, peer).start()
        )
        member_copy(name, src, dyn_e, "own", here_at[name, "sibling"], sibling).start()

    def hand_on(name):
        def body(peer):
            @pl.when(peer < MEMBERS)
            def _():
                owner = jnp.minimum(peer, MEMBERS - 1)
                view = out_of[name].at[owner]
                member_copy(name, view, owner, "on", here_at[name, "like"] + owner, sibling).wait_recv()
                member_copy(name, view, owner, "on", here_at[name, "sibling"], sibling).start()

        like_peers(body)

    even, odd = (MEMBERS + 1) // 2, MEMBERS // 2
    handed = even - core * (even - odd) - jnp.where(is_dyn, 1, 0)

    def from_sibling(name):
        for side, number in ((0, odd), (1, even)):
            @pl.when(core == side)
            def _():
                has_come(out_of[name].at[pl.ds(0, number)], (name, "sibling"))

    def gave(name):
        @pl.when(is_dyn)
        def _():
            for begin in range(0, n_dp // 2, MEMBERS):
                number = min(MEMBERS, n_dp // 2 - begin)
                has_sent(out_of[name].at[pl.ds(0, number)], (name, "own"))

        for number in (even, even - 1, even - 2):
            @pl.when(handed == number)
            def _():
                has_sent(out_of[name].at[pl.ds(0, number)], (name, "on"))

    def line_rows(ref):
        rows = ref[0 : lay.drows, 0:HDYN]
        for block in range(1, n_blk):
            rows = jnp.where(z == block, ref[block * lay.drows : (block + 1) * lay.drows, 0:HDYN], rows)
        return rows

    mine_rows = pl.ds(pl.multiple_of(z * lay.rows, lay.rows), lay.rows)

    def take_matrix(k):
        tiles_on(k).wait_recv()
        for chunk in range(n_dp):
            tile = chunk * lay.mat
            half, row = tile // 32, tile % 32
            at = slice(row * 8, (row + lay.mat) * 8)
            piece = mg[k, chunk % 2, chunk // 2].reshape(lay.mat * 8, 128)
            mat[k, at, half * 128 : (half + 1) * 128] = piece / total
        normalise(mat.at[k])

    chains[2][4]()
    chains[0][3]()

    @pl.when(is_dyn)
    def _():
        dpack[D_IN : D_IN + 24, :] = dacc_w[0:24, :]
        dpack[D_OUT : D_OUT + HALF, :] = dacc_o[0:HALF, :]
        dpack[D_OUT + HALF : D_OUT + DOUT, :] = dacc_o[24 : 24 + HALF, :]
        dpack[D_B2 : D_B2 + 1, :] = dacc_h[HSAC : HSAC + 1, :]
        dpack[D_B3 : D_B3 + 1, 0:48] = dacc_m[0:1, :]
        lanes = lax.broadcasted_iota(jnp.int32, (24, 128), 1)
        bound = jnp.where(
            lanes == 0,
            jnp.sum(dacc_b[0], axis=1, keepdims=True),
            jnp.where(lanes == 1, jnp.sum(dacc_b[1], axis=1, keepdims=True), 0.0),
        )
        dpack[D_UP : D_UP + 2, 0:24] = bound.T[0:2, :]
        dpack[D_LOSS : D_LOSS + 1, 0:128] = jnp.broadcast_to(
            jnp.sum(dacc_l[0:1, :], axis=1, keepdims=True), (1, 128)
        )
        dpack[D_HID : D_HID + lay.drows, 0:HDYN] = line_rows(dacc_h)
        dyn_s[dyn_e] = dpack[...]
        give("pack", dpack)
        dmat[...] = jnp.zeros_like(dmat)
        for block in range(n_blk):
            at = slice(block * lay.drows, (block + 1) * lay.drows)
            dmat[at, 0:HDYN] = MOMENTUM * dmg[block] + dacc_h[at, 0:HDYN] / total
        normalise(dmat)

    def sum_end(step):
        @pl.when(step == 3)
        def _():
            chains[0][4]()
            chains[1][3]()

    take_matrix(2)

    @pl.when(is_dyn)
    def _():
        schulz([dmat, mat.at[2]], NS_ITERS, sum_end)
        rows = line_rows(dmat)
        drow_x[...] = rows
        dyn_x[dyn_e] = rows
        give("x", drow_x)

    @pl.when(jnp.logical_not(is_dyn))
    def _():
        schulz([mat.at[2]], NS_ITERS, sum_end)

    def sent_early():
        has_sent(wg.at[pl.ds(0, n_blk - 1), :, half_rows], "hidden")
        has_sent(wg.at[pl.ds(0, n_blk - 1), :, half_rows], "hidden on")
        has_sent(asked.at[pl.ds(0, n_dp - 1)], "lists")
        has_sent(bk.at[pl.ds(0, n_dp - 1)], "own")
        has_sent(bk.at[pl.ds(0, n_blk - 1)], "line")
        has_sent(bk.at[pl.ds(0, (n_dp - 1) * (n_blk - 1))], "plane")

        @pl.when(is_dyn)
        def _():
            has_sent(dhg.at[pl.ds(0, n_blk - 1)], "dyn h")
            has_sent(dmg.at[pl.ds(0, n_blk - 1)], "dyn m")

        for group in range(3):
            core_sum(group).wait_send()
            has_sent(froms[group].at[pl.ds(0, lay.half - 1)], ("plane sum", group))
        for part in range(4):
            has_sent(line_bytes(part), ("line sum", part))

    def pass_on(step):
        pl.when(step == 2)(functools.partial(hand_on, "pack"))
        pl.when(step == NS_ITERS - 1)(functools.partial(hand_on, "x"))

    chains[1][4]()
    for k in range(2):
        take_matrix(k)
    schulz([mat.at[0], mat.at[1]], NS_ITERS, pass_on)
    for k in range(3):
        sac_x[k] = mat[k, mine_rows, :]
        for half in range(2):
            for piece in range(lay.rows // 8 // lay.mat):
                chunk = (half * 32 + z * (lay.rows // 8)) // lay.mat + piece
                kept = mg[k, lax.rem(chunk, 2), chunk // 2]
                sac_g[half, k, piece * lay.mat : (piece + 1) * lay.mat] = kept

    sent_early()
    small_on().wait_recv()
    from_sibling("pack")
    from_sibling("x")

    has_sent(small.at[pl.ds(0, (lay.half - 1) * lay.sml)], "small")
    small_on().wait_send()
    gave("pack")
    gave("x")

    for k in range(3):
        has_sent(mg.at[k, 0, pl.ds(0, lay.half - 1)], ("tiles", k))
        tiles_on(k).wait_send()


def ordered(lay, n_in, n_out, *refs):
    inputs, outputs, scratch = refs[:n_in], refs[n_in : n_in + n_out], refs[n_in + n_out :]
    main_kernel(lay, *inputs, *scratch[: n_in + 1], *outputs, *scratch[n_in + 1 :])


def adamw(weights, first, second, gradient):
    first = BETA_FIRST * first + (1.0 - BETA_FIRST) * gradient
    second = BETA_SECOND * second + (1.0 - BETA_SECOND) * gradient * gradient
    first_hat = first / (1.0 - BETA_FIRST**STEP)
    second_hat = second / (1.0 - BETA_SECOND**STEP)
    step = first_hat / (jnp.sqrt(second_hat) + 1e-8) + ADAM_DECAY * weights
    return weights - ADAM_RATE * step, first, second


def update_kernel(lay, *refs):
    (
        sac_g, sac_x, dyn_x, dyn_s, small, count, crit_rows, sac_h, dyn_h, dyn_m,
        ci, ci_m, ci_v, ai, ai_m, ai_v, di, di_m, di_v, ao, ao_m, ao_v,
        do, do_m, do_v, bi, bi_m, bi_v,
        sac_new, sac_mom, dyn_new, dyn_mom, ci_n, ci_mn, ci_vn, ai_n, ai_mn, ai_vn, di_n, di_mn,
        di_vn, co_n, co_mn, co_vn, ao_n, ao_mn, ao_vn, do_n, do_mn, do_vn, bi_n, bi_mn, bi_vn,
        loss, counted, bg,
    ) = refs
    total = count[0:1, 0:1]
    for k in range(3):
        for side in range(2):
            tiles = sac_g[side, k].reshape(sac_mom.shape[1], 128)
            sac_mom[k, :, side * 128 : (side + 1) * 128] = tiles / total
    sac_new[...] = sac_h[...] * (1.0 - MUON_RATE * MUON_DECAY) - MUON_RATE * sac_x[...]
    dyn_rows = dyn_s[:, D_HID : D_HID + dyn_m.shape[1], 0:HDYN]
    dyn_mom[...] = MOMENTUM * dyn_m[...] + dyn_rows / total.reshape(1, 1, 1)
    dyn_new[...] = dyn_h[...] * (1.0 - MUON_RATE * MUON_DECAY) - MUON_RATE * dyn_x[...]

    def rows(row, number):
        def tile(at):
            chunk = at // lay.sml
            return small[(chunk % 2 * lay.half + chunk // 2) * lay.sml + at % lay.sml]

        sides = []
        for side in range(2):
            at = side * (R_SMALL // 8) + row // 8
            sides.append(jnp.concatenate([tile(at + more) for more in range(-(-number // 8))], 0))
        return jnp.concatenate(sides, 1)

    def store(outs, at, values):
        for out, value in zip(outs, values):
            out[at] = value

    outs = (ci_n, ci_mn, ci_vn)
    for k in range(2):
        at = (slice(None), k, slice(None))
        grad = rows(R_IN + 24 * k, 24)
        bg[:, CB1 + HSAC * k : CB1 + HSAC * (k + 1)] = grad[IN : IN + 1]
        store(outs, at, adamw(ci[at], ci_m[at], ci_v[at], grad[0:IN] / total))
    grad = rows(R_IN + 48, 24)
    bg[:, AB1 : AB1 + HSAC] = grad[IN : IN + 1]
    store((ai_n, ai_mn, ai_vn), ..., adamw(ai[...], ai_m[...], ai_v[...], grad[0:OBS] / total))
    grad = rows(R_HEAD, 16)
    for at, row in ((slice(0, ACT), slice(1, 1 + ACT)), (slice(ACT, 2 * ACT), slice(9, 9 + ACT))):
        store((ao_n, ao_mn, ao_vn), at, adamw(ao[at], ao_m[at], ao_v[at], grad[row] / total))
    grad = rows(R_OUT, 8)
    held = [crit_rows[2 * at : 2 * at + 2, :] for at in range(3)]
    store((co_n, co_mn, co_vn), ..., adamw(*held, grad[0:2] / total))
    bg[:, CB2 : CB2 + HSAC] = grad[2:3]
    bg[:, CB2 + HSAC : CB2 + 2 * HSAC] = grad[3:4]
    bg[:, AB2 : AB2 + HSAC] = grad[4:5]
    grad = rows(R_MISC, 8)
    bg[:, CB3 : CB3 + 1] = grad[0:1, 16:17]
    bg[:, CB3 + 1 : CB3 + 2] = grad[0:1, 32:33]
    bg[:, AB3 : AB3 + ACT] = grad[0:1, 1 : 1 + ACT]
    bg[:, AB3 + ACT : AB3 + 2 * ACT] = grad[0:1, 9 : 9 + ACT]
    bg[:, LOGA : LOGA + 1] = -grad[0:1, 65:66]
    total_loss = grad[0:1, 64:65]
    up = jnp.zeros((1, HALF), F32)
    low = jnp.zeros((1, HALF), F32)
    for e in range(MEMBERS):
        pack = dyn_s[e]
        total_loss = total_loss + pack[D_LOSS : D_LOSS + 1, 0:1]
        up = up + pack[D_UP : D_UP + 1, 0:HALF]
        low = low + pack[D_LOW : D_LOW + 1, 0:HALF]
        bg[:, DB1 + HDYN * e : DB1 + HDYN * (e + 1)] = pack[IN : IN + 1, 0:HDYN]
        bg[:, DB2 + HDYN * e : DB2 + HDYN * (e + 1)] = pack[D_B2 : D_B2 + 1, 0:HDYN]
        bg[:, DB3 + DOUT * e : DB3 + DOUT * e + HALF] = pack[D_B3 : D_B3 + 1, 0:HALF]
        bg[:, DB3 + DOUT * e + HALF : DB3 + DOUT * (e + 1)] = pack[D_B3 : D_B3 + 1, 24 : 24 + HALF]
        grad = pack[0:IN, 0:HDYN] / total
        store((di_n, di_mn, di_vn), e, adamw(di[e], di_m[e], di_v[e], grad))
        grad = pack[D_OUT : D_OUT + DOUT, 0:HDYN] / total
        store((do_n, do_mn, do_vn), e, adamw(do[e], do_m[e], do_v[e], grad))
    bg[:, MAXLV : MAXLV + HALF] = up
    bg[:, MINLV : MINLV + HALF] = low
    lane = lax.broadcasted_iota(jnp.int32, (1, NB), 1)
    bounds = jnp.where(
        jnp.logical_and(lane >= MAXLV, lane < MINLV),
        BOUND_WEIGHT,
        jnp.where(jnp.logical_and(lane >= MINLV, lane < LOGA), -BOUND_WEIGHT, 0.0),
    )
    grad = bg[...] / total + bounds
    flat = [ref[...].reshape(1, NB) for ref in (bi, bi_m, bi_v)]
    store((bi_n, bi_mn, bi_vn), ..., [value.reshape(NB) for value in adamw(*flat, grad)])
    loss[...] = total_loss
    counted[...] = total


def shards(
    lay, replay, model_rows, requests, member_of, model_live, noise, sac_hidden, sac_hidden_mom,
    dyn_hidden, dyn_hidden_mom, crit_in, crit_in_m, crit_in_v, act_in, act_in_m, act_in_v, dyn_in,
    dyn_in_m, dyn_in_v, crit_out, crit_out_m, crit_out_v, act_out, act_out_m, act_out_v, dyn_out,
    dyn_out_m, dyn_out_v, biases, biases_m, biases_v, targ_in, targ_hidden, targ_out, targ_bias,
):
    n_dp, n_blk = lay.n_dp, lay.n_blk
    spec = pl.BlockSpec(memory_space=pltpu.VMEM)

    def flip(value):
        return jnp.transpose(value, (1, 0, 2))

    def swap(value):
        return jnp.swapaxes(value, -1, -2)

    def kept(value):
        return pltpu.with_memory_space_constraint(value, pltpu.VMEM)

    inputs = (
        sac_hidden, requests, member_of, replay, model_live, model_rows, jnp.transpose(noise, (2, 0, 1)),
        biases, flip(targ_in), flip(crit_in), act_in, targ_bias, targ_hidden, crit_out, targ_out,
        swap(act_out), dyn_hidden, dyn_hidden_mom, crit_out_m, crit_out_v, sac_hidden_mom, dyn_in,
        swap(dyn_out),
    )
    shape = jax.ShapeDtypeStruct
    rows, drows = lay.rows, lay.drows
    out_shape = (
        pltpu.VMEM((2, 3, rows // 8, 8, 128), F32),
        pltpu.VMEM((3, rows, HSAC), F32),
        pltpu.VMEM((MEMBERS, drows, HDYN), F32),
        pltpu.VMEM((MEMBERS, D_ROWS, HSAC), F32),
        pltpu.VMEM((32, 8, 128), F32),
        pltpu.VMEM((8, 128), F32),
        pltpu.VMEM((8, HSAC), F32),
    )

    def vm(*dims, kind=F32):
        return pltpu.VMEM(dims, kind)

    scratch = [
        vm(n_blk, 3, rows, HSAC, kind=BF16),
        vm(2, n_dp, CAP, kind=jnp.int32),
        vm(n_dp, 2, n_dp, CAP, kind=jnp.int32),
        vm(n_blk, drows, HDYN),
        vm(n_blk, drows, HDYN),
        vm(lay.n_dev, 48, lay.width),
        vm(56, lay.batch),
        vm(2, 8, lay.batch),
        vm(8, lay.batch),
        vm(5, 32, HSAC),
        vm(5, HSAC, 32, kind=BF16),
        vm(2, 16, HSAC, kind=BF16),
        vm(5, HSAC, HSAC, kind=BF16),
        vm(3, HSAC, HSAC, kind=BF16),
        vm(5, 16, HSAC, kind=BF16),
        vm(HSAC, 16, kind=BF16),
        vm(16, HSAC),
        vm(8, HSAC),
        vm(7, HSAC, 128),
        vm(128, 8),
        vm(3, HSAC + 16, HSAC),
        vm(3, 32, HSAC),
        vm(2, 16, HSAC),
        vm(16, HSAC),
        vm(16, 48),
        vm(8, max(CRITIC_TILE, ACTOR_TILE)),
        *[vm(2, lay.half, chunk, 8, 128) for chunk in lay.chunks],
        *[vm(lay.half, chunk, 8, 128) for chunk in lay.chunks],
        *[vm(lay.half, chunk, 8, 128) for chunk in lay.chunks],
        *[vm(n_blk, chunk, 8, 128) for chunk in lay.chunks],
        *[vm(chunk, 8, 128) for chunk in lay.chunks],
        *[vm(chunk, 8, 128) for chunk in lay.chunks],
        vm(3, 2, lay.half, lay.mat, 8, 128),
        vm(3, HSAC, HSAC),
        vm(HSAC, 8),
        vm(HSAC + 16, HSAC),
        vm(32, HSAC),
        vm(48, HSAC),
        vm(16, 48),
        vm(2, 24, DYN_TILE),
        vm(8, DYN_TILE),
        vm(48, DYN_TILE),
        vm(HSAC, HSAC),
        vm(D_ROWS, HSAC),
        vm(drows, HDYN),
        vm(1, NB),
        vm(48, HSAC, kind=BF16),
        vm(HSAC, 48, kind=BF16),
    ]
    scratch += [pltpu.SemaphoreType.DMA((lay.departures,)), pltpu.SemaphoreType.DMA((lay.arrivals,))]
    held = [pltpu.VMEM(value.shape, value.dtype) for value in inputs]
    held.append(pltpu.SemaphoreType.DMA((len(inputs),)))
    varying = 4 * (lay.n_dev * 48 * lay.width + 72 * lay.batch + 48 * lay.replay)
    gathered = pl.pallas_call(
        functools.partial(ordered, lay, len(inputs), len(out_shape)),
        out_shape=out_shape,
        in_specs=[pl.BlockSpec(memory_space=pl.ANY)] * len(inputs),
        out_specs=[spec] * len(out_shape),
        scratch_shapes=held + scratch,
        compiler_params=pltpu.CompilerParams(
            collective_id=0, has_side_effects=True, vmem_limit_bytes=26 * 2**20 + varying
        ),
        name="step",
    )(*[pltpu.with_memory_space_constraint(value, pltpu.HBM) for value in inputs])
    params = (
        sac_hidden, dyn_hidden, dyn_hidden_mom,
        flip(crit_in), flip(crit_in_m), flip(crit_in_v), act_in, act_in_m, act_in_v,
        dyn_in, dyn_in_m, dyn_in_v,
        swap(act_out), swap(act_out_m), swap(act_out_v),
        swap(dyn_out), swap(dyn_out_m), swap(dyn_out_v), biases, biases_m, biases_v,
    )
    new_shape = [shape(sac_hidden.shape, F32)] + [shape(value.shape, F32) for value in params[:12]]
    new_shape += [shape(crit_out.shape, F32)] * 3 + [shape(value.shape, F32) for value in params[12:]]
    new_shape += [shape((1, 1), F32)] * 2
    out = pl.pallas_call(
        functools.partial(update_kernel, lay),
        out_shape=tuple(new_shape),
        in_specs=[spec] * (len(gathered) + len(params)),
        out_specs=[spec] * len(new_shape),
        scratch_shapes=[vm(1, NB)],
        compiler_params=pltpu.CompilerParams(vmem_limit_bytes=16 * 2**20),
        name="update",
    )(*[kept(value) for value in gathered], *params)
    out = list(out)
    for at in (4, 5, 6):
        out[at] = flip(out[at])
    for at in (16, 17, 18, 19, 20, 21):
        out[at] = swap(out[at])
    for at in (25, 26):
        out[at] = out[at].reshape(())
    return tuple(out)


def solution(mesh):
    both = ("dp", "blk")
    sharded = (
        P(None, both), P(None, both), P(both, None), P(both, None), P(both), P(None, both, None),
    )
    hidden = (P(None, "blk", None),) * 4

    def step(replay, model_rows, *others):
        lay = Layout(mesh, replay.shape[1], model_rows.shape[1])
        return shards(lay, replay, model_rows, *others)

    return jax.shard_map(
        step,
        mesh=mesh,
        in_specs=sharded + hidden + (P(),) * 25,
        out_specs=hidden + (P(),) * 23,
        check_vma=False,
    )
```

```python
import functools

import jax
import jax.numpy as jnp
from jax import lax
from jax.experimental import pallas as pl
from jax.experimental.pallas import tpu as pltpu
from jax.sharding import PartitionSpec as P

OBS = 17
ACT = 6
IN = OBS + ACT
FEAT = 42
HDYN = 200
HSAC = 256
MEMBERS = 7
DOUT = 36
HALF = DOUT // 2
NB = 4639
NS_ITERS = 5
STEP = 10
CAP = 8
CRITIC_TILE = 640
ACTOR_TILE = 640
DYN_TILE = 1024
ROWS = 32

DISCOUNT = 0.99
TARGET_ENTROPY = -6.0
BOUND_WEIGHT = 0.01
MOMENTUM = 0.95
MUON_RATE = 0.4
MUON_DECAY = 0.01
ADAM_RATE = 0.1
ADAM_DECAY = 0.01
BETA_FIRST = 0.9
BETA_SECOND = 0.999
COEF_LINEAR = 3.4445
COEF_CUBIC = -4.775
COEF_QUINTIC = 2.0315

CB1, CB2, CB3, AB1, AB2, AB3 = 0, 512, 1024, 1026, 1282, 1538
DB1, DB2, DB3, MAXLV, MINLV, LOGA = 1550, 2950, 4350, 4602, 4620, 4638

R_IN, R_HEAD, R_OUT, R_MISC, R_SMALL = 0, 72, 88, 96, 128
D_IN, D_OUT, D_B2, D_B3, D_UP, D_LOW, D_LOSS, D_HID, D_ROWS = 0, 24, 60, 61, 62, 63, 64, 72, 128

F32, BF16 = jnp.float32, jnp.bfloat16
MESH = pl.DeviceIdType.MESH
NN = (((1,), (0,)), ((), ()))
NT = (((1,), (1,)), ((), ()))


def dot(a, b, dims=NN):
    return lax.dot_general(a, b, dims, preferred_element_type=F32)


def rounded(v):
    return v.astype(BF16).astype(F32)


def pieces(v):
    high = v.astype(BF16)
    rest = v - high.astype(F32)
    middle = rest.astype(BF16)
    return high, middle, (rest - middle.astype(F32)).astype(BF16)


def split(v):
    high = v.astype(BF16)
    return high, (v - high.astype(F32)).astype(BF16)


def product(a, b, dims=NN):
    left = jnp.concatenate([a[0], a[0], a[1]], 1)
    right = jnp.concatenate([b[0], b[1], b[0]], dims[0][1][0])
    half = left.shape[0] // 2
    return jnp.concatenate([dot(left[:half], right, dims), dot(left[half:], right, dims)], 0)


def softplus(v):
    return jnp.maximum(v, 0.0) + jnp.log1p(jnp.exp(-jnp.abs(v)))


def sigmoid(v):
    return 0.5 + 0.5 * jnp.tanh(0.5 * v)


def gate(half):
    up = 1.0 + jnp.tanh(half)
    value = half * up
    return value, up + value * (2.0 - up)


def by_rows(body, *arrays):
    done = [
        body(*[array[at : at + ROWS] for array in arrays]) for at in range(0, arrays[0].shape[0], ROWS)
    ]
    return [jnp.concatenate(parts, 0) for parts in zip(*done)]


def spread_to(column, width):
    return jnp.concatenate([column] * (width // 128), 1)


def gated(half, column=None):
    def body(part, *offset):
        value, slope = gate(part + spread_to(offset[0], part.shape[1]) if offset else part)
        return value.astype(BF16), slope

    return by_rows(body, half, *([] if column is None else [column]))


def sloped(grad, slope):
    return by_rows(lambda part, by: ((part * by).astype(BF16),), grad, slope)[0]


def outer_sloped(column, row, slope):
    return by_rows(lambda part, by: (((spread_to(part, by.shape[1]) * row) * by).astype(BF16),), column, slope)[0]


def rows_of(shape):
    return lax.broadcasted_iota(jnp.int32, shape, 0)


def schulz(refs, steps, before=None):
    @pl.loop(0, steps)
    def _(step):
        if before is not None:
            before(step)
        matrices = [ref[...] for ref in refs]
        parts = [split(matrix) for matrix in matrices]
        grams = [product(part, part, NT) for part in parts]
        halves = [split(gram) for gram in grams]
        squares = [product(half, half) for half in halves]
        blends = [
            split(COEF_CUBIC * gram + COEF_QUINTIC * square) for gram, square in zip(grams, squares)
        ]
        moved = [product(blend, part) for blend, part in zip(blends, parts)]
        for ref, matrix, move in zip(refs, matrices, moved):
            ref[...] = COEF_LINEAR * matrix + move


def normalise(ref):
    moment = ref[...]
    norm = jnp.sqrt(jnp.sum(jnp.sum(moment * moment, axis=1, keepdims=True), axis=0, keepdims=True))
    ref[...] = moment / (norm + 1e-7)


class Layout:
    def __init__(self, mesh, replay, model):
        self.n_dp = mesh.shape["dp"]
        self.half = self.n_dp // 2
        self.n_blk = mesh.shape["blk"]
        self.n_dev = self.n_dp * self.n_blk
        self.replay = replay
        self.model = model
        self.real = self.n_dp * CAP
        self.batch = self.real + model
        self.width = -(-(self.real + 2) // 128) * 128
        self.rows = HSAC // self.n_blk
        self.drows = HDYN // self.n_blk
        self.mat = 64 // self.n_dp
        self.sml = 32 // self.n_dp
        self.chunks = (self.mat, self.mat + self.sml, self.mat)
        groups = [(name, g) for name in ("core sum", "plane sum") for g in range(3)]
        groups += [("line sum", g) for g in range(4)]
        common = ["hidden", "hidden on", "lists", "own", "line", "plane", "dyn h", "dyn m", "small", "small on"]
        common += groups
        kinds = [(name, kind) for name in ("pack", "x") for kind in ("own", "on")]
        tiles = [(name, k) for name in ("tiles", "tiles on") for k in range(3)]
        sent = common + tiles + kinds
        self.sent = {name: at for at, name in enumerate(sent)}
        self.departures = len(sent)
        self.here, self.arrivals = {}, 0
        tiles += [("pack", "sibling"), ("x", "sibling")]
        for name in common + tiles:
            self.here[name] = self.arrivals
            self.arrivals += 1
        for name in ("pack", "x"):
            self.here[name, "like"] = self.arrivals
            self.arrivals += MEMBERS


OPERANDS = 23
FIRST, SECOND = 3, 16


def main_kernel(lay, *refs):
    n_in = OPERANDS
    sources, held = refs[:n_in], refs[n_in : 2 * n_in]
    (
        sac_h, requests, member, replay, live, model, noise, biases, targ_in, crit_in, act_in, targ_bias,
        targ_hidden, crit_out, targ_out, act_out, dyn_h, dyn_m, crit_out_m, crit_out_v, sac_m, dyn_in, dyn_out,
    ) = held
    loads = refs[2 * n_in]
    refs = refs[2 * n_in + 1 :]
    (
        sac_g, sac_x, dyn_x, dyn_s, small, count, crit_rows,
        wg, lists, asked, dhg, dmg, bk, xs, nz, ys, w1f, w1t, w1n, w2t, w2h, heads, head_t, head_f,
        rowbuf, wide, headcol, acc_h, acc_w, acc_c, acc_a, acc_m, acc_l, grid_0, grid_1, grid_2, core_0, core_1,
        core_2, from_0, from_1, from_2, zr_0, zr_1, zr_2, zf_0, zf_1, zf_2, sum_0, sum_1, sum_2, mg, mat, dcols, dacc_h, dacc_w, dacc_o, dacc_m, dacc_b, dacc_l, xt, dmat,
        dpack, drow_x, bias, dhead, dhead_t, *rest,
    ) = refs
    send, recv = rest
    sent, here_at = lay.sent, lay.here
    grids, cores, froms = (grid_0, grid_1, grid_2), (core_0, core_1, core_2), (from_0, from_1, from_2)
    zrs, zfs, totals = (zr_0, zr_1, zr_2), (zf_0, zf_1, zf_2), (sum_0, sum_1, sum_2)
    n_dp, n_blk = lay.n_dp, lay.n_blk
    me = lax.axis_index("dp")
    z = lax.axis_index("blk")
    core, like = lax.rem(me, 2), me // 2
    sibling = me + 1 - 2 * core
    is_dyn = me < MEMBERS
    dyn_e = jnp.minimum(me, MEMBERS - 1)

    def on_plane(src, dst, ssem, rsem, peer):
        return pltpu.make_async_remote_copy(
            src_ref=src, dst_ref=dst, send_sem=ssem, recv_sem=rsem,
            device_id={"dp": peer}, device_id_type=MESH,
        )

    def on_line(src, dst, ssem, rsem, peer):
        return pltpu.make_async_remote_copy(
            src_ref=src, dst_ref=dst, send_sem=ssem, recv_sem=rsem,
            device_id={"blk": peer}, device_id_type=MESH,
        )

    def over(number, body):
        if number <= 8:
            for off in range(1, number):
                body(off)
        else:
            pl.loop(1, number)(body)

    def plane_peers(body):
        over(n_dp, lambda off: body(lax.rem(me + off, n_dp)))

    def like_peers(body):
        over(n_dp // 2, lambda off: body(lax.rem(me + 2 * off, n_dp)))

    def line_peers(body):
        over(n_blk, lambda off: body(lax.rem(z + off, n_blk)))

    def has_sent(view, name):
        at = send.at[sent[name]]
        on_plane(view, view, at, at, sibling).wait_send()

    def has_come(view, name):
        at = recv.at[here_at[name]]
        on_plane(view, view, at, at, sibling).wait_recv()

    copies = [
        pltpu.make_async_copy(src, dst, loads.at[at]) for at, (src, dst) in enumerate(zip(sources, held))
    ]

    def arrived(begin, end):
        for copy in copies[begin:end]:
            copy.wait()

    barrier = pltpu.get_barrier_semaphore()
    plane_peers(lambda peer: pl.semaphore_signal(barrier, inc=1, device_id={"dp": peer}, device_id_type=MESH))
    line_peers(lambda peer: pl.semaphore_signal(barrier, inc=1, device_id={"blk": peer}, device_id_type=MESH))
    for copy in copies:
        copy.start()
    arrived(0, FIRST)
    wg[0] = sac_h[...].astype(BF16)
    lists[0] = requests[...]
    lists[1] = member[...]
    pl.semaphore_wait(barrier, n_dp - 1 + n_blk - 1)

    half_rows = pl.ds(pl.multiple_of(core * (lay.rows // 2), lay.rows // 2), lay.rows // 2)

    def slot_from(owner, at):
        return lax.rem(owner - at + n_blk, n_blk)

    def hidden_copy(peer):
        src = wg.at[0, :, half_rows]
        dst = wg.at[slot_from(z, peer), :, half_rows]
        return on_line(src, dst, send.at[sent["hidden"]], recv.at[here_at["hidden"]], peer)

    def hidden_on():
        view = wg.at[pl.ds(1, n_blk - 1), :, half_rows]
        return on_plane(view, view, send.at[sent["hidden on"]], recv.at[here_at["hidden on"]], sibling)

    def list_copy(peer):
        return on_plane(lists, asked.at[me], send.at[sent["lists"]], recv.at[here_at["lists"]], peer)

    line_peers(lambda peer: hidden_copy(peer).start())
    plane_peers(lambda peer: list_copy(peer).start())
    asked[me] = lists[...]

    def dyn_h_copy(peer):
        return on_line(dyn_h.at[dyn_e], dhg.at[z], send.at[sent["dyn h"]], recv.at[here_at["dyn h"]], peer)

    def dyn_m_copy(peer):
        return on_line(dyn_m.at[dyn_e], dmg.at[z], send.at[sent["dyn m"]], recv.at[here_at["dyn m"]], peer)

    arrived(FIRST, SECOND)
    alive = live[...].astype(F32).reshape(1, lay.model)
    data = replay[...]
    sums = jnp.sum(data[0:24], axis=1, keepdims=True)
    squares = jnp.sum(data[0:24] * data[0:24], axis=1, keepdims=True)
    living = jnp.sum(alive, axis=1, keepdims=True)

    has_come(asked.at[pl.ds(0, n_dp - 1)], "lists")
    spread = (
        lax.rem(lax.broadcasted_iota(jnp.int32, (CAP, lay.real), 1), CAP)
        == lax.broadcasted_iota(jnp.int32, (CAP, lay.real), 0)
    ).astype(F32)
    here = (
        lax.broadcasted_iota(jnp.int32, (n_dp, lay.real), 1) // CAP
        == lax.broadcasted_iota(jnp.int32, (n_dp, lay.real), 0)
    )

    def in_lanes(which):
        values = asked[:, which, me, :].astype(F32)
        wide = lax.dot_general(
            values, spread, NN, precision=lax.Precision.HIGHEST, preferred_element_type=F32
        )
        return jnp.sum(jnp.where(here, wide, 0.0), axis=0, keepdims=True)

    slots = in_lanes(0)
    wanted = jnp.maximum(slots, 0.0).astype(jnp.int32)
    hot = (rows_of((lay.replay, lay.real)) == wanted).astype(BF16)
    padded = jnp.concatenate([data, jnp.zeros((48 - FEAT, lay.replay), F32)], 0)
    chosen = dot(jnp.concatenate(pieces(padded), 0), hot)
    chosen = chosen[0:48] + chosen[48:96] + chosen[96:144]
    mine = me * n_blk
    bk[mine, 0:FEAT, 0 : lay.real] = chosen[0:FEAT]
    bk[mine, 42:43, 0 : lay.real] = (slots >= 0.0).astype(F32)
    bk[mine, 43:44, 0 : lay.real] = in_lanes(1)
    bk[mine, 44:48, 0 : lay.real] = jnp.zeros((4, lay.real), F32)
    bk[mine, :, lay.real : lay.width] = jnp.zeros((48, lay.width - lay.real), F32)
    bk[mine, 0:24, lay.real : lay.real + 1] = sums
    bk[mine, 0:24, lay.real + 1 : lay.real + 2] = squares
    bk[mine, 24:25, lay.real : lay.real + 1] = living

    def slot_of(block):
        line = lax.rem(block, n_blk)
        return block - line + slot_from(line, z)

    def block_line(peer):
        dst = bk.at[me * n_blk + slot_from(z, peer)]
        return on_line(bk.at[mine], dst, send.at[sent["line"]], recv.at[here_at["line"]], peer)

    def block_own(peer):
        view = bk.at[mine]
        return on_plane(view, view, send.at[sent["own"]], recv.at[here_at["own"]], peer)

    def block_plane(peer):
        view = bk.at[pl.ds(mine + 1, n_blk - 1)]
        return on_plane(view, view, send.at[sent["plane"]], recv.at[here_at["plane"]], peer)

    plane_peers(lambda peer: block_own(peer).start())
    line_peers(lambda peer: block_line(peer).start())

    arrived(SECOND, n_in)
    crit_rows[0:2, :] = crit_out[...]
    crit_rows[2:4, :] = crit_out_m[...]
    crit_rows[4:6, :] = crit_out_v[...]
    crit_rows[6:8, :] = jnp.zeros((2, HSAC), F32)

    @pl.when(is_dyn)
    def _():
        line_peers(lambda peer: dyn_h_copy(peer).start())
        line_peers(lambda peer: dyn_m_copy(peer).start())

    bias[...] = biases[...].reshape(1, NB)
    xs[42:56, :] = jnp.zeros((14, lay.batch), F32)
    xs[0:FEAT, lay.real : lay.batch] = model[...]
    xs[42:43, lay.real : lay.batch] = alive
    nz[...] = jnp.zeros_like(nz)
    for which in range(2):
        nz[which, 1:7, :] = noise[:, which, :]
    firsts = [
        (targ_in[:, 0, :], targ_bias[0:1, 0:HSAC]),
        (targ_in[:, 1, :], targ_bias[1:2, 0:HSAC]),
        (crit_in[:, 0, :], bias[:, CB1 : CB1 + HSAC]),
        (crit_in[:, 1, :], bias[:, CB1 + HSAC : CB1 + 2 * HSAC]),
        (act_in[...], bias[:, AB1 : AB1 + HSAC]),
    ]
    w1f[...] = jnp.zeros_like(w1f)
    for net, (weights, offset) in enumerate(firsts):
        w1f[net, 0 : weights.shape[0], :] = rounded(weights)
        for at, piece in enumerate(pieces(offset)):
            w1f[net, IN + at : IN + at + 1, :] = piece.astype(F32)
        w1t[net] = (0.5 * w1f[net].T).astype(BF16)
    for k in range(2):
        w1n[k] = w1f[2 + k, 16:32, :].astype(BF16)
    for net in range(2):
        w2t[net] = (0.5 * rounded(targ_hidden[net])).T.astype(BF16)
    has_come(wg.at[pl.ds(0, n_blk - 1), :, half_rows], "hidden")
    hidden_on().start()

    rowbuf[...] = jnp.zeros_like(rowbuf)
    rowbuf[0:1, :] = targ_bias[0:1, HSAC : 2 * HSAC]
    rowbuf[1:2, :] = targ_bias[1:2, HSAC : 2 * HSAC]
    rowbuf[2:3, :] = bias[:, CB2 : CB2 + HSAC]
    rowbuf[3:4, :] = bias[:, CB2 + HSAC : CB2 + 2 * HSAC]
    rowbuf[4:5, :] = bias[:, AB2 : AB2 + HSAC]
    rowbuf[5:7, :] = rounded(crit_out[...])
    columns = 0.5 * rowbuf[...].T
    for at in range(7):
        wide[at] = jnp.broadcast_to(columns[:, at : at + 1], (HSAC, 128))
    rowbuf[...] = jnp.zeros_like(rowbuf)
    rowbuf[0:1, 1:7] = bias[:, AB3 : AB3 + ACT]
    rowbuf[0:1, 9:15] = bias[:, AB3 + ACT : AB3 + 2 * ACT]
    headcol[...] = rowbuf[:, 0:128].T
    head_f[...] = jnp.zeros_like(head_f)
    for k in range(2):
        head_f[0:1, :] = targ_out[k : k + 1, :]
        heads[k] = head_f[...].astype(BF16)
        head_f[0:1, :] = crit_out[k : k + 1, :]
        heads[2 + k] = head_f[...].astype(BF16)
    head_f[0:1, :] = jnp.zeros((1, HSAC), F32)
    head_f[1:7, :] = act_out[0:ACT, :]
    head_f[9:15, :] = act_out[ACT : 2 * ACT, :]
    heads[4] = head_f[...].astype(BF16)
    head_t[...] = (0.5 * rounded(head_f[...])).T.astype(BF16)
    for ref in (acc_h, acc_w, acc_c, acc_a, acc_m, acc_l):
        ref[...] = jnp.zeros_like(ref)

    has_come(wg.at[pl.ds(0, n_blk - 1), :, half_rows], "hidden on")
    for k in range(3):
        for block in range(n_blk):
            w2h[k, block * lay.rows : (block + 1) * lay.rows, :] = (
                0.5 * wg[slot_from(block, z), k].astype(F32)
            ).astype(BF16)
        w2t[2 + k] = w2h[k].astype(F32).T.astype(BF16)

    log_alpha = bias[:, LOGA : LOGA + 1]
    alpha = jnp.exp(log_alpha)
    last = [
        targ_bias[0:1, 2 * HSAC : 2 * HSAC + 1],
        targ_bias[1:2, 2 * HSAC : 2 * HSAC + 1],
        bias[:, CB3 : CB3 + 1],
        bias[:, CB3 + 1 : CB3 + 2],
    ]
    critic_tiles = lay.batch // CRITIC_TILE
    actor_tiles = lay.batch // ACTOR_TILE

    def act_rows(width):
        row8 = rows_of((8, width))
        return jnp.logical_and(row8 >= 1, row8 < 1 + ACT)

    def place_of(step, width):
        return pl.ds(pl.multiple_of(lax.rem(step + 1, lay.batch // width) * width, width), width)

    def ones16(width):
        return jnp.ones((16, width), BF16)

    def framed(first_row, used, where):
        row32 = rows_of((32, where.size))
        ones3 = jnp.logical_and(row32 >= IN, row32 < IN + 3).astype(F32)
        return jnp.where(row32 < used, xs[first_row : first_row + 32, where], ones3)

    def hidden(inputs, net):
        first, slope1 = gated(dot(w1t[net], inputs))
        second, slope2 = gated(dot(w2t[net], first), wide[net])
        return first, slope1, second, slope2

    def policy(inputs, which, where):
        first, slope1, second, slope2 = hidden(inputs, 4)
        out = dot(heads[4], second) + headcol[0:16, 0:1]
        bent = jnp.tanh(out[8:16])
        log_scale = -5.0 + 3.5 * (bent + 1.0)
        draw = nz[which, :, where]
        moved = jnp.exp(log_scale) * draw
        latent = out[0:8] + moved
        terms = (
            -0.5 * draw * draw
            - log_scale
            - 0.9189385
            - 2.0 * (0.6931472 - latent - softplus(-2.0 * latent))
        )
        used = act_rows(where.size)
        log_prob = jnp.sum(jnp.where(used, terms, 0.0), axis=0, keepdims=True)
        action = jnp.where(used, jnp.tanh(latent), 0.0)
        return action, log_prob, bent, moved, (first, slope1, second, slope2)

    def with_action(inputs, action):
        middle_rows = jnp.where(act_rows(action.shape[1]), action, inputs[16:24])
        return jnp.concatenate([inputs[0:16], middle_rows, inputs[24:32]], 0).astype(BF16)

    def critic(inputs, net):
        kept = hidden(inputs, net)
        value = dot(heads[net], kept[2])[0:1] + last[net]
        return value, kept

    def add_hidden(k, first, grad):
        acc_h[k] += dot(jnp.concatenate([first, ones16(grad.shape[1])], 0), grad, NT)

    has_come(bk.at[pl.ds(0, n_blk - 1)], "line")
    plane_peers(lambda peer: block_plane(peer).start())

    def critic_pass(k, now_in, where, target):
        weight = xs[42:43, where]
        value, (c1, dc1, c2, dc2) = critic(now_in, 2 + k)
        miss = value - target
        g3 = rounded(weight * miss)
        g3_rows = jnp.where(rows_of((16, CRITIC_TILE)) == 0, g3, 0.0).astype(BF16)
        acc_c[k] += dot(g3_rows, c2, NT)
        acc_m[:, 16 + 16 * k : 32 + 16 * k] += dot(ones16(CRITIC_TILE), g3_rows, NT)
        g2 = outer_sloped(wide[5 + k], g3, dc2)
        add_hidden(k, c1, g2)
        g1 = sloped(dot(w2h[k], g2), dc1)
        acc_w[k] += dot(now_in, g1, NT)
        acc_l[0:1, 0:CRITIC_TILE] += weight * (0.5 * miss * miss)

    def put_matrix(k):
        for chunk in range(n_dp):
            tile = chunk * lay.mat
            side, row = tile // 32, tile % 32
            grids[k][chunk % 2, chunk // 2, 0 : lay.mat] = acc_h[
                k, row * 8 : (row + lay.mat) * 8, side * 128 : (side + 1) * 128
            ].reshape(lay.mat, 8, 128)

    def put(row, value):
        for at in range(value.shape[0] // 8):
            for side in range(value.shape[1] // 128):
                tile = side * (R_SMALL // 8) + row // 8 + at
                chunk = tile // lay.sml
                grid_1[chunk % 2, chunk // 2, lay.mat + tile % lay.sml] = value[
                    at * 8 : at * 8 + 8, side * 128 : (side + 1) * 128
                ]

    def core_sum(group):
        name = ("core sum", group)
        return on_plane(
            grids[group].at[1 - core], cores[group], send.at[sent[name]], recv.at[here_at[name]], sibling
        )

    def plane_sum(group, peer):
        name = ("plane sum", group)
        return on_plane(
            cores[group].at[peer // 2], froms[group].at[like], send.at[sent[name]], recv.at[here_at[name]], peer
        )

    def fold_core(group):
        core_sum(group).wait_recv()
        cores[group][...] += grids[group][core]
        like_peers(lambda peer: plane_sum(group, peer).start())

    def line_part(part):
        return (1, pl.ds(lay.mat, lay.sml)) if part == 3 else (part, pl.ds(0, lay.mat))

    def line_sum(part, peer):
        group, tiles = line_part(part)
        name = ("line sum", part)
        src, dst = zfs[group].at[tiles], zrs[group].at[z, tiles]
        return on_line(src, dst, send.at[sent[name]], recv.at[here_at[name]], peer)

    def line_bytes(part):
        group, tiles = line_part(part)
        return zrs[group].at[pl.ds(0, n_blk - 1), tiles]

    first_tile = me * lay.mat
    side = first_tile // 32
    row_tile = lax.rem(first_tile, 32)
    keeper_z = row_tile * 8 // lay.rows
    local_tile = row_tile - keeper_z * (lay.rows // 8)

    def fold_plane(group):
        has_come(froms[group].at[pl.ds(0, lay.half - 1)], ("plane sum", group))
        froms[group][like] = cores[group][like]
        whole = froms[group][0]
        for at in range(1, lay.half):
            whole = whole + froms[group][at]
        zfs[group][...] = whole

        @pl.when(z == keeper_z)
        def _():
            held_rows = pl.ds(pl.multiple_of(local_tile * 8, 8), lay.mat * 8)
            held_lanes = pl.ds(pl.multiple_of(side * 128, 128), 128)
            old = sac_m[group, held_rows, held_lanes].reshape(lay.mat, 8, 128)
            zfs[group][0 : lay.mat] += (MOMENTUM * count[0:1, 0:1]).reshape(1, 1, 1) * old

        for part in (1, 3) if group == 1 else (group,):
            line_peers(lambda peer: line_sum(part, peer).start())

    def tile_copy(k, peer):
        name = ("tiles", k)
        src = totals[k].at[pl.ds(0, lay.mat)]
        return on_plane(src, mg.at[k, core, like], send.at[sent[name]], recv.at[here_at[name]], peer)

    def tiles_on(k):
        name = ("tiles on", k)
        view = mg.at[k, core]
        return on_plane(view, view, send.at[sent[name]], recv.at[here_at[name]], sibling)

    small_at = (core * lay.half + like) * lay.sml

    def small_copy(peer):
        return on_plane(
            sum_1.at[pl.ds(lay.mat, lay.sml)], small.at[pl.ds(small_at, lay.sml)],
            send.at[sent["small"]], recv.at[here_at["small"]], peer,
        )

    def small_on():
        view = small.at[pl.ds(core * lay.half * lay.sml, lay.half * lay.sml)]
        return on_plane(view, view, send.at[sent["small on"]], recv.at[here_at["small on"]], sibling)

    def fold_end(part):
        group, tiles = line_part(part)
        has_come(line_bytes(part), ("line sum", part))
        zrs[group][z, tiles] = zfs[group][tiles]
        whole = zrs[group][0, tiles]
        for block in range(1, n_blk):
            whole = whole + zrs[group][block, tiles]
        totals[group][tiles] = whole
        if part == 3:
            like_peers(lambda peer: small_copy(peer).start())
            small[pl.ds(small_at, lay.sml)] = whole
        else:
            like_peers(lambda peer: tile_copy(part, peer).start())
            mg[part, core, like] = whole

    def chain(group):
        def end():
            for part in (1, 3) if group == 1 else (group,):
                fold_end(part)

        def turn():
            has_come(mg.at[group, 0, pl.ds(0, lay.half - 1)], ("tiles", group))
            tiles_on(group).start()
            if group == 1:
                has_come(small.at[pl.ds(0, (lay.half - 1) * lay.sml)], "small")
                small_on().start()

        return [
            lambda: core_sum(group).start(),
            lambda: fold_core(group),
            lambda: fold_plane(group),
            end,
            turn,
        ]

    chains = [chain(group) for group in range(3)]
    per = DYN_TILE // lay.real
    dyn_tiles = lay.n_dev // per

    def take(slots, step):
        for at, events in slots.items():
            @pl.when(step == at)
            def _():
                for event in events:
                    event()

    @pl.loop(0, actor_tiles)
    def _(step):
        @pl.when(step == actor_tiles - 1)
        def _():
            has_come(bk.at[pl.ds(0, n_dp - 1)], "own")
            lanes = lax.broadcasted_iota(jnp.int32, (48, lay.width), 1) // CAP

            def gather(owner, total):
                turned = pltpu.roll(
                    bk[owner * n_blk], lax.rem((owner - me) * CAP + lay.width, lay.width), axis=1
                )
                return jnp.where(lanes == owner, turned, total)

            own = lax.fori_loop(0, n_dp, gather, jnp.zeros((48, lay.width), F32))
            xs[0:48, 0 : lay.real] = own[:, 0 : lay.real]

        where = place_of(step, ACTOR_TILE)
        now_f = framed(0, IN, where)
        now_in = now_f.astype(BF16)
        weight = xs[42:43, where]
        action, log_prob, bent, moved, (a1, da1, a2, da2) = policy(now_in, 0, where)
        judged_in = with_action(now_f, action)
        loss = alpha * log_prob - log_alpha * (log_prob + TARGET_ENTROPY)
        grad_action = jnp.zeros((8, ACTOR_TILE), F32)
        used = act_rows(ACTOR_TILE)
        for k in range(2):
            judged, (_, df1, _, df2) = critic(judged_in, 2 + k)
            loss -= 0.5 * judged
            g2 = outer_sloped(wide[5 + k], -0.5 * weight, df2)
            g1 = sloped(dot(w2h[k], g2), df1)
            grad_action += dot(w1n[k], g1)[0:8]
        grad_latent = 2.0 * alpha * weight * action + grad_action * (1.0 - action * action)
        grad_scale = grad_latent * moved - alpha * weight
        grad_bent = grad_scale * 3.5 * (1.0 - bent * bent)
        g3 = jnp.concatenate(
            [jnp.where(used, grad_latent, 0.0), jnp.where(used, grad_bent, 0.0)], 0
        ).astype(BF16)
        acc_a[...] += dot(g3, a2, NT)
        acc_m[:, 0:16] += dot(ones16(ACTOR_TILE), g3, NT)
        g2 = sloped(dot(head_t[...], g3), da2)
        add_hidden(2, a1, g2)
        g1 = sloped(dot(w2h[2], g2), da1)
        acc_w[2] += dot(now_in, g1, NT)
        acc_l[1:2, 0:ACTOR_TILE] += weight * loss
        acc_l[2:3, 0:ACTOR_TILE] += weight * (log_prob + TARGET_ENTROPY)

    put_matrix(2)
    chains[2][0]()

    @pl.loop(0, critic_tiles)
    def _(step):
        if critic_tiles > 1:
            take({1: [chains[2][1]]}, step)

        where = place_of(step, CRITIC_TILE)
        now_in = framed(0, IN, where).astype(BF16)
        next_f = framed(24, OBS, where)
        reward = xs[23:24, where]
        done = xs[41:42, where]
        next_action, next_prob, _, _, _ = policy(next_f.astype(BF16), 1, where)
        aim_in = with_action(next_f, next_action)
        aim = jnp.minimum(critic(aim_in, 0)[0], critic(aim_in, 1)[0])
        target = reward + DISCOUNT * (1.0 - done) * (aim - alpha * next_prob)
        ys[0:1, where] = target
        critic_pass(0, now_in, where, target)

    put_matrix(0)
    chains[0][0]()
    if critic_tiles == 1:
        chains[2][1]()

    has_come(bk.at[pl.ds(0, (n_dp - 1) * (n_blk - 1))], "plane")
    lane0 = lay.real // 128 * 128

    def add_block(at, carry):
        sides, fills = carry
        slot = slot_of(at)
        return sides + bk[slot, 0:32, lane0 : lane0 + 128], fills + bk[slot, 40:48, 0 : lay.real]

    sides, fills = lax.fori_loop(
        0, lay.n_dev, add_block, (jnp.zeros((32, 128), F32), jnp.zeros((8, lay.real), F32))
    )
    at = lay.real - lane0
    rows_all = float(lay.replay * lay.n_dev)
    centre = sides[0:24, at : at + 1] / rows_all
    scale = lax.rsqrt(sides[0:24, at + 1 : at + 2] / rows_all - centre * centre + 1e-6)
    total = sides[24:25, at : at + 1] + jnp.sum(fills[2:3, :], axis=1, keepdims=True)
    count[...] = jnp.broadcast_to(total, (8, 128))

    @pl.loop(0, critic_tiles)
    def _(step):
        take({critic_tiles - 1: [chains[0][1], chains[2][2]]}, step)
        where = place_of(step, CRITIC_TILE)
        critic_pass(1, framed(0, IN, where).astype(BF16), where, ys[0:1, where])

    put_matrix(1)
    for k in range(3):
        put(R_IN + 24 * k, acc_w[k, 0:24, :])
    put(R_HEAD, acc_a[...])
    rowbuf[0:1, :] = acc_c[0, 0:1, :]
    rowbuf[1:2, :] = acc_c[1, 0:1, :]
    for k in range(3):
        rowbuf[2 + k : 3 + k, :] = acc_h[k, HSAC : HSAC + 1, :]
    put(R_OUT, rowbuf[...])
    folded = jnp.sum(acc_l[...], axis=1, keepdims=True)
    rowbuf[...] = jnp.zeros_like(rowbuf)
    rowbuf[0:1, 0:48] = acc_m[0:1, :]
    rowbuf[0:1, 64:65] = folded[0:1] + folded[1:2]
    rowbuf[0:1, 65:66] = folded[2:3]
    put(R_MISC, rowbuf[...])
    put(R_MISC + 8, jnp.zeros((R_SMALL - R_MISC - 8, HSAC), F32))
    chains[1][0]()

    def dyn_bias(start, width):
        row = jnp.zeros((1, width), F32)
        for e in range(MEMBERS):
            row = jnp.where(me == e, bias[:, start + width * e : start + width * (e + 1)], row)
        return row

    @pl.when(is_dyn)
    def _():
        w1f[0] = jnp.zeros((32, HSAC), F32)
        w1f[0, 0:IN, 0:HDYN] = rounded(dyn_in[dyn_e])
        for at, piece in enumerate(pieces(dyn_bias(DB1, HDYN))):
            w1f[0, IN + at : IN + at + 1, 0:HDYN] = piece.astype(F32)
        w1t[0] = (0.5 * w1f[0].T).astype(BF16)
        rowbuf[...] = jnp.zeros_like(rowbuf)
        rowbuf[0:1, 0:HDYN] = dyn_bias(DB2, HDYN)
        head_row = dyn_bias(DB3, DOUT)
        rowbuf[1:2, 0:HALF] = head_row[:, 0:HALF]
        rowbuf[1:2, 24 : 24 + HALF] = head_row[:, HALF:DOUT]
        rowbuf[2:3, 0:HALF] = bias[:, MAXLV : MAXLV + HALF]
        rowbuf[3:4, 0:HALF] = bias[:, MINLV : MINLV + HALF]
        dcols[...] = rowbuf[...].T
        wide[0] = jnp.broadcast_to(0.5 * dcols[:, 0:1], (HSAC, 128))
        dpack[...] = jnp.zeros_like(dpack)
        dpack[0:HALF, 0:HDYN] = dyn_out[dyn_e, 0:HALF, :]
        dpack[24 : 24 + HALF, 0:HDYN] = dyn_out[dyn_e, HALF:DOUT, :]
        dhead[...] = dpack[0:48, :].astype(BF16)
        dhead_t[...] = (0.5 * rounded(dpack[0:48, :])).T.astype(BF16)
        dpack[...] = jnp.zeros_like(dpack)

        has_come(dhg.at[pl.ds(0, n_blk - 1)], "dyn h")
        has_come(dmg.at[pl.ds(0, n_blk - 1)], "dyn m")
        dhg[z] = dyn_h[dyn_e]
        dmg[z] = dyn_m[dyn_e]
        dmat[...] = jnp.zeros_like(dmat)
        for block in range(n_blk):
            dmat[block * lay.drows : (block + 1) * lay.drows, 0:HDYN] = 0.5 * rounded(dhg[block])
        w2h[0] = dmat[...].astype(BF16)
        w2t[0] = dmat[...].T.astype(BF16)
        for ref in (dacc_h, dacc_w, dacc_o, dacc_m, dacc_b, dacc_l):
            ref[...] = jnp.zeros_like(ref)

    in_dyn = {min(1, dyn_tiles - 1): [chains[0][2], chains[1][1], chains[2][3]]}

    @pl.loop(0, dyn_tiles)
    def _(tile):
        take(in_dyn, tile)

        @pl.when(is_dyn)
        def _():
            for at in range(per):
                slot = slot_of(tile * per + at)
                xt[:, at * lay.real : (at + 1) * lay.real] = bk[slot, :, 0 : lay.real]
            now = xt[0:24, :]
            later = xt[24:48, :]
            row24 = rows_of((24, DYN_TILE))
            scaled = jnp.where(row24 < IN, (now - centre) * scale, 1.0)
            inputs = jnp.concatenate([scaled, (rows_of((8, DYN_TILE)) < 2).astype(F32)], 0).astype(BF16)
            first, slope1 = gated(dot(w1t[0], inputs))
            second, slope2 = gated(dot(w2t[0], first), wide[0])
            out = dot(dhead[...], second) + dcols[0:48, 1:2]
            used = row24 < HALF
            upper = dcols[0:24, 2:3]
            lower = dcols[0:24, 3:4]
            gap1 = upper - out[24:48]
            gap2 = upper - softplus(gap1) - lower
            log_var = lower + softplus(gap2)
            error = out[0:24] - jnp.where(row24 == OBS, now[23:24], later - now)
            inverse = jnp.exp(-log_var)
            weight = xt[42:43, :] * (xt[43:44, :] == me.astype(F32)).astype(F32)
            spread_term = error * error * inverse
            nll = jnp.sum(jnp.where(used, spread_term + log_var, 0.0), axis=0, keepdims=True)
            dacc_l[0:1, :] += weight * nll
            grad_mu = 2.0 * weight * error * inverse
            grad_lv = weight * (1.0 - spread_term)
            open1 = sigmoid(gap1)
            open2 = sigmoid(gap2)
            grad_lv1 = grad_lv * open2
            dacc_b[0] += jnp.where(used, grad_lv1 * (1.0 - open1), 0.0)
            dacc_b[1] += jnp.where(used, grad_lv * (1.0 - open2), 0.0)
            g3 = jnp.concatenate(
                [jnp.where(used, grad_mu, 0.0), jnp.where(used, grad_lv1 * open1, 0.0)], 0
            ).astype(BF16)
            dacc_o[...] += dot(g3, second, NT)
            dacc_m[...] += dot(ones16(DYN_TILE), g3, NT)
            g2 = sloped(dot(dhead_t[...], g3), slope2)
            dacc_h[...] += dot(jnp.concatenate([first, ones16(DYN_TILE)], 0), g2, NT)
            g1 = sloped(dot(w2h[0], g2), slope1)
            dacc_w[...] += dot(inputs, g1, NT)

    out_of = {"pack": dyn_s, "x": dyn_x}

    def member_copy(name, src, owner, kind, sem, peer):
        return on_plane(src, out_of[name].at[owner], send.at[sent[name, kind]], recv.at[sem], peer)

    def give(name, src):
        like_peers(
            lambda peer: member_copy(name, src, dyn_e, "own", here_at[name, "like"] + dyn_e, peer).start()
        )
        member_copy(name, src, dyn_e, "own", here_at[name, "sibling"], sibling).start()

    def hand_on(name):
        def body(peer):
            @pl.when(peer < MEMBERS)
            def _():
                owner = jnp.minimum(peer, MEMBERS - 1)
                view = out_of[name].at[owner]
                member_copy(name, view, owner, "on", here_at[name, "like"] + owner, sibling).wait_recv()
                member_copy(name, view, owner, "on", here_at[name, "sibling"], sibling).start()

        like_peers(body)

    even, odd = (MEMBERS + 1) // 2, MEMBERS // 2
    handed = even - core * (even - odd) - jnp.where(is_dyn, 1, 0)

    def from_sibling(name):
        for side, number in ((0, odd), (1, even)):
            @pl.when(core == side)
            def _():
                has_come(out_of[name].at[pl.ds(0, number)], (name, "sibling"))

    def gave(name):
        @pl.when(is_dyn)
        def _():
            for begin in range(0, n_dp // 2, MEMBERS):
                number = min(MEMBERS, n_dp // 2 - begin)
                has_sent(out_of[name].at[pl.ds(0, number)], (name, "own"))

        for number in (even, even - 1, even - 2):
            @pl.when(handed == number)
            def _():
                has_sent(out_of[name].at[pl.ds(0, number)], (name, "on"))

    def line_rows(ref):
        rows = ref[0 : lay.drows, 0:HDYN]
        for block in range(1, n_blk):
            rows = jnp.where(z == block, ref[block * lay.drows : (block + 1) * lay.drows, 0:HDYN], rows)
        return rows

    mine_rows = pl.ds(pl.multiple_of(z * lay.rows, lay.rows), lay.rows)

    def take_matrix(k):
        tiles_on(k).wait_recv()
        for chunk in range(n_dp):
            tile = chunk * lay.mat
            half, row = tile // 32, tile % 32
            at = slice(row * 8, (row + lay.mat) * 8)
            piece = mg[k, chunk % 2, chunk // 2].reshape(lay.mat * 8, 128)
            mat[k, at, half * 128 : (half + 1) * 128] = piece / total
        normalise(mat.at[k])

    chains[1][2]()
    chains[2][4]()

    @pl.when(is_dyn)
    def _():
        dpack[D_IN : D_IN + 24, :] = dacc_w[0:24, :]
        dpack[D_OUT : D_OUT + HALF, :] = dacc_o[0:HALF, :]
        dpack[D_OUT + HALF : D_OUT + DOUT, :] = dacc_o[24 : 24 + HALF, :]
        dpack[D_B2 : D_B2 + 1, :] = dacc_h[HSAC : HSAC + 1, :]
        dpack[D_B3 : D_B3 + 1, 0:48] = dacc_m[0:1, :]
        lanes = lax.broadcasted_iota(jnp.int32, (24, 128), 1)
        bound = jnp.where(
            lanes == 0,
            jnp.sum(dacc_b[0], axis=1, keepdims=True),
            jnp.where(lanes == 1, jnp.sum(dacc_b[1], axis=1, keepdims=True), 0.0),
        )
        dpack[D_UP : D_UP + 2, 0:24] = bound.T[0:2, :]
        dpack[D_LOSS : D_LOSS + 1, 0:128] = jnp.broadcast_to(
            jnp.sum(dacc_l[0:1, :], axis=1, keepdims=True), (1, 128)
        )
        dpack[D_HID : D_HID + lay.drows, 0:HDYN] = line_rows(dacc_h)
        dyn_s[dyn_e] = dpack[...]
        give("pack", dpack)
        dmat[...] = jnp.zeros_like(dmat)
        for block in range(n_blk):
            at = slice(block * lay.drows, (block + 1) * lay.drows)
            dmat[at, 0:HDYN] = MOMENTUM * dmg[block] + dacc_h[at, 0:HDYN] / total
        normalise(dmat)

    def sum_end(step):
        pl.when(step == 1)(chains[0][3])
        pl.when(step == 3)(chains[1][3])
        pl.when(step == NS_ITERS - 1)(chains[0][4])

    take_matrix(2)

    @pl.when(is_dyn)
    def _():
        schulz([dmat, mat.at[2]], NS_ITERS, sum_end)
        rows = line_rows(dmat)
        drow_x[...] = rows
        dyn_x[dyn_e] = rows
        give("x", drow_x)

    @pl.when(jnp.logical_not(is_dyn))
    def _():
        schulz([mat.at[2]], NS_ITERS, sum_end)

    def sent_early():
        has_sent(wg.at[pl.ds(0, n_blk - 1), :, half_rows], "hidden")
        has_sent(wg.at[pl.ds(0, n_blk - 1), :, half_rows], "hidden on")
        has_sent(asked.at[pl.ds(0, n_dp - 1)], "lists")
        has_sent(bk.at[pl.ds(0, n_dp - 1)], "own")
        has_sent(bk.at[pl.ds(0, n_blk - 1)], "line")
        has_sent(bk.at[pl.ds(0, (n_dp - 1) * (n_blk - 1))], "plane")

        @pl.when(is_dyn)
        def _():
            has_sent(dhg.at[pl.ds(0, n_blk - 1)], "dyn h")
            has_sent(dmg.at[pl.ds(0, n_blk - 1)], "dyn m")

        for group in range(3):
            core_sum(group).wait_send()
            has_sent(froms[group].at[pl.ds(0, lay.half - 1)], ("plane sum", group))
        for part in range(4):
            has_sent(line_bytes(part), ("line sum", part))

    def pass_on(step):
        pl.when(step == 2)(functools.partial(hand_on, "pack"))
        pl.when(step == NS_ITERS - 1)(functools.partial(hand_on, "x"))

    sent_early()
    chains[1][4]()
    for k in range(2):
        take_matrix(k)
    schulz([mat.at[0], mat.at[1]], NS_ITERS, pass_on)
    for k in range(3):
        sac_x[k] = mat[k, mine_rows, :]
        for half in range(2):
            for piece in range(lay.rows // 8 // lay.mat):
                chunk = (half * 32 + z * (lay.rows // 8)) // lay.mat + piece
                kept = mg[k, lax.rem(chunk, 2), chunk // 2]
                sac_g[half, k, piece * lay.mat : (piece + 1) * lay.mat] = kept

    small_on().wait_recv()
    from_sibling("pack")
    from_sibling("x")

    has_sent(small.at[pl.ds(0, (lay.half - 1) * lay.sml)], "small")
    small_on().wait_send()
    gave("pack")
    gave("x")

    for k in range(3):
        has_sent(mg.at[k, 0, pl.ds(0, lay.half - 1)], ("tiles", k))
        tiles_on(k).wait_send()


def ordered(lay, n_in, n_out, *refs):
    inputs, outputs, scratch = refs[:n_in], refs[n_in : n_in + n_out], refs[n_in + n_out :]
    main_kernel(lay, *inputs, *scratch[: n_in + 1], *outputs, *scratch[n_in + 1 :])


def adamw(weights, first, second, gradient):
    first = BETA_FIRST * first + (1.0 - BETA_FIRST) * gradient
    second = BETA_SECOND * second + (1.0 - BETA_SECOND) * gradient * gradient
    first_hat = first / (1.0 - BETA_FIRST**STEP)
    second_hat = second / (1.0 - BETA_SECOND**STEP)
    step = first_hat / (jnp.sqrt(second_hat) + 1e-8) + ADAM_DECAY * weights
    return weights - ADAM_RATE * step, first, second


def update_kernel(lay, *refs):
    (
        sac_g, sac_x, dyn_x, dyn_s, small, count, crit_rows, sac_h, dyn_h, dyn_m,
        ci, ci_m, ci_v, ai, ai_m, ai_v, di, di_m, di_v, ao, ao_m, ao_v,
        do, do_m, do_v, bi, bi_m, bi_v,
        sac_new, sac_mom, dyn_new, dyn_mom, ci_n, ci_mn, ci_vn, ai_n, ai_mn, ai_vn, di_n, di_mn,
        di_vn, co_n, co_mn, co_vn, ao_n, ao_mn, ao_vn, do_n, do_mn, do_vn, bi_n, bi_mn, bi_vn,
        loss, counted, bg,
    ) = refs
    total = count[0:1, 0:1]

    def store(outs, at, values):
        for out, value in zip(outs, values):
            out[at] = value

    @pl.loop(0, MEMBERS)
    def _(e):
        grad = dyn_s[e, 0:IN, 0:HDYN] / total
        store((di_n, di_mn, di_vn), e, adamw(di[e], di_m[e], di_v[e], grad))
        grad = dyn_s[e, D_OUT : D_OUT + DOUT, 0:HDYN] / total
        store((do_n, do_mn, do_vn), e, adamw(do[e], do_m[e], do_v[e], grad))
        grad = dyn_s[e, D_HID : D_HID + dyn_m.shape[1], 0:HDYN] / total
        dyn_mom[e] = MOMENTUM * dyn_m[e] + grad
        dyn_new[e] = dyn_h[e] * (1.0 - MUON_RATE * MUON_DECAY) - MUON_RATE * dyn_x[e]

    for k in range(3):
        for side in range(2):
            tiles = sac_g[side, k].reshape(sac_mom.shape[1], 128)
            sac_mom[k, :, side * 128 : (side + 1) * 128] = tiles / total
    sac_new[...] = sac_h[...] * (1.0 - MUON_RATE * MUON_DECAY) - MUON_RATE * sac_x[...]

    def rows(row, number):
        def tile(at):
            chunk = at // lay.sml
            return small[(chunk % 2 * lay.half + chunk // 2) * lay.sml + at % lay.sml]

        sides = []
        for side in range(2):
            at = side * (R_SMALL // 8) + row // 8
            sides.append(jnp.concatenate([tile(at + more) for more in range(-(-number // 8))], 0))
        return jnp.concatenate(sides, 1)

    outs = (ci_n, ci_mn, ci_vn)
    for k in range(2):
        at = (slice(None), k, slice(None))
        grad = rows(R_IN + 24 * k, 24)
        bg[:, CB1 + HSAC * k : CB1 + HSAC * (k + 1)] = grad[IN : IN + 1]
        store(outs, at, adamw(ci[at], ci_m[at], ci_v[at], grad[0:IN] / total))
    grad = rows(R_IN + 48, 24)
    bg[:, AB1 : AB1 + HSAC] = grad[IN : IN + 1]
    store((ai_n, ai_mn, ai_vn), ..., adamw(ai[...], ai_m[...], ai_v[...], grad[0:OBS] / total))
    grad = rows(R_HEAD, 16)
    for at, row in ((slice(0, ACT), slice(1, 1 + ACT)), (slice(ACT, 2 * ACT), slice(9, 9 + ACT))):
        store((ao_n, ao_mn, ao_vn), at, adamw(ao[at], ao_m[at], ao_v[at], grad[row] / total))
    grad = rows(R_OUT, 8)
    held = [crit_rows[2 * at : 2 * at + 2, :] for at in range(3)]
    store((co_n, co_mn, co_vn), ..., adamw(*held, grad[0:2] / total))
    bg[:, CB2 : CB2 + HSAC] = grad[2:3]
    bg[:, CB2 + HSAC : CB2 + 2 * HSAC] = grad[3:4]
    bg[:, AB2 : AB2 + HSAC] = grad[4:5]
    grad = rows(R_MISC, 8)
    bg[:, CB3 : CB3 + 1] = grad[0:1, 16:17]
    bg[:, CB3 + 1 : CB3 + 2] = grad[0:1, 32:33]
    bg[:, AB3 : AB3 + ACT] = grad[0:1, 1 : 1 + ACT]
    bg[:, AB3 + ACT : AB3 + 2 * ACT] = grad[0:1, 9 : 9 + ACT]
    bg[:, LOGA : LOGA + 1] = -grad[0:1, 65:66]
    total_loss = grad[0:1, 64:65]
    up = jnp.zeros((1, HALF), F32)
    low = jnp.zeros((1, HALF), F32)
    for e in range(MEMBERS):
        pack = dyn_s[e]
        total_loss = total_loss + pack[D_LOSS : D_LOSS + 1, 0:1]
        up = up + pack[D_UP : D_UP + 1, 0:HALF]
        low = low + pack[D_LOW : D_LOW + 1, 0:HALF]
        bg[:, DB1 + HDYN * e : DB1 + HDYN * (e + 1)] = pack[IN : IN + 1, 0:HDYN]
        bg[:, DB2 + HDYN * e : DB2 + HDYN * (e + 1)] = pack[D_B2 : D_B2 + 1, 0:HDYN]
        bg[:, DB3 + DOUT * e : DB3 + DOUT * e + HALF] = pack[D_B3 : D_B3 + 1, 0:HALF]
        bg[:, DB3 + DOUT * e + HALF : DB3 + DOUT * (e + 1)] = pack[D_B3 : D_B3 + 1, 24 : 24 + HALF]
    bg[:, MAXLV : MAXLV + HALF] = up
    bg[:, MINLV : MINLV + HALF] = low
    lane = lax.broadcasted_iota(jnp.int32, (1, NB), 1)
    bounds = jnp.where(
        jnp.logical_and(lane >= MAXLV, lane < MINLV),
        BOUND_WEIGHT,
        jnp.where(jnp.logical_and(lane >= MINLV, lane < LOGA), -BOUND_WEIGHT, 0.0),
    )
    grad = bg[...] / total + bounds
    flat = [ref[...].reshape(1, NB) for ref in (bi, bi_m, bi_v)]
    store((bi_n, bi_mn, bi_vn), ..., [value.reshape(NB) for value in adamw(*flat, grad)])
    loss[...] = total_loss
    counted[...] = total


def shards(
    lay, replay, model_rows, requests, member_of, model_live, noise, sac_hidden, sac_hidden_mom,
    dyn_hidden, dyn_hidden_mom, crit_in, crit_in_m, crit_in_v, act_in, act_in_m, act_in_v, dyn_in,
    dyn_in_m, dyn_in_v, crit_out, crit_out_m, crit_out_v, act_out, act_out_m, act_out_v, dyn_out,
    dyn_out_m, dyn_out_v, biases, biases_m, biases_v, targ_in, targ_hidden, targ_out, targ_bias,
):
    n_dp, n_blk = lay.n_dp, lay.n_blk
    spec = pl.BlockSpec(memory_space=pltpu.VMEM)

    def flip(value):
        return jnp.transpose(value, (1, 0, 2))

    def swap(value):
        return jnp.swapaxes(value, -1, -2)

    def kept(value):
        return pltpu.with_memory_space_constraint(value, pltpu.VMEM)

    inputs = (
        sac_hidden, requests, member_of, replay, model_live, model_rows, jnp.transpose(noise, (2, 0, 1)),
        biases, flip(targ_in), flip(crit_in), act_in, targ_bias, targ_hidden, crit_out, targ_out,
        swap(act_out), dyn_hidden, dyn_hidden_mom, crit_out_m, crit_out_v, sac_hidden_mom, dyn_in,
        swap(dyn_out),
    )
    shape = jax.ShapeDtypeStruct
    rows, drows = lay.rows, lay.drows
    out_shape = (
        pltpu.VMEM((2, 3, rows // 8, 8, 128), F32),
        pltpu.VMEM((3, rows, HSAC), F32),
        pltpu.VMEM((MEMBERS, drows, HDYN), F32),
        pltpu.VMEM((MEMBERS, D_ROWS, HSAC), F32),
        pltpu.VMEM((32, 8, 128), F32),
        pltpu.VMEM((8, 128), F32),
        pltpu.VMEM((8, HSAC), F32),
    )

    def vm(*dims, kind=F32):
        return pltpu.VMEM(dims, kind)

    scratch = [
        vm(n_blk, 3, rows, HSAC, kind=BF16),
        vm(2, n_dp, CAP, kind=jnp.int32),
        vm(n_dp, 2, n_dp, CAP, kind=jnp.int32),
        vm(n_blk, drows, HDYN),
        vm(n_blk, drows, HDYN),
        vm(lay.n_dev, 48, lay.width),
        vm(56, lay.batch),
        vm(2, 8, lay.batch),
        vm(8, lay.batch),
        vm(5, 32, HSAC),
        vm(5, HSAC, 32, kind=BF16),
        vm(2, 16, HSAC, kind=BF16),
        vm(5, HSAC, HSAC, kind=BF16),
        vm(3, HSAC, HSAC, kind=BF16),
        vm(5, 16, HSAC, kind=BF16),
        vm(HSAC, 16, kind=BF16),
        vm(16, HSAC),
        vm(8, HSAC),
        vm(7, HSAC, 128),
        vm(128, 8),
        vm(3, HSAC + 16, HSAC),
        vm(3, 32, HSAC),
        vm(2, 16, HSAC),
        vm(16, HSAC),
        vm(16, 48),
        vm(8, max(CRITIC_TILE, ACTOR_TILE)),
        *[vm(2, lay.half, chunk, 8, 128) for chunk in lay.chunks],
        *[vm(lay.half, chunk, 8, 128) for chunk in lay.chunks],
        *[vm(lay.half, chunk, 8, 128) for chunk in lay.chunks],
        *[vm(n_blk, chunk, 8, 128) for chunk in lay.chunks],
        *[vm(chunk, 8, 128) for chunk in lay.chunks],
        *[vm(chunk, 8, 128) for chunk in lay.chunks],
        vm(3, 2, lay.half, lay.mat, 8, 128),
        vm(3, HSAC, HSAC),
        vm(HSAC, 8),
        vm(HSAC + 16, HSAC),
        vm(32, HSAC),
        vm(48, HSAC),
        vm(16, 48),
        vm(2, 24, DYN_TILE),
        vm(8, DYN_TILE),
        vm(48, DYN_TILE),
        vm(HSAC, HSAC),
        vm(D_ROWS, HSAC),
        vm(drows, HDYN),
        vm(1, NB),
        vm(48, HSAC, kind=BF16),
        vm(HSAC, 48, kind=BF16),
    ]
    scratch += [pltpu.SemaphoreType.DMA((lay.departures,)), pltpu.SemaphoreType.DMA((lay.arrivals,))]
    held = [pltpu.VMEM(value.shape, value.dtype) for value in inputs]
    held.append(pltpu.SemaphoreType.DMA((len(inputs),)))
    varying = 4 * (lay.n_dev * 48 * lay.width + 72 * lay.batch + 48 * lay.replay)
    gathered = pl.pallas_call(
        functools.partial(ordered, lay, len(inputs), len(out_shape)),
        out_shape=out_shape,
        in_specs=[pl.BlockSpec(memory_space=pl.ANY)] * len(inputs),
        out_specs=[spec] * len(out_shape),
        scratch_shapes=held + scratch,
        compiler_params=pltpu.CompilerParams(
            collective_id=0, has_side_effects=True, vmem_limit_bytes=26 * 2**20 + varying
        ),
        name="step",
    )(*[pltpu.with_memory_space_constraint(value, pltpu.HBM) for value in inputs])
    params = (
        sac_hidden, dyn_hidden, dyn_hidden_mom,
        flip(crit_in), flip(crit_in_m), flip(crit_in_v), act_in, act_in_m, act_in_v,
        dyn_in, dyn_in_m, dyn_in_v,
        swap(act_out), swap(act_out_m), swap(act_out_v),
        swap(dyn_out), swap(dyn_out_m), swap(dyn_out_v), biases, biases_m, biases_v,
    )
    new_shape = [shape(sac_hidden.shape, F32)] + [shape(value.shape, F32) for value in params[:12]]
    new_shape += [shape(crit_out.shape, F32)] * 3 + [shape(value.shape, F32) for value in params[12:]]
    new_shape += [shape((1, 1), F32)] * 2
    out = pl.pallas_call(
        functools.partial(update_kernel, lay),
        out_shape=tuple(new_shape),
        in_specs=[spec] * (len(gathered) + len(params)),
        out_specs=[spec] * len(new_shape),
        scratch_shapes=[vm(1, NB)],
        compiler_params=pltpu.CompilerParams(vmem_limit_bytes=16 * 2**20),
        name="update",
    )(*[kept(value) for value in gathered], *params)
    out = list(out)
    for at in (4, 5, 6):
        out[at] = flip(out[at])
    for at in (16, 17, 18, 19, 20, 21):
        out[at] = swap(out[at])
    for at in (25, 26):
        out[at] = out[at].reshape(())
    return tuple(out)


def solution(mesh):
    both = ("dp", "blk")
    sharded = (
        P(None, both), P(None, both), P(both, None), P(both, None), P(both), P(None, both, None),
    )
    hidden = (P(None, "blk", None),) * 4

    def step(replay, model_rows, *others):
        lay = Layout(mesh, replay.shape[1], model_rows.shape[1])
        return shards(lay, replay, model_rows, *others)

    return jax.shard_map(
        step,
        mesh=mesh,
        in_specs=sharded + hidden + (P(),) * 25,
        out_specs=hidden + (P(),) * 23,
        check_vma=False,
    )
```

```python
import functools

import jax
import jax.numpy as jnp
from jax import lax
from jax.experimental import pallas as pl
from jax.experimental.pallas import tpu as pltpu
from jax.sharding import PartitionSpec as P

OBS = 17
ACT = 6
IN = OBS + ACT
FEAT = 42
HDYN = 200
HSAC = 256
MEMBERS = 7
DOUT = 36
HALF = DOUT // 2
NB = 4639
NS_ITERS = 5
STEP = 10
CAP = 8
CRITIC_TILE = 640
ACTOR_TILE = 640
DYN_TILE = 512
ROWS = 32

DISCOUNT = 0.99
TARGET_ENTROPY = -6.0
BOUND_WEIGHT = 0.01
MOMENTUM = 0.95
MUON_RATE = 0.4
MUON_DECAY = 0.01
ADAM_RATE = 0.1
ADAM_DECAY = 0.01
BETA_FIRST = 0.9
BETA_SECOND = 0.999
COEF_LINEAR = 3.4445
COEF_CUBIC = -4.775
COEF_QUINTIC = 2.0315

CB1, CB2, CB3, AB1, AB2, AB3 = 0, 512, 1024, 1026, 1282, 1538
DB1, DB2, DB3, MAXLV, MINLV, LOGA = 1550, 2950, 4350, 4602, 4620, 4638

R_IN, R_HEAD, R_OUT, R_MISC, R_SMALL = 0, 72, 88, 96, 128
D_IN, D_OUT, D_B2, D_B3, D_UP, D_LOW, D_LOSS, D_HID, D_ROWS = 0, 24, 60, 61, 62, 63, 64, 72, 128

F32, BF16 = jnp.float32, jnp.bfloat16
MESH = pl.DeviceIdType.MESH
NN = (((1,), (0,)), ((), ()))
NT = (((1,), (1,)), ((), ()))


def dot(a, b, dims=NN):
    return lax.dot_general(a, b, dims, preferred_element_type=F32)


def rounded(v):
    return v.astype(BF16).astype(F32)


def pieces(v):
    high = v.astype(BF16)
    rest = v - high.astype(F32)
    middle = rest.astype(BF16)
    return high, middle, (rest - middle.astype(F32)).astype(BF16)


def split(v):
    high = v.astype(BF16)
    return high, (v - high.astype(F32)).astype(BF16)


def product(a, b, dims=NN):
    left = jnp.concatenate([a[0], a[0], a[1]], 1)
    right = jnp.concatenate([b[0], b[1], b[0]], dims[0][1][0])
    half = left.shape[0] // 2
    return jnp.concatenate([dot(left[:half], right, dims), dot(left[half:], right, dims)], 0)


def softplus(v):
    return jnp.maximum(v, 0.0) + jnp.log1p(jnp.exp(-jnp.abs(v)))


def sigmoid(v):
    return 0.5 + 0.5 * jnp.tanh(0.5 * v)


def gate(half):
    up = 1.0 + jnp.tanh(half)
    value = half * up
    return value, up + value * (2.0 - up)


def by_rows(body, *arrays):
    done = [
        body(*[array[at : at + ROWS] for array in arrays]) for at in range(0, arrays[0].shape[0], ROWS)
    ]
    return [jnp.concatenate(parts, 0) for parts in zip(*done)]


def spread_to(column, width):
    return jnp.concatenate([column] * (width // 128), 1)


def gated(half, column=None):
    def body(part, *offset):
        value, slope = gate(part + spread_to(offset[0], part.shape[1]) if offset else part)
        return value.astype(BF16), slope

    return by_rows(body, half, *([] if column is None else [column]))


def sloped(grad, slope):
    return by_rows(lambda part, by: ((part * by).astype(BF16),), grad, slope)[0]


def outer_sloped(column, row, slope):
    return by_rows(lambda part, by: (((spread_to(part, by.shape[1]) * row) * by).astype(BF16),), column, slope)[0]


def rows_of(shape):
    return lax.broadcasted_iota(jnp.int32, shape, 0)


def schulz(refs, steps, before=None):
    @pl.loop(0, steps)
    def _(step):
        if before is not None:
            before(step)
        matrices = [ref[...] for ref in refs]
        parts = [split(matrix) for matrix in matrices]
        grams = [product(part, part, NT) for part in parts]
        halves = [split(gram) for gram in grams]
        squares = [product(half, half) for half in halves]
        blends = [
            split(COEF_CUBIC * gram + COEF_QUINTIC * square) for gram, square in zip(grams, squares)
        ]
        moved = [product(blend, part) for blend, part in zip(blends, parts)]
        for ref, matrix, move in zip(refs, matrices, moved):
            ref[...] = COEF_LINEAR * matrix + move


def normalise(ref):
    moment = ref[...]
    norm = jnp.sqrt(jnp.sum(jnp.sum(moment * moment, axis=1, keepdims=True), axis=0, keepdims=True))
    ref[...] = moment / (norm + 1e-7)


class Layout:
    def __init__(self, mesh, replay, model):
        self.n_dp = mesh.shape["dp"]
        self.half = self.n_dp // 2
        self.n_blk = mesh.shape["blk"]
        self.n_dev = self.n_dp * self.n_blk
        self.replay = replay
        self.model = model
        self.real = self.n_dp * CAP
        self.batch = self.real + model
        self.width = -(-(self.real + 2) // 128) * 128
        self.rows = HSAC // self.n_blk
        self.drows = HDYN // self.n_blk
        self.mat = 64 // self.n_dp
        self.sml = 32 // self.n_dp
        self.chunks = (self.mat, self.mat + self.sml, self.mat)
        groups = [(name, g) for name in ("core sum", "plane sum") for g in range(3)]
        groups += [("line sum", g) for g in range(4)]
        common = ["hidden", "hidden on", "lists", "own", "line", "plane", "dyn h", "dyn m", "small", "small on"]
        common += groups
        kinds = [(name, kind) for name in ("pack", "x") for kind in ("own", "on")]
        tiles = [(name, k) for name in ("tiles", "tiles on") for k in range(3)]
        sent = common + tiles + kinds
        self.sent = {name: at for at, name in enumerate(sent)}
        self.departures = len(sent)
        self.here, self.arrivals = {}, 0
        tiles += [("pack", "sibling"), ("x", "sibling")]
        for name in common + tiles:
            self.here[name] = self.arrivals
            self.arrivals += 1
        for name in ("pack", "x"):
            self.here[name, "like"] = self.arrivals
            self.arrivals += MEMBERS


OPERANDS = 23
FIRST, SECOND = 3, 16


def main_kernel(lay, *refs):
    n_in = OPERANDS
    sources, held = refs[:n_in], refs[n_in : 2 * n_in]
    (
        sac_h, requests, member, replay, live, model, noise, biases, targ_in, crit_in, act_in, targ_bias,
        targ_hidden, crit_out, targ_out, act_out, dyn_h, dyn_m, crit_out_m, crit_out_v, sac_m, dyn_in, dyn_out,
    ) = held
    loads = refs[2 * n_in]
    refs = refs[2 * n_in + 1 :]
    (
        sac_g, sac_x, dyn_x, dyn_s, small, count, crit_rows,
        wg, lists, asked, dhg, dmg, bk, xs, nz, ys, ahead, w1f, w1t, w1n, w2t, w2h, heads, head_t, head_f,
        rowbuf, wide, headcol, acc_h, acc_w, acc_c, acc_a, acc_m, acc_l, grid_0, grid_1, grid_2, core_0, core_1,
        core_2, from_0, from_1, from_2, zr_0, zr_1, zr_2, zf_0, zf_1, zf_2, sum_0, sum_1, sum_2, mg, mat, dcols, dacc_h, dacc_w, dacc_o, dacc_m, dacc_b, dacc_l, xt, dmat,
        dpack, drow_x, bias, dhead, dhead_t, *rest,
    ) = refs
    send, recv = rest
    sent, here_at = lay.sent, lay.here
    grids, cores, froms = (grid_0, grid_1, grid_2), (core_0, core_1, core_2), (from_0, from_1, from_2)
    zrs, zfs, totals = (zr_0, zr_1, zr_2), (zf_0, zf_1, zf_2), (sum_0, sum_1, sum_2)
    n_dp, n_blk = lay.n_dp, lay.n_blk
    me = lax.axis_index("dp")
    z = lax.axis_index("blk")
    core, like = lax.rem(me, 2), me // 2
    sibling = me + 1 - 2 * core
    is_dyn = me < MEMBERS
    dyn_e = jnp.minimum(me, MEMBERS - 1)

    def on_plane(src, dst, ssem, rsem, peer):
        return pltpu.make_async_remote_copy(
            src_ref=src, dst_ref=dst, send_sem=ssem, recv_sem=rsem,
            device_id={"dp": peer}, device_id_type=MESH,
        )

    def on_line(src, dst, ssem, rsem, peer):
        return pltpu.make_async_remote_copy(
            src_ref=src, dst_ref=dst, send_sem=ssem, recv_sem=rsem,
            device_id={"blk": peer}, device_id_type=MESH,
        )

    def over(number, body):
        if number <= 8:
            for off in range(1, number):
                body(off)
        else:
            pl.loop(1, number)(body)

    def plane_peers(body):
        over(n_dp, lambda off: body(lax.rem(me + off, n_dp)))

    def like_peers(body):
        over(n_dp // 2, lambda off: body(lax.rem(me + 2 * off, n_dp)))

    def line_peers(body):
        over(n_blk, lambda off: body(lax.rem(z + off, n_blk)))

    def has_sent(view, name):
        at = send.at[sent[name]]
        on_plane(view, view, at, at, sibling).wait_send()

    def has_come(view, name):
        at = recv.at[here_at[name]]
        on_plane(view, view, at, at, sibling).wait_recv()

    copies = [
        pltpu.make_async_copy(src, dst, loads.at[at]) for at, (src, dst) in enumerate(zip(sources, held))
    ]

    def arrived(begin, end):
        for copy in copies[begin:end]:
            copy.wait()

    barrier = pltpu.get_barrier_semaphore()
    plane_peers(lambda peer: pl.semaphore_signal(barrier, inc=1, device_id={"dp": peer}, device_id_type=MESH))
    line_peers(lambda peer: pl.semaphore_signal(barrier, inc=1, device_id={"blk": peer}, device_id_type=MESH))
    for copy in copies:
        copy.start()
    arrived(0, FIRST)
    wg[0] = sac_h[...].astype(BF16)
    lists[0] = requests[...]
    lists[1] = member[...]
    pl.semaphore_wait(barrier, n_dp - 1 + n_blk - 1)

    half_rows = pl.ds(pl.multiple_of(core * (lay.rows // 2), lay.rows // 2), lay.rows // 2)

    def slot_from(owner, at):
        return lax.rem(owner - at + n_blk, n_blk)

    def hidden_copy(peer):
        src = wg.at[0, :, half_rows]
        dst = wg.at[slot_from(z, peer), :, half_rows]
        return on_line(src, dst, send.at[sent["hidden"]], recv.at[here_at["hidden"]], peer)

    def hidden_on():
        view = wg.at[pl.ds(1, n_blk - 1), :, half_rows]
        return on_plane(view, view, send.at[sent["hidden on"]], recv.at[here_at["hidden on"]], sibling)

    def list_copy(peer):
        return on_plane(lists, asked.at[me], send.at[sent["lists"]], recv.at[here_at["lists"]], peer)

    line_peers(lambda peer: hidden_copy(peer).start())
    plane_peers(lambda peer: list_copy(peer).start())
    asked[me] = lists[...]

    def dyn_h_copy(peer):
        return on_line(dyn_h.at[dyn_e], dhg.at[z], send.at[sent["dyn h"]], recv.at[here_at["dyn h"]], peer)

    def dyn_m_copy(peer):
        return on_line(dyn_m.at[dyn_e], dmg.at[z], send.at[sent["dyn m"]], recv.at[here_at["dyn m"]], peer)

    arrived(FIRST, SECOND)
    alive = live[...].astype(F32).reshape(1, lay.model)
    data = replay[...]
    sums = jnp.sum(data[0:24], axis=1, keepdims=True)
    squares = jnp.sum(data[0:24] * data[0:24], axis=1, keepdims=True)
    living = jnp.sum(alive, axis=1, keepdims=True)

    has_come(asked.at[pl.ds(0, n_dp - 1)], "lists")
    spread = (
        lax.rem(lax.broadcasted_iota(jnp.int32, (CAP, lay.real), 1), CAP)
        == lax.broadcasted_iota(jnp.int32, (CAP, lay.real), 0)
    ).astype(F32)
    here = (
        lax.broadcasted_iota(jnp.int32, (n_dp, lay.real), 1) // CAP
        == lax.broadcasted_iota(jnp.int32, (n_dp, lay.real), 0)
    )

    def in_lanes(which):
        values = asked[:, which, me, :].astype(F32)
        wide = lax.dot_general(
            values, spread, NN, precision=lax.Precision.HIGHEST, preferred_element_type=F32
        )
        return jnp.sum(jnp.where(here, wide, 0.0), axis=0, keepdims=True)

    slots = in_lanes(0)
    wanted = jnp.maximum(slots, 0.0).astype(jnp.int32)
    hot = (rows_of((lay.replay, lay.real)) == wanted).astype(BF16)
    padded = jnp.concatenate([data, jnp.zeros((48 - FEAT, lay.replay), F32)], 0)
    chosen = dot(jnp.concatenate(pieces(padded), 0), hot)
    chosen = chosen[0:48] + chosen[48:96] + chosen[96:144]
    mine = me * n_blk
    bk[mine, 0:FEAT, 0 : lay.real] = chosen[0:FEAT]
    bk[mine, 42:43, 0 : lay.real] = (slots >= 0.0).astype(F32)
    bk[mine, 43:44, 0 : lay.real] = in_lanes(1)
    bk[mine, 44:48, 0 : lay.real] = jnp.zeros((4, lay.real), F32)
    bk[mine, :, lay.real : lay.width] = jnp.zeros((48, lay.width - lay.real), F32)
    bk[mine, 0:24, lay.real : lay.real + 1] = sums
    bk[mine, 0:24, lay.real + 1 : lay.real + 2] = squares
    bk[mine, 24:25, lay.real : lay.real + 1] = living

    def slot_of(block):
        line = lax.rem(block, n_blk)
        return block - line + slot_from(line, z)

    def block_line(peer):
        dst = bk.at[me * n_blk + slot_from(z, peer)]
        return on_line(bk.at[mine], dst, send.at[sent["line"]], recv.at[here_at["line"]], peer)

    def block_own(peer):
        view = bk.at[mine]
        return on_plane(view, view, send.at[sent["own"]], recv.at[here_at["own"]], peer)

    def block_plane(peer):
        view = bk.at[pl.ds(mine + 1, n_blk - 1)]
        return on_plane(view, view, send.at[sent["plane"]], recv.at[here_at["plane"]], peer)

    plane_peers(lambda peer: block_own(peer).start())
    line_peers(lambda peer: block_line(peer).start())

    arrived(SECOND, n_in)
    crit_rows[0:2, :] = crit_out[...]
    crit_rows[2:4, :] = crit_out_m[...]
    crit_rows[4:6, :] = crit_out_v[...]
    crit_rows[6:8, :] = jnp.zeros((2, HSAC), F32)

    @pl.when(is_dyn)
    def _():
        line_peers(lambda peer: dyn_h_copy(peer).start())
        line_peers(lambda peer: dyn_m_copy(peer).start())

    bias[...] = biases[...].reshape(1, NB)
    xs[42:56, :] = jnp.zeros((14, lay.batch), F32)
    xs[0:FEAT, lay.real : lay.batch] = model[...]
    xs[42:43, lay.real : lay.batch] = alive
    nz[...] = jnp.zeros_like(nz)
    for which in range(2):
        nz[which, 1:7, :] = noise[:, which, :]
    firsts = [
        (targ_in[:, 0, :], targ_bias[0:1, 0:HSAC]),
        (targ_in[:, 1, :], targ_bias[1:2, 0:HSAC]),
        (crit_in[:, 0, :], bias[:, CB1 : CB1 + HSAC]),
        (crit_in[:, 1, :], bias[:, CB1 + HSAC : CB1 + 2 * HSAC]),
        (act_in[...], bias[:, AB1 : AB1 + HSAC]),
    ]
    w1f[...] = jnp.zeros_like(w1f)
    for net, (weights, offset) in enumerate(firsts):
        w1f[net, 0 : weights.shape[0], :] = rounded(weights)
        for at, piece in enumerate(pieces(offset)):
            w1f[net, IN + at : IN + at + 1, :] = piece.astype(F32)
        w1t[net] = (0.5 * w1f[net].T).astype(BF16)
    for k in range(2):
        w1n[k] = w1f[2 + k, 16:32, :].astype(BF16)
    for net in range(2):
        w2t[net] = (0.5 * rounded(targ_hidden[net])).T.astype(BF16)
    has_come(wg.at[pl.ds(0, n_blk - 1), :, half_rows], "hidden")
    hidden_on().start()

    rowbuf[...] = jnp.zeros_like(rowbuf)
    rowbuf[0:1, :] = targ_bias[0:1, HSAC : 2 * HSAC]
    rowbuf[1:2, :] = targ_bias[1:2, HSAC : 2 * HSAC]
    rowbuf[2:3, :] = bias[:, CB2 : CB2 + HSAC]
    rowbuf[3:4, :] = bias[:, CB2 + HSAC : CB2 + 2 * HSAC]
    rowbuf[4:5, :] = bias[:, AB2 : AB2 + HSAC]
    rowbuf[5:7, :] = rounded(crit_out[...])
    columns = 0.5 * rowbuf[...].T
    for at in range(7):
        wide[at] = jnp.broadcast_to(columns[:, at : at + 1], (HSAC, 128))
    rowbuf[...] = jnp.zeros_like(rowbuf)
    rowbuf[0:1, 1:7] = bias[:, AB3 : AB3 + ACT]
    rowbuf[0:1, 9:15] = bias[:, AB3 + ACT : AB3 + 2 * ACT]
    headcol[...] = rowbuf[:, 0:128].T
    head_f[...] = jnp.zeros_like(head_f)
    for k in range(2):
        head_f[0:1, :] = targ_out[k : k + 1, :]
        heads[k] = head_f[...].astype(BF16)
        head_f[0:1, :] = crit_out[k : k + 1, :]
        heads[2 + k] = head_f[...].astype(BF16)
    head_f[0:1, :] = jnp.zeros((1, HSAC), F32)
    head_f[1:7, :] = act_out[0:ACT, :]
    head_f[9:15, :] = act_out[ACT : 2 * ACT, :]
    heads[4] = head_f[...].astype(BF16)
    head_t[...] = (0.5 * rounded(head_f[...])).T.astype(BF16)
    for ref in (acc_h, acc_w, acc_c, acc_a, acc_m, acc_l):
        ref[...] = jnp.zeros_like(ref)

    has_come(wg.at[pl.ds(0, n_blk - 1), :, half_rows], "hidden on")
    for k in range(3):
        for block in range(n_blk):
            w2h[k, block * lay.rows : (block + 1) * lay.rows, :] = (
                0.5 * wg[slot_from(block, z), k].astype(F32)
            ).astype(BF16)
        w2t[2 + k] = w2h[k].astype(F32).T.astype(BF16)

    log_alpha = bias[:, LOGA : LOGA + 1]
    alpha = jnp.exp(log_alpha)
    last = [
        targ_bias[0:1, 2 * HSAC : 2 * HSAC + 1],
        targ_bias[1:2, 2 * HSAC : 2 * HSAC + 1],
        bias[:, CB3 : CB3 + 1],
        bias[:, CB3 + 1 : CB3 + 2],
    ]
    critic_tiles = lay.batch // CRITIC_TILE
    actor_tiles = lay.batch // ACTOR_TILE

    def act_rows(width):
        row8 = rows_of((8, width))
        return jnp.logical_and(row8 >= 1, row8 < 1 + ACT)

    def place_of(step, width):
        return pl.ds(pl.multiple_of(lax.rem(step + 1, lay.batch // width) * width, width), width)

    def ones16(width):
        return jnp.ones((16, width), BF16)

    def framed(first_row, used, where):
        row32 = rows_of((32, where.size))
        ones3 = jnp.logical_and(row32 >= IN, row32 < IN + 3).astype(F32)
        return jnp.where(row32 < used, xs[first_row : first_row + 32, where], ones3)

    def hidden(inputs, net):
        first, slope1 = gated(dot(w1t[net], inputs))
        second, slope2 = gated(dot(w2t[net], first), wide[net])
        return first, slope1, second, slope2

    def policy(inputs, which, where):
        first, slope1, second, slope2 = hidden(inputs, 4)
        out = dot(heads[4], second) + headcol[0:16, 0:1]
        bent = jnp.tanh(out[8:16])
        log_scale = -5.0 + 3.5 * (bent + 1.0)
        draw = nz[which, :, where]
        moved = jnp.exp(log_scale) * draw
        latent = out[0:8] + moved
        terms = (
            -0.5 * draw * draw
            - log_scale
            - 0.9189385
            - 2.0 * (0.6931472 - latent - softplus(-2.0 * latent))
        )
        used = act_rows(where.size)
        log_prob = jnp.sum(jnp.where(used, terms, 0.0), axis=0, keepdims=True)
        action = jnp.where(used, jnp.tanh(latent), 0.0)
        return action, log_prob, bent, moved, (first, slope1, second, slope2)

    def with_action(inputs, action):
        middle_rows = jnp.where(act_rows(action.shape[1]), action, inputs[16:24])
        return jnp.concatenate([inputs[0:16], middle_rows, inputs[24:32]], 0).astype(BF16)

    def critic(inputs, net):
        kept = hidden(inputs, net)
        value = dot(heads[net], kept[2])[0:1] + last[net]
        return value, kept

    def add_hidden(k, first, grad):
        acc_h[k] += dot(jnp.concatenate([first, ones16(grad.shape[1])], 0), grad, NT)

    has_come(bk.at[pl.ds(0, n_blk - 1)], "line")
    plane_peers(lambda peer: block_plane(peer).start())

    def critic_pass(k, now_in, where, target):
        weight = xs[42:43, where]
        value, (c1, dc1, c2, dc2) = critic(now_in, 2 + k)
        miss = value - target
        g3 = rounded(weight * miss)
        g3_rows = jnp.where(rows_of((16, CRITIC_TILE)) == 0, g3, 0.0).astype(BF16)
        acc_c[k] += dot(g3_rows, c2, NT)
        acc_m[:, 16 + 16 * k : 32 + 16 * k] += dot(ones16(CRITIC_TILE), g3_rows, NT)
        g2 = outer_sloped(wide[5 + k], g3, dc2)
        add_hidden(k, c1, g2)
        g1 = sloped(dot(w2h[k], g2), dc1)
        acc_w[k] += dot(now_in, g1, NT)
        acc_l[0:1, 0:CRITIC_TILE] += weight * (0.5 * miss * miss)

    def put_matrix(k):
        for chunk in range(n_dp):
            tile = chunk * lay.mat
            side, row = tile // 32, tile % 32
            grids[k][chunk % 2, chunk // 2, 0 : lay.mat] = acc_h[
                k, row * 8 : (row + lay.mat) * 8, side * 128 : (side + 1) * 128
            ].reshape(lay.mat, 8, 128)

    def put(row, value):
        for at in range(value.shape[0] // 8):
            for side in range(value.shape[1] // 128):
                tile = side * (R_SMALL // 8) + row // 8 + at
                chunk = tile // lay.sml
                grid_1[chunk % 2, chunk // 2, lay.mat + tile % lay.sml] = value[
                    at * 8 : at * 8 + 8, side * 128 : (side + 1) * 128
                ]

    def core_sum(group):
        name = ("core sum", group)
        return on_plane(
            grids[group].at[1 - core], cores[group], send.at[sent[name]], recv.at[here_at[name]], sibling
        )

    def plane_sum(group, peer):
        name = ("plane sum", group)
        return on_plane(
            cores[group].at[peer // 2], froms[group].at[like], send.at[sent[name]], recv.at[here_at[name]], peer
        )

    def fold_core(group):
        core_sum(group).wait_recv()
        cores[group][...] += grids[group][core]
        like_peers(lambda peer: plane_sum(group, peer).start())

    def line_part(part):
        return (1, pl.ds(lay.mat, lay.sml)) if part == 3 else (part, pl.ds(0, lay.mat))

    def line_sum(part, peer):
        group, tiles = line_part(part)
        name = ("line sum", part)
        src, dst = zfs[group].at[tiles], zrs[group].at[z, tiles]
        return on_line(src, dst, send.at[sent[name]], recv.at[here_at[name]], peer)

    def line_bytes(part):
        group, tiles = line_part(part)
        return zrs[group].at[pl.ds(0, n_blk - 1), tiles]

    first_tile = me * lay.mat
    side = first_tile // 32
    row_tile = lax.rem(first_tile, 32)
    keeper_z = row_tile * 8 // lay.rows
    local_tile = row_tile - keeper_z * (lay.rows // 8)

    def fold_plane(group):
        has_come(froms[group].at[pl.ds(0, lay.half - 1)], ("plane sum", group))
        froms[group][like] = cores[group][like]
        whole = froms[group][0]
        for at in range(1, lay.half):
            whole = whole + froms[group][at]
        zfs[group][...] = whole

        @pl.when(z == keeper_z)
        def _():
            held_rows = pl.ds(pl.multiple_of(local_tile * 8, 8), lay.mat * 8)
            held_lanes = pl.ds(pl.multiple_of(side * 128, 128), 128)
            old = sac_m[group, held_rows, held_lanes].reshape(lay.mat, 8, 128)
            zfs[group][0 : lay.mat] += (MOMENTUM * count[0:1, 0:1]).reshape(1, 1, 1) * old

        for part in (1, 3) if group == 1 else (group,):
            line_peers(lambda peer: line_sum(part, peer).start())

    def tile_copy(k, peer):
        name = ("tiles", k)
        src = totals[k].at[pl.ds(0, lay.mat)]
        return on_plane(src, mg.at[k, core, like], send.at[sent[name]], recv.at[here_at[name]], peer)

    def tiles_on(k):
        name = ("tiles on", k)
        view = mg.at[k, core]
        return on_plane(view, view, send.at[sent[name]], recv.at[here_at[name]], sibling)

    small_at = (core * lay.half + like) * lay.sml

    def small_copy(peer):
        return on_plane(
            sum_1.at[pl.ds(lay.mat, lay.sml)], small.at[pl.ds(small_at, lay.sml)],
            send.at[sent["small"]], recv.at[here_at["small"]], peer,
        )

    def small_on():
        view = small.at[pl.ds(core * lay.half * lay.sml, lay.half * lay.sml)]
        return on_plane(view, view, send.at[sent["small on"]], recv.at[here_at["small on"]], sibling)

    def fold_end(part):
        group, tiles = line_part(part)
        has_come(line_bytes(part), ("line sum", part))
        zrs[group][z, tiles] = zfs[group][tiles]
        whole = zrs[group][0, tiles]
        for block in range(1, n_blk):
            whole = whole + zrs[group][block, tiles]
        totals[group][tiles] = whole
        if part == 3:
            like_peers(lambda peer: small_copy(peer).start())
            small[pl.ds(small_at, lay.sml)] = whole
        else:
            like_peers(lambda peer: tile_copy(part, peer).start())
            mg[part, core, like] = whole

    def chain(group):
        def end():
            for part in (1, 3) if group == 1 else (group,):
                fold_end(part)

        def turn():
            has_come(mg.at[group, 0, pl.ds(0, lay.half - 1)], ("tiles", group))
            tiles_on(group).start()
            if group == 1:
                has_come(small.at[pl.ds(0, (lay.half - 1) * lay.sml)], "small")
                small_on().start()

        return [
            lambda: core_sum(group).start(),
            lambda: fold_core(group),
            lambda: fold_plane(group),
            end,
            turn,
        ]

    chains = [chain(group) for group in range(3)]
    per = DYN_TILE // lay.real
    dyn_tiles = lay.n_dev // per

    def take(slots, step):
        for at, events in slots.items():
            @pl.when(step == at)
            def _():
                for event in events:
                    event()

    @pl.loop(0, actor_tiles)
    def _(step):
        @pl.when(step == actor_tiles - 1)
        def _():
            has_come(bk.at[pl.ds(0, n_dp - 1)], "own")
            lanes = lax.broadcasted_iota(jnp.int32, (48, lay.width), 1) // CAP

            def gather(owner, total):
                turned = pltpu.roll(
                    bk[owner * n_blk], lax.rem((owner - me) * CAP + lay.width, lay.width), axis=1
                )
                return jnp.where(lanes == owner, turned, total)

            own = lax.fori_loop(0, n_dp, gather, jnp.zeros((48, lay.width), F32))
            xs[0:48, 0 : lay.real] = own[:, 0 : lay.real]

        where = place_of(step, ACTOR_TILE)
        now_f = framed(0, IN, where)
        now_in = now_f.astype(BF16)
        weight = xs[42:43, where]
        next_action, next_prob, _, _, _ = policy(framed(24, OBS, where).astype(BF16), 1, where)
        ahead[0:8, where] = next_action
        ys[1:2, where] = next_prob
        action, log_prob, bent, moved, (a1, da1, a2, da2) = policy(now_in, 0, where)
        judged_in = with_action(now_f, action)
        loss = alpha * log_prob - log_alpha * (log_prob + TARGET_ENTROPY)
        grad_action = jnp.zeros((8, ACTOR_TILE), F32)
        used = act_rows(ACTOR_TILE)
        for k in range(2):
            judged, (_, df1, _, df2) = critic(judged_in, 2 + k)
            loss -= 0.5 * judged
            g2 = outer_sloped(wide[5 + k], -0.5 * weight, df2)
            g1 = sloped(dot(w2h[k], g2), df1)
            grad_action += dot(w1n[k], g1)[0:8]
        grad_latent = 2.0 * alpha * weight * action + grad_action * (1.0 - action * action)
        grad_scale = grad_latent * moved - alpha * weight
        grad_bent = grad_scale * 3.5 * (1.0 - bent * bent)
        g3 = jnp.concatenate(
            [jnp.where(used, grad_latent, 0.0), jnp.where(used, grad_bent, 0.0)], 0
        ).astype(BF16)
        acc_a[...] += dot(g3, a2, NT)
        acc_m[:, 0:16] += dot(ones16(ACTOR_TILE), g3, NT)
        g2 = sloped(dot(head_t[...], g3), da2)
        add_hidden(2, a1, g2)
        g1 = sloped(dot(w2h[2], g2), da1)
        acc_w[2] += dot(now_in, g1, NT)
        acc_l[1:2, 0:ACTOR_TILE] += weight * loss
        acc_l[2:3, 0:ACTOR_TILE] += weight * (log_prob + TARGET_ENTROPY)

    put_matrix(2)
    chains[2][0]()

    @pl.loop(0, critic_tiles)
    def _(step):
        if critic_tiles > 1:
            take({1: [chains[2][1]]}, step)

        where = place_of(step, CRITIC_TILE)
        now_in = framed(0, IN, where).astype(BF16)
        reward = xs[23:24, where]
        done = xs[41:42, where]
        aim_in = with_action(framed(24, OBS, where), ahead[0:8, where])
        next_prob = ys[1:2, where]
        aim = jnp.minimum(critic(aim_in, 0)[0], critic(aim_in, 1)[0])
        target = reward + DISCOUNT * (1.0 - done) * (aim - alpha * next_prob)
        ys[0:1, where] = target
        critic_pass(0, now_in, where, target)

    put_matrix(0)
    chains[0][0]()
    if critic_tiles == 1:
        chains[2][1]()

    has_come(bk.at[pl.ds(0, (n_dp - 1) * (n_blk - 1))], "plane")
    lane0 = lay.real // 128 * 128

    def add_block(at, carry):
        sides, fills = carry
        slot = slot_of(at)
        return sides + bk[slot, 0:32, lane0 : lane0 + 128], fills + bk[slot, 40:48, 0 : lay.real]

    sides, fills = lax.fori_loop(
        0, lay.n_dev, add_block, (jnp.zeros((32, 128), F32), jnp.zeros((8, lay.real), F32))
    )
    at = lay.real - lane0
    rows_all = float(lay.replay * lay.n_dev)
    centre = sides[0:24, at : at + 1] / rows_all
    scale = lax.rsqrt(sides[0:24, at + 1 : at + 2] / rows_all - centre * centre + 1e-6)
    total = sides[24:25, at : at + 1] + jnp.sum(fills[2:3, :], axis=1, keepdims=True)
    count[...] = jnp.broadcast_to(total, (8, 128))

    @pl.loop(0, critic_tiles)
    def _(step):
        take({critic_tiles - 1: [chains[0][1], chains[2][2]]}, step)
        where = place_of(step, CRITIC_TILE)
        critic_pass(1, framed(0, IN, where).astype(BF16), where, ys[0:1, where])

    put_matrix(1)
    for k in range(3):
        put(R_IN + 24 * k, acc_w[k, 0:24, :])
    put(R_HEAD, acc_a[...])
    rowbuf[0:1, :] = acc_c[0, 0:1, :]
    rowbuf[1:2, :] = acc_c[1, 0:1, :]
    for k in range(3):
        rowbuf[2 + k : 3 + k, :] = acc_h[k, HSAC : HSAC + 1, :]
    put(R_OUT, rowbuf[...])
    folded = jnp.sum(acc_l[...], axis=1, keepdims=True)
    rowbuf[...] = jnp.zeros_like(rowbuf)
    rowbuf[0:1, 0:48] = acc_m[0:1, :]
    rowbuf[0:1, 64:65] = folded[0:1] + folded[1:2]
    rowbuf[0:1, 65:66] = folded[2:3]
    put(R_MISC, rowbuf[...])
    put(R_MISC + 8, jnp.zeros((R_SMALL - R_MISC - 8, HSAC), F32))
    chains[1][0]()

    def dyn_bias(start, width):
        row = jnp.zeros((1, width), F32)
        for e in range(MEMBERS):
            row = jnp.where(me == e, bias[:, start + width * e : start + width * (e + 1)], row)
        return row

    @pl.when(is_dyn)
    def _():
        w1f[0] = jnp.zeros((32, HSAC), F32)
        w1f[0, 0:IN, 0:HDYN] = rounded(dyn_in[dyn_e])
        for at, piece in enumerate(pieces(dyn_bias(DB1, HDYN))):
            w1f[0, IN + at : IN + at + 1, 0:HDYN] = piece.astype(F32)
        w1t[0] = (0.5 * w1f[0].T).astype(BF16)
        rowbuf[...] = jnp.zeros_like(rowbuf)
        rowbuf[0:1, 0:HDYN] = dyn_bias(DB2, HDYN)
        head_row = dyn_bias(DB3, DOUT)
        rowbuf[1:2, 0:HALF] = head_row[:, 0:HALF]
        rowbuf[1:2, 24 : 24 + HALF] = head_row[:, HALF:DOUT]
        rowbuf[2:3, 0:HALF] = bias[:, MAXLV : MAXLV + HALF]
        rowbuf[3:4, 0:HALF] = bias[:, MINLV : MINLV + HALF]
        dcols[...] = rowbuf[...].T
        wide[0] = jnp.broadcast_to(0.5 * dcols[:, 0:1], (HSAC, 128))
        dpack[...] = jnp.zeros_like(dpack)
        dpack[0:HALF, 0:HDYN] = dyn_out[dyn_e, 0:HALF, :]
        dpack[24 : 24 + HALF, 0:HDYN] = dyn_out[dyn_e, HALF:DOUT, :]
        dhead[...] = dpack[0:48, :].astype(BF16)
        dhead_t[...] = (0.5 * rounded(dpack[0:48, :])).T.astype(BF16)
        dpack[...] = jnp.zeros_like(dpack)

        has_come(dhg.at[pl.ds(0, n_blk - 1)], "dyn h")
        has_come(dmg.at[pl.ds(0, n_blk - 1)], "dyn m")
        dhg[z] = dyn_h[dyn_e]
        dmg[z] = dyn_m[dyn_e]
        dmat[...] = jnp.zeros_like(dmat)
        for block in range(n_blk):
            dmat[block * lay.drows : (block + 1) * lay.drows, 0:HDYN] = 0.5 * rounded(dhg[block])
        w2h[0] = dmat[...].astype(BF16)
        w2t[0] = dmat[...].T.astype(BF16)
        for ref in (dacc_h, dacc_w, dacc_o, dacc_m, dacc_b, dacc_l):
            ref[...] = jnp.zeros_like(ref)

    in_dyn = {}
    for at, event in (
        (1, chains[0][2]), (1, chains[1][1]), (2, chains[2][3]), (dyn_tiles - 1, chains[1][2]),
    ):
        in_dyn.setdefault(min(at, dyn_tiles - 1), []).append(event)

    @pl.loop(0, dyn_tiles)
    def _(tile):
        take(in_dyn, tile)

        @pl.when(is_dyn)
        def _():
            for at in range(per):
                slot = slot_of(tile * per + at)
                xt[:, at * lay.real : (at + 1) * lay.real] = bk[slot, :, 0 : lay.real]
            now = xt[0:24, :]
            later = xt[24:48, :]
            row24 = rows_of((24, DYN_TILE))
            scaled = jnp.where(row24 < IN, (now - centre) * scale, 1.0)
            inputs = jnp.concatenate([scaled, (rows_of((8, DYN_TILE)) < 2).astype(F32)], 0).astype(BF16)
            first, slope1 = gated(dot(w1t[0], inputs))
            second, slope2 = gated(dot(w2t[0], first), wide[0])
            out = dot(dhead[...], second) + dcols[0:48, 1:2]
            used = row24 < HALF
            upper = dcols[0:24, 2:3]
            lower = dcols[0:24, 3:4]
            gap1 = upper - out[24:48]
            gap2 = upper - softplus(gap1) - lower
            log_var = lower + softplus(gap2)
            error = out[0:24] - jnp.where(row24 == OBS, now[23:24], later - now)
            inverse = jnp.exp(-log_var)
            weight = xt[42:43, :] * (xt[43:44, :] == me.astype(F32)).astype(F32)
            spread_term = error * error * inverse
            nll = jnp.sum(jnp.where(used, spread_term + log_var, 0.0), axis=0, keepdims=True)
            dacc_l[0:1, :] += weight * nll
            grad_mu = 2.0 * weight * error * inverse
            grad_lv = weight * (1.0 - spread_term)
            open1 = sigmoid(gap1)
            open2 = sigmoid(gap2)
            grad_lv1 = grad_lv * open2
            dacc_b[0] += jnp.where(used, grad_lv1 * (1.0 - open1), 0.0)
            dacc_b[1] += jnp.where(used, grad_lv * (1.0 - open2), 0.0)
            g3 = jnp.concatenate(
                [jnp.where(used, grad_mu, 0.0), jnp.where(used, grad_lv1 * open1, 0.0)], 0
            ).astype(BF16)
            dacc_o[...] += dot(g3, second, NT)
            dacc_m[...] += dot(ones16(DYN_TILE), g3, NT)
            g2 = sloped(dot(dhead_t[...], g3), slope2)
            dacc_h[...] += dot(jnp.concatenate([first, ones16(DYN_TILE)], 0), g2, NT)
            g1 = sloped(dot(w2h[0], g2), slope1)
            dacc_w[...] += dot(inputs, g1, NT)

    out_of = {"pack": dyn_s, "x": dyn_x}

    def member_copy(name, src, owner, kind, sem, peer):
        return on_plane(src, out_of[name].at[owner], send.at[sent[name, kind]], recv.at[sem], peer)

    def give(name, src):
        like_peers(
            lambda peer: member_copy(name, src, dyn_e, "own", here_at[name, "like"] + dyn_e, peer).start()
        )
        member_copy(name, src, dyn_e, "own", here_at[name, "sibling"], sibling).start()

    def hand_on(name):
        def body(peer):
            @pl.when(peer < MEMBERS)
            def _():
                owner = jnp.minimum(peer, MEMBERS - 1)
                view = out_of[name].at[owner]
                member_copy(name, view, owner, "on", here_at[name, "like"] + owner, sibling).wait_recv()
                member_copy(name, view, owner, "on", here_at[name, "sibling"], sibling).start()

        like_peers(body)

    even, odd = (MEMBERS + 1) // 2, MEMBERS // 2
    handed = even - core * (even - odd) - jnp.where(is_dyn, 1, 0)

    def from_sibling(name):
        for side, number in ((0, odd), (1, even)):
            @pl.when(core == side)
            def _():
                has_come(out_of[name].at[pl.ds(0, number)], (name, "sibling"))

    def gave(name):
        @pl.when(is_dyn)
        def _():
            for begin in range(0, n_dp // 2, MEMBERS):
                number = min(MEMBERS, n_dp // 2 - begin)
                has_sent(out_of[name].at[pl.ds(0, number)], (name, "own"))

        for number in (even, even - 1, even - 2):
            @pl.when(handed == number)
            def _():
                has_sent(out_of[name].at[pl.ds(0, number)], (name, "on"))

    def line_rows(ref):
        rows = ref[0 : lay.drows, 0:HDYN]
        for block in range(1, n_blk):
            rows = jnp.where(z == block, ref[block * lay.drows : (block + 1) * lay.drows, 0:HDYN], rows)
        return rows

    mine_rows = pl.ds(pl.multiple_of(z * lay.rows, lay.rows), lay.rows)

    def take_matrix(k):
        tiles_on(k).wait_recv()
        for chunk in range(n_dp):
            tile = chunk * lay.mat
            half, row = tile // 32, tile % 32
            at = slice(row * 8, (row + lay.mat) * 8)
            piece = mg[k, chunk % 2, chunk // 2].reshape(lay.mat * 8, 128)
            mat[k, at, half * 128 : (half + 1) * 128] = piece / total
        normalise(mat.at[k])

    chains[2][4]()
    chains[0][3]()

    @pl.when(is_dyn)
    def _():
        dpack[D_IN : D_IN + 24, :] = dacc_w[0:24, :]
        dpack[D_OUT : D_OUT + HALF, :] = dacc_o[0:HALF, :]
        dpack[D_OUT + HALF : D_OUT + DOUT, :] = dacc_o[24 : 24 + HALF, :]
        dpack[D_B2 : D_B2 + 1, :] = dacc_h[HSAC : HSAC + 1, :]
        dpack[D_B3 : D_B3 + 1, 0:48] = dacc_m[0:1, :]
        lanes = lax.broadcasted_iota(jnp.int32, (24, 128), 1)
        bound = jnp.where(
            lanes == 0,
            jnp.sum(dacc_b[0], axis=1, keepdims=True),
            jnp.where(lanes == 1, jnp.sum(dacc_b[1], axis=1, keepdims=True), 0.0),
        )
        dpack[D_UP : D_UP + 2, 0:24] = bound.T[0:2, :]
        dpack[D_LOSS : D_LOSS + 1, 0:128] = jnp.broadcast_to(
            jnp.sum(dacc_l[0:1, :], axis=1, keepdims=True), (1, 128)
        )
        dpack[D_HID : D_HID + lay.drows, 0:HDYN] = line_rows(dacc_h)
        dyn_s[dyn_e] = dpack[...]
        give("pack", dpack)
        dmat[...] = jnp.zeros_like(dmat)
        for block in range(n_blk):
            at = slice(block * lay.drows, (block + 1) * lay.drows)
            dmat[at, 0:HDYN] = MOMENTUM * dmg[block] + dacc_h[at, 0:HDYN] / total
        normalise(dmat)

    def sum_end(step):
        @pl.when(step == 3)
        def _():
            chains[0][4]()
            chains[1][3]()

    take_matrix(2)

    @pl.when(is_dyn)
    def _():
        schulz([dmat, mat.at[2]], NS_ITERS, sum_end)
        rows = line_rows(dmat)
        drow_x[...] = rows
        dyn_x[dyn_e] = rows
        give("x", drow_x)

    @pl.when(jnp.logical_not(is_dyn))
    def _():
        schulz([mat.at[2]], NS_ITERS, sum_end)

    def sent_early():
        has_sent(wg.at[pl.ds(0, n_blk - 1), :, half_rows], "hidden")
        has_sent(wg.at[pl.ds(0, n_blk - 1), :, half_rows], "hidden on")
        has_sent(asked.at[pl.ds(0, n_dp - 1)], "lists")
        has_sent(bk.at[pl.ds(0, n_dp - 1)], "own")
        has_sent(bk.at[pl.ds(0, n_blk - 1)], "line")
        has_sent(bk.at[pl.ds(0, (n_dp - 1) * (n_blk - 1))], "plane")

        @pl.when(is_dyn)
        def _():
            has_sent(dhg.at[pl.ds(0, n_blk - 1)], "dyn h")
            has_sent(dmg.at[pl.ds(0, n_blk - 1)], "dyn m")

        for group in range(3):
            core_sum(group).wait_send()
            has_sent(froms[group].at[pl.ds(0, lay.half - 1)], ("plane sum", group))
        for part in range(4):
            has_sent(line_bytes(part), ("line sum", part))

    def pass_on(step):
        pl.when(step == 2)(functools.partial(hand_on, "pack"))
        pl.when(step == NS_ITERS - 1)(functools.partial(hand_on, "x"))

    sent_early()
    chains[1][4]()
    for k in range(2):
        take_matrix(k)
    schulz([mat.at[0], mat.at[1]], NS_ITERS, pass_on)
    for k in range(3):
        sac_x[k] = mat[k, mine_rows, :]
        for half in range(2):
            for piece in range(lay.rows // 8 // lay.mat):
                chunk = (half * 32 + z * (lay.rows // 8)) // lay.mat + piece
                kept = mg[k, lax.rem(chunk, 2), chunk // 2]
                sac_g[half, k, piece * lay.mat : (piece + 1) * lay.mat] = kept

    small_on().wait_recv()
    from_sibling("pack")
    from_sibling("x")

    has_sent(small.at[pl.ds(0, (lay.half - 1) * lay.sml)], "small")
    small_on().wait_send()
    gave("pack")
    gave("x")

    for k in range(3):
        has_sent(mg.at[k, 0, pl.ds(0, lay.half - 1)], ("tiles", k))
        tiles_on(k).wait_send()


def ordered(lay, n_in, n_out, *refs):
    inputs, outputs, scratch = refs[:n_in], refs[n_in : n_in + n_out], refs[n_in + n_out :]
    main_kernel(lay, *inputs, *scratch[: n_in + 1], *outputs, *scratch[n_in + 1 :])


def adamw(weights, first, second, gradient):
    first = BETA_FIRST * first + (1.0 - BETA_FIRST) * gradient
    second = BETA_SECOND * second + (1.0 - BETA_SECOND) * gradient * gradient
    first_hat = first / (1.0 - BETA_FIRST**STEP)
    second_hat = second / (1.0 - BETA_SECOND**STEP)
    step = first_hat / (jnp.sqrt(second_hat) + 1e-8) + ADAM_DECAY * weights
    return weights - ADAM_RATE * step, first, second


def update_kernel(lay, *refs):
    (
        sac_g, sac_x, dyn_x, dyn_s, small, count, crit_rows, sac_h, dyn_h, dyn_m,
        ci, ci_m, ci_v, ai, ai_m, ai_v, di, di_m, di_v, ao, ao_m, ao_v,
        do, do_m, do_v, bi, bi_m, bi_v,
        sac_new, sac_mom, dyn_new, dyn_mom, ci_n, ci_mn, ci_vn, ai_n, ai_mn, ai_vn, di_n, di_mn,
        di_vn, co_n, co_mn, co_vn, ao_n, ao_mn, ao_vn, do_n, do_mn, do_vn, bi_n, bi_mn, bi_vn,
        loss, counted, bg,
    ) = refs
    total = count[0:1, 0:1]
    for k in range(3):
        for side in range(2):
            tiles = sac_g[side, k].reshape(sac_mom.shape[1], 128)
            sac_mom[k, :, side * 128 : (side + 1) * 128] = tiles / total
    sac_new[...] = sac_h[...] * (1.0 - MUON_RATE * MUON_DECAY) - MUON_RATE * sac_x[...]
    dyn_rows = dyn_s[:, D_HID : D_HID + dyn_m.shape[1], 0:HDYN]
    dyn_mom[...] = MOMENTUM * dyn_m[...] + dyn_rows / total.reshape(1, 1, 1)
    dyn_new[...] = dyn_h[...] * (1.0 - MUON_RATE * MUON_DECAY) - MUON_RATE * dyn_x[...]

    def rows(row, number):
        def tile(at):
            chunk = at // lay.sml
            return small[(chunk % 2 * lay.half + chunk // 2) * lay.sml + at % lay.sml]

        sides = []
        for side in range(2):
            at = side * (R_SMALL // 8) + row // 8
            sides.append(jnp.concatenate([tile(at + more) for more in range(-(-number // 8))], 0))
        return jnp.concatenate(sides, 1)

    def store(outs, at, values):
        for out, value in zip(outs, values):
            out[at] = value

    outs = (ci_n, ci_mn, ci_vn)
    for k in range(2):
        at = (slice(None), k, slice(None))
        grad = rows(R_IN + 24 * k, 24)
        bg[:, CB1 + HSAC * k : CB1 + HSAC * (k + 1)] = grad[IN : IN + 1]
        store(outs, at, adamw(ci[at], ci_m[at], ci_v[at], grad[0:IN] / total))
    grad = rows(R_IN + 48, 24)
    bg[:, AB1 : AB1 + HSAC] = grad[IN : IN + 1]
    store((ai_n, ai_mn, ai_vn), ..., adamw(ai[...], ai_m[...], ai_v[...], grad[0:OBS] / total))
    grad = rows(R_HEAD, 16)
    for at, row in ((slice(0, ACT), slice(1, 1 + ACT)), (slice(ACT, 2 * ACT), slice(9, 9 + ACT))):
        store((ao_n, ao_mn, ao_vn), at, adamw(ao[at], ao_m[at], ao_v[at], grad[row] / total))
    grad = rows(R_OUT, 8)
    held = [crit_rows[2 * at : 2 * at + 2, :] for at in range(3)]
    store((co_n, co_mn, co_vn), ..., adamw(*held, grad[0:2] / total))
    bg[:, CB2 : CB2 + HSAC] = grad[2:3]
    bg[:, CB2 + HSAC : CB2 + 2 * HSAC] = grad[3:4]
    bg[:, AB2 : AB2 + HSAC] = grad[4:5]
    grad = rows(R_MISC, 8)
    bg[:, CB3 : CB3 + 1] = grad[0:1, 16:17]
    bg[:, CB3 + 1 : CB3 + 2] = grad[0:1, 32:33]
    bg[:, AB3 : AB3 + ACT] = grad[0:1, 1 : 1 + ACT]
    bg[:, AB3 + ACT : AB3 + 2 * ACT] = grad[0:1, 9 : 9 + ACT]
    bg[:, LOGA : LOGA + 1] = -grad[0:1, 65:66]
    total_loss = grad[0:1, 64:65]
    up = jnp.zeros((1, HALF), F32)
    low = jnp.zeros((1, HALF), F32)
    for e in range(MEMBERS):
        pack = dyn_s[e]
        total_loss = total_loss + pack[D_LOSS : D_LOSS + 1, 0:1]
        up = up + pack[D_UP : D_UP + 1, 0:HALF]
        low = low + pack[D_LOW : D_LOW + 1, 0:HALF]
        bg[:, DB1 + HDYN * e : DB1 + HDYN * (e + 1)] = pack[IN : IN + 1, 0:HDYN]
        bg[:, DB2 + HDYN * e : DB2 + HDYN * (e + 1)] = pack[D_B2 : D_B2 + 1, 0:HDYN]
        bg[:, DB3 + DOUT * e : DB3 + DOUT * e + HALF] = pack[D_B3 : D_B3 + 1, 0:HALF]
        bg[:, DB3 + DOUT * e + HALF : DB3 + DOUT * (e + 1)] = pack[D_B3 : D_B3 + 1, 24 : 24 + HALF]
        grad = pack[0:IN, 0:HDYN] / total
        store((di_n, di_mn, di_vn), e, adamw(di[e], di_m[e], di_v[e], grad))
        grad = pack[D_OUT : D_OUT + DOUT, 0:HDYN] / total
        store((do_n, do_mn, do_vn), e, adamw(do[e], do_m[e], do_v[e], grad))
    bg[:, MAXLV : MAXLV + HALF] = up
    bg[:, MINLV : MINLV + HALF] = low
    lane = lax.broadcasted_iota(jnp.int32, (1, NB), 1)
    bounds = jnp.where(
        jnp.logical_and(lane >= MAXLV, lane < MINLV),
        BOUND_WEIGHT,
        jnp.where(jnp.logical_and(lane >= MINLV, lane < LOGA), -BOUND_WEIGHT, 0.0),
    )
    grad = bg[...] / total + bounds
    flat = [ref[...].reshape(1, NB) for ref in (bi, bi_m, bi_v)]
    store((bi_n, bi_mn, bi_vn), ..., [value.reshape(NB) for value in adamw(*flat, grad)])
    loss[...] = total_loss
    counted[...] = total


def shards(
    lay, replay, model_rows, requests, member_of, model_live, noise, sac_hidden, sac_hidden_mom,
    dyn_hidden, dyn_hidden_mom, crit_in, crit_in_m, crit_in_v, act_in, act_in_m, act_in_v, dyn_in,
    dyn_in_m, dyn_in_v, crit_out, crit_out_m, crit_out_v, act_out, act_out_m, act_out_v, dyn_out,
    dyn_out_m, dyn_out_v, biases, biases_m, biases_v, targ_in, targ_hidden, targ_out, targ_bias,
):
    n_dp, n_blk = lay.n_dp, lay.n_blk
    spec = pl.BlockSpec(memory_space=pltpu.VMEM)

    def flip(value):
        return jnp.transpose(value, (1, 0, 2))

    def swap(value):
        return jnp.swapaxes(value, -1, -2)

    def kept(value):
        return pltpu.with_memory_space_constraint(value, pltpu.VMEM)

    inputs = (
        sac_hidden, requests, member_of, replay, model_live, model_rows, jnp.transpose(noise, (2, 0, 1)),
        biases, flip(targ_in), flip(crit_in), act_in, targ_bias, targ_hidden, crit_out, targ_out,
        swap(act_out), dyn_hidden, dyn_hidden_mom, crit_out_m, crit_out_v, sac_hidden_mom, dyn_in,
        swap(dyn_out),
    )
    shape = jax.ShapeDtypeStruct
    rows, drows = lay.rows, lay.drows
    out_shape = (
        pltpu.VMEM((2, 3, rows // 8, 8, 128), F32),
        pltpu.VMEM((3, rows, HSAC), F32),
        pltpu.VMEM((MEMBERS, drows, HDYN), F32),
        pltpu.VMEM((MEMBERS, D_ROWS, HSAC), F32),
        pltpu.VMEM((32, 8, 128), F32),
        pltpu.VMEM((8, 128), F32),
        pltpu.VMEM((8, HSAC), F32),
    )

    def vm(*dims, kind=F32):
        return pltpu.VMEM(dims, kind)

    scratch = [
        vm(n_blk, 3, rows, HSAC, kind=BF16),
        vm(2, n_dp, CAP, kind=jnp.int32),
        vm(n_dp, 2, n_dp, CAP, kind=jnp.int32),
        vm(n_blk, drows, HDYN),
        vm(n_blk, drows, HDYN),
        vm(lay.n_dev, 48, lay.width),
        vm(56, lay.batch),
        vm(2, 8, lay.batch),
        vm(8, lay.batch),
        vm(8, lay.batch),
        vm(5, 32, HSAC),
        vm(5, HSAC, 32, kind=BF16),
        vm(2, 16, HSAC, kind=BF16),
        vm(5, HSAC, HSAC, kind=BF16),
        vm(3, HSAC, HSAC, kind=BF16),
        vm(5, 16, HSAC, kind=BF16),
        vm(HSAC, 16, kind=BF16),
        vm(16, HSAC),
        vm(8, HSAC),
        vm(7, HSAC, 128),
        vm(128, 8),
        vm(3, HSAC + 16, HSAC),
        vm(3, 32, HSAC),
        vm(2, 16, HSAC),
        vm(16, HSAC),
        vm(16, 48),
        vm(8, max(CRITIC_TILE, ACTOR_TILE)),
        *[vm(2, lay.half, chunk, 8, 128) for chunk in lay.chunks],
        *[vm(lay.half, chunk, 8, 128) for chunk in lay.chunks],
        *[vm(lay.half, chunk, 8, 128) for chunk in lay.chunks],
        *[vm(n_blk, chunk, 8, 128) for chunk in lay.chunks],
        *[vm(chunk, 8, 128) for chunk in lay.chunks],
        *[vm(chunk, 8, 128) for chunk in lay.chunks],
        vm(3, 2, lay.half, lay.mat, 8, 128),
        vm(3, HSAC, HSAC),
        vm(HSAC, 8),
        vm(HSAC + 16, HSAC),
        vm(32, HSAC),
        vm(48, HSAC),
        vm(16, 48),
        vm(2, 24, DYN_TILE),
        vm(8, DYN_TILE),
        vm(48, DYN_TILE),
        vm(HSAC, HSAC),
        vm(D_ROWS, HSAC),
        vm(drows, HDYN),
        vm(1, NB),
        vm(48, HSAC, kind=BF16),
        vm(HSAC, 48, kind=BF16),
    ]
    scratch += [pltpu.SemaphoreType.DMA((lay.departures,)), pltpu.SemaphoreType.DMA((lay.arrivals,))]
    held = [pltpu.VMEM(value.shape, value.dtype) for value in inputs]
    held.append(pltpu.SemaphoreType.DMA((len(inputs),)))
    varying = 4 * (lay.n_dev * 48 * lay.width + 72 * lay.batch + 48 * lay.replay)
    gathered = pl.pallas_call(
        functools.partial(ordered, lay, len(inputs), len(out_shape)),
        out_shape=out_shape,
        in_specs=[pl.BlockSpec(memory_space=pl.ANY)] * len(inputs),
        out_specs=[spec] * len(out_shape),
        scratch_shapes=held + scratch,
        compiler_params=pltpu.CompilerParams(
            collective_id=0, has_side_effects=True, vmem_limit_bytes=26 * 2**20 + varying
        ),
        name="step",
    )(*[pltpu.with_memory_space_constraint(value, pltpu.HBM) for value in inputs])
    params = (
        sac_hidden, dyn_hidden, dyn_hidden_mom,
        flip(crit_in), flip(crit_in_m), flip(crit_in_v), act_in, act_in_m, act_in_v,
        dyn_in, dyn_in_m, dyn_in_v,
        swap(act_out), swap(act_out_m), swap(act_out_v),
        swap(dyn_out), swap(dyn_out_m), swap(dyn_out_v), biases, biases_m, biases_v,
    )
    new_shape = [shape(sac_hidden.shape, F32)] + [shape(value.shape, F32) for value in params[:12]]
    new_shape += [shape(crit_out.shape, F32)] * 3 + [shape(value.shape, F32) for value in params[12:]]
    new_shape += [shape((1, 1), F32)] * 2
    out = pl.pallas_call(
        functools.partial(update_kernel, lay),
        out_shape=tuple(new_shape),
        in_specs=[spec] * (len(gathered) + len(params)),
        out_specs=[spec] * len(new_shape),
        scratch_shapes=[vm(1, NB)],
        compiler_params=pltpu.CompilerParams(vmem_limit_bytes=16 * 2**20),
        name="update",
    )(*[kept(value) for value in gathered], *params)
    out = list(out)
    for at in (4, 5, 6):
        out[at] = flip(out[at])
    for at in (16, 17, 18, 19, 20, 21):
        out[at] = swap(out[at])
    for at in (25, 26):
        out[at] = out[at].reshape(())
    return tuple(out)


def solution(mesh):
    both = ("dp", "blk")
    sharded = (
        P(None, both), P(None, both), P(both, None), P(both, None), P(both), P(None, both, None),
    )
    hidden = (P(None, "blk", None),) * 4

    def step(replay, model_rows, *others):
        lay = Layout(mesh, replay.shape[1], model_rows.shape[1])
        return shards(lay, replay, model_rows, *others)

    return jax.shard_map(
        step,
        mesh=mesh,
        in_specs=sharded + hidden + (P(),) * 25,
        out_specs=hidden + (P(),) * 23,
        check_vma=False,
    )
```

```python
import functools

import jax
import jax.numpy as jnp
from jax import lax
from jax.experimental import pallas as pl
from jax.experimental.pallas import tpu as pltpu
from jax.sharding import PartitionSpec as P

OBS = 17
ACT = 6
IN = OBS + ACT
FEAT = 42
HDYN = 200
HSAC = 256
MEMBERS = 7
DOUT = 36
HALF = DOUT // 2
NB = 4639
NS_ITERS = 5
STEP = 10
CAP = 8
CRITIC_TILE = 640
ACTOR_TILE = 640
DYN_TILE = 512
ROWS = 32

DISCOUNT = 0.99
TARGET_ENTROPY = -6.0
BOUND_WEIGHT = 0.01
MOMENTUM = 0.95
MUON_RATE = 0.4
MUON_DECAY = 0.01
ADAM_RATE = 0.1
ADAM_DECAY = 0.01
BETA_FIRST = 0.9
BETA_SECOND = 0.999
COEF_LINEAR = 3.4445
COEF_CUBIC = -4.775
COEF_QUINTIC = 2.0315

CB1, CB2, CB3, AB1, AB2, AB3 = 0, 512, 1024, 1026, 1282, 1538
DB1, DB2, DB3, MAXLV, MINLV, LOGA = 1550, 2950, 4350, 4602, 4620, 4638

R_IN, R_HEAD, R_OUT, R_MISC, R_SMALL = 0, 72, 88, 96, 128
D_IN, D_OUT, D_B2, D_B3, D_UP, D_LOW, D_LOSS, D_HID, D_ROWS = 0, 24, 60, 61, 62, 63, 64, 72, 128

F32, BF16 = jnp.float32, jnp.bfloat16
MESH = pl.DeviceIdType.MESH
NN = (((1,), (0,)), ((), ()))
NT = (((1,), (1,)), ((), ()))


def dot(a, b, dims=NN):
    return lax.dot_general(a, b, dims, preferred_element_type=F32)


def rounded(v):
    return v.astype(BF16).astype(F32)


def pieces(v):
    high = v.astype(BF16)
    rest = v - high.astype(F32)
    middle = rest.astype(BF16)
    return high, middle, (rest - middle.astype(F32)).astype(BF16)


def split(v):
    high = v.astype(BF16)
    return high, (v - high.astype(F32)).astype(BF16)


def product(a, b, dims=NN, cuts=1):
    left = jnp.concatenate([a[0], a[0], a[1]], 1)
    right = jnp.concatenate([b[0], b[1], b[0]], dims[0][1][0])
    rows = left.shape[0] // cuts
    done = [dot(left[at * rows : (at + 1) * rows], right, dims) for at in range(cuts)]
    return done[0] if cuts == 1 else jnp.concatenate(done, 0)


def softplus(v):
    return jnp.maximum(v, 0.0) + jnp.log1p(jnp.exp(-jnp.abs(v)))


def sigmoid(v):
    return 0.5 + 0.5 * jnp.tanh(0.5 * v)


def gate(half):
    up = 1.0 + jnp.tanh(half)
    value = half * up
    return value, up + value * (2.0 - up)


def by_rows(body, *arrays):
    done = [
        body(*[array[at : at + ROWS] for array in arrays]) for at in range(0, arrays[0].shape[0], ROWS)
    ]
    return [jnp.concatenate(parts, 0) for parts in zip(*done)]


def spread_to(column, width):
    return jnp.concatenate([column] * (width // 128), 1)


def gated(half, column=None):
    def body(part, *offset):
        value, slope = gate(part + spread_to(offset[0], part.shape[1]) if offset else part)
        return value.astype(BF16), slope

    return by_rows(body, half, *([] if column is None else [column]))


def sloped(grad, slope):
    return by_rows(lambda part, by: ((part * by).astype(BF16),), grad, slope)[0]


def outer_sloped(column, row, slope):
    return by_rows(lambda part, by: (((spread_to(part, by.shape[1]) * row) * by).astype(BF16),), column, slope)[0]


def rows_of(shape):
    return lax.broadcasted_iota(jnp.int32, shape, 0)


def blend(gram, square):
    return split(COEF_CUBIC * gram + COEF_QUINTIC * square)


def schulz(refs, steps, before=None):
    cuts = 2 if len(refs) == 1 else 1

    @pl.loop(0, steps)
    def _(step):
        if before is not None:
            before(step)
        matrices = [ref[...] for ref in refs]
        parts = [split(matrix) for matrix in matrices]
        grams = [product(part, part, NT, cuts) for part in parts]
        halves = [split(gram) for gram in grams]
        squares = [product(half, half, NN, cuts) for half in halves]
        blends = [blend(gram, square) for gram, square in zip(grams, squares)]
        moved = [product(mix, part, NN, cuts) for mix, part in zip(blends, parts)]
        for ref, matrix, move in zip(refs, matrices, moved):
            ref[...] = COEF_LINEAR * matrix + move


def schulz_rows(refs, windows, held):
    cuts = 2 if len(refs) == 1 else 1
    parts = [split(ref[...]) for ref in refs]
    grams = [product(part, part, NT, cuts) for part in parts]
    for at, gram in enumerate(grams):
        held[at] = gram
    halves = [split(gram) for gram in grams]
    grams = [held[at, window] for at, window in enumerate(windows)]
    squares = [product(split(gram), half) for gram, half in zip(grams, halves)]
    blends = [blend(gram, square) for gram, square in zip(grams, squares)]
    moved = [product(mix, part) for mix, part in zip(blends, parts)]
    return [
        COEF_LINEAR * ref[window, :] + move for ref, window, move in zip(refs, windows, moved)
    ]


def normalise(ref):
    moment = ref[...]
    norm = jnp.sqrt(jnp.sum(jnp.sum(moment * moment, axis=1, keepdims=True), axis=0, keepdims=True))
    ref[...] = moment / (norm + 1e-7)


class Layout:
    def __init__(self, mesh, replay, model):
        self.n_dp = mesh.shape["dp"]
        self.half = self.n_dp // 2
        self.n_blk = mesh.shape["blk"]
        self.n_dev = self.n_dp * self.n_blk
        self.replay = replay
        self.model = model
        self.real = self.n_dp * CAP
        self.batch = self.real + model
        self.width = -(-(self.real + 2) // 128) * 128
        self.rows = HSAC // self.n_blk
        self.drows = HDYN // self.n_blk
        self.mat = 64 // self.n_dp
        self.sml = 32 // self.n_dp
        self.chunks = (self.mat, self.mat + self.sml, self.mat)
        groups = [(name, g) for name in ("core sum", "plane sum") for g in range(3)]
        groups += [("line sum", g) for g in range(4)]
        common = ["hidden", "hidden on", "lists", "own", "line", "plane", "dyn h", "dyn m", "small", "small on"]
        common += groups
        kinds = [(name, kind) for name in ("pack", "x") for kind in ("own", "on")]
        tiles = [(name, k) for name in ("tiles", "tiles on") for k in range(3)]
        sent = common + tiles + kinds
        self.sent = {name: at for at, name in enumerate(sent)}
        self.departures = len(sent)
        self.here, self.arrivals = {}, 0
        tiles += [("pack", "sibling"), ("x", "sibling")]
        for name in common + tiles:
            self.here[name] = self.arrivals
            self.arrivals += 1
        for name in ("pack", "x"):
            self.here[name, "like"] = self.arrivals
            self.arrivals += MEMBERS


OPERANDS = 23
FIRST, SECOND = 3, 16


def main_kernel(lay, *refs):
    n_in = OPERANDS
    sources, held = refs[:n_in], refs[n_in : 2 * n_in]
    (
        sac_h, requests, member, replay, live, model, noise, biases, targ_in, crit_in, act_in, targ_bias,
        targ_hidden, crit_out, targ_out, act_out, dyn_h, dyn_m, crit_out_m, crit_out_v, sac_m, dyn_in, dyn_out,
    ) = held
    loads = refs[2 * n_in]
    refs = refs[2 * n_in + 1 :]
    (
        sac_g, sac_x, dyn_x, dyn_s, small, count, crit_rows,
        wg, lists, asked, dhg, dmg, bk, xs, nz, ys, ahead, w1f, w1t, w1n, w2t, w2h, heads, head_t, head_f,
        rowbuf, wide, headcol, acc_h, acc_w, acc_c, acc_a, acc_m, acc_l, grid_0, grid_1, grid_2, core_0, core_1,
        core_2, from_0, from_1, from_2, zr_0, zr_1, zr_2, zf_0, zf_1, zf_2, sum_0, sum_1, sum_2, mg, mat, gram, dcols, dacc_h, dacc_w, dacc_o, dacc_m, dacc_b, dacc_l, xt, dmat,
        dpack, drow_x, bias, dhead, dhead_t, *rest,
    ) = refs
    send, recv = rest
    sent, here_at = lay.sent, lay.here
    grids, cores, froms = (grid_0, grid_1, grid_2), (core_0, core_1, core_2), (from_0, from_1, from_2)
    zrs, zfs, totals = (zr_0, zr_1, zr_2), (zf_0, zf_1, zf_2), (sum_0, sum_1, sum_2)
    n_dp, n_blk = lay.n_dp, lay.n_blk
    me = lax.axis_index("dp")
    z = lax.axis_index("blk")
    core, like = lax.rem(me, 2), me // 2
    sibling = me + 1 - 2 * core
    is_dyn = me < MEMBERS
    dyn_e = jnp.minimum(me, MEMBERS - 1)

    def on_plane(src, dst, ssem, rsem, peer):
        return pltpu.make_async_remote_copy(
            src_ref=src, dst_ref=dst, send_sem=ssem, recv_sem=rsem,
            device_id={"dp": peer}, device_id_type=MESH,
        )

    def on_line(src, dst, ssem, rsem, peer):
        return pltpu.make_async_remote_copy(
            src_ref=src, dst_ref=dst, send_sem=ssem, recv_sem=rsem,
            device_id={"blk": peer}, device_id_type=MESH,
        )

    def over(number, body):
        if number <= 8:
            for off in range(1, number):
                body(off)
        else:
            pl.loop(1, number)(body)

    def plane_peers(body):
        over(n_dp, lambda off: body(lax.rem(me + off, n_dp)))

    def like_peers(body):
        over(n_dp // 2, lambda off: body(lax.rem(me + 2 * off, n_dp)))

    def line_peers(body):
        over(n_blk, lambda off: body(lax.rem(z + off, n_blk)))

    def has_sent(view, name):
        at = send.at[sent[name]]
        on_plane(view, view, at, at, sibling).wait_send()

    def has_come(view, name):
        at = recv.at[here_at[name]]
        on_plane(view, view, at, at, sibling).wait_recv()

    copies = [
        pltpu.make_async_copy(src, dst, loads.at[at]) for at, (src, dst) in enumerate(zip(sources, held))
    ]

    def arrived(begin, end):
        for copy in copies[begin:end]:
            copy.wait()

    barrier = pltpu.get_barrier_semaphore()
    plane_peers(lambda peer: pl.semaphore_signal(barrier, inc=1, device_id={"dp": peer}, device_id_type=MESH))
    line_peers(lambda peer: pl.semaphore_signal(barrier, inc=1, device_id={"blk": peer}, device_id_type=MESH))
    for copy in copies:
        copy.start()
    arrived(0, FIRST)
    wg[0] = sac_h[...].astype(BF16)
    lists[0] = requests[...]
    lists[1] = member[...]
    pl.semaphore_wait(barrier, n_dp - 1 + n_blk - 1)

    half_rows = pl.ds(pl.multiple_of(core * (lay.rows // 2), lay.rows // 2), lay.rows // 2)

    def slot_from(owner, at):
        return lax.rem(owner - at + n_blk, n_blk)

    def hidden_copy(peer):
        src = wg.at[0, :, half_rows]
        dst = wg.at[slot_from(z, peer), :, half_rows]
        return on_line(src, dst, send.at[sent["hidden"]], recv.at[here_at["hidden"]], peer)

    def hidden_on():
        view = wg.at[pl.ds(1, n_blk - 1), :, half_rows]
        return on_plane(view, view, send.at[sent["hidden on"]], recv.at[here_at["hidden on"]], sibling)

    def list_copy(peer):
        return on_plane(lists, asked.at[me], send.at[sent["lists"]], recv.at[here_at["lists"]], peer)

    line_peers(lambda peer: hidden_copy(peer).start())
    plane_peers(lambda peer: list_copy(peer).start())
    asked[me] = lists[...]

    def dyn_h_copy(peer):
        return on_line(dyn_h.at[dyn_e], dhg.at[z], send.at[sent["dyn h"]], recv.at[here_at["dyn h"]], peer)

    def dyn_m_copy(peer):
        return on_line(dyn_m.at[dyn_e], dmg.at[z], send.at[sent["dyn m"]], recv.at[here_at["dyn m"]], peer)

    arrived(FIRST, SECOND)
    alive = live[...].astype(F32).reshape(1, lay.model)
    data = replay[...]
    sums = jnp.sum(data[0:24], axis=1, keepdims=True)
    squares = jnp.sum(data[0:24] * data[0:24], axis=1, keepdims=True)
    living = jnp.sum(alive, axis=1, keepdims=True)

    has_come(asked.at[pl.ds(0, n_dp - 1)], "lists")
    spread = (
        lax.rem(lax.broadcasted_iota(jnp.int32, (CAP, lay.real), 1), CAP)
        == lax.broadcasted_iota(jnp.int32, (CAP, lay.real), 0)
    ).astype(F32)
    here = (
        lax.broadcasted_iota(jnp.int32, (n_dp, lay.real), 1) // CAP
        == lax.broadcasted_iota(jnp.int32, (n_dp, lay.real), 0)
    )

    def in_lanes(which):
        values = asked[:, which, me, :].astype(F32)
        wide = lax.dot_general(
            values, spread, NN, precision=lax.Precision.HIGHEST, preferred_element_type=F32
        )
        return jnp.sum(jnp.where(here, wide, 0.0), axis=0, keepdims=True)

    slots = in_lanes(0)
    wanted = jnp.maximum(slots, 0.0).astype(jnp.int32)
    hot = (rows_of((lay.replay, lay.real)) == wanted).astype(BF16)
    padded = jnp.concatenate([data, jnp.zeros((48 - FEAT, lay.replay), F32)], 0)
    chosen = dot(jnp.concatenate(pieces(padded), 0), hot)
    chosen = chosen[0:48] + chosen[48:96] + chosen[96:144]
    mine = me * n_blk
    bk[mine, 0:FEAT, 0 : lay.real] = chosen[0:FEAT]
    bk[mine, 42:43, 0 : lay.real] = (slots >= 0.0).astype(F32)
    bk[mine, 43:44, 0 : lay.real] = in_lanes(1)
    bk[mine, 44:48, 0 : lay.real] = jnp.zeros((4, lay.real), F32)
    bk[mine, :, lay.real : lay.width] = jnp.zeros((48, lay.width - lay.real), F32)
    bk[mine, 0:24, lay.real : lay.real + 1] = sums
    bk[mine, 0:24, lay.real + 1 : lay.real + 2] = squares
    bk[mine, 24:25, lay.real : lay.real + 1] = living

    def slot_of(block):
        line = lax.rem(block, n_blk)
        return block - line + slot_from(line, z)

    def block_line(peer):
        dst = bk.at[me * n_blk + slot_from(z, peer)]
        return on_line(bk.at[mine], dst, send.at[sent["line"]], recv.at[here_at["line"]], peer)

    def block_own(peer):
        view = bk.at[mine]
        return on_plane(view, view, send.at[sent["own"]], recv.at[here_at["own"]], peer)

    def block_plane(peer):
        view = bk.at[pl.ds(mine + 1, n_blk - 1)]
        return on_plane(view, view, send.at[sent["plane"]], recv.at[here_at["plane"]], peer)

    plane_peers(lambda peer: block_own(peer).start())
    line_peers(lambda peer: block_line(peer).start())

    arrived(SECOND, n_in)
    crit_rows[0:2, :] = crit_out[...]
    crit_rows[2:4, :] = crit_out_m[...]
    crit_rows[4:6, :] = crit_out_v[...]
    crit_rows[6:8, :] = jnp.zeros((2, HSAC), F32)

    @pl.when(is_dyn)
    def _():
        line_peers(lambda peer: dyn_h_copy(peer).start())
        line_peers(lambda peer: dyn_m_copy(peer).start())

    bias[...] = biases[...].reshape(1, NB)
    xs[42:56, :] = jnp.zeros((14, lay.batch), F32)
    xs[0:FEAT, lay.real : lay.batch] = model[...]
    xs[42:43, lay.real : lay.batch] = alive
    nz[...] = jnp.zeros_like(nz)
    for which in range(2):
        nz[which, 1:7, :] = noise[:, which, :]
    firsts = [
        (targ_in[:, 0, :], targ_bias[0:1, 0:HSAC]),
        (targ_in[:, 1, :], targ_bias[1:2, 0:HSAC]),
        (crit_in[:, 0, :], bias[:, CB1 : CB1 + HSAC]),
        (crit_in[:, 1, :], bias[:, CB1 + HSAC : CB1 + 2 * HSAC]),
        (act_in[...], bias[:, AB1 : AB1 + HSAC]),
    ]
    w1f[...] = jnp.zeros_like(w1f)
    for net, (weights, offset) in enumerate(firsts):
        w1f[net, 0 : weights.shape[0], :] = rounded(weights)
        for at, piece in enumerate(pieces(offset)):
            w1f[net, IN + at : IN + at + 1, :] = piece.astype(F32)
        w1t[net] = (0.5 * w1f[net].T).astype(BF16)
    for k in range(2):
        w1n[k] = w1f[2 + k, 16:32, :].astype(BF16)
    for net in range(2):
        w2t[net] = (0.5 * rounded(targ_hidden[net])).T.astype(BF16)
    has_come(wg.at[pl.ds(0, n_blk - 1), :, half_rows], "hidden")
    hidden_on().start()

    rowbuf[...] = jnp.zeros_like(rowbuf)
    rowbuf[0:1, :] = targ_bias[0:1, HSAC : 2 * HSAC]
    rowbuf[1:2, :] = targ_bias[1:2, HSAC : 2 * HSAC]
    rowbuf[2:3, :] = bias[:, CB2 : CB2 + HSAC]
    rowbuf[3:4, :] = bias[:, CB2 + HSAC : CB2 + 2 * HSAC]
    rowbuf[4:5, :] = bias[:, AB2 : AB2 + HSAC]
    rowbuf[5:7, :] = rounded(crit_out[...])
    columns = 0.5 * rowbuf[...].T
    for at in range(7):
        wide[at] = jnp.broadcast_to(columns[:, at : at + 1], (HSAC, 128))
    rowbuf[...] = jnp.zeros_like(rowbuf)
    rowbuf[0:1, 1:7] = bias[:, AB3 : AB3 + ACT]
    rowbuf[0:1, 9:15] = bias[:, AB3 + ACT : AB3 + 2 * ACT]
    headcol[...] = rowbuf[:, 0:128].T
    head_f[...] = jnp.zeros_like(head_f)
    for k in range(2):
        head_f[0:1, :] = targ_out[k : k + 1, :]
        heads[k] = head_f[...].astype(BF16)
        head_f[0:1, :] = crit_out[k : k + 1, :]
        heads[2 + k] = head_f[...].astype(BF16)
    head_f[0:1, :] = jnp.zeros((1, HSAC), F32)
    head_f[1:7, :] = act_out[0:ACT, :]
    head_f[9:15, :] = act_out[ACT : 2 * ACT, :]
    heads[4] = head_f[...].astype(BF16)
    head_t[...] = (0.5 * rounded(head_f[...])).T.astype(BF16)
    for ref in (acc_h, acc_w, acc_c, acc_a, acc_m, acc_l):
        ref[...] = jnp.zeros_like(ref)

    has_come(wg.at[pl.ds(0, n_blk - 1), :, half_rows], "hidden on")
    for k in range(3):
        for block in range(n_blk):
            w2h[k, block * lay.rows : (block + 1) * lay.rows, :] = (
                0.5 * wg[slot_from(block, z), k].astype(F32)
            ).astype(BF16)
        w2t[2 + k] = w2h[k].astype(F32).T.astype(BF16)

    log_alpha = bias[:, LOGA : LOGA + 1]
    alpha = jnp.exp(log_alpha)
    last = [
        targ_bias[0:1, 2 * HSAC : 2 * HSAC + 1],
        targ_bias[1:2, 2 * HSAC : 2 * HSAC + 1],
        bias[:, CB3 : CB3 + 1],
        bias[:, CB3 + 1 : CB3 + 2],
    ]
    critic_tiles = lay.batch // CRITIC_TILE
    actor_tiles = lay.batch // ACTOR_TILE

    def act_rows(width):
        row8 = rows_of((8, width))
        return jnp.logical_and(row8 >= 1, row8 < 1 + ACT)

    def place_of(step, width):
        return pl.ds(pl.multiple_of(lax.rem(step + 1, lay.batch // width) * width, width), width)

    def ones16(width):
        return jnp.ones((16, width), BF16)

    def framed(first_row, used, where):
        row32 = rows_of((32, where.size))
        ones3 = jnp.logical_and(row32 >= IN, row32 < IN + 3).astype(F32)
        return jnp.where(row32 < used, xs[first_row : first_row + 32, where], ones3)

    def hidden(inputs, net):
        first, slope1 = gated(dot(w1t[net], inputs))
        second, slope2 = gated(dot(w2t[net], first), wide[net])
        return first, slope1, second, slope2

    def policy(inputs, which, where):
        first, slope1, second, slope2 = hidden(inputs, 4)
        out = dot(heads[4], second) + headcol[0:16, 0:1]
        bent = jnp.tanh(out[8:16])
        log_scale = -5.0 + 3.5 * (bent + 1.0)
        draw = nz[which, :, where]
        moved = jnp.exp(log_scale) * draw
        latent = out[0:8] + moved
        terms = (
            -0.5 * draw * draw
            - log_scale
            - 0.9189385
            - 2.0 * (0.6931472 - latent - softplus(-2.0 * latent))
        )
        used = act_rows(where.size)
        log_prob = jnp.sum(jnp.where(used, terms, 0.0), axis=0, keepdims=True)
        action = jnp.where(used, jnp.tanh(latent), 0.0)
        return action, log_prob, bent, moved, (first, slope1, second, slope2)

    def with_action(inputs, action):
        middle_rows = jnp.where(act_rows(action.shape[1]), action, inputs[16:24])
        return jnp.concatenate([inputs[0:16], middle_rows, inputs[24:32]], 0).astype(BF16)

    def critic(inputs, net):
        kept = hidden(inputs, net)
        value = dot(heads[net], kept[2])[0:1] + last[net]
        return value, kept

    def add_hidden(k, first, grad):
        acc_h[k] += dot(jnp.concatenate([first, ones16(grad.shape[1])], 0), grad, NT)

    has_come(bk.at[pl.ds(0, n_blk - 1)], "line")
    plane_peers(lambda peer: block_plane(peer).start())

    def critic_pass(k, now_in, where, target):
        weight = xs[42:43, where]
        value, (c1, dc1, c2, dc2) = critic(now_in, 2 + k)
        miss = value - target
        g3 = rounded(weight * miss)
        g3_rows = jnp.where(rows_of((16, CRITIC_TILE)) == 0, g3, 0.0).astype(BF16)
        acc_c[k] += dot(g3_rows, c2, NT)
        acc_m[:, 16 + 16 * k : 32 + 16 * k] += dot(ones16(CRITIC_TILE), g3_rows, NT)
        g2 = outer_sloped(wide[5 + k], g3, dc2)
        add_hidden(k, c1, g2)
        g1 = sloped(dot(w2h[k], g2), dc1)
        acc_w[k] += dot(now_in, g1, NT)
        acc_l[0:1, 0:CRITIC_TILE] += weight * (0.5 * miss * miss)

    def put_matrix(k):
        for chunk in range(n_dp):
            tile = chunk * lay.mat
            side, row = tile // 32, tile % 32
            grids[k][chunk % 2, chunk // 2, 0 : lay.mat] = acc_h[
                k, row * 8 : (row + lay.mat) * 8, side * 128 : (side + 1) * 128
            ].reshape(lay.mat, 8, 128)

    def put(row, value):
        for at in range(value.shape[0] // 8):
            for side in range(value.shape[1] // 128):
                tile = side * (R_SMALL // 8) + row // 8 + at
                chunk = tile // lay.sml
                grid_1[chunk % 2, chunk // 2, lay.mat + tile % lay.sml] = value[
                    at * 8 : at * 8 + 8, side * 128 : (side + 1) * 128
                ]

    def core_sum(group):
        name = ("core sum", group)
        return on_plane(
            grids[group].at[1 - core], cores[group], send.at[sent[name]], recv.at[here_at[name]], sibling
        )

    def plane_sum(group, peer):
        name = ("plane sum", group)
        return on_plane(
            cores[group].at[peer // 2], froms[group].at[like], send.at[sent[name]], recv.at[here_at[name]], peer
        )

    def fold_core(group):
        core_sum(group).wait_recv()
        cores[group][...] += grids[group][core]
        like_peers(lambda peer: plane_sum(group, peer).start())

    def line_part(part):
        return (1, pl.ds(lay.mat, lay.sml)) if part == 3 else (part, pl.ds(0, lay.mat))

    def line_sum(part, peer):
        group, tiles = line_part(part)
        name = ("line sum", part)
        src, dst = zfs[group].at[tiles], zrs[group].at[z, tiles]
        return on_line(src, dst, send.at[sent[name]], recv.at[here_at[name]], peer)

    def line_bytes(part):
        group, tiles = line_part(part)
        return zrs[group].at[pl.ds(0, n_blk - 1), tiles]

    first_tile = me * lay.mat
    side = first_tile // 32
    row_tile = lax.rem(first_tile, 32)
    keeper_z = row_tile * 8 // lay.rows
    local_tile = row_tile - keeper_z * (lay.rows // 8)

    def fold_plane(group):
        has_come(froms[group].at[pl.ds(0, lay.half - 1)], ("plane sum", group))
        froms[group][like] = cores[group][like]
        whole = froms[group][0]
        for at in range(1, lay.half):
            whole = whole + froms[group][at]
        zfs[group][...] = whole

        @pl.when(z == keeper_z)
        def _():
            held_rows = pl.ds(pl.multiple_of(local_tile * 8, 8), lay.mat * 8)
            held_lanes = pl.ds(pl.multiple_of(side * 128, 128), 128)
            old = sac_m[group, held_rows, held_lanes].reshape(lay.mat, 8, 128)
            zfs[group][0 : lay.mat] += (MOMENTUM * count[0:1, 0:1]).reshape(1, 1, 1) * old

        for part in (1, 3) if group == 1 else (group,):
            line_peers(lambda peer: line_sum(part, peer).start())

    def tile_copy(k, peer):
        name = ("tiles", k)
        src = totals[k].at[pl.ds(0, lay.mat)]
        return on_plane(src, mg.at[k, core, like], send.at[sent[name]], recv.at[here_at[name]], peer)

    def tiles_on(k):
        name = ("tiles on", k)
        view = mg.at[k, core]
        return on_plane(view, view, send.at[sent[name]], recv.at[here_at[name]], sibling)

    small_at = (core * lay.half + like) * lay.sml

    def small_copy(peer):
        return on_plane(
            sum_1.at[pl.ds(lay.mat, lay.sml)], small.at[pl.ds(small_at, lay.sml)],
            send.at[sent["small"]], recv.at[here_at["small"]], peer,
        )

    def small_on():
        view = small.at[pl.ds(core * lay.half * lay.sml, lay.half * lay.sml)]
        return on_plane(view, view, send.at[sent["small on"]], recv.at[here_at["small on"]], sibling)

    def fold_end(part):
        group, tiles = line_part(part)
        has_come(line_bytes(part), ("line sum", part))
        zrs[group][z, tiles] = zfs[group][tiles]
        whole = zrs[group][0, tiles]
        for block in range(1, n_blk):
            whole = whole + zrs[group][block, tiles]
        totals[group][tiles] = whole
        if part == 3:
            like_peers(lambda peer: small_copy(peer).start())
            small[pl.ds(small_at, lay.sml)] = whole
        else:
            like_peers(lambda peer: tile_copy(part, peer).start())
            mg[part, core, like] = whole

    def chain(group):
        def end():
            for part in (1, 3) if group == 1 else (group,):
                fold_end(part)

        def turn():
            has_come(mg.at[group, 0, pl.ds(0, lay.half - 1)], ("tiles", group))
            tiles_on(group).start()
            if group == 1:
                has_come(small.at[pl.ds(0, (lay.half - 1) * lay.sml)], "small")
                small_on().start()

        return [
            lambda: core_sum(group).start(),
            lambda: fold_core(group),
            lambda: fold_plane(group),
            end,
            turn,
        ]

    chains = [chain(group) for group in range(3)]
    per = DYN_TILE // lay.real
    dyn_tiles = lay.n_dev // per

    def take(slots, step):
        for at, events in slots.items():
            @pl.when(step == at)
            def _():
                for event in events:
                    event()

    @pl.loop(0, actor_tiles)
    def _(step):
        @pl.when(step == actor_tiles - 1)
        def _():
            has_come(bk.at[pl.ds(0, n_dp - 1)], "own")
            lanes = lax.broadcasted_iota(jnp.int32, (48, lay.width), 1) // CAP

            def gather(owner, total):
                turned = pltpu.roll(
                    bk[owner * n_blk], lax.rem((owner - me) * CAP + lay.width, lay.width), axis=1
                )
                return jnp.where(lanes == owner, turned, total)

            own = lax.fori_loop(0, n_dp, gather, jnp.zeros((48, lay.width), F32))
            xs[0:48, 0 : lay.real] = own[:, 0 : lay.real]

        where = place_of(step, ACTOR_TILE)
        now_f = framed(0, IN, where)
        now_in = now_f.astype(BF16)
        weight = xs[42:43, where]
        next_action, next_prob, _, _, _ = policy(framed(24, OBS, where).astype(BF16), 1, where)
        ahead[0:8, where] = next_action
        ys[1:2, where] = next_prob
        action, log_prob, bent, moved, (a1, da1, a2, da2) = policy(now_in, 0, where)
        judged_in = with_action(now_f, action)
        loss = alpha * log_prob - log_alpha * (log_prob + TARGET_ENTROPY)
        grad_action = jnp.zeros((8, ACTOR_TILE), F32)
        used = act_rows(ACTOR_TILE)
        for k in range(2):
            judged, (_, df1, _, df2) = critic(judged_in, 2 + k)
            loss -= 0.5 * judged
            g2 = outer_sloped(wide[5 + k], -0.5 * weight, df2)
            g1 = sloped(dot(w2h[k], g2), df1)
            grad_action += dot(w1n[k], g1)[0:8]
        grad_latent = 2.0 * alpha * weight * action + grad_action * (1.0 - action * action)
        grad_scale = grad_latent * moved - alpha * weight
        grad_bent = grad_scale * 3.5 * (1.0 - bent * bent)
        g3 = jnp.concatenate(
            [jnp.where(used, grad_latent, 0.0), jnp.where(used, grad_bent, 0.0)], 0
        ).astype(BF16)
        acc_a[...] += dot(g3, a2, NT)
        acc_m[:, 0:16] += dot(ones16(ACTOR_TILE), g3, NT)
        g2 = sloped(dot(head_t[...], g3), da2)
        add_hidden(2, a1, g2)
        g1 = sloped(dot(w2h[2], g2), da1)
        acc_w[2] += dot(now_in, g1, NT)
        acc_l[1:2, 0:ACTOR_TILE] += weight * loss
        acc_l[2:3, 0:ACTOR_TILE] += weight * (log_prob + TARGET_ENTROPY)

    put_matrix(2)
    chains[2][0]()

    @pl.loop(0, critic_tiles)
    def _(step):
        if critic_tiles > 1:
            take({1: [chains[2][1]]}, step)

        where = place_of(step, CRITIC_TILE)
        now_in = framed(0, IN, where).astype(BF16)
        reward = xs[23:24, where]
        done = xs[41:42, where]
        aim_in = with_action(framed(24, OBS, where), ahead[0:8, where])
        next_prob = ys[1:2, where]
        aim = jnp.minimum(critic(aim_in, 0)[0], critic(aim_in, 1)[0])
        target = reward + DISCOUNT * (1.0 - done) * (aim - alpha * next_prob)
        ys[0:1, where] = target
        critic_pass(0, now_in, where, target)

    put_matrix(0)
    chains[0][0]()
    if critic_tiles == 1:
        chains[2][1]()

    has_come(bk.at[pl.ds(0, (n_dp - 1) * (n_blk - 1))], "plane")
    lane0 = lay.real // 128 * 128

    def add_block(at, carry):
        sides, fills = carry
        slot = slot_of(at)
        return sides + bk[slot, 0:32, lane0 : lane0 + 128], fills + bk[slot, 40:48, 0 : lay.real]

    sides, fills = lax.fori_loop(
        0, lay.n_dev, add_block, (jnp.zeros((32, 128), F32), jnp.zeros((8, lay.real), F32))
    )
    at = lay.real - lane0
    rows_all = float(lay.replay * lay.n_dev)
    centre = sides[0:24, at : at + 1] / rows_all
    scale = lax.rsqrt(sides[0:24, at + 1 : at + 2] / rows_all - centre * centre + 1e-6)
    total = sides[24:25, at : at + 1] + jnp.sum(fills[2:3, :], axis=1, keepdims=True)
    count[...] = jnp.broadcast_to(total, (8, 128))

    @pl.loop(0, critic_tiles)
    def _(step):
        take({critic_tiles - 1: [chains[0][1], chains[2][2]]}, step)
        where = place_of(step, CRITIC_TILE)
        critic_pass(1, framed(0, IN, where).astype(BF16), where, ys[0:1, where])

    put_matrix(1)
    for k in range(3):
        put(R_IN + 24 * k, acc_w[k, 0:24, :])
    put(R_HEAD, acc_a[...])
    rowbuf[0:1, :] = acc_c[0, 0:1, :]
    rowbuf[1:2, :] = acc_c[1, 0:1, :]
    for k in range(3):
        rowbuf[2 + k : 3 + k, :] = acc_h[k, HSAC : HSAC + 1, :]
    put(R_OUT, rowbuf[...])
    folded = jnp.sum(acc_l[...], axis=1, keepdims=True)
    rowbuf[...] = jnp.zeros_like(rowbuf)
    rowbuf[0:1, 0:48] = acc_m[0:1, :]
    rowbuf[0:1, 64:65] = folded[0:1] + folded[1:2]
    rowbuf[0:1, 65:66] = folded[2:3]
    put(R_MISC, rowbuf[...])
    put(R_MISC + 8, jnp.zeros((R_SMALL - R_MISC - 8, HSAC), F32))
    chains[1][0]()

    def dyn_bias(start, width):
        row = jnp.zeros((1, width), F32)
        for e in range(MEMBERS):
            row = jnp.where(me == e, bias[:, start + width * e : start + width * (e + 1)], row)
        return row

    @pl.when(is_dyn)
    def _():
        w1f[0] = jnp.zeros((32, HSAC), F32)
        w1f[0, 0:IN, 0:HDYN] = rounded(dyn_in[dyn_e])
        for at, piece in enumerate(pieces(dyn_bias(DB1, HDYN))):
            w1f[0, IN + at : IN + at + 1, 0:HDYN] = piece.astype(F32)
        w1t[0] = (0.5 * w1f[0].T).astype(BF16)
        rowbuf[...] = jnp.zeros_like(rowbuf)
        rowbuf[0:1, 0:HDYN] = dyn_bias(DB2, HDYN)
        head_row = dyn_bias(DB3, DOUT)
        rowbuf[1:2, 0:HALF] = head_row[:, 0:HALF]
        rowbuf[1:2, 24 : 24 + HALF] = head_row[:, HALF:DOUT]
        rowbuf[2:3, 0:HALF] = bias[:, MAXLV : MAXLV + HALF]
        rowbuf[3:4, 0:HALF] = bias[:, MINLV : MINLV + HALF]
        dcols[...] = rowbuf[...].T
        wide[0] = jnp.broadcast_to(0.5 * dcols[:, 0:1], (HSAC, 128))
        dpack[...] = jnp.zeros_like(dpack)
        dpack[0:HALF, 0:HDYN] = dyn_out[dyn_e, 0:HALF, :]
        dpack[24 : 24 + HALF, 0:HDYN] = dyn_out[dyn_e, HALF:DOUT, :]
        dhead[...] = dpack[0:48, :].astype(BF16)
        dhead_t[...] = (0.5 * rounded(dpack[0:48, :])).T.astype(BF16)
        dpack[...] = jnp.zeros_like(dpack)

        has_come(dhg.at[pl.ds(0, n_blk - 1)], "dyn h")
        has_come(dmg.at[pl.ds(0, n_blk - 1)], "dyn m")
        dhg[z] = dyn_h[dyn_e]
        dmg[z] = dyn_m[dyn_e]
        dmat[...] = jnp.zeros_like(dmat)
        for block in range(n_blk):
            dmat[block * lay.drows : (block + 1) * lay.drows, 0:HDYN] = 0.5 * rounded(dhg[block])
        w2h[0] = dmat[...].astype(BF16)
        w2t[0] = dmat[...].T.astype(BF16)
        for ref in (dacc_h, dacc_w, dacc_o, dacc_m, dacc_b, dacc_l):
            ref[...] = jnp.zeros_like(ref)

    in_dyn = {}
    for at, event in (
        (1, chains[0][2]), (1, chains[1][1]), (2, chains[2][3]), (dyn_tiles - 1, chains[1][2]),
    ):
        in_dyn.setdefault(min(at, dyn_tiles - 1), []).append(event)

    @pl.loop(0, dyn_tiles)
    def _(tile):
        take(in_dyn, tile)

        @pl.when(is_dyn)
        def _():
            for at in range(per):
                slot = slot_of(tile * per + at)
                xt[:, at * lay.real : (at + 1) * lay.real] = bk[slot, :, 0 : lay.real]
            now = xt[0:24, :]
            later = xt[24:48, :]
            row24 = rows_of((24, DYN_TILE))
            scaled = jnp.where(row24 < IN, (now - centre) * scale, 1.0)
            inputs = jnp.concatenate([scaled, (rows_of((8, DYN_TILE)) < 2).astype(F32)], 0).astype(BF16)
            first, slope1 = gated(dot(w1t[0], inputs))
            second, slope2 = gated(dot(w2t[0], first), wide[0])
            out = dot(dhead[...], second) + dcols[0:48, 1:2]
            used = row24 < HALF
            upper = dcols[0:24, 2:3]
            lower = dcols[0:24, 3:4]
            gap1 = upper - out[24:48]
            gap2 = upper - softplus(gap1) - lower
            log_var = lower + softplus(gap2)
            error = out[0:24] - jnp.where(row24 == OBS, now[23:24], later - now)
            inverse = jnp.exp(-log_var)
            weight = xt[42:43, :] * (xt[43:44, :] == me.astype(F32)).astype(F32)
            spread_term = error * error * inverse
            nll = jnp.sum(jnp.where(used, spread_term + log_var, 0.0), axis=0, keepdims=True)
            dacc_l[0:1, :] += weight * nll
            grad_mu = 2.0 * weight * error * inverse
            grad_lv = weight * (1.0 - spread_term)
            open1 = sigmoid(gap1)
            open2 = sigmoid(gap2)
            grad_lv1 = grad_lv * open2
            dacc_b[0] += jnp.where(used, grad_lv1 * (1.0 - open1), 0.0)
            dacc_b[1] += jnp.where(used, grad_lv * (1.0 - open2), 0.0)
            g3 = jnp.concatenate(
                [jnp.where(used, grad_mu, 0.0), jnp.where(used, grad_lv1 * open1, 0.0)], 0
            ).astype(BF16)
            dacc_o[...] += dot(g3, second, NT)
            dacc_m[...] += dot(ones16(DYN_TILE), g3, NT)
            g2 = sloped(dot(dhead_t[...], g3), slope2)
            dacc_h[...] += dot(jnp.concatenate([first, ones16(DYN_TILE)], 0), g2, NT)
            g1 = sloped(dot(w2h[0], g2), slope1)
            dacc_w[...] += dot(inputs, g1, NT)

    out_of = {"pack": dyn_s, "x": dyn_x}

    def member_copy(name, src, owner, kind, sem, peer):
        return on_plane(src, out_of[name].at[owner], send.at[sent[name, kind]], recv.at[sem], peer)

    def give(name, src):
        like_peers(
            lambda peer: member_copy(name, src, dyn_e, "own", here_at[name, "like"] + dyn_e, peer).start()
        )
        member_copy(name, src, dyn_e, "own", here_at[name, "sibling"], sibling).start()

    def hand_on(name):
        def body(peer):
            @pl.when(peer < MEMBERS)
            def _():
                owner = jnp.minimum(peer, MEMBERS - 1)
                view = out_of[name].at[owner]
                member_copy(name, view, owner, "on", here_at[name, "like"] + owner, sibling).wait_recv()
                member_copy(name, view, owner, "on", here_at[name, "sibling"], sibling).start()

        like_peers(body)

    even, odd = (MEMBERS + 1) // 2, MEMBERS // 2
    handed = even - core * (even - odd) - jnp.where(is_dyn, 1, 0)

    def from_sibling(name):
        for side, number in ((0, odd), (1, even)):
            @pl.when(core == side)
            def _():
                has_come(out_of[name].at[pl.ds(0, number)], (name, "sibling"))

    def gave(name):
        @pl.when(is_dyn)
        def _():
            for begin in range(0, n_dp // 2, MEMBERS):
                number = min(MEMBERS, n_dp // 2 - begin)
                has_sent(out_of[name].at[pl.ds(0, number)], (name, "own"))

        for number in (even, even - 1, even - 2):
            @pl.when(handed == number)
            def _():
                has_sent(out_of[name].at[pl.ds(0, number)], (name, "on"))

    def line_rows(ref):
        rows = ref[0 : lay.drows, 0:HDYN]
        for block in range(1, n_blk):
            rows = jnp.where(z == block, ref[block * lay.drows : (block + 1) * lay.drows, 0:HDYN], rows)
        return rows

    mine_rows = pl.ds(pl.multiple_of(z * lay.rows, lay.rows), lay.rows)
    dyn_window = pl.ds(pl.multiple_of(z * lay.drows // 8 * 8, 8), -(-(lay.drows + 7) // 8) * 8)

    def from_window(value):
        rows = value[0 : lay.drows, 0:HDYN]
        for block in range(1, n_blk):
            begin = block * lay.drows % 8
            rows = jnp.where(z == block, value[begin : begin + lay.drows, 0:HDYN], rows)
        return rows

    def take_matrix(k):
        tiles_on(k).wait_recv()
        for chunk in range(n_dp):
            tile = chunk * lay.mat
            half, row = tile // 32, tile % 32
            at = slice(row * 8, (row + lay.mat) * 8)
            piece = mg[k, chunk % 2, chunk // 2].reshape(lay.mat * 8, 128)
            mat[k, at, half * 128 : (half + 1) * 128] = piece / total
        normalise(mat.at[k])

    chains[2][4]()
    chains[0][3]()

    @pl.when(is_dyn)
    def _():
        dpack[D_IN : D_IN + 24, :] = dacc_w[0:24, :]
        dpack[D_OUT : D_OUT + HALF, :] = dacc_o[0:HALF, :]
        dpack[D_OUT + HALF : D_OUT + DOUT, :] = dacc_o[24 : 24 + HALF, :]
        dpack[D_B2 : D_B2 + 1, :] = dacc_h[HSAC : HSAC + 1, :]
        dpack[D_B3 : D_B3 + 1, 0:48] = dacc_m[0:1, :]
        lanes = lax.broadcasted_iota(jnp.int32, (24, 128), 1)
        bound = jnp.where(
            lanes == 0,
            jnp.sum(dacc_b[0], axis=1, keepdims=True),
            jnp.where(lanes == 1, jnp.sum(dacc_b[1], axis=1, keepdims=True), 0.0),
        )
        dpack[D_UP : D_UP + 2, 0:24] = bound.T[0:2, :]
        dpack[D_LOSS : D_LOSS + 1, 0:128] = jnp.broadcast_to(
            jnp.sum(dacc_l[0:1, :], axis=1, keepdims=True), (1, 128)
        )
        dpack[D_HID : D_HID + lay.drows, 0:HDYN] = line_rows(dacc_h)
        dyn_s[dyn_e] = dpack[...]
        give("pack", dpack)
        dmat[...] = jnp.zeros_like(dmat)
        for block in range(n_blk):
            at = slice(block * lay.drows, (block + 1) * lay.drows)
            dmat[at, 0:HDYN] = MOMENTUM * dmg[block] + dacc_h[at, 0:HDYN] / total
        normalise(dmat)

    def sum_end(step):
        @pl.when(step == 3)
        def _():
            chains[0][4]()
            chains[1][3]()

    take_matrix(2)

    @pl.when(is_dyn)
    def _():
        both = [dmat, mat.at[2]]
        schulz(both, NS_ITERS - 1, sum_end)
        window, sac_x[2] = schulz_rows(both, [dyn_window, mine_rows], gram)
        rows = from_window(window)
        drow_x[...] = rows
        dyn_x[dyn_e] = rows
        give("x", drow_x)

    @pl.when(jnp.logical_not(is_dyn))
    def _():
        schulz([mat.at[2]], NS_ITERS - 1, sum_end)
        (sac_x[2],) = schulz_rows([mat.at[2]], [mine_rows], gram)

    def sent_early():
        has_sent(wg.at[pl.ds(0, n_blk - 1), :, half_rows], "hidden")
        has_sent(wg.at[pl.ds(0, n_blk - 1), :, half_rows], "hidden on")
        has_sent(asked.at[pl.ds(0, n_dp - 1)], "lists")
        has_sent(bk.at[pl.ds(0, n_dp - 1)], "own")
        has_sent(bk.at[pl.ds(0, n_blk - 1)], "line")
        has_sent(bk.at[pl.ds(0, (n_dp - 1) * (n_blk - 1))], "plane")

        @pl.when(is_dyn)
        def _():
            has_sent(dhg.at[pl.ds(0, n_blk - 1)], "dyn h")
            has_sent(dmg.at[pl.ds(0, n_blk - 1)], "dyn m")

        for group in range(3):
            core_sum(group).wait_send()
            has_sent(froms[group].at[pl.ds(0, lay.half - 1)], ("plane sum", group))
        for part in range(4):
            has_sent(line_bytes(part), ("line sum", part))

    def pass_on(step):
        pl.when(step == 2)(functools.partial(hand_on, "pack"))

    sent_early()
    chains[1][4]()
    for k in range(2):
        take_matrix(k)
    both = [mat.at[0], mat.at[1]]
    schulz(both, NS_ITERS - 1, pass_on)
    hand_on("x")
    sac_x[0], sac_x[1] = schulz_rows(both, [mine_rows, mine_rows], gram)
    for k in range(3):
        for half in range(2):
            for piece in range(lay.rows // 8 // lay.mat):
                chunk = (half * 32 + z * (lay.rows // 8)) // lay.mat + piece
                kept = mg[k, lax.rem(chunk, 2), chunk // 2]
                sac_g[half, k, piece * lay.mat : (piece + 1) * lay.mat] = kept

    small_on().wait_recv()
    from_sibling("pack")
    from_sibling("x")

    has_sent(small.at[pl.ds(0, (lay.half - 1) * lay.sml)], "small")
    small_on().wait_send()
    gave("pack")
    gave("x")

    for k in range(3):
        has_sent(mg.at[k, 0, pl.ds(0, lay.half - 1)], ("tiles", k))
        tiles_on(k).wait_send()


def ordered(lay, n_in, n_out, *refs):
    inputs, outputs, scratch = refs[:n_in], refs[n_in : n_in + n_out], refs[n_in + n_out :]
    main_kernel(lay, *inputs, *scratch[: n_in + 1], *outputs, *scratch[n_in + 1 :])


def adamw(weights, first, second, gradient):
    first = BETA_FIRST * first + (1.0 - BETA_FIRST) * gradient
    second = BETA_SECOND * second + (1.0 - BETA_SECOND) * gradient * gradient
    first_hat = first / (1.0 - BETA_FIRST**STEP)
    second_hat = second / (1.0 - BETA_SECOND**STEP)
    step = first_hat / (jnp.sqrt(second_hat) + 1e-8) + ADAM_DECAY * weights
    return weights - ADAM_RATE * step, first, second


def update_kernel(lay, *refs):
    (
        sac_g, sac_x, dyn_x, dyn_s, small, count, crit_rows, sac_h, dyn_h, dyn_m,
        ci, ci_m, ci_v, ai, ai_m, ai_v, di, di_m, di_v, ao, ao_m, ao_v,
        do, do_m, do_v, bi, bi_m, bi_v,
        sac_new, sac_mom, dyn_new, dyn_mom, ci_n, ci_mn, ci_vn, ai_n, ai_mn, ai_vn, di_n, di_mn,
        di_vn, co_n, co_mn, co_vn, ao_n, ao_mn, ao_vn, do_n, do_mn, do_vn, bi_n, bi_mn, bi_vn,
        loss, counted, bg,
    ) = refs
    total = count[0:1, 0:1]
    for k in range(3):
        for side in range(2):
            tiles = sac_g[side, k].reshape(sac_mom.shape[1], 128)
            sac_mom[k, :, side * 128 : (side + 1) * 128] = tiles / total
    sac_new[...] = sac_h[...] * (1.0 - MUON_RATE * MUON_DECAY) - MUON_RATE * sac_x[...]
    dyn_rows = dyn_s[:, D_HID : D_HID + dyn_m.shape[1], 0:HDYN]
    dyn_mom[...] = MOMENTUM * dyn_m[...] + dyn_rows / total.reshape(1, 1, 1)
    dyn_new[...] = dyn_h[...] * (1.0 - MUON_RATE * MUON_DECAY) - MUON_RATE * dyn_x[...]

    def rows(row, number):
        def tile(at):
            chunk = at // lay.sml
            return small[(chunk % 2 * lay.half + chunk // 2) * lay.sml + at % lay.sml]

        sides = []
        for side in range(2):
            at = side * (R_SMALL // 8) + row // 8
            sides.append(jnp.concatenate([tile(at + more) for more in range(-(-number // 8))], 0))
        return jnp.concatenate(sides, 1)

    def store(outs, at, values):
        for out, value in zip(outs, values):
            out[at] = value

    outs = (ci_n, ci_mn, ci_vn)
    for k in range(2):
        at = (slice(None), k, slice(None))
        grad = rows(R_IN + 24 * k, 24)
        bg[:, CB1 + HSAC * k : CB1 + HSAC * (k + 1)] = grad[IN : IN + 1]
        store(outs, at, adamw(ci[at], ci_m[at], ci_v[at], grad[0:IN] / total))
    grad = rows(R_IN + 48, 24)
    bg[:, AB1 : AB1 + HSAC] = grad[IN : IN + 1]
    store((ai_n, ai_mn, ai_vn), ..., adamw(ai[...], ai_m[...], ai_v[...], grad[0:OBS] / total))
    grad = rows(R_HEAD, 16)
    for at, row in ((slice(0, ACT), slice(1, 1 + ACT)), (slice(ACT, 2 * ACT), slice(9, 9 + ACT))):
        store((ao_n, ao_mn, ao_vn), at, adamw(ao[at], ao_m[at], ao_v[at], grad[row] / total))
    grad = rows(R_OUT, 8)
    held = [crit_rows[2 * at : 2 * at + 2, :] for at in range(3)]
    store((co_n, co_mn, co_vn), ..., adamw(*held, grad[0:2] / total))
    bg[:, CB2 : CB2 + HSAC] = grad[2:3]
    bg[:, CB2 + HSAC : CB2 + 2 * HSAC] = grad[3:4]
    bg[:, AB2 : AB2 + HSAC] = grad[4:5]
    grad = rows(R_MISC, 8)
    bg[:, CB3 : CB3 + 1] = grad[0:1, 16:17]
    bg[:, CB3 + 1 : CB3 + 2] = grad[0:1, 32:33]
    bg[:, AB3 : AB3 + ACT] = grad[0:1, 1 : 1 + ACT]
    bg[:, AB3 + ACT : AB3 + 2 * ACT] = grad[0:1, 9 : 9 + ACT]
    bg[:, LOGA : LOGA + 1] = -grad[0:1, 65:66]
    total_loss = grad[0:1, 64:65]
    up = jnp.zeros((1, HALF), F32)
    low = jnp.zeros((1, HALF), F32)
    for e in range(MEMBERS):
        pack = dyn_s[e]
        total_loss = total_loss + pack[D_LOSS : D_LOSS + 1, 0:1]
        up = up + pack[D_UP : D_UP + 1, 0:HALF]
        low = low + pack[D_LOW : D_LOW + 1, 0:HALF]
        bg[:, DB1 + HDYN * e : DB1 + HDYN * (e + 1)] = pack[IN : IN + 1, 0:HDYN]
        bg[:, DB2 + HDYN * e : DB2 + HDYN * (e + 1)] = pack[D_B2 : D_B2 + 1, 0:HDYN]
        bg[:, DB3 + DOUT * e : DB3 + DOUT * e + HALF] = pack[D_B3 : D_B3 + 1, 0:HALF]
        bg[:, DB3 + DOUT * e + HALF : DB3 + DOUT * (e + 1)] = pack[D_B3 : D_B3 + 1, 24 : 24 + HALF]
        grad = pack[0:IN, 0:HDYN] / total
        store((di_n, di_mn, di_vn), e, adamw(di[e], di_m[e], di_v[e], grad))
        grad = pack[D_OUT : D_OUT + DOUT, 0:HDYN] / total
        store((do_n, do_mn, do_vn), e, adamw(do[e], do_m[e], do_v[e], grad))
    bg[:, MAXLV : MAXLV + HALF] = up
    bg[:, MINLV : MINLV + HALF] = low
    lane = lax.broadcasted_iota(jnp.int32, (1, NB), 1)
    bounds = jnp.where(
        jnp.logical_and(lane >= MAXLV, lane < MINLV),
        BOUND_WEIGHT,
        jnp.where(jnp.logical_and(lane >= MINLV, lane < LOGA), -BOUND_WEIGHT, 0.0),
    )
    grad = bg[...] / total + bounds
    flat = [ref[...].reshape(1, NB) for ref in (bi, bi_m, bi_v)]
    store((bi_n, bi_mn, bi_vn), ..., [value.reshape(NB) for value in adamw(*flat, grad)])
    loss[...] = total_loss
    counted[...] = total


def shards(
    lay, replay, model_rows, requests, member_of, model_live, noise, sac_hidden, sac_hidden_mom,
    dyn_hidden, dyn_hidden_mom, crit_in, crit_in_m, crit_in_v, act_in, act_in_m, act_in_v, dyn_in,
    dyn_in_m, dyn_in_v, crit_out, crit_out_m, crit_out_v, act_out, act_out_m, act_out_v, dyn_out,
    dyn_out_m, dyn_out_v, biases, biases_m, biases_v, targ_in, targ_hidden, targ_out, targ_bias,
):
    n_dp, n_blk = lay.n_dp, lay.n_blk
    spec = pl.BlockSpec(memory_space=pltpu.VMEM)

    def flip(value):
        return jnp.transpose(value, (1, 0, 2))

    def swap(value):
        return jnp.swapaxes(value, -1, -2)

    def kept(value):
        return pltpu.with_memory_space_constraint(value, pltpu.VMEM)

    inputs = (
        sac_hidden, requests, member_of, replay, model_live, model_rows, jnp.transpose(noise, (2, 0, 1)),
        biases, flip(targ_in), flip(crit_in), act_in, targ_bias, targ_hidden, crit_out, targ_out,
        swap(act_out), dyn_hidden, dyn_hidden_mom, crit_out_m, crit_out_v, sac_hidden_mom, dyn_in,
        swap(dyn_out),
    )
    shape = jax.ShapeDtypeStruct
    rows, drows = lay.rows, lay.drows
    out_shape = (
        pltpu.VMEM((2, 3, rows // 8, 8, 128), F32),
        pltpu.VMEM((3, rows, HSAC), F32),
        pltpu.VMEM((MEMBERS, drows, HDYN), F32),
        pltpu.VMEM((MEMBERS, D_ROWS, HSAC), F32),
        pltpu.VMEM((32, 8, 128), F32),
        pltpu.VMEM((8, 128), F32),
        pltpu.VMEM((8, HSAC), F32),
    )

    def vm(*dims, kind=F32):
        return pltpu.VMEM(dims, kind)

    scratch = [
        vm(n_blk, 3, rows, HSAC, kind=BF16),
        vm(2, n_dp, CAP, kind=jnp.int32),
        vm(n_dp, 2, n_dp, CAP, kind=jnp.int32),
        vm(n_blk, drows, HDYN),
        vm(n_blk, drows, HDYN),
        vm(lay.n_dev, 48, lay.width),
        vm(56, lay.batch),
        vm(2, 8, lay.batch),
        vm(8, lay.batch),
        vm(8, lay.batch),
        vm(5, 32, HSAC),
        vm(5, HSAC, 32, kind=BF16),
        vm(2, 16, HSAC, kind=BF16),
        vm(5, HSAC, HSAC, kind=BF16),
        vm(3, HSAC, HSAC, kind=BF16),
        vm(5, 16, HSAC, kind=BF16),
        vm(HSAC, 16, kind=BF16),
        vm(16, HSAC),
        vm(8, HSAC),
        vm(7, HSAC, 128),
        vm(128, 8),
        vm(3, HSAC + 16, HSAC),
        vm(3, 32, HSAC),
        vm(2, 16, HSAC),
        vm(16, HSAC),
        vm(16, 48),
        vm(8, max(CRITIC_TILE, ACTOR_TILE)),
        *[vm(2, lay.half, chunk, 8, 128) for chunk in lay.chunks],
        *[vm(lay.half, chunk, 8, 128) for chunk in lay.chunks],
        *[vm(lay.half, chunk, 8, 128) for chunk in lay.chunks],
        *[vm(n_blk, chunk, 8, 128) for chunk in lay.chunks],
        *[vm(chunk, 8, 128) for chunk in lay.chunks],
        *[vm(chunk, 8, 128) for chunk in lay.chunks],
        vm(3, 2, lay.half, lay.mat, 8, 128),
        vm(3, HSAC, HSAC),
        vm(2, HSAC, HSAC),
        vm(HSAC, 8),
        vm(HSAC + 16, HSAC),
        vm(32, HSAC),
        vm(48, HSAC),
        vm(16, 48),
        vm(2, 24, DYN_TILE),
        vm(8, DYN_TILE),
        vm(48, DYN_TILE),
        vm(HSAC, HSAC),
        vm(D_ROWS, HSAC),
        vm(drows, HDYN),
        vm(1, NB),
        vm(48, HSAC, kind=BF16),
        vm(HSAC, 48, kind=BF16),
    ]
    scratch += [pltpu.SemaphoreType.DMA((lay.departures,)), pltpu.SemaphoreType.DMA((lay.arrivals,))]
    held = [pltpu.VMEM(value.shape, value.dtype) for value in inputs]
    held.append(pltpu.SemaphoreType.DMA((len(inputs),)))
    varying = 4 * (lay.n_dev * 48 * lay.width + 72 * lay.batch + 48 * lay.replay)
    gathered = pl.pallas_call(
        functools.partial(ordered, lay, len(inputs), len(out_shape)),
        out_shape=out_shape,
        in_specs=[pl.BlockSpec(memory_space=pl.ANY)] * len(inputs),
        out_specs=[spec] * len(out_shape),
        scratch_shapes=held + scratch,
        compiler_params=pltpu.CompilerParams(
            collective_id=0, has_side_effects=True, vmem_limit_bytes=26 * 2**20 + varying
        ),
        name="step",
    )(*[pltpu.with_memory_space_constraint(value, pltpu.HBM) for value in inputs])
    params = (
        sac_hidden, dyn_hidden, dyn_hidden_mom,
        flip(crit_in), flip(crit_in_m), flip(crit_in_v), act_in, act_in_m, act_in_v,
        dyn_in, dyn_in_m, dyn_in_v,
        swap(act_out), swap(act_out_m), swap(act_out_v),
        swap(dyn_out), swap(dyn_out_m), swap(dyn_out_v), biases, biases_m, biases_v,
    )
    new_shape = [shape(sac_hidden.shape, F32)] + [shape(value.shape, F32) for value in params[:12]]
    new_shape += [shape(crit_out.shape, F32)] * 3 + [shape(value.shape, F32) for value in params[12:]]
    new_shape += [shape((1, 1), F32)] * 2
    out = pl.pallas_call(
        functools.partial(update_kernel, lay),
        out_shape=tuple(new_shape),
        in_specs=[spec] * (len(gathered) + len(params)),
        out_specs=[spec] * len(new_shape),
        scratch_shapes=[vm(1, NB)],
        compiler_params=pltpu.CompilerParams(vmem_limit_bytes=16 * 2**20),
        name="update",
    )(*[kept(value) for value in gathered], *params)
    out = list(out)
    for at in (4, 5, 6):
        out[at] = flip(out[at])
    for at in (16, 17, 18, 19, 20, 21):
        out[at] = swap(out[at])
    for at in (25, 26):
        out[at] = out[at].reshape(())
    return tuple(out)


def solution(mesh):
    both = ("dp", "blk")
    sharded = (
        P(None, both), P(None, both), P(both, None), P(both, None), P(both), P(None, both, None),
    )
    hidden = (P(None, "blk", None),) * 4

    def step(replay, model_rows, *others):
        lay = Layout(mesh, replay.shape[1], model_rows.shape[1])
        return shards(lay, replay, model_rows, *others)

    return jax.shard_map(
        step,
        mesh=mesh,
        in_specs=sharded + hidden + (P(),) * 25,
        out_specs=hidden + (P(),) * 23,
        check_vma=False,
    )
```

```python
import functools

import jax
import jax.numpy as jnp
from jax import lax
from jax.experimental import pallas as pl
from jax.experimental.pallas import tpu as pltpu
from jax.sharding import PartitionSpec as P

OBS = 17
ACT = 6
IN = OBS + ACT
FEAT = 42
HDYN = 200
HSAC = 256
MEMBERS = 7
DOUT = 36
HALF = DOUT // 2
NB = 4639
NS_ITERS = 5
STEP = 10
CAP = 8
CRITIC_TILE = 640
ACTOR_TILE = 640
DYN_TILE = 512
ROWS = 32

DISCOUNT = 0.99
TARGET_ENTROPY = -6.0
BOUND_WEIGHT = 0.01
MOMENTUM = 0.95
MUON_RATE = 0.4
MUON_DECAY = 0.01
ADAM_RATE = 0.1
ADAM_DECAY = 0.01
BETA_FIRST = 0.9
BETA_SECOND = 0.999
COEF_LINEAR = 3.4445
COEF_CUBIC = -4.775
COEF_QUINTIC = 2.0315

CB1, CB2, CB3, AB1, AB2, AB3 = 0, 512, 1024, 1026, 1282, 1538
DB1, DB2, DB3, MAXLV, MINLV, LOGA = 1550, 2950, 4350, 4602, 4620, 4638

R_IN, R_HEAD, R_OUT, R_MISC, R_SMALL = 0, 72, 88, 96, 128
D_IN, D_OUT, D_B2, D_B3, D_UP, D_LOW, D_LOSS, D_HID, D_ROWS = 0, 24, 60, 61, 62, 63, 64, 72, 128

F32, BF16 = jnp.float32, jnp.bfloat16
MESH = pl.DeviceIdType.MESH
NN = (((1,), (0,)), ((), ()))
NT = (((1,), (1,)), ((), ()))


def dot(a, b, dims=NN):
    return lax.dot_general(a, b, dims, preferred_element_type=F32)


def rounded(v):
    return v.astype(BF16).astype(F32)


def pieces(v):
    high = v.astype(BF16)
    rest = v - high.astype(F32)
    middle = rest.astype(BF16)
    return high, middle, (rest - middle.astype(F32)).astype(BF16)


def split(v):
    high = v.astype(BF16)
    return high, (v - high.astype(F32)).astype(BF16)


def product(a, b, dims=NN, cuts=1):
    left = jnp.concatenate([a[0], a[0], a[1]], 1)
    right = jnp.concatenate([b[0], b[1], b[0]], dims[0][1][0])
    rows = left.shape[0] // cuts
    done = [dot(left[at * rows : (at + 1) * rows], right, dims) for at in range(cuts)]
    return done[0] if cuts == 1 else jnp.concatenate(done, 0)


def softplus(v):
    return jnp.maximum(v, 0.0) + jnp.log1p(jnp.exp(-jnp.abs(v)))


def sigmoid(v):
    return 0.5 + 0.5 * jnp.tanh(0.5 * v)


def gate(half):
    up = 1.0 + jnp.tanh(half)
    value = half * up
    return value, up + value * (2.0 - up)


def by_rows(body, *arrays):
    done = [
        body(*[array[at : at + ROWS] for array in arrays]) for at in range(0, arrays[0].shape[0], ROWS)
    ]
    return [jnp.concatenate(parts, 0) for parts in zip(*done)]


def spread_to(column, width):
    return jnp.concatenate([column] * (width // 128), 1)


def gated(half, column=None):
    def body(part, *offset):
        value, slope = gate(part + spread_to(offset[0], part.shape[1]) if offset else part)
        return value.astype(BF16), slope

    return by_rows(body, half, *([] if column is None else [column]))


def sloped(grad, slope):
    return by_rows(lambda part, by: ((part * by).astype(BF16),), grad, slope)[0]


def outer_sloped(column, row, slope):
    return by_rows(lambda part, by: (((spread_to(part, by.shape[1]) * row) * by).astype(BF16),), column, slope)[0]


def rows_of(shape):
    return lax.broadcasted_iota(jnp.int32, shape, 0)


def blend(gram, square):
    return split(COEF_CUBIC * gram + COEF_QUINTIC * square)


def schulz(refs, steps, before=None):
    cuts = 2 if len(refs) == 1 else 1

    @pl.loop(0, steps)
    def _(step):
        if before is not None:
            before(step)
        matrices = [ref[...] for ref in refs]
        parts = [split(matrix) for matrix in matrices]
        grams = [product(part, part, NT, cuts) for part in parts]
        halves = [split(gram) for gram in grams]
        squares = [product(half, half, NN, cuts) for half in halves]
        blends = [blend(gram, square) for gram, square in zip(grams, squares)]
        moved = [product(mix, part, NN, cuts) for mix, part in zip(blends, parts)]
        for ref, matrix, move in zip(refs, matrices, moved):
            ref[...] = COEF_LINEAR * matrix + move


def schulz_rows(refs, windows, held):
    cuts = 2 if len(refs) == 1 else 1
    parts = [split(ref[...]) for ref in refs]
    grams = [product(part, part, NT, cuts) for part in parts]
    for at, gram in enumerate(grams):
        held[at] = gram
    halves = [split(gram) for gram in grams]
    grams = [held[at, window] for at, window in enumerate(windows)]
    squares = [product(split(gram), half) for gram, half in zip(grams, halves)]
    blends = [blend(gram, square) for gram, square in zip(grams, squares)]
    moved = [product(mix, part) for mix, part in zip(blends, parts)]
    return [
        COEF_LINEAR * ref[window, :] + move for ref, window, move in zip(refs, windows, moved)
    ]


def normalise(ref):
    moment = ref[...]
    norm = jnp.sqrt(jnp.sum(jnp.sum(moment * moment, axis=1, keepdims=True), axis=0, keepdims=True))
    ref[...] = moment / (norm + 1e-7)


class Layout:
    def __init__(self, mesh, replay, model):
        self.n_dp = mesh.shape["dp"]
        self.half = self.n_dp // 2
        self.n_blk = mesh.shape["blk"]
        self.n_dev = self.n_dp * self.n_blk
        self.replay = replay
        self.model = model
        self.real = self.n_dp * CAP
        self.batch = self.real + model
        self.width = -(-(self.real + 2) // 128) * 128
        self.rows = HSAC // self.n_blk
        self.drows = HDYN // self.n_blk
        self.mat = 64 // self.n_dp
        self.sml = 32 // self.n_dp
        self.chunks = (self.mat, self.mat + self.sml, self.mat)
        groups = [(name, g) for name in ("core sum", "plane sum") for g in range(3)]
        groups += [("line sum", g) for g in range(4)]
        common = ["hidden", "hidden on", "lists", "own", "line", "plane", "dyn h", "dyn m", "small", "small on"]
        common += groups
        kinds = [(name, kind) for name in ("pack", "x") for kind in ("own", "on")]
        tiles = [(name, k) for name in ("tiles", "tiles on") for k in range(3)]
        sent = common + tiles + kinds
        self.sent = {name: at for at, name in enumerate(sent)}
        self.departures = len(sent)
        self.here, self.arrivals = {}, 0
        tiles += [("pack", "sibling"), ("x", "sibling")]
        for name in common + tiles:
            self.here[name] = self.arrivals
            self.arrivals += 1
        for name in ("pack", "x"):
            self.here[name, "like"] = self.arrivals
            self.arrivals += MEMBERS


OPERANDS = 23
FIRST, SECOND = 3, 16


def main_kernel(lay, *refs):
    n_in = OPERANDS
    sources, held = refs[:n_in], refs[n_in : 2 * n_in]
    (
        sac_h, requests, member, replay, live, model, noise, biases, targ_in, crit_in, act_in, targ_bias,
        targ_hidden, crit_out, targ_out, act_out, dyn_h, dyn_m, crit_out_m, crit_out_v, sac_m, dyn_in, dyn_out,
    ) = held
    loads = refs[2 * n_in]
    refs = refs[2 * n_in + 1 :]
    (
        sac_g, sac_x, dyn_x, dyn_s, small, count, crit_rows,
        wg, lists, asked, dhg, dmg, bk, xs, nz, ys, ahead, w1f, w1t, w1n, w2t, w2h, heads, head_t, head_f,
        rowbuf, wide, headcol, acc_h, acc_w, acc_c, acc_a, acc_m, acc_l, grid_0, grid_1, grid_2, core_0, core_1,
        core_2, from_0, from_1, from_2, zr_0, zr_1, zr_2, zf_0, zf_1, zf_2, sum_0, sum_1, sum_2, mg, mat, gram, dcols, dacc_h, dacc_w, dacc_o, dacc_m, dacc_b, dacc_l, xt, dmat,
        dpack, drow_x, bias, dhead, dhead_t, *rest,
    ) = refs
    send, recv = rest
    sent, here_at = lay.sent, lay.here
    grids, cores, froms = (grid_0, grid_1, grid_2), (core_0, core_1, core_2), (from_0, from_1, from_2)
    zrs, zfs, totals = (zr_0, zr_1, zr_2), (zf_0, zf_1, zf_2), (sum_0, sum_1, sum_2)
    n_dp, n_blk = lay.n_dp, lay.n_blk
    me = lax.axis_index("dp")
    z = lax.axis_index("blk")
    core, like = lax.rem(me, 2), me // 2
    sibling = me + 1 - 2 * core
    is_dyn = me < MEMBERS
    dyn_e = jnp.minimum(me, MEMBERS - 1)

    def on_plane(src, dst, ssem, rsem, peer):
        return pltpu.make_async_remote_copy(
            src_ref=src, dst_ref=dst, send_sem=ssem, recv_sem=rsem,
            device_id={"dp": peer}, device_id_type=MESH,
        )

    def on_line(src, dst, ssem, rsem, peer):
        return pltpu.make_async_remote_copy(
            src_ref=src, dst_ref=dst, send_sem=ssem, recv_sem=rsem,
            device_id={"blk": peer}, device_id_type=MESH,
        )

    def over(number, body):
        if number <= 8:
            for off in range(1, number):
                body(off)
        else:
            pl.loop(1, number)(body)

    def plane_peers(body):
        over(n_dp, lambda off: body(lax.rem(me + off, n_dp)))

    def like_peers(body):
        over(n_dp // 2, lambda off: body(lax.rem(me + 2 * off, n_dp)))

    def line_peers(body):
        over(n_blk, lambda off: body(lax.rem(z + off, n_blk)))

    def has_sent(view, name):
        at = send.at[sent[name]]
        on_plane(view, view, at, at, sibling).wait_send()

    def has_come(view, name):
        at = recv.at[here_at[name]]
        on_plane(view, view, at, at, sibling).wait_recv()

    copies = [
        pltpu.make_async_copy(src, dst, loads.at[at]) for at, (src, dst) in enumerate(zip(sources, held))
    ]

    def arrived(begin, end):
        for copy in copies[begin:end]:
            copy.wait()

    barrier = pltpu.get_barrier_semaphore()
    plane_peers(lambda peer: pl.semaphore_signal(barrier, inc=1, device_id={"dp": peer}, device_id_type=MESH))
    line_peers(lambda peer: pl.semaphore_signal(barrier, inc=1, device_id={"blk": peer}, device_id_type=MESH))
    for copy in copies:
        copy.start()
    arrived(0, FIRST)
    wg[0] = sac_h[...].astype(BF16)
    lists[0] = requests[...]
    lists[1] = member[...]
    pl.semaphore_wait(barrier, n_dp - 1 + n_blk - 1)

    half_rows = pl.ds(pl.multiple_of(core * (lay.rows // 2), lay.rows // 2), lay.rows // 2)

    def slot_from(owner, at):
        return lax.rem(owner - at + n_blk, n_blk)

    def hidden_copy(peer):
        src = wg.at[0, :, half_rows]
        dst = wg.at[slot_from(z, peer), :, half_rows]
        return on_line(src, dst, send.at[sent["hidden"]], recv.at[here_at["hidden"]], peer)

    def hidden_on():
        view = wg.at[pl.ds(1, n_blk - 1), :, half_rows]
        return on_plane(view, view, send.at[sent["hidden on"]], recv.at[here_at["hidden on"]], sibling)

    def list_copy(peer):
        return on_plane(lists, asked.at[me], send.at[sent["lists"]], recv.at[here_at["lists"]], peer)

    line_peers(lambda peer: hidden_copy(peer).start())
    plane_peers(lambda peer: list_copy(peer).start())
    asked[me] = lists[...]

    def dyn_h_copy(peer):
        return on_line(dyn_h.at[dyn_e], dhg.at[z], send.at[sent["dyn h"]], recv.at[here_at["dyn h"]], peer)

    def dyn_m_copy(peer):
        return on_line(dyn_m.at[dyn_e], dmg.at[z], send.at[sent["dyn m"]], recv.at[here_at["dyn m"]], peer)

    arrived(FIRST, SECOND)
    alive = live[...].astype(F32).reshape(1, lay.model)
    data = replay[...]
    sums = jnp.sum(data[0:24], axis=1, keepdims=True)
    squares = jnp.sum(data[0:24] * data[0:24], axis=1, keepdims=True)
    living = jnp.sum(alive, axis=1, keepdims=True)

    has_come(asked.at[pl.ds(0, n_dp - 1)], "lists")
    spread = (
        lax.rem(lax.broadcasted_iota(jnp.int32, (CAP, lay.real), 1), CAP)
        == lax.broadcasted_iota(jnp.int32, (CAP, lay.real), 0)
    ).astype(F32)
    here = (
        lax.broadcasted_iota(jnp.int32, (n_dp, lay.real), 1) // CAP
        == lax.broadcasted_iota(jnp.int32, (n_dp, lay.real), 0)
    )

    def in_lanes(which):
        values = asked[:, which, me, :].astype(F32)
        wide = lax.dot_general(
            values, spread, NN, precision=lax.Precision.HIGHEST, preferred_element_type=F32
        )
        return jnp.sum(jnp.where(here, wide, 0.0), axis=0, keepdims=True)

    slots = in_lanes(0)
    wanted = jnp.maximum(slots, 0.0).astype(jnp.int32)
    hot = (rows_of((lay.replay, lay.real)) == wanted).astype(BF16)
    padded = jnp.concatenate([data, jnp.zeros((48 - FEAT, lay.replay), F32)], 0)
    chosen = dot(jnp.concatenate(pieces(padded), 0), hot)
    chosen = chosen[0:48] + chosen[48:96] + chosen[96:144]
    mine = me * n_blk
    bk[mine, 0:FEAT, 0 : lay.real] = chosen[0:FEAT]
    bk[mine, 42:43, 0 : lay.real] = (slots >= 0.0).astype(F32)
    bk[mine, 43:44, 0 : lay.real] = in_lanes(1)
    bk[mine, 44:48, 0 : lay.real] = jnp.zeros((4, lay.real), F32)
    bk[mine, :, lay.real : lay.width] = jnp.zeros((48, lay.width - lay.real), F32)
    bk[mine, 0:24, lay.real : lay.real + 1] = sums
    bk[mine, 0:24, lay.real + 1 : lay.real + 2] = squares
    bk[mine, 24:25, lay.real : lay.real + 1] = living

    def slot_of(block):
        line = lax.rem(block, n_blk)
        return block - line + slot_from(line, z)

    def block_line(peer):
        dst = bk.at[me * n_blk + slot_from(z, peer)]
        return on_line(bk.at[mine], dst, send.at[sent["line"]], recv.at[here_at["line"]], peer)

    def block_own(peer):
        view = bk.at[mine]
        return on_plane(view, view, send.at[sent["own"]], recv.at[here_at["own"]], peer)

    def block_plane(peer):
        view = bk.at[pl.ds(mine + 1, n_blk - 1)]
        return on_plane(view, view, send.at[sent["plane"]], recv.at[here_at["plane"]], peer)

    plane_peers(lambda peer: block_own(peer).start())
    line_peers(lambda peer: block_line(peer).start())

    arrived(SECOND, n_in)
    crit_rows[0:2, :] = crit_out[...]
    crit_rows[2:4, :] = crit_out_m[...]
    crit_rows[4:6, :] = crit_out_v[...]
    crit_rows[6:8, :] = jnp.zeros((2, HSAC), F32)

    @pl.when(is_dyn)
    def _():
        line_peers(lambda peer: dyn_h_copy(peer).start())
        line_peers(lambda peer: dyn_m_copy(peer).start())

    bias[...] = biases[...].reshape(1, NB)
    xs[42:56, :] = jnp.zeros((14, lay.batch), F32)
    xs[0:FEAT, lay.real : lay.batch] = model[...]
    xs[42:43, lay.real : lay.batch] = alive
    nz[...] = jnp.zeros_like(nz)
    for which in range(2):
        nz[which, 1:7, :] = noise[:, which, :]
    firsts = [
        (targ_in[:, 0, :], targ_bias[0:1, 0:HSAC]),
        (targ_in[:, 1, :], targ_bias[1:2, 0:HSAC]),
        (crit_in[:, 0, :], bias[:, CB1 : CB1 + HSAC]),
        (crit_in[:, 1, :], bias[:, CB1 + HSAC : CB1 + 2 * HSAC]),
        (act_in[...], bias[:, AB1 : AB1 + HSAC]),
    ]
    w1f[...] = jnp.zeros_like(w1f)
    for net, (weights, offset) in enumerate(firsts):
        w1f[net, 0 : weights.shape[0], :] = rounded(weights)
        for at, piece in enumerate(pieces(offset)):
            w1f[net, IN + at : IN + at + 1, :] = piece.astype(F32)
        w1t[net] = (0.5 * w1f[net].T).astype(BF16)
    for k in range(2):
        w1n[k] = w1f[2 + k, 16:32, :].astype(BF16)
    for net in range(2):
        w2t[net] = (0.5 * rounded(targ_hidden[net])).T.astype(BF16)
    has_come(wg.at[pl.ds(0, n_blk - 1), :, half_rows], "hidden")
    hidden_on().start()

    rowbuf[...] = jnp.zeros_like(rowbuf)
    rowbuf[0:1, :] = targ_bias[0:1, HSAC : 2 * HSAC]
    rowbuf[1:2, :] = targ_bias[1:2, HSAC : 2 * HSAC]
    rowbuf[2:3, :] = bias[:, CB2 : CB2 + HSAC]
    rowbuf[3:4, :] = bias[:, CB2 + HSAC : CB2 + 2 * HSAC]
    rowbuf[4:5, :] = bias[:, AB2 : AB2 + HSAC]
    rowbuf[5:7, :] = rounded(crit_out[...])
    columns = 0.5 * rowbuf[...].T
    for at in range(7):
        wide[at] = jnp.broadcast_to(columns[:, at : at + 1], (HSAC, 128))
    rowbuf[...] = jnp.zeros_like(rowbuf)
    rowbuf[0:1, 1:7] = bias[:, AB3 : AB3 + ACT]
    rowbuf[0:1, 9:15] = bias[:, AB3 + ACT : AB3 + 2 * ACT]
    headcol[...] = rowbuf[:, 0:128].T
    head_f[...] = jnp.zeros_like(head_f)
    for k in range(2):
        head_f[0:1, :] = targ_out[k : k + 1, :]
        heads[k] = head_f[...].astype(BF16)
        head_f[0:1, :] = crit_out[k : k + 1, :]
        heads[2 + k] = head_f[...].astype(BF16)
    head_f[0:1, :] = jnp.zeros((1, HSAC), F32)
    head_f[1:7, :] = act_out[0:ACT, :]
    head_f[9:15, :] = act_out[ACT : 2 * ACT, :]
    heads[4] = head_f[...].astype(BF16)
    head_t[...] = (0.5 * rounded(head_f[...])).T.astype(BF16)
    for ref in (acc_h, acc_w, acc_c, acc_a, acc_m, acc_l):
        ref[...] = jnp.zeros_like(ref)

    has_come(wg.at[pl.ds(0, n_blk - 1), :, half_rows], "hidden on")
    for k in range(3):
        for block in range(n_blk):
            w2h[k, block * lay.rows : (block + 1) * lay.rows, :] = (
                0.5 * wg[slot_from(block, z), k].astype(F32)
            ).astype(BF16)
        w2t[2 + k] = w2h[k].astype(F32).T.astype(BF16)

    log_alpha = bias[:, LOGA : LOGA + 1]
    alpha = jnp.exp(log_alpha)
    last = [
        targ_bias[0:1, 2 * HSAC : 2 * HSAC + 1],
        targ_bias[1:2, 2 * HSAC : 2 * HSAC + 1],
        bias[:, CB3 : CB3 + 1],
        bias[:, CB3 + 1 : CB3 + 2],
    ]
    critic_tiles = lay.batch // CRITIC_TILE
    actor_tiles = lay.batch // ACTOR_TILE

    def act_rows(width):
        row8 = rows_of((8, width))
        return jnp.logical_and(row8 >= 1, row8 < 1 + ACT)

    def place_of(step, width):
        return pl.ds(pl.multiple_of(lax.rem(step + 1, lay.batch // width) * width, width), width)

    def ones16(width):
        return jnp.ones((16, width), BF16)

    def framed(first_row, used, where):
        row32 = rows_of((32, where.size))
        ones3 = jnp.logical_and(row32 >= IN, row32 < IN + 3).astype(F32)
        return jnp.where(row32 < used, xs[first_row : first_row + 32, where], ones3)

    def hidden(inputs, net):
        first, slope1 = gated(dot(w1t[net], inputs))
        second, slope2 = gated(dot(w2t[net], first), wide[net])
        return first, slope1, second, slope2

    def policy(inputs, which, where):
        first, slope1, second, slope2 = hidden(inputs, 4)
        out = dot(heads[4], second) + headcol[0:16, 0:1]
        bent = jnp.tanh(out[8:16])
        log_scale = -5.0 + 3.5 * (bent + 1.0)
        draw = nz[which, :, where]
        moved = jnp.exp(log_scale) * draw
        latent = out[0:8] + moved
        terms = (
            -0.5 * draw * draw
            - log_scale
            - 0.9189385
            - 2.0 * (0.6931472 - latent - softplus(-2.0 * latent))
        )
        used = act_rows(where.size)
        log_prob = jnp.sum(jnp.where(used, terms, 0.0), axis=0, keepdims=True)
        action = jnp.where(used, jnp.tanh(latent), 0.0)
        return action, log_prob, bent, moved, (first, slope1, second, slope2)

    def with_action(inputs, action):
        middle_rows = jnp.where(act_rows(action.shape[1]), action, inputs[16:24])
        return jnp.concatenate([inputs[0:16], middle_rows, inputs[24:32]], 0).astype(BF16)

    def critic(inputs, net):
        kept = hidden(inputs, net)
        value = dot(heads[net], kept[2])[0:1] + last[net]
        return value, kept

    def add_hidden(k, first, grad):
        acc_h[k] += dot(jnp.concatenate([first, ones16(grad.shape[1])], 0), grad, NT)

    has_come(bk.at[pl.ds(0, n_blk - 1)], "line")
    plane_peers(lambda peer: block_plane(peer).start())

    def critic_pass(k, now_in, where, target):
        weight = xs[42:43, where]
        value, (c1, dc1, c2, dc2) = critic(now_in, 2 + k)
        miss = value - target
        g3 = rounded(weight * miss)
        g3_rows = jnp.where(rows_of((16, CRITIC_TILE)) == 0, g3, 0.0).astype(BF16)
        acc_c[k] += dot(g3_rows, c2, NT)
        acc_m[:, 16 + 16 * k : 32 + 16 * k] += dot(ones16(CRITIC_TILE), g3_rows, NT)
        g2 = outer_sloped(wide[5 + k], g3, dc2)
        add_hidden(k, c1, g2)
        g1 = sloped(dot(w2h[k], g2), dc1)
        acc_w[k] += dot(now_in, g1, NT)
        acc_l[0:1, 0:CRITIC_TILE] += weight * (0.5 * miss * miss)

    def put_matrix(k):
        for chunk in range(n_dp):
            tile = chunk * lay.mat
            side, row = tile // 32, tile % 32
            grids[k][chunk % 2, chunk // 2, 0 : lay.mat] = acc_h[
                k, row * 8 : (row + lay.mat) * 8, side * 128 : (side + 1) * 128
            ].reshape(lay.mat, 8, 128)

    def put(row, value):
        for at in range(value.shape[0] // 8):
            for side in range(value.shape[1] // 128):
                tile = side * (R_SMALL // 8) + row // 8 + at
                chunk = tile // lay.sml
                grid_1[chunk % 2, chunk // 2, lay.mat + tile % lay.sml] = value[
                    at * 8 : at * 8 + 8, side * 128 : (side + 1) * 128
                ]

    def core_sum(group):
        name = ("core sum", group)
        return on_plane(
            grids[group].at[1 - core], cores[group], send.at[sent[name]], recv.at[here_at[name]], sibling
        )

    def plane_sum(group, peer):
        name = ("plane sum", group)
        return on_plane(
            cores[group].at[peer // 2], froms[group].at[like], send.at[sent[name]], recv.at[here_at[name]], peer
        )

    def fold_core(group):
        core_sum(group).wait_recv()
        cores[group][...] += grids[group][core]
        like_peers(lambda peer: plane_sum(group, peer).start())

    def line_part(part):
        return (1, pl.ds(lay.mat, lay.sml)) if part == 3 else (part, pl.ds(0, lay.mat))

    def line_sum(part, peer):
        group, tiles = line_part(part)
        name = ("line sum", part)
        src, dst = zfs[group].at[tiles], zrs[group].at[z, tiles]
        return on_line(src, dst, send.at[sent[name]], recv.at[here_at[name]], peer)

    def line_bytes(part):
        group, tiles = line_part(part)
        return zrs[group].at[pl.ds(0, n_blk - 1), tiles]

    first_tile = me * lay.mat
    side = first_tile // 32
    row_tile = lax.rem(first_tile, 32)
    keeper_z = row_tile * 8 // lay.rows
    local_tile = row_tile - keeper_z * (lay.rows // 8)

    def fold_plane(group):
        has_come(froms[group].at[pl.ds(0, lay.half - 1)], ("plane sum", group))
        froms[group][like] = cores[group][like]
        whole = froms[group][0]
        for at in range(1, lay.half):
            whole = whole + froms[group][at]
        zfs[group][...] = whole

        @pl.when(z == keeper_z)
        def _():
            held_rows = pl.ds(pl.multiple_of(local_tile * 8, 8), lay.mat * 8)
            held_lanes = pl.ds(pl.multiple_of(side * 128, 128), 128)
            old = sac_m[group, held_rows, held_lanes].reshape(lay.mat, 8, 128)
            zfs[group][0 : lay.mat] += (MOMENTUM * count[0:1, 0:1]).reshape(1, 1, 1) * old

        for part in (1, 3) if group == 1 else (group,):
            line_peers(lambda peer: line_sum(part, peer).start())

    def tile_copy(k, peer):
        name = ("tiles", k)
        src = totals[k].at[pl.ds(0, lay.mat)]
        return on_plane(src, mg.at[k, core, like], send.at[sent[name]], recv.at[here_at[name]], peer)

    def tiles_on(k):
        name = ("tiles on", k)
        view = mg.at[k, core]
        return on_plane(view, view, send.at[sent[name]], recv.at[here_at[name]], sibling)

    small_at = (core * lay.half + like) * lay.sml

    def small_copy(peer):
        return on_plane(
            sum_1.at[pl.ds(lay.mat, lay.sml)], small.at[pl.ds(small_at, lay.sml)],
            send.at[sent["small"]], recv.at[here_at["small"]], peer,
        )

    def small_on():
        view = small.at[pl.ds(core * lay.half * lay.sml, lay.half * lay.sml)]
        return on_plane(view, view, send.at[sent["small on"]], recv.at[here_at["small on"]], sibling)

    def fold_end(part):
        group, tiles = line_part(part)
        has_come(line_bytes(part), ("line sum", part))
        zrs[group][z, tiles] = zfs[group][tiles]
        whole = zrs[group][0, tiles]
        for block in range(1, n_blk):
            whole = whole + zrs[group][block, tiles]
        totals[group][tiles] = whole
        if part == 3:
            like_peers(lambda peer: small_copy(peer).start())
            small[pl.ds(small_at, lay.sml)] = whole
        else:
            like_peers(lambda peer: tile_copy(part, peer).start())
            mg[part, core, like] = whole

    def chain(group):
        def turn():
            has_come(mg.at[group, 0, pl.ds(0, lay.half - 1)], ("tiles", group))
            tiles_on(group).start()

        return [
            lambda: core_sum(group).start(),
            lambda: fold_core(group),
            lambda: fold_plane(group),
            lambda: fold_end(group),
            turn,
        ]

    def small_turn():
        has_come(small.at[pl.ds(0, (lay.half - 1) * lay.sml)], "small")
        small_on().start()

    chains = [chain(group) for group in range(3)]
    per = DYN_TILE // lay.real
    dyn_tiles = lay.n_dev // per

    def take(slots, step):
        for at, events in slots.items():
            @pl.when(step == at)
            def _():
                for event in events:
                    event()

    @pl.loop(0, actor_tiles)
    def _(step):
        @pl.when(step == actor_tiles - 1)
        def _():
            has_come(bk.at[pl.ds(0, n_dp - 1)], "own")
            lanes = lax.broadcasted_iota(jnp.int32, (48, lay.width), 1) // CAP

            def gather(owner, total):
                turned = pltpu.roll(
                    bk[owner * n_blk], lax.rem((owner - me) * CAP + lay.width, lay.width), axis=1
                )
                return jnp.where(lanes == owner, turned, total)

            own = lax.fori_loop(0, n_dp, gather, jnp.zeros((48, lay.width), F32))
            xs[0:48, 0 : lay.real] = own[:, 0 : lay.real]

        where = place_of(step, ACTOR_TILE)
        now_f = framed(0, IN, where)
        now_in = now_f.astype(BF16)
        weight = xs[42:43, where]
        next_action, next_prob, _, _, _ = policy(framed(24, OBS, where).astype(BF16), 1, where)
        ahead[0:8, where] = next_action
        ys[1:2, where] = next_prob
        action, log_prob, bent, moved, (a1, da1, a2, da2) = policy(now_in, 0, where)
        judged_in = with_action(now_f, action)
        loss = alpha * log_prob - log_alpha * (log_prob + TARGET_ENTROPY)
        grad_action = jnp.zeros((8, ACTOR_TILE), F32)
        used = act_rows(ACTOR_TILE)
        for k in range(2):
            judged, (_, df1, _, df2) = critic(judged_in, 2 + k)
            loss -= 0.5 * judged
            g2 = outer_sloped(wide[5 + k], -0.5 * weight, df2)
            g1 = sloped(dot(w2h[k], g2), df1)
            grad_action += dot(w1n[k], g1)[0:8]
        grad_latent = 2.0 * alpha * weight * action + grad_action * (1.0 - action * action)
        grad_scale = grad_latent * moved - alpha * weight
        grad_bent = grad_scale * 3.5 * (1.0 - bent * bent)
        g3 = jnp.concatenate(
            [jnp.where(used, grad_latent, 0.0), jnp.where(used, grad_bent, 0.0)], 0
        ).astype(BF16)
        acc_a[...] += dot(g3, a2, NT)
        acc_m[:, 0:16] += dot(ones16(ACTOR_TILE), g3, NT)
        g2 = sloped(dot(head_t[...], g3), da2)
        add_hidden(2, a1, g2)
        g1 = sloped(dot(w2h[2], g2), da1)
        acc_w[2] += dot(now_in, g1, NT)
        acc_l[1:2, 0:ACTOR_TILE] += weight * loss
        acc_l[2:3, 0:ACTOR_TILE] += weight * (log_prob + TARGET_ENTROPY)

    put_matrix(2)
    chains[2][0]()

    @pl.loop(0, critic_tiles)
    def _(step):
        if critic_tiles > 1:
            take({1: [chains[2][1]]}, step)

        where = place_of(step, CRITIC_TILE)
        now_in = framed(0, IN, where).astype(BF16)
        reward = xs[23:24, where]
        done = xs[41:42, where]
        aim_in = with_action(framed(24, OBS, where), ahead[0:8, where])
        next_prob = ys[1:2, where]
        aim = jnp.minimum(critic(aim_in, 0)[0], critic(aim_in, 1)[0])
        target = reward + DISCOUNT * (1.0 - done) * (aim - alpha * next_prob)
        ys[0:1, where] = target
        critic_pass(0, now_in, where, target)

    put_matrix(0)
    chains[0][0]()
    if critic_tiles == 1:
        chains[2][1]()

    has_come(bk.at[pl.ds(0, (n_dp - 1) * (n_blk - 1))], "plane")
    lane0 = lay.real // 128 * 128

    def add_block(at, carry):
        sides, fills = carry
        slot = slot_of(at)
        return sides + bk[slot, 0:32, lane0 : lane0 + 128], fills + bk[slot, 40:48, 0 : lay.real]

    sides, fills = lax.fori_loop(
        0, lay.n_dev, add_block, (jnp.zeros((32, 128), F32), jnp.zeros((8, lay.real), F32))
    )
    at = lay.real - lane0
    rows_all = float(lay.replay * lay.n_dev)
    centre = sides[0:24, at : at + 1] / rows_all
    scale = lax.rsqrt(sides[0:24, at + 1 : at + 2] / rows_all - centre * centre + 1e-6)
    total = sides[24:25, at : at + 1] + jnp.sum(fills[2:3, :], axis=1, keepdims=True)
    count[...] = jnp.broadcast_to(total, (8, 128))

    @pl.loop(0, critic_tiles)
    def _(step):
        slots = {0: [chains[2][2]]}
        slots.setdefault(critic_tiles - 1, []).append(chains[0][1])
        take(slots, step)
        where = place_of(step, CRITIC_TILE)
        critic_pass(1, framed(0, IN, where).astype(BF16), where, ys[0:1, where])

    put_matrix(1)
    for k in range(3):
        put(R_IN + 24 * k, acc_w[k, 0:24, :])
    put(R_HEAD, acc_a[...])
    rowbuf[0:1, :] = acc_c[0, 0:1, :]
    rowbuf[1:2, :] = acc_c[1, 0:1, :]
    for k in range(3):
        rowbuf[2 + k : 3 + k, :] = acc_h[k, HSAC : HSAC + 1, :]
    put(R_OUT, rowbuf[...])
    folded = jnp.sum(acc_l[...], axis=1, keepdims=True)
    rowbuf[...] = jnp.zeros_like(rowbuf)
    rowbuf[0:1, 0:48] = acc_m[0:1, :]
    rowbuf[0:1, 64:65] = folded[0:1] + folded[1:2]
    rowbuf[0:1, 65:66] = folded[2:3]
    put(R_MISC, rowbuf[...])
    put(R_MISC + 8, jnp.zeros((R_SMALL - R_MISC - 8, HSAC), F32))
    chains[1][0]()

    def dyn_bias(start, width):
        row = jnp.zeros((1, width), F32)
        for e in range(MEMBERS):
            row = jnp.where(me == e, bias[:, start + width * e : start + width * (e + 1)], row)
        return row

    @pl.when(is_dyn)
    def _():
        w1f[0] = jnp.zeros((32, HSAC), F32)
        w1f[0, 0:IN, 0:HDYN] = rounded(dyn_in[dyn_e])
        for at, piece in enumerate(pieces(dyn_bias(DB1, HDYN))):
            w1f[0, IN + at : IN + at + 1, 0:HDYN] = piece.astype(F32)
        w1t[0] = (0.5 * w1f[0].T).astype(BF16)
        rowbuf[...] = jnp.zeros_like(rowbuf)
        rowbuf[0:1, 0:HDYN] = dyn_bias(DB2, HDYN)
        head_row = dyn_bias(DB3, DOUT)
        rowbuf[1:2, 0:HALF] = head_row[:, 0:HALF]
        rowbuf[1:2, 24 : 24 + HALF] = head_row[:, HALF:DOUT]
        rowbuf[2:3, 0:HALF] = bias[:, MAXLV : MAXLV + HALF]
        rowbuf[3:4, 0:HALF] = bias[:, MINLV : MINLV + HALF]
        dcols[...] = rowbuf[...].T
        wide[0] = jnp.broadcast_to(0.5 * dcols[:, 0:1], (HSAC, 128))
        dpack[...] = jnp.zeros_like(dpack)
        dpack[0:HALF, 0:HDYN] = dyn_out[dyn_e, 0:HALF, :]
        dpack[24 : 24 + HALF, 0:HDYN] = dyn_out[dyn_e, HALF:DOUT, :]
        dhead[...] = dpack[0:48, :].astype(BF16)
        dhead_t[...] = (0.5 * rounded(dpack[0:48, :])).T.astype(BF16)
        dpack[...] = jnp.zeros_like(dpack)

        has_come(dhg.at[pl.ds(0, n_blk - 1)], "dyn h")
        has_come(dmg.at[pl.ds(0, n_blk - 1)], "dyn m")
        dhg[z] = dyn_h[dyn_e]
        dmg[z] = dyn_m[dyn_e]
        dmat[...] = jnp.zeros_like(dmat)
        for block in range(n_blk):
            dmat[block * lay.drows : (block + 1) * lay.drows, 0:HDYN] = 0.5 * rounded(dhg[block])
        w2h[0] = dmat[...].astype(BF16)
        w2t[0] = dmat[...].T.astype(BF16)
        for ref in (dacc_h, dacc_w, dacc_o, dacc_m, dacc_b, dacc_l):
            ref[...] = jnp.zeros_like(ref)

    in_dyn = {}
    for at, event in (
        (1, chains[0][2]), (1, chains[1][1]), (1, chains[2][3]),
        (dyn_tiles - 1, chains[1][2]), (dyn_tiles - 1, chains[2][4]),
    ):
        in_dyn.setdefault(min(at, dyn_tiles - 1), []).append(event)

    @pl.loop(0, dyn_tiles)
    def _(tile):
        take(in_dyn, tile)

        @pl.when(is_dyn)
        def _():
            for at in range(per):
                slot = slot_of(tile * per + at)
                xt[:, at * lay.real : (at + 1) * lay.real] = bk[slot, :, 0 : lay.real]
            now = xt[0:24, :]
            later = xt[24:48, :]
            row24 = rows_of((24, DYN_TILE))
            scaled = jnp.where(row24 < IN, (now - centre) * scale, 1.0)
            inputs = jnp.concatenate([scaled, (rows_of((8, DYN_TILE)) < 2).astype(F32)], 0).astype(BF16)
            first, slope1 = gated(dot(w1t[0], inputs))
            second, slope2 = gated(dot(w2t[0], first), wide[0])
            out = dot(dhead[...], second) + dcols[0:48, 1:2]
            used = row24 < HALF
            upper = dcols[0:24, 2:3]
            lower = dcols[0:24, 3:4]
            gap1 = upper - out[24:48]
            gap2 = upper - softplus(gap1) - lower
            log_var = lower + softplus(gap2)
            error = out[0:24] - jnp.where(row24 == OBS, now[23:24], later - now)
            inverse = jnp.exp(-log_var)
            weight = xt[42:43, :] * (xt[43:44, :] == me.astype(F32)).astype(F32)
            spread_term = error * error * inverse
            nll = jnp.sum(jnp.where(used, spread_term + log_var, 0.0), axis=0, keepdims=True)
            dacc_l[0:1, :] += weight * nll
            grad_mu = 2.0 * weight * error * inverse
            grad_lv = weight * (1.0 - spread_term)
            open1 = sigmoid(gap1)
            open2 = sigmoid(gap2)
            grad_lv1 = grad_lv * open2
            dacc_b[0] += jnp.where(used, grad_lv1 * (1.0 - open1), 0.0)
            dacc_b[1] += jnp.where(used, grad_lv * (1.0 - open2), 0.0)
            g3 = jnp.concatenate(
                [jnp.where(used, grad_mu, 0.0), jnp.where(used, grad_lv1 * open1, 0.0)], 0
            ).astype(BF16)
            dacc_o[...] += dot(g3, second, NT)
            dacc_m[...] += dot(ones16(DYN_TILE), g3, NT)
            g2 = sloped(dot(dhead_t[...], g3), slope2)
            dacc_h[...] += dot(jnp.concatenate([first, ones16(DYN_TILE)], 0), g2, NT)
            g1 = sloped(dot(w2h[0], g2), slope1)
            dacc_w[...] += dot(inputs, g1, NT)

    out_of = {"pack": dyn_s, "x": dyn_x}

    def member_copy(name, src, owner, kind, sem, peer):
        return on_plane(src, out_of[name].at[owner], send.at[sent[name, kind]], recv.at[sem], peer)

    def give(name, src):
        like_peers(
            lambda peer: member_copy(name, src, dyn_e, "own", here_at[name, "like"] + dyn_e, peer).start()
        )
        member_copy(name, src, dyn_e, "own", here_at[name, "sibling"], sibling).start()

    def hand_on(name):
        def body(peer):
            @pl.when(peer < MEMBERS)
            def _():
                owner = jnp.minimum(peer, MEMBERS - 1)
                view = out_of[name].at[owner]
                member_copy(name, view, owner, "on", here_at[name, "like"] + owner, sibling).wait_recv()
                member_copy(name, view, owner, "on", here_at[name, "sibling"], sibling).start()

        like_peers(body)

    even, odd = (MEMBERS + 1) // 2, MEMBERS // 2
    handed = even - core * (even - odd) - jnp.where(is_dyn, 1, 0)

    def from_sibling(name):
        for side, number in ((0, odd), (1, even)):
            @pl.when(core == side)
            def _():
                has_come(out_of[name].at[pl.ds(0, number)], (name, "sibling"))

    def gave(name):
        @pl.when(is_dyn)
        def _():
            for begin in range(0, n_dp // 2, MEMBERS):
                number = min(MEMBERS, n_dp // 2 - begin)
                has_sent(out_of[name].at[pl.ds(0, number)], (name, "own"))

        for number in (even, even - 1, even - 2):
            @pl.when(handed == number)
            def _():
                has_sent(out_of[name].at[pl.ds(0, number)], (name, "on"))

    def line_rows(ref):
        rows = ref[0 : lay.drows, 0:HDYN]
        for block in range(1, n_blk):
            rows = jnp.where(z == block, ref[block * lay.drows : (block + 1) * lay.drows, 0:HDYN], rows)
        return rows

    mine_rows = pl.ds(pl.multiple_of(z * lay.rows, lay.rows), lay.rows)
    dyn_window = pl.ds(pl.multiple_of(z * lay.drows // 8 * 8, 8), -(-(lay.drows + 7) // 8) * 8)

    def from_window(value):
        rows = value[0 : lay.drows, 0:HDYN]
        for block in range(1, n_blk):
            begin = block * lay.drows % 8
            rows = jnp.where(z == block, value[begin : begin + lay.drows, 0:HDYN], rows)
        return rows

    def take_matrix(k):
        tiles_on(k).wait_recv()
        for chunk in range(n_dp):
            tile = chunk * lay.mat
            half, row = tile // 32, tile % 32
            at = slice(row * 8, (row + lay.mat) * 8)
            piece = mg[k, chunk % 2, chunk // 2].reshape(lay.mat * 8, 128)
            mat[k, at, half * 128 : (half + 1) * 128] = piece / total
        normalise(mat.at[k])

    chains[0][3]()

    @pl.when(is_dyn)
    def _():
        dpack[D_IN : D_IN + 24, :] = dacc_w[0:24, :]
        dpack[D_OUT : D_OUT + HALF, :] = dacc_o[0:HALF, :]
        dpack[D_OUT + HALF : D_OUT + DOUT, :] = dacc_o[24 : 24 + HALF, :]
        dpack[D_B2 : D_B2 + 1, :] = dacc_h[HSAC : HSAC + 1, :]
        dpack[D_B3 : D_B3 + 1, 0:48] = dacc_m[0:1, :]
        lanes = lax.broadcasted_iota(jnp.int32, (24, 128), 1)
        bound = jnp.where(
            lanes == 0,
            jnp.sum(dacc_b[0], axis=1, keepdims=True),
            jnp.where(lanes == 1, jnp.sum(dacc_b[1], axis=1, keepdims=True), 0.0),
        )
        dpack[D_UP : D_UP + 2, 0:24] = bound.T[0:2, :]
        dpack[D_LOSS : D_LOSS + 1, 0:128] = jnp.broadcast_to(
            jnp.sum(dacc_l[0:1, :], axis=1, keepdims=True), (1, 128)
        )
        dpack[D_HID : D_HID + lay.drows, 0:HDYN] = line_rows(dacc_h)
        dyn_s[dyn_e] = dpack[...]
        give("pack", dpack)
        dmat[...] = jnp.zeros_like(dmat)
        for block in range(n_blk):
            at = slice(block * lay.drows, (block + 1) * lay.drows)
            dmat[at, 0:HDYN] = MOMENTUM * dmg[block] + dacc_h[at, 0:HDYN] / total
        normalise(dmat)

    def sum_end(step):
        @pl.when(step == 2)
        def _():
            chains[0][4]()
            chains[1][3]()

        pl.when(step == 3)(functools.partial(fold_end, 3))

    take_matrix(2)

    @pl.when(is_dyn)
    def _():
        both = [dmat, mat.at[2]]
        schulz(both, NS_ITERS - 1, sum_end)
        chains[1][4]()
        window, sac_x[2] = schulz_rows(both, [dyn_window, mine_rows], gram)
        rows = from_window(window)
        drow_x[...] = rows
        dyn_x[dyn_e] = rows
        give("x", drow_x)

    @pl.when(jnp.logical_not(is_dyn))
    def _():
        schulz([mat.at[2]], NS_ITERS - 1, sum_end)
        chains[1][4]()
        (sac_x[2],) = schulz_rows([mat.at[2]], [mine_rows], gram)

    def sent_early():
        has_sent(wg.at[pl.ds(0, n_blk - 1), :, half_rows], "hidden")
        has_sent(wg.at[pl.ds(0, n_blk - 1), :, half_rows], "hidden on")
        has_sent(asked.at[pl.ds(0, n_dp - 1)], "lists")
        has_sent(bk.at[pl.ds(0, n_dp - 1)], "own")
        has_sent(bk.at[pl.ds(0, n_blk - 1)], "line")
        has_sent(bk.at[pl.ds(0, (n_dp - 1) * (n_blk - 1))], "plane")

        @pl.when(is_dyn)
        def _():
            has_sent(dhg.at[pl.ds(0, n_blk - 1)], "dyn h")
            has_sent(dmg.at[pl.ds(0, n_blk - 1)], "dyn m")

        for group in range(3):
            core_sum(group).wait_send()
            has_sent(froms[group].at[pl.ds(0, lay.half - 1)], ("plane sum", group))
        for part in range(4):
            has_sent(line_bytes(part), ("line sum", part))

    def pass_on(step):
        pl.when(step == 1)(small_turn)
        pl.when(step == 2)(functools.partial(hand_on, "pack"))

    sent_early()
    for k in range(2):
        take_matrix(k)
    both = [mat.at[0], mat.at[1]]
    schulz(both, NS_ITERS - 1, pass_on)
    hand_on("x")
    sac_x[0], sac_x[1] = schulz_rows(both, [mine_rows, mine_rows], gram)
    for k in range(3):
        for half in range(2):
            for piece in range(lay.rows // 8 // lay.mat):
                chunk = (half * 32 + z * (lay.rows // 8)) // lay.mat + piece
                kept = mg[k, lax.rem(chunk, 2), chunk // 2]
                sac_g[half, k, piece * lay.mat : (piece + 1) * lay.mat] = kept

    small_on().wait_recv()
    from_sibling("pack")
    from_sibling("x")

    has_sent(small.at[pl.ds(0, (lay.half - 1) * lay.sml)], "small")
    small_on().wait_send()
    gave("pack")
    gave("x")

    for k in range(3):
        has_sent(mg.at[k, 0, pl.ds(0, lay.half - 1)], ("tiles", k))
        tiles_on(k).wait_send()


def ordered(lay, n_in, n_out, *refs):
    inputs, outputs, scratch = refs[:n_in], refs[n_in : n_in + n_out], refs[n_in + n_out :]
    main_kernel(lay, *inputs, *scratch[: n_in + 1], *outputs, *scratch[n_in + 1 :])


def adamw(weights, first, second, gradient):
    first = BETA_FIRST * first + (1.0 - BETA_FIRST) * gradient
    second = BETA_SECOND * second + (1.0 - BETA_SECOND) * gradient * gradient
    first_hat = first / (1.0 - BETA_FIRST**STEP)
    second_hat = second / (1.0 - BETA_SECOND**STEP)
    step = first_hat / (jnp.sqrt(second_hat) + 1e-8) + ADAM_DECAY * weights
    return weights - ADAM_RATE * step, first, second


def update_kernel(lay, *refs):
    (
        sac_g, sac_x, dyn_x, dyn_s, small, count, crit_rows, sac_h, dyn_h, dyn_m,
        ci, ci_m, ci_v, ai, ai_m, ai_v, di, di_m, di_v, ao, ao_m, ao_v,
        do, do_m, do_v, bi, bi_m, bi_v,
        sac_new, sac_mom, dyn_new, dyn_mom, ci_n, ci_mn, ci_vn, ai_n, ai_mn, ai_vn, di_n, di_mn,
        di_vn, co_n, co_mn, co_vn, ao_n, ao_mn, ao_vn, do_n, do_mn, do_vn, bi_n, bi_mn, bi_vn,
        loss, counted, bg,
    ) = refs
    total = count[0:1, 0:1]
    for k in range(3):
        for side in range(2):
            tiles = sac_g[side, k].reshape(sac_mom.shape[1], 128)
            sac_mom[k, :, side * 128 : (side + 1) * 128] = tiles / total
    sac_new[...] = sac_h[...] * (1.0 - MUON_RATE * MUON_DECAY) - MUON_RATE * sac_x[...]
    dyn_rows = dyn_s[:, D_HID : D_HID + dyn_m.shape[1], 0:HDYN]
    dyn_mom[...] = MOMENTUM * dyn_m[...] + dyn_rows / total.reshape(1, 1, 1)
    dyn_new[...] = dyn_h[...] * (1.0 - MUON_RATE * MUON_DECAY) - MUON_RATE * dyn_x[...]

    def rows(row, number):
        def tile(at):
            chunk = at // lay.sml
            return small[(chunk % 2 * lay.half + chunk // 2) * lay.sml + at % lay.sml]

        sides = []
        for side in range(2):
            at = side * (R_SMALL // 8) + row // 8
            sides.append(jnp.concatenate([tile(at + more) for more in range(-(-number // 8))], 0))
        return jnp.concatenate(sides, 1)

    def store(outs, at, values):
        for out, value in zip(outs, values):
            out[at] = value

    outs = (ci_n, ci_mn, ci_vn)
    for k in range(2):
        at = (slice(None), k, slice(None))
        grad = rows(R_IN + 24 * k, 24)
        bg[:, CB1 + HSAC * k : CB1 + HSAC * (k + 1)] = grad[IN : IN + 1]
        store(outs, at, adamw(ci[at], ci_m[at], ci_v[at], grad[0:IN] / total))
    grad = rows(R_IN + 48, 24)
    bg[:, AB1 : AB1 + HSAC] = grad[IN : IN + 1]
    store((ai_n, ai_mn, ai_vn), ..., adamw(ai[...], ai_m[...], ai_v[...], grad[0:OBS] / total))
    grad = rows(R_HEAD, 16)
    for at, row in ((slice(0, ACT), slice(1, 1 + ACT)), (slice(ACT, 2 * ACT), slice(9, 9 + ACT))):
        store((ao_n, ao_mn, ao_vn), at, adamw(ao[at], ao_m[at], ao_v[at], grad[row] / total))
    grad = rows(R_OUT, 8)
    held = [crit_rows[2 * at : 2 * at + 2, :] for at in range(3)]
    store((co_n, co_mn, co_vn), ..., adamw(*held, grad[0:2] / total))
    bg[:, CB2 : CB2 + HSAC] = grad[2:3]
    bg[:, CB2 + HSAC : CB2 + 2 * HSAC] = grad[3:4]
    bg[:, AB2 : AB2 + HSAC] = grad[4:5]
    grad = rows(R_MISC, 8)
    bg[:, CB3 : CB3 + 1] = grad[0:1, 16:17]
    bg[:, CB3 + 1 : CB3 + 2] = grad[0:1, 32:33]
    bg[:, AB3 : AB3 + ACT] = grad[0:1, 1 : 1 + ACT]
    bg[:, AB3 + ACT : AB3 + 2 * ACT] = grad[0:1, 9 : 9 + ACT]
    bg[:, LOGA : LOGA + 1] = -grad[0:1, 65:66]
    total_loss = grad[0:1, 64:65]
    up = jnp.zeros((1, HALF), F32)
    low = jnp.zeros((1, HALF), F32)
    for e in range(MEMBERS):
        pack = dyn_s[e]
        total_loss = total_loss + pack[D_LOSS : D_LOSS + 1, 0:1]
        up = up + pack[D_UP : D_UP + 1, 0:HALF]
        low = low + pack[D_LOW : D_LOW + 1, 0:HALF]
        bg[:, DB1 + HDYN * e : DB1 + HDYN * (e + 1)] = pack[IN : IN + 1, 0:HDYN]
        bg[:, DB2 + HDYN * e : DB2 + HDYN * (e + 1)] = pack[D_B2 : D_B2 + 1, 0:HDYN]
        bg[:, DB3 + DOUT * e : DB3 + DOUT * e + HALF] = pack[D_B3 : D_B3 + 1, 0:HALF]
        bg[:, DB3 + DOUT * e + HALF : DB3 + DOUT * (e + 1)] = pack[D_B3 : D_B3 + 1, 24 : 24 + HALF]
        grad = pack[0:IN, 0:HDYN] / total
        store((di_n, di_mn, di_vn), e, adamw(di[e], di_m[e], di_v[e], grad))
        grad = pack[D_OUT : D_OUT + DOUT, 0:HDYN] / total
        store((do_n, do_mn, do_vn), e, adamw(do[e], do_m[e], do_v[e], grad))
    bg[:, MAXLV : MAXLV + HALF] = up
    bg[:, MINLV : MINLV + HALF] = low
    lane = lax.broadcasted_iota(jnp.int32, (1, NB), 1)
    bounds = jnp.where(
        jnp.logical_and(lane >= MAXLV, lane < MINLV),
        BOUND_WEIGHT,
        jnp.where(jnp.logical_and(lane >= MINLV, lane < LOGA), -BOUND_WEIGHT, 0.0),
    )
    grad = bg[...] / total + bounds
    flat = [ref[...].reshape(1, NB) for ref in (bi, bi_m, bi_v)]
    store((bi_n, bi_mn, bi_vn), ..., [value.reshape(NB) for value in adamw(*flat, grad)])
    loss[...] = total_loss
    counted[...] = total


def shards(
    lay, replay, model_rows, requests, member_of, model_live, noise, sac_hidden, sac_hidden_mom,
    dyn_hidden, dyn_hidden_mom, crit_in, crit_in_m, crit_in_v, act_in, act_in_m, act_in_v, dyn_in,
    dyn_in_m, dyn_in_v, crit_out, crit_out_m, crit_out_v, act_out, act_out_m, act_out_v, dyn_out,
    dyn_out_m, dyn_out_v, biases, biases_m, biases_v, targ_in, targ_hidden, targ_out, targ_bias,
):
    n_dp, n_blk = lay.n_dp, lay.n_blk
    spec = pl.BlockSpec(memory_space=pltpu.VMEM)

    def flip(value):
        return jnp.transpose(value, (1, 0, 2))

    def swap(value):
        return jnp.swapaxes(value, -1, -2)

    def kept(value):
        return pltpu.with_memory_space_constraint(value, pltpu.VMEM)

    inputs = (
        sac_hidden, requests, member_of, replay, model_live, model_rows, jnp.transpose(noise, (2, 0, 1)),
        biases, flip(targ_in), flip(crit_in), act_in, targ_bias, targ_hidden, crit_out, targ_out,
        swap(act_out), dyn_hidden, dyn_hidden_mom, crit_out_m, crit_out_v, sac_hidden_mom, dyn_in,
        swap(dyn_out),
    )
    shape = jax.ShapeDtypeStruct
    rows, drows = lay.rows, lay.drows
    out_shape = (
        pltpu.VMEM((2, 3, rows // 8, 8, 128), F32),
        pltpu.VMEM((3, rows, HSAC), F32),
        pltpu.VMEM((MEMBERS, drows, HDYN), F32),
        pltpu.VMEM((MEMBERS, D_ROWS, HSAC), F32),
        pltpu.VMEM((32, 8, 128), F32),
        pltpu.VMEM((8, 128), F32),
        pltpu.VMEM((8, HSAC), F32),
    )

    def vm(*dims, kind=F32):
        return pltpu.VMEM(dims, kind)

    scratch = [
        vm(n_blk, 3, rows, HSAC, kind=BF16),
        vm(2, n_dp, CAP, kind=jnp.int32),
        vm(n_dp, 2, n_dp, CAP, kind=jnp.int32),
        vm(n_blk, drows, HDYN),
        vm(n_blk, drows, HDYN),
        vm(lay.n_dev, 48, lay.width),
        vm(56, lay.batch),
        vm(2, 8, lay.batch),
        vm(8, lay.batch),
        vm(8, lay.batch),
        vm(5, 32, HSAC),
        vm(5, HSAC, 32, kind=BF16),
        vm(2, 16, HSAC, kind=BF16),
        vm(5, HSAC, HSAC, kind=BF16),
        vm(3, HSAC, HSAC, kind=BF16),
        vm(5, 16, HSAC, kind=BF16),
        vm(HSAC, 16, kind=BF16),
        vm(16, HSAC),
        vm(8, HSAC),
        vm(7, HSAC, 128),
        vm(128, 8),
        vm(3, HSAC + 16, HSAC),
        vm(3, 32, HSAC),
        vm(2, 16, HSAC),
        vm(16, HSAC),
        vm(16, 48),
        vm(8, max(CRITIC_TILE, ACTOR_TILE)),
        *[vm(2, lay.half, chunk, 8, 128) for chunk in lay.chunks],
        *[vm(lay.half, chunk, 8, 128) for chunk in lay.chunks],
        *[vm(lay.half, chunk, 8, 128) for chunk in lay.chunks],
        *[vm(n_blk, chunk, 8, 128) for chunk in lay.chunks],
        *[vm(chunk, 8, 128) for chunk in lay.chunks],
        *[vm(chunk, 8, 128) for chunk in lay.chunks],
        vm(3, 2, lay.half, lay.mat, 8, 128),
        vm(3, HSAC, HSAC),
        vm(2, HSAC, HSAC),
        vm(HSAC, 8),
        vm(HSAC + 16, HSAC),
        vm(32, HSAC),
        vm(48, HSAC),
        vm(16, 48),
        vm(2, 24, DYN_TILE),
        vm(8, DYN_TILE),
        vm(48, DYN_TILE),
        vm(HSAC, HSAC),
        vm(D_ROWS, HSAC),
        vm(drows, HDYN),
        vm(1, NB),
        vm(48, HSAC, kind=BF16),
        vm(HSAC, 48, kind=BF16),
    ]
    scratch += [pltpu.SemaphoreType.DMA((lay.departures,)), pltpu.SemaphoreType.DMA((lay.arrivals,))]
    held = [pltpu.VMEM(value.shape, value.dtype) for value in inputs]
    held.append(pltpu.SemaphoreType.DMA((len(inputs),)))
    varying = 4 * (lay.n_dev * 48 * lay.width + 72 * lay.batch + 48 * lay.replay)
    gathered = pl.pallas_call(
        functools.partial(ordered, lay, len(inputs), len(out_shape)),
        out_shape=out_shape,
        in_specs=[pl.BlockSpec(memory_space=pl.ANY)] * len(inputs),
        out_specs=[spec] * len(out_shape),
        scratch_shapes=held + scratch,
        compiler_params=pltpu.CompilerParams(
            collective_id=0, has_side_effects=True, vmem_limit_bytes=26 * 2**20 + varying
        ),
        name="step",
    )(*[pltpu.with_memory_space_constraint(value, pltpu.HBM) for value in inputs])
    params = (
        sac_hidden, dyn_hidden, dyn_hidden_mom,
        flip(crit_in), flip(crit_in_m), flip(crit_in_v), act_in, act_in_m, act_in_v,
        dyn_in, dyn_in_m, dyn_in_v,
        swap(act_out), swap(act_out_m), swap(act_out_v),
        swap(dyn_out), swap(dyn_out_m), swap(dyn_out_v), biases, biases_m, biases_v,
    )
    new_shape = [shape(sac_hidden.shape, F32)] + [shape(value.shape, F32) for value in params[:12]]
    new_shape += [shape(crit_out.shape, F32)] * 3 + [shape(value.shape, F32) for value in params[12:]]
    new_shape += [shape((1, 1), F32)] * 2
    out = pl.pallas_call(
        functools.partial(update_kernel, lay),
        out_shape=tuple(new_shape),
        in_specs=[spec] * (len(gathered) + len(params)),
        out_specs=[spec] * len(new_shape),
        scratch_shapes=[vm(1, NB)],
        compiler_params=pltpu.CompilerParams(vmem_limit_bytes=16 * 2**20),
        name="update",
    )(*[kept(value) for value in gathered], *params)
    out = list(out)
    for at in (4, 5, 6):
        out[at] = flip(out[at])
    for at in (16, 17, 18, 19, 20, 21):
        out[at] = swap(out[at])
    for at in (25, 26):
        out[at] = out[at].reshape(())
    return tuple(out)


def solution(mesh):
    both = ("dp", "blk")
    sharded = (
        P(None, both), P(None, both), P(both, None), P(both, None), P(both), P(None, both, None),
    )
    hidden = (P(None, "blk", None),) * 4

    def step(replay, model_rows, *others):
        lay = Layout(mesh, replay.shape[1], model_rows.shape[1])
        return shards(lay, replay, model_rows, *others)

    return jax.shard_map(
        step,
        mesh=mesh,
        in_specs=sharded + hidden + (P(),) * 25,
        out_specs=hidden + (P(),) * 23,
        check_vma=False,
    )
```

```python
import functools

import jax
import jax.numpy as jnp
from jax import lax
from jax.experimental import pallas as pl
from jax.experimental.pallas import tpu as pltpu
from jax.sharding import PartitionSpec as P

OBS = 17
ACT = 6
IN = OBS + ACT
FEAT = 42
HDYN = 200
HSAC = 256
MEMBERS = 7
DOUT = 36
HALF = DOUT // 2
NB = 4639
NS_ITERS = 5
STEP = 10
CAP = 8
CRITIC_TILE = 640
ACTOR_TILE = 640
DYN_TILE = 512
ROWS = 16

DISCOUNT = 0.99
TARGET_ENTROPY = -6.0
BOUND_WEIGHT = 0.01
MOMENTUM = 0.95
MUON_RATE = 0.4
MUON_DECAY = 0.01
ADAM_RATE = 0.1
ADAM_DECAY = 0.01
BETA_FIRST = 0.9
BETA_SECOND = 0.999
COEF_LINEAR = 3.4445
COEF_CUBIC = -4.775
COEF_QUINTIC = 2.0315

CB1, CB2, CB3, AB1, AB2, AB3 = 0, 512, 1024, 1026, 1282, 1538
DB1, DB2, DB3, MAXLV, MINLV, LOGA = 1550, 2950, 4350, 4602, 4620, 4638

R_IN, R_HEAD, R_OUT, R_MISC, R_SMALL = 0, 72, 88, 96, 128
D_IN, D_OUT, D_B2, D_B3, D_UP, D_LOW, D_LOSS, D_HID, D_ROWS = 0, 24, 60, 61, 62, 63, 64, 72, 128

F32, BF16 = jnp.float32, jnp.bfloat16
MESH = pl.DeviceIdType.MESH
NN = (((1,), (0,)), ((), ()))
NT = (((1,), (1,)), ((), ()))


def dot(a, b, dims=NN):
    return lax.dot_general(a, b, dims, preferred_element_type=F32)


def rounded(v):
    return v.astype(BF16).astype(F32)


def pieces(v):
    high = v.astype(BF16)
    rest = v - high.astype(F32)
    middle = rest.astype(BF16)
    return high, middle, (rest - middle.astype(F32)).astype(BF16)


def split(v):
    high = v.astype(BF16)
    return high, (v - high.astype(F32)).astype(BF16)


def product(a, b, dims=NN, cuts=1):
    left = jnp.concatenate([a[0], a[0], a[1]], 1)
    right = jnp.concatenate([b[0], b[1], b[0]], dims[0][1][0])
    rows = left.shape[0] // cuts
    done = [dot(left[at * rows : (at + 1) * rows], right, dims) for at in range(cuts)]
    return done[0] if cuts == 1 else jnp.concatenate(done, 0)


def softplus(v):
    return jnp.maximum(v, 0.0) + jnp.log1p(jnp.exp(-jnp.abs(v)))


def sigmoid(v):
    return 0.5 + 0.5 * jnp.tanh(0.5 * v)


def gate(half):
    up = 1.0 + jnp.tanh(half)
    value = half * up
    return value, up + value * (2.0 - up)


def by_rows(body, *arrays):
    done = [
        body(*[array[at : at + ROWS] for array in arrays]) for at in range(0, arrays[0].shape[0], ROWS)
    ]
    return [jnp.concatenate(parts, 0) for parts in zip(*done)]


def spread_to(column, width):
    return jnp.concatenate([column] * (width // 128), 1)


def gated(half, column=None):
    def body(part, *offset):
        value, slope = gate(part + spread_to(offset[0], part.shape[1]) if offset else part)
        return value.astype(BF16), slope

    return by_rows(body, half, *([] if column is None else [column]))


def sloped(grad, slope):
    return by_rows(lambda part, by: ((part * by).astype(BF16),), grad, slope)[0]


def outer_sloped(column, row, slope):
    return by_rows(lambda part, by: (((spread_to(part, by.shape[1]) * row) * by).astype(BF16),), column, slope)[0]


def rows_of(shape):
    return lax.broadcasted_iota(jnp.int32, shape, 0)


def blend(gram, square):
    return split(COEF_CUBIC * gram + COEF_QUINTIC * square)


def schulz(refs, steps, before=None):
    cuts = 2 if len(refs) == 1 else 1

    @pl.loop(0, steps)
    def _(step):
        if before is not None:
            before(step)
        matrices = [ref[...] for ref in refs]
        parts = [split(matrix) for matrix in matrices]
        grams = [product(part, part, NT, cuts) for part in parts]
        halves = [split(gram) for gram in grams]
        squares = [product(half, half, NN, cuts) for half in halves]
        blends = [blend(gram, square) for gram, square in zip(grams, squares)]
        moved = [product(mix, part, NN, cuts) for mix, part in zip(blends, parts)]
        for ref, matrix, move in zip(refs, matrices, moved):
            ref[...] = COEF_LINEAR * matrix + move


def schulz_rows(refs, windows, held):
    cuts = 2 if len(refs) == 1 else 1
    parts = [split(ref[...]) for ref in refs]
    grams = [product(part, part, NT, cuts) for part in parts]
    for at, gram in enumerate(grams):
        held[at] = gram
    halves = [split(gram) for gram in grams]
    grams = [held[at, window] for at, window in enumerate(windows)]
    squares = [product(split(gram), half) for gram, half in zip(grams, halves)]
    blends = [blend(gram, square) for gram, square in zip(grams, squares)]
    moved = [product(mix, part) for mix, part in zip(blends, parts)]
    return [
        COEF_LINEAR * ref[window, :] + move for ref, window, move in zip(refs, windows, moved)
    ]


def normalise(ref):
    moment = ref[...]
    norm = jnp.sqrt(jnp.sum(jnp.sum(moment * moment, axis=1, keepdims=True), axis=0, keepdims=True))
    ref[...] = moment / (norm + 1e-7)


class Layout:
    def __init__(self, mesh, replay, model):
        self.n_dp = mesh.shape["dp"]
        self.half = self.n_dp // 2
        self.n_blk = mesh.shape["blk"]
        self.n_dev = self.n_dp * self.n_blk
        self.replay = replay
        self.model = model
        self.real = self.n_dp * CAP
        self.batch = self.real + model
        self.width = -(-(self.real + 2) // 128) * 128
        self.rows = HSAC // self.n_blk
        self.drows = HDYN // self.n_blk
        self.mat = 64 // self.n_dp
        self.sml = 32 // self.n_dp
        self.chunks = (self.mat, self.mat + self.sml, self.mat)
        groups = [(name, g) for name in ("core sum", "plane sum") for g in range(3)]
        groups += [("line sum", g) for g in range(4)]
        common = ["hidden", "hidden on", "lists", "own", "line", "plane", "dyn h", "dyn m", "small", "small on"]
        common += groups
        kinds = [(name, kind) for name in ("pack", "x") for kind in ("own", "on")]
        tiles = [(name, k) for name in ("tiles", "tiles on") for k in range(3)]
        sent = common + tiles + kinds
        self.sent = {name: at for at, name in enumerate(sent)}
        self.departures = len(sent)
        self.here, self.arrivals = {}, 0
        tiles += [("pack", "sibling"), ("x", "sibling")]
        for name in common + tiles:
            self.here[name] = self.arrivals
            self.arrivals += 1
        for name in ("pack", "x"):
            self.here[name, "like"] = self.arrivals
            self.arrivals += MEMBERS


OPERANDS = 23
FIRST, SECOND = 3, 16


def main_kernel(lay, *refs):
    n_in = OPERANDS
    sources, held = refs[:n_in], refs[n_in : 2 * n_in]
    (
        sac_h, requests, member, replay, live, model, noise, biases, targ_in, crit_in, act_in, targ_bias,
        targ_hidden, crit_out, targ_out, act_out, dyn_h, dyn_m, crit_out_m, crit_out_v, sac_m, dyn_in, dyn_out,
    ) = held
    loads = refs[2 * n_in]
    refs = refs[2 * n_in + 1 :]
    (
        sac_g, sac_x, dyn_x, dyn_s, small, count, crit_rows,
        wg, lists, asked, dhg, dmg, bk, xs, nz, ys, ahead, w1f, w1t, w1n, w2t, w2h, heads, head_t, head_f,
        rowbuf, wide, headcol, acc_h, acc_w, acc_c, acc_a, acc_m, acc_l, grid_0, grid_1, grid_2, core_0, core_1,
        core_2, from_0, from_1, from_2, zr_0, zr_1, zr_2, zf_0, zf_1, zf_2, sum_0, sum_1, sum_2, mg, mat, gram, dcols, dacc_h, dacc_w, dacc_o, dacc_m, dacc_b, dacc_l, xt, dmat,
        dpack, drow_x, bias, dhead, dhead_t, *rest,
    ) = refs
    send, recv = rest
    sent, here_at = lay.sent, lay.here
    grids, cores, froms = (grid_0, grid_1, grid_2), (core_0, core_1, core_2), (from_0, from_1, from_2)
    zrs, zfs, totals = (zr_0, zr_1, zr_2), (zf_0, zf_1, zf_2), (sum_0, sum_1, sum_2)
    n_dp, n_blk = lay.n_dp, lay.n_blk
    me = lax.axis_index("dp")
    z = lax.axis_index("blk")
    core, like = lax.rem(me, 2), me // 2
    sibling = me + 1 - 2 * core
    is_dyn = me < MEMBERS
    dyn_e = jnp.minimum(me, MEMBERS - 1)

    def on_plane(src, dst, ssem, rsem, peer):
        return pltpu.make_async_remote_copy(
            src_ref=src, dst_ref=dst, send_sem=ssem, recv_sem=rsem,
            device_id={"dp": peer}, device_id_type=MESH,
        )

    def on_line(src, dst, ssem, rsem, peer):
        return pltpu.make_async_remote_copy(
            src_ref=src, dst_ref=dst, send_sem=ssem, recv_sem=rsem,
            device_id={"blk": peer}, device_id_type=MESH,
        )

    def over(number, body):
        if number <= 8:
            for off in range(1, number):
                body(off)
        else:
            pl.loop(1, number)(body)

    def plane_peers(body):
        over(n_dp, lambda off: body(lax.rem(me + off, n_dp)))

    def like_peers(body):
        over(n_dp // 2, lambda off: body(lax.rem(me + 2 * off, n_dp)))

    def line_peers(body):
        over(n_blk, lambda off: body(lax.rem(z + off, n_blk)))

    def has_sent(view, name):
        at = send.at[sent[name]]
        on_plane(view, view, at, at, sibling).wait_send()

    def has_come(view, name):
        at = recv.at[here_at[name]]
        on_plane(view, view, at, at, sibling).wait_recv()

    copies = [
        pltpu.make_async_copy(src, dst, loads.at[at]) for at, (src, dst) in enumerate(zip(sources, held))
    ]

    def arrived(begin, end):
        for copy in copies[begin:end]:
            copy.wait()

    barrier = pltpu.get_barrier_semaphore()
    plane_peers(lambda peer: pl.semaphore_signal(barrier, inc=1, device_id={"dp": peer}, device_id_type=MESH))
    line_peers(lambda peer: pl.semaphore_signal(barrier, inc=1, device_id={"blk": peer}, device_id_type=MESH))
    for copy in copies:
        copy.start()
    arrived(0, FIRST)
    wg[0] = sac_h[...].astype(BF16)
    lists[0] = requests[...]
    lists[1] = member[...]
    pl.semaphore_wait(barrier, n_dp - 1 + n_blk - 1)

    half_rows = pl.ds(pl.multiple_of(core * (lay.rows // 2), lay.rows // 2), lay.rows // 2)

    def slot_from(owner, at):
        return lax.rem(owner - at + n_blk, n_blk)

    def hidden_copy(peer):
        src = wg.at[0, :, half_rows]
        dst = wg.at[slot_from(z, peer), :, half_rows]
        return on_line(src, dst, send.at[sent["hidden"]], recv.at[here_at["hidden"]], peer)

    def hidden_on():
        view = wg.at[pl.ds(1, n_blk - 1), :, half_rows]
        return on_plane(view, view, send.at[sent["hidden on"]], recv.at[here_at["hidden on"]], sibling)

    def list_copy(peer):
        return on_plane(lists, asked.at[me], send.at[sent["lists"]], recv.at[here_at["lists"]], peer)

    line_peers(lambda peer: hidden_copy(peer).start())
    plane_peers(lambda peer: list_copy(peer).start())
    asked[me] = lists[...]

    def dyn_h_copy(peer):
        return on_line(dyn_h.at[dyn_e], dhg.at[z], send.at[sent["dyn h"]], recv.at[here_at["dyn h"]], peer)

    def dyn_m_copy(peer):
        return on_line(dyn_m.at[dyn_e], dmg.at[z], send.at[sent["dyn m"]], recv.at[here_at["dyn m"]], peer)

    arrived(FIRST, SECOND)
    alive = live[...].astype(F32).reshape(1, lay.model)
    data = replay[...]
    sums = jnp.sum(data[0:24], axis=1, keepdims=True)
    squares = jnp.sum(data[0:24] * data[0:24], axis=1, keepdims=True)
    living = jnp.sum(alive, axis=1, keepdims=True)

    has_come(asked.at[pl.ds(0, n_dp - 1)], "lists")
    spread = (
        lax.rem(lax.broadcasted_iota(jnp.int32, (CAP, lay.real), 1), CAP)
        == lax.broadcasted_iota(jnp.int32, (CAP, lay.real), 0)
    ).astype(F32)
    here = (
        lax.broadcasted_iota(jnp.int32, (n_dp, lay.real), 1) // CAP
        == lax.broadcasted_iota(jnp.int32, (n_dp, lay.real), 0)
    )

    def in_lanes(which):
        values = asked[:, which, me, :].astype(F32)
        wide = lax.dot_general(
            values, spread, NN, precision=lax.Precision.HIGHEST, preferred_element_type=F32
        )
        return jnp.sum(jnp.where(here, wide, 0.0), axis=0, keepdims=True)

    slots = in_lanes(0)
    wanted = jnp.maximum(slots, 0.0).astype(jnp.int32)
    hot = (rows_of((lay.replay, lay.real)) == wanted).astype(BF16)
    padded = jnp.concatenate([data, jnp.zeros((48 - FEAT, lay.replay), F32)], 0)
    chosen = dot(jnp.concatenate(pieces(padded), 0), hot)
    chosen = chosen[0:48] + chosen[48:96] + chosen[96:144]
    mine = me * n_blk
    bk[mine, 0:FEAT, 0 : lay.real] = chosen[0:FEAT]
    bk[mine, 42:43, 0 : lay.real] = (slots >= 0.0).astype(F32)
    bk[mine, 43:44, 0 : lay.real] = in_lanes(1)
    bk[mine, 44:48, 0 : lay.real] = jnp.zeros((4, lay.real), F32)
    bk[mine, :, lay.real : lay.width] = jnp.zeros((48, lay.width - lay.real), F32)
    bk[mine, 0:24, lay.real : lay.real + 1] = sums
    bk[mine, 0:24, lay.real + 1 : lay.real + 2] = squares
    bk[mine, 24:25, lay.real : lay.real + 1] = living

    def slot_of(block):
        line = lax.rem(block, n_blk)
        return block - line + slot_from(line, z)

    def block_line(peer):
        dst = bk.at[me * n_blk + slot_from(z, peer)]
        return on_line(bk.at[mine], dst, send.at[sent["line"]], recv.at[here_at["line"]], peer)

    def block_own(peer):
        view = bk.at[mine]
        return on_plane(view, view, send.at[sent["own"]], recv.at[here_at["own"]], peer)

    def block_plane(peer):
        view = bk.at[pl.ds(mine + 1, n_blk - 1)]
        return on_plane(view, view, send.at[sent["plane"]], recv.at[here_at["plane"]], peer)

    plane_peers(lambda peer: block_own(peer).start())
    line_peers(lambda peer: block_line(peer).start())

    arrived(SECOND, n_in)
    crit_rows[0:2, :] = crit_out[...]
    crit_rows[2:4, :] = crit_out_m[...]
    crit_rows[4:6, :] = crit_out_v[...]
    crit_rows[6:8, :] = jnp.zeros((2, HSAC), F32)

    @pl.when(is_dyn)
    def _():
        line_peers(lambda peer: dyn_h_copy(peer).start())
        line_peers(lambda peer: dyn_m_copy(peer).start())

    bias[...] = biases[...].reshape(1, NB)
    xs[42:56, :] = jnp.zeros((14, lay.batch), F32)
    xs[0:FEAT, lay.real : lay.batch] = model[...]
    xs[42:43, lay.real : lay.batch] = alive
    nz[...] = jnp.zeros_like(nz)
    for which in range(2):
        nz[which, 1:7, :] = noise[:, which, :]
    firsts = [
        (targ_in[:, 0, :], targ_bias[0:1, 0:HSAC]),
        (targ_in[:, 1, :], targ_bias[1:2, 0:HSAC]),
        (crit_in[:, 0, :], bias[:, CB1 : CB1 + HSAC]),
        (crit_in[:, 1, :], bias[:, CB1 + HSAC : CB1 + 2 * HSAC]),
        (act_in[...], bias[:, AB1 : AB1 + HSAC]),
    ]
    w1f[...] = jnp.zeros_like(w1f)
    for net, (weights, offset) in enumerate(firsts):
        w1f[net, 0 : weights.shape[0], :] = rounded(weights)
        for at, piece in enumerate(pieces(offset)):
            w1f[net, IN + at : IN + at + 1, :] = piece.astype(F32)
        w1t[net] = (0.5 * w1f[net].T).astype(BF16)
    for k in range(2):
        w1n[k] = w1f[2 + k, 16:32, :].astype(BF16)
    for net in range(2):
        w2t[net] = (0.5 * rounded(targ_hidden[net])).T.astype(BF16)
    has_come(wg.at[pl.ds(0, n_blk - 1), :, half_rows], "hidden")
    hidden_on().start()

    rowbuf[...] = jnp.zeros_like(rowbuf)
    rowbuf[0:1, :] = targ_bias[0:1, HSAC : 2 * HSAC]
    rowbuf[1:2, :] = targ_bias[1:2, HSAC : 2 * HSAC]
    rowbuf[2:3, :] = bias[:, CB2 : CB2 + HSAC]
    rowbuf[3:4, :] = bias[:, CB2 + HSAC : CB2 + 2 * HSAC]
    rowbuf[4:5, :] = bias[:, AB2 : AB2 + HSAC]
    rowbuf[5:7, :] = rounded(crit_out[...])
    columns = 0.5 * rowbuf[...].T
    for at in range(7):
        wide[at] = jnp.broadcast_to(columns[:, at : at + 1], (HSAC, 128))
    rowbuf[...] = jnp.zeros_like(rowbuf)
    rowbuf[0:1, 1:7] = bias[:, AB3 : AB3 + ACT]
    rowbuf[0:1, 9:15] = bias[:, AB3 + ACT : AB3 + 2 * ACT]
    headcol[...] = rowbuf[:, 0:128].T
    head_f[...] = jnp.zeros_like(head_f)
    for k in range(2):
        head_f[0:1, :] = targ_out[k : k + 1, :]
        heads[k] = head_f[...].astype(BF16)
        head_f[0:1, :] = crit_out[k : k + 1, :]
        heads[2 + k] = head_f[...].astype(BF16)
    head_f[0:1, :] = jnp.zeros((1, HSAC), F32)
    head_f[1:7, :] = act_out[0:ACT, :]
    head_f[9:15, :] = act_out[ACT : 2 * ACT, :]
    heads[4] = head_f[...].astype(BF16)
    head_t[...] = (0.5 * rounded(head_f[...])).T.astype(BF16)
    for ref in (acc_h, acc_w, acc_c, acc_a, acc_m, acc_l):
        ref[...] = jnp.zeros_like(ref)

    has_come(wg.at[pl.ds(0, n_blk - 1), :, half_rows], "hidden on")
    for k in range(3):
        for block in range(n_blk):
            w2h[k, block * lay.rows : (block + 1) * lay.rows, :] = (
                0.5 * wg[slot_from(block, z), k].astype(F32)
            ).astype(BF16)
        w2t[2 + k] = w2h[k].astype(F32).T.astype(BF16)

    log_alpha = bias[:, LOGA : LOGA + 1]
    alpha = jnp.exp(log_alpha)
    last = [
        targ_bias[0:1, 2 * HSAC : 2 * HSAC + 1],
        targ_bias[1:2, 2 * HSAC : 2 * HSAC + 1],
        bias[:, CB3 : CB3 + 1],
        bias[:, CB3 + 1 : CB3 + 2],
    ]
    critic_tiles = lay.batch // CRITIC_TILE
    actor_tiles = lay.batch // ACTOR_TILE

    def act_rows(width):
        row8 = rows_of((8, width))
        return jnp.logical_and(row8 >= 1, row8 < 1 + ACT)

    def place_of(step, width):
        return pl.ds(pl.multiple_of(lax.rem(step + 1, lay.batch // width) * width, width), width)

    def ones16(width):
        return jnp.ones((16, width), BF16)

    def framed(first_row, used, where):
        row32 = rows_of((32, where.size))
        ones3 = jnp.logical_and(row32 >= IN, row32 < IN + 3).astype(F32)
        return jnp.where(row32 < used, xs[first_row : first_row + 32, where], ones3)

    def hidden(inputs, net):
        first, slope1 = gated(dot(w1t[net], inputs))
        second, slope2 = gated(dot(w2t[net], first), wide[net])
        return first, slope1, second, slope2

    def policy(inputs, which, where):
        first, slope1, second, slope2 = hidden(inputs, 4)
        out = dot(heads[4], second) + headcol[0:16, 0:1]
        bent = jnp.tanh(out[8:16])
        log_scale = -5.0 + 3.5 * (bent + 1.0)
        draw = nz[which, :, where]
        moved = jnp.exp(log_scale) * draw
        latent = out[0:8] + moved
        terms = (
            -0.5 * draw * draw
            - log_scale
            - 0.9189385
            - 2.0 * (0.6931472 - latent - softplus(-2.0 * latent))
        )
        used = act_rows(where.size)
        log_prob = jnp.sum(jnp.where(used, terms, 0.0), axis=0, keepdims=True)
        action = jnp.where(used, jnp.tanh(latent), 0.0)
        return action, log_prob, bent, moved, (first, slope1, second, slope2)

    def with_action(inputs, action):
        middle_rows = jnp.where(act_rows(action.shape[1]), action, inputs[16:24])
        return jnp.concatenate([inputs[0:16], middle_rows, inputs[24:32]], 0).astype(BF16)

    def critic(inputs, net):
        kept = hidden(inputs, net)
        value = dot(heads[net], kept[2])[0:1] + last[net]
        return value, kept

    def add_hidden(k, first, grad):
        acc_h[k] += dot(jnp.concatenate([first, ones16(grad.shape[1])], 0), grad, NT)

    has_come(bk.at[pl.ds(0, n_blk - 1)], "line")
    plane_peers(lambda peer: block_plane(peer).start())

    def critic_pass(k, now_in, where, target):
        weight = xs[42:43, where]
        value, (c1, dc1, c2, dc2) = critic(now_in, 2 + k)
        miss = value - target
        g3 = rounded(weight * miss)
        g3_rows = jnp.where(rows_of((16, CRITIC_TILE)) == 0, g3, 0.0).astype(BF16)
        acc_c[k] += dot(g3_rows, c2, NT)
        acc_m[:, 16 + 16 * k : 32 + 16 * k] += dot(ones16(CRITIC_TILE), g3_rows, NT)
        g2 = outer_sloped(wide[5 + k], g3, dc2)
        add_hidden(k, c1, g2)
        g1 = sloped(dot(w2h[k], g2), dc1)
        acc_w[k] += dot(now_in, g1, NT)
        acc_l[0:1, 0:CRITIC_TILE] += weight * (0.5 * miss * miss)

    def put_matrix(k):
        for chunk in range(n_dp):
            tile = chunk * lay.mat
            side, row = tile // 32, tile % 32
            grids[k][chunk % 2, chunk // 2, 0 : lay.mat] = acc_h[
                k, row * 8 : (row + lay.mat) * 8, side * 128 : (side + 1) * 128
            ].reshape(lay.mat, 8, 128)

    def put(row, value):
        for at in range(value.shape[0] // 8):
            for side in range(value.shape[1] // 128):
                tile = side * (R_SMALL // 8) + row // 8 + at
                chunk = tile // lay.sml
                grid_1[chunk % 2, chunk // 2, lay.mat + tile % lay.sml] = value[
                    at * 8 : at * 8 + 8, side * 128 : (side + 1) * 128
                ]

    def core_sum(group):
        name = ("core sum", group)
        return on_plane(
            grids[group].at[1 - core], cores[group], send.at[sent[name]], recv.at[here_at[name]], sibling
        )

    def plane_sum(group, peer):
        name = ("plane sum", group)
        return on_plane(
            cores[group].at[peer // 2], froms[group].at[like], send.at[sent[name]], recv.at[here_at[name]], peer
        )

    def fold_core(group):
        core_sum(group).wait_recv()
        cores[group][...] += grids[group][core]
        like_peers(lambda peer: plane_sum(group, peer).start())

    def line_part(part):
        return (1, pl.ds(lay.mat, lay.sml)) if part == 3 else (part, pl.ds(0, lay.mat))

    def line_sum(part, peer):
        group, tiles = line_part(part)
        name = ("line sum", part)
        src, dst = zfs[group].at[tiles], zrs[group].at[z, tiles]
        return on_line(src, dst, send.at[sent[name]], recv.at[here_at[name]], peer)

    def line_bytes(part):
        group, tiles = line_part(part)
        return zrs[group].at[pl.ds(0, n_blk - 1), tiles]

    first_tile = me * lay.mat
    side = first_tile // 32
    row_tile = lax.rem(first_tile, 32)
    keeper_z = row_tile * 8 // lay.rows
    local_tile = row_tile - keeper_z * (lay.rows // 8)

    def fold_plane(group):
        has_come(froms[group].at[pl.ds(0, lay.half - 1)], ("plane sum", group))
        froms[group][like] = cores[group][like]
        whole = froms[group][0]
        for at in range(1, lay.half):
            whole = whole + froms[group][at]
        zfs[group][...] = whole

        @pl.when(z == keeper_z)
        def _():
            held_rows = pl.ds(pl.multiple_of(local_tile * 8, 8), lay.mat * 8)
            held_lanes = pl.ds(pl.multiple_of(side * 128, 128), 128)
            old = sac_m[group, held_rows, held_lanes].reshape(lay.mat, 8, 128)
            zfs[group][0 : lay.mat] += (MOMENTUM * count[0:1, 0:1]).reshape(1, 1, 1) * old

        for part in (1, 3) if group == 1 else (group,):
            line_peers(lambda peer: line_sum(part, peer).start())

    def tile_copy(k, peer):
        name = ("tiles", k)
        src = totals[k].at[pl.ds(0, lay.mat)]
        return on_plane(src, mg.at[k, core, like], send.at[sent[name]], recv.at[here_at[name]], peer)

    def tiles_on(k):
        name = ("tiles on", k)
        view = mg.at[k, core]
        return on_plane(view, view, send.at[sent[name]], recv.at[here_at[name]], sibling)

    small_at = (core * lay.half + like) * lay.sml

    def small_copy(peer):
        return on_plane(
            sum_1.at[pl.ds(lay.mat, lay.sml)], small.at[pl.ds(small_at, lay.sml)],
            send.at[sent["small"]], recv.at[here_at["small"]], peer,
        )

    def small_on():
        view = small.at[pl.ds(core * lay.half * lay.sml, lay.half * lay.sml)]
        return on_plane(view, view, send.at[sent["small on"]], recv.at[here_at["small on"]], sibling)

    def fold_end(part):
        group, tiles = line_part(part)
        has_come(line_bytes(part), ("line sum", part))
        zrs[group][z, tiles] = zfs[group][tiles]
        whole = zrs[group][0, tiles]
        for block in range(1, n_blk):
            whole = whole + zrs[group][block, tiles]
        totals[group][tiles] = whole
        if part == 3:
            like_peers(lambda peer: small_copy(peer).start())
            small[pl.ds(small_at, lay.sml)] = whole
        else:
            like_peers(lambda peer: tile_copy(part, peer).start())
            mg[part, core, like] = whole

    def chain(group):
        def end():
            for part in (1, 3) if group == 1 else (group,):
                fold_end(part)

        def turn():
            has_come(mg.at[group, 0, pl.ds(0, lay.half - 1)], ("tiles", group))
            tiles_on(group).start()
            if group == 1:
                has_come(small.at[pl.ds(0, (lay.half - 1) * lay.sml)], "small")
                small_on().start()

        return [
            lambda: core_sum(group).start(),
            lambda: fold_core(group),
            lambda: fold_plane(group),
            end,
            turn,
        ]

    chains = [chain(group) for group in range(3)]
    per = DYN_TILE // lay.real
    dyn_tiles = lay.n_dev // per

    def take(slots, step):
        for at, events in slots.items():
            @pl.when(step == at)
            def _():
                for event in events:
                    event()

    @pl.loop(0, actor_tiles)
    def _(step):
        @pl.when(step == actor_tiles - 1)
        def _():
            has_come(bk.at[pl.ds(0, n_dp - 1)], "own")
            lanes = lax.broadcasted_iota(jnp.int32, (48, lay.width), 1) // CAP

            def gather(owner, total):
                turned = pltpu.roll(
                    bk[owner * n_blk], lax.rem((owner - me) * CAP + lay.width, lay.width), axis=1
                )
                return jnp.where(lanes == owner, turned, total)

            own = lax.fori_loop(0, n_dp, gather, jnp.zeros((48, lay.width), F32))
            xs[0:48, 0 : lay.real] = own[:, 0 : lay.real]

        where = place_of(step, ACTOR_TILE)
        now_f = framed(0, IN, where)
        now_in = now_f.astype(BF16)
        weight = xs[42:43, where]
        next_action, next_prob, _, _, _ = policy(framed(24, OBS, where).astype(BF16), 1, where)
        ahead[0:8, where] = next_action
        ys[1:2, where] = next_prob
        action, log_prob, bent, moved, (a1, da1, a2, da2) = policy(now_in, 0, where)
        judged_in = with_action(now_f, action)
        loss = alpha * log_prob - log_alpha * (log_prob + TARGET_ENTROPY)
        grad_action = jnp.zeros((8, ACTOR_TILE), F32)
        used = act_rows(ACTOR_TILE)
        for k in range(2):
            judged, (_, df1, _, df2) = critic(judged_in, 2 + k)
            loss -= 0.5 * judged
            g2 = outer_sloped(wide[5 + k], -0.5 * weight, df2)
            g1 = sloped(dot(w2h[k], g2), df1)
            grad_action += dot(w1n[k], g1)[0:8]
        grad_latent = 2.0 * alpha * weight * action + grad_action * (1.0 - action * action)
        grad_scale = grad_latent * moved - alpha * weight
        grad_bent = grad_scale * 3.5 * (1.0 - bent * bent)
        g3 = jnp.concatenate(
            [jnp.where(used, grad_latent, 0.0), jnp.where(used, grad_bent, 0.0)], 0
        ).astype(BF16)
        acc_a[...] += dot(g3, a2, NT)
        acc_m[:, 0:16] += dot(ones16(ACTOR_TILE), g3, NT)
        g2 = sloped(dot(head_t[...], g3), da2)
        add_hidden(2, a1, g2)
        g1 = sloped(dot(w2h[2], g2), da1)
        acc_w[2] += dot(now_in, g1, NT)
        acc_l[1:2, 0:ACTOR_TILE] += weight * loss
        acc_l[2:3, 0:ACTOR_TILE] += weight * (log_prob + TARGET_ENTROPY)

    put_matrix(2)
    chains[2][0]()

    @pl.loop(0, critic_tiles)
    def _(step):
        if critic_tiles > 1:
            take({1: [chains[2][1]]}, step)

        where = place_of(step, CRITIC_TILE)
        now_in = framed(0, IN, where).astype(BF16)
        reward = xs[23:24, where]
        done = xs[41:42, where]
        aim_in = with_action(framed(24, OBS, where), ahead[0:8, where])
        next_prob = ys[1:2, where]
        aim = jnp.minimum(critic(aim_in, 0)[0], critic(aim_in, 1)[0])
        target = reward + DISCOUNT * (1.0 - done) * (aim - alpha * next_prob)
        ys[0:1, where] = target
        critic_pass(0, now_in, where, target)

    put_matrix(0)
    chains[0][0]()
    if critic_tiles == 1:
        chains[2][1]()

    has_come(bk.at[pl.ds(0, (n_dp - 1) * (n_blk - 1))], "plane")
    lane0 = lay.real // 128 * 128

    def add_block(at, carry):
        sides, fills = carry
        slot = slot_of(at)
        return sides + bk[slot, 0:32, lane0 : lane0 + 128], fills + bk[slot, 40:48, 0 : lay.real]

    sides, fills = lax.fori_loop(
        0, lay.n_dev, add_block, (jnp.zeros((32, 128), F32), jnp.zeros((8, lay.real), F32))
    )
    at = lay.real - lane0
    rows_all = float(lay.replay * lay.n_dev)
    centre = sides[0:24, at : at + 1] / rows_all
    scale = lax.rsqrt(sides[0:24, at + 1 : at + 2] / rows_all - centre * centre + 1e-6)
    total = sides[24:25, at : at + 1] + jnp.sum(fills[2:3, :], axis=1, keepdims=True)
    count[...] = jnp.broadcast_to(total, (8, 128))

    @pl.loop(0, critic_tiles)
    def _(step):
        take({critic_tiles - 1: [chains[0][1], chains[2][2]]}, step)
        where = place_of(step, CRITIC_TILE)
        critic_pass(1, framed(0, IN, where).astype(BF16), where, ys[0:1, where])

    put_matrix(1)
    for k in range(3):
        put(R_IN + 24 * k, acc_w[k, 0:24, :])
    put(R_HEAD, acc_a[...])
    rowbuf[0:1, :] = acc_c[0, 0:1, :]
    rowbuf[1:2, :] = acc_c[1, 0:1, :]
    for k in range(3):
        rowbuf[2 + k : 3 + k, :] = acc_h[k, HSAC : HSAC + 1, :]
    put(R_OUT, rowbuf[...])
    folded = jnp.sum(acc_l[...], axis=1, keepdims=True)
    rowbuf[...] = jnp.zeros_like(rowbuf)
    rowbuf[0:1, 0:48] = acc_m[0:1, :]
    rowbuf[0:1, 64:65] = folded[0:1] + folded[1:2]
    rowbuf[0:1, 65:66] = folded[2:3]
    put(R_MISC, rowbuf[...])
    put(R_MISC + 8, jnp.zeros((R_SMALL - R_MISC - 8, HSAC), F32))
    chains[1][0]()

    def dyn_bias(start, width):
        row = jnp.zeros((1, width), F32)
        for e in range(MEMBERS):
            row = jnp.where(me == e, bias[:, start + width * e : start + width * (e + 1)], row)
        return row

    @pl.when(is_dyn)
    def _():
        w1f[0] = jnp.zeros((32, HSAC), F32)
        w1f[0, 0:IN, 0:HDYN] = rounded(dyn_in[dyn_e])
        for at, piece in enumerate(pieces(dyn_bias(DB1, HDYN))):
            w1f[0, IN + at : IN + at + 1, 0:HDYN] = piece.astype(F32)
        w1t[0] = (0.5 * w1f[0].T).astype(BF16)
        rowbuf[...] = jnp.zeros_like(rowbuf)
        rowbuf[0:1, 0:HDYN] = dyn_bias(DB2, HDYN)
        head_row = dyn_bias(DB3, DOUT)
        rowbuf[1:2, 0:HALF] = head_row[:, 0:HALF]
        rowbuf[1:2, 24 : 24 + HALF] = head_row[:, HALF:DOUT]
        rowbuf[2:3, 0:HALF] = bias[:, MAXLV : MAXLV + HALF]
        rowbuf[3:4, 0:HALF] = bias[:, MINLV : MINLV + HALF]
        dcols[...] = rowbuf[...].T
        wide[0] = jnp.broadcast_to(0.5 * dcols[:, 0:1], (HSAC, 128))
        dpack[...] = jnp.zeros_like(dpack)
        dpack[0:HALF, 0:HDYN] = dyn_out[dyn_e, 0:HALF, :]
        dpack[24 : 24 + HALF, 0:HDYN] = dyn_out[dyn_e, HALF:DOUT, :]
        dhead[...] = dpack[0:48, :].astype(BF16)
        dhead_t[...] = (0.5 * rounded(dpack[0:48, :])).T.astype(BF16)
        dpack[...] = jnp.zeros_like(dpack)

        has_come(dhg.at[pl.ds(0, n_blk - 1)], "dyn h")
        has_come(dmg.at[pl.ds(0, n_blk - 1)], "dyn m")
        dhg[z] = dyn_h[dyn_e]
        dmg[z] = dyn_m[dyn_e]
        dmat[...] = jnp.zeros_like(dmat)
        for block in range(n_blk):
            dmat[block * lay.drows : (block + 1) * lay.drows, 0:HDYN] = 0.5 * rounded(dhg[block])
        w2h[0] = dmat[...].astype(BF16)
        w2t[0] = dmat[...].T.astype(BF16)
        for ref in (dacc_h, dacc_w, dacc_o, dacc_m, dacc_b, dacc_l):
            ref[...] = jnp.zeros_like(ref)

    in_dyn = {}
    for at, event in (
        (1, chains[0][2]), (1, chains[1][1]), (2, chains[2][3]), (dyn_tiles - 1, chains[1][2]),
    ):
        in_dyn.setdefault(min(at, dyn_tiles - 1), []).append(event)

    @pl.loop(0, dyn_tiles)
    def _(tile):
        take(in_dyn, tile)

        @pl.when(is_dyn)
        def _():
            for at in range(per):
                slot = slot_of(tile * per + at)
                xt[:, at * lay.real : (at + 1) * lay.real] = bk[slot, :, 0 : lay.real]
            now = xt[0:24, :]
            later = xt[24:48, :]
            row24 = rows_of((24, DYN_TILE))
            scaled = jnp.where(row24 < IN, (now - centre) * scale, 1.0)
            inputs = jnp.concatenate([scaled, (rows_of((8, DYN_TILE)) < 2).astype(F32)], 0).astype(BF16)
            first, slope1 = gated(dot(w1t[0], inputs))
            second, slope2 = gated(dot(w2t[0], first), wide[0])
            out = dot(dhead[...], second) + dcols[0:48, 1:2]
            used = row24 < HALF
            upper = dcols[0:24, 2:3]
            lower = dcols[0:24, 3:4]
            gap1 = upper - out[24:48]
            gap2 = upper - softplus(gap1) - lower
            log_var = lower + softplus(gap2)
            error = out[0:24] - jnp.where(row24 == OBS, now[23:24], later - now)
            inverse = jnp.exp(-log_var)
            weight = xt[42:43, :] * (xt[43:44, :] == me.astype(F32)).astype(F32)
            spread_term = error * error * inverse
            nll = jnp.sum(jnp.where(used, spread_term + log_var, 0.0), axis=0, keepdims=True)
            dacc_l[0:1, :] += weight * nll
            grad_mu = 2.0 * weight * error * inverse
            grad_lv = weight * (1.0 - spread_term)
            open1 = sigmoid(gap1)
            open2 = sigmoid(gap2)
            grad_lv1 = grad_lv * open2
            dacc_b[0] += jnp.where(used, grad_lv1 * (1.0 - open1), 0.0)
            dacc_b[1] += jnp.where(used, grad_lv * (1.0 - open2), 0.0)
            g3 = jnp.concatenate(
                [jnp.where(used, grad_mu, 0.0), jnp.where(used, grad_lv1 * open1, 0.0)], 0
            ).astype(BF16)
            dacc_o[...] += dot(g3, second, NT)
            dacc_m[...] += dot(ones16(DYN_TILE), g3, NT)
            g2 = sloped(dot(dhead_t[...], g3), slope2)
            dacc_h[...] += dot(jnp.concatenate([first, ones16(DYN_TILE)], 0), g2, NT)
            g1 = sloped(dot(w2h[0], g2), slope1)
            dacc_w[...] += dot(inputs, g1, NT)

    out_of = {"pack": dyn_s, "x": dyn_x}

    def member_copy(name, src, owner, kind, sem, peer):
        return on_plane(src, out_of[name].at[owner], send.at[sent[name, kind]], recv.at[sem], peer)

    def give(name, src):
        like_peers(
            lambda peer: member_copy(name, src, dyn_e, "own", here_at[name, "like"] + dyn_e, peer).start()
        )
        member_copy(name, src, dyn_e, "own", here_at[name, "sibling"], sibling).start()

    def hand_on(name):
        def body(peer):
            @pl.when(peer < MEMBERS)
            def _():
                owner = jnp.minimum(peer, MEMBERS - 1)
                view = out_of[name].at[owner]
                member_copy(name, view, owner, "on", here_at[name, "like"] + owner, sibling).wait_recv()
                member_copy(name, view, owner, "on", here_at[name, "sibling"], sibling).start()

        like_peers(body)

    even, odd = (MEMBERS + 1) // 2, MEMBERS // 2
    handed = even - core * (even - odd) - jnp.where(is_dyn, 1, 0)

    def from_sibling(name):
        for side, number in ((0, odd), (1, even)):
            @pl.when(core == side)
            def _():
                has_come(out_of[name].at[pl.ds(0, number)], (name, "sibling"))

    def gave(name):
        @pl.when(is_dyn)
        def _():
            for begin in range(0, n_dp // 2, MEMBERS):
                number = min(MEMBERS, n_dp // 2 - begin)
                has_sent(out_of[name].at[pl.ds(0, number)], (name, "own"))

        for number in (even, even - 1, even - 2):
            @pl.when(handed == number)
            def _():
                has_sent(out_of[name].at[pl.ds(0, number)], (name, "on"))

    def line_rows(ref):
        rows = ref[0 : lay.drows, 0:HDYN]
        for block in range(1, n_blk):
            rows = jnp.where(z == block, ref[block * lay.drows : (block + 1) * lay.drows, 0:HDYN], rows)
        return rows

    mine_rows = pl.ds(pl.multiple_of(z * lay.rows, lay.rows), lay.rows)
    dyn_window = pl.ds(pl.multiple_of(z * lay.drows // 8 * 8, 8), -(-(lay.drows + 7) // 8) * 8)

    def from_window(value):
        rows = value[0 : lay.drows, 0:HDYN]
        for block in range(1, n_blk):
            begin = block * lay.drows % 8
            rows = jnp.where(z == block, value[begin : begin + lay.drows, 0:HDYN], rows)
        return rows

    def take_matrix(k):
        tiles_on(k).wait_recv()
        for chunk in range(n_dp):
            tile = chunk * lay.mat
            half, row = tile // 32, tile % 32
            at = slice(row * 8, (row + lay.mat) * 8)
            piece = mg[k, chunk % 2, chunk // 2].reshape(lay.mat * 8, 128)
            mat[k, at, half * 128 : (half + 1) * 128] = piece / total
        normalise(mat.at[k])

    chains[2][4]()
    chains[0][3]()

    @pl.when(is_dyn)
    def _():
        dpack[D_IN : D_IN + 24, :] = dacc_w[0:24, :]
        dpack[D_OUT : D_OUT + HALF, :] = dacc_o[0:HALF, :]
        dpack[D_OUT + HALF : D_OUT + DOUT, :] = dacc_o[24 : 24 + HALF, :]
        dpack[D_B2 : D_B2 + 1, :] = dacc_h[HSAC : HSAC + 1, :]
        dpack[D_B3 : D_B3 + 1, 0:48] = dacc_m[0:1, :]
        lanes = lax.broadcasted_iota(jnp.int32, (24, 128), 1)
        bound = jnp.where(
            lanes == 0,
            jnp.sum(dacc_b[0], axis=1, keepdims=True),
            jnp.where(lanes == 1, jnp.sum(dacc_b[1], axis=1, keepdims=True), 0.0),
        )
        dpack[D_UP : D_UP + 2, 0:24] = bound.T[0:2, :]
        dpack[D_LOSS : D_LOSS + 1, 0:128] = jnp.broadcast_to(
            jnp.sum(dacc_l[0:1, :], axis=1, keepdims=True), (1, 128)
        )
        dpack[D_HID : D_HID + lay.drows, 0:HDYN] = line_rows(dacc_h)
        dyn_s[dyn_e] = dpack[...]
        give("pack", dpack)
        dmat[...] = jnp.zeros_like(dmat)
        for block in range(n_blk):
            at = slice(block * lay.drows, (block + 1) * lay.drows)
            dmat[at, 0:HDYN] = MOMENTUM * dmg[block] + dacc_h[at, 0:HDYN] / total
        normalise(dmat)

    def sum_end(step):
        @pl.when(step == 3)
        def _():
            chains[0][4]()
            chains[1][3]()

    take_matrix(2)

    @pl.when(is_dyn)
    def _():
        both = [dmat, mat.at[2]]
        schulz(both, NS_ITERS - 1, sum_end)
        window, sac_x[2] = schulz_rows(both, [dyn_window, mine_rows], gram)
        rows = from_window(window)
        drow_x[...] = rows
        dyn_x[dyn_e] = rows
        give("x", drow_x)

    @pl.when(jnp.logical_not(is_dyn))
    def _():
        schulz([mat.at[2]], NS_ITERS - 1, sum_end)
        (sac_x[2],) = schulz_rows([mat.at[2]], [mine_rows], gram)

    def sent_early():
        has_sent(wg.at[pl.ds(0, n_blk - 1), :, half_rows], "hidden")
        has_sent(wg.at[pl.ds(0, n_blk - 1), :, half_rows], "hidden on")
        has_sent(asked.at[pl.ds(0, n_dp - 1)], "lists")
        has_sent(bk.at[pl.ds(0, n_dp - 1)], "own")
        has_sent(bk.at[pl.ds(0, n_blk - 1)], "line")
        has_sent(bk.at[pl.ds(0, (n_dp - 1) * (n_blk - 1))], "plane")

        @pl.when(is_dyn)
        def _():
            has_sent(dhg.at[pl.ds(0, n_blk - 1)], "dyn h")
            has_sent(dmg.at[pl.ds(0, n_blk - 1)], "dyn m")

        for group in range(3):
            core_sum(group).wait_send()
            has_sent(froms[group].at[pl.ds(0, lay.half - 1)], ("plane sum", group))
        for part in range(4):
            has_sent(line_bytes(part), ("line sum", part))

    def pass_on(step):
        pl.when(step == 2)(functools.partial(hand_on, "pack"))

    sent_early()
    chains[1][4]()
    for k in range(2):
        take_matrix(k)
    both = [mat.at[0], mat.at[1]]
    schulz(both, NS_ITERS - 1, pass_on)
    hand_on("x")
    sac_x[0], sac_x[1] = schulz_rows(both, [mine_rows, mine_rows], gram)
    for k in range(3):
        for half in range(2):
            for piece in range(lay.rows // 8 // lay.mat):
                chunk = (half * 32 + z * (lay.rows // 8)) // lay.mat + piece
                kept = mg[k, lax.rem(chunk, 2), chunk // 2]
                sac_g[half, k, piece * lay.mat : (piece + 1) * lay.mat] = kept

    small_on().wait_recv()
    from_sibling("pack")
    from_sibling("x")

    has_sent(small.at[pl.ds(0, (lay.half - 1) * lay.sml)], "small")
    small_on().wait_send()
    gave("pack")
    gave("x")

    for k in range(3):
        has_sent(mg.at[k, 0, pl.ds(0, lay.half - 1)], ("tiles", k))
        tiles_on(k).wait_send()


def ordered(lay, n_in, n_out, *refs):
    inputs, outputs, scratch = refs[:n_in], refs[n_in : n_in + n_out], refs[n_in + n_out :]
    main_kernel(lay, *inputs, *scratch[: n_in + 1], *outputs, *scratch[n_in + 1 :])


def adamw(weights, first, second, gradient):
    first = BETA_FIRST * first + (1.0 - BETA_FIRST) * gradient
    second = BETA_SECOND * second + (1.0 - BETA_SECOND) * gradient * gradient
    first_hat = first / (1.0 - BETA_FIRST**STEP)
    second_hat = second / (1.0 - BETA_SECOND**STEP)
    step = first_hat / (jnp.sqrt(second_hat) + 1e-8) + ADAM_DECAY * weights
    return weights - ADAM_RATE * step, first, second


def update_kernel(lay, *refs):
    (
        sac_g, sac_x, dyn_x, dyn_s, small, count, crit_rows, sac_h, dyn_h, dyn_m,
        ci, ci_m, ci_v, ai, ai_m, ai_v, di, di_m, di_v, ao, ao_m, ao_v,
        do, do_m, do_v, bi, bi_m, bi_v,
        sac_new, sac_mom, dyn_new, dyn_mom, ci_n, ci_mn, ci_vn, ai_n, ai_mn, ai_vn, di_n, di_mn,
        di_vn, co_n, co_mn, co_vn, ao_n, ao_mn, ao_vn, do_n, do_mn, do_vn, bi_n, bi_mn, bi_vn,
        loss, counted, bg,
    ) = refs
    total = count[0:1, 0:1]
    for k in range(3):
        for side in range(2):
            tiles = sac_g[side, k].reshape(sac_mom.shape[1], 128)
            sac_mom[k, :, side * 128 : (side + 1) * 128] = tiles / total
    sac_new[...] = sac_h[...] * (1.0 - MUON_RATE * MUON_DECAY) - MUON_RATE * sac_x[...]
    dyn_rows = dyn_s[:, D_HID : D_HID + dyn_m.shape[1], 0:HDYN]
    dyn_mom[...] = MOMENTUM * dyn_m[...] + dyn_rows / total.reshape(1, 1, 1)
    dyn_new[...] = dyn_h[...] * (1.0 - MUON_RATE * MUON_DECAY) - MUON_RATE * dyn_x[...]

    def rows(row, number):
        def tile(at):
            chunk = at // lay.sml
            return small[(chunk % 2 * lay.half + chunk // 2) * lay.sml + at % lay.sml]

        sides = []
        for side in range(2):
            at = side * (R_SMALL // 8) + row // 8
            sides.append(jnp.concatenate([tile(at + more) for more in range(-(-number // 8))], 0))
        return jnp.concatenate(sides, 1)

    def store(outs, at, values):
        for out, value in zip(outs, values):
            out[at] = value

    outs = (ci_n, ci_mn, ci_vn)
    for k in range(2):
        at = (slice(None), k, slice(None))
        grad = rows(R_IN + 24 * k, 24)
        bg[:, CB1 + HSAC * k : CB1 + HSAC * (k + 1)] = grad[IN : IN + 1]
        store(outs, at, adamw(ci[at], ci_m[at], ci_v[at], grad[0:IN] / total))
    grad = rows(R_IN + 48, 24)
    bg[:, AB1 : AB1 + HSAC] = grad[IN : IN + 1]
    store((ai_n, ai_mn, ai_vn), ..., adamw(ai[...], ai_m[...], ai_v[...], grad[0:OBS] / total))
    grad = rows(R_HEAD, 16)
    for at, row in ((slice(0, ACT), slice(1, 1 + ACT)), (slice(ACT, 2 * ACT), slice(9, 9 + ACT))):
        store((ao_n, ao_mn, ao_vn), at, adamw(ao[at], ao_m[at], ao_v[at], grad[row] / total))
    grad = rows(R_OUT, 8)
    held = [crit_rows[2 * at : 2 * at + 2, :] for at in range(3)]
    store((co_n, co_mn, co_vn), ..., adamw(*held, grad[0:2] / total))
    bg[:, CB2 : CB2 + HSAC] = grad[2:3]
    bg[:, CB2 + HSAC : CB2 + 2 * HSAC] = grad[3:4]
    bg[:, AB2 : AB2 + HSAC] = grad[4:5]
    grad = rows(R_MISC, 8)
    bg[:, CB3 : CB3 + 1] = grad[0:1, 16:17]
    bg[:, CB3 + 1 : CB3 + 2] = grad[0:1, 32:33]
    bg[:, AB3 : AB3 + ACT] = grad[0:1, 1 : 1 + ACT]
    bg[:, AB3 + ACT : AB3 + 2 * ACT] = grad[0:1, 9 : 9 + ACT]
    bg[:, LOGA : LOGA + 1] = -grad[0:1, 65:66]
    total_loss = grad[0:1, 64:65]
    up = jnp.zeros((1, HALF), F32)
    low = jnp.zeros((1, HALF), F32)
    for e in range(MEMBERS):
        pack = dyn_s[e]
        total_loss = total_loss + pack[D_LOSS : D_LOSS + 1, 0:1]
        up = up + pack[D_UP : D_UP + 1, 0:HALF]
        low = low + pack[D_LOW : D_LOW + 1, 0:HALF]
        bg[:, DB1 + HDYN * e : DB1 + HDYN * (e + 1)] = pack[IN : IN + 1, 0:HDYN]
        bg[:, DB2 + HDYN * e : DB2 + HDYN * (e + 1)] = pack[D_B2 : D_B2 + 1, 0:HDYN]
        bg[:, DB3 + DOUT * e : DB3 + DOUT * e + HALF] = pack[D_B3 : D_B3 + 1, 0:HALF]
        bg[:, DB3 + DOUT * e + HALF : DB3 + DOUT * (e + 1)] = pack[D_B3 : D_B3 + 1, 24 : 24 + HALF]
        grad = pack[0:IN, 0:HDYN] / total
        store((di_n, di_mn, di_vn), e, adamw(di[e], di_m[e], di_v[e], grad))
        grad = pack[D_OUT : D_OUT + DOUT, 0:HDYN] / total
        store((do_n, do_mn, do_vn), e, adamw(do[e], do_m[e], do_v[e], grad))
    bg[:, MAXLV : MAXLV + HALF] = up
    bg[:, MINLV : MINLV + HALF] = low
    lane = lax.broadcasted_iota(jnp.int32, (1, NB), 1)
    bounds = jnp.where(
        jnp.logical_and(lane >= MAXLV, lane < MINLV),
        BOUND_WEIGHT,
        jnp.where(jnp.logical_and(lane >= MINLV, lane < LOGA), -BOUND_WEIGHT, 0.0),
    )
    grad = bg[...] / total + bounds
    flat = [ref[...].reshape(1, NB) for ref in (bi, bi_m, bi_v)]
    store((bi_n, bi_mn, bi_vn), ..., [value.reshape(NB) for value in adamw(*flat, grad)])
    loss[...] = total_loss
    counted[...] = total


def shards(
    lay, replay, model_rows, requests, member_of, model_live, noise, sac_hidden, sac_hidden_mom,
    dyn_hidden, dyn_hidden_mom, crit_in, crit_in_m, crit_in_v, act_in, act_in_m, act_in_v, dyn_in,
    dyn_in_m, dyn_in_v, crit_out, crit_out_m, crit_out_v, act_out, act_out_m, act_out_v, dyn_out,
    dyn_out_m, dyn_out_v, biases, biases_m, biases_v, targ_in, targ_hidden, targ_out, targ_bias,
):
    n_dp, n_blk = lay.n_dp, lay.n_blk
    spec = pl.BlockSpec(memory_space=pltpu.VMEM)

    def flip(value):
        return jnp.transpose(value, (1, 0, 2))

    def swap(value):
        return jnp.swapaxes(value, -1, -2)

    def kept(value):
        return pltpu.with_memory_space_constraint(value, pltpu.VMEM)

    inputs = (
        sac_hidden, requests, member_of, replay, model_live, model_rows, jnp.transpose(noise, (2, 0, 1)),
        biases, flip(targ_in), flip(crit_in), act_in, targ_bias, targ_hidden, crit_out, targ_out,
        swap(act_out), dyn_hidden, dyn_hidden_mom, crit_out_m, crit_out_v, sac_hidden_mom, dyn_in,
        swap(dyn_out),
    )
    shape = jax.ShapeDtypeStruct
    rows, drows = lay.rows, lay.drows
    out_shape = (
        pltpu.VMEM((2, 3, rows // 8, 8, 128), F32),
        pltpu.VMEM((3, rows, HSAC), F32),
        pltpu.VMEM((MEMBERS, drows, HDYN), F32),
        pltpu.VMEM((MEMBERS, D_ROWS, HSAC), F32),
        pltpu.VMEM((32, 8, 128), F32),
        pltpu.VMEM((8, 128), F32),
        pltpu.VMEM((8, HSAC), F32),
    )

    def vm(*dims, kind=F32):
        return pltpu.VMEM(dims, kind)

    scratch = [
        vm(n_blk, 3, rows, HSAC, kind=BF16),
        vm(2, n_dp, CAP, kind=jnp.int32),
        vm(n_dp, 2, n_dp, CAP, kind=jnp.int32),
        vm(n_blk, drows, HDYN),
        vm(n_blk, drows, HDYN),
        vm(lay.n_dev, 48, lay.width),
        vm(56, lay.batch),
        vm(2, 8, lay.batch),
        vm(8, lay.batch),
        vm(8, lay.batch),
        vm(5, 32, HSAC),
        vm(5, HSAC, 32, kind=BF16),
        vm(2, 16, HSAC, kind=BF16),
        vm(5, HSAC, HSAC, kind=BF16),
        vm(3, HSAC, HSAC, kind=BF16),
        vm(5, 16, HSAC, kind=BF16),
        vm(HSAC, 16, kind=BF16),
        vm(16, HSAC),
        vm(8, HSAC),
        vm(7, HSAC, 128),
        vm(128, 8),
        vm(3, HSAC + 16, HSAC),
        vm(3, 32, HSAC),
        vm(2, 16, HSAC),
        vm(16, HSAC),
        vm(16, 48),
        vm(8, max(CRITIC_TILE, ACTOR_TILE)),
        *[vm(2, lay.half, chunk, 8, 128) for chunk in lay.chunks],
        *[vm(lay.half, chunk, 8, 128) for chunk in lay.chunks],
        *[vm(lay.half, chunk, 8, 128) for chunk in lay.chunks],
        *[vm(n_blk, chunk, 8, 128) for chunk in lay.chunks],
        *[vm(chunk, 8, 128) for chunk in lay.chunks],
        *[vm(chunk, 8, 128) for chunk in lay.chunks],
        vm(3, 2, lay.half, lay.mat, 8, 128),
        vm(3, HSAC, HSAC),
        vm(2, HSAC, HSAC),
        vm(HSAC, 8),
        vm(HSAC + 16, HSAC),
        vm(32, HSAC),
        vm(48, HSAC),
        vm(16, 48),
        vm(2, 24, DYN_TILE),
        vm(8, DYN_TILE),
        vm(48, DYN_TILE),
        vm(HSAC, HSAC),
        vm(D_ROWS, HSAC),
        vm(drows, HDYN),
        vm(1, NB),
        vm(48, HSAC, kind=BF16),
        vm(HSAC, 48, kind=BF16),
    ]
    scratch += [pltpu.SemaphoreType.DMA((lay.departures,)), pltpu.SemaphoreType.DMA((lay.arrivals,))]
    held = [pltpu.VMEM(value.shape, value.dtype) for value in inputs]
    held.append(pltpu.SemaphoreType.DMA((len(inputs),)))
    varying = 4 * (lay.n_dev * 48 * lay.width + 72 * lay.batch + 48 * lay.replay)
    gathered = pl.pallas_call(
        functools.partial(ordered, lay, len(inputs), len(out_shape)),
        out_shape=out_shape,
        in_specs=[pl.BlockSpec(memory_space=pl.ANY)] * len(inputs),
        out_specs=[spec] * len(out_shape),
        scratch_shapes=held + scratch,
        compiler_params=pltpu.CompilerParams(
            collective_id=0, has_side_effects=True, vmem_limit_bytes=26 * 2**20 + varying
        ),
        name="step",
    )(*[pltpu.with_memory_space_constraint(value, pltpu.HBM) for value in inputs])
    params = (
        sac_hidden, dyn_hidden, dyn_hidden_mom,
        flip(crit_in), flip(crit_in_m), flip(crit_in_v), act_in, act_in_m, act_in_v,
        dyn_in, dyn_in_m, dyn_in_v,
        swap(act_out), swap(act_out_m), swap(act_out_v),
        swap(dyn_out), swap(dyn_out_m), swap(dyn_out_v), biases, biases_m, biases_v,
    )
    new_shape = [shape(sac_hidden.shape, F32)] + [shape(value.shape, F32) for value in params[:12]]
    new_shape += [shape(crit_out.shape, F32)] * 3 + [shape(value.shape, F32) for value in params[12:]]
    new_shape += [shape((1, 1), F32)] * 2
    out = pl.pallas_call(
        functools.partial(update_kernel, lay),
        out_shape=tuple(new_shape),
        in_specs=[spec] * (len(gathered) + len(params)),
        out_specs=[spec] * len(new_shape),
        scratch_shapes=[vm(1, NB)],
        compiler_params=pltpu.CompilerParams(vmem_limit_bytes=16 * 2**20),
        name="update",
    )(*[kept(value) for value in gathered], *params)
    out = list(out)
    for at in (4, 5, 6):
        out[at] = flip(out[at])
    for at in (16, 17, 18, 19, 20, 21):
        out[at] = swap(out[at])
    for at in (25, 26):
        out[at] = out[at].reshape(())
    return tuple(out)


def solution(mesh):
    both = ("dp", "blk")
    sharded = (
        P(None, both), P(None, both), P(both, None), P(both, None), P(both), P(None, both, None),
    )
    hidden = (P(None, "blk", None),) * 4

    def step(replay, model_rows, *others):
        lay = Layout(mesh, replay.shape[1], model_rows.shape[1])
        return shards(lay, replay, model_rows, *others)

    return jax.shard_map(
        step,
        mesh=mesh,
        in_specs=sharded + hidden + (P(),) * 25,
        out_specs=hidden + (P(),) * 23,
        check_vma=False,
    )
```

```python
import functools

import jax
import jax.numpy as jnp
from jax import lax
from jax.experimental import pallas as pl
from jax.experimental.pallas import tpu as pltpu
from jax.sharding import PartitionSpec as P

OBS = 17
ACT = 6
IN = OBS + ACT
FEAT = 42
HDYN = 200
HSAC = 256
MEMBERS = 7
DOUT = 36
HALF = DOUT // 2
NB = 4639
NS_ITERS = 5
STEP = 10
CAP = 8
CRITIC_TILE = 640
ACTOR_TILE = 1280
DYN_TILE = 512
ROWS = 32

DISCOUNT = 0.99
TARGET_ENTROPY = -6.0
BOUND_WEIGHT = 0.01
MOMENTUM = 0.95
MUON_RATE = 0.4
MUON_DECAY = 0.01
ADAM_RATE = 0.1
ADAM_DECAY = 0.01
BETA_FIRST = 0.9
BETA_SECOND = 0.999
COEF_LINEAR = 3.4445
COEF_CUBIC = -4.775
COEF_QUINTIC = 2.0315

CB1, CB2, CB3, AB1, AB2, AB3 = 0, 512, 1024, 1026, 1282, 1538
DB1, DB2, DB3, MAXLV, MINLV, LOGA = 1550, 2950, 4350, 4602, 4620, 4638

R_IN, R_HEAD, R_OUT, R_MISC, R_SMALL = 0, 72, 88, 96, 128
D_IN, D_OUT, D_B2, D_B3, D_UP, D_LOW, D_LOSS, D_HID, D_ROWS = 0, 24, 60, 61, 62, 63, 64, 72, 128

F32, BF16 = jnp.float32, jnp.bfloat16
MESH = pl.DeviceIdType.MESH
NN = (((1,), (0,)), ((), ()))
NT = (((1,), (1,)), ((), ()))


def dot(a, b, dims=NN):
    return lax.dot_general(a, b, dims, preferred_element_type=F32)


def rounded(v):
    return v.astype(BF16).astype(F32)


def pieces(v):
    high = v.astype(BF16)
    rest = v - high.astype(F32)
    middle = rest.astype(BF16)
    return high, middle, (rest - middle.astype(F32)).astype(BF16)


def split(v):
    high = v.astype(BF16)
    return high, (v - high.astype(F32)).astype(BF16)


def product(a, b, dims=NN, cuts=1):
    left = jnp.concatenate([a[0], a[0], a[1]], 1)
    right = jnp.concatenate([b[0], b[1], b[0]], dims[0][1][0])
    rows = left.shape[0] // cuts
    done = [dot(left[at * rows : (at + 1) * rows], right, dims) for at in range(cuts)]
    return done[0] if cuts == 1 else jnp.concatenate(done, 0)


def softplus(v):
    return jnp.maximum(v, 0.0) + jnp.log1p(jnp.exp(-jnp.abs(v)))


def sigmoid(v):
    return 0.5 + 0.5 * jnp.tanh(0.5 * v)


def gate(half):
    up = 1.0 + jnp.tanh(half)
    value = half * up
    return value, up + value * (2.0 - up)


def by_rows(body, *arrays):
    done = [
        body(*[array[at : at + ROWS] for array in arrays]) for at in range(0, arrays[0].shape[0], ROWS)
    ]
    return [jnp.concatenate(parts, 0) for parts in zip(*done)]


def spread_to(column, width):
    return jnp.concatenate([column] * (width // 128), 1)


def gated(half, column=None):
    def body(part, *offset):
        value, slope = gate(part + spread_to(offset[0], part.shape[1]) if offset else part)
        return value.astype(BF16), slope

    return by_rows(body, half, *([] if column is None else [column]))


def sloped(grad, slope):
    return by_rows(lambda part, by: ((part * by).astype(BF16),), grad, slope)[0]


def outer_sloped(column, row, slope):
    return by_rows(lambda part, by: (((spread_to(part, by.shape[1]) * row) * by).astype(BF16),), column, slope)[0]


def rows_of(shape):
    return lax.broadcasted_iota(jnp.int32, shape, 0)


def blend(gram, square):
    return split(COEF_CUBIC * gram + COEF_QUINTIC * square)


def schulz(refs, steps, before=None):
    cuts = 2 if len(refs) == 1 else 1

    @pl.loop(0, steps)
    def _(step):
        if before is not None:
            before(step)
        matrices = [ref[...] for ref in refs]
        parts = [split(matrix) for matrix in matrices]
        grams = [product(part, part, NT, cuts) for part in parts]
        halves = [split(gram) for gram in grams]
        squares = [product(half, half, NN, cuts) for half in halves]
        blends = [blend(gram, square) for gram, square in zip(grams, squares)]
        moved = [product(mix, part, NN, cuts) for mix, part in zip(blends, parts)]
        for ref, matrix, move in zip(refs, matrices, moved):
            ref[...] = COEF_LINEAR * matrix + move


def schulz_rows(refs, windows, held):
    cuts = 2 if len(refs) == 1 else 1
    parts = [split(ref[...]) for ref in refs]
    grams = [product(part, part, NT, cuts) for part in parts]
    for at, gram in enumerate(grams):
        held[at] = gram
    halves = [split(gram) for gram in grams]
    grams = [held[at, window] for at, window in enumerate(windows)]
    squares = [product(split(gram), half) for gram, half in zip(grams, halves)]
    blends = [blend(gram, square) for gram, square in zip(grams, squares)]
    moved = [product(mix, part) for mix, part in zip(blends, parts)]
    return [
        COEF_LINEAR * ref[window, :] + move for ref, window, move in zip(refs, windows, moved)
    ]


def normalise(ref):
    moment = ref[...]
    norm = jnp.sqrt(jnp.sum(jnp.sum(moment * moment, axis=1, keepdims=True), axis=0, keepdims=True))
    ref[...] = moment / (norm + 1e-7)


class Layout:
    def __init__(self, mesh, replay, model):
        self.n_dp = mesh.shape["dp"]
        self.half = self.n_dp // 2
        self.n_blk = mesh.shape["blk"]
        self.n_dev = self.n_dp * self.n_blk
        self.replay = replay
        self.model = model
        self.real = self.n_dp * CAP
        self.batch = self.real + model
        self.width = -(-(self.real + 2) // 128) * 128
        self.rows = HSAC // self.n_blk
        self.drows = HDYN // self.n_blk
        self.mat = 64 // self.n_dp
        self.sml = 32 // self.n_dp
        self.chunks = (self.mat, self.mat + self.sml, self.mat)
        groups = [(name, g) for name in ("core sum", "plane sum") for g in range(3)]
        groups += [("line sum", g) for g in range(4)]
        common = ["hidden", "hidden on", "lists", "own", "line", "plane", "dyn h", "dyn m", "small", "small on"]
        common += groups
        kinds = [(name, kind) for name in ("pack", "x") for kind in ("own", "on")]
        tiles = [(name, k) for name in ("tiles", "tiles on") for k in range(3)]
        sent = common + tiles + kinds
        self.sent = {name: at for at, name in enumerate(sent)}
        self.departures = len(sent)
        self.here, self.arrivals = {}, 0
        tiles += [("pack", "sibling"), ("x", "sibling")]
        for name in common + tiles:
            self.here[name] = self.arrivals
            self.arrivals += 1
        for name in ("pack", "x"):
            self.here[name, "like"] = self.arrivals
            self.arrivals += MEMBERS


OPERANDS = 23
FIRST, SECOND = 3, 16


def main_kernel(lay, *refs):
    n_in = OPERANDS
    sources, held = refs[:n_in], refs[n_in : 2 * n_in]
    (
        sac_h, requests, member, replay, live, model, noise, biases, targ_in, crit_in, act_in, targ_bias,
        targ_hidden, crit_out, targ_out, act_out, dyn_h, dyn_m, crit_out_m, crit_out_v, sac_m, dyn_in, dyn_out,
    ) = held
    loads = refs[2 * n_in]
    refs = refs[2 * n_in + 1 :]
    (
        sac_g, sac_x, dyn_x, dyn_s, small, count, crit_rows,
        wg, lists, asked, dhg, dmg, bk, xs, nz, ys, ahead, w1f, w1t, w1n, w2t, w2h, heads, head_t, head_f,
        rowbuf, wide, headcol, acc_h, acc_w, acc_c, acc_a, acc_m, acc_l, grid_0, grid_1, grid_2, core_0, core_1,
        core_2, from_0, from_1, from_2, zr_0, zr_1, zr_2, zf_0, zf_1, zf_2, sum_0, sum_1, sum_2, mg, mat, gram, dcols, dacc_h, dacc_w, dacc_o, dacc_m, dacc_b, dacc_l, xt, dmat,
        dpack, drow_x, bias, dhead, dhead_t, *rest,
    ) = refs
    send, recv = rest
    sent, here_at = lay.sent, lay.here
    grids, cores, froms = (grid_0, grid_1, grid_2), (core_0, core_1, core_2), (from_0, from_1, from_2)
    zrs, zfs, totals = (zr_0, zr_1, zr_2), (zf_0, zf_1, zf_2), (sum_0, sum_1, sum_2)
    n_dp, n_blk = lay.n_dp, lay.n_blk
    me = lax.axis_index("dp")
    z = lax.axis_index("blk")
    core, like = lax.rem(me, 2), me // 2
    sibling = me + 1 - 2 * core
    is_dyn = me < MEMBERS
    dyn_e = jnp.minimum(me, MEMBERS - 1)

    def on_plane(src, dst, ssem, rsem, peer):
        return pltpu.make_async_remote_copy(
            src_ref=src, dst_ref=dst, send_sem=ssem, recv_sem=rsem,
            device_id={"dp": peer}, device_id_type=MESH,
        )

    def on_line(src, dst, ssem, rsem, peer):
        return pltpu.make_async_remote_copy(
            src_ref=src, dst_ref=dst, send_sem=ssem, recv_sem=rsem,
            device_id={"blk": peer}, device_id_type=MESH,
        )

    def over(number, body):
        if number <= 8:
            for off in range(1, number):
                body(off)
        else:
            pl.loop(1, number)(body)

    def plane_peers(body):
        over(n_dp, lambda off: body(lax.rem(me + off, n_dp)))

    def like_peers(body):
        over(n_dp // 2, lambda off: body(lax.rem(me + 2 * off, n_dp)))

    def line_peers(body):
        over(n_blk, lambda off: body(lax.rem(z + off, n_blk)))

    def has_sent(view, name):
        at = send.at[sent[name]]
        on_plane(view, view, at, at, sibling).wait_send()

    def has_come(view, name):
        at = recv.at[here_at[name]]
        on_plane(view, view, at, at, sibling).wait_recv()

    copies = [
        pltpu.make_async_copy(src, dst, loads.at[at]) for at, (src, dst) in enumerate(zip(sources, held))
    ]

    def arrived(begin, end):
        for copy in copies[begin:end]:
            copy.wait()

    barrier = pltpu.get_barrier_semaphore()
    plane_peers(lambda peer: pl.semaphore_signal(barrier, inc=1, device_id={"dp": peer}, device_id_type=MESH))
    line_peers(lambda peer: pl.semaphore_signal(barrier, inc=1, device_id={"blk": peer}, device_id_type=MESH))
    for copy in copies:
        copy.start()
    arrived(0, FIRST)
    wg[0] = sac_h[...].astype(BF16)
    lists[0] = requests[...]
    lists[1] = member[...]
    pl.semaphore_wait(barrier, n_dp - 1 + n_blk - 1)

    half_rows = pl.ds(pl.multiple_of(core * (lay.rows // 2), lay.rows // 2), lay.rows // 2)

    def slot_from(owner, at):
        return lax.rem(owner - at + n_blk, n_blk)

    def hidden_copy(peer):
        src = wg.at[0, :, half_rows]
        dst = wg.at[slot_from(z, peer), :, half_rows]
        return on_line(src, dst, send.at[sent["hidden"]], recv.at[here_at["hidden"]], peer)

    def hidden_on():
        view = wg.at[pl.ds(1, n_blk - 1), :, half_rows]
        return on_plane(view, view, send.at[sent["hidden on"]], recv.at[here_at["hidden on"]], sibling)

    def list_copy(peer):
        return on_plane(lists, asked.at[me], send.at[sent["lists"]], recv.at[here_at["lists"]], peer)

    line_peers(lambda peer: hidden_copy(peer).start())
    plane_peers(lambda peer: list_copy(peer).start())
    asked[me] = lists[...]

    def dyn_h_copy(peer):
        return on_line(dyn_h.at[dyn_e], dhg.at[z], send.at[sent["dyn h"]], recv.at[here_at["dyn h"]], peer)

    def dyn_m_copy(peer):
        return on_line(dyn_m.at[dyn_e], dmg.at[z], send.at[sent["dyn m"]], recv.at[here_at["dyn m"]], peer)

    arrived(FIRST, SECOND)
    alive = live[...].astype(F32).reshape(1, lay.model)
    data = replay[...]
    sums = jnp.sum(data[0:24], axis=1, keepdims=True)
    squares = jnp.sum(data[0:24] * data[0:24], axis=1, keepdims=True)
    living = jnp.sum(alive, axis=1, keepdims=True)

    has_come(asked.at[pl.ds(0, n_dp - 1)], "lists")
    spread = (
        lax.rem(lax.broadcasted_iota(jnp.int32, (CAP, lay.real), 1), CAP)
        == lax.broadcasted_iota(jnp.int32, (CAP, lay.real), 0)
    ).astype(F32)
    here = (
        lax.broadcasted_iota(jnp.int32, (n_dp, lay.real), 1) // CAP
        == lax.broadcasted_iota(jnp.int32, (n_dp, lay.real), 0)
    )

    def in_lanes(which):
        values = asked[:, which, me, :].astype(F32)
        wide = lax.dot_general(
            values, spread, NN, precision=lax.Precision.HIGHEST, preferred_element_type=F32
        )
        return jnp.sum(jnp.where(here, wide, 0.0), axis=0, keepdims=True)

    slots = in_lanes(0)
    wanted = jnp.maximum(slots, 0.0).astype(jnp.int32)
    hot = (rows_of((lay.replay, lay.real)) == wanted).astype(BF16)
    padded = jnp.concatenate([data, jnp.zeros((48 - FEAT, lay.replay), F32)], 0)
    chosen = dot(jnp.concatenate(pieces(padded), 0), hot)
    chosen = chosen[0:48] + chosen[48:96] + chosen[96:144]
    mine = me * n_blk
    bk[mine, 0:FEAT, 0 : lay.real] = chosen[0:FEAT]
    bk[mine, 42:43, 0 : lay.real] = (slots >= 0.0).astype(F32)
    bk[mine, 43:44, 0 : lay.real] = in_lanes(1)
    bk[mine, 44:48, 0 : lay.real] = jnp.zeros((4, lay.real), F32)
    bk[mine, :, lay.real : lay.width] = jnp.zeros((48, lay.width - lay.real), F32)
    bk[mine, 0:24, lay.real : lay.real + 1] = sums
    bk[mine, 0:24, lay.real + 1 : lay.real + 2] = squares
    bk[mine, 24:25, lay.real : lay.real + 1] = living

    def slot_of(block):
        line = lax.rem(block, n_blk)
        return block - line + slot_from(line, z)

    def block_line(peer):
        dst = bk.at[me * n_blk + slot_from(z, peer)]
        return on_line(bk.at[mine], dst, send.at[sent["line"]], recv.at[here_at["line"]], peer)

    def block_own(peer):
        view = bk.at[mine]
        return on_plane(view, view, send.at[sent["own"]], recv.at[here_at["own"]], peer)

    def block_plane(peer):
        view = bk.at[pl.ds(mine + 1, n_blk - 1)]
        return on_plane(view, view, send.at[sent["plane"]], recv.at[here_at["plane"]], peer)

    plane_peers(lambda peer: block_own(peer).start())
    line_peers(lambda peer: block_line(peer).start())

    arrived(SECOND, n_in)
    crit_rows[0:2, :] = crit_out[...]
    crit_rows[2:4, :] = crit_out_m[...]
    crit_rows[4:6, :] = crit_out_v[...]
    crit_rows[6:8, :] = jnp.zeros((2, HSAC), F32)

    @pl.when(is_dyn)
    def _():
        line_peers(lambda peer: dyn_h_copy(peer).start())
        line_peers(lambda peer: dyn_m_copy(peer).start())

    bias[...] = biases[...].reshape(1, NB)
    xs[42:56, :] = jnp.zeros((14, lay.batch), F32)
    xs[0:FEAT, lay.real : lay.batch] = model[...]
    xs[42:43, lay.real : lay.batch] = alive
    nz[...] = jnp.zeros_like(nz)
    for which in range(2):
        nz[which, 1:7, :] = noise[:, which, :]
    firsts = [
        (targ_in[:, 0, :], targ_bias[0:1, 0:HSAC]),
        (targ_in[:, 1, :], targ_bias[1:2, 0:HSAC]),
        (crit_in[:, 0, :], bias[:, CB1 : CB1 + HSAC]),
        (crit_in[:, 1, :], bias[:, CB1 + HSAC : CB1 + 2 * HSAC]),
        (act_in[...], bias[:, AB1 : AB1 + HSAC]),
    ]
    w1f[...] = jnp.zeros_like(w1f)
    for net, (weights, offset) in enumerate(firsts):
        w1f[net, 0 : weights.shape[0], :] = rounded(weights)
        for at, piece in enumerate(pieces(offset)):
            w1f[net, IN + at : IN + at + 1, :] = piece.astype(F32)
        w1t[net] = (0.5 * w1f[net].T).astype(BF16)
    for k in range(2):
        w1n[k] = w1f[2 + k, 16:32, :].astype(BF16)
    for net in range(2):
        w2t[net] = (0.5 * rounded(targ_hidden[net])).T.astype(BF16)
    has_come(wg.at[pl.ds(0, n_blk - 1), :, half_rows], "hidden")
    hidden_on().start()

    rowbuf[...] = jnp.zeros_like(rowbuf)
    rowbuf[0:1, :] = targ_bias[0:1, HSAC : 2 * HSAC]
    rowbuf[1:2, :] = targ_bias[1:2, HSAC : 2 * HSAC]
    rowbuf[2:3, :] = bias[:, CB2 : CB2 + HSAC]
    rowbuf[3:4, :] = bias[:, CB2 + HSAC : CB2 + 2 * HSAC]
    rowbuf[4:5, :] = bias[:, AB2 : AB2 + HSAC]
    rowbuf[5:7, :] = rounded(crit_out[...])
    columns = 0.5 * rowbuf[...].T
    for at in range(7):
        wide[at] = jnp.broadcast_to(columns[:, at : at + 1], (HSAC, 128))
    rowbuf[...] = jnp.zeros_like(rowbuf)
    rowbuf[0:1, 1:7] = bias[:, AB3 : AB3 + ACT]
    rowbuf[0:1, 9:15] = bias[:, AB3 + ACT : AB3 + 2 * ACT]
    headcol[...] = rowbuf[:, 0:128].T
    head_f[...] = jnp.zeros_like(head_f)
    for k in range(2):
        head_f[0:1, :] = targ_out[k : k + 1, :]
        heads[k] = head_f[...].astype(BF16)
        head_f[0:1, :] = crit_out[k : k + 1, :]
        heads[2 + k] = head_f[...].astype(BF16)
    head_f[0:1, :] = jnp.zeros((1, HSAC), F32)
    head_f[1:7, :] = act_out[0:ACT, :]
    head_f[9:15, :] = act_out[ACT : 2 * ACT, :]
    heads[4] = head_f[...].astype(BF16)
    head_t[...] = (0.5 * rounded(head_f[...])).T.astype(BF16)
    for ref in (acc_h, acc_w, acc_c, acc_a, acc_m, acc_l):
        ref[...] = jnp.zeros_like(ref)

    has_come(wg.at[pl.ds(0, n_blk - 1), :, half_rows], "hidden on")
    for k in range(3):
        for block in range(n_blk):
            w2h[k, block * lay.rows : (block + 1) * lay.rows, :] = (
                0.5 * wg[slot_from(block, z), k].astype(F32)
            ).astype(BF16)
        w2t[2 + k] = w2h[k].astype(F32).T.astype(BF16)

    log_alpha = bias[:, LOGA : LOGA + 1]
    alpha = jnp.exp(log_alpha)
    last = [
        targ_bias[0:1, 2 * HSAC : 2 * HSAC + 1],
        targ_bias[1:2, 2 * HSAC : 2 * HSAC + 1],
        bias[:, CB3 : CB3 + 1],
        bias[:, CB3 + 1 : CB3 + 2],
    ]
    critic_tiles = lay.batch // CRITIC_TILE
    actor_tiles = lay.batch // ACTOR_TILE

    def act_rows(width):
        row8 = rows_of((8, width))
        return jnp.logical_and(row8 >= 1, row8 < 1 + ACT)

    def place_of(step, width):
        return pl.ds(pl.multiple_of(lax.rem(step + 1, lay.batch // width) * width, width), width)

    def ones16(width):
        return jnp.ones((16, width), BF16)

    def framed(first_row, used, where):
        row32 = rows_of((32, where.size))
        ones3 = jnp.logical_and(row32 >= IN, row32 < IN + 3).astype(F32)
        return jnp.where(row32 < used, xs[first_row : first_row + 32, where], ones3)

    def hidden(inputs, net):
        first, slope1 = gated(dot(w1t[net], inputs))
        second, slope2 = gated(dot(w2t[net], first), wide[net])
        return first, slope1, second, slope2

    def policy(inputs, which, where):
        first, slope1, second, slope2 = hidden(inputs, 4)
        out = dot(heads[4], second) + headcol[0:16, 0:1]
        bent = jnp.tanh(out[8:16])
        log_scale = -5.0 + 3.5 * (bent + 1.0)
        draw = nz[which, :, where]
        moved = jnp.exp(log_scale) * draw
        latent = out[0:8] + moved
        terms = (
            -0.5 * draw * draw
            - log_scale
            - 0.9189385
            - 2.0 * (0.6931472 - latent - softplus(-2.0 * latent))
        )
        used = act_rows(where.size)
        log_prob = jnp.sum(jnp.where(used, terms, 0.0), axis=0, keepdims=True)
        action = jnp.where(used, jnp.tanh(latent), 0.0)
        return action, log_prob, bent, moved, (first, slope1, second, slope2)

    def with_action(inputs, action):
        middle_rows = jnp.where(act_rows(action.shape[1]), action, inputs[16:24])
        return jnp.concatenate([inputs[0:16], middle_rows, inputs[24:32]], 0).astype(BF16)

    def critic(inputs, net):
        kept = hidden(inputs, net)
        value = dot(heads[net], kept[2])[0:1] + last[net]
        return value, kept

    def add_hidden(k, first, grad):
        acc_h[k] += dot(jnp.concatenate([first, ones16(grad.shape[1])], 0), grad, NT)

    has_come(bk.at[pl.ds(0, n_blk - 1)], "line")
    plane_peers(lambda peer: block_plane(peer).start())

    def critic_pass(k, now_in, where, target):
        weight = xs[42:43, where]
        value, (c1, dc1, c2, dc2) = critic(now_in, 2 + k)
        miss = value - target
        g3 = rounded(weight * miss)
        g3_rows = jnp.where(rows_of((16, CRITIC_TILE)) == 0, g3, 0.0).astype(BF16)
        acc_c[k] += dot(g3_rows, c2, NT)
        acc_m[:, 16 + 16 * k : 32 + 16 * k] += dot(ones16(CRITIC_TILE), g3_rows, NT)
        g2 = outer_sloped(wide[5 + k], g3, dc2)
        add_hidden(k, c1, g2)
        g1 = sloped(dot(w2h[k], g2), dc1)
        acc_w[k] += dot(now_in, g1, NT)
        acc_l[0:1, 0:CRITIC_TILE] += weight * (0.5 * miss * miss)

    def put_matrix(k):
        for chunk in range(n_dp):
            tile = chunk * lay.mat
            side, row = tile // 32, tile % 32
            grids[k][chunk % 2, chunk // 2, 0 : lay.mat] = acc_h[
                k, row * 8 : (row + lay.mat) * 8, side * 128 : (side + 1) * 128
            ].reshape(lay.mat, 8, 128)

    def put(row, value):
        for at in range(value.shape[0] // 8):
            for side in range(value.shape[1] // 128):
                tile = side * (R_SMALL // 8) + row // 8 + at
                chunk = tile // lay.sml
                grid_1[chunk % 2, chunk // 2, lay.mat + tile % lay.sml] = value[
                    at * 8 : at * 8 + 8, side * 128 : (side + 1) * 128
                ]

    def core_sum(group):
        name = ("core sum", group)
        return on_plane(
            grids[group].at[1 - core], cores[group], send.at[sent[name]], recv.at[here_at[name]], sibling
        )

    def plane_sum(group, peer):
        name = ("plane sum", group)
        return on_plane(
            cores[group].at[peer // 2], froms[group].at[like], send.at[sent[name]], recv.at[here_at[name]], peer
        )

    def fold_core(group):
        core_sum(group).wait_recv()
        cores[group][...] += grids[group][core]
        like_peers(lambda peer: plane_sum(group, peer).start())

    def line_part(part):
        return (1, pl.ds(lay.mat, lay.sml)) if part == 3 else (part, pl.ds(0, lay.mat))

    def line_sum(part, peer):
        group, tiles = line_part(part)
        name = ("line sum", part)
        src, dst = zfs[group].at[tiles], zrs[group].at[z, tiles]
        return on_line(src, dst, send.at[sent[name]], recv.at[here_at[name]], peer)

    def line_bytes(part):
        group, tiles = line_part(part)
        return zrs[group].at[pl.ds(0, n_blk - 1), tiles]

    first_tile = me * lay.mat
    side = first_tile // 32
    row_tile = lax.rem(first_tile, 32)
    keeper_z = row_tile * 8 // lay.rows
    local_tile = row_tile - keeper_z * (lay.rows // 8)

    def fold_plane(group):
        has_come(froms[group].at[pl.ds(0, lay.half - 1)], ("plane sum", group))
        froms[group][like] = cores[group][like]
        whole = froms[group][0]
        for at in range(1, lay.half):
            whole = whole + froms[group][at]
        zfs[group][...] = whole

        @pl.when(z == keeper_z)
        def _():
            held_rows = pl.ds(pl.multiple_of(local_tile * 8, 8), lay.mat * 8)
            held_lanes = pl.ds(pl.multiple_of(side * 128, 128), 128)
            old = sac_m[group, held_rows, held_lanes].reshape(lay.mat, 8, 128)
            zfs[group][0 : lay.mat] += (MOMENTUM * count[0:1, 0:1]).reshape(1, 1, 1) * old

        for part in (1, 3) if group == 1 else (group,):
            line_peers(lambda peer: line_sum(part, peer).start())

    def tile_copy(k, peer):
        name = ("tiles", k)
        src = totals[k].at[pl.ds(0, lay.mat)]
        return on_plane(src, mg.at[k, core, like], send.at[sent[name]], recv.at[here_at[name]], peer)

    def tiles_on(k):
        name = ("tiles on", k)
        view = mg.at[k, core]
        return on_plane(view, view, send.at[sent[name]], recv.at[here_at[name]], sibling)

    small_at = (core * lay.half + like) * lay.sml

    def small_copy(peer):
        return on_plane(
            sum_1.at[pl.ds(lay.mat, lay.sml)], small.at[pl.ds(small_at, lay.sml)],
            send.at[sent["small"]], recv.at[here_at["small"]], peer,
        )

    def small_on():
        view = small.at[pl.ds(core * lay.half * lay.sml, lay.half * lay.sml)]
        return on_plane(view, view, send.at[sent["small on"]], recv.at[here_at["small on"]], sibling)

    def fold_end(part):
        group, tiles = line_part(part)
        has_come(line_bytes(part), ("line sum", part))
        zrs[group][z, tiles] = zfs[group][tiles]
        whole = zrs[group][0, tiles]
        for block in range(1, n_blk):
            whole = whole + zrs[group][block, tiles]
        totals[group][tiles] = whole
        if part == 3:
            like_peers(lambda peer: small_copy(peer).start())
            small[pl.ds(small_at, lay.sml)] = whole
        else:
            like_peers(lambda peer: tile_copy(part, peer).start())
            mg[part, core, like] = whole

    def chain(group):
        def end():
            for part in (1, 3) if group == 1 else (group,):
                fold_end(part)

        def turn():
            has_come(mg.at[group, 0, pl.ds(0, lay.half - 1)], ("tiles", group))
            tiles_on(group).start()
            if group == 1:
                has_come(small.at[pl.ds(0, (lay.half - 1) * lay.sml)], "small")
                small_on().start()

        return [
            lambda: core_sum(group).start(),
            lambda: fold_core(group),
            lambda: fold_plane(group),
            end,
            turn,
        ]

    chains = [chain(group) for group in range(3)]
    per = DYN_TILE // lay.real
    dyn_tiles = lay.n_dev // per

    def take(slots, step):
        for at, events in slots.items():
            @pl.when(step == at)
            def _():
                for event in events:
                    event()

    @pl.loop(0, actor_tiles)
    def _(step):
        @pl.when(step == actor_tiles - 1)
        def _():
            has_come(bk.at[pl.ds(0, n_dp - 1)], "own")
            lanes = lax.broadcasted_iota(jnp.int32, (48, lay.width), 1) // CAP

            def gather(owner, total):
                turned = pltpu.roll(
                    bk[owner * n_blk], lax.rem((owner - me) * CAP + lay.width, lay.width), axis=1
                )
                return jnp.where(lanes == owner, turned, total)

            own = lax.fori_loop(0, n_dp, gather, jnp.zeros((48, lay.width), F32))
            xs[0:48, 0 : lay.real] = own[:, 0 : lay.real]

        where = place_of(step, ACTOR_TILE)
        now_f = framed(0, IN, where)
        now_in = now_f.astype(BF16)
        weight = xs[42:43, where]
        next_action, next_prob, _, _, _ = policy(framed(24, OBS, where).astype(BF16), 1, where)
        ahead[0:8, where] = next_action
        ys[1:2, where] = next_prob
        action, log_prob, bent, moved, (a1, da1, a2, da2) = policy(now_in, 0, where)
        judged_in = with_action(now_f, action)
        loss = alpha * log_prob - log_alpha * (log_prob + TARGET_ENTROPY)
        grad_action = jnp.zeros((8, ACTOR_TILE), F32)
        used = act_rows(ACTOR_TILE)
        for k in range(2):
            judged, (_, df1, _, df2) = critic(judged_in, 2 + k)
            loss -= 0.5 * judged
            g2 = outer_sloped(wide[5 + k], -0.5 * weight, df2)
            g1 = sloped(dot(w2h[k], g2), df1)
            grad_action += dot(w1n[k], g1)[0:8]
        grad_latent = 2.0 * alpha * weight * action + grad_action * (1.0 - action * action)
        grad_scale = grad_latent * moved - alpha * weight
        grad_bent = grad_scale * 3.5 * (1.0 - bent * bent)
        g3 = jnp.concatenate(
            [jnp.where(used, grad_latent, 0.0), jnp.where(used, grad_bent, 0.0)], 0
        ).astype(BF16)
        acc_a[...] += dot(g3, a2, NT)
        acc_m[:, 0:16] += dot(ones16(ACTOR_TILE), g3, NT)
        g2 = sloped(dot(head_t[...], g3), da2)
        add_hidden(2, a1, g2)
        g1 = sloped(dot(w2h[2], g2), da1)
        acc_w[2] += dot(now_in, g1, NT)
        acc_l[1:2, 0:ACTOR_TILE] += weight * loss
        acc_l[2:3, 0:ACTOR_TILE] += weight * (log_prob + TARGET_ENTROPY)

    put_matrix(2)
    chains[2][0]()

    @pl.loop(0, critic_tiles)
    def _(step):
        if critic_tiles > 1:
            take({1: [chains[2][1]]}, step)

        where = place_of(step, CRITIC_TILE)
        now_in = framed(0, IN, where).astype(BF16)
        reward = xs[23:24, where]
        done = xs[41:42, where]
        aim_in = with_action(framed(24, OBS, where), ahead[0:8, where])
        next_prob = ys[1:2, where]
        aim = jnp.minimum(critic(aim_in, 0)[0], critic(aim_in, 1)[0])
        target = reward + DISCOUNT * (1.0 - done) * (aim - alpha * next_prob)
        ys[0:1, where] = target
        critic_pass(0, now_in, where, target)

    put_matrix(0)
    chains[0][0]()
    if critic_tiles == 1:
        chains[2][1]()

    has_come(bk.at[pl.ds(0, (n_dp - 1) * (n_blk - 1))], "plane")
    lane0 = lay.real // 128 * 128

    def add_block(at, carry):
        sides, fills = carry
        slot = slot_of(at)
        return sides + bk[slot, 0:32, lane0 : lane0 + 128], fills + bk[slot, 40:48, 0 : lay.real]

    sides, fills = lax.fori_loop(
        0, lay.n_dev, add_block, (jnp.zeros((32, 128), F32), jnp.zeros((8, lay.real), F32))
    )
    at = lay.real - lane0
    rows_all = float(lay.replay * lay.n_dev)
    centre = sides[0:24, at : at + 1] / rows_all
    scale = lax.rsqrt(sides[0:24, at + 1 : at + 2] / rows_all - centre * centre + 1e-6)
    total = sides[24:25, at : at + 1] + jnp.sum(fills[2:3, :], axis=1, keepdims=True)
    count[...] = jnp.broadcast_to(total, (8, 128))

    @pl.loop(0, critic_tiles)
    def _(step):
        take({critic_tiles - 1: [chains[0][1], chains[2][2]]}, step)
        where = place_of(step, CRITIC_TILE)
        critic_pass(1, framed(0, IN, where).astype(BF16), where, ys[0:1, where])

    put_matrix(1)
    for k in range(3):
        put(R_IN + 24 * k, acc_w[k, 0:24, :])
    put(R_HEAD, acc_a[...])
    rowbuf[0:1, :] = acc_c[0, 0:1, :]
    rowbuf[1:2, :] = acc_c[1, 0:1, :]
    for k in range(3):
        rowbuf[2 + k : 3 + k, :] = acc_h[k, HSAC : HSAC + 1, :]
    put(R_OUT, rowbuf[...])
    folded = jnp.sum(acc_l[...], axis=1, keepdims=True)
    rowbuf[...] = jnp.zeros_like(rowbuf)
    rowbuf[0:1, 0:48] = acc_m[0:1, :]
    rowbuf[0:1, 64:65] = folded[0:1] + folded[1:2]
    rowbuf[0:1, 65:66] = folded[2:3]
    put(R_MISC, rowbuf[...])
    put(R_MISC + 8, jnp.zeros((R_SMALL - R_MISC - 8, HSAC), F32))
    chains[1][0]()

    def dyn_bias(start, width):
        row = jnp.zeros((1, width), F32)
        for e in range(MEMBERS):
            row = jnp.where(me == e, bias[:, start + width * e : start + width * (e + 1)], row)
        return row

    @pl.when(is_dyn)
    def _():
        w1f[0] = jnp.zeros((32, HSAC), F32)
        w1f[0, 0:IN, 0:HDYN] = rounded(dyn_in[dyn_e])
        for at, piece in enumerate(pieces(dyn_bias(DB1, HDYN))):
            w1f[0, IN + at : IN + at + 1, 0:HDYN] = piece.astype(F32)
        w1t[0] = (0.5 * w1f[0].T).astype(BF16)
        rowbuf[...] = jnp.zeros_like(rowbuf)
        rowbuf[0:1, 0:HDYN] = dyn_bias(DB2, HDYN)
        head_row = dyn_bias(DB3, DOUT)
        rowbuf[1:2, 0:HALF] = head_row[:, 0:HALF]
        rowbuf[1:2, 24 : 24 + HALF] = head_row[:, HALF:DOUT]
        rowbuf[2:3, 0:HALF] = bias[:, MAXLV : MAXLV + HALF]
        rowbuf[3:4, 0:HALF] = bias[:, MINLV : MINLV + HALF]
        dcols[...] = rowbuf[...].T
        wide[0] = jnp.broadcast_to(0.5 * dcols[:, 0:1], (HSAC, 128))
        dpack[...] = jnp.zeros_like(dpack)
        dpack[0:HALF, 0:HDYN] = dyn_out[dyn_e, 0:HALF, :]
        dpack[24 : 24 + HALF, 0:HDYN] = dyn_out[dyn_e, HALF:DOUT, :]
        dhead[...] = dpack[0:48, :].astype(BF16)
        dhead_t[...] = (0.5 * rounded(dpack[0:48, :])).T.astype(BF16)
        dpack[...] = jnp.zeros_like(dpack)

        has_come(dhg.at[pl.ds(0, n_blk - 1)], "dyn h")
        has_come(dmg.at[pl.ds(0, n_blk - 1)], "dyn m")
        dhg[z] = dyn_h[dyn_e]
        dmg[z] = dyn_m[dyn_e]
        dmat[...] = jnp.zeros_like(dmat)
        for block in range(n_blk):
            dmat[block * lay.drows : (block + 1) * lay.drows, 0:HDYN] = 0.5 * rounded(dhg[block])
        w2h[0] = dmat[...].astype(BF16)
        w2t[0] = dmat[...].T.astype(BF16)
        for ref in (dacc_h, dacc_w, dacc_o, dacc_m, dacc_b, dacc_l):
            ref[...] = jnp.zeros_like(ref)

    in_dyn = {}
    for at, event in (
        (1, chains[0][2]), (1, chains[1][1]), (2, chains[2][3]), (dyn_tiles - 1, chains[1][2]),
    ):
        in_dyn.setdefault(min(at, dyn_tiles - 1), []).append(event)

    @pl.loop(0, dyn_tiles)
    def _(tile):
        take(in_dyn, tile)

        @pl.when(is_dyn)
        def _():
            for at in range(per):
                slot = slot_of(tile * per + at)
                xt[:, at * lay.real : (at + 1) * lay.real] = bk[slot, :, 0 : lay.real]
            now = xt[0:24, :]
            later = xt[24:48, :]
            row24 = rows_of((24, DYN_TILE))
            scaled = jnp.where(row24 < IN, (now - centre) * scale, 1.0)
            inputs = jnp.concatenate([scaled, (rows_of((8, DYN_TILE)) < 2).astype(F32)], 0).astype(BF16)
            first, slope1 = gated(dot(w1t[0], inputs))
            second, slope2 = gated(dot(w2t[0], first), wide[0])
            out = dot(dhead[...], second) + dcols[0:48, 1:2]
            used = row24 < HALF
            upper = dcols[0:24, 2:3]
            lower = dcols[0:24, 3:4]
            gap1 = upper - out[24:48]
            gap2 = upper - softplus(gap1) - lower
            log_var = lower + softplus(gap2)
            error = out[0:24] - jnp.where(row24 == OBS, now[23:24], later - now)
            inverse = jnp.exp(-log_var)
            weight = xt[42:43, :] * (xt[43:44, :] == me.astype(F32)).astype(F32)
            spread_term = error * error * inverse
            nll = jnp.sum(jnp.where(used, spread_term + log_var, 0.0), axis=0, keepdims=True)
            dacc_l[0:1, :] += weight * nll
            grad_mu = 2.0 * weight * error * inverse
            grad_lv = weight * (1.0 - spread_term)
            open1 = sigmoid(gap1)
            open2 = sigmoid(gap2)
            grad_lv1 = grad_lv * open2
            dacc_b[0] += jnp.where(used, grad_lv1 * (1.0 - open1), 0.0)
            dacc_b[1] += jnp.where(used, grad_lv * (1.0 - open2), 0.0)
            g3 = jnp.concatenate(
                [jnp.where(used, grad_mu, 0.0), jnp.where(used, grad_lv1 * open1, 0.0)], 0
            ).astype(BF16)
            dacc_o[...] += dot(g3, second, NT)
            dacc_m[...] += dot(ones16(DYN_TILE), g3, NT)
            g2 = sloped(dot(dhead_t[...], g3), slope2)
            dacc_h[...] += dot(jnp.concatenate([first, ones16(DYN_TILE)], 0), g2, NT)
            g1 = sloped(dot(w2h[0], g2), slope1)
            dacc_w[...] += dot(inputs, g1, NT)

    out_of = {"pack": dyn_s, "x": dyn_x}

    def member_copy(name, src, owner, kind, sem, peer):
        return on_plane(src, out_of[name].at[owner], send.at[sent[name, kind]], recv.at[sem], peer)

    def give(name, src):
        like_peers(
            lambda peer: member_copy(name, src, dyn_e, "own", here_at[name, "like"] + dyn_e, peer).start()
        )
        member_copy(name, src, dyn_e, "own", here_at[name, "sibling"], sibling).start()

    def hand_on(name):
        def body(peer):
            @pl.when(peer < MEMBERS)
            def _():
                owner = jnp.minimum(peer, MEMBERS - 1)
                view = out_of[name].at[owner]
                member_copy(name, view, owner, "on", here_at[name, "like"] + owner, sibling).wait_recv()
                member_copy(name, view, owner, "on", here_at[name, "sibling"], sibling).start()

        like_peers(body)

    even, odd = (MEMBERS + 1) // 2, MEMBERS // 2
    handed = even - core * (even - odd) - jnp.where(is_dyn, 1, 0)

    def from_sibling(name):
        for side, number in ((0, odd), (1, even)):
            @pl.when(core == side)
            def _():
                has_come(out_of[name].at[pl.ds(0, number)], (name, "sibling"))

    def gave(name):
        @pl.when(is_dyn)
        def _():
            for begin in range(0, n_dp // 2, MEMBERS):
                number = min(MEMBERS, n_dp // 2 - begin)
                has_sent(out_of[name].at[pl.ds(0, number)], (name, "own"))

        for number in (even, even - 1, even - 2):
            @pl.when(handed == number)
            def _():
                has_sent(out_of[name].at[pl.ds(0, number)], (name, "on"))

    def line_rows(ref):
        rows = ref[0 : lay.drows, 0:HDYN]
        for block in range(1, n_blk):
            rows = jnp.where(z == block, ref[block * lay.drows : (block + 1) * lay.drows, 0:HDYN], rows)
        return rows

    mine_rows = pl.ds(pl.multiple_of(z * lay.rows, lay.rows), lay.rows)
    dyn_window = pl.ds(pl.multiple_of(z * lay.drows // 8 * 8, 8), -(-(lay.drows + 7) // 8) * 8)

    def from_window(value):
        rows = value[0 : lay.drows, 0:HDYN]
        for block in range(1, n_blk):
            begin = block * lay.drows % 8
            rows = jnp.where(z == block, value[begin : begin + lay.drows, 0:HDYN], rows)
        return rows

    def take_matrix(k):
        tiles_on(k).wait_recv()
        for chunk in range(n_dp):
            tile = chunk * lay.mat
            half, row = tile // 32, tile % 32
            at = slice(row * 8, (row + lay.mat) * 8)
            piece = mg[k, chunk % 2, chunk // 2].reshape(lay.mat * 8, 128)
            mat[k, at, half * 128 : (half + 1) * 128] = piece / total
        normalise(mat.at[k])

    chains[2][4]()
    chains[0][3]()

    @pl.when(is_dyn)
    def _():
        dpack[D_IN : D_IN + 24, :] = dacc_w[0:24, :]
        dpack[D_OUT : D_OUT + HALF, :] = dacc_o[0:HALF, :]
        dpack[D_OUT + HALF : D_OUT + DOUT, :] = dacc_o[24 : 24 + HALF, :]
        dpack[D_B2 : D_B2 + 1, :] = dacc_h[HSAC : HSAC + 1, :]
        dpack[D_B3 : D_B3 + 1, 0:48] = dacc_m[0:1, :]
        lanes = lax.broadcasted_iota(jnp.int32, (24, 128), 1)
        bound = jnp.where(
            lanes == 0,
            jnp.sum(dacc_b[0], axis=1, keepdims=True),
            jnp.where(lanes == 1, jnp.sum(dacc_b[1], axis=1, keepdims=True), 0.0),
        )
        dpack[D_UP : D_UP + 2, 0:24] = bound.T[0:2, :]
        dpack[D_LOSS : D_LOSS + 1, 0:128] = jnp.broadcast_to(
            jnp.sum(dacc_l[0:1, :], axis=1, keepdims=True), (1, 128)
        )
        dpack[D_HID : D_HID + lay.drows, 0:HDYN] = line_rows(dacc_h)
        dyn_s[dyn_e] = dpack[...]
        give("pack", dpack)
        dmat[...] = jnp.zeros_like(dmat)
        for block in range(n_blk):
            at = slice(block * lay.drows, (block + 1) * lay.drows)
            dmat[at, 0:HDYN] = MOMENTUM * dmg[block] + dacc_h[at, 0:HDYN] / total
        normalise(dmat)

    def sum_end(step):
        @pl.when(step == 3)
        def _():
            chains[0][4]()
            chains[1][3]()

    take_matrix(2)

    @pl.when(is_dyn)
    def _():
        both = [dmat, mat.at[2]]
        schulz(both, NS_ITERS - 1, sum_end)
        window, sac_x[2] = schulz_rows(both, [dyn_window, mine_rows], gram)
        rows = from_window(window)
        drow_x[...] = rows
        dyn_x[dyn_e] = rows
        give("x", drow_x)

    @pl.when(jnp.logical_not(is_dyn))
    def _():
        schulz([mat.at[2]], NS_ITERS - 1, sum_end)
        (sac_x[2],) = schulz_rows([mat.at[2]], [mine_rows], gram)

    def sent_early():
        has_sent(wg.at[pl.ds(0, n_blk - 1), :, half_rows], "hidden")
        has_sent(wg.at[pl.ds(0, n_blk - 1), :, half_rows], "hidden on")
        has_sent(asked.at[pl.ds(0, n_dp - 1)], "lists")
        has_sent(bk.at[pl.ds(0, n_dp - 1)], "own")
        has_sent(bk.at[pl.ds(0, n_blk - 1)], "line")
        has_sent(bk.at[pl.ds(0, (n_dp - 1) * (n_blk - 1))], "plane")

        @pl.when(is_dyn)
        def _():
            has_sent(dhg.at[pl.ds(0, n_blk - 1)], "dyn h")
            has_sent(dmg.at[pl.ds(0, n_blk - 1)], "dyn m")

        for group in range(3):
            core_sum(group).wait_send()
            has_sent(froms[group].at[pl.ds(0, lay.half - 1)], ("plane sum", group))
        for part in range(4):
            has_sent(line_bytes(part), ("line sum", part))

    def pass_on(step):
        pl.when(step == 2)(functools.partial(hand_on, "pack"))

    sent_early()
    chains[1][4]()
    for k in range(2):
        take_matrix(k)
    both = [mat.at[0], mat.at[1]]
    schulz(both, NS_ITERS - 1, pass_on)
    hand_on("x")
    sac_x[0], sac_x[1] = schulz_rows(both, [mine_rows, mine_rows], gram)
    for k in range(3):
        for half in range(2):
            for piece in range(lay.rows // 8 // lay.mat):
                chunk = (half * 32 + z * (lay.rows // 8)) // lay.mat + piece
                kept = mg[k, lax.rem(chunk, 2), chunk // 2]
                sac_g[half, k, piece * lay.mat : (piece + 1) * lay.mat] = kept

    small_on().wait_recv()
    from_sibling("pack")
    from_sibling("x")

    has_sent(small.at[pl.ds(0, (lay.half - 1) * lay.sml)], "small")
    small_on().wait_send()
    gave("pack")
    gave("x")

    for k in range(3):
        has_sent(mg.at[k, 0, pl.ds(0, lay.half - 1)], ("tiles", k))
        tiles_on(k).wait_send()


def ordered(lay, n_in, n_out, *refs):
    inputs, outputs, scratch = refs[:n_in], refs[n_in : n_in + n_out], refs[n_in + n_out :]
    main_kernel(lay, *inputs, *scratch[: n_in + 1], *outputs, *scratch[n_in + 1 :])


def adamw(weights, first, second, gradient):
    first = BETA_FIRST * first + (1.0 - BETA_FIRST) * gradient
    second = BETA_SECOND * second + (1.0 - BETA_SECOND) * gradient * gradient
    first_hat = first / (1.0 - BETA_FIRST**STEP)
    second_hat = second / (1.0 - BETA_SECOND**STEP)
    step = first_hat / (jnp.sqrt(second_hat) + 1e-8) + ADAM_DECAY * weights
    return weights - ADAM_RATE * step, first, second


def update_kernel(lay, *refs):
    (
        sac_g, sac_x, dyn_x, dyn_s, small, count, crit_rows, sac_h, dyn_h, dyn_m,
        ci, ci_m, ci_v, ai, ai_m, ai_v, di, di_m, di_v, ao, ao_m, ao_v,
        do, do_m, do_v, bi, bi_m, bi_v,
        sac_new, sac_mom, dyn_new, dyn_mom, ci_n, ci_mn, ci_vn, ai_n, ai_mn, ai_vn, di_n, di_mn,
        di_vn, co_n, co_mn, co_vn, ao_n, ao_mn, ao_vn, do_n, do_mn, do_vn, bi_n, bi_mn, bi_vn,
        loss, counted, bg,
    ) = refs
    total = count[0:1, 0:1]
    for k in range(3):
        for side in range(2):
            tiles = sac_g[side, k].reshape(sac_mom.shape[1], 128)
            sac_mom[k, :, side * 128 : (side + 1) * 128] = tiles / total
    sac_new[...] = sac_h[...] * (1.0 - MUON_RATE * MUON_DECAY) - MUON_RATE * sac_x[...]
    dyn_rows = dyn_s[:, D_HID : D_HID + dyn_m.shape[1], 0:HDYN]
    dyn_mom[...] = MOMENTUM * dyn_m[...] + dyn_rows / total.reshape(1, 1, 1)
    dyn_new[...] = dyn_h[...] * (1.0 - MUON_RATE * MUON_DECAY) - MUON_RATE * dyn_x[...]

    def rows(row, number):
        def tile(at):
            chunk = at // lay.sml
            return small[(chunk % 2 * lay.half + chunk // 2) * lay.sml + at % lay.sml]

        sides = []
        for side in range(2):
            at = side * (R_SMALL // 8) + row // 8
            sides.append(jnp.concatenate([tile(at + more) for more in range(-(-number // 8))], 0))
        return jnp.concatenate(sides, 1)

    def store(outs, at, values):
        for out, value in zip(outs, values):
            out[at] = value

    outs = (ci_n, ci_mn, ci_vn)
    for k in range(2):
        at = (slice(None), k, slice(None))
        grad = rows(R_IN + 24 * k, 24)
        bg[:, CB1 + HSAC * k : CB1 + HSAC * (k + 1)] = grad[IN : IN + 1]
        store(outs, at, adamw(ci[at], ci_m[at], ci_v[at], grad[0:IN] / total))
    grad = rows(R_IN + 48, 24)
    bg[:, AB1 : AB1 + HSAC] = grad[IN : IN + 1]
    store((ai_n, ai_mn, ai_vn), ..., adamw(ai[...], ai_m[...], ai_v[...], grad[0:OBS] / total))
    grad = rows(R_HEAD, 16)
    for at, row in ((slice(0, ACT), slice(1, 1 + ACT)), (slice(ACT, 2 * ACT), slice(9, 9 + ACT))):
        store((ao_n, ao_mn, ao_vn), at, adamw(ao[at], ao_m[at], ao_v[at], grad[row] / total))
    grad = rows(R_OUT, 8)
    held = [crit_rows[2 * at : 2 * at + 2, :] for at in range(3)]
    store((co_n, co_mn, co_vn), ..., adamw(*held, grad[0:2] / total))
    bg[:, CB2 : CB2 + HSAC] = grad[2:3]
    bg[:, CB2 + HSAC : CB2 + 2 * HSAC] = grad[3:4]
    bg[:, AB2 : AB2 + HSAC] = grad[4:5]
    grad = rows(R_MISC, 8)
    bg[:, CB3 : CB3 + 1] = grad[0:1, 16:17]
    bg[:, CB3 + 1 : CB3 + 2] = grad[0:1, 32:33]
    bg[:, AB3 : AB3 + ACT] = grad[0:1, 1 : 1 + ACT]
    bg[:, AB3 + ACT : AB3 + 2 * ACT] = grad[0:1, 9 : 9 + ACT]
    bg[:, LOGA : LOGA + 1] = -grad[0:1, 65:66]
    total_loss = grad[0:1, 64:65]
    up = jnp.zeros((1, HALF), F32)
    low = jnp.zeros((1, HALF), F32)
    for e in range(MEMBERS):
        pack = dyn_s[e]
        total_loss = total_loss + pack[D_LOSS : D_LOSS + 1, 0:1]
        up = up + pack[D_UP : D_UP + 1, 0:HALF]
        low = low + pack[D_LOW : D_LOW + 1, 0:HALF]
        bg[:, DB1 + HDYN * e : DB1 + HDYN * (e + 1)] = pack[IN : IN + 1, 0:HDYN]
        bg[:, DB2 + HDYN * e : DB2 + HDYN * (e + 1)] = pack[D_B2 : D_B2 + 1, 0:HDYN]
        bg[:, DB3 + DOUT * e : DB3 + DOUT * e + HALF] = pack[D_B3 : D_B3 + 1, 0:HALF]
        bg[:, DB3 + DOUT * e + HALF : DB3 + DOUT * (e + 1)] = pack[D_B3 : D_B3 + 1, 24 : 24 + HALF]
        grad = pack[0:IN, 0:HDYN] / total
        store((di_n, di_mn, di_vn), e, adamw(di[e], di_m[e], di_v[e], grad))
        grad = pack[D_OUT : D_OUT + DOUT, 0:HDYN] / total
        store((do_n, do_mn, do_vn), e, adamw(do[e], do_m[e], do_v[e], grad))
    bg[:, MAXLV : MAXLV + HALF] = up
    bg[:, MINLV : MINLV + HALF] = low
    lane = lax.broadcasted_iota(jnp.int32, (1, NB), 1)
    bounds = jnp.where(
        jnp.logical_and(lane >= MAXLV, lane < MINLV),
        BOUND_WEIGHT,
        jnp.where(jnp.logical_and(lane >= MINLV, lane < LOGA), -BOUND_WEIGHT, 0.0),
    )
    grad = bg[...] / total + bounds
    flat = [ref[...].reshape(1, NB) for ref in (bi, bi_m, bi_v)]
    store((bi_n, bi_mn, bi_vn), ..., [value.reshape(NB) for value in adamw(*flat, grad)])
    loss[...] = total_loss
    counted[...] = total


def shards(
    lay, replay, model_rows, requests, member_of, model_live, noise, sac_hidden, sac_hidden_mom,
    dyn_hidden, dyn_hidden_mom, crit_in, crit_in_m, crit_in_v, act_in, act_in_m, act_in_v, dyn_in,
    dyn_in_m, dyn_in_v, crit_out, crit_out_m, crit_out_v, act_out, act_out_m, act_out_v, dyn_out,
    dyn_out_m, dyn_out_v, biases, biases_m, biases_v, targ_in, targ_hidden, targ_out, targ_bias,
):
    n_dp, n_blk = lay.n_dp, lay.n_blk
    spec = pl.BlockSpec(memory_space=pltpu.VMEM)

    def flip(value):
        return jnp.transpose(value, (1, 0, 2))

    def swap(value):
        return jnp.swapaxes(value, -1, -2)

    def kept(value):
        return pltpu.with_memory_space_constraint(value, pltpu.VMEM)

    inputs = (
        sac_hidden, requests, member_of, replay, model_live, model_rows, jnp.transpose(noise, (2, 0, 1)),
        biases, flip(targ_in), flip(crit_in), act_in, targ_bias, targ_hidden, crit_out, targ_out,
        swap(act_out), dyn_hidden, dyn_hidden_mom, crit_out_m, crit_out_v, sac_hidden_mom, dyn_in,
        swap(dyn_out),
    )
    shape = jax.ShapeDtypeStruct
    rows, drows = lay.rows, lay.drows
    out_shape = (
        pltpu.VMEM((2, 3, rows // 8, 8, 128), F32),
        pltpu.VMEM((3, rows, HSAC), F32),
        pltpu.VMEM((MEMBERS, drows, HDYN), F32),
        pltpu.VMEM((MEMBERS, D_ROWS, HSAC), F32),
        pltpu.VMEM((32, 8, 128), F32),
        pltpu.VMEM((8, 128), F32),
        pltpu.VMEM((8, HSAC), F32),
    )

    def vm(*dims, kind=F32):
        return pltpu.VMEM(dims, kind)

    scratch = [
        vm(n_blk, 3, rows, HSAC, kind=BF16),
        vm(2, n_dp, CAP, kind=jnp.int32),
        vm(n_dp, 2, n_dp, CAP, kind=jnp.int32),
        vm(n_blk, drows, HDYN),
        vm(n_blk, drows, HDYN),
        vm(lay.n_dev, 48, lay.width),
        vm(56, lay.batch),
        vm(2, 8, lay.batch),
        vm(8, lay.batch),
        vm(8, lay.batch),
        vm(5, 32, HSAC),
        vm(5, HSAC, 32, kind=BF16),
        vm(2, 16, HSAC, kind=BF16),
        vm(5, HSAC, HSAC, kind=BF16),
        vm(3, HSAC, HSAC, kind=BF16),
        vm(5, 16, HSAC, kind=BF16),
        vm(HSAC, 16, kind=BF16),
        vm(16, HSAC),
        vm(8, HSAC),
        vm(7, HSAC, 128),
        vm(128, 8),
        vm(3, HSAC + 16, HSAC),
        vm(3, 32, HSAC),
        vm(2, 16, HSAC),
        vm(16, HSAC),
        vm(16, 48),
        vm(8, max(CRITIC_TILE, ACTOR_TILE)),
        *[vm(2, lay.half, chunk, 8, 128) for chunk in lay.chunks],
        *[vm(lay.half, chunk, 8, 128) for chunk in lay.chunks],
        *[vm(lay.half, chunk, 8, 128) for chunk in lay.chunks],
        *[vm(n_blk, chunk, 8, 128) for chunk in lay.chunks],
        *[vm(chunk, 8, 128) for chunk in lay.chunks],
        *[vm(chunk, 8, 128) for chunk in lay.chunks],
        vm(3, 2, lay.half, lay.mat, 8, 128),
        vm(3, HSAC, HSAC),
        vm(2, HSAC, HSAC),
        vm(HSAC, 8),
        vm(HSAC + 16, HSAC),
        vm(32, HSAC),
        vm(48, HSAC),
        vm(16, 48),
        vm(2, 24, DYN_TILE),
        vm(8, DYN_TILE),
        vm(48, DYN_TILE),
        vm(HSAC, HSAC),
        vm(D_ROWS, HSAC),
        vm(drows, HDYN),
        vm(1, NB),
        vm(48, HSAC, kind=BF16),
        vm(HSAC, 48, kind=BF16),
    ]
    scratch += [pltpu.SemaphoreType.DMA((lay.departures,)), pltpu.SemaphoreType.DMA((lay.arrivals,))]
    held = [pltpu.VMEM(value.shape, value.dtype) for value in inputs]
    held.append(pltpu.SemaphoreType.DMA((len(inputs),)))
    varying = 4 * (lay.n_dev * 48 * lay.width + 72 * lay.batch + 48 * lay.replay)
    gathered = pl.pallas_call(
        functools.partial(ordered, lay, len(inputs), len(out_shape)),
        out_shape=out_shape,
        in_specs=[pl.BlockSpec(memory_space=pl.ANY)] * len(inputs),
        out_specs=[spec] * len(out_shape),
        scratch_shapes=held + scratch,
        compiler_params=pltpu.CompilerParams(
            collective_id=0, has_side_effects=True, vmem_limit_bytes=26 * 2**20 + varying
        ),
        name="step",
    )(*[pltpu.with_memory_space_constraint(value, pltpu.HBM) for value in inputs])
    params = (
        sac_hidden, dyn_hidden, dyn_hidden_mom,
        flip(crit_in), flip(crit_in_m), flip(crit_in_v), act_in, act_in_m, act_in_v,
        dyn_in, dyn_in_m, dyn_in_v,
        swap(act_out), swap(act_out_m), swap(act_out_v),
        swap(dyn_out), swap(dyn_out_m), swap(dyn_out_v), biases, biases_m, biases_v,
    )
    new_shape = [shape(sac_hidden.shape, F32)] + [shape(value.shape, F32) for value in params[:12]]
    new_shape += [shape(crit_out.shape, F32)] * 3 + [shape(value.shape, F32) for value in params[12:]]
    new_shape += [shape((1, 1), F32)] * 2
    out = pl.pallas_call(
        functools.partial(update_kernel, lay),
        out_shape=tuple(new_shape),
        in_specs=[spec] * (len(gathered) + len(params)),
        out_specs=[spec] * len(new_shape),
        scratch_shapes=[vm(1, NB)],
        compiler_params=pltpu.CompilerParams(vmem_limit_bytes=16 * 2**20),
        name="update",
    )(*[kept(value) for value in gathered], *params)
    out = list(out)
    for at in (4, 5, 6):
        out[at] = flip(out[at])
    for at in (16, 17, 18, 19, 20, 21):
        out[at] = swap(out[at])
    for at in (25, 26):
        out[at] = out[at].reshape(())
    return tuple(out)


def solution(mesh):
    both = ("dp", "blk")
    sharded = (
        P(None, both), P(None, both), P(both, None), P(both, None), P(both), P(None, both, None),
    )
    hidden = (P(None, "blk", None),) * 4

    def step(replay, model_rows, *others):
        lay = Layout(mesh, replay.shape[1], model_rows.shape[1])
        return shards(lay, replay, model_rows, *others)

    return jax.shard_map(
        step,
        mesh=mesh,
        in_specs=sharded + hidden + (P(),) * 25,
        out_specs=hidden + (P(),) * 23,
        check_vma=False,
    )
```
